512 devices in a mesh: dp: 64 (over z, y), head: 8 (over x, core).
Axes of the slice: x: 4, y: 4, z: 16, core: 2. Of those that a mesh axis runs over, the one named last changes fastest.
Arguments:
- tokens: bfloat16 [8192, 1536], P('dp'), may hold values from -6 to 6
- cotangent: bfloat16 [8192, 1536], P('dp'), may hold values from -2 to 2
- w_qkv: bfloat16 [1536, 3, 1024], P(None, None, 'head'), may hold values from -0.15625 to 0.15625
- w_out: bfloat16 [1024, 1536], P('head'), may hold values from -0.5 to 0.5
- qk_gain: float32 [2, 64], replicated, may hold values from 1 to 4.5
- modulation: bfloat16 [32, 3, 1536], replicated, may hold values from -4 to 4
- image_counts: int32 [32], replicated, may hold values from 1 to 768, as said below
Outputs:
- layer_out: bfloat16 [8192, 1536], P(('dp', 'head'))
- input_grad: bfloat16 [8192, 1536], P(('dp', 'head'))
The draws below stay inside these ranges and needn't reach their ends.
Inputs may be any that keep to these rules, and one draw needn't show every extreme that they name: `image_counts`: the counts sum to 8192; each image's rows are consecutive in the pack, images in the order of this array; 8 of the images, at places drawn anew, hold exactly 768 tokens each, and every other image fewer.
All inputs are finite; a program needn't handle non-finite values.
Results may differ from the reference program's by a relative error of at most 0.028.
The reference program's roundings to bfloat16 on the way count: a program that leaves them out, or rounds other values in their place, can miss the bound.
Values may be sent and summed in bfloat16 or wider, within the bound.
No kernel may reach another device: no remote copies, remote signals or barrier semaphores. Data moves between devices by JAX's collectives and lax.ppermute only.
A program may use at most 64 MiB of HBM per device.

```python
import math
import jax
import jax.numpy as jnp
from jax import lax

D = 1536
HD = 64
HEADS = 16
TOK_DEV = 128
REACH = 6
TOKENS = 8192
MOST_IMG = 768
IMAGES = 32
N_DP = 64
N_HEAD = 8


def draw_qk_gain(key, part):
    key = jax.random.fold_in(key, 7)
    return jax.random.uniform(key, (2, HD), jnp.float32, 1.0, 1.5)


def draw_image_counts(key, part):
    key = jax.random.fold_in(key, 11)
    weight_key, order_key = jax.random.split(key)
    big_count = IMAGES // 4
    small_count = IMAGES - big_count
    small_total = TOKENS - big_count * MOST_IMG
    spare = small_total - small_count
    weights = jax.random.randint(weight_key, (small_count,), 1, 5).astype(jnp.int32)
    shares = (spare * weights // jnp.sum(weights)).astype(jnp.int32)
    leftover = spare - jnp.sum(shares)
    first_slot = jnp.arange(small_count, dtype=jnp.int32) == 0
    small_counts = 1 + shares + jnp.where(first_slot, leftover, 0)
    big_counts = jnp.full((big_count,), MOST_IMG, jnp.int32)
    counts = jnp.concatenate([big_counts, small_counts.astype(jnp.int32)])
    order = jax.random.permutation(order_key, IMAGES)
    return counts[order].astype(jnp.int32)


def level_of(rng, dims, cuts, smallest, top_value):
    def one(position, blocks):
        draws = jax.random.uniform(jax.random.fold_in(jax.random.fold_in(rng, 6), position), (blocks,), jnp.float32, smallest / len(cuts), top_value / len(cuts))
        return jnp.repeat(jnp.exp(draws), dims[position] // blocks).reshape((-1,) + (1,) * (len(dims) - position - 1))

    loudness = one(*cuts[0])
    for cut in cuts[1:]:
        loudness = loudness * one(*cut)
    return loudness


def gaussian(stream_key, dims, spread, most, shards=(), held_as=jnp.bfloat16):
    loudness = level_of(stream_key, dims, shards, -0.22, 0.18) if shards else 1.0
    values = jax.random.normal(stream_key, dims, jnp.float32) * spread * loudness
    return jnp.minimum(jnp.maximum(values, -most), most).astype(held_as)


def setup_inputs(seed: int = 0) -> dict:
    streams_of = jax.random.split(jax.random.key(seed), 8)
    return {
        "tokens": gaussian(streams_of[0], (TOKENS, D), 1.0, 6.0, ((0, 64),)),
        "cotangent": gaussian(streams_of[1], (TOKENS, D), 0.333, 2.0, ((0, 64),)),
        "w_qkv": gaussian(streams_of[2], (D, 3, HEADS * HD), D ** -0.5, 0.15625, ((2, 8),)),
        "w_out": gaussian(streams_of[3], (HEADS * HD, D), (HEADS * HD // 9) ** -0.5, 0.5, ((0, 8),)),
        "qk_gain": draw_qk_gain(jax.random.fold_in(streams_of[7], 71), 0),
        "modulation": gaussian(streams_of[5], (IMAGES, 3, D), 1.0, 4.0),
        "image_counts": draw_image_counts(jax.random.fold_in(streams_of[7], 71), 0),
    }


EPS = 1e-06
NEGATIVE = -1e+30

def head_attend(queries, keys_in, values_in, gains, key_mask):
    q_norm = queries * lax.rsqrt(lax.optimization_barrier(jnp.mean(queries * queries, axis=-1, keepdims=True)) + EPS) * gains[0]
    k_norm = keys_in * lax.rsqrt(lax.optimization_barrier(jnp.mean(keys_in * keys_in, axis=-1, keepdims=True)) + EPS) * gains[1]
    scores = lax.dot_general(q_norm.astype(jnp.bfloat16), k_norm.astype(jnp.bfloat16), (((1,), (1,)), ((), ())), preferred_element_type=jnp.float32) * (1.0 / math.sqrt(queries.shape[-1]))
    scores = jnp.where(key_mask, scores, NEGATIVE)
    highest = lax.stop_gradient(lax.optimization_barrier(jnp.max(scores, axis=-1, keepdims=True)))
    weights = jnp.exp(scores - highest)
    probabilities = weights / lax.optimization_barrier(jnp.sum(weights, axis=-1, keepdims=True))
    return jnp.dot(probabilities.astype(jnp.bfloat16), values_in.astype(jnp.bfloat16), preferred_element_type=jnp.float32)

def block_attend(queries, keys_in, values_in, gains, key_mask, grad_out):

    def attend_here(query_set, key_set, value_set):
        return jax.vmap(head_attend, in_axes=(0, 0, 0, None, None))(query_set, key_set, value_set, gains, key_mask)
    result, pullback = jax.vjp(attend_here, queries, keys_in, values_in)
    return (result, pullback(grad_out))

def segment_rows(positions, starts, total):
    inside = (positions[:, None] >= starts[None, :]).astype(jnp.int32)
    found = lax.optimization_barrier(jnp.sum(inside, axis=1)) - 1
    return jnp.where(positions >= total, -2, found).astype(jnp.int32)

def reference(tokens, cotangent, w_qkv, w_out, qk_gain, modulation, image_counts):
    inner_width = HEADS * HD
    local_cols = inner_width // N_HEAD
    image_ends = jnp.cumsum(image_counts).astype(jnp.int32)
    starts = (image_ends - image_counts).astype(jnp.int32)
    positions = jnp.arange(TOKENS, dtype=jnp.int32)
    segment = segment_rows(positions, starts, TOKENS)
    per_token = modulation.astype(jnp.float32)[segment]
    shift_rows = per_token[:, 0]
    scale_rows = per_token[:, 1]
    gate_rows = per_token[:, 2]
    token_values = tokens.astype(jnp.float32)
    average = lax.optimization_barrier(jnp.mean(token_values, axis=-1, keepdims=True))
    centred = token_values - average
    inv_std = lax.rsqrt(lax.optimization_barrier(jnp.mean(centred * centred, axis=-1, keepdims=True)) + EPS)
    normed = centred * inv_std
    hidden = (normed * (1.0 + scale_rows) + shift_rows).astype(jnp.bfloat16)
    qkv_rows = jnp.dot(hidden, w_qkv.reshape(D, 3 * inner_width), preferred_element_type=jnp.float32).astype(jnp.bfloat16)
    d_mixed = (cotangent.astype(jnp.float32) * gate_rows).astype(jnp.bfloat16)
    d_attn = lax.dot_general(d_mixed, w_out, (((1,), (1,)), ((), ())), preferred_element_type=jnp.float32).astype(jnp.bfloat16)
    margin = REACH * TOK_DEV
    window_rows = (2 * REACH + 1) * TOK_DEV
    key_values = qkv_rows[:, inner_width:]
    margin_zeros = jnp.zeros((margin, 2 * inner_width), jnp.bfloat16)
    padded_kv = jnp.concatenate([margin_zeros, key_values, margin_zeros], axis=0)
    block_rows = jnp.arange(TOK_DEV, dtype=jnp.int32)
    window_offsets = jnp.arange(window_rows, dtype=jnp.int32) - margin

    def one_block(grad_acc, block_index):
        row_start = (block_index * TOK_DEV).astype(jnp.int32)
        query_rows = lax.dynamic_slice_in_dim(qkv_rows, row_start, TOK_DEV, 0)[:, :inner_width]
        given = lax.dynamic_slice_in_dim(d_attn, row_start, TOK_DEV, 0)
        window = lax.dynamic_slice_in_dim(padded_kv, row_start, window_rows, 0)
        query_seg = segment_rows(row_start + block_rows, starts, TOKENS)
        key_seg = segment_rows(row_start + window_offsets, starts, TOKENS)
        key_mask = query_seg[:, None] == key_seg[None, :]
        queries = query_rows.astype(jnp.float32).reshape(TOK_DEV, HEADS, HD).transpose(1, 0, 2)
        kv_heads = window.astype(jnp.float32).reshape(window_rows, 2, HEADS, HD).transpose(1, 2, 0, 3)
        grad_out = given.astype(jnp.float32).reshape(TOK_DEV, HEADS, HD).transpose(1, 0, 2)
        result, grad_parts = block_attend(queries, kv_heads[0], kv_heads[1], qk_gain, key_mask, grad_out)
        attn_block = result.astype(jnp.bfloat16).transpose(1, 0, 2).reshape(TOK_DEV, inner_width)
        query_block = grad_parts[0].astype(jnp.bfloat16).transpose(1, 0, 2).reshape(TOK_DEV, inner_width)
        kv_grad = jnp.stack([grad_parts[1], grad_parts[2]], axis=0).transpose(2, 0, 1, 3).reshape(window_rows, 2 * inner_width)
        current = lax.dynamic_slice_in_dim(grad_acc, row_start, window_rows, 0)
        grad_acc = lax.dynamic_update_slice_in_dim(grad_acc, current + kv_grad, row_start, 0)
        return (grad_acc, (attn_block, query_block))
    start_acc = jnp.zeros((TOKENS + 2 * margin, 2 * inner_width), jnp.float32)
    grad_acc, (attn_blocks, query_blocks) = lax.scan(one_block, start_acc, jnp.arange(N_DP, dtype=jnp.int32))
    attn_all = attn_blocks.reshape(TOKENS, inner_width)
    kv_grads = grad_acc[margin:margin + TOKENS].astype(jnp.bfloat16)
    grad_all = jnp.concatenate([query_blocks.reshape(TOKENS, inner_width), kv_grads], axis=1)

    def out_group(running, group_index):
        columns = lax.dynamic_slice_in_dim(attn_all, group_index * local_cols, local_cols, 1)
        weight_rows = lax.dynamic_slice_in_dim(w_out, group_index * local_cols, local_cols, 0)
        partial_sum = jnp.dot(columns, weight_rows, preferred_element_type=jnp.float32).astype(jnp.bfloat16)
        return (running + lax.optimization_barrier(partial_sum).astype(jnp.float32), None)
    group_iota = jnp.arange(N_HEAD, dtype=jnp.int32)
    mixed_rows, unused = lax.scan(out_group, jnp.zeros((TOKENS, D), jnp.float32), group_iota)
    layer_out = (token_values + gate_rows * mixed_rows).astype(jnp.bfloat16)
    grad_split = grad_all.reshape(TOKENS, 3, inner_width)
    weight_split = w_qkv.reshape(D, 3, inner_width)

    def grad_group(running, group_index):
        columns = lax.dynamic_slice_in_dim(grad_split, group_index * local_cols, local_cols, 2).reshape(TOKENS, 3 * local_cols)
        weight_cols = lax.dynamic_slice_in_dim(weight_split, group_index * local_cols, local_cols, 2).reshape(D, 3 * local_cols)
        partial_sum = lax.dot_general(columns, weight_cols, (((1,), (1,)), ((), ())), preferred_element_type=jnp.float32).astype(jnp.bfloat16)
        return (running + lax.optimization_barrier(partial_sum).astype(jnp.float32), None)
    d_hidden, unused = lax.scan(grad_group, jnp.zeros((TOKENS, D), jnp.float32), group_iota)
    d_normed = d_hidden * (1.0 + scale_rows)
    input_grad = cotangent.astype(jnp.float32) + inv_std * (d_normed - lax.optimization_barrier(jnp.mean(d_normed, axis=-1, keepdims=True)) - normed * lax.optimization_barrier(jnp.mean(d_normed * normed, axis=-1, keepdims=True)))
    return (layer_out, input_grad.astype(jnp.bfloat16))
```

```python
import functools
import math

import jax
import jax.numpy as jnp
from jax import lax
from jax.sharding import PartitionSpec as P

REACH = 6


EPS = 1e-06
NEGATIVE = -1e30


def passed_along(x, axis, by):
    count = lax.axis_size(axis)
    pairs = [(i, i + by) for i in range(count) if 0 <= i + by < count]
    return lax.ppermute(x, axis, pairs)


def head_attend(queries, keys_in, values_in, gains, key_mask):
    q_norm = (
        queries * lax.rsqrt(jnp.mean(queries * queries, axis=-1, keepdims=True) + EPS) * gains[0]
    )
    k_norm = (
        keys_in * lax.rsqrt(jnp.mean(keys_in * keys_in, axis=-1, keepdims=True) + EPS) * gains[1]
    )
    scores = lax.dot_general(
        q_norm.astype(jnp.bfloat16),
        k_norm.astype(jnp.bfloat16),
        (((1,), (1,)), ((), ())),
        preferred_element_type=jnp.float32,
    ) * (1.0 / math.sqrt(queries.shape[-1]))
    scores = jnp.where(key_mask, scores, NEGATIVE)
    highest = lax.stop_gradient(jnp.max(scores, axis=-1, keepdims=True))
    weights = jnp.exp(scores - highest)
    probabilities = weights / jnp.sum(weights, axis=-1, keepdims=True)
    return jnp.dot(
        probabilities.astype(jnp.bfloat16),
        values_in.astype(jnp.bfloat16),
        preferred_element_type=jnp.float32,
    )


def segment_rows(positions, starts, total):
    inside = (positions[:, None] >= starts[None, :]).astype(jnp.int32)
    found = jnp.sum(inside, axis=1) - 1
    return jnp.where(positions >= total, -2, found)


def window_attend(
    query_heads, kv_heads, grad_heads, gains, key_mask, reach_blocks, tok_rows, width_blocks
):

    def per_head(pieces):

        def attend_here(query_set, key_set, value_set):
            return head_attend(query_set, key_set, value_set, gains, key_mask)

        result, pullback = jax.vjp(attend_here, pieces[0], pieces[1], pieces[2])
        grad_parts = pullback(pieces[3])
        return (
            result.astype(jnp.bfloat16),
            grad_parts[0].astype(jnp.bfloat16),
            grad_parts[1],
            grad_parts[2],
        )

    outputs = lax.map(per_head, (query_heads, kv_heads[0], kv_heads[1], grad_heads))
    kv_grad = jnp.stack([outputs[2], outputs[3]], axis=0)
    return (outputs[0], outputs[1], kv_grad)


def per_device(tokens, cotangent, w_qkv, w_out, qk_gain, modulation, image_counts):
    tok_rows, model_width = tokens.shape
    local_cols = w_out.shape[0]
    head_dim = qk_gain.shape[1]
    head_count = local_cols // head_dim
    image_count = image_counts.shape[0]
    head_devices = lax.axis_size("head")
    share_rows = tok_rows // head_devices
    first_row = lax.axis_index("head") * share_rows
    first_global = lax.axis_index("dp") * tok_rows
    reach_blocks = REACH
    window_rows = (2 * reach_blocks + 1) * tok_rows
    image_ends = jnp.cumsum(image_counts)
    starts = image_ends - image_counts
    total_rows = image_ends[-1]
    query_seg = segment_rows(
        first_global + jnp.arange(tok_rows, dtype=jnp.int32), starts, total_rows
    )
    key_seg = segment_rows(
        first_global - reach_blocks * tok_rows + jnp.arange(window_rows, dtype=jnp.int32),
        starts,
        total_rows,
    )
    key_mask = query_seg[:, None] == key_seg[None, :]
    image_iota = jnp.arange(image_count, dtype=jnp.int32)
    member = (query_seg[:, None] == image_iota[None, :]).astype(jnp.bfloat16)
    per_token = jnp.dot(
        member, modulation.reshape(image_count, 3 * model_width), preferred_element_type=jnp.float32
    )
    shift_rows = per_token[:, :model_width]
    scale_rows = per_token[:, model_width : 2 * model_width]
    gate_rows = per_token[:, 2 * model_width :]
    token_values = tokens.astype(jnp.float32)
    average = jnp.mean(token_values, axis=-1, keepdims=True)
    centred = token_values - average
    inv_std = lax.rsqrt(jnp.mean(centred * centred, axis=-1, keepdims=True) + EPS)
    normed = centred * inv_std
    hidden = (normed * (1.0 + scale_rows) + shift_rows).astype(jnp.bfloat16)
    w_flat = w_qkv.reshape(model_width, 3 * local_cols)
    qkv_rows = jnp.dot(hidden, w_flat, preferred_element_type=jnp.float32).astype(jnp.bfloat16)
    d_mixed = (cotangent.astype(jnp.float32) * gate_rows).astype(jnp.bfloat16)
    d_attn = lax.dot_general(
        d_mixed, w_out, (((1,), (1,)), ((), ())), preferred_element_type=jnp.float32
    ).astype(jnp.bfloat16)
    key_values = qkv_rows[:, local_cols:]
    kv_width = key_values.shape[1]
    offsets = list(range(1, reach_blocks + 1)) + list(range(-reach_blocks, 0))
    dp_count = lax.axis_size("dp")
    quads = [[4 * i + j for j in range(4)] for i in range(dp_count // 4)]
    quad = lax.all_gather(key_values, "dp", axis_index_groups=quads, tiled=True)
    half = 2 * tok_rows
    window16 = jnp.concatenate(
        [
            passed_along(quad[half:], "dp", 8),
            passed_along(quad, "dp", 4),
            quad,
            passed_along(quad, "dp", -4),
            passed_along(quad[:half], "dp", -8),
        ],
        axis=0,
    )
    place = lax.rem(lax.axis_index("dp"), 4)
    window = lax.dynamic_slice_in_dim(window16, place * tok_rows, window_rows, 0)
    kv_width = key_values.shape[1]
    query_heads = (
        qkv_rows[:, :local_cols]
        .astype(jnp.float32)
        .reshape(tok_rows, head_count, head_dim)
        .transpose(1, 0, 2)
    )
    grad_heads = (
        d_attn.astype(jnp.float32).reshape(tok_rows, head_count, head_dim).transpose(1, 0, 2)
    )
    kv_heads = (
        window.astype(jnp.float32)
        .reshape(window_rows, 2, head_count, head_dim)
        .transpose(1, 2, 0, 3)
    )
    attend_width = functools.partial(
        window_attend, query_heads, kv_heads, grad_heads, qk_gain, key_mask, reach_blocks, tok_rows
    )
    attn_heads, query_grad_heads, kv_grad = attend_width(reach_blocks)
    attn_rows = attn_heads.transpose(1, 0, 2).reshape(tok_rows, local_cols)
    query_grad = query_grad_heads.transpose(1, 0, 2).reshape(tok_rows, local_cols)
    grad_blocks = kv_grad.transpose(2, 0, 1, 3).reshape(2 * reach_blocks + 1, tok_rows, kv_width)
    own_grad = grad_blocks[reach_blocks]
    for offset in offsets:
        own_grad = own_grad + passed_along(grad_blocks[reach_blocks - offset], "dp", -offset)
    grad_rows = jnp.concatenate([query_grad, own_grad.astype(jnp.bfloat16)], axis=1)
    def head_sum(values):
        shares = values.reshape(head_devices, share_rows, model_width)
        shares = lax.all_to_all(shares, "head", 0, 0)
        return jnp.sum(shares.astype(jnp.float32), axis=0)

    mixed_rows = head_sum(
        jnp.dot(attn_rows, w_out, preferred_element_type=jnp.float32).astype(jnp.bfloat16)
    )

    def own_rows(values):
        return lax.dynamic_slice_in_dim(values, first_row, share_rows, 0)

    layer_out = (own_rows(token_values) + own_rows(gate_rows) * mixed_rows).astype(jnp.bfloat16)
    d_hidden = head_sum(
        lax.dot_general(
            grad_rows, w_flat, (((1,), (1,)), ((), ())), preferred_element_type=jnp.float32
        ).astype(jnp.bfloat16)
    )
    d_normed = d_hidden * (1.0 + own_rows(scale_rows))
    own_normed = own_rows(normed)
    input_grad = own_rows(cotangent).astype(jnp.float32) + own_rows(inv_std) * (
        d_normed
        - jnp.mean(d_normed, axis=-1, keepdims=True)
        - own_normed * jnp.mean(d_normed * own_normed, axis=-1, keepdims=True)
    )
    return (layer_out, input_grad.astype(jnp.bfloat16))


def solution(mesh):
    in_specs = (P("dp", None), P("dp", None), P(None, None, "head"), P("head", None), P(), P(), P())
    out_specs = (P(("dp", "head"), None), P(("dp", "head"), None))
    return jax.shard_map(
        per_device, mesh=mesh, in_specs=in_specs, out_specs=out_specs, check_vma=False
    )
```

```python
import functools
import math

import jax
import jax.numpy as jnp
from jax import lax
from jax.experimental import pallas as pl
from jax.experimental.pallas import tpu as pltpu
from jax.sharding import PartitionSpec as P

REACH = 6
EPS = 1e-06
SAME_IMAGE = 512.0
F32 = jnp.float32
BF16 = jnp.bfloat16
VMEM_LIMIT = 56 * 1024 * 1024


def rows_dot(a, b):
    return lax.dot_general(a, b, (((1,), (1,)), ((), ())), preferred_element_type=F32)


def attend_kernel(
    span_ref, bounds_ref, gains_ref, raw_ref, *refs, pair_rows, pieces, head_dim
):
    piece_refs = refs[:pieces]
    out_ref, qx_ref, kx_ref, vx_ref, dx_ref, dk_ref, dv_ref = refs[pieces:]
    own = pieces // 2
    lane = lax.broadcasted_iota(jnp.int32, (pair_rows, 128), 1)
    row = lax.broadcasted_iota(jnp.int32, (pair_rows, 128), 0)
    starts = bounds_ref[0:1, :]
    ends = bounds_ref[1:2, :]
    low = lane < head_dim
    for w in range(pieces):
        at = pl.ds(w * pair_rows, pair_rows)
        place = row + w * pair_rows
        same = ((place >= starts) & (place < ends)).astype(F32)
        first = piece_refs[w][:, 0:128].astype(F32)
        second = piece_refs[w][:, 128:256].astype(F32)
        qx_ref[at, :] = jnp.where(low, first * (1.0 / math.sqrt(head_dim)), same * SAME_IMAGE).astype(BF16)
        kx_ref[at, :] = jnp.where(low, second, same).astype(BF16)
        vx_ref[at, :] = jnp.where(low, 0.0, first).astype(BF16)
        dx_ref[at, :] = second.astype(BF16)
    own_rows = pl.ds(own * pair_rows, pair_rows)

    def block_parts(q_block, d_block):
        scores = rows_dot(kx_ref[...], q_block)
        d_probs = rows_dot(vx_ref[...], d_block).astype(BF16).astype(F32)
        highest = jnp.max(scores, axis=0, keepdims=True)
        weights = jnp.exp(scores - highest)
        scale = 1.0 / jnp.sum(weights, axis=0, keepdims=True)
        mean_grad = jnp.sum(weights * d_probs, axis=0, keepdims=True) * scale
        return weights, d_probs, scale, mean_grad

    q_own = qx_ref[own_rows, :]
    d_own = dx_ref[own_rows, :]
    weights, d_probs, scale, mean_grad = block_parts(q_own, d_own)
    probs = weights * scale
    d_scores = (probs * (d_probs - mean_grad)).astype(BF16)
    probs = probs.astype(BF16)
    near = slice(own * pair_rows, (own + 1) * pair_rows)
    dk_ref[...] = jnp.dot(d_scores[near], q_own, preferred_element_type=F32)
    dv_ref[...] = jnp.dot(probs[near], d_own, preferred_element_type=F32)
    contract_rows = (((0,), (0,)), ((), ()))
    result = lax.dot_general(probs, vx_ref[...], contract_rows, preferred_element_type=F32)
    dq_norm = lax.dot_general(d_scores, kx_ref[...], contract_rows, preferred_element_type=F32)

    def one_block(step, carry):
        block = step + jnp.where(step >= own, 1, 0)
        begin = block * pair_rows

        @pl.when((begin < span_ref[1]) & (begin + pair_rows > span_ref[0]))
        def _():
            at = pl.ds(pl.multiple_of(begin, pair_rows), pair_rows)
            q_block = qx_ref[at, :]
            d_block = dx_ref[at, :]
            weights, d_probs, scale, mean_grad = block_parts(q_block, d_block)
            probs = weights[near] * scale
            d_scores = (probs * (d_probs[near] - mean_grad)).astype(BF16)
            dk_ref[...] += jnp.dot(d_scores, q_block, preferred_element_type=F32)
            dv_ref[...] += jnp.dot(probs.astype(BF16), d_block, preferred_element_type=F32)

        return carry

    lax.fori_loop(0, pieces - 1, one_block, 0)

    def lower_sum(values):
        return jnp.sum(jnp.where(low, values, 0.0), axis=-1, keepdims=True)

    def norm_grad(raw, gain, d_norm):
        inverse = lax.rsqrt(lower_sum(raw * raw) * (1.0 / head_dim) + EPS)
        scaled = d_norm.astype(BF16).astype(F32) * gain
        inner = lower_sum(raw * scaled) * (1.0 / head_dim)
        return inverse * scaled - raw * (inverse * inverse * inverse * inner)

    raw_q = raw_ref[...].astype(F32)
    raw_k = pltpu.roll(raw_q, head_dim, 1)
    d_q = norm_grad(raw_q, gains_ref[0:1, :], dq_norm * (1.0 / math.sqrt(head_dim)))
    d_k = norm_grad(raw_k, gains_ref[1:2, :], dk_ref[...])
    out_ref[:, 0:128] = jnp.where(low, d_q, result).astype(BF16)
    out_ref[:, 128:256] = jnp.where(low, d_k, dv_ref[...]).astype(BF16)


def attend_pair(span, bounds, gains, raw, window):
    pieces = len(window)
    pair_rows = raw.shape[0]
    head_dim = raw.shape[1] // 2
    rows = pieces * pair_rows
    vmem = pl.BlockSpec(memory_space=pltpu.VMEM)
    return pl.pallas_call(
        functools.partial(
            attend_kernel, pair_rows=pair_rows, pieces=pieces, head_dim=head_dim
        ),
        out_shape=jax.ShapeDtypeStruct((pair_rows, 256), BF16),
        in_specs=[pl.BlockSpec(memory_space=pltpu.SMEM)] + [vmem] * (3 + pieces),
        out_specs=vmem,
        scratch_shapes=[pltpu.VMEM((rows, 128), BF16)] * 4
        + [pltpu.VMEM((pair_rows, 128), F32)] * 2,
        compiler_params=pltpu.CompilerParams(vmem_limit_bytes=VMEM_LIMIT),
    )(span, bounds, gains, raw, *window)


def project_kernel(parity_ref, kept_ref, swapped_ref, w_out_ref, w_qkv_ref, out_ref):
    rows = swapped_ref.shape[0]
    width = w_out_ref.shape[1]
    first = parity_ref[0] == 0
    lane = lax.broadcasted_iota(jnp.int32, (rows, 128), 1)
    low = lane < 64
    kept = kept_ref[pl.ds(pl.multiple_of(parity_ref[0] * rows, rows), rows), :].astype(F32)
    swapped = swapped_ref[...].astype(F32)
    head0 = jnp.where(first, kept, swapped)
    head1 = jnp.where(first, swapped, kept)
    a0, a1 = head0[:, 0:128], head1[:, 0:128]
    b0, b1 = head0[:, 128:256], head1[:, 128:256]
    d_q = jnp.where(low, a0, pltpu.roll(a1, 64, 1)).astype(BF16)
    attn = jnp.where(low, pltpu.roll(a0, 64, 1), a1).astype(BF16)
    d_k = jnp.where(low, b0, pltpu.roll(b1, 64, 1)).astype(BF16)
    d_v = jnp.where(low, pltpu.roll(b0, 64, 1), b1).astype(BF16)
    mixed = jnp.dot(attn, w_out_ref[...], preferred_element_type=F32)
    out_ref[:, 0:width] = mixed.astype(BF16)
    grads = jnp.concatenate([d_q, d_k, d_v], axis=1)
    out_ref[:, width:] = rows_dot(grads, w_qkv_ref[...]).astype(BF16)


def project(parity, kept, swapped, w_out, w_flat):
    vmem = pl.BlockSpec(memory_space=pltpu.VMEM)
    return pl.pallas_call(
        project_kernel,
        out_shape=jax.ShapeDtypeStruct((swapped.shape[0], 2 * w_out.shape[1]), BF16),
        in_specs=[pl.BlockSpec(memory_space=pltpu.SMEM)] + [vmem] * 4,
        out_specs=vmem,
        compiler_params=pltpu.CompilerParams(vmem_limit_bytes=VMEM_LIMIT),
    )(parity, kept, swapped, w_out, w_flat)


def moved(x, by):
    count = lax.axis_size("dp")
    return lax.ppermute(x, "dp", [(i, (i + by) % count) for i in range(count)])


def swapped_in_pair(x):
    count = lax.axis_size("dp")
    return lax.ppermute(x, "dp", [(i, i ^ 1) for i in range(count)])


def per_device(tokens, cotangent, w_qkv, w_out, qk_gain, modulation, image_counts):
    tok_rows, model_width = tokens.shape
    local_cols = w_out.shape[0]
    head_dim = qk_gain.shape[1]
    image_count = image_counts.shape[0]
    head_devices = lax.axis_size("head")
    share_rows = tok_rows // head_devices
    first_row = lax.axis_index("head") * share_rows
    block = lax.axis_index("dp")
    parity = lax.rem(block, 2)
    even = parity == 0
    pair_rows = 2 * tok_rows
    reach_pairs = REACH // 2
    first_global = block * tok_rows
    pair_start = (block - parity) * tok_rows
    image_ends = jnp.cumsum(image_counts)
    starts = image_ends - image_counts
    positions = first_global + jnp.arange(tok_rows, dtype=jnp.int32)
    member = (
        (positions[:, None] >= starts[None, :]) & (positions[:, None] < image_ends[None, :])
    ).astype(BF16)
    per_token = jnp.dot(
        member, modulation.reshape(image_count, 3 * model_width), preferred_element_type=F32
    )
    shift_rows = per_token[:, :model_width]
    scale_rows = per_token[:, model_width : 2 * model_width]
    gate_rows = per_token[:, 2 * model_width :]
    token_values = tokens.astype(F32)
    average = jnp.mean(token_values, axis=-1, keepdims=True)
    centred = token_values - average
    inv_std = lax.rsqrt(jnp.mean(centred * centred, axis=-1, keepdims=True) + EPS)
    normed = centred * inv_std
    hidden = (normed * (1.0 + scale_rows) + shift_rows).astype(BF16)
    w_flat = w_qkv.reshape(model_width, 3 * local_cols)
    qkv_rows = jnp.dot(hidden, w_flat, preferred_element_type=F32).astype(BF16)
    d_mixed = (cotangent.astype(F32) * gate_rows).astype(BF16)
    d_attn = rows_dot(d_mixed, w_out).astype(BF16)

    def head_norm(rows, gain):
        values = rows.astype(F32)
        inverse = lax.rsqrt(jnp.mean(values * values, axis=-1, keepdims=True) + EPS)
        return (values * inverse * gain).astype(BF16)

    def payload(head):
        cols = slice(head * head_dim, (head + 1) * head_dim)
        q = qkv_rows[:, :local_cols][:, cols]
        k = qkv_rows[:, local_cols : 2 * local_cols][:, cols]
        v = qkv_rows[:, 2 * local_cols :][:, cols]
        return jnp.concatenate(
            [head_norm(q, qk_gain[0]), v, head_norm(k, qk_gain[1]), d_attn[:, cols], q, k], axis=1
        )

    payload0, payload1 = payload(0), payload(1)
    kept = jnp.where(even, payload0, payload1)
    swapped = swapped_in_pair(jnp.where(even, payload1, payload0))
    pair = jnp.concatenate(
        [jnp.where(even, kept, swapped), jnp.where(even, swapped, kept)], axis=0
    )
    sent = pair[:, : 4 * head_dim]
    raw = pair[:, 4 * head_dim :]
    window = [
        sent if shift == 0 else moved(sent, -2 * shift)
        for shift in range(-reach_pairs, reach_pairs + 1)
    ]
    window_start = pair_start - reach_pairs * pair_rows
    rel_starts = starts - window_start
    rel_ends = image_ends - window_start
    own_first = reach_pairs * pair_rows
    own_last = own_first + pair_rows - 1
    span = jnp.stack(
        [
            jnp.max(jnp.where(rel_starts <= own_first, rel_starts, -TOKENS_FAR)),
            jnp.min(jnp.where(rel_ends > own_last, rel_ends, TOKENS_FAR)),
        ]
    )
    bounds = jnp.zeros((8, 128), jnp.int32)
    bounds = bounds.at[0, head_dim : head_dim + image_count].set(rel_starts)
    bounds = bounds.at[1, head_dim : head_dim + image_count].set(rel_ends)
    gains = jnp.zeros((8, 128), F32).at[0:2, :head_dim].set(qk_gain)
    pair_out = attend_pair(span, bounds, gains, raw, window)
    back = swapped_in_pair(
        lax.dynamic_slice_in_dim(pair_out, (1 - parity) * tok_rows, tok_rows, 0)
    )
    partial = project(parity.reshape(1), pair_out, back, w_out, w_flat)
    shares = lax.all_to_all(
        partial.reshape(head_devices, share_rows, 2 * model_width), "head", 0, 0
    )
    sums = jnp.sum(shares.astype(F32), axis=0)
    mixed_rows = sums[:, :model_width]
    d_hidden = sums[:, model_width:]

    def own_rows(values):
        return lax.dynamic_slice_in_dim(values, first_row, share_rows, 0)

    layer_out = (own_rows(token_values) + own_rows(gate_rows) * mixed_rows).astype(BF16)
    d_normed = d_hidden * (1.0 + own_rows(scale_rows))
    own_normed = own_rows(normed)
    input_grad = own_rows(cotangent).astype(F32) + own_rows(inv_std) * (
        d_normed
        - jnp.mean(d_normed, axis=-1, keepdims=True)
        - own_normed * jnp.mean(d_normed * own_normed, axis=-1, keepdims=True)
    )
    return (layer_out, input_grad.astype(BF16))


TOKENS_FAR = 1 << 20


def solution(mesh):
    in_specs = (P("dp", None), P("dp", None), P(None, None, "head"), P("head", None), P(), P(), P())
    out_specs = (P(("dp", "head"), None), P(("dp", "head"), None))
    return jax.shard_map(
        per_device, mesh=mesh, in_specs=in_specs, out_specs=out_specs, check_vma=False
    )
```

```python
import functools
import math

import jax
import jax.numpy as jnp
from jax import lax
from jax.experimental import pallas as pl
from jax.experimental.pallas import tpu as pltpu
from jax.sharding import PartitionSpec as P

EPS = 1e-06
SAME_IMAGE = 512.0
FAR = 1 << 20
LANES = 128
HEAD = 64
F32 = jnp.float32
BF16 = jnp.bfloat16
VMEM_LIMIT = 56 * 1024 * 1024
VMEM = pl.BlockSpec(memory_space=pltpu.VMEM)
SMEM = pl.BlockSpec(memory_space=pltpu.SMEM)


def rows_dot(a, b):
    return lax.dot_general(a, b, (((1,), (1,)), ((), ())), preferred_element_type=F32)


def image_bounds(counts_ref, first_lane):
    lane = lax.broadcasted_iota(jnp.int32, (1, LANES), 1)
    starts = jnp.zeros((1, LANES), jnp.int32)
    ends = jnp.zeros((1, LANES), jnp.int32)
    total = jnp.int32(0)
    for image in range(counts_ref.shape[0]):
        here = lane == first_lane + image
        starts = jnp.where(here, total, starts)
        total = total + counts_ref[image]
        ends = jnp.where(here, total, ends)
    return starts, ends


def modulation_rows(counts_ref, modulation_ref, first, rows):
    starts, ends = image_bounds(counts_ref, 0)
    place = first + lax.broadcasted_iota(jnp.int32, (rows, LANES), 0)
    member = ((place >= starts) & (place < ends)).astype(F32).astype(BF16)
    per_token = jnp.dot(
        member[:, : modulation_ref.shape[0]], modulation_ref[...], preferred_element_type=F32
    )
    width = per_token.shape[1] // 3
    return per_token[:, :width], per_token[:, width : 2 * width], per_token[:, 2 * width :]


def layer_norm(values):
    average = jnp.mean(values, axis=-1, keepdims=True)
    centred = values - average
    inv_std = lax.rsqrt(jnp.mean(centred * centred, axis=-1, keepdims=True) + EPS)
    return centred * inv_std, inv_std


def enter_kernel(
    counts_ref, tokens_ref, cotangent_ref, w_qkv_ref, w_out_ref, modulation_ref, out_ref
):
    rows = tokens_ref.shape[0]
    first = lax.axis_index("dp") * rows
    shift, scale, gate = modulation_rows(counts_ref, modulation_ref, first, rows)
    normed, _ = layer_norm(tokens_ref[...].astype(F32))
    hidden = (normed * (1.0 + scale) + shift).astype(BF16)
    qkv = jnp.dot(hidden, w_qkv_ref[...], preferred_element_type=F32)
    d_mixed = (cotangent_ref[...].astype(F32) * gate).astype(BF16)
    d_attn = rows_dot(d_mixed, w_out_ref[...])
    low = lax.broadcasted_iota(jnp.int32, (rows, LANES), 1) < HEAD
    q, k, v = qkv[:, :LANES], qkv[:, LANES : 2 * LANES], qkv[:, 2 * LANES :]

    def beside(left, right):
        return jnp.where(low, left, right).astype(BF16)

    q_v = (beside(q, pltpu.roll(v, HEAD, 1)), beside(pltpu.roll(q, HEAD, 1), v))
    k_d = (beside(k, pltpu.roll(d_attn, HEAD, 1)), beside(pltpu.roll(k, HEAD, 1), d_attn))
    for place in range(out_ref.shape[0]):
        out_ref[place, :, 0:LANES] = q_v[place % 2]
        out_ref[place, :, LANES:] = k_d[place % 2]


def enter(counts, tokens, cotangent, w_flat, w_out, modulation, quad):
    return pl.pallas_call(
        enter_kernel,
        out_shape=jax.ShapeDtypeStruct((quad, tokens.shape[0], 2 * LANES), BF16),
        in_specs=[SMEM] + [VMEM] * 5,
        out_specs=VMEM,
        compiler_params=pltpu.CompilerParams(vmem_limit_bytes=VMEM_LIMIT),
    )(counts, tokens, cotangent, w_flat, w_out, modulation)


def attend_kernel(
    counts_ref,
    gains_ref,
    before_ref,
    quad_ref,
    after_ref,
    far_ref,
    kept_ref,
    sent_ref,
    qx_ref,
    kx_ref,
    vx_ref,
    dx_ref,
    dk_ref,
    dv_ref,
    done_ref,
):
    pair_rows = far_ref.shape[0]
    quad_rows = quad_ref.shape[0]
    tok_rows = pair_rows // 2
    own = 3
    slots = 7
    block = lax.axis_index("dp")
    parity = lax.rem(block, 2)
    half = lax.rem(block, 4) // 2
    origin = (block // 4 - 1) * quad_rows
    own_at = quad_rows + half * pair_rows
    other_at = quad_rows + (1 - half) * pair_rows
    far_at = jnp.where(half == 0, -pair_rows, 3 * quad_rows)
    places = [
        jnp.int32(0),
        jnp.int32(pair_rows),
        other_at,
        own_at,
        jnp.int32(2 * quad_rows),
        jnp.int32(2 * quad_rows + pair_rows),
        far_at,
    ]
    sources = [
        before_ref.at[0:pair_rows],
        before_ref.at[pair_rows:quad_rows],
        quad_ref.at[pl.ds(pl.multiple_of((1 - half) * pair_rows, pair_rows), pair_rows)],
        quad_ref.at[pl.ds(pl.multiple_of(half * pair_rows, pair_rows), pair_rows)],
        after_ref.at[0:pair_rows],
        after_ref.at[pair_rows:quad_rows],
        far_ref,
    ]
    lane = lax.broadcasted_iota(jnp.int32, (pair_rows, LANES), 1)
    row = lax.broadcasted_iota(jnp.int32, (pair_rows, LANES), 0)
    low = lane < HEAD
    starts, ends = image_bounds(counts_ref, HEAD)
    starts = starts - origin
    ends = ends - origin
    inv_root = 1.0 / math.sqrt(HEAD)

    def lower_mean(values):
        return jnp.sum(jnp.where(low, values, 0.0), axis=-1, keepdims=True) * (1.0 / HEAD)

    def normed(raw, gain):
        return (raw * lax.rsqrt(lower_mean(raw * raw) + EPS) * gain).astype(BF16).astype(F32)

    q_gain, k_gain = gains_ref[0:1, :], gains_ref[1:2, :]
    for slot in range(slots):
        at = pl.ds(slot * pair_rows, pair_rows)
        place = row + places[slot]
        same = ((place >= starts) & (place < ends)).astype(F32)
        first = sources[slot][:, 0:LANES].astype(F32)
        second = sources[slot][:, LANES:].astype(F32)
        qx_ref[at, :] = jnp.where(low, normed(first, q_gain) * inv_root, same * SAME_IMAGE).astype(BF16)
        kx_ref[at, :] = jnp.where(low, normed(second, k_gain), same).astype(BF16)
        vx_ref[at, :] = jnp.where(low, 0.0, first).astype(BF16)
        dx_ref[at, :] = second.astype(BF16)

    def block_parts(q_block, d_block):
        scores = rows_dot(kx_ref[...], q_block)
        d_probs = rows_dot(vx_ref[...], d_block).astype(BF16).astype(F32)
        highest = jnp.max(scores, axis=0, keepdims=True)
        weights = jnp.exp(scores - highest)
        scale = 1.0 / jnp.sum(weights, axis=0, keepdims=True)
        mean_grad = jnp.sum(weights * d_probs, axis=0, keepdims=True) * scale
        return weights, d_probs, scale, mean_grad

    own_rows = pl.ds(own * pair_rows, pair_rows)
    near = slice(own * pair_rows, (own + 1) * pair_rows)
    q_own = qx_ref[own_rows, :]
    d_own = dx_ref[own_rows, :]
    weights, d_probs, scale, mean_grad = block_parts(q_own, d_own)
    probs = weights * scale
    d_scores = (probs * (d_probs - mean_grad)).astype(BF16)
    probs = probs.astype(BF16)
    dk_ref[...] = jnp.dot(d_scores[near], q_own, preferred_element_type=F32)
    dv_ref[...] = jnp.dot(probs[near], d_own, preferred_element_type=F32)
    contract_rows = (((0,), (0,)), ((), ()))
    result = lax.dot_general(probs, vx_ref[...], contract_rows, preferred_element_type=F32)
    dq_norm = lax.dot_general(d_scores, kx_ref[...], contract_rows, preferred_element_type=F32)

    span_from = jnp.int32(-FAR)
    span_to = jnp.int32(FAR)
    total = -origin
    for image in range(counts_ref.shape[0]):
        span_from = jnp.where(total <= own_at, total, span_from)
        total = total + counts_ref[image]
        span_to = jnp.where((total >= own_at + pair_rows) & (span_to == FAR), total, span_to)

    def one_block(step, carry):
        slot = step + jnp.where(step >= own, 1, 0)
        begin = jnp.where(slot == 2, other_at, jnp.where(slot == slots - 1, far_at, 0))
        begin = jnp.where(slot < 2, slot * pair_rows, begin)
        begin = jnp.where((slot == 4) | (slot == 5), slot * pair_rows, begin)

        @pl.when((begin < span_to) & (begin + pair_rows > span_from))
        def _():
            at = pl.ds(pl.multiple_of(slot * pair_rows, pair_rows), pair_rows)
            q_block = qx_ref[at, :]
            d_block = dx_ref[at, :]
            weights, d_probs, scale, mean_grad = block_parts(q_block, d_block)
            probs = weights[near] * scale
            d_scores = (probs * (d_probs[near] - mean_grad)).astype(BF16)
            dk_ref[...] += jnp.dot(d_scores, q_block, preferred_element_type=F32)
            dv_ref[...] += jnp.dot(probs.astype(BF16), d_block, preferred_element_type=F32)

        return carry

    lax.fori_loop(0, slots - 1, one_block, 0)

    def norm_grad(raw, gain, d_norm):
        inverse = lax.rsqrt(lower_mean(raw * raw) + EPS)
        scaled = d_norm.astype(BF16).astype(F32) * gain
        inner = lower_mean(raw * scaled)
        return inverse * scaled - raw * (inverse * inverse * inverse * inner)

    raw_q = sources[own][:, 0:LANES].astype(F32)
    raw_k = sources[own][:, LANES:].astype(F32)
    d_q = norm_grad(raw_q, q_gain, dq_norm * inv_root)
    d_k = norm_grad(raw_k, k_gain, dk_ref[...])
    done_ref[:, 0:LANES] = jnp.where(low, d_q, result).astype(BF16)
    done_ref[:, LANES:] = jnp.where(low, d_k, dv_ref[...]).astype(BF16)
    kept_ref[...] = done_ref[pl.ds(pl.multiple_of(parity * tok_rows, tok_rows), tok_rows), :]
    sent_ref[...] = done_ref[pl.ds(pl.multiple_of((1 - parity) * tok_rows, tok_rows), tok_rows), :]


def attend_pair(counts, gains, before, quad, after, far):
    pair_rows = far.shape[0]
    rows = 7 * pair_rows
    half_out = jax.ShapeDtypeStruct((pair_rows // 2, 2 * LANES), BF16)
    return pl.pallas_call(
        attend_kernel,
        out_shape=(half_out, half_out),
        in_specs=[SMEM] + [VMEM] * 5,
        out_specs=(VMEM, VMEM),
        scratch_shapes=[pltpu.VMEM((rows, LANES), BF16)] * 4
        + [pltpu.VMEM((pair_rows, LANES), F32)] * 2
        + [pltpu.VMEM((pair_rows, 2 * LANES), BF16)],
        compiler_params=pltpu.CompilerParams(vmem_limit_bytes=VMEM_LIMIT),
    )(counts, gains, before, quad, after, far)


def project_kernel(kept_ref, swapped_ref, w_out_ref, w_qkv_ref, out_ref):
    rows = kept_ref.shape[0]
    width = w_out_ref.shape[1]
    first = lax.rem(lax.axis_index("dp"), 2) == 0
    low = lax.broadcasted_iota(jnp.int32, (rows, LANES), 1) < HEAD
    kept = kept_ref[...].astype(F32)
    swapped = swapped_ref[...].astype(F32)
    head0 = jnp.where(first, kept, swapped)
    head1 = jnp.where(first, swapped, kept)
    a0, a1 = head0[:, :LANES], head1[:, :LANES]
    b0, b1 = head0[:, LANES:], head1[:, LANES:]
    d_q = jnp.where(low, a0, pltpu.roll(a1, HEAD, 1)).astype(BF16)
    attn = jnp.where(low, pltpu.roll(a0, HEAD, 1), a1).astype(BF16)
    d_k = jnp.where(low, b0, pltpu.roll(b1, HEAD, 1)).astype(BF16)
    d_v = jnp.where(low, pltpu.roll(b0, HEAD, 1), b1).astype(BF16)
    mixed = jnp.dot(attn, w_out_ref[...], preferred_element_type=F32)
    out_ref[:, :width] = mixed.astype(BF16)
    grads = jnp.concatenate([d_q, d_k, d_v], axis=1)
    out_ref[:, width:] = rows_dot(grads, w_qkv_ref[...]).astype(BF16)


def project(kept, swapped, w_out, w_flat):
    return pl.pallas_call(
        project_kernel,
        out_shape=jax.ShapeDtypeStruct((kept.shape[0], 2 * w_out.shape[1]), BF16),
        in_specs=[VMEM] * 4,
        out_specs=VMEM,
        compiler_params=pltpu.CompilerParams(vmem_limit_bytes=VMEM_LIMIT),
    )(kept, swapped, w_out, w_flat)


def leave_kernel(
    counts_ref, tokens_ref, cotangent_ref, modulation_ref, shares_ref, layer_ref, grad_ref
):
    rows = layer_ref.shape[0]
    width = layer_ref.shape[1]
    first_row = lax.axis_index("head") * rows
    first = lax.axis_index("dp") * tokens_ref.shape[0] + first_row
    _, scale, gate = modulation_rows(counts_ref, modulation_ref, first, rows)
    at = pl.ds(pl.multiple_of(first_row, rows), rows)
    values = tokens_ref[at, :].astype(F32)
    normed, inv_std = layer_norm(values)
    sums = shares_ref[0].astype(F32)
    for share in range(1, shares_ref.shape[0]):
        sums = sums + shares_ref[share].astype(F32)
    layer_ref[...] = (values + gate * sums[:, :width]).astype(BF16)
    d_normed = sums[:, width:] * (1.0 + scale)
    input_grad = cotangent_ref[at, :].astype(F32) + inv_std * (
        d_normed
        - jnp.mean(d_normed, axis=-1, keepdims=True)
        - normed * jnp.mean(d_normed * normed, axis=-1, keepdims=True)
    )
    grad_ref[...] = input_grad.astype(BF16)


def leave(counts, tokens, cotangent, modulation, shares):
    out = jax.ShapeDtypeStruct((shares.shape[1], tokens.shape[1]), BF16)
    return pl.pallas_call(
        leave_kernel,
        out_shape=(out, out),
        in_specs=[SMEM] + [VMEM] * 4,
        out_specs=(VMEM, VMEM),
        compiler_params=pltpu.CompilerParams(vmem_limit_bytes=VMEM_LIMIT),
    )(counts, tokens, cotangent, modulation, shares)


def per_device(quad, tokens, cotangent, w_qkv, w_out, qk_gain, modulation, image_counts):
    tok_rows, model_width = tokens.shape
    head_devices = lax.axis_size("head")
    dp_count = lax.axis_size("dp")
    share_rows = tok_rows // head_devices
    pair_rows = 2 * tok_rows
    w_flat = w_qkv.reshape(model_width, 3 * w_out.shape[0])
    mod_flat = modulation.reshape(modulation.shape[0], 3 * model_width)
    gains = jnp.pad(qk_gain, ((0, 6), (0, LANES - HEAD)))

    def moved(x, target):
        return lax.ppermute(x, "dp", [(i, target(i) % dp_count) for i in range(dp_count)])

    heads = enter(image_counts, tokens, cotangent, w_flat, w_out, mod_flat, quad)
    quads = [[quad * i + j for j in range(quad)] for i in range(dp_count // quad)]
    mine = lax.all_to_all(heads, "dp", 0, 0, axis_index_groups=quads)
    mine = mine.reshape(quad * tok_rows, 2 * LANES)
    before = moved(mine, lambda i: i + quad)
    after = moved(mine, lambda i: i - quad)
    half = lax.rem(lax.axis_index("dp"), quad) // 2
    far_half = jnp.where(half == 0, mine[pair_rows:], mine[:pair_rows])
    far = moved(far_half, lambda i: i + 2 * quad if i % quad < 2 else i - 2 * quad)
    kept, sent = attend_pair(image_counts, gains, before, mine, after, far)
    swapped = moved(sent, lambda i: i ^ 1)
    partial = project(kept, swapped, w_out, w_flat)
    shares = lax.all_to_all(
        partial.reshape(head_devices, share_rows, 2 * model_width), "head", 0, 0
    )
    return leave(image_counts, tokens, cotangent, mod_flat, shares)


def solution(mesh):
    in_specs = (P("dp", None), P("dp", None), P(None, None, "head"), P("head", None), P(), P(), P())
    out_specs = (P(("dp", "head"), None), P(("dp", "head"), None))
    return jax.shard_map(
        functools.partial(per_device, 4),
        mesh=mesh,
        in_specs=in_specs,
        out_specs=out_specs,
        check_vma=False,
    )
```

```python
import math

import jax
import jax.numpy as jnp
from jax import lax
from jax.experimental import pallas as pl
from jax.experimental.pallas import tpu as pltpu
from jax.sharding import PartitionSpec as P

EPS = 1e-06
SAME_IMAGE = 512.0
LANES = 128
HEAD = 64
F32 = jnp.float32
BF16 = jnp.bfloat16
VMEM_LIMIT = 56 * 1024 * 1024
VMEM = pl.BlockSpec(memory_space=pltpu.VMEM)
SMEM = pl.BlockSpec(memory_space=pltpu.SMEM)


def rows_dot(a, b):
    return lax.dot_general(a, b, (((1,), (1,)), ((), ())), preferred_element_type=F32)


def block_index():
    return (lax.axis_index("z") * 2 + lax.axis_index("yh")) * 2 + lax.axis_index("yl")


def image_bounds(counts_ref, first_lane):
    lane = lax.broadcasted_iota(jnp.int32, (1, LANES), 1)
    starts = jnp.zeros((1, LANES), jnp.int32)
    ends = jnp.zeros((1, LANES), jnp.int32)
    total = jnp.int32(0)
    for image in range(counts_ref.shape[0]):
        here = lane == first_lane + image
        starts = jnp.where(here, total, starts)
        total = total + counts_ref[image]
        ends = jnp.where(here, total, ends)
    return starts, ends


def modulation_rows(counts_ref, modulation_ref, first, rows):
    starts, ends = image_bounds(counts_ref, 0)
    place = first + lax.broadcasted_iota(jnp.int32, (rows, LANES), 0)
    member = ((place >= starts) & (place < ends)).astype(F32).astype(BF16)
    per_token = jnp.dot(
        member[:, : modulation_ref.shape[0]], modulation_ref[...], preferred_element_type=F32
    )
    width = per_token.shape[1] // 3
    return per_token[:, :width], per_token[:, width : 2 * width], per_token[:, 2 * width :]


def layer_norm(values):
    average = jnp.mean(values, axis=-1, keepdims=True)
    centred = values - average
    inv_std = lax.rsqrt(jnp.mean(centred * centred, axis=-1, keepdims=True) + EPS)
    return centred * inv_std, inv_std


def enter_kernel(
    counts_ref, tokens_ref, cotangent_ref, w_qkv_ref, w_out_ref, modulation_ref, out_ref
):
    rows = tokens_ref.shape[0]
    first = block_index() * rows
    shift, scale, gate = modulation_rows(counts_ref, modulation_ref, first, rows)
    normed, _ = layer_norm(tokens_ref[...].astype(F32))
    hidden = (normed * (1.0 + scale) + shift).astype(BF16)
    q, k, v = (
        jnp.dot(hidden, w_qkv_ref[part], preferred_element_type=F32) for part in range(3)
    )
    d_mixed = (cotangent_ref[...].astype(F32) * gate).astype(BF16)
    d_attn = rows_dot(d_mixed, w_out_ref[...])
    low = lax.broadcasted_iota(jnp.int32, (rows, LANES), 1) < HEAD

    def beside(left, right):
        return jnp.where(low, left, right).astype(BF16)

    q_v = (beside(q, pltpu.roll(v, HEAD, 1)), beside(pltpu.roll(q, HEAD, 1), v))
    k_d = (beside(k, pltpu.roll(d_attn, HEAD, 1)), beside(pltpu.roll(k, HEAD, 1), d_attn))
    for place in range(out_ref.shape[0]):
        out_ref[place, :, 0:LANES] = q_v[place % 2]
        out_ref[place, :, LANES:] = k_d[place % 2]


def enter(counts, tokens, cotangent, w_parts, w_out, modulation, quad):
    return pl.pallas_call(
        enter_kernel,
        out_shape=jax.ShapeDtypeStruct((quad, tokens.shape[0], 2 * LANES), BF16),
        in_specs=[SMEM] + [VMEM] * 5,
        out_specs=VMEM,
        compiler_params=pltpu.CompilerParams(vmem_limit_bytes=VMEM_LIMIT),
    )(counts, tokens, cotangent, w_parts, w_out, modulation)


def attend_kernel(
    counts_ref,
    gains_ref,
    before_ref,
    quad_ref,
    after_ref,
    far_ref,
    out_ref,
    qx_ref,
    kx_ref,
    vx_ref,
    dx_ref,
    s_ref,
    p_ref,
    dk_ref,
    dv_ref,
    done_ref,
):
    chunk = far_ref.shape[0]
    own = 3
    slots = 7
    reach = 4
    half = lax.axis_index("yh")
    origin = (block_index() // 2 - own) * chunk
    own_at = own * chunk
    lane = lax.broadcasted_iota(jnp.int32, (chunk, LANES), 1)
    row = lax.broadcasted_iota(jnp.int32, (chunk, LANES), 0)
    low = lane < HEAD
    starts, ends = image_bounds(counts_ref, HEAD)
    starts = starts - origin
    ends = ends - origin
    inv_root = 1.0 / math.sqrt(HEAD)

    def lower_mean(values):
        return jnp.sum(jnp.where(low, values, 0.0), axis=-1, keepdims=True) * (1.0 / HEAD)

    def normed(raw, gain):
        return (raw * lax.rsqrt(lower_mean(raw * raw) + EPS) * gain).astype(BF16).astype(F32)

    q_gain, k_gain = gains_ref[0:1, :], gains_ref[1:2, :]

    def place_chunk(source, slot):
        begin = pl.multiple_of(slot * chunk, chunk)
        at = pl.ds(begin, chunk)
        place = row + begin
        same = ((place >= starts) & (place < ends)).astype(F32)
        first = source[:, 0:LANES].astype(F32)
        second = source[:, LANES:].astype(F32)
        qx_ref[at, :] = jnp.where(low, normed(first, q_gain) * inv_root, same * SAME_IMAGE).astype(BF16)
        kx_ref[at, :] = jnp.where(low, normed(second, k_gain), same).astype(BF16)
        vx_ref[at, :] = jnp.where(low, 0.0, first).astype(BF16)
        dx_ref[at, :] = second.astype(BF16)

    place_chunk(before_ref.at[0:chunk], 1 - half)
    place_chunk(before_ref.at[chunk : 2 * chunk], 2 - half)
    place_chunk(quad_ref.at[0:chunk], 3 - half)
    place_chunk(quad_ref.at[chunk : 2 * chunk], 4 - half)
    place_chunk(after_ref.at[0:chunk], 5 - half)
    place_chunk(after_ref.at[chunk : 2 * chunk], 6 - half)
    place_chunk(far_ref, half * (slots - 1))

    left_from = jnp.int32(0)
    right_to = jnp.int32(slots * chunk)
    total = -origin
    for image in range(counts_ref.shape[0]):
        left_from = jnp.where(total <= own_at, total, left_from)
        ended = total >= own_at + chunk
        total = total + counts_ref[image]
        right_to = jnp.where((total >= own_at + chunk) & jnp.logical_not(ended), total, right_to)
    left_chunk = jnp.clip(left_from // chunk, 0, slots - reach)
    right_chunk = jnp.clip((right_to - 1) // chunk - (reach - 1), 0, slots - reach)

    def block_parts(keys, values, q_block, d_block):
        scores = rows_dot(keys, q_block)
        d_probs = rows_dot(values, d_block).astype(BF16).astype(F32)
        highest = jnp.max(scores, axis=0, keepdims=True)
        weights = jnp.exp(scores - highest)
        scale = 1.0 / jnp.sum(weights, axis=0, keepdims=True)
        mean_grad = jnp.sum(weights * d_probs, axis=0, keepdims=True) * scale
        return weights, d_probs, scale, mean_grad

    near = slice(own_at, own_at + chunk)
    q_own = qx_ref[near, :]
    d_own = dx_ref[near, :]
    weights, d_probs, scale, mean_grad = block_parts(kx_ref[...], vx_ref[...], q_own, d_own)
    probs = weights * scale
    d_scores = (probs * (d_probs - mean_grad)).astype(BF16)
    probs = probs.astype(BF16)
    dk_ref[...] = jnp.dot(d_scores[near], q_own, preferred_element_type=F32)
    dv_ref[...] = jnp.dot(probs[near], d_own, preferred_element_type=F32)
    contract_rows = (((0,), (0,)), ((), ()))
    result = lax.dot_general(probs, vx_ref[...], contract_rows, preferred_element_type=F32)
    dq_norm = lax.dot_general(d_scores, kx_ref[...], contract_rows, preferred_element_type=F32)

    query_lane = lax.broadcasted_iota(jnp.int32, (1, chunk), 1)

    def one_block(step, carry):
        slot = step + jnp.where(step >= own, 1, 0)
        begin = slot * chunk

        @pl.when((begin < right_to) & (begin + chunk > left_from))
        def _():
            at = pl.ds(pl.multiple_of(begin, chunk), chunk)
            key_chunk = jnp.where(slot < own, left_chunk, right_chunk)
            keys_at = pl.ds(pl.multiple_of(key_chunk * chunk, chunk), reach * chunk)
            near_at = pl.ds(pl.multiple_of((own - key_chunk) * chunk, chunk), chunk)
            q_block = qx_ref[at, :]
            d_block = dx_ref[at, :]
            weights, d_probs, scale, mean_grad = block_parts(
                kx_ref[keys_at, :], vx_ref[keys_at, :], q_block, d_block
            )
            s_ref[...] = weights
            p_ref[...] = d_probs
            place = query_lane + begin
            scale = jnp.where((place >= left_from) & (place < right_to), scale, 0.0)
            probs = s_ref[near_at, :] * scale
            d_scores = (probs * (p_ref[near_at, :] - mean_grad)).astype(BF16)
            dk_ref[...] += jnp.dot(d_scores, q_block, preferred_element_type=F32)
            dv_ref[...] += jnp.dot(probs.astype(BF16), d_block, preferred_element_type=F32)

        return carry

    lax.fori_loop(0, slots - 1, one_block, 0)

    def norm_grad(raw, gain, d_norm):
        inverse = lax.rsqrt(lower_mean(raw * raw) + EPS)
        scaled = d_norm.astype(BF16).astype(F32) * gain
        inner = lower_mean(raw * scaled)
        return inverse * scaled - raw * (inverse * inverse * inverse * inner)

    own_in_quad = pl.ds(pl.multiple_of(half * chunk, chunk), chunk)
    raw_q = quad_ref[own_in_quad, 0:LANES].astype(F32)
    raw_k = quad_ref[own_in_quad, LANES:].astype(F32)
    d_q = norm_grad(raw_q, q_gain, dq_norm * inv_root)
    d_k = norm_grad(raw_k, k_gain, dk_ref[...])
    done_ref[:, 0:LANES] = jnp.where(low, d_q, result).astype(BF16)
    done_ref[:, LANES:] = jnp.where(low, d_k, dv_ref[...]).astype(BF16)
    share = 16
    for member in range(out_ref.shape[0]):
        block, core = member // 2, member % 2
        for part in range(out_ref.shape[1] // share):
            begin = (block * 8 + part * 2 + core) * share
            out_ref[member, part * share : (part + 1) * share, :] = done_ref[
                begin : begin + share, :
            ]


def attend_pair(counts, gains, before, quad, after, far):
    chunk = far.shape[0]
    rows = 7 * chunk
    return pl.pallas_call(
        attend_kernel,
        out_shape=jax.ShapeDtypeStruct((4, chunk // 4, 2 * LANES), BF16),
        in_specs=[SMEM] + [VMEM] * 5,
        out_specs=VMEM,
        scratch_shapes=[pltpu.VMEM((rows, LANES), BF16)] * 4
        + [pltpu.VMEM((4 * chunk, chunk), F32)] * 2
        + [pltpu.VMEM((chunk, LANES), F32)] * 2
        + [pltpu.VMEM((chunk, 2 * LANES), BF16)],
        compiler_params=pltpu.CompilerParams(vmem_limit_bytes=VMEM_LIMIT),
    )(counts, gains, before, quad, after, far)


def project_kernel(parts_ref, w_out_ref, w_qkv_ref, w_out_far_ref, w_qkv_far_ref, out_ref):
    rows = parts_ref.shape[1]
    width = w_out_ref.shape[1]
    share = out_ref.shape[1]
    core = lax.axis_index("core")
    low = lax.broadcasted_iota(jnp.int32, (rows, LANES), 1) < HEAD

    def products(which, w_out, w_qkv):
        head0 = parts_ref[which].astype(F32)
        head1 = parts_ref[2 + which].astype(F32)
        a0, a1 = head0[:, :LANES], head1[:, :LANES]
        b0, b1 = head0[:, LANES:], head1[:, LANES:]
        d_q = jnp.where(low, a0, pltpu.roll(a1, HEAD, 1)).astype(BF16)
        attn = jnp.where(low, pltpu.roll(a0, HEAD, 1), a1).astype(BF16)
        d_k = jnp.where(low, b0, pltpu.roll(b1, HEAD, 1)).astype(BF16)
        d_v = jnp.where(low, pltpu.roll(b0, HEAD, 1), b1).astype(BF16)
        mixed = jnp.dot(attn, w_out[...], preferred_element_type=F32)
        d_hidden = rows_dot(d_q, w_qkv[0]) + rows_dot(d_k, w_qkv[1]) + rows_dot(d_v, w_qkv[2])
        return mixed, d_hidden

    mixed, d_hidden = products(core, w_out_ref, w_qkv_ref)
    mixed_far, d_hidden_far = products(1 - core, w_out_far_ref, w_qkv_far_ref)
    mixed = (mixed + mixed_far).astype(BF16)
    d_hidden = (d_hidden + d_hidden_far).astype(BF16)
    for place in range(out_ref.shape[0]):
        at = slice(place * share, (place + 1) * share)
        out_ref[place, :, :width] = mixed[at]
        out_ref[place, :, width:] = d_hidden[at]


def project(parts, w_out, w_parts, w_out_far, w_parts_far, x_count):
    return pl.pallas_call(
        project_kernel,
        out_shape=jax.ShapeDtypeStruct(
            (x_count, parts.shape[1] // x_count, 2 * w_out.shape[1]), BF16
        ),
        in_specs=[VMEM] * 5,
        out_specs=VMEM,
        compiler_params=pltpu.CompilerParams(vmem_limit_bytes=VMEM_LIMIT),
    )(parts, w_out, w_parts, w_out_far, w_parts_far)


def ready_kernel(
    counts_ref,
    tokens_ref,
    cotangent_ref,
    modulation_ref,
    rows_ref,
    factors_ref,
):
    rows = rows_ref.shape[1]
    first_row = (lax.axis_index("x") * 2 + lax.axis_index("core")) * rows
    first = block_index() * tokens_ref.shape[0] + first_row
    _, scale, gate = modulation_rows(counts_ref, modulation_ref, first, rows)
    at = pl.ds(pl.multiple_of(first_row, rows), rows)
    normed, inv_std = layer_norm(tokens_ref[at, :].astype(F32))
    rows_ref[0] = tokens_ref[at, :]
    rows_ref[1] = cotangent_ref[at, :]
    factors_ref[0] = gate
    factors_ref[1] = 1.0 + scale
    factors_ref[2] = normed
    factors_ref[3] = jnp.broadcast_to(inv_std, normed.shape)


def ready(counts, tokens, cotangent, modulation, share):
    width = tokens.shape[1]
    return pl.pallas_call(
        ready_kernel,
        out_shape=(
            jax.ShapeDtypeStruct((2, share, width), BF16),
            jax.ShapeDtypeStruct((4, share, width), F32),
        ),
        in_specs=[SMEM] + [VMEM] * 3,
        out_specs=(VMEM, VMEM),
        compiler_params=pltpu.CompilerParams(vmem_limit_bytes=VMEM_LIMIT),
    )(counts, tokens, cotangent, modulation)


def leave_kernel(rows_ref, factors_ref, shares_ref, layer_ref, grad_ref):
    width = layer_ref.shape[1]
    sums = shares_ref[0].astype(F32)
    for share in range(1, shares_ref.shape[0]):
        sums = sums + shares_ref[share].astype(F32)
    layer = rows_ref[0].astype(F32) + factors_ref[0] * sums[:, :width]
    layer_ref[...] = layer.astype(BF16)
    d_normed = sums[:, width:] * factors_ref[1]
    normed = factors_ref[2]
    input_grad = rows_ref[1].astype(F32) + factors_ref[3] * (
        d_normed
        - jnp.mean(d_normed, axis=-1, keepdims=True)
        - normed * jnp.mean(d_normed * normed, axis=-1, keepdims=True)
    )
    grad_ref[...] = input_grad.astype(BF16)


def leave(rows, factors, shares):
    out = jax.ShapeDtypeStruct(rows.shape[1:], BF16)
    return pl.pallas_call(
        leave_kernel,
        out_shape=(out, out),
        in_specs=[VMEM] * 3,
        out_specs=(VMEM, VMEM),
        compiler_params=pltpu.CompilerParams(vmem_limit_bytes=VMEM_LIMIT),
    )(rows, factors, shares)


def per_device(tokens, cotangent, w_qkv, w_out, qk_gain, modulation, image_counts):
    tok_rows, model_width = tokens.shape
    z_count = lax.axis_size("z")
    x_count = lax.axis_size("x")
    quad = 4
    pair_rows = 2 * tok_rows
    share = tok_rows // (2 * x_count)
    w_parts = w_qkv.transpose(1, 0, 2)
    mod_flat = modulation.reshape(modulation.shape[0], 3 * model_width)
    gains = jnp.pad(qk_gain, ((0, 6), (0, LANES - HEAD)))

    heads = enter(image_counts, tokens, cotangent, w_parts, w_out, mod_flat, quad)
    mine = lax.all_to_all(heads, ("yh", "yl"), 0, 0)
    mine = mine.reshape(quad * tok_rows, 2 * LANES)
    before = lax.ppermute(mine, "z", [(i, (i + 1) % z_count) for i in range(z_count)])
    after = lax.ppermute(mine, "z", [(i, (i - 1) % z_count) for i in range(z_count)])
    far_half = jnp.where(lax.axis_index("yh") == 0, mine[pair_rows:], mine[:pair_rows])
    halves = 2 * z_count
    far = lax.ppermute(
        far_half,
        ("z", "yh"),
        [(i, (i + (4 if i % 2 == 0 else -4)) % halves) for i in range(halves)],
    )
    later = lax.optimization_barrier((mine, w_parts, w_out, tokens, cotangent, mod_flat))
    _, w_parts_late, w_out_late, tokens_late, cotangent_late, mod_late = later
    w_parts_far = lax.ppermute(w_parts_late, "core", [(0, 1), (1, 0)])
    w_out_far = lax.ppermute(w_out_late, "core", [(0, 1), (1, 0)])
    rows, factors = ready(image_counts, tokens_late, cotangent_late, mod_late, share)
    parts = attend_pair(image_counts, gains, before, mine, after, far)
    parts = lax.all_to_all(parts, ("yl", "core"), 0, 0)
    partial = project(parts, w_out, w_parts, w_out_far, w_parts_far, x_count)
    shares = lax.all_to_all(partial, "x", 0, 0)
    return leave(rows, factors, shares)


def solution(mesh):
    split = jax.sharding.Mesh(mesh.devices.reshape(16, 2, 2, 4, 2), ("z", "yh", "yl", "x", "core"))
    dp, head = ("z", "yh", "yl"), ("x", "core")
    in_specs = (P(dp, None), P(dp, None), P(None, None, head), P(head, None), P(), P(), P())
    out_specs = (P(dp + head, None), P(dp + head, None))
    return jax.shard_map(
        per_device, mesh=split, in_specs=in_specs, out_specs=out_specs, check_vma=False
    )
```

```python
import math

import jax
import jax.numpy as jnp
from jax import lax
from jax.experimental import pallas as pl
from jax.experimental.pallas import tpu as pltpu
from jax.sharding import PartitionSpec as P

EPS = 1e-06
SAME_IMAGE = 512.0
LANES = 128
HEAD = 64
F32 = jnp.float32
BF16 = jnp.bfloat16
VMEM_LIMIT = 24 * 1024 * 1024
ENTER_LIMIT = 60 * 1024 * 1024
VMEM = pl.BlockSpec(memory_space=pltpu.VMEM)
SMEM = pl.BlockSpec(memory_space=pltpu.SMEM)


def rows_dot(a, b):
    return lax.dot_general(a, b, (((1,), (1,)), ((), ())), preferred_element_type=F32)


def block_index():
    return (lax.axis_index("z") * 2 + lax.axis_index("yh")) * 2 + lax.axis_index("yl")


def image_bounds(counts_ref, first_lane):
    lane = lax.broadcasted_iota(jnp.int32, (1, LANES), 1)
    starts = jnp.zeros((1, LANES), jnp.int32)
    ends = jnp.zeros((1, LANES), jnp.int32)
    total = jnp.int32(0)
    for image in range(counts_ref.shape[0]):
        here = lane == first_lane + image
        starts = jnp.where(here, total, starts)
        total = total + counts_ref[image]
        ends = jnp.where(here, total, ends)
    return starts, ends


def modulation_rows(counts_ref, modulation_ref, first, rows):
    starts, ends = image_bounds(counts_ref, 0)
    place = first + lax.broadcasted_iota(jnp.int32, (rows, LANES), 0)
    member = ((place >= starts) & (place < ends)).astype(F32).astype(BF16)
    member = member[:, : modulation_ref.shape[1]]
    return [
        jnp.dot(member, modulation_ref[part], preferred_element_type=F32) for part in range(3)
    ]


def layer_norm(values):
    average = jnp.mean(values, axis=-1, keepdims=True)
    centred = values - average
    inv_std = lax.rsqrt(jnp.mean(centred * centred, axis=-1, keepdims=True) + EPS)
    return centred * inv_std, inv_std


def enter_kernel(
    counts_ref, tokens_ref, cotangent_ref, w_qkv_ref, w_out_ref, modulation_ref, out_ref
):
    rows = tokens_ref.shape[0]
    first = block_index() * rows
    shift, scale, gate = modulation_rows(counts_ref, modulation_ref, first, rows)
    normed, _ = layer_norm(tokens_ref[...].astype(F32))
    hidden = (normed * (1.0 + scale) + shift).astype(BF16)
    q, k, v = (
        jnp.dot(hidden, w_qkv_ref[part], preferred_element_type=F32) for part in range(3)
    )
    d_mixed = (cotangent_ref[...].astype(F32) * gate).astype(BF16)
    d_attn = rows_dot(d_mixed, w_out_ref[...])
    low = lax.broadcasted_iota(jnp.int32, (rows, LANES), 1) < HEAD

    def beside(left, right):
        return jnp.where(low, left, right).astype(BF16)

    q_v = (beside(q, pltpu.roll(v, HEAD, 1)), beside(pltpu.roll(q, HEAD, 1), v))
    k_d = (beside(k, pltpu.roll(d_attn, HEAD, 1)), beside(pltpu.roll(k, HEAD, 1), d_attn))
    for place in range(out_ref.shape[0]):
        out_ref[place, :, 0:LANES] = q_v[place % 2]
        out_ref[place, :, LANES:] = k_d[place % 2]


def enter(counts, tokens, cotangent, w_parts, w_out, modulation, quad):
    return pl.pallas_call(
        enter_kernel,
        out_shape=jax.ShapeDtypeStruct((quad, tokens.shape[0], 2 * LANES), BF16),
        in_specs=[SMEM] + [VMEM] * 5,
        out_specs=VMEM,
        compiler_params=pltpu.CompilerParams(vmem_limit_bytes=ENTER_LIMIT),
    )(counts, tokens, cotangent, w_parts, w_out, modulation)


def attend_kernel(
    counts_ref,
    gains_ref,
    before_ref,
    quad_ref,
    after_ref,
    far_ref,
    kept_ref,
    sent_ref,
    qx_ref,
    kx_ref,
    vx_ref,
    dx_ref,
    s_ref,
    p_ref,
    dk_ref,
    dv_ref,
    done_ref,
):
    chunk = far_ref.shape[0]
    own = 3
    slots = 7
    reach = 4
    half = lax.axis_index("yh")
    origin = (block_index() // 2 - own) * chunk
    own_at = own * chunk
    lane = lax.broadcasted_iota(jnp.int32, (chunk, LANES), 1)
    row = lax.broadcasted_iota(jnp.int32, (chunk, LANES), 0)
    low = lane < HEAD
    starts, ends = image_bounds(counts_ref, HEAD)
    starts = starts - origin
    ends = ends - origin
    inv_root = 1.0 / math.sqrt(HEAD)

    def lower_mean(values):
        return jnp.sum(jnp.where(low, values, 0.0), axis=-1, keepdims=True) * (1.0 / HEAD)

    def normed(raw, gain):
        return (raw * lax.rsqrt(lower_mean(raw * raw) + EPS) * gain).astype(BF16).astype(F32)

    q_gain, k_gain = gains_ref[0:1, :], gains_ref[1:2, :]

    def place_chunk(source, slot):
        begin = pl.multiple_of(slot * chunk, chunk)
        at = pl.ds(begin, chunk)
        place = row + begin
        same = ((place >= starts) & (place < ends)).astype(F32)
        first = source[:, 0:LANES].astype(F32)
        second = source[:, LANES:].astype(F32)
        qx_ref[at, :] = jnp.where(low, normed(first, q_gain) * inv_root, same * SAME_IMAGE).astype(BF16)
        kx_ref[at, :] = jnp.where(low, normed(second, k_gain), same).astype(BF16)
        vx_ref[at, :] = jnp.where(low, 0.0, first).astype(BF16)
        dx_ref[at, :] = second.astype(BF16)

    place_chunk(before_ref.at[0:chunk], 1 - half)
    place_chunk(before_ref.at[chunk : 2 * chunk], 2 - half)
    place_chunk(quad_ref.at[0:chunk], 3 - half)
    place_chunk(quad_ref.at[chunk : 2 * chunk], 4 - half)
    place_chunk(after_ref.at[0:chunk], 5 - half)
    place_chunk(after_ref.at[chunk : 2 * chunk], 6 - half)
    place_chunk(far_ref, half * (slots - 1))

    left_from = jnp.int32(0)
    right_to = jnp.int32(slots * chunk)
    total = -origin
    for image in range(counts_ref.shape[0]):
        left_from = jnp.where(total <= own_at, total, left_from)
        ended = total >= own_at + chunk
        total = total + counts_ref[image]
        right_to = jnp.where((total >= own_at + chunk) & jnp.logical_not(ended), total, right_to)
    left_chunk = jnp.clip(left_from // chunk, 0, slots - reach)
    right_chunk = jnp.clip((right_to - 1) // chunk - (reach - 1), 0, slots - reach)

    def block_parts(keys, values, q_block, d_block):
        scores = rows_dot(keys, q_block)
        d_probs = rows_dot(values, d_block).astype(BF16).astype(F32)
        highest = jnp.max(scores, axis=0, keepdims=True)
        weights = jnp.exp(scores - highest)
        scale = 1.0 / jnp.sum(weights, axis=0, keepdims=True)
        mean_grad = jnp.sum(weights * d_probs, axis=0, keepdims=True) * scale
        return weights, d_probs, scale, mean_grad

    near = slice(own_at, own_at + chunk)
    q_own = qx_ref[near, :]
    d_own = dx_ref[near, :]
    weights, d_probs, scale, mean_grad = block_parts(kx_ref[...], vx_ref[...], q_own, d_own)
    probs = weights * scale
    d_scores = (probs * (d_probs - mean_grad)).astype(BF16)
    probs = probs.astype(BF16)
    dk_ref[...] = jnp.dot(d_scores[near], q_own, preferred_element_type=F32)
    dv_ref[...] = jnp.dot(probs[near], d_own, preferred_element_type=F32)
    contract_rows = (((0,), (0,)), ((), ()))
    result = lax.dot_general(probs, vx_ref[...], contract_rows, preferred_element_type=F32)
    dq_norm = lax.dot_general(d_scores, kx_ref[...], contract_rows, preferred_element_type=F32)

    query_lane = lax.broadcasted_iota(jnp.int32, (1, chunk), 1)

    def one_block(step, carry):
        slot = step + jnp.where(step >= own, 1, 0)
        begin = slot * chunk

        @pl.when((begin < right_to) & (begin + chunk > left_from))
        def _():
            at = pl.ds(pl.multiple_of(begin, chunk), chunk)
            key_chunk = jnp.where(slot < own, left_chunk, right_chunk)
            keys_at = pl.ds(pl.multiple_of(key_chunk * chunk, chunk), reach * chunk)
            near_at = pl.ds(pl.multiple_of((own - key_chunk) * chunk, chunk), chunk)
            q_block = qx_ref[at, :]
            d_block = dx_ref[at, :]
            weights, d_probs, scale, mean_grad = block_parts(
                kx_ref[keys_at, :], vx_ref[keys_at, :], q_block, d_block
            )
            s_ref[...] = weights
            p_ref[...] = d_probs
            place = query_lane + begin
            scale = jnp.where((place >= left_from) & (place < right_to), scale, 0.0)
            probs = s_ref[near_at, :] * scale
            d_scores = (probs * (p_ref[near_at, :] - mean_grad)).astype(BF16)
            dk_ref[...] += jnp.dot(d_scores, q_block, preferred_element_type=F32)
            dv_ref[...] += jnp.dot(probs.astype(BF16), d_block, preferred_element_type=F32)

        return carry

    lax.fori_loop(0, slots - 1, one_block, 0)

    def norm_grad(raw, gain, d_norm):
        inverse = lax.rsqrt(lower_mean(raw * raw) + EPS)
        scaled = d_norm.astype(BF16).astype(F32) * gain
        inner = lower_mean(raw * scaled)
        return inverse * scaled - raw * (inverse * inverse * inverse * inner)

    own_in_quad = pl.ds(pl.multiple_of(half * chunk, chunk), chunk)
    raw_q = quad_ref[own_in_quad, 0:LANES].astype(F32)
    raw_k = quad_ref[own_in_quad, LANES:].astype(F32)
    d_q = norm_grad(raw_q, q_gain, dq_norm * inv_root)
    d_k = norm_grad(raw_k, k_gain, dk_ref[...])
    done_ref[:, 0:LANES] = jnp.where(low, d_q, result).astype(BF16)
    done_ref[:, LANES:] = jnp.where(low, d_k, dv_ref[...]).astype(BF16)
    tok_rows = kept_ref.shape[0]
    parity = lax.axis_index("yl")
    kept_ref[...] = done_ref[pl.ds(pl.multiple_of(parity * tok_rows, tok_rows), tok_rows), :]
    sent_ref[...] = done_ref[pl.ds(pl.multiple_of((1 - parity) * tok_rows, tok_rows), tok_rows), :]


def attend_pair(counts, gains, before, quad, after, far):
    chunk = far.shape[0]
    rows = 7 * chunk
    half_out = jax.ShapeDtypeStruct((chunk // 2, 2 * LANES), BF16)
    return pl.pallas_call(
        attend_kernel,
        out_shape=(half_out, half_out),
        in_specs=[SMEM] + [VMEM] * 5,
        out_specs=(VMEM, VMEM),
        scratch_shapes=[pltpu.VMEM((rows, LANES), BF16)] * 4
        + [pltpu.VMEM((4 * chunk, chunk), F32)] * 2
        + [pltpu.VMEM((chunk, LANES), F32)] * 2
        + [pltpu.VMEM((chunk, 2 * LANES), BF16)],
        compiler_params=pltpu.CompilerParams(vmem_limit_bytes=VMEM_LIMIT),
    )(counts, gains, before, quad, after, far)


def project_kernel(kept_ref, swapped_ref, w_out_ref, w_qkv_ref, out_ref):
    rows = kept_ref.shape[0]
    width = w_out_ref.shape[1]
    first = lax.axis_index("yl") == 0
    low = lax.broadcasted_iota(jnp.int32, (rows, LANES), 1) < HEAD
    kept = kept_ref[...].astype(F32)
    swapped = swapped_ref[...].astype(F32)
    head0 = jnp.where(first, kept, swapped)
    head1 = jnp.where(first, swapped, kept)
    a0, a1 = head0[:, :LANES], head1[:, :LANES]
    b0, b1 = head0[:, LANES:], head1[:, LANES:]
    d_q = jnp.where(low, a0, pltpu.roll(a1, HEAD, 1)).astype(BF16)
    attn = jnp.where(low, pltpu.roll(a0, HEAD, 1), a1).astype(BF16)
    d_k = jnp.where(low, b0, pltpu.roll(b1, HEAD, 1)).astype(BF16)
    d_v = jnp.where(low, pltpu.roll(b0, HEAD, 1), b1).astype(BF16)
    mixed = jnp.dot(attn, w_out_ref[...], preferred_element_type=F32)
    out_ref[:, :width] = mixed.astype(BF16)
    d_hidden = (
        rows_dot(d_q, w_qkv_ref[0]) + rows_dot(d_k, w_qkv_ref[1]) + rows_dot(d_v, w_qkv_ref[2])
    )
    out_ref[:, width:] = d_hidden.astype(BF16)


def project(kept, swapped, w_out, w_parts):
    return pl.pallas_call(
        project_kernel,
        out_shape=jax.ShapeDtypeStruct((kept.shape[0], 2 * w_out.shape[1]), BF16),
        in_specs=[VMEM] * 4,
        out_specs=VMEM,
        compiler_params=pltpu.CompilerParams(vmem_limit_bytes=VMEM_LIMIT),
    )(kept, swapped, w_out, w_parts)


def ready_kernel(
    counts_ref,
    tokens_ref,
    cotangent_ref,
    modulation_ref,
    rows_ref,
    factors_ref,
):
    rows = rows_ref.shape[1]
    first_row = (lax.axis_index("x") * 2 + lax.axis_index("core")) * rows
    first = block_index() * tokens_ref.shape[0] + first_row
    _, scale, gate = modulation_rows(counts_ref, modulation_ref, first, rows)
    at = pl.ds(pl.multiple_of(first_row, rows), rows)
    normed, inv_std = layer_norm(tokens_ref[at, :].astype(F32))
    rows_ref[0] = tokens_ref[at, :]
    rows_ref[1] = cotangent_ref[at, :]
    factors_ref[0] = gate
    factors_ref[1] = 1.0 + scale
    factors_ref[2] = normed
    factors_ref[3] = jnp.broadcast_to(inv_std, normed.shape)


def ready(counts, tokens, cotangent, modulation, share):
    width = tokens.shape[1]
    return pl.pallas_call(
        ready_kernel,
        out_shape=(
            jax.ShapeDtypeStruct((2, share, width), BF16),
            jax.ShapeDtypeStruct((4, share, width), F32),
        ),
        in_specs=[SMEM] + [VMEM] * 3,
        out_specs=(VMEM, VMEM),
        compiler_params=pltpu.CompilerParams(vmem_limit_bytes=VMEM_LIMIT),
    )(counts, tokens, cotangent, modulation)


def leave_kernel(rows_ref, factors_ref, shares_ref, layer_ref, grad_ref):
    width = layer_ref.shape[1]
    sums = shares_ref[0].astype(F32)
    for share in range(1, shares_ref.shape[0]):
        sums = sums + shares_ref[share].astype(F32)
    layer = rows_ref[0].astype(F32) + factors_ref[0] * sums[:, :width]
    layer_ref[...] = layer.astype(BF16)
    d_normed = sums[:, width:] * factors_ref[1]
    normed = factors_ref[2]
    input_grad = rows_ref[1].astype(F32) + factors_ref[3] * (
        d_normed
        - jnp.mean(d_normed, axis=-1, keepdims=True)
        - normed * jnp.mean(d_normed * normed, axis=-1, keepdims=True)
    )
    grad_ref[...] = input_grad.astype(BF16)


def leave(rows, factors, shares):
    out = jax.ShapeDtypeStruct(rows.shape[1:], BF16)
    return pl.pallas_call(
        leave_kernel,
        out_shape=(out, out),
        in_specs=[VMEM] * 3,
        out_specs=(VMEM, VMEM),
        compiler_params=pltpu.CompilerParams(vmem_limit_bytes=VMEM_LIMIT),
    )(rows, factors, shares)


def per_device(tokens, cotangent, w_qkv, w_out, qk_gain, modulation, image_counts):
    tok_rows, model_width = tokens.shape
    z_count = lax.axis_size("z")
    x_count = lax.axis_size("x")
    quad = 4
    pair_rows = 2 * tok_rows
    share = tok_rows // (2 * x_count)
    w_parts = w_qkv.transpose(1, 0, 2)
    mod_parts = modulation.transpose(1, 0, 2)
    gains = jnp.pad(qk_gain, ((0, 6), (0, LANES - HEAD)))

    heads = enter(image_counts, tokens, cotangent, w_parts, w_out, mod_parts, quad)
    mine = lax.all_to_all(heads, ("yh", "yl"), 0, 0)
    mine = mine.reshape(quad * tok_rows, 2 * LANES)
    before = lax.ppermute(mine, "z", [(i, (i + 1) % z_count) for i in range(z_count)])
    after = lax.ppermute(mine, "z", [(i, (i - 1) % z_count) for i in range(z_count)])
    far_half = jnp.where(lax.axis_index("yh") == 0, mine[pair_rows:], mine[:pair_rows])
    halves = 2 * z_count
    far = lax.ppermute(
        far_half,
        ("z", "yh"),
        [(i, (i + (4 if i % 2 == 0 else -4)) % halves) for i in range(halves)],
    )
    _, tokens_late, cotangent_late, mod_late = lax.optimization_barrier(
        (mine, tokens, cotangent, mod_parts)
    )
    rows, factors = ready(image_counts, tokens_late, cotangent_late, mod_late, share)
    kept, sent = attend_pair(image_counts, gains, before, mine, after, far)
    swapped = lax.ppermute(sent, "yl", [(0, 1), (1, 0)])
    partial = project(kept, swapped, w_out, w_parts)
    shares = lax.all_to_all(
        partial.reshape(2 * x_count, share, 2 * model_width), ("x", "core"), 0, 0
    )
    return leave(rows, factors, shares)


def solution(mesh):
    split = jax.sharding.Mesh(mesh.devices.reshape(16, 2, 2, 4, 2), ("z", "yh", "yl", "x", "core"))
    dp, head = ("z", "yh", "yl"), ("x", "core")
    in_specs = (P(dp, None), P(dp, None), P(None, None, head), P(head, None), P(), P(), P())
    out_specs = (P(dp + head, None), P(dp + head, None))
    return jax.shard_map(
        per_device, mesh=split, in_specs=in_specs, out_specs=out_specs, check_vma=False
    )
```

```python
import math

import jax
import jax.numpy as jnp
from jax import lax
from jax.experimental import pallas as pl
from jax.experimental.pallas import tpu as pltpu
from jax.sharding import PartitionSpec as P

EPS = 1e-06
SAME_IMAGE = 512.0
LANES = 128
HEAD = 64
F32 = jnp.float32
BF16 = jnp.bfloat16
VMEM_LIMIT = 24 * 1024 * 1024
ENTER_LIMIT = 60 * 1024 * 1024
VMEM = pl.BlockSpec(memory_space=pltpu.VMEM)
SMEM = pl.BlockSpec(memory_space=pltpu.SMEM)


def rows_dot(a, b):
    return lax.dot_general(a, b, (((1,), (1,)), ((), ())), preferred_element_type=F32)


def block_index():
    return (lax.axis_index("z") * 2 + lax.axis_index("yh")) * 2 + lax.axis_index("yl")


def image_bounds(counts_ref, first_lane):
    lane = lax.broadcasted_iota(jnp.int32, (1, LANES), 1)
    starts = jnp.zeros((1, LANES), jnp.int32)
    ends = jnp.zeros((1, LANES), jnp.int32)
    total = jnp.int32(0)
    for image in range(counts_ref.shape[0]):
        here = lane == first_lane + image
        starts = jnp.where(here, total, starts)
        total = total + counts_ref[image]
        ends = jnp.where(here, total, ends)
    return starts, ends


def modulation_rows(counts_ref, modulation_ref, first, rows):
    starts, ends = image_bounds(counts_ref, 0)
    place = first + lax.broadcasted_iota(jnp.int32, (rows, LANES), 0)
    member = ((place >= starts) & (place < ends)).astype(F32).astype(BF16)
    member = member[:, : modulation_ref.shape[1]]
    return [
        jnp.dot(member, modulation_ref[part], preferred_element_type=F32) for part in range(3)
    ]


def layer_norm(values):
    average = jnp.mean(values, axis=-1, keepdims=True)
    centred = values - average
    inv_std = lax.rsqrt(jnp.mean(centred * centred, axis=-1, keepdims=True) + EPS)
    return centred * inv_std, inv_std


def enter_kernel(
    counts_ref, tokens_ref, cotangent_ref, w_qkv_ref, w_out_ref, modulation_ref, own_ref, other_ref
):
    rows = tokens_ref.shape[0]
    first = block_index() * rows
    shift, scale, gate = modulation_rows(counts_ref, modulation_ref, first, rows)
    normed, _ = layer_norm(tokens_ref[...].astype(F32))
    hidden = (normed * (1.0 + scale) + shift).astype(BF16)
    q, k, v = (
        jnp.dot(hidden, w_qkv_ref[part], preferred_element_type=F32) for part in range(3)
    )
    d_mixed = (cotangent_ref[...].astype(F32) * gate).astype(BF16)
    d_attn = rows_dot(d_mixed, w_out_ref[...])
    low = lax.broadcasted_iota(jnp.int32, (rows, LANES), 1) < HEAD

    first_head = lax.axis_index("yl") == 0

    def both(left, right, at):
        head0 = jnp.where(low, left, pltpu.roll(right, HEAD, 1))
        head1 = jnp.where(low, pltpu.roll(left, HEAD, 1), right)
        own_ref[:, at] = jnp.where(first_head, head0, head1).astype(BF16)
        other_ref[:, at] = jnp.where(first_head, head1, head0).astype(BF16)

    both(q, v, slice(0, LANES))
    both(k, d_attn, slice(LANES, 2 * LANES))


def enter(counts, tokens, cotangent, w_parts, w_out, modulation):
    head_rows = jax.ShapeDtypeStruct((tokens.shape[0], 2 * LANES), BF16)
    return pl.pallas_call(
        enter_kernel,
        out_shape=(head_rows, head_rows),
        in_specs=[SMEM] + [VMEM] * 5,
        out_specs=(VMEM, VMEM),
        compiler_params=pltpu.CompilerParams(vmem_limit_bytes=ENTER_LIMIT),
    )(counts, tokens, cotangent, w_parts, w_out, modulation)


def attend_kernel(
    counts_ref,
    gains_ref,
    before_ref,
    quad_ref,
    after_ref,
    far_ref,
    kept_ref,
    to_core_ref,
    to_block_ref,
    to_both_ref,
    qx_ref,
    kx_ref,
    vx_ref,
    dx_ref,
    s_ref,
    p_ref,
    dk_ref,
    dv_ref,
    done_ref,
):
    chunk = far_ref.shape[0]
    own = 3
    slots = 7
    reach = 4
    half = lax.axis_index("yh")
    origin = (block_index() // 2 - own) * chunk
    own_at = own * chunk
    block_rows = chunk // 2
    row = lax.broadcasted_iota(jnp.int32, (block_rows, LANES), 0)
    low = lax.broadcasted_iota(jnp.int32, (1, LANES), 1) < HEAD
    starts, ends = image_bounds(counts_ref, HEAD)
    starts = starts - origin
    ends = ends - origin
    inv_root = 1.0 / math.sqrt(HEAD)

    def lower_mean(values):
        return jnp.sum(jnp.where(low, values, 0.0), axis=-1, keepdims=True) * (1.0 / HEAD)

    def normed(raw, gain):
        return (raw * lax.rsqrt(lower_mean(raw * raw) + EPS) * gain).astype(BF16).astype(F32)

    q_gain, k_gain = gains_ref[0:1, :], gains_ref[1:2, :]

    def place_block(source, begin):
        begin = pl.multiple_of(begin, block_rows)
        at = pl.ds(begin, block_rows)
        place = row + begin
        same = ((place >= starts) & (place < ends)).astype(F32)
        first = source[:, 0:LANES].astype(F32)
        second = source[:, LANES:].astype(F32)
        qx_ref[at, :] = jnp.where(low, normed(first, q_gain) * inv_root, same * SAME_IMAGE).astype(BF16)
        kx_ref[at, :] = jnp.where(low, normed(second, k_gain), same).astype(BF16)
        vx_ref[at, :] = jnp.where(low, 0.0, first).astype(BF16)
        dx_ref[at, :] = second.astype(BF16)

    along_y = 2 * half + lax.axis_index("yl")
    for turn in range(4):
        at = slice(turn * block_rows, (turn + 1) * block_rows)
        begin = own_at + (lax.rem(along_y - turn + 4, 4) - 2 * half) * block_rows
        place_block(before_ref.at[at], begin - 4 * block_rows)
        place_block(quad_ref.at[at], begin)
        place_block(after_ref.at[at], begin + 4 * block_rows)
    far_at = half * (slots - 1) * chunk
    place_block(far_ref.at[0:block_rows], far_at + block_rows)
    place_block(far_ref.at[block_rows:chunk], far_at)

    left_from = jnp.int32(0)
    right_to = jnp.int32(slots * chunk)
    total = -origin
    for image in range(counts_ref.shape[0]):
        left_from = jnp.where(total <= own_at, total, left_from)
        ended = total >= own_at + chunk
        total = total + counts_ref[image]
        right_to = jnp.where((total >= own_at + chunk) & jnp.logical_not(ended), total, right_to)
    left_chunk = jnp.clip(left_from // chunk, 0, slots - reach)
    right_chunk = jnp.clip((right_to - 1) // chunk - (reach - 1), 0, slots - reach)

    def block_parts(keys, values, q_block, d_block):
        scores = rows_dot(keys, q_block)
        d_probs = rows_dot(values, d_block).astype(BF16).astype(F32)
        highest = jnp.max(scores, axis=0, keepdims=True)
        weights = jnp.exp(scores - highest)
        scale = 1.0 / jnp.sum(weights, axis=0, keepdims=True)
        mean_grad = jnp.sum(weights * d_probs, axis=0, keepdims=True) * scale
        return weights, d_probs, scale, mean_grad

    near = slice(own_at, own_at + chunk)
    q_own = qx_ref[near, :]
    d_own = dx_ref[near, :]
    weights, d_probs, scale, mean_grad = block_parts(kx_ref[...], vx_ref[...], q_own, d_own)
    probs = weights * scale
    d_scores = (probs * (d_probs - mean_grad)).astype(BF16)
    probs = probs.astype(BF16)
    dk_ref[...] = jnp.dot(d_scores[near], q_own, preferred_element_type=F32)
    dv_ref[...] = jnp.dot(probs[near], d_own, preferred_element_type=F32)
    contract_rows = (((0,), (0,)), ((), ()))
    result = lax.dot_general(probs, vx_ref[...], contract_rows, preferred_element_type=F32)
    dq_norm = lax.dot_general(d_scores, kx_ref[...], contract_rows, preferred_element_type=F32)

    query_lane = lax.broadcasted_iota(jnp.int32, (1, chunk), 1)

    def one_block(step, carry):
        slot = step + jnp.where(step >= own, 1, 0)
        begin = slot * chunk

        @pl.when((begin < right_to) & (begin + chunk > left_from))
        def _():
            at = pl.ds(pl.multiple_of(begin, chunk), chunk)
            key_chunk = jnp.where(slot < own, left_chunk, right_chunk)
            keys_at = pl.ds(pl.multiple_of(key_chunk * chunk, chunk), reach * chunk)
            near_at = pl.ds(pl.multiple_of((own - key_chunk) * chunk, chunk), chunk)
            q_block = qx_ref[at, :]
            d_block = dx_ref[at, :]
            weights, d_probs, scale, mean_grad = block_parts(
                kx_ref[keys_at, :], vx_ref[keys_at, :], q_block, d_block
            )
            s_ref[...] = weights
            p_ref[...] = d_probs
            place = query_lane + begin
            scale = jnp.where((place >= left_from) & (place < right_to), scale, 0.0)
            probs = s_ref[near_at, :] * scale
            d_scores = (probs * (p_ref[near_at, :] - mean_grad)).astype(BF16)
            dk_ref[...] += jnp.dot(d_scores, q_block, preferred_element_type=F32)
            dv_ref[...] += jnp.dot(probs.astype(BF16), d_block, preferred_element_type=F32)

        return carry

    lax.fori_loop(0, slots - 1, one_block, 0)

    def norm_grad(raw, gain, d_norm):
        inverse = lax.rsqrt(lower_mean(raw * raw) + EPS)
        scaled = d_norm.astype(BF16).astype(F32) * gain
        inner = lower_mean(raw * scaled)
        return inverse * scaled - raw * (inverse * inverse * inverse * inner)

    yl = lax.axis_index("yl")
    raw = jnp.concatenate(
        [
            quad_ref[pl.ds(pl.multiple_of(yl * block_rows, block_rows), block_rows), :],
            quad_ref[pl.ds(pl.multiple_of((1 - yl) * 3 * block_rows, block_rows), block_rows), :],
        ],
        axis=0,
    ).astype(F32)
    d_q = norm_grad(raw[:, 0:LANES], q_gain, dq_norm * inv_root)
    d_k = norm_grad(raw[:, LANES:], k_gain, dk_ref[...])
    done_ref[:, 0:LANES] = jnp.where(low, d_q, result).astype(BF16)
    done_ref[:, LANES:] = jnp.where(low, d_k, dv_ref[...]).astype(BF16)
    core = lax.axis_index("core")
    share = 16

    def hand_out(ref, block, core):
        for part in range(ref.shape[0] // share):
            begin = block * block_rows + part * 2 * share + core * share
            ref[part * share : (part + 1) * share, :] = done_ref[
                pl.ds(pl.multiple_of(begin, share), share), :
            ]

    hand_out(kept_ref, yl, core)
    hand_out(to_core_ref, yl, 1 - core)
    hand_out(to_block_ref, 1 - yl, core)
    hand_out(to_both_ref, 1 - yl, 1 - core)


def attend_pair(counts, gains, before, quad, after, far):
    chunk = far.shape[0]
    rows = 7 * chunk
    part = jax.ShapeDtypeStruct((chunk // 4, 2 * LANES), BF16)
    return pl.pallas_call(
        attend_kernel,
        out_shape=(part,) * 4,
        in_specs=[SMEM] + [VMEM] * 5,
        out_specs=(VMEM,) * 4,
        scratch_shapes=[pltpu.VMEM((rows, LANES), BF16)] * 4
        + [pltpu.VMEM((4 * chunk, chunk), F32)] * 2
        + [pltpu.VMEM((chunk, LANES), F32)] * 2
        + [pltpu.VMEM((chunk, 2 * LANES), BF16)],
        compiler_params=pltpu.CompilerParams(vmem_limit_bytes=VMEM_LIMIT),
    )(counts, gains, before, quad, after, far)


def project_kernel(
    kept_ref,
    from_core_ref,
    from_block_ref,
    from_both_ref,
    w_out_ref,
    w_qkv_ref,
    w_out_far_ref,
    w_qkv_far_ref,
    *refs,
):
    out_refs, done_ref = refs[:-1], refs[-1]
    rows = kept_ref.shape[0]
    width = w_out_ref.shape[1]
    share = out_refs[0].shape[0]
    first = lax.axis_index("yl") == 0
    low = lax.broadcasted_iota(jnp.int32, (rows, LANES), 1) < HEAD

    def products(same_ref, swapped_ref, w_out, w_qkv):
        same = same_ref[...].astype(F32)
        swapped = swapped_ref[...].astype(F32)
        head0 = jnp.where(first, same, swapped)
        head1 = jnp.where(first, swapped, same)
        a0, a1 = head0[:, :LANES], head1[:, :LANES]
        b0, b1 = head0[:, LANES:], head1[:, LANES:]
        d_q = jnp.where(low, a0, pltpu.roll(a1, HEAD, 1)).astype(BF16)
        attn = jnp.where(low, pltpu.roll(a0, HEAD, 1), a1).astype(BF16)
        d_k = jnp.where(low, b0, pltpu.roll(b1, HEAD, 1)).astype(BF16)
        d_v = jnp.where(low, pltpu.roll(b0, HEAD, 1), b1).astype(BF16)
        mixed = jnp.dot(attn, w_out[...], preferred_element_type=F32)
        d_hidden = rows_dot(d_q, w_qkv[0]) + rows_dot(d_k, w_qkv[1]) + rows_dot(d_v, w_qkv[2])
        return mixed, d_hidden

    mixed, d_hidden = products(kept_ref, from_block_ref, w_out_ref, w_qkv_ref)
    mixed_far, d_hidden_far = products(from_core_ref, from_both_ref, w_out_far_ref, w_qkv_far_ref)
    done_ref[:, :width] = (mixed + mixed_far).astype(BF16)
    done_ref[:, width:] = (d_hidden + d_hidden_far).astype(BF16)
    count = len(out_refs)
    for turn in range(count):
        place = lax.rem(lax.axis_index("x") + turn, count)
        out_refs[turn][...] = done_ref[pl.ds(pl.multiple_of(place * share, share), share), :]


def project(parts, weights, x_count):
    rows = parts[0].shape[0]
    width = 2 * weights[0].shape[1]
    out = jax.ShapeDtypeStruct((rows // x_count, width), BF16)
    return pl.pallas_call(
        project_kernel,
        out_shape=(out,) * x_count,
        in_specs=[VMEM] * 8,
        out_specs=(VMEM,) * x_count,
        scratch_shapes=[pltpu.VMEM((rows, width), BF16)],
        compiler_params=pltpu.CompilerParams(vmem_limit_bytes=VMEM_LIMIT),
    )(*parts, *weights)


def ready_kernel(
    counts_ref,
    tokens_ref,
    cotangent_ref,
    modulation_ref,
    rows_ref,
    factors_ref,
):
    rows = rows_ref.shape[1]
    first_row = (lax.axis_index("x") * 2 + lax.axis_index("core")) * rows
    first = block_index() * tokens_ref.shape[0] + first_row
    _, scale, gate = modulation_rows(counts_ref, modulation_ref, first, rows)
    at = pl.ds(pl.multiple_of(first_row, rows), rows)
    normed, inv_std = layer_norm(tokens_ref[at, :].astype(F32))
    rows_ref[0] = tokens_ref[at, :]
    rows_ref[1] = cotangent_ref[at, :]
    factors_ref[0] = gate
    factors_ref[1] = 1.0 + scale
    factors_ref[2] = normed
    factors_ref[3] = jnp.broadcast_to(inv_std, normed.shape)


def ready(counts, tokens, cotangent, modulation, share):
    width = tokens.shape[1]
    return pl.pallas_call(
        ready_kernel,
        out_shape=(
            jax.ShapeDtypeStruct((2, share, width), BF16),
            jax.ShapeDtypeStruct((4, share, width), F32),
        ),
        in_specs=[SMEM] + [VMEM] * 3,
        out_specs=(VMEM, VMEM),
        compiler_params=pltpu.CompilerParams(vmem_limit_bytes=VMEM_LIMIT),
    )(counts, tokens, cotangent, modulation)


def leave_kernel(rows_ref, factors_ref, *refs):
    share_refs, (layer_ref, grad_ref) = refs[:-2], refs[-2:]
    width = layer_ref.shape[1]
    sums = share_refs[0][...].astype(F32)
    for share_ref in share_refs[1:]:
        sums = sums + share_ref[...].astype(F32)
    layer = rows_ref[0].astype(F32) + factors_ref[0] * sums[:, :width]
    layer_ref[...] = layer.astype(BF16)
    d_normed = sums[:, width:] * factors_ref[1]
    normed = factors_ref[2]
    input_grad = rows_ref[1].astype(F32) + factors_ref[3] * (
        d_normed
        - jnp.mean(d_normed, axis=-1, keepdims=True)
        - normed * jnp.mean(d_normed * normed, axis=-1, keepdims=True)
    )
    grad_ref[...] = input_grad.astype(BF16)


def leave(rows, factors, shares):
    out = jax.ShapeDtypeStruct(rows.shape[1:], BF16)
    return pl.pallas_call(
        leave_kernel,
        out_shape=(out, out),
        in_specs=[VMEM] * (2 + len(shares)),
        out_specs=(VMEM, VMEM),
        compiler_params=pltpu.CompilerParams(vmem_limit_bytes=VMEM_LIMIT),
    )(rows, factors, *shares)


def turned(x, axes, by):
    count = lax.axis_size(axes)
    return lax.ppermute(x, axes, [(i, (i + by) % count) for i in range(count)])


def per_device(tokens, cotangent, w_qkv, w_out, qk_gain, modulation, image_counts):
    tok_rows = tokens.shape[0]
    x_count = lax.axis_size("x")
    pair_rows = 2 * tok_rows
    share = tok_rows // (2 * x_count)
    w_parts = w_qkv.transpose(1, 0, 2)
    mod_parts = modulation.transpose(1, 0, 2)
    gains = jnp.pad(qk_gain, ((0, 6), (0, LANES - HEAD)))
    along_y = ("yh", "yl")

    w_parts_far = turned(w_parts, "core", 1)
    w_out_far = turned(w_out, "core", 1)
    own, other = enter(image_counts, tokens, cotangent, w_parts, w_out, mod_parts)
    next_block = turned(other, along_y, 1)
    last_block = turned(other, along_y, 3)
    far_block = turned(own, along_y, 2)
    mine = jnp.concatenate([own, next_block, far_block, last_block], axis=0)
    before = turned(mine, "z", 1)
    after = turned(mine, "z", -1)
    far_from = (1 + lax.axis_index("yl")) * tok_rows
    far_half = lax.dynamic_slice_in_dim(mine, far_from, pair_rows, 0)
    halves = 2 * lax.axis_size("z")
    far = lax.ppermute(
        far_half,
        ("z", "yh"),
        [(i, (i + (4 if i % 2 == 0 else -4)) % halves) for i in range(halves)],
    )
    _, tokens_late, cotangent_late, mod_late = lax.optimization_barrier(
        (mine, tokens, cotangent, mod_parts)
    )
    rows, factors = ready(image_counts, tokens_late, cotangent_late, mod_late, share)
    kept, to_core, to_block, to_both = attend_pair(
        image_counts, gains, before, mine, after, far
    )
    from_both = lax.ppermute(to_both, ("yl", "core"), [(i, 3 - i) for i in range(4)])
    from_block = turned(to_block, "yl", 1)
    from_core = turned(to_core, "core", 1)
    shares = project(
        (kept, from_core, from_block, from_both),
        (w_out, w_parts, w_out_far, w_parts_far),
        x_count,
    )
    shares = [shares[0]] + [turned(shares[by], "x", by) for by in (2, 1, 3)]
    return leave(rows, factors, shares)


def solution(mesh):
    split = jax.sharding.Mesh(mesh.devices.reshape(16, 2, 2, 4, 2), ("z", "yh", "yl", "x", "core"))
    dp, head = ("z", "yh", "yl"), ("x", "core")
    in_specs = (P(dp, None), P(dp, None), P(None, None, head), P(head, None), P(), P(), P())
    out_specs = (P(dp + head, None), P(dp + head, None))
    return jax.shard_map(
        per_device, mesh=split, in_specs=in_specs, out_specs=out_specs, check_vma=False
    )
```

```python
import math

import jax
import jax.numpy as jnp
from jax import lax
from jax.experimental import pallas as pl
from jax.experimental.pallas import tpu as pltpu
from jax.sharding import PartitionSpec as P

EPS = 1e-06
SAME_IMAGE = 512.0
LANES = 128
HEAD = 64
F32 = jnp.float32
BF16 = jnp.bfloat16
VMEM_LIMIT = 24 * 1024 * 1024
ENTER_LIMIT = 60 * 1024 * 1024
VMEM = pl.BlockSpec(memory_space=pltpu.VMEM)
SMEM = pl.BlockSpec(memory_space=pltpu.SMEM)


def rows_dot(a, b):
    return lax.dot_general(a, b, (((1,), (1,)), ((), ())), preferred_element_type=F32)


def block_index():
    return (lax.axis_index("z") * 2 + lax.axis_index("yh")) * 2 + lax.axis_index("yl")


def image_bounds(counts_ref, first_lane):
    lane = lax.broadcasted_iota(jnp.int32, (1, LANES), 1)
    starts = jnp.zeros((1, LANES), jnp.int32)
    ends = jnp.zeros((1, LANES), jnp.int32)
    total = jnp.int32(0)
    for image in range(counts_ref.shape[0]):
        here = lane == first_lane + image
        starts = jnp.where(here, total, starts)
        total = total + counts_ref[image]
        ends = jnp.where(here, total, ends)
    return starts, ends


def modulation_rows(counts_ref, modulation_ref, first, rows):
    starts, ends = image_bounds(counts_ref, 0)
    place = first + lax.broadcasted_iota(jnp.int32, (rows, LANES), 0)
    member = ((place >= starts) & (place < ends)).astype(F32).astype(BF16)
    member = member[:, : modulation_ref.shape[1]]
    return [
        jnp.dot(member, modulation_ref[part], preferred_element_type=F32) for part in range(3)
    ]


def layer_norm(values):
    average = jnp.mean(values, axis=-1, keepdims=True)
    centred = values - average
    inv_std = lax.rsqrt(jnp.mean(centred * centred, axis=-1, keepdims=True) + EPS)
    return centred * inv_std, inv_std


def enter_kernel(
    counts_ref, tokens_ref, cotangent_ref, w_qkv_ref, w_out_ref, modulation_ref, out_ref
):
    rows = tokens_ref.shape[0]
    first = block_index() * rows
    shift, scale, gate = modulation_rows(counts_ref, modulation_ref, first, rows)
    normed, _ = layer_norm(tokens_ref[...].astype(F32))
    hidden = (normed * (1.0 + scale) + shift).astype(BF16)
    q, k, v = (
        jnp.dot(hidden, w_qkv_ref[part], preferred_element_type=F32) for part in range(3)
    )
    d_mixed = (cotangent_ref[...].astype(F32) * gate).astype(BF16)
    d_attn = rows_dot(d_mixed, w_out_ref[...])
    low = lax.broadcasted_iota(jnp.int32, (rows, LANES), 1) < HEAD

    def beside(left, right):
        return jnp.where(low, left, right).astype(BF16)

    q_v = (beside(q, pltpu.roll(v, HEAD, 1)), beside(pltpu.roll(q, HEAD, 1), v))
    k_d = (beside(k, pltpu.roll(d_attn, HEAD, 1)), beside(pltpu.roll(k, HEAD, 1), d_attn))
    for place in range(out_ref.shape[0]):
        out_ref[place, :, 0:LANES] = q_v[place % 2]
        out_ref[place, :, LANES:] = k_d[place % 2]


def enter(counts, tokens, cotangent, w_parts, w_out, modulation, quad):
    return pl.pallas_call(
        enter_kernel,
        out_shape=jax.ShapeDtypeStruct((quad, tokens.shape[0], 2 * LANES), BF16),
        in_specs=[SMEM] + [VMEM] * 5,
        out_specs=VMEM,
        compiler_params=pltpu.CompilerParams(vmem_limit_bytes=ENTER_LIMIT),
    )(counts, tokens, cotangent, w_parts, w_out, modulation)


def attend_kernel(
    counts_ref,
    gains_ref,
    first_ref,
    quad_ref,
    second_ref,
    far_ref,
    kept_ref,
    sent_ref,
    qx_ref,
    kx_ref,
    vx_ref,
    dx_ref,
    kv_ref,
    s_ref,
    g_ref,
    p_ref,
    d_ref,
    dk_ref,
    dv_ref,
    done_ref,
):
    chunk = far_ref.shape[0]
    tile = 64
    own = 3
    slots = 7
    reach = 4
    half = lax.axis_index("yh")
    origin = (block_index() // 2 - own) * chunk
    own_at = own * chunk
    block_rows = chunk // 2
    row = lax.broadcasted_iota(jnp.int32, (block_rows, LANES), 0)
    low = lax.broadcasted_iota(jnp.int32, (1, LANES), 1) < HEAD
    starts, ends = image_bounds(counts_ref, HEAD)
    starts = starts - origin
    ends = ends - origin
    inv_root = 1.0 / math.sqrt(HEAD)
    log2_e = math.log2(math.e)

    def lower_mean(values):
        return jnp.sum(jnp.where(low, values, 0.0), axis=-1, keepdims=True) * (1.0 / HEAD)

    def normed(raw, gain):
        return (raw * lax.rsqrt(lower_mean(raw * raw) + EPS) * gain).astype(BF16).astype(F32)

    q_gain, k_gain = gains_ref[0:1, :], gains_ref[1:2, :]

    def place_block(source, begin):
        begin = pl.multiple_of(begin, block_rows)
        at = pl.ds(begin, block_rows)
        place = row + begin
        same = ((place >= starts) & (place < ends)).astype(F32)
        first = source[:, 0:LANES].astype(F32)
        second = source[:, LANES:].astype(F32)
        keys = normed(second, k_gain)
        qx_ref[at, :] = jnp.where(low, normed(first, q_gain) * inv_root, same * SAME_IMAGE).astype(BF16)
        kx_ref[at, :] = jnp.where(low, keys, same).astype(BF16)
        vx_ref[at, :] = jnp.where(low, 0.0, first).astype(BF16)
        dx_ref[at, :] = second.astype(BF16)
        kv_ref[:, at] = jnp.where(low, keys, first).T.astype(BF16)

    step_to_first = jnp.where(lax.rem(lax.axis_index("z"), 2) == 0, 2 * chunk, -2 * chunk)
    quad_at = own_at - half * chunk
    for block in range(4):
        at = slice(block * block_rows, (block + 1) * block_rows)
        begin = quad_at + block * block_rows
        place_block(quad_ref.at[at], begin)
        place_block(first_ref.at[at], begin + step_to_first)
        place_block(second_ref.at[at], begin - step_to_first)
    far_at = half * (slots - 1) * chunk
    place_block(far_ref.at[0:block_rows], far_at)
    place_block(far_ref.at[block_rows:chunk], far_at + block_rows)

    left_from = jnp.int32(0)
    right_to = jnp.int32(slots * chunk)
    total = -origin
    for image in range(counts_ref.shape[0]):
        left_from = jnp.where(total <= own_at, total, left_from)
        ended = total >= own_at + chunk
        total = total + counts_ref[image]
        right_to = jnp.where((total >= own_at + chunk) & jnp.logical_not(ended), total, right_to)
    left_chunk = jnp.clip(left_from // chunk, 0, slots - reach)
    right_chunk = jnp.clip((right_to - 1) // chunk - (reach - 1), 0, slots - reach)

    def by_eight(values):
        return values.reshape(values.shape[0] // 8, 8, values.shape[1])

    def softmax_parts(q_block, d_block, key_chunk, chunks, keep):
        highest = jnp.full((8, chunk), -jnp.inf, F32)
        for piece in range(chunks):
            begin = pl.multiple_of((key_chunk + piece) * chunk, chunk)
            keys_at = pl.ds(begin, chunk)
            at = slice(piece * chunk, (piece + 1) * chunk)
            scores = rows_dot(kx_ref[keys_at, :], q_block)
            s_ref[at, :] = scores
            highest = jnp.maximum(highest, jnp.max(by_eight(scores), axis=0))
            g_ref[at, :] = rows_dot(vx_ref[keys_at, :], d_block)
        highest = jnp.max(highest, axis=0, keepdims=True) * log2_e
        total = jnp.zeros((8, chunk), F32)
        grads = jnp.zeros((8, chunk), F32)
        for piece in range(chunks * chunk // tile):
            at = slice(piece * tile, (piece + 1) * tile)
            weights = jnp.exp2(s_ref[at, :] * log2_e - highest)
            if keep:
                s_ref[at, :] = weights
            total = total + jnp.sum(by_eight(weights), axis=0)
            grads = grads + jnp.sum(by_eight(weights * g_ref[at, :]), axis=0)
        scale = 1.0 / jnp.sum(total, axis=0, keepdims=True)
        mean_grad = jnp.sum(grads, axis=0, keepdims=True) * scale
        return highest, scale, mean_grad

    near = slice(own_at, own_at + chunk)
    q_own = qx_ref[near, :]
    d_own = dx_ref[near, :]
    _, scale, mean_grad = softmax_parts(q_own, d_own, jnp.int32(0), slots, True)
    for piece in range(slots * chunk // tile):
        at = slice(piece * tile, (piece + 1) * tile)
        probs = s_ref[at, :] * scale
        p_ref[at, :] = probs.astype(BF16)
        d_ref[at, :] = (probs * (g_ref[at, :] - mean_grad)).astype(BF16)
    dk_ref[...] = jnp.dot(d_ref[near, :], q_own, preferred_element_type=F32)
    dv_ref[...] = jnp.dot(p_ref[near, :], d_own, preferred_element_type=F32)
    result = jnp.dot(kv_ref[...], p_ref[...], preferred_element_type=F32)
    d_query = jnp.dot(kv_ref[...], d_ref[...], preferred_element_type=F32)
    upper = lax.broadcasted_iota(jnp.int32, (LANES, chunk), 0) < HEAD
    own_out = jnp.where(upper, d_query * inv_root, result).T

    query_lane = lax.broadcasted_iota(jnp.int32, (1, chunk), 1)

    def one_block(step, carry):
        slot = step + jnp.where(step >= own, 1, 0)
        begin = slot * chunk

        @pl.when((begin < right_to) & (begin + chunk > left_from))
        def _():
            at = pl.ds(pl.multiple_of(begin, chunk), chunk)
            key_chunk = jnp.where(slot < own, left_chunk, right_chunk)
            q_block = qx_ref[at, :]
            d_block = dx_ref[at, :]
            highest, scale, mean_grad = softmax_parts(q_block, d_block, key_chunk, reach, False)
            place = query_lane + begin
            scale = jnp.where((place >= left_from) & (place < right_to), scale, 0.0)
            for piece in range(chunk // tile):
                near_at = pl.multiple_of((own - key_chunk) * chunk + piece * tile, tile)
                near_at = pl.ds(near_at, tile)
                at = slice(piece * tile, (piece + 1) * tile)
                probs = jnp.exp2(s_ref[near_at, :] * log2_e - highest) * scale
                p_ref[at, :] = probs.astype(BF16)
                d_ref[at, :] = (probs * (g_ref[near_at, :] - mean_grad)).astype(BF16)
            dk_ref[...] += jnp.dot(d_ref[0:chunk, :], q_block, preferred_element_type=F32)
            dv_ref[...] += jnp.dot(p_ref[0:chunk, :], d_block, preferred_element_type=F32)

        return carry

    lax.fori_loop(0, slots - 1, one_block, 0)

    def norm_grad(raw, gain, d_norm):
        inverse = lax.rsqrt(lower_mean(raw * raw) + EPS)
        scaled = d_norm.astype(BF16).astype(F32) * gain
        inner = lower_mean(raw * scaled)
        return inverse * scaled - raw * (inverse * inverse * inverse * inner)

    own_in_quad = pl.ds(pl.multiple_of(half * chunk, chunk), chunk)
    raw_q = quad_ref[own_in_quad, 0:LANES].astype(F32)
    raw_k = quad_ref[own_in_quad, LANES:].astype(F32)
    d_q = norm_grad(raw_q, q_gain, own_out)
    d_k = norm_grad(raw_k, k_gain, dk_ref[...])
    done_ref[:, 0:LANES] = jnp.where(low, d_q, own_out).astype(BF16)
    done_ref[:, LANES:] = jnp.where(low, d_k, dv_ref[...]).astype(BF16)
    parity = lax.axis_index("yl")
    kept_ref[...] = done_ref[pl.ds(pl.multiple_of(parity * block_rows, block_rows), block_rows), :]
    sent_ref[...] = done_ref[
        pl.ds(pl.multiple_of((1 - parity) * block_rows, block_rows), block_rows), :
    ]


def attend_pair(counts, gains, first, quad, second, far):
    chunk = far.shape[0]
    rows = 7 * chunk
    half_out = jax.ShapeDtypeStruct((chunk // 2, 2 * LANES), BF16)
    return pl.pallas_call(
        attend_kernel,
        out_shape=(half_out, half_out),
        in_specs=[SMEM] + [VMEM] * 5,
        out_specs=(VMEM, VMEM),
        scratch_shapes=[pltpu.VMEM((rows, LANES), BF16)] * 4
        + [pltpu.VMEM((LANES, rows), BF16)]
        + [pltpu.VMEM((rows, chunk), F32)] * 2
        + [pltpu.VMEM((rows, chunk), BF16)] * 2
        + [pltpu.VMEM((chunk, LANES), F32)] * 2
        + [pltpu.VMEM((chunk, 2 * LANES), BF16)],
        compiler_params=pltpu.CompilerParams(vmem_limit_bytes=VMEM_LIMIT),
    )(counts, gains, first, quad, second, far)


def project_kernel(kept_ref, swapped_ref, w_out_ref, w_qkv_ref, out_ref):
    rows = kept_ref.shape[0]
    width = w_out_ref.shape[1]
    first = lax.axis_index("yl") == 0
    low = lax.broadcasted_iota(jnp.int32, (rows, LANES), 1) < HEAD
    kept = kept_ref[...].astype(F32)
    swapped = swapped_ref[...].astype(F32)
    head0 = jnp.where(first, kept, swapped)
    head1 = jnp.where(first, swapped, kept)
    a0, a1 = head0[:, :LANES], head1[:, :LANES]
    b0, b1 = head0[:, LANES:], head1[:, LANES:]
    d_q = jnp.where(low, a0, pltpu.roll(a1, HEAD, 1)).astype(BF16)
    attn = jnp.where(low, pltpu.roll(a0, HEAD, 1), a1).astype(BF16)
    d_k = jnp.where(low, b0, pltpu.roll(b1, HEAD, 1)).astype(BF16)
    d_v = jnp.where(low, pltpu.roll(b0, HEAD, 1), b1).astype(BF16)
    mixed = jnp.dot(attn, w_out_ref[...], preferred_element_type=F32)
    out_ref[:, :width] = mixed.astype(BF16)
    d_hidden = (
        rows_dot(d_q, w_qkv_ref[0]) + rows_dot(d_k, w_qkv_ref[1]) + rows_dot(d_v, w_qkv_ref[2])
    )
    out_ref[:, width:] = d_hidden.astype(BF16)


def project(kept, swapped, w_out, w_parts):
    return pl.pallas_call(
        project_kernel,
        out_shape=jax.ShapeDtypeStruct((kept.shape[0], 2 * w_out.shape[1]), BF16),
        in_specs=[VMEM] * 4,
        out_specs=VMEM,
        compiler_params=pltpu.CompilerParams(vmem_limit_bytes=VMEM_LIMIT),
    )(kept, swapped, w_out, w_parts)


def ready_kernel(
    counts_ref,
    tokens_ref,
    cotangent_ref,
    modulation_ref,
    rows_ref,
    factors_ref,
):
    rows = rows_ref.shape[1]
    first_row = (lax.axis_index("x") * 2 + lax.axis_index("core")) * rows
    first = block_index() * tokens_ref.shape[0] + first_row
    _, scale, gate = modulation_rows(counts_ref, modulation_ref, first, rows)
    at = pl.ds(pl.multiple_of(first_row, rows), rows)
    normed, inv_std = layer_norm(tokens_ref[at, :].astype(F32))
    rows_ref[0] = tokens_ref[at, :]
    rows_ref[1] = cotangent_ref[at, :]
    factors_ref[0] = gate
    factors_ref[1] = 1.0 + scale
    factors_ref[2] = normed
    factors_ref[3] = jnp.broadcast_to(inv_std, normed.shape)


def ready(counts, tokens, cotangent, modulation, share):
    width = tokens.shape[1]
    return pl.pallas_call(
        ready_kernel,
        out_shape=(
            jax.ShapeDtypeStruct((2, share, width), BF16),
            jax.ShapeDtypeStruct((4, share, width), F32),
        ),
        in_specs=[SMEM] + [VMEM] * 3,
        out_specs=(VMEM, VMEM),
        compiler_params=pltpu.CompilerParams(vmem_limit_bytes=VMEM_LIMIT),
    )(counts, tokens, cotangent, modulation)


def leave_kernel(rows_ref, factors_ref, shares_ref, layer_ref, grad_ref):
    width = layer_ref.shape[1]
    sums = shares_ref[0].astype(F32)
    for share in range(1, shares_ref.shape[0]):
        sums = sums + shares_ref[share].astype(F32)
    layer = rows_ref[0].astype(F32) + factors_ref[0] * sums[:, :width]
    layer_ref[...] = layer.astype(BF16)
    d_normed = sums[:, width:] * factors_ref[1]
    normed = factors_ref[2]
    input_grad = rows_ref[1].astype(F32) + factors_ref[3] * (
        d_normed
        - jnp.mean(d_normed, axis=-1, keepdims=True)
        - normed * jnp.mean(d_normed * normed, axis=-1, keepdims=True)
    )
    grad_ref[...] = input_grad.astype(BF16)


def leave(rows, factors, shares):
    out = jax.ShapeDtypeStruct(rows.shape[1:], BF16)
    return pl.pallas_call(
        leave_kernel,
        out_shape=(out, out),
        in_specs=[VMEM] * 3,
        out_specs=(VMEM, VMEM),
        compiler_params=pltpu.CompilerParams(vmem_limit_bytes=VMEM_LIMIT),
    )(rows, factors, shares)


def per_device(tokens, cotangent, w_qkv, w_out, qk_gain, modulation, image_counts):
    tok_rows, model_width = tokens.shape
    z_count = lax.axis_size("z")
    x_count = lax.axis_size("x")
    quad = 4
    pair_rows = 2 * tok_rows
    share = tok_rows // (2 * x_count)
    w_parts = w_qkv.transpose(1, 0, 2)
    mod_parts = modulation.transpose(1, 0, 2)
    gains = jnp.pad(qk_gain, ((0, 6), (0, LANES - HEAD)))

    heads = enter(image_counts, tokens, cotangent, w_parts, w_out, mod_parts, quad)
    mine = lax.all_to_all(heads, ("yh", "yl"), 0, 0)
    mine = mine.reshape(quad * tok_rows, 2 * LANES)
    evens = range(0, z_count, 2)
    swaps = [(i, i + 1) for i in evens], [((i - 1) % z_count, i) for i in evens]
    first, second = (
        lax.ppermute(mine, "z", pairs + [(j, i) for i, j in pairs]) for pairs in swaps
    )
    far_half = jnp.where(lax.axis_index("yh") == 0, mine[pair_rows:], mine[:pair_rows])
    halves = 2 * z_count
    far = lax.ppermute(
        far_half,
        ("z", "yh"),
        [(i, (i + (4 if i % 2 == 0 else -4)) % halves) for i in range(halves)],
    )
    _, tokens_late, cotangent_late, mod_late = lax.optimization_barrier(
        (mine, tokens, cotangent, mod_parts)
    )
    rows, factors = ready(image_counts, tokens_late, cotangent_late, mod_late, share)
    kept, sent = attend_pair(image_counts, gains, first, mine, second, far)
    swapped = lax.ppermute(sent, "yl", [(0, 1), (1, 0)])
    partial = project(kept, swapped, w_out, w_parts)
    shares = lax.all_to_all(
        partial.reshape(2 * x_count, share, 2 * model_width), ("x", "core"), 0, 0
    )
    return leave(rows, factors, shares)


def solution(mesh):
    split = jax.sharding.Mesh(mesh.devices.reshape(16, 2, 2, 4, 2), ("z", "yh", "yl", "x", "core"))
    dp, head = ("z", "yh", "yl"), ("x", "core")
    in_specs = (P(dp, None), P(dp, None), P(None, None, head), P(head, None), P(), P(), P())
    out_specs = (P(dp + head, None), P(dp + head, None))
    return jax.shard_map(
        per_device, mesh=split, in_specs=in_specs, out_specs=out_specs, check_vma=False
    )
```

```python
import math

import jax
import jax.numpy as jnp
from jax import lax
from jax.experimental import pallas as pl
from jax.experimental.pallas import tpu as pltpu
from jax.sharding import PartitionSpec as P

EPS = 1e-06
SAME_IMAGE = 512.0
LANES = 128
HEAD = 64
F32 = jnp.float32
BF16 = jnp.bfloat16
VMEM_LIMIT = 24 * 1024 * 1024
ENTER_LIMIT = 60 * 1024 * 1024
VMEM = pl.BlockSpec(memory_space=pltpu.VMEM)
SMEM = pl.BlockSpec(memory_space=pltpu.SMEM)


def rows_dot(a, b):
    return lax.dot_general(a, b, (((1,), (1,)), ((), ())), preferred_element_type=F32)


def block_index():
    return (lax.axis_index("z") * 2 + lax.axis_index("yh")) * 2 + lax.axis_index("yl")


def image_bounds(counts_ref, first_lane):
    lane = lax.broadcasted_iota(jnp.int32, (1, LANES), 1)
    starts = jnp.zeros((1, LANES), jnp.int32)
    ends = jnp.zeros((1, LANES), jnp.int32)
    total = jnp.int32(0)
    for image in range(counts_ref.shape[0]):
        here = lane == first_lane + image
        starts = jnp.where(here, total, starts)
        total = total + counts_ref[image]
        ends = jnp.where(here, total, ends)
    return starts, ends


def modulation_rows(counts_ref, modulation_ref, first, rows):
    starts, ends = image_bounds(counts_ref, 0)
    place = first + lax.broadcasted_iota(jnp.int32, (rows, LANES), 0)
    member = ((place >= starts) & (place < ends)).astype(F32).astype(BF16)
    member = member[:, : modulation_ref.shape[1]]
    return [
        jnp.dot(member, modulation_ref[part], preferred_element_type=F32) for part in range(3)
    ]


def layer_norm(values):
    average = jnp.mean(values, axis=-1, keepdims=True)
    centred = values - average
    inv_std = lax.rsqrt(jnp.mean(centred * centred, axis=-1, keepdims=True) + EPS)
    return centred * inv_std, inv_std


def enter_kernel(
    counts_ref, tokens_ref, cotangent_ref, w_qkv_ref, w_out_ref, modulation_ref, out_ref
):
    rows = tokens_ref.shape[0]
    first = block_index() * rows
    shift, scale, gate = modulation_rows(counts_ref, modulation_ref, first, rows)
    normed, _ = layer_norm(tokens_ref[...].astype(F32))
    hidden = (normed * (1.0 + scale) + shift).astype(BF16)
    q, k, v = (
        jnp.dot(hidden, w_qkv_ref[part], preferred_element_type=F32) for part in range(3)
    )
    d_mixed = (cotangent_ref[...].astype(F32) * gate).astype(BF16)
    d_attn = rows_dot(d_mixed, w_out_ref[...])
    low = lax.broadcasted_iota(jnp.int32, (rows, LANES), 1) < HEAD

    def beside(left, right):
        return jnp.where(low, left, right).astype(BF16)

    q_v = (beside(q, pltpu.roll(v, HEAD, 1)), beside(pltpu.roll(q, HEAD, 1), v))
    k_d = (beside(k, pltpu.roll(d_attn, HEAD, 1)), beside(pltpu.roll(k, HEAD, 1), d_attn))
    for place in range(out_ref.shape[0]):
        out_ref[place, :, 0:LANES] = q_v[place % 2]
        out_ref[place, :, LANES:] = k_d[place % 2]


def enter(counts, tokens, cotangent, w_parts, w_out, modulation, quad):
    return pl.pallas_call(
        enter_kernel,
        out_shape=jax.ShapeDtypeStruct((quad, tokens.shape[0], 2 * LANES), BF16),
        in_specs=[SMEM] + [VMEM] * 5,
        out_specs=VMEM,
        compiler_params=pltpu.CompilerParams(vmem_limit_bytes=ENTER_LIMIT),
    )(counts, tokens, cotangent, w_parts, w_out, modulation)


LOG2_E = math.log2(math.e)
INV_ROOT = 1.0 / math.sqrt(HEAD)
CHUNK = 256
TILE = 64
MAIN = 6
REACH_CHUNKS = 4


def low_lanes():
    return lax.broadcasted_iota(jnp.int32, (1, LANES), 1) < HEAD


def lower_mean(values):
    return jnp.sum(jnp.where(low_lanes(), values, 0.0), axis=-1, keepdims=True) * (1.0 / HEAD)


def place_block(source, place, starts, ends, gains_ref, stores):
    low = low_lanes()
    rows = source.shape[0]
    at = place + lax.broadcasted_iota(jnp.int32, (rows, LANES), 0)
    same = ((at >= starts) & (at < ends)).astype(F32)
    first = source[:, 0:LANES].astype(F32)
    second = source[:, LANES:].astype(F32)

    def normed(raw, gain):
        return (raw * lax.rsqrt(lower_mean(raw * raw) + EPS) * gain).astype(BF16).astype(F32)

    keys = normed(second, gains_ref[1:2, :])
    queries = normed(first, gains_ref[0:1, :]) * INV_ROOT
    q_store, k_store, v_store, d_store, kv_store = stores
    q_store[...] = jnp.where(low, queries, same * SAME_IMAGE).astype(BF16)
    k_store[...] = jnp.where(low, keys, same).astype(BF16)
    v_store[...] = jnp.where(low, 0.0, first).astype(BF16)
    d_store[...] = second.astype(BF16)
    kv_store[...] = jnp.where(low, keys, first).T.astype(BF16)


def window_facts(counts_ref):
    half = lax.axis_index("yh")
    origin = (block_index() // 4 - 1) * 2 * CHUNK
    own_at = (2 + half) * CHUNK
    starts, ends = image_bounds(counts_ref, HEAD)
    left_from = jnp.int32(-CHUNK)
    right_to = jnp.int32((MAIN + 1) * CHUNK)
    total = -origin
    for image in range(counts_ref.shape[0]):
        left_from = jnp.where(total <= own_at, total, left_from)
        ended = total >= own_at + CHUNK
        total = total + counts_ref[image]
        right_to = jnp.where((total >= own_at + CHUNK) & jnp.logical_not(ended), total, right_to)
    return half, own_at, starts - origin, ends - origin, left_from, right_to


def by_eight(values):
    return values.reshape(values.shape[0] // 8, 8, values.shape[1])


def add_tiles(s_ref, g_ref, rows, highest, total, grads):
    for piece in range(rows // TILE):
        at = slice(piece * TILE, (piece + 1) * TILE)
        weights = jnp.exp2(s_ref[at, :] * LOG2_E - highest)
        total = total + jnp.sum(by_eight(weights), axis=0)
        grads = grads + jnp.sum(by_eight(weights * g_ref[at, :]), axis=0)
    return total, grads


def rows_max(values):
    return jnp.max(by_eight(values), axis=0)


def near_kernel(
    counts_ref,
    gains_ref,
    first_ref,
    quad_ref,
    second_ref,
    qx_ref,
    kx_ref,
    vx_ref,
    dx_ref,
    kv_ref,
    so_ref,
    go_ref,
    sn_ref,
    gn_ref,
    stats_ref,
    s_ref,
    g_ref,
):
    half, own_at, starts, ends, left_from, right_to = window_facts(counts_ref)
    block_rows = CHUNK // 2

    def place(source, begin):
        begin = pl.multiple_of(begin, block_rows)
        at = pl.ds(begin, block_rows)
        stores = [ref.at[at, :] for ref in (qx_ref, kx_ref, vx_ref, dx_ref)]
        place_block(source, begin, starts, ends, gains_ref, stores + [kv_ref.at[:, at]])

    to_first = jnp.where(lax.rem(lax.axis_index("z"), 2) == 0, 2 * CHUNK, -2 * CHUNK)
    for block in range(4):
        at = slice(block * block_rows, (block + 1) * block_rows)
        begin = 2 * CHUNK + block * block_rows
        place(quad_ref.at[at], begin)
        place(first_ref.at[at], begin + to_first)
        place(second_ref.at[at], begin - to_first)

    own_rows = pl.ds(pl.multiple_of(own_at, CHUNK), CHUNK)
    q_own = qx_ref[own_rows, :]
    d_own = dx_ref[own_rows, :]
    highest = jnp.full((8, CHUNK), -jnp.inf, F32)
    for piece in range(MAIN):
        at = slice(piece * CHUNK, (piece + 1) * CHUNK)
        scores = rows_dot(kx_ref[at, :], q_own)
        so_ref[at, :] = scores
        highest = jnp.maximum(highest, rows_max(scores))
        go_ref[at, :] = rows_dot(vx_ref[at, :], d_own)
    stats_ref[MAIN, :, :] = highest

    left_key = jnp.clip((left_from + CHUNK) // CHUNK - 1, 0, MAIN - REACH_CHUNKS)
    right_key = jnp.clip((right_to - 1) // CHUNK - (REACH_CHUNKS - 1), 0, MAIN - REACH_CHUNKS)

    def one_chunk(step, carry):
        slot = step + jnp.where(step >= 2 + half, 1, 0)
        begin = slot * CHUNK

        @pl.when((begin < right_to) & (begin + CHUNK > left_from))
        def _():
            at = pl.ds(pl.multiple_of(begin, CHUNK), CHUNK)
            key = jnp.where(begin < own_at, left_key, right_key) * CHUNK
            q_block = qx_ref[at, :]
            d_block = dx_ref[at, :]
            highest = jnp.full((8, CHUNK), -jnp.inf, F32)
            for piece in range(REACH_CHUNKS):
                keys_at = pl.ds(pl.multiple_of(key + piece * CHUNK, CHUNK), CHUNK)
                here = slice(piece * CHUNK, (piece + 1) * CHUNK)
                scores = rows_dot(kx_ref[keys_at, :], q_block)
                s_ref[here, :] = scores
                highest = jnp.maximum(highest, rows_max(scores))
                g_ref[here, :] = rows_dot(vx_ref[keys_at, :], d_block)
            highest = jnp.max(highest, axis=0, keepdims=True) * LOG2_E
            zeros = jnp.zeros((8, CHUNK), F32)
            total, grads = add_tiles(s_ref, g_ref, REACH_CHUNKS * CHUNK, highest, zeros, zeros)
            stats_ref[slot, 0:1, :] = highest
            stats_ref[slot, 1:2, :] = jnp.sum(total, axis=0, keepdims=True)
            stats_ref[slot, 2:3, :] = jnp.sum(grads, axis=0, keepdims=True)
            near_at = pl.ds(pl.multiple_of(own_at - key, CHUNK), CHUNK)
            sn_ref[slot, :, :] = s_ref[near_at, :]
            gn_ref[slot, :, :] = g_ref[near_at, :]

        return carry

    lax.fori_loop(0, MAIN - 1, one_chunk, 0)


def attend_near(counts, gains, first, quad, second):
    rows = MAIN * CHUNK
    head_rows = jax.ShapeDtypeStruct((rows, LANES), BF16)
    scores = jax.ShapeDtypeStruct((rows, CHUNK), F32)
    tiles = jax.ShapeDtypeStruct((MAIN, CHUNK, CHUNK), F32)
    return pl.pallas_call(
        near_kernel,
        out_shape=(head_rows,) * 4
        + (jax.ShapeDtypeStruct((LANES, rows), BF16),)
        + (scores, scores, tiles, tiles, jax.ShapeDtypeStruct((MAIN + 1, 8, CHUNK), F32)),
        in_specs=[SMEM] + [VMEM] * 4,
        out_specs=(VMEM,) * 10,
        scratch_shapes=[pltpu.VMEM((REACH_CHUNKS * CHUNK, CHUNK), F32)] * 2,
        compiler_params=pltpu.CompilerParams(vmem_limit_bytes=VMEM_LIMIT),
    )(counts, gains, first, quad, second)


def far_kernel(
    counts_ref,
    gains_ref,
    far_ref,
    quad_ref,
    qx_ref,
    kx_ref,
    vx_ref,
    dx_ref,
    kv_ref,
    so_ref,
    go_ref,
    sn_ref,
    gn_ref,
    stats_ref,
    kept_ref,
    sent_ref,
    qf_ref,
    kf_ref,
    vf_ref,
    df_ref,
    kvf_ref,
    s_ref,
    g_ref,
    p_ref,
    d_ref,
    sums_ref,
    dk_ref,
    dv_ref,
    done_ref,
):
    half, own_at, starts, ends, left_from, right_to = window_facts(counts_ref)
    block_rows = CHUNK // 2
    rows = MAIN * CHUNK
    far_at = jnp.where(half == 0, -CHUNK, rows)
    for block in range(2):
        at = slice(block * block_rows, (block + 1) * block_rows)
        stores = [ref.at[at, :] for ref in (qf_ref, kf_ref, vf_ref, df_ref)]
        place_block(
            far_ref.at[at],
            far_at + block * block_rows,
            starts,
            ends,
            gains_ref,
            stores + [kvf_ref.at[:, at]],
        )

    own_rows = pl.ds(pl.multiple_of(own_at, CHUNK), CHUNK)
    q_own = qx_ref[own_rows, :]
    d_own = dx_ref[own_rows, :]
    scores = rows_dot(kf_ref[...], q_own)
    s_ref[0:CHUNK, :] = scores
    g_ref[0:CHUNK, :] = rows_dot(vf_ref[...], d_own)
    highest = jnp.maximum(stats_ref[MAIN, :, :], rows_max(scores))
    highest = jnp.max(highest, axis=0, keepdims=True) * LOG2_E
    zeros = jnp.zeros((8, CHUNK), F32)
    total, grads = add_tiles(so_ref, go_ref, rows, highest, zeros, zeros)
    total, grads = add_tiles(s_ref, g_ref, CHUNK, highest, total, grads)
    scale = 1.0 / jnp.sum(total, axis=0, keepdims=True)
    mean_grad = jnp.sum(grads, axis=0, keepdims=True) * scale

    def write_tile(scores, grads, highest, scale, mean_grad, to):
        probs = jnp.exp2(scores * LOG2_E - highest) * scale
        p_ref[to, :] = probs.astype(BF16)
        d_ref[to, :] = (probs * (grads - mean_grad)).astype(BF16)

    for piece in range(rows // TILE):
        at = slice(piece * TILE, (piece + 1) * TILE)
        write_tile(so_ref[at, :], go_ref[at, :], highest, scale, mean_grad, at)
    for piece in range(CHUNK // TILE):
        at = slice(piece * TILE, (piece + 1) * TILE)
        to = slice(rows + piece * TILE, rows + (piece + 1) * TILE)
        write_tile(s_ref[at, :], g_ref[at, :], highest, scale, mean_grad, to)
    dk_ref[...] = jnp.dot(d_ref[own_rows, :], q_own, preferred_element_type=F32)
    dv_ref[...] = jnp.dot(p_ref[own_rows, :], d_own, preferred_element_type=F32)

    def times_window(values_ref):
        main = jnp.dot(kv_ref[...], values_ref[0:rows, :], preferred_element_type=F32)
        return main + jnp.dot(
            kvf_ref[...], values_ref[rows : rows + CHUNK, :], preferred_element_type=F32
        )

    upper = lax.broadcasted_iota(jnp.int32, (LANES, CHUNK), 0) < HEAD
    own_out = jnp.where(upper, times_window(d_ref) * INV_ROOT, times_window(p_ref)).T

    query_lane = lax.broadcasted_iota(jnp.int32, (1, CHUNK), 1)
    reaches_far = jnp.where(half == 0, left_from < 0, right_to > rows)

    def add_gradients(tiles, begin, q_block, d_block, highest, total, grads):
        place = query_lane + begin
        scale = jnp.where((place >= left_from) & (place < right_to), 1.0 / total, 0.0)
        mean_grad = grads * scale
        for piece in range(CHUNK // TILE):
            scores, given = tiles(piece)
            at = slice(piece * TILE, (piece + 1) * TILE)
            write_tile(scores, given, highest, scale, mean_grad, at)
        dk_ref[...] += jnp.dot(d_ref[0:CHUNK, :], q_block, preferred_element_type=F32)
        dv_ref[...] += jnp.dot(p_ref[0:CHUNK, :], d_block, preferred_element_type=F32)

    def one_chunk(step, carry):
        slot = step + jnp.where(step >= 2 + half, 1, 0)
        begin = slot * CHUNK

        @pl.when((begin < right_to) & (begin + CHUNK > left_from))
        def _():
            at = pl.ds(pl.multiple_of(begin, CHUNK), CHUNK)
            q_block = qx_ref[at, :]
            d_block = dx_ref[at, :]
            sums_ref[...] = stats_ref[slot, :, :]
            same_side = (begin < own_at) == (half == 0)

            @pl.when(reaches_far & same_side)
            def _():
                scores = rows_dot(kf_ref[...], q_block)
                s_ref[0:CHUNK, :] = scores
                g_ref[0:CHUNK, :] = rows_dot(vf_ref[...], d_block)
                before = sums_ref[0:1, :]
                highest = jnp.max(rows_max(scores), axis=0, keepdims=True) * LOG2_E
                highest = jnp.maximum(before, highest)
                total, grads = add_tiles(s_ref, g_ref, CHUNK, highest, zeros, zeros)
                shrink = jnp.exp2(before - highest)
                sums_ref[0:1, :] = highest
                total = jnp.sum(total, axis=0, keepdims=True)
                grads = jnp.sum(grads, axis=0, keepdims=True)
                sums_ref[1:2, :] = sums_ref[1:2, :] * shrink + total
                sums_ref[2:3, :] = sums_ref[2:3, :] * shrink + grads

            def tiles(piece):
                at = slice(piece * TILE, (piece + 1) * TILE)
                return sn_ref[slot, at, :], gn_ref[slot, at, :]

            add_gradients(
                tiles, begin, q_block, d_block, sums_ref[0:1, :], sums_ref[1:2, :], sums_ref[2:3, :]
            )

        return carry

    lax.fori_loop(0, MAIN - 1, one_chunk, 0)

    @pl.when(reaches_far)
    def _():
        q_block = qf_ref[...]
        d_block = df_ref[...]
        key = half * (MAIN // 2) * CHUNK
        highest = jnp.full((8, CHUNK), -jnp.inf, F32)
        for piece in range(REACH_CHUNKS):
            here = slice(piece * CHUNK, (piece + 1) * CHUNK)
            if piece < REACH_CHUNKS - 1:
                keys_at = pl.ds(pl.multiple_of(key + piece * CHUNK, CHUNK), CHUNK)
                keys, values = kx_ref[keys_at, :], vx_ref[keys_at, :]
            else:
                keys, values = kf_ref[...], vf_ref[...]
            scores = rows_dot(keys, q_block)
            s_ref[here, :] = scores
            highest = jnp.maximum(highest, rows_max(scores))
            g_ref[here, :] = rows_dot(values, d_block)
        highest = jnp.max(highest, axis=0, keepdims=True) * LOG2_E
        total, grads = add_tiles(s_ref, g_ref, REACH_CHUNKS * CHUNK, highest, zeros, zeros)

        def tiles(piece):
            at = pl.ds(pl.multiple_of(own_at - key + piece * TILE, TILE), TILE)
            return s_ref[at, :], g_ref[at, :]

        add_gradients(
            tiles,
            far_at,
            q_block,
            d_block,
            highest,
            jnp.sum(total, axis=0, keepdims=True),
            jnp.sum(grads, axis=0, keepdims=True),
        )

    def norm_grad(raw, gain, d_norm):
        inverse = lax.rsqrt(lower_mean(raw * raw) + EPS)
        scaled = d_norm.astype(BF16).astype(F32) * gain
        inner = lower_mean(raw * scaled)
        return inverse * scaled - raw * (inverse * inverse * inverse * inner)

    low = low_lanes()
    own_in_quad = pl.ds(pl.multiple_of(half * CHUNK, CHUNK), CHUNK)
    raw_q = quad_ref[own_in_quad, 0:LANES].astype(F32)
    raw_k = quad_ref[own_in_quad, LANES:].astype(F32)
    d_q = norm_grad(raw_q, gains_ref[0:1, :], own_out)
    d_k = norm_grad(raw_k, gains_ref[1:2, :], dk_ref[...])
    done_ref[:, 0:LANES] = jnp.where(low, d_q, own_out).astype(BF16)
    done_ref[:, LANES:] = jnp.where(low, d_k, dv_ref[...]).astype(BF16)
    parity = lax.axis_index("yl")
    kept_ref[...] = done_ref[pl.ds(pl.multiple_of(parity * block_rows, block_rows), block_rows), :]
    sent_ref[...] = done_ref[
        pl.ds(pl.multiple_of((1 - parity) * block_rows, block_rows), block_rows), :
    ]


def attend_far(counts, gains, far, quad, near_parts):
    half_out = jax.ShapeDtypeStruct((CHUNK // 2, 2 * LANES), BF16)
    return pl.pallas_call(
        far_kernel,
        out_shape=(half_out, half_out),
        in_specs=[SMEM] + [VMEM] * (3 + len(near_parts)),
        out_specs=(VMEM, VMEM),
        scratch_shapes=[pltpu.VMEM((CHUNK, LANES), BF16)] * 4
        + [pltpu.VMEM((LANES, CHUNK), BF16)]
        + [pltpu.VMEM((REACH_CHUNKS * CHUNK, CHUNK), F32)] * 2
        + [pltpu.VMEM(((MAIN + 1) * CHUNK, CHUNK), BF16)] * 2
        + [pltpu.VMEM((8, CHUNK), F32)]
        + [pltpu.VMEM((CHUNK, LANES), F32)] * 2
        + [pltpu.VMEM((CHUNK, 2 * LANES), BF16)],
        compiler_params=pltpu.CompilerParams(vmem_limit_bytes=VMEM_LIMIT),
    )(counts, gains, far, quad, *near_parts)


def project_kernel(kept_ref, swapped_ref, w_out_ref, w_qkv_ref, out_ref):
    rows = kept_ref.shape[0]
    width = w_out_ref.shape[1]
    first = lax.axis_index("yl") == 0
    low = lax.broadcasted_iota(jnp.int32, (rows, LANES), 1) < HEAD
    kept = kept_ref[...].astype(F32)
    swapped = swapped_ref[...].astype(F32)
    head0 = jnp.where(first, kept, swapped)
    head1 = jnp.where(first, swapped, kept)
    a0, a1 = head0[:, :LANES], head1[:, :LANES]
    b0, b1 = head0[:, LANES:], head1[:, LANES:]
    d_q = jnp.where(low, a0, pltpu.roll(a1, HEAD, 1)).astype(BF16)
    attn = jnp.where(low, pltpu.roll(a0, HEAD, 1), a1).astype(BF16)
    d_k = jnp.where(low, b0, pltpu.roll(b1, HEAD, 1)).astype(BF16)
    d_v = jnp.where(low, pltpu.roll(b0, HEAD, 1), b1).astype(BF16)
    mixed = jnp.dot(attn, w_out_ref[...], preferred_element_type=F32)
    out_ref[:, :width] = mixed.astype(BF16)
    d_hidden = (
        rows_dot(d_q, w_qkv_ref[0]) + rows_dot(d_k, w_qkv_ref[1]) + rows_dot(d_v, w_qkv_ref[2])
    )
    out_ref[:, width:] = d_hidden.astype(BF16)


def project(kept, swapped, w_out, w_parts):
    return pl.pallas_call(
        project_kernel,
        out_shape=jax.ShapeDtypeStruct((kept.shape[0], 2 * w_out.shape[1]), BF16),
        in_specs=[VMEM] * 4,
        out_specs=VMEM,
        compiler_params=pltpu.CompilerParams(vmem_limit_bytes=VMEM_LIMIT),
    )(kept, swapped, w_out, w_parts)


def ready_kernel(
    counts_ref,
    tokens_ref,
    cotangent_ref,
    modulation_ref,
    rows_ref,
    factors_ref,
):
    rows = rows_ref.shape[1]
    first_row = (lax.axis_index("x") * 2 + lax.axis_index("core")) * rows
    first = block_index() * tokens_ref.shape[0] + first_row
    _, scale, gate = modulation_rows(counts_ref, modulation_ref, first, rows)
    at = pl.ds(pl.multiple_of(first_row, rows), rows)
    normed, inv_std = layer_norm(tokens_ref[at, :].astype(F32))
    rows_ref[0] = tokens_ref[at, :]
    rows_ref[1] = cotangent_ref[at, :]
    factors_ref[0] = gate
    factors_ref[1] = 1.0 + scale
    factors_ref[2] = normed
    factors_ref[3] = jnp.broadcast_to(inv_std, normed.shape)


def ready(counts, tokens, cotangent, modulation, share):
    width = tokens.shape[1]
    return pl.pallas_call(
        ready_kernel,
        out_shape=(
            jax.ShapeDtypeStruct((2, share, width), BF16),
            jax.ShapeDtypeStruct((4, share, width), F32),
        ),
        in_specs=[SMEM] + [VMEM] * 3,
        out_specs=(VMEM, VMEM),
        compiler_params=pltpu.CompilerParams(vmem_limit_bytes=VMEM_LIMIT),
    )(counts, tokens, cotangent, modulation)


def leave_kernel(rows_ref, factors_ref, shares_ref, layer_ref, grad_ref):
    width = layer_ref.shape[1]
    sums = shares_ref[0].astype(F32)
    for share in range(1, shares_ref.shape[0]):
        sums = sums + shares_ref[share].astype(F32)
    layer = rows_ref[0].astype(F32) + factors_ref[0] * sums[:, :width]
    layer_ref[...] = layer.astype(BF16)
    d_normed = sums[:, width:] * factors_ref[1]
    normed = factors_ref[2]
    input_grad = rows_ref[1].astype(F32) + factors_ref[3] * (
        d_normed
        - jnp.mean(d_normed, axis=-1, keepdims=True)
        - normed * jnp.mean(d_normed * normed, axis=-1, keepdims=True)
    )
    grad_ref[...] = input_grad.astype(BF16)


def leave(rows, factors, shares):
    out = jax.ShapeDtypeStruct(rows.shape[1:], BF16)
    return pl.pallas_call(
        leave_kernel,
        out_shape=(out, out),
        in_specs=[VMEM] * 3,
        out_specs=(VMEM, VMEM),
        compiler_params=pltpu.CompilerParams(vmem_limit_bytes=VMEM_LIMIT),
    )(rows, factors, shares)


def per_device(tokens, cotangent, w_qkv, w_out, qk_gain, modulation, image_counts):
    tok_rows, model_width = tokens.shape
    z_count = lax.axis_size("z")
    x_count = lax.axis_size("x")
    quad = 4
    pair_rows = 2 * tok_rows
    share = tok_rows // (2 * x_count)
    w_parts = w_qkv.transpose(1, 0, 2)
    mod_parts = modulation.transpose(1, 0, 2)
    gains = jnp.pad(qk_gain, ((0, 6), (0, LANES - HEAD)))

    heads = enter(image_counts, tokens, cotangent, w_parts, w_out, mod_parts, quad)
    mine = lax.all_to_all(heads, ("yh", "yl"), 0, 0)
    mine = mine.reshape(quad * tok_rows, 2 * LANES)
    evens = range(0, z_count, 2)
    swaps = [(i, i + 1) for i in evens], [((i - 1) % z_count, i) for i in evens]
    first, second = (
        lax.ppermute(mine, "z", pairs + [(j, i) for i, j in pairs]) for pairs in swaps
    )
    far_half = jnp.where(lax.axis_index("yh") == 0, mine[pair_rows:], mine[:pair_rows])
    halves = 2 * z_count
    far = lax.ppermute(
        far_half,
        ("z", "yh"),
        [(i, (i + (4 if i % 2 == 0 else -4)) % halves) for i in range(halves)],
    )
    _, tokens_late, cotangent_late, mod_late = lax.optimization_barrier(
        (mine, tokens, cotangent, mod_parts)
    )
    rows, factors = ready(image_counts, tokens_late, cotangent_late, mod_late, share)
    near_parts = attend_near(image_counts, gains, first, mine, second)
    kept, sent = attend_far(image_counts, gains, far, mine, near_parts)
    swapped = lax.ppermute(sent, "yl", [(0, 1), (1, 0)])
    partial = project(kept, swapped, w_out, w_parts)
    shares = lax.all_to_all(
        partial.reshape(2 * x_count, share, 2 * model_width), ("x", "core"), 0, 0
    )
    return leave(rows, factors, shares)


def solution(mesh):
    split = jax.sharding.Mesh(mesh.devices.reshape(16, 2, 2, 4, 2), ("z", "yh", "yl", "x", "core"))
    dp, head = ("z", "yh", "yl"), ("x", "core")
    in_specs = (P(dp, None), P(dp, None), P(None, None, head), P(head, None), P(), P(), P())
    out_specs = (P(dp + head, None), P(dp + head, None))
    return jax.shard_map(
        per_device, mesh=split, in_specs=in_specs, out_specs=out_specs, check_vma=False
    )
```

```python
import math

import jax
import jax.numpy as jnp
from jax import lax
from jax.experimental import pallas as pl
from jax.experimental.pallas import tpu as pltpu
from jax.sharding import PartitionSpec as P

EPS = 1e-06
SAME_IMAGE = 512.0
LANES = 128
HEAD = 64
F32 = jnp.float32
BF16 = jnp.bfloat16
VMEM_LIMIT = 24 * 1024 * 1024
ENTER_LIMIT = 60 * 1024 * 1024
VMEM = pl.BlockSpec(memory_space=pltpu.VMEM)
SMEM = pl.BlockSpec(memory_space=pltpu.SMEM)


def rows_dot(a, b):
    return lax.dot_general(a, b, (((1,), (1,)), ((), ())), preferred_element_type=F32)


def block_index():
    return (lax.axis_index("z") * 2 + lax.axis_index("yh")) * 2 + lax.axis_index("yl")


def image_bounds(counts_ref, first_lane):
    lane = lax.broadcasted_iota(jnp.int32, (1, LANES), 1)
    starts = jnp.zeros((1, LANES), jnp.int32)
    ends = jnp.zeros((1, LANES), jnp.int32)
    total = jnp.int32(0)
    for image in range(counts_ref.shape[0]):
        here = lane == first_lane + image
        starts = jnp.where(here, total, starts)
        total = total + counts_ref[image]
        ends = jnp.where(here, total, ends)
    return starts, ends


def modulation_rows(counts_ref, modulation_ref, first, rows):
    starts, ends = image_bounds(counts_ref, 0)
    place = first + lax.broadcasted_iota(jnp.int32, (rows, LANES), 0)
    member = ((place >= starts) & (place < ends)).astype(F32).astype(BF16)
    member = member[:, : modulation_ref.shape[1]]
    return [
        jnp.dot(member, modulation_ref[part], preferred_element_type=F32) for part in range(3)
    ]


def layer_norm(values):
    average = jnp.mean(values, axis=-1, keepdims=True)
    centred = values - average
    inv_std = lax.rsqrt(jnp.mean(centred * centred, axis=-1, keepdims=True) + EPS)
    return centred * inv_std, inv_std


def enter_kernel(
    counts_ref, tokens_ref, cotangent_ref, w_qkv_ref, w_out_ref, modulation_ref, out_ref
):
    rows = tokens_ref.shape[0]
    first = block_index() * rows
    shift, scale, gate = modulation_rows(counts_ref, modulation_ref, first, rows)
    normed, _ = layer_norm(tokens_ref[...].astype(F32))
    hidden = (normed * (1.0 + scale) + shift).astype(BF16)
    q, k, v = (
        jnp.dot(hidden, w_qkv_ref[part], preferred_element_type=F32) for part in range(3)
    )
    d_mixed = (cotangent_ref[...].astype(F32) * gate).astype(BF16)
    d_attn = rows_dot(d_mixed, w_out_ref[...])
    low = lax.broadcasted_iota(jnp.int32, (rows, LANES), 1) < HEAD

    def beside(left, right):
        return jnp.where(low, left, right).astype(BF16)

    q_v = (beside(q, pltpu.roll(v, HEAD, 1)), beside(pltpu.roll(q, HEAD, 1), v))
    k_d = (beside(k, pltpu.roll(d_attn, HEAD, 1)), beside(pltpu.roll(k, HEAD, 1), d_attn))
    for place in range(out_ref.shape[0]):
        out_ref[place, :, 0:LANES] = q_v[place % 2]
        out_ref[place, :, LANES:] = k_d[place % 2]


def enter(counts, tokens, cotangent, w_parts, w_out, modulation, quad):
    return pl.pallas_call(
        enter_kernel,
        out_shape=jax.ShapeDtypeStruct((quad, tokens.shape[0], 2 * LANES), BF16),
        in_specs=[SMEM] + [VMEM] * 5,
        out_specs=VMEM,
        compiler_params=pltpu.CompilerParams(vmem_limit_bytes=ENTER_LIMIT),
    )(counts, tokens, cotangent, w_parts, w_out, modulation)


LOG2_E = math.log2(math.e)
INV_ROOT = 1.0 / math.sqrt(HEAD)
CHUNK = 256
TILE = 64
MAIN = 6
REACH_CHUNKS = 4


def low_lanes():
    return lax.broadcasted_iota(jnp.int32, (1, LANES), 1) < HEAD


def lower_mean(values):
    return jnp.sum(jnp.where(low_lanes(), values, 0.0), axis=-1, keepdims=True) * (1.0 / HEAD)


def lower_sums(values):
    ones = (lax.broadcasted_iota(jnp.int32, (LANES, LANES), 0) < HEAD).astype(F32).astype(BF16)
    squares = values * values
    large = squares.astype(BF16)
    small = (squares - large.astype(F32)).astype(BF16)
    large = jnp.dot(large, ones, preferred_element_type=F32)
    return large + jnp.dot(small, ones, preferred_element_type=F32)


def place_block(source, place, starts, ends, gains_ref, stores):
    low = low_lanes()
    rows = source.shape[0]
    at = place + lax.broadcasted_iota(jnp.int32, (rows, LANES), 0)
    same = ((at >= starts) & (at < ends)).astype(F32)
    first = source[:, 0:LANES].astype(F32)
    second = source[:, LANES:].astype(F32)

    def normed(raw, gain):
        mean = lower_sums(raw) * (1.0 / HEAD)
        return (raw * lax.rsqrt(mean + EPS) * gain).astype(BF16).astype(F32)

    keys = normed(second, gains_ref[1:2, :])
    queries = normed(first, gains_ref[0:1, :]) * INV_ROOT
    q_store, k_store, v_store, d_store, kv_store = stores
    q_store[...] = jnp.where(low, queries, same * SAME_IMAGE).astype(BF16)
    k_store[...] = jnp.where(low, keys, same).astype(BF16)
    v_store[...] = jnp.where(low, 0.0, first).astype(BF16)
    d_store[...] = second.astype(BF16)
    kv_store[...] = jnp.where(low, keys, first).astype(BF16).T


def window_facts(counts_ref):
    half = lax.axis_index("yh")
    origin = (block_index() // 4 - 1) * 2 * CHUNK
    own_at = (2 + half) * CHUNK
    starts, ends = image_bounds(counts_ref, HEAD)
    left_from = jnp.int32(-CHUNK)
    right_to = jnp.int32((MAIN + 1) * CHUNK)
    total = -origin
    for image in range(counts_ref.shape[0]):
        left_from = jnp.where(total <= own_at, total, left_from)
        ended = total >= own_at + CHUNK
        total = total + counts_ref[image]
        right_to = jnp.where((total >= own_at + CHUNK) & jnp.logical_not(ended), total, right_to)
    return half, own_at, starts - origin, ends - origin, left_from, right_to


def by_eight(values):
    return values.reshape(values.shape[0] // 8, 8, values.shape[1])


def add_tiles(s_ref, g_ref, rows, highest, total, grads):
    for piece in range(rows // TILE):
        at = slice(piece * TILE, (piece + 1) * TILE)
        weights = jnp.exp2(s_ref[at, :] * LOG2_E - highest)
        total = total + jnp.sum(by_eight(weights), axis=0)
        grads = grads + jnp.sum(by_eight(weights * g_ref[at, :]), axis=0)
    return total, grads


def rows_max(values):
    return jnp.max(by_eight(values), axis=0)


def near_kernel(
    counts_ref,
    gains_ref,
    first_ref,
    quad_ref,
    second_ref,
    qx_ref,
    kx_ref,
    vx_ref,
    dx_ref,
    kv_ref,
    so_ref,
    go_ref,
    sn_ref,
    gn_ref,
    stats_ref,
    s_ref,
    g_ref,
):
    half, own_at, starts, ends, left_from, right_to = window_facts(counts_ref)
    block_rows = CHUNK // 2

    def place(source, begin):
        begin = pl.multiple_of(begin, block_rows)
        at = pl.ds(begin, block_rows)
        stores = [ref.at[at, :] for ref in (qx_ref, kx_ref, vx_ref, dx_ref)]
        place_block(source, begin, starts, ends, gains_ref, stores + [kv_ref.at[:, at]])

    to_first = jnp.where(lax.rem(lax.axis_index("z"), 2) == 0, 2 * CHUNK, -2 * CHUNK)
    for block in range(4):
        at = slice(block * block_rows, (block + 1) * block_rows)
        begin = 2 * CHUNK + block * block_rows
        place(quad_ref.at[at], begin)
        place(first_ref.at[at], begin + to_first)
        place(second_ref.at[at], begin - to_first)

    own_rows = pl.ds(pl.multiple_of(own_at, CHUNK), CHUNK)
    q_own = qx_ref[own_rows, :]
    d_own = dx_ref[own_rows, :]
    highest = jnp.full((8, CHUNK), -jnp.inf, F32)
    for piece in range(MAIN):
        at = slice(piece * CHUNK, (piece + 1) * CHUNK)
        scores = rows_dot(kx_ref[at, :], q_own)
        so_ref[at, :] = scores
        highest = jnp.maximum(highest, rows_max(scores))
        go_ref[at, :] = rows_dot(vx_ref[at, :], d_own)
    stats_ref[MAIN, :, :] = highest

    left_key = jnp.clip((left_from + CHUNK) // CHUNK - 1, 0, MAIN - REACH_CHUNKS)
    right_key = jnp.clip((right_to - 1) // CHUNK - (REACH_CHUNKS - 1), 0, MAIN - REACH_CHUNKS)

    def one_chunk(step, carry):
        slot = step + jnp.where(step >= 2 + half, 1, 0)
        begin = slot * CHUNK

        @pl.when((begin < right_to) & (begin + CHUNK > left_from))
        def _():
            at = pl.ds(pl.multiple_of(begin, CHUNK), CHUNK)
            key = jnp.where(begin < own_at, left_key, right_key) * CHUNK
            q_block = qx_ref[at, :]
            d_block = dx_ref[at, :]
            highest = jnp.full((8, CHUNK), -jnp.inf, F32)
            for piece in range(REACH_CHUNKS):
                keys_at = pl.ds(pl.multiple_of(key + piece * CHUNK, CHUNK), CHUNK)
                here = slice(piece * CHUNK, (piece + 1) * CHUNK)
                scores = rows_dot(kx_ref[keys_at, :], q_block)
                s_ref[here, :] = scores
                highest = jnp.maximum(highest, rows_max(scores))
                g_ref[here, :] = rows_dot(vx_ref[keys_at, :], d_block)
            highest = jnp.max(highest, axis=0, keepdims=True) * LOG2_E
            zeros = jnp.zeros((8, CHUNK), F32)
            total, grads = add_tiles(s_ref, g_ref, REACH_CHUNKS * CHUNK, highest, zeros, zeros)
            stats_ref[slot, 0:1, :] = highest
            stats_ref[slot, 1:2, :] = jnp.sum(total, axis=0, keepdims=True)
            stats_ref[slot, 2:3, :] = jnp.sum(grads, axis=0, keepdims=True)
            near_at = pl.ds(pl.multiple_of(own_at - key, CHUNK), CHUNK)
            sn_ref[slot, :, :] = s_ref[near_at, :]
            gn_ref[slot, :, :] = g_ref[near_at, :]

        return carry

    lax.fori_loop(0, MAIN - 1, one_chunk, 0)


def attend_near(counts, gains, first, quad, second):
    rows = MAIN * CHUNK
    head_rows = jax.ShapeDtypeStruct((rows, LANES), BF16)
    scores = jax.ShapeDtypeStruct((rows, CHUNK), F32)
    tiles = jax.ShapeDtypeStruct((MAIN, CHUNK, CHUNK), F32)
    return pl.pallas_call(
        near_kernel,
        out_shape=(head_rows,) * 4
        + (jax.ShapeDtypeStruct((LANES, rows), BF16),)
        + (scores, scores, tiles, tiles, jax.ShapeDtypeStruct((MAIN + 1, 8, CHUNK), F32)),
        in_specs=[SMEM] + [VMEM] * 4,
        out_specs=(VMEM,) * 10,
        scratch_shapes=[pltpu.VMEM((REACH_CHUNKS * CHUNK, CHUNK), F32)] * 2,
        cost_estimate=pl.CostEstimate(
            flops=10000000000, bytes_accessed=1 << 20, transcendentals=1 << 20
        ),
        compiler_params=pltpu.CompilerParams(vmem_limit_bytes=VMEM_LIMIT),
    )(counts, gains, first, quad, second)


def far_kernel(
    counts_ref,
    gains_ref,
    far_ref,
    quad_ref,
    qx_ref,
    kx_ref,
    vx_ref,
    dx_ref,
    kv_ref,
    so_ref,
    go_ref,
    sn_ref,
    gn_ref,
    stats_ref,
    out_ref,
    qf_ref,
    kf_ref,
    vf_ref,
    df_ref,
    kvf_ref,
    s_ref,
    g_ref,
    p_ref,
    d_ref,
    sums_ref,
    dk_ref,
    dv_ref,
    done_ref,
):
    half, own_at, starts, ends, left_from, right_to = window_facts(counts_ref)
    block_rows = CHUNK // 2
    rows = MAIN * CHUNK
    far_at = jnp.where(half == 0, -CHUNK, rows)
    for block in range(2):
        at = slice(block * block_rows, (block + 1) * block_rows)
        stores = [ref.at[at, :] for ref in (qf_ref, kf_ref, vf_ref, df_ref)]
        place_block(
            far_ref.at[at],
            far_at + block * block_rows,
            starts,
            ends,
            gains_ref,
            stores + [kvf_ref.at[:, at]],
        )

    own_rows = pl.ds(pl.multiple_of(own_at, CHUNK), CHUNK)
    q_own = qx_ref[own_rows, :]
    d_own = dx_ref[own_rows, :]
    scores = rows_dot(kf_ref[...], q_own)
    s_ref[0:CHUNK, :] = scores
    g_ref[0:CHUNK, :] = rows_dot(vf_ref[...], d_own)
    highest = jnp.maximum(stats_ref[MAIN, :, :], rows_max(scores))
    highest = jnp.max(highest, axis=0, keepdims=True) * LOG2_E
    zeros = jnp.zeros((8, CHUNK), F32)
    total, grads = add_tiles(so_ref, go_ref, rows, highest, zeros, zeros)
    total, grads = add_tiles(s_ref, g_ref, CHUNK, highest, total, grads)
    scale = 1.0 / jnp.sum(total, axis=0, keepdims=True)
    mean_grad = jnp.sum(grads, axis=0, keepdims=True) * scale

    def write_tile(scores, grads, highest, scale, mean_grad, to):
        probs = jnp.exp2(scores * LOG2_E - highest) * scale
        p_ref[to, :] = probs.astype(BF16)
        d_ref[to, :] = (probs * (grads - mean_grad)).astype(BF16)

    for piece in range(rows // TILE):
        at = slice(piece * TILE, (piece + 1) * TILE)
        write_tile(so_ref[at, :], go_ref[at, :], highest, scale, mean_grad, at)
    for piece in range(CHUNK // TILE):
        at = slice(piece * TILE, (piece + 1) * TILE)
        to = slice(rows + piece * TILE, rows + (piece + 1) * TILE)
        write_tile(s_ref[at, :], g_ref[at, :], highest, scale, mean_grad, to)
    dk_ref[...] = jnp.dot(d_ref[own_rows, :], q_own, preferred_element_type=F32)
    dv_ref[...] = jnp.dot(p_ref[own_rows, :], d_own, preferred_element_type=F32)

    def times_window(values_ref):
        main = jnp.dot(kv_ref[...], values_ref[0:rows, :], preferred_element_type=F32)
        return main + jnp.dot(
            kvf_ref[...], values_ref[rows : rows + CHUNK, :], preferred_element_type=F32
        )

    upper = lax.broadcasted_iota(jnp.int32, (LANES, CHUNK), 0) < HEAD
    own_out = jnp.where(upper, times_window(d_ref) * INV_ROOT, times_window(p_ref)).T

    query_lane = lax.broadcasted_iota(jnp.int32, (1, CHUNK), 1)
    reaches_far = jnp.where(half == 0, left_from < 0, right_to > rows)

    def add_gradients(tiles, begin, q_block, d_block, highest, total, grads):
        place = query_lane + begin
        scale = jnp.where((place >= left_from) & (place < right_to), 1.0 / total, 0.0)
        mean_grad = grads * scale
        for piece in range(CHUNK // TILE):
            scores, given = tiles(piece)
            at = slice(piece * TILE, (piece + 1) * TILE)
            write_tile(scores, given, highest, scale, mean_grad, at)
        dk_ref[...] += jnp.dot(d_ref[0:CHUNK, :], q_block, preferred_element_type=F32)
        dv_ref[...] += jnp.dot(p_ref[0:CHUNK, :], d_block, preferred_element_type=F32)

    def one_chunk(step, carry):
        slot = step + jnp.where(step >= 2 + half, 1, 0)
        begin = slot * CHUNK

        @pl.when((begin < right_to) & (begin + CHUNK > left_from))
        def _():
            at = pl.ds(pl.multiple_of(begin, CHUNK), CHUNK)
            q_block = qx_ref[at, :]
            d_block = dx_ref[at, :]
            sums_ref[...] = stats_ref[slot, :, :]
            same_side = (begin < own_at) == (half == 0)

            @pl.when(reaches_far & same_side)
            def _():
                scores = rows_dot(kf_ref[...], q_block)
                s_ref[0:CHUNK, :] = scores
                g_ref[0:CHUNK, :] = rows_dot(vf_ref[...], d_block)
                before = sums_ref[0:1, :]
                highest = jnp.max(rows_max(scores), axis=0, keepdims=True) * LOG2_E
                highest = jnp.maximum(before, highest)
                total, grads = add_tiles(s_ref, g_ref, CHUNK, highest, zeros, zeros)
                shrink = jnp.exp2(before - highest)
                sums_ref[0:1, :] = highest
                total = jnp.sum(total, axis=0, keepdims=True)
                grads = jnp.sum(grads, axis=0, keepdims=True)
                sums_ref[1:2, :] = sums_ref[1:2, :] * shrink + total
                sums_ref[2:3, :] = sums_ref[2:3, :] * shrink + grads

            def tiles(piece):
                at = slice(piece * TILE, (piece + 1) * TILE)
                return sn_ref[slot, at, :], gn_ref[slot, at, :]

            add_gradients(
                tiles, begin, q_block, d_block, sums_ref[0:1, :], sums_ref[1:2, :], sums_ref[2:3, :]
            )

        return carry

    lax.fori_loop(0, MAIN - 1, one_chunk, 0)

    @pl.when(reaches_far)
    def _():
        q_block = qf_ref[...]
        d_block = df_ref[...]
        key = half * (MAIN // 2) * CHUNK
        highest = jnp.full((8, CHUNK), -jnp.inf, F32)
        for piece in range(REACH_CHUNKS):
            here = slice(piece * CHUNK, (piece + 1) * CHUNK)
            if piece < REACH_CHUNKS - 1:
                keys_at = pl.ds(pl.multiple_of(key + piece * CHUNK, CHUNK), CHUNK)
                keys, values = kx_ref[keys_at, :], vx_ref[keys_at, :]
            else:
                keys, values = kf_ref[...], vf_ref[...]
            scores = rows_dot(keys, q_block)
            s_ref[here, :] = scores
            highest = jnp.maximum(highest, rows_max(scores))
            g_ref[here, :] = rows_dot(values, d_block)
        highest = jnp.max(highest, axis=0, keepdims=True) * LOG2_E
        total, grads = add_tiles(s_ref, g_ref, REACH_CHUNKS * CHUNK, highest, zeros, zeros)

        def tiles(piece):
            at = pl.ds(pl.multiple_of(own_at - key + piece * TILE, TILE), TILE)
            return s_ref[at, :], g_ref[at, :]

        add_gradients(
            tiles,
            far_at,
            q_block,
            d_block,
            highest,
            jnp.sum(total, axis=0, keepdims=True),
            jnp.sum(grads, axis=0, keepdims=True),
        )

    def norm_grad(raw, gain, d_norm):
        inverse = lax.rsqrt(lower_mean(raw * raw) + EPS)
        scaled = d_norm.astype(BF16).astype(F32) * gain
        inner = lower_mean(raw * scaled)
        return inverse * scaled - raw * (inverse * inverse * inverse * inner)

    low = low_lanes()
    own_in_quad = pl.ds(pl.multiple_of(half * CHUNK, CHUNK), CHUNK)
    raw_q = quad_ref[own_in_quad, 0:LANES].astype(F32)
    raw_k = quad_ref[own_in_quad, LANES:].astype(F32)
    d_q = norm_grad(raw_q, gains_ref[0:1, :], own_out)
    d_k = norm_grad(raw_k, gains_ref[1:2, :], dk_ref[...])
    done_ref[:, 0:LANES] = jnp.where(low, d_q, own_out).astype(BF16)
    done_ref[:, LANES:] = jnp.where(low, d_k, dv_ref[...]).astype(BF16)
    share = 16
    for member in range(out_ref.shape[0]):
        block, core = member // 2, member % 2
        for part in range(out_ref.shape[1] // share):
            begin = (block * 8 + part * 2 + core) * share
            out_ref[member, part * share : (part + 1) * share, :] = done_ref[
                begin : begin + share, :
            ]


def attend_far(counts, gains, far, quad, near_parts):
    return pl.pallas_call(
        far_kernel,
        out_shape=jax.ShapeDtypeStruct((4, CHUNK // 4, 2 * LANES), BF16),
        in_specs=[SMEM] + [VMEM] * (3 + len(near_parts)),
        out_specs=VMEM,
        scratch_shapes=[pltpu.VMEM((CHUNK, LANES), BF16)] * 4
        + [pltpu.VMEM((LANES, CHUNK), BF16)]
        + [pltpu.VMEM((REACH_CHUNKS * CHUNK, CHUNK), F32)] * 2
        + [pltpu.VMEM(((MAIN + 1) * CHUNK, CHUNK), BF16)] * 2
        + [pltpu.VMEM((8, CHUNK), F32)]
        + [pltpu.VMEM((CHUNK, LANES), F32)] * 2
        + [pltpu.VMEM((CHUNK, 2 * LANES), BF16)],
        cost_estimate=pl.CostEstimate(
            flops=10000000000, bytes_accessed=1 << 20, transcendentals=1 << 20
        ),
        compiler_params=pltpu.CompilerParams(vmem_limit_bytes=VMEM_LIMIT),
    )(counts, gains, far, quad, *near_parts)


def project_kernel(parts_ref, w_out_ref, w_qkv_ref, w_out_far_ref, w_qkv_far_ref, out_ref):
    rows = parts_ref.shape[1]
    width = w_out_ref.shape[1]
    share = out_ref.shape[1]
    core = lax.axis_index("core")
    low = lax.broadcasted_iota(jnp.int32, (rows, LANES), 1) < HEAD

    def products(which, w_out, w_qkv):
        head0 = parts_ref[which].astype(F32)
        head1 = parts_ref[2 + which].astype(F32)
        a0, a1 = head0[:, :LANES], head1[:, :LANES]
        b0, b1 = head0[:, LANES:], head1[:, LANES:]
        d_q = jnp.where(low, a0, pltpu.roll(a1, HEAD, 1)).astype(BF16)
        attn = jnp.where(low, pltpu.roll(a0, HEAD, 1), a1).astype(BF16)
        d_k = jnp.where(low, b0, pltpu.roll(b1, HEAD, 1)).astype(BF16)
        d_v = jnp.where(low, pltpu.roll(b0, HEAD, 1), b1).astype(BF16)
        mixed = jnp.dot(attn, w_out[...], preferred_element_type=F32)
        d_hidden = rows_dot(d_q, w_qkv[0]) + rows_dot(d_k, w_qkv[1]) + rows_dot(d_v, w_qkv[2])
        return mixed, d_hidden

    mixed, d_hidden = products(core, w_out_ref, w_qkv_ref)
    mixed_far, d_hidden_far = products(1 - core, w_out_far_ref, w_qkv_far_ref)
    mixed = (mixed + mixed_far).astype(BF16)
    d_hidden = (d_hidden + d_hidden_far).astype(BF16)
    for place in range(out_ref.shape[0]):
        at = slice(place * share, (place + 1) * share)
        out_ref[place, :, :width] = mixed[at]
        out_ref[place, :, width:] = d_hidden[at]


def project(parts, w_out, w_parts, w_out_far, w_parts_far, x_count):
    return pl.pallas_call(
        project_kernel,
        out_shape=jax.ShapeDtypeStruct(
            (x_count, parts.shape[1] // x_count, 2 * w_out.shape[1]), BF16
        ),
        in_specs=[VMEM] * 5,
        out_specs=VMEM,
        compiler_params=pltpu.CompilerParams(vmem_limit_bytes=VMEM_LIMIT),
    )(parts, w_out, w_parts, w_out_far, w_parts_far)


def ready_kernel(
    counts_ref,
    tokens_ref,
    cotangent_ref,
    modulation_ref,
    rows_ref,
    factors_ref,
):
    rows = rows_ref.shape[1]
    first_row = (lax.axis_index("x") * 2 + lax.axis_index("core")) * rows
    first = block_index() * tokens_ref.shape[0] + first_row
    _, scale, gate = modulation_rows(counts_ref, modulation_ref, first, rows)
    at = pl.ds(pl.multiple_of(first_row, rows), rows)
    normed, inv_std = layer_norm(tokens_ref[at, :].astype(F32))
    rows_ref[0] = tokens_ref[at, :]
    rows_ref[1] = cotangent_ref[at, :]
    factors_ref[0] = gate
    factors_ref[1] = 1.0 + scale
    factors_ref[2] = normed
    factors_ref[3] = jnp.broadcast_to(inv_std, normed.shape)


def ready(counts, tokens, cotangent, modulation, share):
    width = tokens.shape[1]
    return pl.pallas_call(
        ready_kernel,
        out_shape=(
            jax.ShapeDtypeStruct((2, share, width), BF16),
            jax.ShapeDtypeStruct((4, share, width), F32),
        ),
        in_specs=[SMEM] + [VMEM] * 3,
        out_specs=(VMEM, VMEM),
        compiler_params=pltpu.CompilerParams(vmem_limit_bytes=VMEM_LIMIT),
    )(counts, tokens, cotangent, modulation)


def leave_kernel(rows_ref, factors_ref, shares_ref, layer_ref, grad_ref):
    width = layer_ref.shape[1]
    sums = shares_ref[0].astype(F32)
    for share in range(1, shares_ref.shape[0]):
        sums = sums + shares_ref[share].astype(F32)
    layer = rows_ref[0].astype(F32) + factors_ref[0] * sums[:, :width]
    layer_ref[...] = layer.astype(BF16)
    d_normed = sums[:, width:] * factors_ref[1]
    normed = factors_ref[2]
    input_grad = rows_ref[1].astype(F32) + factors_ref[3] * (
        d_normed
        - jnp.mean(d_normed, axis=-1, keepdims=True)
        - normed * jnp.mean(d_normed * normed, axis=-1, keepdims=True)
    )
    grad_ref[...] = input_grad.astype(BF16)


def leave(rows, factors, shares):
    out = jax.ShapeDtypeStruct(rows.shape[1:], BF16)
    return pl.pallas_call(
        leave_kernel,
        out_shape=(out, out),
        in_specs=[VMEM] * 3,
        out_specs=(VMEM, VMEM),
        compiler_params=pltpu.CompilerParams(vmem_limit_bytes=VMEM_LIMIT),
    )(rows, factors, shares)


def per_device(tokens, cotangent, w_qkv, w_out, qk_gain, modulation, image_counts):
    tok_rows, model_width = tokens.shape
    z_count = lax.axis_size("z")
    x_count = lax.axis_size("x")
    quad = 4
    pair_rows = 2 * tok_rows
    share = tok_rows // (2 * x_count)
    w_parts = w_qkv.transpose(1, 0, 2)
    mod_parts = modulation.transpose(1, 0, 2)
    gains = jnp.pad(qk_gain, ((0, 6), (0, LANES - HEAD)))

    heads = enter(image_counts, tokens, cotangent, w_parts, w_out, mod_parts, quad)
    mine = lax.all_to_all(heads, ("yh", "yl"), 0, 0)
    mine = mine.reshape(quad * tok_rows, 2 * LANES)
    evens = range(0, z_count, 2)
    swaps = [(i, i + 1) for i in evens], [((i - 1) % z_count, i) for i in evens]
    first, second = (
        lax.ppermute(mine, "z", pairs + [(j, i) for i, j in pairs]) for pairs in swaps
    )
    far_half = jnp.where(lax.axis_index("yh") == 0, mine[pair_rows:], mine[:pair_rows])
    halves = 2 * z_count
    far = lax.ppermute(
        far_half,
        ("z", "yh"),
        [(i, (i + (4 if i % 2 == 0 else -4)) % halves) for i in range(halves)],
    )
    _, tokens_late, cotangent_late, mod_late = lax.optimization_barrier(
        (mine, tokens, cotangent, mod_parts)
    )
    rows, factors = ready(image_counts, tokens_late, cotangent_late, mod_late, share)
    near_parts = attend_near(image_counts, gains, first, mine, second)
    _, _, w_parts_late, w_out_late = lax.optimization_barrier((mine, mine, w_parts, w_out))
    w_parts_far, w_out_far = (
        lax.ppermute(w, "core", [(0, 1), (1, 0)]) for w in (w_parts_late, w_out_late)
    )
    parts = attend_far(image_counts, gains, far, mine, near_parts)
    parts = lax.all_to_all(parts, ("yl", "core"), 0, 0)
    partial = project(parts, w_out, w_parts, w_out_far, w_parts_far, x_count)
    shares = lax.all_to_all(partial, "x", 0, 0)
    return leave(rows, factors, shares)


def solution(mesh):
    split = jax.sharding.Mesh(mesh.devices.reshape(16, 2, 2, 4, 2), ("z", "yh", "yl", "x", "core"))
    dp, head = ("z", "yh", "yl"), ("x", "core")
    in_specs = (P(dp, None), P(dp, None), P(None, None, head), P(head, None), P(), P(), P())
    out_specs = (P(dp + head, None), P(dp + head, None))
    return jax.shard_map(
        per_device, mesh=split, in_specs=in_specs, out_specs=out_specs, check_vma=False
    )
```

```python
import math

import jax
import jax.numpy as jnp
from jax import lax
from jax.experimental import pallas as pl
from jax.experimental.pallas import tpu as pltpu
from jax.sharding import PartitionSpec as P

EPS = 1e-06
SAME_IMAGE = 512.0
LANES = 128
HEAD = 64
F32 = jnp.float32
BF16 = jnp.bfloat16
VMEM_LIMIT = 24 * 1024 * 1024
ENTER_LIMIT = 60 * 1024 * 1024
VMEM = pl.BlockSpec(memory_space=pltpu.VMEM)
SMEM = pl.BlockSpec(memory_space=pltpu.SMEM)


def rows_dot(a, b):
    return lax.dot_general(a, b, (((1,), (1,)), ((), ())), preferred_element_type=F32)


def block_index():
    return (lax.axis_index("z") * 2 + lax.axis_index("yh")) * 2 + lax.axis_index("yl")


def image_bounds(counts_ref, first_lane):
    lane = lax.broadcasted_iota(jnp.int32, (1, LANES), 1)
    starts = jnp.zeros((1, LANES), jnp.int32)
    ends = jnp.zeros((1, LANES), jnp.int32)
    total = jnp.int32(0)
    for image in range(counts_ref.shape[0]):
        here = lane == first_lane + image
        starts = jnp.where(here, total, starts)
        total = total + counts_ref[image]
        ends = jnp.where(here, total, ends)
    return starts, ends


def modulation_rows(counts_ref, modulation_ref, first, rows):
    starts, ends = image_bounds(counts_ref, 0)
    place = first + lax.broadcasted_iota(jnp.int32, (rows, LANES), 0)
    member = ((place >= starts) & (place < ends)).astype(F32).astype(BF16)
    member = member[:, : modulation_ref.shape[1]]
    return [
        jnp.dot(member, modulation_ref[part], preferred_element_type=F32) for part in range(3)
    ]


def layer_norm(values):
    average = jnp.mean(values, axis=-1, keepdims=True)
    centred = values - average
    inv_std = lax.rsqrt(jnp.mean(centred * centred, axis=-1, keepdims=True) + EPS)
    return centred * inv_std, inv_std


def enter_kernel(
    counts_ref, tokens_ref, cotangent_ref, w_qkv_ref, w_out_ref, modulation_ref, out_ref
):
    rows = tokens_ref.shape[0]
    first = block_index() * rows
    shift, scale, gate = modulation_rows(counts_ref, modulation_ref, first, rows)
    normed, _ = layer_norm(tokens_ref[...].astype(F32))
    hidden = (normed * (1.0 + scale) + shift).astype(BF16)
    weights = jnp.concatenate([w_qkv_ref[part] for part in range(3)], axis=1)
    qkv = jnp.dot(hidden, weights, preferred_element_type=F32)
    q, k, v = (qkv[:, part * LANES : (part + 1) * LANES] for part in range(3))
    d_mixed = (cotangent_ref[...].astype(F32) * gate).astype(BF16)
    d_attn = rows_dot(d_mixed, w_out_ref[...])
    low = lax.broadcasted_iota(jnp.int32, (rows, LANES), 1) < HEAD

    def beside(left, right):
        return jnp.where(low, left, right).astype(BF16)

    q_v = (beside(q, pltpu.roll(v, HEAD, 1)), beside(pltpu.roll(q, HEAD, 1), v))
    k_d = (beside(k, pltpu.roll(d_attn, HEAD, 1)), beside(pltpu.roll(k, HEAD, 1), d_attn))
    for place in range(out_ref.shape[0]):
        out_ref[place, :, 0:LANES] = q_v[place % 2]
        out_ref[place, :, LANES:] = k_d[place % 2]


def enter(counts, tokens, cotangent, w_parts, w_out, modulation, quad):
    return pl.pallas_call(
        enter_kernel,
        out_shape=jax.ShapeDtypeStruct((quad, tokens.shape[0], 2 * LANES), BF16),
        in_specs=[SMEM] + [VMEM] * 5,
        out_specs=VMEM,
        compiler_params=pltpu.CompilerParams(vmem_limit_bytes=ENTER_LIMIT),
    )(counts, tokens, cotangent, w_parts, w_out, modulation)


LOG2_E = math.log2(math.e)
INV_ROOT = 1.0 / math.sqrt(HEAD)
CHUNK = 256
TILE = 64
MAIN = 6
REACH_CHUNKS = 4


def low_lanes():
    return lax.broadcasted_iota(jnp.int32, (1, LANES), 1) < HEAD


def lower_mean(values):
    return jnp.sum(jnp.where(low_lanes(), values, 0.0), axis=-1, keepdims=True) * (1.0 / HEAD)


def lower_sums(values):
    ones = (lax.broadcasted_iota(jnp.int32, (LANES, LANES), 0) < HEAD).astype(F32).astype(BF16)
    squares = values * values
    large = squares.astype(BF16)
    small = (squares - large.astype(F32)).astype(BF16)
    large = jnp.dot(large, ones, preferred_element_type=F32)
    return large + jnp.dot(small, ones, preferred_element_type=F32)


def place_block(source, place, starts, ends, gains_ref, stores):
    low = low_lanes()
    rows = source.shape[0]
    at = place + lax.broadcasted_iota(jnp.int32, (rows, LANES), 0)
    same = ((at >= starts) & (at < ends)).astype(F32)
    first = source[:, 0:LANES].astype(F32)
    second = source[:, LANES:].astype(F32)

    def normed(raw, gain):
        return raw * lax.rsqrt(lower_sums(raw) * (1.0 / HEAD) + EPS) * gain

    keys = normed(second, gains_ref[1:2, :])
    queries = normed(first, gains_ref[0:1, :] * INV_ROOT)
    q_store, k_store, v_store, d_store, kv_store = stores
    q_store[...] = jnp.where(low, queries, same * SAME_IMAGE).astype(BF16)
    k_store[...] = jnp.where(low, keys, same).astype(BF16)
    v_store[...] = jnp.where(low, 0.0, first).astype(BF16)
    d_store[...] = source[:, LANES:]
    kv_store[...] = jnp.where(low, keys, first).astype(BF16).T


def window_facts(counts_ref):
    half = lax.axis_index("yh")
    origin = (block_index() // 4 - 1) * 2 * CHUNK
    own_at = (2 + half) * CHUNK
    starts, ends = image_bounds(counts_ref, HEAD)
    left_from = jnp.int32(-CHUNK)
    right_to = jnp.int32((MAIN + 1) * CHUNK)
    total = -origin
    for image in range(counts_ref.shape[0]):
        left_from = jnp.where(total <= own_at, total, left_from)
        ended = total >= own_at + CHUNK
        total = total + counts_ref[image]
        right_to = jnp.where((total >= own_at + CHUNK) & jnp.logical_not(ended), total, right_to)
    return half, own_at, starts - origin, ends - origin, left_from, right_to


def by_eight(values):
    return values.reshape(values.shape[0] // 8, 8, values.shape[1])


def add_tiles(s_ref, g_ref, rows, highest, total, grads):
    for piece in range(rows // TILE):
        at = slice(piece * TILE, (piece + 1) * TILE)
        weights = jnp.exp2(s_ref[at, :] * LOG2_E - highest)
        total = total + jnp.sum(by_eight(weights), axis=0)
        grads = grads + jnp.sum(by_eight(weights * g_ref[at, :]), axis=0)
    return total, grads


def rows_max(values):
    return jnp.max(by_eight(values), axis=0)


def near_kernel(
    counts_ref,
    gains_ref,
    first_ref,
    quad_ref,
    second_ref,
    qx_ref,
    kx_ref,
    vx_ref,
    dx_ref,
    kv_ref,
    so_ref,
    go_ref,
    sn_ref,
    gn_ref,
    stats_ref,
    s_ref,
    g_ref,
):
    half, own_at, starts, ends, left_from, right_to = window_facts(counts_ref)
    block_rows = CHUNK // 2

    def place(source, begin):
        begin = pl.multiple_of(begin, block_rows)
        at = pl.ds(begin, block_rows)
        stores = [ref.at[at, :] for ref in (qx_ref, kx_ref, vx_ref, dx_ref)]
        place_block(source, begin, starts, ends, gains_ref, stores + [kv_ref.at[:, at]])

    to_first = jnp.where(lax.rem(lax.axis_index("z"), 2) == 0, 2 * CHUNK, -2 * CHUNK)
    for block in range(4):
        at = slice(block * block_rows, (block + 1) * block_rows)
        begin = 2 * CHUNK + block * block_rows
        place(quad_ref.at[at], begin)
        place(first_ref.at[at], begin + to_first)
        place(second_ref.at[at], begin - to_first)

    own_rows = pl.ds(pl.multiple_of(own_at, CHUNK), CHUNK)
    q_own = qx_ref[own_rows, :]
    d_own = dx_ref[own_rows, :]
    highest = jnp.full((8, CHUNK), -jnp.inf, F32)
    for piece in range(MAIN):
        at = slice(piece * CHUNK, (piece + 1) * CHUNK)
        scores = rows_dot(kx_ref[at, :], q_own)
        so_ref[at, :] = scores
        highest = jnp.maximum(highest, rows_max(scores))
        go_ref[at, :] = rows_dot(vx_ref[at, :], d_own)
    stats_ref[MAIN, :, :] = highest

    left_key = jnp.clip((left_from + CHUNK) // CHUNK - 1, 0, MAIN - REACH_CHUNKS)
    right_key = jnp.clip((right_to - 1) // CHUNK - (REACH_CHUNKS - 1), 0, MAIN - REACH_CHUNKS)

    def one_chunk(step, carry):
        slot = step + jnp.where(step >= 2 + half, 1, 0)
        begin = slot * CHUNK

        @pl.when((begin < right_to) & (begin + CHUNK > left_from))
        def _():
            at = pl.ds(pl.multiple_of(begin, CHUNK), CHUNK)
            key = jnp.where(begin < own_at, left_key, right_key) * CHUNK
            q_block = qx_ref[at, :]
            d_block = dx_ref[at, :]
            highest = jnp.full((8, CHUNK), -jnp.inf, F32)
            for piece in range(REACH_CHUNKS):
                keys_at = pl.ds(pl.multiple_of(key + piece * CHUNK, CHUNK), CHUNK)
                here = slice(piece * CHUNK, (piece + 1) * CHUNK)
                scores = rows_dot(kx_ref[keys_at, :], q_block)
                s_ref[here, :] = scores
                highest = jnp.maximum(highest, rows_max(scores))
                g_ref[here, :] = rows_dot(vx_ref[keys_at, :], d_block)
            highest = jnp.max(highest, axis=0, keepdims=True) * LOG2_E
            zeros = jnp.zeros((8, CHUNK), F32)
            total, grads = add_tiles(s_ref, g_ref, REACH_CHUNKS * CHUNK, highest, zeros, zeros)
            stats_ref[slot, 0:1, :] = highest
            stats_ref[slot, 1:2, :] = jnp.sum(total, axis=0, keepdims=True)
            stats_ref[slot, 2:3, :] = jnp.sum(grads, axis=0, keepdims=True)
            near_at = pl.ds(pl.multiple_of(own_at - key, CHUNK), CHUNK)
            sn_ref[slot, :, :] = s_ref[near_at, :]
            gn_ref[slot, :, :] = g_ref[near_at, :]

        return carry

    lax.fori_loop(0, MAIN - 1, one_chunk, 0)


def attend_near(counts, gains, first, quad, second):
    rows = MAIN * CHUNK
    head_rows = jax.ShapeDtypeStruct((rows, LANES), BF16)
    scores = jax.ShapeDtypeStruct((rows, CHUNK), F32)
    tiles = jax.ShapeDtypeStruct((MAIN, CHUNK, CHUNK), F32)
    return pl.pallas_call(
        near_kernel,
        out_shape=(head_rows,) * 4
        + (jax.ShapeDtypeStruct((LANES, rows), BF16),)
        + (scores, scores, tiles, tiles, jax.ShapeDtypeStruct((MAIN + 1, 8, CHUNK), F32)),
        in_specs=[SMEM] + [VMEM] * 4,
        out_specs=(VMEM,) * 10,
        scratch_shapes=[pltpu.VMEM((REACH_CHUNKS * CHUNK, CHUNK), F32)] * 2,
        cost_estimate=pl.CostEstimate(
            flops=10000000000, bytes_accessed=1 << 20, transcendentals=1 << 20
        ),
        compiler_params=pltpu.CompilerParams(vmem_limit_bytes=VMEM_LIMIT),
    )(counts, gains, first, quad, second)


def far_kernel(
    counts_ref,
    gains_ref,
    far_ref,
    quad_ref,
    qx_ref,
    kx_ref,
    vx_ref,
    dx_ref,
    kv_ref,
    so_ref,
    go_ref,
    sn_ref,
    gn_ref,
    stats_ref,
    out_ref,
    qf_ref,
    kf_ref,
    vf_ref,
    df_ref,
    kvf_ref,
    s_ref,
    g_ref,
    p_ref,
    d_ref,
    sums_ref,
    dk_ref,
    dv_ref,
    done_ref,
):
    half, own_at, starts, ends, left_from, right_to = window_facts(counts_ref)
    block_rows = CHUNK // 2
    rows = MAIN * CHUNK
    far_at = jnp.where(half == 0, -CHUNK, rows)
    for block in range(2):
        at = slice(block * block_rows, (block + 1) * block_rows)
        stores = [ref.at[at, :] for ref in (qf_ref, kf_ref, vf_ref, df_ref)]
        place_block(
            far_ref.at[at],
            far_at + block * block_rows,
            starts,
            ends,
            gains_ref,
            stores + [kvf_ref.at[:, at]],
        )

    own_rows = pl.ds(pl.multiple_of(own_at, CHUNK), CHUNK)
    q_own = qx_ref[own_rows, :]
    d_own = dx_ref[own_rows, :]
    scores = rows_dot(kf_ref[...], q_own)
    s_ref[0:CHUNK, :] = scores
    g_ref[0:CHUNK, :] = rows_dot(vf_ref[...], d_own)
    highest = jnp.maximum(stats_ref[MAIN, :, :], rows_max(scores))
    highest = jnp.max(highest, axis=0, keepdims=True) * LOG2_E
    zeros = jnp.zeros((8, CHUNK), F32)
    total, grads = add_tiles(so_ref, go_ref, rows, highest, zeros, zeros)
    total, grads = add_tiles(s_ref, g_ref, CHUNK, highest, total, grads)
    scale = 1.0 / jnp.sum(total, axis=0, keepdims=True)
    mean_grad = jnp.sum(grads, axis=0, keepdims=True) * scale

    def write_tile(scores, grads, highest, scale, mean_grad, to):
        probs = jnp.exp2(scores * LOG2_E - highest) * scale
        p_ref[to, :] = probs.astype(BF16)
        d_ref[to, :] = (probs * (grads - mean_grad)).astype(BF16)

    for piece in range(rows // TILE):
        at = slice(piece * TILE, (piece + 1) * TILE)
        write_tile(so_ref[at, :], go_ref[at, :], highest, scale, mean_grad, at)
    for piece in range(CHUNK // TILE):
        at = slice(piece * TILE, (piece + 1) * TILE)
        to = slice(rows + piece * TILE, rows + (piece + 1) * TILE)
        write_tile(s_ref[at, :], g_ref[at, :], highest, scale, mean_grad, to)
    dk_ref[...] = jnp.dot(d_ref[own_rows, :], q_own, preferred_element_type=F32)
    dv_ref[...] = jnp.dot(p_ref[own_rows, :], d_own, preferred_element_type=F32)

    def times_window(values_ref):
        main = jnp.dot(kv_ref[...], values_ref[0:rows, :], preferred_element_type=F32)
        return main + jnp.dot(
            kvf_ref[...], values_ref[rows : rows + CHUNK, :], preferred_element_type=F32
        )

    upper = lax.broadcasted_iota(jnp.int32, (LANES, CHUNK), 0) < HEAD
    own_out = jnp.where(upper, times_window(d_ref) * INV_ROOT, times_window(p_ref)).T

    query_lane = lax.broadcasted_iota(jnp.int32, (1, CHUNK), 1)
    reaches_far = jnp.where(half == 0, left_from < 0, right_to > rows)

    def add_gradients(tiles, begin, q_block, d_block, highest, total, grads):
        place = query_lane + begin
        scale = jnp.where((place >= left_from) & (place < right_to), 1.0 / total, 0.0)
        mean_grad = grads * scale
        for piece in range(CHUNK // TILE):
            scores, given = tiles(piece)
            at = slice(piece * TILE, (piece + 1) * TILE)
            write_tile(scores, given, highest, scale, mean_grad, at)
        dk_ref[...] += jnp.dot(d_ref[0:CHUNK, :], q_block, preferred_element_type=F32)
        dv_ref[...] += jnp.dot(p_ref[0:CHUNK, :], d_block, preferred_element_type=F32)

    def one_chunk(step, carry):
        slot = step + jnp.where(step >= 2 + half, 1, 0)
        begin = slot * CHUNK

        @pl.when((begin < right_to) & (begin + CHUNK > left_from))
        def _():
            at = pl.ds(pl.multiple_of(begin, CHUNK), CHUNK)
            q_block = qx_ref[at, :]
            d_block = dx_ref[at, :]
            sums_ref[...] = stats_ref[slot, :, :]
            same_side = (begin < own_at) == (half == 0)

            @pl.when(reaches_far & same_side)
            def _():
                scores = rows_dot(kf_ref[...], q_block)
                s_ref[0:CHUNK, :] = scores
                g_ref[0:CHUNK, :] = rows_dot(vf_ref[...], d_block)
                before = sums_ref[0:1, :]
                highest = jnp.max(rows_max(scores), axis=0, keepdims=True) * LOG2_E
                highest = jnp.maximum(before, highest)
                total, grads = add_tiles(s_ref, g_ref, CHUNK, highest, zeros, zeros)
                shrink = jnp.exp2(before - highest)
                sums_ref[0:1, :] = highest
                total = jnp.sum(total, axis=0, keepdims=True)
                grads = jnp.sum(grads, axis=0, keepdims=True)
                sums_ref[1:2, :] = sums_ref[1:2, :] * shrink + total
                sums_ref[2:3, :] = sums_ref[2:3, :] * shrink + grads

            def tiles(piece):
                at = slice(piece * TILE, (piece + 1) * TILE)
                return sn_ref[slot, at, :], gn_ref[slot, at, :]

            add_gradients(
                tiles, begin, q_block, d_block, sums_ref[0:1, :], sums_ref[1:2, :], sums_ref[2:3, :]
            )

        return carry

    lax.fori_loop(0, MAIN - 1, one_chunk, 0)

    @pl.when(reaches_far)
    def _():
        q_block = qf_ref[...]
        d_block = df_ref[...]
        key = half * (MAIN // 2) * CHUNK
        highest = jnp.full((8, CHUNK), -jnp.inf, F32)
        for piece in range(REACH_CHUNKS):
            here = slice(piece * CHUNK, (piece + 1) * CHUNK)
            if piece < REACH_CHUNKS - 1:
                keys_at = pl.ds(pl.multiple_of(key + piece * CHUNK, CHUNK), CHUNK)
                keys, values = kx_ref[keys_at, :], vx_ref[keys_at, :]
            else:
                keys, values = kf_ref[...], vf_ref[...]
            scores = rows_dot(keys, q_block)
            s_ref[here, :] = scores
            highest = jnp.maximum(highest, rows_max(scores))
            g_ref[here, :] = rows_dot(values, d_block)
        highest = jnp.max(highest, axis=0, keepdims=True) * LOG2_E
        total, grads = add_tiles(s_ref, g_ref, REACH_CHUNKS * CHUNK, highest, zeros, zeros)

        def tiles(piece):
            at = pl.ds(pl.multiple_of(own_at - key + piece * TILE, TILE), TILE)
            return s_ref[at, :], g_ref[at, :]

        add_gradients(
            tiles,
            far_at,
            q_block,
            d_block,
            highest,
            jnp.sum(total, axis=0, keepdims=True),
            jnp.sum(grads, axis=0, keepdims=True),
        )

    def norm_grad(raw, gain, d_norm):
        inverse = lax.rsqrt(lower_mean(raw * raw) + EPS)
        scaled = d_norm.astype(BF16).astype(F32) * gain
        inner = lower_mean(raw * scaled)
        return inverse * scaled - raw * (inverse * inverse * inverse * inner)

    low = low_lanes()
    own_in_quad = pl.ds(pl.multiple_of(half * CHUNK, CHUNK), CHUNK)
    raw_q = quad_ref[own_in_quad, 0:LANES].astype(F32)
    raw_k = quad_ref[own_in_quad, LANES:].astype(F32)
    d_q = norm_grad(raw_q, gains_ref[0:1, :], own_out)
    d_k = norm_grad(raw_k, gains_ref[1:2, :], dk_ref[...])
    done_ref[:, 0:LANES] = jnp.where(low, d_q, own_out).astype(BF16)
    done_ref[:, LANES:] = jnp.where(low, d_k, dv_ref[...]).astype(BF16)
    share = 16
    for member in range(out_ref.shape[0]):
        block, core = member // 2, member % 2
        for part in range(out_ref.shape[1] // share):
            begin = (block * 8 + part * 2 + core) * share
            out_ref[member, part * share : (part + 1) * share, :] = done_ref[
                begin : begin + share, :
            ]


def attend_far(counts, gains, far, quad, near_parts):
    return pl.pallas_call(
        far_kernel,
        out_shape=jax.ShapeDtypeStruct((4, CHUNK // 4, 2 * LANES), BF16),
        in_specs=[SMEM] + [VMEM] * (3 + len(near_parts)),
        out_specs=VMEM,
        scratch_shapes=[pltpu.VMEM((CHUNK, LANES), BF16)] * 4
        + [pltpu.VMEM((LANES, CHUNK), BF16)]
        + [pltpu.VMEM((REACH_CHUNKS * CHUNK, CHUNK), F32)] * 2
        + [pltpu.VMEM(((MAIN + 1) * CHUNK, CHUNK), BF16)] * 2
        + [pltpu.VMEM((8, CHUNK), F32)]
        + [pltpu.VMEM((CHUNK, LANES), F32)] * 2
        + [pltpu.VMEM((CHUNK, 2 * LANES), BF16)],
        cost_estimate=pl.CostEstimate(
            flops=10000000000, bytes_accessed=1 << 20, transcendentals=1 << 20
        ),
        compiler_params=pltpu.CompilerParams(vmem_limit_bytes=VMEM_LIMIT),
    )(counts, gains, far, quad, *near_parts)


def project_kernel(parts_ref, w_out_ref, w_qkv_ref, w_out_far_ref, w_qkv_far_ref, out_ref):
    rows = parts_ref.shape[1]
    width = w_out_ref.shape[1]
    share = out_ref.shape[1]
    core = lax.axis_index("core")
    low = lax.broadcasted_iota(jnp.int32, (rows, LANES), 1) < HEAD

    def by_column(which):
        head0 = parts_ref[which].astype(F32)
        head1 = parts_ref[2 + which].astype(F32)
        a0, a1 = head0[:, :LANES], head1[:, :LANES]
        b0, b1 = head0[:, LANES:], head1[:, LANES:]
        d_q = jnp.where(low, a0, pltpu.roll(a1, HEAD, 1)).astype(BF16)
        attn = jnp.where(low, pltpu.roll(a0, HEAD, 1), a1).astype(BF16)
        d_k = jnp.where(low, b0, pltpu.roll(b1, HEAD, 1)).astype(BF16)
        d_v = jnp.where(low, pltpu.roll(b0, HEAD, 1), b1).astype(BF16)
        return attn, [d_q, d_k, d_v]

    attn, grads = by_column(core)
    attn_far, grads_far = by_column(1 - core)
    mixed = jnp.dot(
        jnp.concatenate([attn, attn_far], axis=1),
        jnp.concatenate([w_out_ref[...], w_out_far_ref[...]], axis=0),
        preferred_element_type=F32,
    ).astype(BF16)
    weights = [ref[part] for ref in (w_qkv_ref, w_qkv_far_ref) for part in range(3)]
    d_hidden = rows_dot(
        jnp.concatenate(grads + grads_far, axis=1), jnp.concatenate(weights, axis=1)
    ).astype(BF16)
    for place in range(out_ref.shape[0]):
        at = slice(place * share, (place + 1) * share)
        out_ref[place, :, :width] = mixed[at]
        out_ref[place, :, width:] = d_hidden[at]


def project(parts, w_out, w_parts, w_out_far, w_parts_far, x_count):
    return pl.pallas_call(
        project_kernel,
        out_shape=jax.ShapeDtypeStruct(
            (x_count, parts.shape[1] // x_count, 2 * w_out.shape[1]), BF16
        ),
        in_specs=[VMEM] * 5,
        out_specs=VMEM,
        compiler_params=pltpu.CompilerParams(vmem_limit_bytes=VMEM_LIMIT),
    )(parts, w_out, w_parts, w_out_far, w_parts_far)


def ready_kernel(
    counts_ref,
    tokens_ref,
    cotangent_ref,
    modulation_ref,
    rows_ref,
    factors_ref,
):
    rows = rows_ref.shape[1]
    first_row = (lax.axis_index("x") * 2 + lax.axis_index("core")) * rows
    first = block_index() * tokens_ref.shape[0] + first_row
    _, scale, gate = modulation_rows(counts_ref, modulation_ref, first, rows)
    at = pl.ds(pl.multiple_of(first_row, rows), rows)
    normed, inv_std = layer_norm(tokens_ref[at, :].astype(F32))
    rows_ref[0] = tokens_ref[at, :]
    rows_ref[1] = cotangent_ref[at, :]
    factors_ref[0] = gate
    factors_ref[1] = 1.0 + scale
    factors_ref[2] = normed
    factors_ref[3] = jnp.broadcast_to(inv_std, normed.shape)


def ready(counts, tokens, cotangent, modulation, share):
    width = tokens.shape[1]
    return pl.pallas_call(
        ready_kernel,
        out_shape=(
            jax.ShapeDtypeStruct((2, share, width), BF16),
            jax.ShapeDtypeStruct((4, share, width), F32),
        ),
        in_specs=[SMEM] + [VMEM] * 3,
        out_specs=(VMEM, VMEM),
        compiler_params=pltpu.CompilerParams(vmem_limit_bytes=VMEM_LIMIT),
    )(counts, tokens, cotangent, modulation)


def leave_kernel(rows_ref, factors_ref, shares_ref, layer_ref, grad_ref):
    width = layer_ref.shape[1]
    sums = shares_ref[0].astype(F32)
    for share in range(1, shares_ref.shape[0]):
        sums = sums + shares_ref[share].astype(F32)
    layer = rows_ref[0].astype(F32) + factors_ref[0] * sums[:, :width]
    layer_ref[...] = layer.astype(BF16)
    d_normed = sums[:, width:] * factors_ref[1]
    normed = factors_ref[2]
    input_grad = rows_ref[1].astype(F32) + factors_ref[3] * (
        d_normed
        - jnp.mean(d_normed, axis=-1, keepdims=True)
        - normed * jnp.mean(d_normed * normed, axis=-1, keepdims=True)
    )
    grad_ref[...] = input_grad.astype(BF16)


def leave(rows, factors, shares):
    out = jax.ShapeDtypeStruct(rows.shape[1:], BF16)
    return pl.pallas_call(
        leave_kernel,
        out_shape=(out, out),
        in_specs=[VMEM] * 3,
        out_specs=(VMEM, VMEM),
        compiler_params=pltpu.CompilerParams(vmem_limit_bytes=VMEM_LIMIT),
    )(rows, factors, shares)


def per_device(tokens, cotangent, w_qkv, w_out, qk_gain, modulation, image_counts):
    tok_rows, model_width = tokens.shape
    z_count = lax.axis_size("z")
    x_count = lax.axis_size("x")
    quad = 4
    pair_rows = 2 * tok_rows
    share = tok_rows // (2 * x_count)
    w_parts = w_qkv.transpose(1, 0, 2)
    mod_parts = modulation.transpose(1, 0, 2)
    gains = jnp.pad(qk_gain, ((0, 6), (0, LANES - HEAD)))

    heads = enter(image_counts, tokens, cotangent, w_parts, w_out, mod_parts, quad)
    mine = lax.all_to_all(heads, ("yh", "yl"), 0, 0)
    mine = mine.reshape(quad * tok_rows, 2 * LANES)
    evens = range(0, z_count, 2)
    swaps = [(i, i + 1) for i in evens], [((i - 1) % z_count, i) for i in evens]
    first, second = (
        lax.ppermute(mine, "z", pairs + [(j, i) for i, j in pairs]) for pairs in swaps
    )
    halves = 4 * z_count
    far_half = jnp.where(
        lax.axis_index("yh") == lax.axis_index("core"), mine[pair_rows:], mine[:pair_rows]
    )

    def far_source(target):
        z, yh, core = target // 4, target // 2 % 2, target % 2
        return (z + (2 if yh else -2)) % z_count * 4 + (yh ^ core) * 2 + core

    far = lax.ppermute(
        far_half, ("z", "yh", "core"), [(far_source(i), i) for i in range(halves)]
    )
    _, tokens_late, cotangent_late, mod_late = lax.optimization_barrier(
        (mine, tokens, cotangent, mod_parts)
    )
    rows, factors = ready(image_counts, tokens_late, cotangent_late, mod_late, share)
    near_parts = attend_near(image_counts, gains, first, mine, second)
    _, _, w_parts_late, w_out_late = lax.optimization_barrier((mine, mine, w_parts, w_out))
    w_parts_far, w_out_far = (
        lax.ppermute(w, "core", [(0, 1), (1, 0)]) for w in (w_parts_late, w_out_late)
    )
    parts = attend_far(image_counts, gains, far, mine, near_parts)
    parts = lax.all_to_all(parts, ("yl", "core"), 0, 0)
    partial = project(parts, w_out, w_parts, w_out_far, w_parts_far, x_count)
    shares = lax.all_to_all(partial, "x", 0, 0)
    return leave(rows, factors, shares)


def solution(mesh):
    split = jax.sharding.Mesh(mesh.devices.reshape(16, 2, 2, 4, 2), ("z", "yh", "yl", "x", "core"))
    dp, head = ("z", "yh", "yl"), ("x", "core")
    in_specs = (P(dp, None), P(dp, None), P(None, None, head), P(head, None), P(), P(), P())
    out_specs = (P(dp + head, None), P(dp + head, None))
    return jax.shard_map(
        per_device, mesh=split, in_specs=in_specs, out_specs=out_specs, check_vma=False
    )
```

```python
import math

import jax
import jax.numpy as jnp
from jax import lax
from jax.experimental import pallas as pl
from jax.experimental.pallas import tpu as pltpu
from jax.sharding import PartitionSpec as P

EPS = 1e-06
SAME_IMAGE = 512.0
LANES = 128
HEAD = 64
F32 = jnp.float32
BF16 = jnp.bfloat16
VMEM_LIMIT = 24 * 1024 * 1024
ENTER_LIMIT = 60 * 1024 * 1024
VMEM = pl.BlockSpec(memory_space=pltpu.VMEM)
SMEM = pl.BlockSpec(memory_space=pltpu.SMEM)


def rows_dot(a, b):
    return lax.dot_general(a, b, (((1,), (1,)), ((), ())), preferred_element_type=F32)


def block_index():
    return (lax.axis_index("z") * 2 + lax.axis_index("yh")) * 2 + lax.axis_index("yl")


def image_bounds(counts_ref, first_lane):
    lane = lax.broadcasted_iota(jnp.int32, (1, LANES), 1)
    starts = jnp.zeros((1, LANES), jnp.int32)
    ends = jnp.zeros((1, LANES), jnp.int32)
    total = jnp.int32(0)
    for image in range(counts_ref.shape[0]):
        here = lane == first_lane + image
        starts = jnp.where(here, total, starts)
        total = total + counts_ref[image]
        ends = jnp.where(here, total, ends)
    return starts, ends


def modulation_rows(counts_ref, modulation_ref, first, rows):
    starts, ends = image_bounds(counts_ref, 0)
    place = first + lax.broadcasted_iota(jnp.int32, (rows, LANES), 0)
    member = ((place >= starts) & (place < ends)).astype(F32).astype(BF16)
    member = member[:, : modulation_ref.shape[1]]
    return [
        jnp.dot(member, modulation_ref[part], preferred_element_type=F32) for part in range(3)
    ]


def layer_norm(values):
    average = jnp.mean(values, axis=-1, keepdims=True)
    centred = values - average
    inv_std = lax.rsqrt(jnp.mean(centred * centred, axis=-1, keepdims=True) + EPS)
    return centred * inv_std, inv_std


def w_out_of(weights_ref):
    tiles = weights_ref.shape[1] // LANES
    return jnp.concatenate(
        [weights_ref[3, tile * LANES : (tile + 1) * LANES, :] for tile in range(tiles)], axis=1
    )


def enter_kernel(
    counts_ref,
    tokens_hbm,
    cotangent_hbm,
    w_qkv_hbm,
    w_out_hbm,
    modulation_hbm,
    out_ref,
    weights_ref,
    tokens_ref,
    cotangent_ref,
    modulation_ref,
    sems,
):
    pairs = [
        (tokens_hbm, tokens_ref),
        (modulation_hbm, modulation_ref),
        (w_qkv_hbm, weights_ref.at[0:3]),
        (cotangent_hbm, cotangent_ref),
    ]
    for tile in range(weights_ref.shape[1] // LANES):
        at = slice(tile * LANES, (tile + 1) * LANES)
        pairs.append((w_out_hbm.at[:, at], weights_ref.at[3, at, :]))
    copies = [
        pltpu.make_async_copy(source, target, sems.at[place])
        for place, (source, target) in enumerate(pairs)
    ]
    for copy in copies:
        copy.start()
    rows = tokens_ref.shape[0]
    first = block_index() * rows
    copies[0].wait()
    normed, _ = layer_norm(tokens_ref[...].astype(F32))
    copies[1].wait()
    shift, scale, gate = modulation_rows(counts_ref, modulation_ref, first, rows)
    hidden = (normed * (1.0 + scale) + shift).astype(BF16)
    copies[2].wait()
    weights = jnp.concatenate([weights_ref[part] for part in range(3)], axis=1)
    qkv = jnp.dot(hidden, weights, preferred_element_type=F32)
    q, k, v = (qkv[:, part * LANES : (part + 1) * LANES] for part in range(3))
    copies[3].wait()
    d_mixed = (cotangent_ref[...].astype(F32) * gate).astype(BF16)
    for copy in copies[4:]:
        copy.wait()
    d_attn = rows_dot(d_mixed, w_out_of(weights_ref))
    low = lax.broadcasted_iota(jnp.int32, (rows, LANES), 1) < HEAD

    def beside(left, right):
        return jnp.where(low, left, right).astype(BF16)

    q_v = (beside(q, pltpu.roll(v, HEAD, 1)), beside(pltpu.roll(q, HEAD, 1), v))
    k_d = (beside(k, pltpu.roll(d_attn, HEAD, 1)), beside(pltpu.roll(k, HEAD, 1), d_attn))
    for place in range(out_ref.shape[0]):
        out_ref[place, :, 0:LANES] = q_v[place % 2]
        out_ref[place, :, LANES:] = k_d[place % 2]


def enter(counts, tokens, cotangent, w_parts, w_out, modulation, quad):
    rows, width = tokens.shape
    whole = pl.BlockSpec(memory_space=pl.ANY)
    return pl.pallas_call(
        enter_kernel,
        out_shape=(
            jax.ShapeDtypeStruct((quad, rows, 2 * LANES), BF16),
            jax.ShapeDtypeStruct((4, width, LANES), BF16),
        ),
        in_specs=[SMEM] + [whole] * 5,
        out_specs=(VMEM, VMEM),
        scratch_shapes=[
            pltpu.VMEM((rows, width), BF16),
            pltpu.VMEM((rows, width), BF16),
            pltpu.VMEM(modulation.shape, BF16),
            pltpu.SemaphoreType.DMA((4 + width // LANES,)),
        ],
        compiler_params=pltpu.CompilerParams(vmem_limit_bytes=ENTER_LIMIT),
    )(counts, tokens, cotangent, w_parts, w_out, modulation)


LOG2_E = math.log2(math.e)
INV_ROOT = 1.0 / math.sqrt(HEAD)
CHUNK = 256
TILE = 64
MAIN = 6
REACH_CHUNKS = 4


def low_lanes():
    return lax.broadcasted_iota(jnp.int32, (1, LANES), 1) < HEAD


def lower_mean(values):
    return jnp.sum(jnp.where(low_lanes(), values, 0.0), axis=-1, keepdims=True) * (1.0 / HEAD)


def lower_sums(values):
    ones = (lax.broadcasted_iota(jnp.int32, (LANES, LANES), 0) < HEAD).astype(F32).astype(BF16)
    squares = values * values
    large = squares.astype(BF16)
    small = (squares - large.astype(F32)).astype(BF16)
    large = jnp.dot(large, ones, preferred_element_type=F32)
    return large + jnp.dot(small, ones, preferred_element_type=F32)


def place_block(source, place, starts, ends, gains_ref, stores):
    low = low_lanes()
    rows = source.shape[0]
    at = place + lax.broadcasted_iota(jnp.int32, (rows, LANES), 0)
    same = ((at >= starts) & (at < ends)).astype(F32)
    first = source[:, 0:LANES].astype(F32)
    second = source[:, LANES:].astype(F32)

    def normed(raw, gain):
        return raw * lax.rsqrt(lower_sums(raw) * (1.0 / HEAD) + EPS) * gain

    keys = normed(second, gains_ref[1:2, :])
    queries = normed(first, gains_ref[0:1, :] * INV_ROOT)
    q_store, k_store, v_store, d_store, kv_store = stores
    q_store[...] = jnp.where(low, queries, same * SAME_IMAGE).astype(BF16)
    k_store[...] = jnp.where(low, keys, same).astype(BF16)
    v_store[...] = jnp.where(low, 0.0, first).astype(BF16)
    d_store[...] = source[:, LANES:]
    kv_store[...] = jnp.where(low, keys, first).astype(BF16).T


def window_facts(counts_ref):
    half = lax.axis_index("yh")
    origin = (block_index() // 4 - 1) * 2 * CHUNK
    own_at = (2 + half) * CHUNK
    starts, ends = image_bounds(counts_ref, HEAD)
    left_from = jnp.int32(-CHUNK)
    right_to = jnp.int32((MAIN + 1) * CHUNK)
    total = -origin
    for image in range(counts_ref.shape[0]):
        left_from = jnp.where(total <= own_at, total, left_from)
        ended = total >= own_at + CHUNK
        total = total + counts_ref[image]
        right_to = jnp.where((total >= own_at + CHUNK) & jnp.logical_not(ended), total, right_to)
    return half, own_at, starts - origin, ends - origin, left_from, right_to


def by_eight(values):
    return values.reshape(values.shape[0] // 8, 8, values.shape[1])


def add_tiles(s_ref, g_ref, rows, highest, total, grads):
    for piece in range(rows // TILE):
        at = slice(piece * TILE, (piece + 1) * TILE)
        weights = jnp.exp2(s_ref[at, :] * LOG2_E - highest)
        total = total + jnp.sum(by_eight(weights), axis=0)
        grads = grads + jnp.sum(by_eight(weights * g_ref[at, :]), axis=0)
    return total, grads


def rows_max(values):
    return jnp.max(by_eight(values), axis=0)


def near_kernel(
    counts_ref,
    gains_ref,
    first_ref,
    quad_ref,
    second_ref,
    qx_ref,
    kx_ref,
    vx_ref,
    dx_ref,
    kv_ref,
    so_ref,
    go_ref,
    sn_ref,
    gn_ref,
    stats_ref,
    s_ref,
    g_ref,
):
    half, own_at, starts, ends, left_from, right_to = window_facts(counts_ref)
    block_rows = CHUNK // 2

    def place(source, begin):
        begin = pl.multiple_of(begin, block_rows)
        at = pl.ds(begin, block_rows)
        stores = [ref.at[at, :] for ref in (qx_ref, kx_ref, vx_ref, dx_ref)]
        place_block(source, begin, starts, ends, gains_ref, stores + [kv_ref.at[:, at]])

    to_first = jnp.where(lax.rem(lax.axis_index("z"), 2) == 0, 2 * CHUNK, -2 * CHUNK)
    for block in range(4):
        at = slice(block * block_rows, (block + 1) * block_rows)
        begin = 2 * CHUNK + block * block_rows
        place(quad_ref.at[at], begin)
        place(first_ref.at[at], begin + to_first)
        place(second_ref.at[at], begin - to_first)

    own_rows = pl.ds(pl.multiple_of(own_at, CHUNK), CHUNK)
    q_own = qx_ref[own_rows, :]
    d_own = dx_ref[own_rows, :]
    highest = jnp.full((8, CHUNK), -jnp.inf, F32)
    for piece in range(MAIN):
        at = slice(piece * CHUNK, (piece + 1) * CHUNK)
        scores = rows_dot(kx_ref[at, :], q_own)
        so_ref[at, :] = scores
        highest = jnp.maximum(highest, rows_max(scores))
        go_ref[at, :] = rows_dot(vx_ref[at, :], d_own)
    highest = jnp.max(highest, axis=0, keepdims=True) * LOG2_E
    total = jnp.zeros((8, CHUNK), F32)
    grads = jnp.zeros((8, CHUNK), F32)
    for piece in range(MAIN * CHUNK // TILE):
        at = slice(piece * TILE, (piece + 1) * TILE)
        weights = jnp.exp2(so_ref[at, :] * LOG2_E - highest)
        so_ref[at, :] = weights
        total = total + jnp.sum(by_eight(weights), axis=0)
        grads = grads + jnp.sum(by_eight(weights * go_ref[at, :]), axis=0)
    stats_ref[MAIN, 0:1, :] = highest
    stats_ref[MAIN, 1:2, :] = jnp.sum(total, axis=0, keepdims=True)
    stats_ref[MAIN, 2:3, :] = jnp.sum(grads, axis=0, keepdims=True)

    left_key = jnp.clip((left_from + CHUNK) // CHUNK - 1, 0, MAIN - REACH_CHUNKS)
    right_key = jnp.clip((right_to - 1) // CHUNK - (REACH_CHUNKS - 1), 0, MAIN - REACH_CHUNKS)

    def one_chunk(step, carry):
        slot = step + jnp.where(step >= 2 + half, 1, 0)
        begin = slot * CHUNK

        @pl.when((begin < right_to) & (begin + CHUNK > left_from))
        def _():
            at = pl.ds(pl.multiple_of(begin, CHUNK), CHUNK)
            key = jnp.where(begin < own_at, left_key, right_key) * CHUNK
            q_block = qx_ref[at, :]
            d_block = dx_ref[at, :]
            highest = jnp.full((8, CHUNK), -jnp.inf, F32)
            for piece in range(REACH_CHUNKS):
                keys_at = pl.ds(pl.multiple_of(key + piece * CHUNK, CHUNK), CHUNK)
                here = slice(piece * CHUNK, (piece + 1) * CHUNK)
                scores = rows_dot(kx_ref[keys_at, :], q_block)
                s_ref[here, :] = scores
                highest = jnp.maximum(highest, rows_max(scores))
                g_ref[here, :] = rows_dot(vx_ref[keys_at, :], d_block)
            highest = jnp.max(highest, axis=0, keepdims=True) * LOG2_E
            zeros = jnp.zeros((8, CHUNK), F32)
            total, grads = add_tiles(s_ref, g_ref, REACH_CHUNKS * CHUNK, highest, zeros, zeros)
            stats_ref[slot, 0:1, :] = highest
            stats_ref[slot, 1:2, :] = jnp.sum(total, axis=0, keepdims=True)
            stats_ref[slot, 2:3, :] = jnp.sum(grads, axis=0, keepdims=True)
            near_at = pl.ds(pl.multiple_of(own_at - key, CHUNK), CHUNK)
            sn_ref[slot, :, :] = s_ref[near_at, :]
            gn_ref[slot, :, :] = g_ref[near_at, :]

        return carry

    lax.fori_loop(0, MAIN - 1, one_chunk, 0)


def attend_near(counts, gains, first, quad, second):
    rows = MAIN * CHUNK
    head_rows = jax.ShapeDtypeStruct((rows, LANES), BF16)
    scores = jax.ShapeDtypeStruct((rows, CHUNK), F32)
    tiles = jax.ShapeDtypeStruct((MAIN, CHUNK, CHUNK), F32)
    return pl.pallas_call(
        near_kernel,
        out_shape=(head_rows,) * 4
        + (jax.ShapeDtypeStruct((LANES, rows), BF16),)
        + (scores, scores, tiles, tiles, jax.ShapeDtypeStruct((MAIN + 1, 8, CHUNK), F32)),
        in_specs=[SMEM] + [VMEM] * 4,
        out_specs=(VMEM,) * 10,
        scratch_shapes=[pltpu.VMEM((REACH_CHUNKS * CHUNK, CHUNK), F32)] * 2,
        cost_estimate=pl.CostEstimate(
            flops=7000000000, bytes_accessed=1 << 20, transcendentals=1 << 20
        ),
        compiler_params=pltpu.CompilerParams(vmem_limit_bytes=VMEM_LIMIT),
    )(counts, gains, first, quad, second)


def far_kernel(
    counts_ref,
    gains_ref,
    far_ref,
    quad_ref,
    qx_ref,
    kx_ref,
    vx_ref,
    dx_ref,
    kv_ref,
    so_ref,
    go_ref,
    sn_ref,
    gn_ref,
    stats_ref,
    out_ref,
    qf_ref,
    kf_ref,
    vf_ref,
    df_ref,
    kvf_ref,
    s_ref,
    g_ref,
    p_ref,
    d_ref,
    sums_ref,
    dk_ref,
    dv_ref,
    done_ref,
):
    half, own_at, starts, ends, left_from, right_to = window_facts(counts_ref)
    block_rows = CHUNK // 2
    rows = MAIN * CHUNK
    far_at = jnp.where(half == 0, -CHUNK, rows)
    for block in range(2):
        at = slice(block * block_rows, (block + 1) * block_rows)
        stores = [ref.at[at, :] for ref in (qf_ref, kf_ref, vf_ref, df_ref)]
        place_block(
            far_ref.at[at],
            far_at + block * block_rows,
            starts,
            ends,
            gains_ref,
            stores + [kvf_ref.at[:, at]],
        )

    own_rows = pl.ds(pl.multiple_of(own_at, CHUNK), CHUNK)
    q_own = qx_ref[own_rows, :]
    d_own = dx_ref[own_rows, :]
    scores = rows_dot(kf_ref[...], q_own)
    s_ref[0:CHUNK, :] = scores
    g_ref[0:CHUNK, :] = rows_dot(vf_ref[...], d_own)
    near_highest = stats_ref[MAIN, 0:1, :]
    highest = jnp.max(rows_max(scores), axis=0, keepdims=True) * LOG2_E
    highest = jnp.maximum(near_highest, highest)
    shrink = jnp.exp2(near_highest - highest)
    zeros = jnp.zeros((8, CHUNK), F32)
    total, grads = add_tiles(s_ref, g_ref, CHUNK, highest, zeros, zeros)
    total = jnp.sum(total, axis=0, keepdims=True) + stats_ref[MAIN, 1:2, :] * shrink
    grads = jnp.sum(grads, axis=0, keepdims=True) + stats_ref[MAIN, 2:3, :] * shrink
    scale = 1.0 / total
    mean_grad = grads * scale

    def write_tile(scores, grads, highest, scale, mean_grad, to):
        probs = jnp.exp2(scores * LOG2_E - highest) * scale
        p_ref[to, :] = probs.astype(BF16)
        d_ref[to, :] = (probs * (grads - mean_grad)).astype(BF16)

    near_scale = shrink * scale
    for piece in range(rows // TILE):
        at = slice(piece * TILE, (piece + 1) * TILE)
        probs = so_ref[at, :] * near_scale
        p_ref[at, :] = probs.astype(BF16)
        d_ref[at, :] = (probs * (go_ref[at, :] - mean_grad)).astype(BF16)
    for piece in range(CHUNK // TILE):
        at = slice(piece * TILE, (piece + 1) * TILE)
        to = slice(rows + piece * TILE, rows + (piece + 1) * TILE)
        write_tile(s_ref[at, :], g_ref[at, :], highest, scale, mean_grad, to)
    dk_ref[...] = jnp.dot(d_ref[own_rows, :], q_own, preferred_element_type=F32)
    dv_ref[...] = jnp.dot(p_ref[own_rows, :], d_own, preferred_element_type=F32)

    def times_window(values_ref):
        main = jnp.dot(kv_ref[...], values_ref[0:rows, :], preferred_element_type=F32)
        return main + jnp.dot(
            kvf_ref[...], values_ref[rows : rows + CHUNK, :], preferred_element_type=F32
        )

    upper = lax.broadcasted_iota(jnp.int32, (LANES, CHUNK), 0) < HEAD
    own_out = jnp.where(upper, times_window(d_ref) * INV_ROOT, times_window(p_ref)).T

    query_lane = lax.broadcasted_iota(jnp.int32, (1, CHUNK), 1)
    reaches_far = jnp.where(half == 0, left_from < 0, right_to > rows)

    def add_gradients(tiles, begin, q_block, d_block, highest, total, grads):
        place = query_lane + begin
        scale = jnp.where((place >= left_from) & (place < right_to), 1.0 / total, 0.0)
        mean_grad = grads * scale
        for piece in range(CHUNK // TILE):
            scores, given = tiles(piece)
            at = slice(piece * TILE, (piece + 1) * TILE)
            write_tile(scores, given, highest, scale, mean_grad, at)
        dk_ref[...] += jnp.dot(d_ref[0:CHUNK, :], q_block, preferred_element_type=F32)
        dv_ref[...] += jnp.dot(p_ref[0:CHUNK, :], d_block, preferred_element_type=F32)

    def one_chunk(step, carry):
        slot = step + jnp.where(step >= 2 + half, 1, 0)
        begin = slot * CHUNK

        @pl.when((begin < right_to) & (begin + CHUNK > left_from))
        def _():
            at = pl.ds(pl.multiple_of(begin, CHUNK), CHUNK)
            q_block = qx_ref[at, :]
            d_block = dx_ref[at, :]
            sums_ref[...] = stats_ref[slot, :, :]
            same_side = (begin < own_at) == (half == 0)

            @pl.when(reaches_far & same_side)
            def _():
                scores = rows_dot(kf_ref[...], q_block)
                s_ref[0:CHUNK, :] = scores
                g_ref[0:CHUNK, :] = rows_dot(vf_ref[...], d_block)
                before = sums_ref[0:1, :]
                highest = jnp.max(rows_max(scores), axis=0, keepdims=True) * LOG2_E
                highest = jnp.maximum(before, highest)
                total, grads = add_tiles(s_ref, g_ref, CHUNK, highest, zeros, zeros)
                shrink = jnp.exp2(before - highest)
                sums_ref[0:1, :] = highest
                total = jnp.sum(total, axis=0, keepdims=True)
                grads = jnp.sum(grads, axis=0, keepdims=True)
                sums_ref[1:2, :] = sums_ref[1:2, :] * shrink + total
                sums_ref[2:3, :] = sums_ref[2:3, :] * shrink + grads

            def tiles(piece):
                at = slice(piece * TILE, (piece + 1) * TILE)
                return sn_ref[slot, at, :], gn_ref[slot, at, :]

            add_gradients(
                tiles, begin, q_block, d_block, sums_ref[0:1, :], sums_ref[1:2, :], sums_ref[2:3, :]
            )

        return carry

    lax.fori_loop(0, MAIN - 1, one_chunk, 0)

    @pl.when(reaches_far)
    def _():
        q_block = qf_ref[...]
        d_block = df_ref[...]
        key = half * (MAIN // 2) * CHUNK
        highest = jnp.full((8, CHUNK), -jnp.inf, F32)
        for piece in range(REACH_CHUNKS):
            here = slice(piece * CHUNK, (piece + 1) * CHUNK)
            if piece < REACH_CHUNKS - 1:
                keys_at = pl.ds(pl.multiple_of(key + piece * CHUNK, CHUNK), CHUNK)
                keys, values = kx_ref[keys_at, :], vx_ref[keys_at, :]
            else:
                keys, values = kf_ref[...], vf_ref[...]
            scores = rows_dot(keys, q_block)
            s_ref[here, :] = scores
            highest = jnp.maximum(highest, rows_max(scores))
            g_ref[here, :] = rows_dot(values, d_block)
        highest = jnp.max(highest, axis=0, keepdims=True) * LOG2_E
        total, grads = add_tiles(s_ref, g_ref, REACH_CHUNKS * CHUNK, highest, zeros, zeros)

        def tiles(piece):
            at = pl.ds(pl.multiple_of(own_at - key + piece * TILE, TILE), TILE)
            return s_ref[at, :], g_ref[at, :]

        add_gradients(
            tiles,
            far_at,
            q_block,
            d_block,
            highest,
            jnp.sum(total, axis=0, keepdims=True),
            jnp.sum(grads, axis=0, keepdims=True),
        )

    def norm_grad(raw, gain, d_norm):
        inverse = lax.rsqrt(lower_mean(raw * raw) + EPS)
        scaled = d_norm.astype(BF16).astype(F32) * gain
        inner = lower_mean(raw * scaled)
        return inverse * scaled - raw * (inverse * inverse * inverse * inner)

    low = low_lanes()
    own_in_quad = pl.ds(pl.multiple_of(half * CHUNK, CHUNK), CHUNK)
    raw_q = quad_ref[own_in_quad, 0:LANES].astype(F32)
    raw_k = quad_ref[own_in_quad, LANES:].astype(F32)
    d_q = norm_grad(raw_q, gains_ref[0:1, :], own_out)
    d_k = norm_grad(raw_k, gains_ref[1:2, :], dk_ref[...])
    done_ref[:, 0:LANES] = jnp.where(low, d_q, own_out).astype(BF16)
    done_ref[:, LANES:] = jnp.where(low, d_k, dv_ref[...]).astype(BF16)
    share = 16
    for member in range(out_ref.shape[0]):
        block, core = member // 2, member % 2
        for part in range(out_ref.shape[1] // share):
            begin = (block * 8 + part * 2 + core) * share
            out_ref[member, part * share : (part + 1) * share, :] = done_ref[
                begin : begin + share, :
            ]


def attend_far(counts, gains, far, quad, near_parts):
    return pl.pallas_call(
        far_kernel,
        out_shape=jax.ShapeDtypeStruct((4, CHUNK // 4, 2 * LANES), BF16),
        in_specs=[SMEM] + [VMEM] * (3 + len(near_parts)),
        out_specs=VMEM,
        scratch_shapes=[pltpu.VMEM((CHUNK, LANES), BF16)] * 4
        + [pltpu.VMEM((LANES, CHUNK), BF16)]
        + [pltpu.VMEM((REACH_CHUNKS * CHUNK, CHUNK), F32)] * 2
        + [pltpu.VMEM(((MAIN + 1) * CHUNK, CHUNK), BF16)] * 2
        + [pltpu.VMEM((8, CHUNK), F32)]
        + [pltpu.VMEM((CHUNK, LANES), F32)] * 2
        + [pltpu.VMEM((CHUNK, 2 * LANES), BF16)],
        cost_estimate=pl.CostEstimate(
            flops=7000000000, bytes_accessed=1 << 20, transcendentals=1 << 20
        ),
        compiler_params=pltpu.CompilerParams(vmem_limit_bytes=VMEM_LIMIT),
    )(counts, gains, far, quad, *near_parts)


def project_kernel(parts_ref, weights_ref, weights_far_ref, out_ref):
    rows = parts_ref.shape[1]
    width = weights_ref.shape[1]
    share = out_ref.shape[1]
    core = lax.axis_index("core")
    low = lax.broadcasted_iota(jnp.int32, (rows, LANES), 1) < HEAD

    def by_column(which):
        head0 = parts_ref[which].astype(F32)
        head1 = parts_ref[2 + which].astype(F32)
        a0, a1 = head0[:, :LANES], head1[:, :LANES]
        b0, b1 = head0[:, LANES:], head1[:, LANES:]
        d_q = jnp.where(low, a0, pltpu.roll(a1, HEAD, 1)).astype(BF16)
        attn = jnp.where(low, pltpu.roll(a0, HEAD, 1), a1).astype(BF16)
        d_k = jnp.where(low, b0, pltpu.roll(b1, HEAD, 1)).astype(BF16)
        d_v = jnp.where(low, pltpu.roll(b0, HEAD, 1), b1).astype(BF16)
        return attn, [d_q, d_k, d_v]

    attn, grads = by_column(core)
    attn_far, grads_far = by_column(1 - core)
    mixed = jnp.dot(
        jnp.concatenate([attn, attn_far], axis=1),
        jnp.concatenate([w_out_of(weights_ref), w_out_of(weights_far_ref)], axis=0),
        preferred_element_type=F32,
    ).astype(BF16)
    weights = [ref[part] for ref in (weights_ref, weights_far_ref) for part in range(3)]
    d_hidden = rows_dot(
        jnp.concatenate(grads + grads_far, axis=1), jnp.concatenate(weights, axis=1)
    ).astype(BF16)
    for place in range(out_ref.shape[0]):
        at = slice(place * share, (place + 1) * share)
        out_ref[place, :, :width] = mixed[at]
        out_ref[place, :, width:] = d_hidden[at]


def project(parts, weights, weights_far, x_count):
    return pl.pallas_call(
        project_kernel,
        out_shape=jax.ShapeDtypeStruct(
            (x_count, parts.shape[1] // x_count, 2 * weights.shape[1]), BF16
        ),
        in_specs=[VMEM] * 3,
        out_specs=VMEM,
        compiler_params=pltpu.CompilerParams(vmem_limit_bytes=VMEM_LIMIT),
    )(parts, weights, weights_far)


def ready_kernel(
    counts_ref,
    tokens_ref,
    cotangent_ref,
    modulation_ref,
    rows_ref,
    factors_ref,
):
    rows = rows_ref.shape[1]
    first_row = (lax.axis_index("x") * 2 + lax.axis_index("core")) * rows
    first = block_index() * tokens_ref.shape[0] + first_row
    _, scale, gate = modulation_rows(counts_ref, modulation_ref, first, rows)
    at = pl.ds(pl.multiple_of(first_row, rows), rows)
    normed, inv_std = layer_norm(tokens_ref[at, :].astype(F32))
    rows_ref[0] = tokens_ref[at, :]
    rows_ref[1] = cotangent_ref[at, :]
    factors_ref[0] = gate
    factors_ref[1] = 1.0 + scale
    factors_ref[2] = normed
    factors_ref[3] = jnp.broadcast_to(inv_std, normed.shape)


def ready(counts, tokens, cotangent, modulation, share):
    width = tokens.shape[1]
    return pl.pallas_call(
        ready_kernel,
        out_shape=(
            jax.ShapeDtypeStruct((2, share, width), BF16),
            jax.ShapeDtypeStruct((4, share, width), F32),
        ),
        in_specs=[SMEM] + [VMEM] * 3,
        out_specs=(VMEM, VMEM),
        compiler_params=pltpu.CompilerParams(vmem_limit_bytes=VMEM_LIMIT),
    )(counts, tokens, cotangent, modulation)


def leave_kernel(rows_ref, factors_ref, shares_ref, layer_ref, grad_ref):
    width = layer_ref.shape[1]
    sums = shares_ref[0].astype(F32)
    for share in range(1, shares_ref.shape[0]):
        sums = sums + shares_ref[share].astype(F32)
    layer = rows_ref[0].astype(F32) + factors_ref[0] * sums[:, :width]
    layer_ref[...] = layer.astype(BF16)
    d_normed = sums[:, width:] * factors_ref[1]
    normed = factors_ref[2]
    input_grad = rows_ref[1].astype(F32) + factors_ref[3] * (
        d_normed
        - jnp.mean(d_normed, axis=-1, keepdims=True)
        - normed * jnp.mean(d_normed * normed, axis=-1, keepdims=True)
    )
    grad_ref[...] = input_grad.astype(BF16)


def leave(rows, factors, shares):
    out = jax.ShapeDtypeStruct(rows.shape[1:], BF16)
    return pl.pallas_call(
        leave_kernel,
        out_shape=(out, out),
        in_specs=[VMEM] * 3,
        out_specs=(VMEM, VMEM),
        compiler_params=pltpu.CompilerParams(vmem_limit_bytes=VMEM_LIMIT),
    )(rows, factors, shares)


def per_device(tokens, cotangent, w_qkv, w_out, qk_gain, modulation, image_counts):
    tok_rows, model_width = tokens.shape
    z_count = lax.axis_size("z")
    x_count = lax.axis_size("x")
    quad = 4
    pair_rows = 2 * tok_rows
    share = tok_rows // (2 * x_count)
    w_parts = w_qkv.transpose(1, 0, 2)
    mod_parts = modulation.transpose(1, 0, 2)
    gains = jnp.pad(qk_gain, ((0, 6), (0, LANES - HEAD)))

    heads, weights = enter(image_counts, tokens, cotangent, w_parts, w_out, mod_parts, quad)
    mine = lax.all_to_all(heads, ("yh", "yl"), 0, 0)
    mine = mine.reshape(quad * tok_rows, 2 * LANES)
    evens = range(0, z_count, 2)
    swaps = [(i, i + 1) for i in evens], [((i - 1) % z_count, i) for i in evens]
    first, second = (
        lax.ppermute(mine, "z", pairs + [(j, i) for i, j in pairs]) for pairs in swaps
    )
    halves = 4 * z_count
    far_half = jnp.where(
        lax.axis_index("yh") == lax.axis_index("core"), mine[pair_rows:], mine[:pair_rows]
    )

    def far_source(target):
        z, yh, core = target // 4, target // 2 % 2, target % 2
        return (z + (2 if yh else -2)) % z_count * 4 + (yh ^ core) * 2 + core

    far = lax.ppermute(
        far_half, ("z", "yh", "core"), [(far_source(i), i) for i in range(halves)]
    )
    _, tokens_late, cotangent_late, mod_late = lax.optimization_barrier(
        (mine, tokens, cotangent, mod_parts)
    )
    rows, factors = ready(image_counts, tokens_late, cotangent_late, mod_late, share)
    near_parts = attend_near(image_counts, gains, first, mine, second)
    _, weights_late = lax.optimization_barrier((mine, weights))
    weights_far = lax.ppermute(weights_late, "core", [(0, 1), (1, 0)])
    parts = attend_far(image_counts, gains, far, mine, near_parts)
    parts = lax.all_to_all(parts, ("yl", "core"), 0, 0)
    partial = project(parts, weights, weights_far, x_count)
    shares = lax.all_to_all(partial, "x", 0, 0)
    return leave(rows, factors, shares)


def solution(mesh):
    split = jax.sharding.Mesh(mesh.devices.reshape(16, 2, 2, 4, 2), ("z", "yh", "yl", "x", "core"))
    dp, head = ("z", "yh", "yl"), ("x", "core")
    in_specs = (P(dp, None), P(dp, None), P(None, None, head), P(head, None), P(), P(), P())
    out_specs = (P(dp + head, None), P(dp + head, None))
    return jax.shard_map(
        per_device, mesh=split, in_specs=in_specs, out_specs=out_specs, check_vma=False
    )
```

```python
import math

import jax
import jax.numpy as jnp
from jax import lax
from jax.experimental import pallas as pl
from jax.experimental.pallas import tpu as pltpu
from jax.sharding import PartitionSpec as P

EPS = 1e-06
SAME_IMAGE = 512.0
LANES = 128
HEAD = 64
F32 = jnp.float32
BF16 = jnp.bfloat16
VMEM_LIMIT = 24 * 1024 * 1024
ENTER_LIMIT = 60 * 1024 * 1024
VMEM = pl.BlockSpec(memory_space=pltpu.VMEM)
SMEM = pl.BlockSpec(memory_space=pltpu.SMEM)


def rows_dot(a, b):
    return lax.dot_general(a, b, (((1,), (1,)), ((), ())), preferred_element_type=F32)


def block_index():
    return (lax.axis_index("z") * 2 + lax.axis_index("yh")) * 2 + lax.axis_index("yl")


def image_bounds(counts_ref, first_lane):
    lane = lax.broadcasted_iota(jnp.int32, (1, LANES), 1)
    starts = jnp.zeros((1, LANES), jnp.int32)
    ends = jnp.zeros((1, LANES), jnp.int32)
    total = jnp.int32(0)
    for image in range(counts_ref.shape[0]):
        here = lane == first_lane + image
        starts = jnp.where(here, total, starts)
        total = total + counts_ref[image]
        ends = jnp.where(here, total, ends)
    return starts, ends


def modulation_rows(counts_ref, modulation_ref, first, rows):
    starts, ends = image_bounds(counts_ref, 0)
    place = first + lax.broadcasted_iota(jnp.int32, (rows, LANES), 0)
    member = ((place >= starts) & (place < ends)).astype(F32).astype(BF16)
    member = member[:, : modulation_ref.shape[1]]
    return [
        jnp.dot(member, modulation_ref[part], preferred_element_type=F32) for part in range(3)
    ]


def layer_norm(values):
    average = jnp.mean(values, axis=-1, keepdims=True)
    centred = values - average
    inv_std = lax.rsqrt(jnp.mean(centred * centred, axis=-1, keepdims=True) + EPS)
    return centred * inv_std, inv_std


def w_out_of(weights_ref):
    tiles = weights_ref.shape[1] // LANES
    return jnp.concatenate(
        [weights_ref[3, tile * LANES : (tile + 1) * LANES, :] for tile in range(tiles)], axis=1
    )


def enter_kernel(
    counts_ref, tokens_ref, cotangent_ref, w_qkv_ref, w_out_ref, modulation_ref, out_ref
):
    rows = tokens_ref.shape[0]
    first = block_index() * rows
    shift, scale, gate = modulation_rows(counts_ref, modulation_ref, first, rows)
    normed, _ = layer_norm(tokens_ref[...].astype(F32))
    hidden = (normed * (1.0 + scale) + shift).astype(BF16)
    weights = jnp.concatenate([w_qkv_ref[part] for part in range(3)], axis=1)
    qkv = jnp.dot(hidden, weights, preferred_element_type=F32)
    q, k, v = (qkv[:, part * LANES : (part + 1) * LANES] for part in range(3))
    d_mixed = (cotangent_ref[...].astype(F32) * gate).astype(BF16)
    d_attn = rows_dot(d_mixed, w_out_ref[...])
    low = lax.broadcasted_iota(jnp.int32, (rows, LANES), 1) < HEAD

    def beside(left, right):
        return jnp.where(low, left, right).astype(BF16)

    q_v = (beside(q, pltpu.roll(v, HEAD, 1)), beside(pltpu.roll(q, HEAD, 1), v))
    k_d = (beside(k, pltpu.roll(d_attn, HEAD, 1)), beside(pltpu.roll(k, HEAD, 1), d_attn))
    for place in range(out_ref.shape[0]):
        out_ref[place, :, 0:LANES] = q_v[place % 2]
        out_ref[place, :, LANES:] = k_d[place % 2]


def enter(counts, tokens, cotangent, w_parts, w_out, modulation, quad):
    return pl.pallas_call(
        enter_kernel,
        out_shape=jax.ShapeDtypeStruct((quad, tokens.shape[0], 2 * LANES), BF16),
        in_specs=[SMEM] + [VMEM] * 5,
        out_specs=VMEM,
        compiler_params=pltpu.CompilerParams(vmem_limit_bytes=ENTER_LIMIT),
    )(counts, tokens, cotangent, w_parts, w_out, modulation)


def pack_kernel(w_qkv_ref, w_out_ref, weights_ref, sems):
    pairs = [(w_qkv_ref, weights_ref.at[0:3])]
    for tile in range(weights_ref.shape[1] // LANES):
        at = slice(tile * LANES, (tile + 1) * LANES)
        pairs.append((w_out_ref.at[:, at], weights_ref.at[3, at, :]))
    copies = [
        pltpu.make_async_copy(source, target, sems.at[place])
        for place, (source, target) in enumerate(pairs)
    ]
    for copy in copies:
        copy.start()
    for copy in copies:
        copy.wait()


def pack(w_parts, w_out):
    width = w_out.shape[1]
    whole = pl.BlockSpec(memory_space=pl.ANY)
    return pl.pallas_call(
        pack_kernel,
        out_shape=jax.ShapeDtypeStruct((4, width, LANES), BF16),
        in_specs=[whole] * 2,
        out_specs=VMEM,
        scratch_shapes=[pltpu.SemaphoreType.DMA((1 + width // LANES,))],
        compiler_params=pltpu.CompilerParams(vmem_limit_bytes=8 * 1024 * 1024),
    )(w_parts, w_out)


def w_out_of(weights_ref):
    tiles = weights_ref.shape[1] // LANES
    return jnp.concatenate(
        [weights_ref[3, tile * LANES : (tile + 1) * LANES, :] for tile in range(tiles)], axis=1
    )


LOG2_E = math.log2(math.e)
INV_ROOT = 1.0 / math.sqrt(HEAD)
CHUNK = 256
TILE = 64
MAIN = 6
REACH_CHUNKS = 4


def low_lanes():
    return lax.broadcasted_iota(jnp.int32, (1, LANES), 1) < HEAD


def lower_mean(values):
    return jnp.sum(jnp.where(low_lanes(), values, 0.0), axis=-1, keepdims=True) * (1.0 / HEAD)


def lower_sums(values):
    ones = (lax.broadcasted_iota(jnp.int32, (LANES, LANES), 0) < HEAD).astype(F32).astype(BF16)
    squares = values * values
    large = squares.astype(BF16)
    small = (squares - large.astype(F32)).astype(BF16)
    large = jnp.dot(large, ones, preferred_element_type=F32)
    return large + jnp.dot(small, ones, preferred_element_type=F32)


def place_block(source, place, starts, ends, gains_ref, stores):
    low = low_lanes()
    rows = source.shape[0]
    at = place + lax.broadcasted_iota(jnp.int32, (rows, LANES), 0)
    same = ((at >= starts) & (at < ends)).astype(F32)
    first = source[:, 0:LANES].astype(F32)
    second = source[:, LANES:].astype(F32)

    def normed(raw, gain):
        return raw * lax.rsqrt(lower_sums(raw) * (1.0 / HEAD) + EPS) * gain

    keys = normed(second, gains_ref[1:2, :])
    queries = normed(first, gains_ref[0:1, :] * INV_ROOT)
    q_store, k_store, v_store, d_store, kv_store = stores
    q_store[...] = jnp.where(low, queries, same * SAME_IMAGE).astype(BF16)
    k_store[...] = jnp.where(low, keys, same).astype(BF16)
    v_store[...] = jnp.where(low, 0.0, first).astype(BF16)
    d_store[...] = source[:, LANES:]
    kv_store[...] = jnp.where(low, keys, first).astype(BF16).T


def window_facts(counts_ref):
    half = lax.axis_index("yh")
    origin = (block_index() // 4 - 1) * 2 * CHUNK
    own_at = (2 + half) * CHUNK
    starts, ends = image_bounds(counts_ref, HEAD)
    left_from = jnp.int32(-CHUNK)
    right_to = jnp.int32((MAIN + 1) * CHUNK)
    total = -origin
    for image in range(counts_ref.shape[0]):
        left_from = jnp.where(total <= own_at, total, left_from)
        ended = total >= own_at + CHUNK
        total = total + counts_ref[image]
        right_to = jnp.where((total >= own_at + CHUNK) & jnp.logical_not(ended), total, right_to)
    return half, own_at, starts - origin, ends - origin, left_from, right_to


def by_eight(values):
    return values.reshape(values.shape[0] // 8, 8, values.shape[1])


def add_tiles(s_ref, g_ref, rows, highest, total, grads):
    for piece in range(rows // TILE):
        at = slice(piece * TILE, (piece + 1) * TILE)
        weights = jnp.exp2(s_ref[at, :] * LOG2_E - highest)
        total = total + jnp.sum(by_eight(weights), axis=0)
        grads = grads + jnp.sum(by_eight(weights * g_ref[at, :]), axis=0)
    return total, grads


def rows_max(values):
    return jnp.max(by_eight(values), axis=0)


def near_kernel(
    counts_ref,
    gains_ref,
    first_ref,
    quad_ref,
    second_ref,
    qx_ref,
    kx_ref,
    vx_ref,
    dx_ref,
    kv_ref,
    so_ref,
    go_ref,
    sn_ref,
    gn_ref,
    stats_ref,
    s_ref,
    g_ref,
):
    half, own_at, starts, ends, left_from, right_to = window_facts(counts_ref)
    block_rows = CHUNK // 2

    def place(source, begin):
        begin = pl.multiple_of(begin, block_rows)
        at = pl.ds(begin, block_rows)
        stores = [ref.at[at, :] for ref in (qx_ref, kx_ref, vx_ref, dx_ref)]
        place_block(source, begin, starts, ends, gains_ref, stores + [kv_ref.at[:, at]])

    to_first = jnp.where(lax.rem(lax.axis_index("z"), 2) == 0, 2 * CHUNK, -2 * CHUNK)
    for block in range(4):
        at = slice(block * block_rows, (block + 1) * block_rows)
        begin = 2 * CHUNK + block * block_rows
        place(quad_ref.at[at], begin)
        place(first_ref.at[at], begin + to_first)
        place(second_ref.at[at], begin - to_first)

    own_rows = pl.ds(pl.multiple_of(own_at, CHUNK), CHUNK)
    q_own = qx_ref[own_rows, :]
    d_own = dx_ref[own_rows, :]
    highest = jnp.full((8, CHUNK), -jnp.inf, F32)
    for piece in range(MAIN):
        at = slice(piece * CHUNK, (piece + 1) * CHUNK)
        scores = rows_dot(kx_ref[at, :], q_own)
        so_ref[at, :] = scores
        highest = jnp.maximum(highest, rows_max(scores))
        go_ref[at, :] = rows_dot(vx_ref[at, :], d_own)
    highest = jnp.max(highest, axis=0, keepdims=True) * LOG2_E
    total = jnp.zeros((8, CHUNK), F32)
    grads = jnp.zeros((8, CHUNK), F32)
    for piece in range(MAIN * CHUNK // TILE):
        at = slice(piece * TILE, (piece + 1) * TILE)
        weights = jnp.exp2(so_ref[at, :] * LOG2_E - highest)
        so_ref[at, :] = weights
        total = total + jnp.sum(by_eight(weights), axis=0)
        grads = grads + jnp.sum(by_eight(weights * go_ref[at, :]), axis=0)
    stats_ref[MAIN, 0:1, :] = highest
    stats_ref[MAIN, 1:2, :] = jnp.sum(total, axis=0, keepdims=True)
    stats_ref[MAIN, 2:3, :] = jnp.sum(grads, axis=0, keepdims=True)

    left_key = jnp.clip((left_from + CHUNK) // CHUNK - 1, 0, MAIN - REACH_CHUNKS)
    right_key = jnp.clip((right_to - 1) // CHUNK - (REACH_CHUNKS - 1), 0, MAIN - REACH_CHUNKS)

    def one_chunk(step, carry):
        slot = step + jnp.where(step >= 2 + half, 1, 0)
        begin = slot * CHUNK

        @pl.when((begin < right_to) & (begin + CHUNK > left_from))
        def _():
            at = pl.ds(pl.multiple_of(begin, CHUNK), CHUNK)
            key = jnp.where(begin < own_at, left_key, right_key) * CHUNK
            q_block = qx_ref[at, :]
            d_block = dx_ref[at, :]
            highest = jnp.full((8, CHUNK), -jnp.inf, F32)
            for piece in range(REACH_CHUNKS):
                keys_at = pl.ds(pl.multiple_of(key + piece * CHUNK, CHUNK), CHUNK)
                here = slice(piece * CHUNK, (piece + 1) * CHUNK)
                scores = rows_dot(kx_ref[keys_at, :], q_block)
                s_ref[here, :] = scores
                highest = jnp.maximum(highest, rows_max(scores))
                g_ref[here, :] = rows_dot(vx_ref[keys_at, :], d_block)
            highest = jnp.max(highest, axis=0, keepdims=True) * LOG2_E
            zeros = jnp.zeros((8, CHUNK), F32)
            total, grads = add_tiles(s_ref, g_ref, REACH_CHUNKS * CHUNK, highest, zeros, zeros)
            stats_ref[slot, 0:1, :] = highest
            stats_ref[slot, 1:2, :] = jnp.sum(total, axis=0, keepdims=True)
            stats_ref[slot, 2:3, :] = jnp.sum(grads, axis=0, keepdims=True)
            near_at = pl.ds(pl.multiple_of(own_at - key, CHUNK), CHUNK)
            sn_ref[slot, :, :] = s_ref[near_at, :]
            gn_ref[slot, :, :] = g_ref[near_at, :]

        return carry

    lax.fori_loop(0, MAIN - 1, one_chunk, 0)


def attend_near(counts, gains, first, quad, second):
    rows = MAIN * CHUNK
    head_rows = jax.ShapeDtypeStruct((rows, LANES), BF16)
    scores = jax.ShapeDtypeStruct((rows, CHUNK), F32)
    tiles = jax.ShapeDtypeStruct((MAIN, CHUNK, CHUNK), F32)
    return pl.pallas_call(
        near_kernel,
        out_shape=(head_rows,) * 4
        + (jax.ShapeDtypeStruct((LANES, rows), BF16),)
        + (scores, scores, tiles, tiles, jax.ShapeDtypeStruct((MAIN + 1, 8, CHUNK), F32)),
        in_specs=[SMEM] + [VMEM] * 4,
        out_specs=(VMEM,) * 10,
        scratch_shapes=[pltpu.VMEM((REACH_CHUNKS * CHUNK, CHUNK), F32)] * 2,
        cost_estimate=pl.CostEstimate(
            flops=7000000000, bytes_accessed=1 << 20, transcendentals=1 << 20
        ),
        compiler_params=pltpu.CompilerParams(vmem_limit_bytes=VMEM_LIMIT),
    )(counts, gains, first, quad, second)


def far_kernel(
    counts_ref,
    gains_ref,
    far_ref,
    quad_ref,
    qx_ref,
    kx_ref,
    vx_ref,
    dx_ref,
    kv_ref,
    so_ref,
    go_ref,
    sn_ref,
    gn_ref,
    stats_ref,
    out_ref,
    qf_ref,
    kf_ref,
    vf_ref,
    df_ref,
    kvf_ref,
    s_ref,
    g_ref,
    p_ref,
    d_ref,
    sums_ref,
    dk_ref,
    dv_ref,
    done_ref,
):
    half, own_at, starts, ends, left_from, right_to = window_facts(counts_ref)
    block_rows = CHUNK // 2
    rows = MAIN * CHUNK
    far_at = jnp.where(half == 0, -CHUNK, rows)
    for block in range(2):
        at = slice(block * block_rows, (block + 1) * block_rows)
        stores = [ref.at[at, :] for ref in (qf_ref, kf_ref, vf_ref, df_ref)]
        place_block(
            far_ref.at[at],
            far_at + block * block_rows,
            starts,
            ends,
            gains_ref,
            stores + [kvf_ref.at[:, at]],
        )

    own_rows = pl.ds(pl.multiple_of(own_at, CHUNK), CHUNK)
    q_own = qx_ref[own_rows, :]
    d_own = dx_ref[own_rows, :]
    scores = rows_dot(kf_ref[...], q_own)
    s_ref[0:CHUNK, :] = scores
    g_ref[0:CHUNK, :] = rows_dot(vf_ref[...], d_own)
    near_highest = stats_ref[MAIN, 0:1, :]
    highest = jnp.max(rows_max(scores), axis=0, keepdims=True) * LOG2_E
    highest = jnp.maximum(near_highest, highest)
    shrink = jnp.exp2(near_highest - highest)
    zeros = jnp.zeros((8, CHUNK), F32)
    total, grads = add_tiles(s_ref, g_ref, CHUNK, highest, zeros, zeros)
    total = jnp.sum(total, axis=0, keepdims=True) + stats_ref[MAIN, 1:2, :] * shrink
    grads = jnp.sum(grads, axis=0, keepdims=True) + stats_ref[MAIN, 2:3, :] * shrink
    scale = 1.0 / total
    mean_grad = grads * scale

    def write_tile(scores, grads, highest, scale, mean_grad, to):
        probs = jnp.exp2(scores * LOG2_E - highest) * scale
        p_ref[to, :] = probs.astype(BF16)
        d_ref[to, :] = (probs * (grads - mean_grad)).astype(BF16)

    near_scale = shrink * scale
    for piece in range(rows // TILE):
        at = slice(piece * TILE, (piece + 1) * TILE)
        probs = so_ref[at, :] * near_scale
        p_ref[at, :] = probs.astype(BF16)
        d_ref[at, :] = (probs * (go_ref[at, :] - mean_grad)).astype(BF16)
    for piece in range(CHUNK // TILE):
        at = slice(piece * TILE, (piece + 1) * TILE)
        to = slice(rows + piece * TILE, rows + (piece + 1) * TILE)
        write_tile(s_ref[at, :], g_ref[at, :], highest, scale, mean_grad, to)
    dk_ref[...] = jnp.dot(d_ref[own_rows, :], q_own, preferred_element_type=F32)
    dv_ref[...] = jnp.dot(p_ref[own_rows, :], d_own, preferred_element_type=F32)

    def times_window(values_ref):
        main = jnp.dot(kv_ref[...], values_ref[0:rows, :], preferred_element_type=F32)
        return main + jnp.dot(
            kvf_ref[...], values_ref[rows : rows + CHUNK, :], preferred_element_type=F32
        )

    upper = lax.broadcasted_iota(jnp.int32, (LANES, CHUNK), 0) < HEAD
    own_out = jnp.where(upper, times_window(d_ref) * INV_ROOT, times_window(p_ref)).T

    query_lane = lax.broadcasted_iota(jnp.int32, (1, CHUNK), 1)
    reaches_far = jnp.where(half == 0, left_from < 0, right_to > rows)

    def add_gradients(tiles, begin, q_block, d_block, highest, total, grads):
        place = query_lane + begin
        scale = jnp.where((place >= left_from) & (place < right_to), 1.0 / total, 0.0)
        mean_grad = grads * scale
        for piece in range(CHUNK // TILE):
            scores, given = tiles(piece)
            at = slice(piece * TILE, (piece + 1) * TILE)
            write_tile(scores, given, highest, scale, mean_grad, at)
        dk_ref[...] += jnp.dot(d_ref[0:CHUNK, :], q_block, preferred_element_type=F32)
        dv_ref[...] += jnp.dot(p_ref[0:CHUNK, :], d_block, preferred_element_type=F32)

    def one_chunk(step, carry):
        slot = step + jnp.where(step >= 2 + half, 1, 0)
        begin = slot * CHUNK

        @pl.when((begin < right_to) & (begin + CHUNK > left_from))
        def _():
            at = pl.ds(pl.multiple_of(begin, CHUNK), CHUNK)
            q_block = qx_ref[at, :]
            d_block = dx_ref[at, :]
            sums_ref[...] = stats_ref[slot, :, :]
            same_side = (begin < own_at) == (half == 0)

            @pl.when(reaches_far & same_side)
            def _():
                scores = rows_dot(kf_ref[...], q_block)
                s_ref[0:CHUNK, :] = scores
                g_ref[0:CHUNK, :] = rows_dot(vf_ref[...], d_block)
                before = sums_ref[0:1, :]
                highest = jnp.max(rows_max(scores), axis=0, keepdims=True) * LOG2_E
                highest = jnp.maximum(before, highest)
                total, grads = add_tiles(s_ref, g_ref, CHUNK, highest, zeros, zeros)
                shrink = jnp.exp2(before - highest)
                sums_ref[0:1, :] = highest
                total = jnp.sum(total, axis=0, keepdims=True)
                grads = jnp.sum(grads, axis=0, keepdims=True)
                sums_ref[1:2, :] = sums_ref[1:2, :] * shrink + total
                sums_ref[2:3, :] = sums_ref[2:3, :] * shrink + grads

            def tiles(piece):
                at = slice(piece * TILE, (piece + 1) * TILE)
                return sn_ref[slot, at, :], gn_ref[slot, at, :]

            add_gradients(
                tiles, begin, q_block, d_block, sums_ref[0:1, :], sums_ref[1:2, :], sums_ref[2:3, :]
            )

        return carry

    lax.fori_loop(0, MAIN - 1, one_chunk, 0)

    @pl.when(reaches_far)
    def _():
        q_block = qf_ref[...]
        d_block = df_ref[...]
        key = half * (MAIN // 2) * CHUNK
        highest = jnp.full((8, CHUNK), -jnp.inf, F32)
        for piece in range(REACH_CHUNKS):
            here = slice(piece * CHUNK, (piece + 1) * CHUNK)
            if piece < REACH_CHUNKS - 1:
                keys_at = pl.ds(pl.multiple_of(key + piece * CHUNK, CHUNK), CHUNK)
                keys, values = kx_ref[keys_at, :], vx_ref[keys_at, :]
            else:
                keys, values = kf_ref[...], vf_ref[...]
            scores = rows_dot(keys, q_block)
            s_ref[here, :] = scores
            highest = jnp.maximum(highest, rows_max(scores))
            g_ref[here, :] = rows_dot(values, d_block)
        highest = jnp.max(highest, axis=0, keepdims=True) * LOG2_E
        total, grads = add_tiles(s_ref, g_ref, REACH_CHUNKS * CHUNK, highest, zeros, zeros)

        def tiles(piece):
            at = pl.ds(pl.multiple_of(own_at - key + piece * TILE, TILE), TILE)
            return s_ref[at, :], g_ref[at, :]

        add_gradients(
            tiles,
            far_at,
            q_block,
            d_block,
            highest,
            jnp.sum(total, axis=0, keepdims=True),
            jnp.sum(grads, axis=0, keepdims=True),
        )

    def norm_grad(raw, gain, d_norm):
        inverse = lax.rsqrt(lower_mean(raw * raw) + EPS)
        scaled = d_norm.astype(BF16).astype(F32) * gain
        inner = lower_mean(raw * scaled)
        return inverse * scaled - raw * (inverse * inverse * inverse * inner)

    low = low_lanes()
    own_in_quad = pl.ds(pl.multiple_of(half * CHUNK, CHUNK), CHUNK)
    raw_q = quad_ref[own_in_quad, 0:LANES].astype(F32)
    raw_k = quad_ref[own_in_quad, LANES:].astype(F32)
    d_q = norm_grad(raw_q, gains_ref[0:1, :], own_out)
    d_k = norm_grad(raw_k, gains_ref[1:2, :], dk_ref[...])
    done_ref[:, 0:LANES] = jnp.where(low, d_q, own_out).astype(BF16)
    done_ref[:, LANES:] = jnp.where(low, d_k, dv_ref[...]).astype(BF16)
    share = 16
    for member in range(out_ref.shape[0]):
        block, core = member // 2, member % 2
        for part in range(out_ref.shape[1] // share):
            begin = (block * 8 + part * 2 + core) * share
            out_ref[member, part * share : (part + 1) * share, :] = done_ref[
                begin : begin + share, :
            ]


def attend_far(counts, gains, far, quad, near_parts):
    return pl.pallas_call(
        far_kernel,
        out_shape=jax.ShapeDtypeStruct((4, CHUNK // 4, 2 * LANES), BF16),
        in_specs=[SMEM] + [VMEM] * (3 + len(near_parts)),
        out_specs=VMEM,
        scratch_shapes=[pltpu.VMEM((CHUNK, LANES), BF16)] * 4
        + [pltpu.VMEM((LANES, CHUNK), BF16)]
        + [pltpu.VMEM((REACH_CHUNKS * CHUNK, CHUNK), F32)] * 2
        + [pltpu.VMEM(((MAIN + 1) * CHUNK, CHUNK), BF16)] * 2
        + [pltpu.VMEM((8, CHUNK), F32)]
        + [pltpu.VMEM((CHUNK, LANES), F32)] * 2
        + [pltpu.VMEM((CHUNK, 2 * LANES), BF16)],
        cost_estimate=pl.CostEstimate(
            flops=7000000000, bytes_accessed=1 << 20, transcendentals=1 << 20
        ),
        compiler_params=pltpu.CompilerParams(vmem_limit_bytes=VMEM_LIMIT),
    )(counts, gains, far, quad, *near_parts)


def project_kernel(parts_ref, weights_ref, weights_far_ref, out_ref):
    rows = parts_ref.shape[1]
    width = weights_ref.shape[1]
    share = out_ref.shape[1]
    core = lax.axis_index("core")
    low = lax.broadcasted_iota(jnp.int32, (rows, LANES), 1) < HEAD

    def by_column(which):
        head0 = parts_ref[which].astype(F32)
        head1 = parts_ref[2 + which].astype(F32)
        a0, a1 = head0[:, :LANES], head1[:, :LANES]
        b0, b1 = head0[:, LANES:], head1[:, LANES:]
        d_q = jnp.where(low, a0, pltpu.roll(a1, HEAD, 1)).astype(BF16)
        attn = jnp.where(low, pltpu.roll(a0, HEAD, 1), a1).astype(BF16)
        d_k = jnp.where(low, b0, pltpu.roll(b1, HEAD, 1)).astype(BF16)
        d_v = jnp.where(low, pltpu.roll(b0, HEAD, 1), b1).astype(BF16)
        return attn, [d_q, d_k, d_v]

    attn, grads = by_column(core)
    attn_far, grads_far = by_column(1 - core)
    mixed = jnp.dot(
        jnp.concatenate([attn, attn_far], axis=1),
        jnp.concatenate([w_out_of(weights_ref), w_out_of(weights_far_ref)], axis=0),
        preferred_element_type=F32,
    ).astype(BF16)
    weights = [ref[part] for ref in (weights_ref, weights_far_ref) for part in range(3)]
    d_hidden = rows_dot(
        jnp.concatenate(grads + grads_far, axis=1), jnp.concatenate(weights, axis=1)
    ).astype(BF16)
    for place in range(out_ref.shape[0]):
        at = slice(place * share, (place + 1) * share)
        out_ref[place, :, :width] = mixed[at]
        out_ref[place, :, width:] = d_hidden[at]


def project(parts, weights, weights_far, x_count):
    return pl.pallas_call(
        project_kernel,
        out_shape=jax.ShapeDtypeStruct(
            (x_count, parts.shape[1] // x_count, 2 * weights.shape[1]), BF16
        ),
        in_specs=[VMEM] * 3,
        out_specs=VMEM,
        compiler_params=pltpu.CompilerParams(vmem_limit_bytes=VMEM_LIMIT),
    )(parts, weights, weights_far)


def ready_kernel(
    counts_ref,
    tokens_ref,
    cotangent_ref,
    modulation_ref,
    rows_ref,
    factors_ref,
):
    rows = rows_ref.shape[1]
    first_row = (lax.axis_index("x") * 2 + lax.axis_index("core")) * rows
    first = block_index() * tokens_ref.shape[0] + first_row
    _, scale, gate = modulation_rows(counts_ref, modulation_ref, first, rows)
    at = pl.ds(pl.multiple_of(first_row, rows), rows)
    normed, inv_std = layer_norm(tokens_ref[at, :].astype(F32))
    rows_ref[0] = tokens_ref[at, :]
    rows_ref[1] = cotangent_ref[at, :]
    factors_ref[0] = gate
    factors_ref[1] = 1.0 + scale
    factors_ref[2] = normed
    factors_ref[3] = jnp.broadcast_to(inv_std, normed.shape)


def ready(counts, tokens, cotangent, modulation, share):
    width = tokens.shape[1]
    return pl.pallas_call(
        ready_kernel,
        out_shape=(
            jax.ShapeDtypeStruct((2, share, width), BF16),
            jax.ShapeDtypeStruct((4, share, width), F32),
        ),
        in_specs=[SMEM] + [VMEM] * 3,
        out_specs=(VMEM, VMEM),
        compiler_params=pltpu.CompilerParams(vmem_limit_bytes=VMEM_LIMIT),
    )(counts, tokens, cotangent, modulation)


def leave_kernel(rows_ref, factors_ref, shares_ref, layer_ref, grad_ref):
    width = layer_ref.shape[1]
    sums = shares_ref[0].astype(F32)
    for share in range(1, shares_ref.shape[0]):
        sums = sums + shares_ref[share].astype(F32)
    layer = rows_ref[0].astype(F32) + factors_ref[0] * sums[:, :width]
    layer_ref[...] = layer.astype(BF16)
    d_normed = sums[:, width:] * factors_ref[1]
    normed = factors_ref[2]
    input_grad = rows_ref[1].astype(F32) + factors_ref[3] * (
        d_normed
        - jnp.mean(d_normed, axis=-1, keepdims=True)
        - normed * jnp.mean(d_normed * normed, axis=-1, keepdims=True)
    )
    grad_ref[...] = input_grad.astype(BF16)


def leave(rows, factors, shares):
    out = jax.ShapeDtypeStruct(rows.shape[1:], BF16)
    return pl.pallas_call(
        leave_kernel,
        out_shape=(out, out),
        in_specs=[VMEM] * 3,
        out_specs=(VMEM, VMEM),
        compiler_params=pltpu.CompilerParams(vmem_limit_bytes=VMEM_LIMIT),
    )(rows, factors, shares)


def per_device(tokens, cotangent, w_qkv, w_out, qk_gain, modulation, image_counts):
    tok_rows, model_width = tokens.shape
    z_count = lax.axis_size("z")
    x_count = lax.axis_size("x")
    quad = 4
    pair_rows = 2 * tok_rows
    share = tok_rows // (2 * x_count)
    w_parts = w_qkv.transpose(1, 0, 2)
    mod_parts = modulation.transpose(1, 0, 2)
    gains = jnp.pad(qk_gain, ((0, 6), (0, LANES - HEAD)))

    heads = enter(image_counts, tokens, cotangent, w_parts, w_out, mod_parts, quad)
    mine = lax.all_to_all(heads, ("yh", "yl"), 0, 0)
    mine = mine.reshape(quad * tok_rows, 2 * LANES)
    evens = range(0, z_count, 2)
    swaps = [(i, i + 1) for i in evens], [((i - 1) % z_count, i) for i in evens]
    first, second = (
        lax.ppermute(mine, "z", pairs + [(j, i) for i, j in pairs]) for pairs in swaps
    )
    halves = 4 * z_count
    far_half = jnp.where(
        lax.axis_index("yh") == lax.axis_index("core"), mine[pair_rows:], mine[:pair_rows]
    )

    def far_source(target):
        z, yh, core = target // 4, target // 2 % 2, target % 2
        return (z + (2 if yh else -2)) % z_count * 4 + (yh ^ core) * 2 + core

    far = lax.ppermute(
        far_half, ("z", "yh", "core"), [(far_source(i), i) for i in range(halves)]
    )
    _, tokens_late, cotangent_late, mod_late = lax.optimization_barrier(
        (mine, tokens, cotangent, mod_parts)
    )
    rows, factors = ready(image_counts, tokens_late, cotangent_late, mod_late, share)
    near_parts = attend_near(image_counts, gains, first, mine, second)
    _, w_parts_late, w_out_late = lax.optimization_barrier((mine, w_parts, w_out))
    weights = pack(w_parts_late, w_out_late)
    weights_far = lax.ppermute(weights, "core", [(0, 1), (1, 0)])
    parts = attend_far(image_counts, gains, far, mine, near_parts)
    parts = lax.all_to_all(parts, ("yl", "core"), 0, 0)
    partial = project(parts, weights, weights_far, x_count)
    shares = lax.all_to_all(partial, "x", 0, 0)
    return leave(rows, factors, shares)


def solution(mesh):
    split = jax.sharding.Mesh(mesh.devices.reshape(16, 2, 2, 4, 2), ("z", "yh", "yl", "x", "core"))
    dp, head = ("z", "yh", "yl"), ("x", "core")
    in_specs = (P(dp, None), P(dp, None), P(None, None, head), P(head, None), P(), P(), P())
    out_specs = (P(dp + head, None), P(dp + head, None))
    return jax.shard_map(
        per_device, mesh=split, in_specs=in_specs, out_specs=out_specs, check_vma=False
    )
```

```python
import math

import jax
import jax.numpy as jnp
from jax import lax
from jax.experimental import pallas as pl
from jax.experimental.pallas import tpu as pltpu
from jax.sharding import PartitionSpec as P

EPS = 1e-06
SAME_IMAGE = 512.0
LANES = 128
HEAD = 64
F32 = jnp.float32
BF16 = jnp.bfloat16
VMEM_LIMIT = 24 * 1024 * 1024
ENTER_LIMIT = 60 * 1024 * 1024
VMEM = pl.BlockSpec(memory_space=pltpu.VMEM)
SMEM = pl.BlockSpec(memory_space=pltpu.SMEM)


def rows_dot(a, b):
    return lax.dot_general(a, b, (((1,), (1,)), ((), ())), preferred_element_type=F32)


def block_index():
    return (lax.axis_index("z") * 2 + lax.axis_index("yh")) * 2 + lax.axis_index("yl")


def image_bounds(counts_ref, first_lane):
    lane = lax.broadcasted_iota(jnp.int32, (1, LANES), 1)
    starts = jnp.zeros((1, LANES), jnp.int32)
    ends = jnp.zeros((1, LANES), jnp.int32)
    total = jnp.int32(0)
    for image in range(counts_ref.shape[0]):
        here = lane == first_lane + image
        starts = jnp.where(here, total, starts)
        total = total + counts_ref[image]
        ends = jnp.where(here, total, ends)
    return starts, ends


def modulation_rows(counts_ref, modulation_ref, first, rows):
    starts, ends = image_bounds(counts_ref, 0)
    place = first + lax.broadcasted_iota(jnp.int32, (rows, LANES), 0)
    member = ((place >= starts) & (place < ends)).astype(F32).astype(BF16)
    member = member[:, : modulation_ref.shape[1]]
    return [
        jnp.dot(member, modulation_ref[part], preferred_element_type=F32) for part in range(3)
    ]


def layer_norm(values):
    average = jnp.mean(values, axis=-1, keepdims=True)
    centred = values - average
    inv_std = lax.rsqrt(jnp.mean(centred * centred, axis=-1, keepdims=True) + EPS)
    return centred * inv_std, inv_std


def w_out_of(weights_ref):
    tiles = weights_ref.shape[1] // LANES
    return jnp.concatenate(
        [weights_ref[3, tile * LANES : (tile + 1) * LANES, :] for tile in range(tiles)], axis=1
    )


def head_sums(values):
    lanes = (LANES, LANES)
    first = lax.broadcasted_iota(jnp.int32, lanes, 0) < HEAD
    second = lax.broadcasted_iota(jnp.int32, lanes, 1) < HEAD
    ones = (first == second).astype(F32).astype(BF16)
    large = values.astype(BF16)
    small = (values - large.astype(F32)).astype(BF16)
    large = jnp.dot(large, ones, preferred_element_type=F32)
    return large + jnp.dot(small, ones, preferred_element_type=F32)


def head_scale(raw):
    return lax.rsqrt(head_sums(raw * raw) * (1.0 / HEAD) + EPS)


def enter_kernel(
    counts_ref,
    gains_ref,
    tokens_ref,
    cotangent_ref,
    w_qkv_ref,
    w_out_ref,
    modulation_ref,
    out_ref,
    raw_ref,
    raw_far_ref,
    rows_ref,
):
    rows = tokens_ref.shape[0]
    first = block_index() * rows
    shift, scale, gate = modulation_rows(counts_ref, modulation_ref, first, rows)
    normed, _ = layer_norm(tokens_ref[...].astype(F32))
    hidden = (normed * (1.0 + scale) + shift).astype(BF16)
    weights = jnp.concatenate([w_qkv_ref[part] for part in range(3)], axis=1)
    qkv = jnp.dot(hidden, weights, preferred_element_type=F32)
    q, k, v = (qkv[:, part * LANES : (part + 1) * LANES] for part in range(3))
    d_mixed = (cotangent_ref[...].astype(F32) * gate).astype(BF16)
    d_attn = rows_dot(d_mixed, w_out_ref[...])
    rows_ref[0] = q.astype(BF16)
    rows_ref[1] = k.astype(BF16)
    q = rows_ref[0].astype(F32)
    k = rows_ref[1].astype(F32)
    q = q * head_scale(q) * (gains_ref[0:1, :] * (1.0 / math.sqrt(HEAD)))
    k = k * head_scale(k) * gains_ref[1:2, :]
    core = lax.axis_index("core")
    share = raw_ref.shape[1] // 4
    for ref, side in ((raw_ref, core), (raw_far_ref, 1 - core)):
        for part in range(4):
            begin = pl.multiple_of((2 * part + side) * share, share)
            for array in range(2):
                ref[array, part * share : (part + 1) * share, :] = rows_ref[
                    array, pl.ds(begin, share), :
                ]
    low = low_lanes()

    def beside(left, right):
        return jnp.where(low, left, right).astype(BF16)

    q_v = (beside(q, pltpu.roll(v, HEAD, 1)), beside(pltpu.roll(q, HEAD, 1), v))
    k_d = (beside(k, pltpu.roll(d_attn, HEAD, 1)), beside(pltpu.roll(k, HEAD, 1), d_attn))
    for place in range(out_ref.shape[0]):
        out_ref[place, :, 0:LANES] = q_v[place % 2]
        out_ref[place, :, LANES:] = k_d[place % 2]


def enter(counts, gains, tokens, cotangent, w_parts, w_out, modulation, quad):
    rows = tokens.shape[0]
    raw = jax.ShapeDtypeStruct((2, rows // 2, LANES), BF16)
    return pl.pallas_call(
        enter_kernel,
        out_shape=(jax.ShapeDtypeStruct((quad, rows, 2 * LANES), BF16), raw, raw),
        in_specs=[SMEM] + [VMEM] * 6,
        out_specs=(VMEM,) * 3,
        scratch_shapes=[pltpu.VMEM((2, rows, LANES), BF16)],
        compiler_params=pltpu.CompilerParams(vmem_limit_bytes=ENTER_LIMIT),
    )(counts, gains, tokens, cotangent, w_parts, w_out, modulation)


def pack_kernel(w_qkv_ref, w_out_ref, raw_ref, weights_ref, sems):
    width = w_out_ref.shape[1]
    rows = raw_ref.shape[1]
    pairs = []
    for part in range(3):
        pairs.append((w_qkv_ref.at[part], weights_ref.at[part * width : (part + 1) * width, :]))
    for tile in range(width // LANES):
        at = slice(tile * LANES, (tile + 1) * LANES)
        to = slice(3 * width + tile * LANES, 3 * width + (tile + 1) * LANES)
        pairs.append((w_out_ref.at[:, at], weights_ref.at[to, :]))
    for array in range(2):
        to = slice(4 * width + array * rows, 4 * width + (array + 1) * rows)
        pairs.append((raw_ref.at[array], weights_ref.at[to, :]))
    copies = [
        pltpu.make_async_copy(source, target, sems.at[place])
        for place, (source, target) in enumerate(pairs)
    ]
    for copy in copies:
        copy.start()
    for copy in copies:
        copy.wait()


def pack(w_parts, w_out, raw):
    width = w_out.shape[1]
    whole = pl.BlockSpec(memory_space=pl.ANY)
    return pl.pallas_call(
        pack_kernel,
        out_shape=jax.ShapeDtypeStruct((4 * width + 2 * raw.shape[1], LANES), BF16),
        in_specs=[whole] * 3,
        out_specs=VMEM,
        scratch_shapes=[pltpu.SemaphoreType.DMA((5 + width // LANES,))],
        compiler_params=pltpu.CompilerParams(vmem_limit_bytes=8 * 1024 * 1024),
    )(w_parts, w_out, raw)


def w_out_of(weights_ref, width):
    return jnp.concatenate(
        [
            weights_ref[3 * width + tile * LANES : 3 * width + (tile + 1) * LANES, :]
            for tile in range(width // LANES)
        ],
        axis=1,
    )


LOG2_E = math.log2(math.e)
INV_ROOT = 1.0 / math.sqrt(HEAD)
CHUNK = 256
TILE = 64
MAIN = 6
REACH_CHUNKS = 4


def low_lanes():
    return lax.broadcasted_iota(jnp.int32, (1, LANES), 1) < HEAD


def place_block(source, place, starts, ends, stores):
    low = low_lanes()
    rows = source.shape[0]
    at = place + lax.broadcasted_iota(jnp.int32, (rows, LANES), 0)
    same = ((at >= starts) & (at < ends)).astype(F32)
    first = source[:, 0:LANES].astype(F32)
    second = source[:, LANES:].astype(F32)
    q_store, k_store, v_store, d_store, kv_store = stores
    q_store[...] = jnp.where(low, first, same * SAME_IMAGE).astype(BF16)
    k_store[...] = jnp.where(low, second, same).astype(BF16)
    v_store[...] = jnp.where(low, 0.0, first).astype(BF16)
    d_store[...] = source[:, LANES:]
    kv_store[...] = jnp.where(low, second, first).astype(BF16).T


def window_facts(counts_ref):
    half = lax.axis_index("yh")
    origin = (block_index() // 4 - 1) * 2 * CHUNK
    own_at = (2 + half) * CHUNK
    starts, ends = image_bounds(counts_ref, HEAD)
    left_from = jnp.int32(-CHUNK)
    right_to = jnp.int32((MAIN + 1) * CHUNK)
    total = -origin
    for image in range(counts_ref.shape[0]):
        left_from = jnp.where(total <= own_at, total, left_from)
        ended = total >= own_at + CHUNK
        total = total + counts_ref[image]
        right_to = jnp.where((total >= own_at + CHUNK) & jnp.logical_not(ended), total, right_to)
    return half, own_at, starts - origin, ends - origin, left_from, right_to


def by_eight(values):
    return values.reshape(values.shape[0] // 8, 8, values.shape[1])


def add_tiles(s_ref, g_ref, rows, highest, total, grads):
    for piece in range(rows // TILE):
        at = slice(piece * TILE, (piece + 1) * TILE)
        weights = jnp.exp2(s_ref[at, :] * LOG2_E - highest)
        total = total + jnp.sum(by_eight(weights), axis=0)
        grads = grads + jnp.sum(by_eight(weights * g_ref[at, :]), axis=0)
    return total, grads


def rows_max(values):
    return jnp.max(by_eight(values), axis=0)


def near_kernel(
    counts_ref,
    first_ref,
    quad_ref,
    second_ref,
    qx_ref,
    kx_ref,
    vx_ref,
    dx_ref,
    kv_ref,
    so_ref,
    go_ref,
    sn_ref,
    gn_ref,
    stats_ref,
    s_ref,
    g_ref,
):
    half, own_at, starts, ends, left_from, right_to = window_facts(counts_ref)
    block_rows = CHUNK // 2

    def place(source, begin):
        begin = pl.multiple_of(begin, block_rows)
        at = pl.ds(begin, block_rows)
        stores = [ref.at[at, :] for ref in (qx_ref, kx_ref, vx_ref, dx_ref)]
        place_block(source, begin, starts, ends, stores + [kv_ref.at[:, at]])

    to_first = jnp.where(lax.rem(lax.axis_index("z"), 2) == 0, 2 * CHUNK, -2 * CHUNK)
    for block in range(4):
        at = slice(block * block_rows, (block + 1) * block_rows)
        begin = 2 * CHUNK + block * block_rows
        place(quad_ref.at[at], begin)
        place(first_ref.at[at], begin + to_first)
        place(second_ref.at[at], begin - to_first)

    own_rows = pl.ds(pl.multiple_of(own_at, CHUNK), CHUNK)
    q_own = qx_ref[own_rows, :]
    d_own = dx_ref[own_rows, :]
    highest = jnp.full((8, CHUNK), -jnp.inf, F32)
    for piece in range(MAIN):
        at = slice(piece * CHUNK, (piece + 1) * CHUNK)
        scores = rows_dot(kx_ref[at, :], q_own)
        so_ref[at, :] = scores
        highest = jnp.maximum(highest, rows_max(scores))
        go_ref[at, :] = rows_dot(vx_ref[at, :], d_own)
    highest = jnp.max(highest, axis=0, keepdims=True) * LOG2_E
    total = jnp.zeros((8, CHUNK), F32)
    grads = jnp.zeros((8, CHUNK), F32)
    for piece in range(MAIN * CHUNK // TILE):
        at = slice(piece * TILE, (piece + 1) * TILE)
        weights = jnp.exp2(so_ref[at, :] * LOG2_E - highest)
        so_ref[at, :] = weights
        total = total + jnp.sum(by_eight(weights), axis=0)
        grads = grads + jnp.sum(by_eight(weights * go_ref[at, :]), axis=0)
    stats_ref[MAIN, 0:1, :] = highest
    stats_ref[MAIN, 1:2, :] = jnp.sum(total, axis=0, keepdims=True)
    stats_ref[MAIN, 2:3, :] = jnp.sum(grads, axis=0, keepdims=True)

    left_key = jnp.clip((left_from + CHUNK) // CHUNK - 1, 0, MAIN - REACH_CHUNKS)
    right_key = jnp.clip((right_to - 1) // CHUNK - (REACH_CHUNKS - 1), 0, MAIN - REACH_CHUNKS)

    def one_chunk(step, carry):
        slot = step + jnp.where(step >= 2 + half, 1, 0)
        begin = slot * CHUNK

        @pl.when((begin < right_to) & (begin + CHUNK > left_from))
        def _():
            at = pl.ds(pl.multiple_of(begin, CHUNK), CHUNK)
            key = jnp.where(begin < own_at, left_key, right_key) * CHUNK
            q_block = qx_ref[at, :]
            d_block = dx_ref[at, :]
            highest = jnp.full((8, CHUNK), -jnp.inf, F32)
            for piece in range(REACH_CHUNKS):
                keys_at = pl.ds(pl.multiple_of(key + piece * CHUNK, CHUNK), CHUNK)
                here = slice(piece * CHUNK, (piece + 1) * CHUNK)
                scores = rows_dot(kx_ref[keys_at, :], q_block)
                s_ref[here, :] = scores
                highest = jnp.maximum(highest, rows_max(scores))
                g_ref[here, :] = rows_dot(vx_ref[keys_at, :], d_block)
            highest = jnp.max(highest, axis=0, keepdims=True) * LOG2_E
            zeros = jnp.zeros((8, CHUNK), F32)
            total, grads = add_tiles(s_ref, g_ref, REACH_CHUNKS * CHUNK, highest, zeros, zeros)
            stats_ref[slot, 0:1, :] = highest
            stats_ref[slot, 1:2, :] = jnp.sum(total, axis=0, keepdims=True)
            stats_ref[slot, 2:3, :] = jnp.sum(grads, axis=0, keepdims=True)
            near_at = pl.ds(pl.multiple_of(own_at - key, CHUNK), CHUNK)
            sn_ref[slot, :, :] = s_ref[near_at, :]
            gn_ref[slot, :, :] = g_ref[near_at, :]

        return carry

    lax.fori_loop(0, MAIN - 1, one_chunk, 0)


def attend_near(counts, first, quad, second):
    rows = MAIN * CHUNK
    head_rows = jax.ShapeDtypeStruct((rows, LANES), BF16)
    scores = jax.ShapeDtypeStruct((rows, CHUNK), F32)
    tiles = jax.ShapeDtypeStruct((MAIN, CHUNK, CHUNK), F32)
    return pl.pallas_call(
        near_kernel,
        out_shape=(head_rows,) * 4
        + (jax.ShapeDtypeStruct((LANES, rows), BF16),)
        + (scores, scores, tiles, tiles, jax.ShapeDtypeStruct((MAIN + 1, 8, CHUNK), F32)),
        in_specs=[SMEM] + [VMEM] * 3,
        out_specs=(VMEM,) * 10,
        scratch_shapes=[pltpu.VMEM((REACH_CHUNKS * CHUNK, CHUNK), F32)] * 2,
        cost_estimate=pl.CostEstimate(
            flops=7000000000, bytes_accessed=1 << 20, transcendentals=1 << 20
        ),
        compiler_params=pltpu.CompilerParams(vmem_limit_bytes=VMEM_LIMIT),
    )(counts, first, quad, second)


def far_kernel(
    counts_ref,
    far_ref,
    qx_ref,
    kx_ref,
    vx_ref,
    dx_ref,
    kv_ref,
    so_ref,
    go_ref,
    sn_ref,
    gn_ref,
    stats_ref,
    out_ref,
    qf_ref,
    kf_ref,
    vf_ref,
    df_ref,
    kvf_ref,
    s_ref,
    g_ref,
    p_ref,
    d_ref,
    pn_ref,
    dn_ref,
    sums_ref,
    dk_ref,
    dv_ref,
    done_ref,
):
    half, own_at, starts, ends, left_from, right_to = window_facts(counts_ref)
    block_rows = CHUNK // 2
    rows = MAIN * CHUNK
    far_at = jnp.where(half == 0, -CHUNK, rows)
    for block in range(2):
        at = slice(block * block_rows, (block + 1) * block_rows)
        stores = [ref.at[at, :] for ref in (qf_ref, kf_ref, vf_ref, df_ref)]
        place_block(
            far_ref.at[at],
            far_at + block * block_rows,
            starts,
            ends,
            stores + [kvf_ref.at[:, at]],
        )

    own_rows = pl.ds(pl.multiple_of(own_at, CHUNK), CHUNK)
    q_own = qx_ref[own_rows, :]
    d_own = dx_ref[own_rows, :]
    scores = rows_dot(kf_ref[...], q_own)
    s_ref[0:CHUNK, :] = scores
    g_ref[0:CHUNK, :] = rows_dot(vf_ref[...], d_own)
    near_highest = stats_ref[MAIN, 0:1, :]
    highest = jnp.max(rows_max(scores), axis=0, keepdims=True) * LOG2_E
    highest = jnp.maximum(near_highest, highest)
    shrink = jnp.exp2(near_highest - highest)
    zeros = jnp.zeros((8, CHUNK), F32)
    total, grads = add_tiles(s_ref, g_ref, CHUNK, highest, zeros, zeros)
    total = jnp.sum(total, axis=0, keepdims=True) + stats_ref[MAIN, 1:2, :] * shrink
    grads = jnp.sum(grads, axis=0, keepdims=True) + stats_ref[MAIN, 2:3, :] * shrink
    scale = 1.0 / total
    mean_grad = grads * scale

    near_scale = shrink * scale
    for piece in range(rows // TILE):
        at = slice(piece * TILE, (piece + 1) * TILE)
        probs = so_ref[at, :] * near_scale
        p_ref[at, :] = probs.astype(BF16)
        d_ref[at, :] = (probs * (go_ref[at, :] - mean_grad)).astype(BF16)
    for piece in range(CHUNK // TILE):
        at = slice(piece * TILE, (piece + 1) * TILE)
        to = slice(rows + piece * TILE, rows + (piece + 1) * TILE)
        probs = jnp.exp2(s_ref[at, :] * LOG2_E - highest) * scale
        p_ref[to, :] = probs.astype(BF16)
        d_ref[to, :] = (probs * (g_ref[at, :] - mean_grad)).astype(BF16)
    pn_ref[:, own_rows] = p_ref[own_rows, :]
    dn_ref[:, own_rows] = d_ref[own_rows, :]

    def times_window(values_ref):
        main = jnp.dot(kv_ref[...], values_ref[0:rows, :], preferred_element_type=F32)
        return main + jnp.dot(
            kvf_ref[...], values_ref[rows : rows + CHUNK, :], preferred_element_type=F32
        )

    upper = lax.broadcasted_iota(jnp.int32, (LANES, CHUNK), 0) < HEAD
    own_out = jnp.where(upper, times_window(d_ref) * INV_ROOT, times_window(p_ref)).T

    query_lane = lax.broadcasted_iota(jnp.int32, (1, CHUNK), 1)
    reaches_far = jnp.where(half == 0, left_from < 0, right_to > rows)
    sums_ref[...] = stats_ref[...]
    dk_ref[...] = jnp.zeros_like(dk_ref)
    dv_ref[...] = jnp.zeros_like(dv_ref)

    @pl.when(reaches_far)
    def _():
        for step in range(2):
            slot = half * (MAIN - 2) + step
            begin = slot * CHUNK

            @pl.when((begin < right_to) & (begin + CHUNK > left_from))
            def _():
                at = pl.ds(pl.multiple_of(begin, CHUNK), CHUNK)
                scores = rows_dot(kf_ref[...], qx_ref[at, :])
                s_ref[0:CHUNK, :] = scores
                g_ref[0:CHUNK, :] = rows_dot(vf_ref[...], dx_ref[at, :])
                before = sums_ref[slot, 0:1, :]
                highest = jnp.max(rows_max(scores), axis=0, keepdims=True) * LOG2_E
                highest = jnp.maximum(before, highest)
                total, grads = add_tiles(s_ref, g_ref, CHUNK, highest, zeros, zeros)
                shrink = jnp.exp2(before - highest)
                total = jnp.sum(total, axis=0, keepdims=True)
                grads = jnp.sum(grads, axis=0, keepdims=True)
                sums_ref[slot, 0:1, :] = highest
                sums_ref[slot, 1:2, :] = sums_ref[slot, 1:2, :] * shrink + total
                sums_ref[slot, 2:3, :] = sums_ref[slot, 2:3, :] * shrink + grads

        q_block = qf_ref[...]
        d_block = df_ref[...]
        key = half * (MAIN // 2) * CHUNK
        highest = jnp.full((8, CHUNK), -jnp.inf, F32)
        for piece in range(REACH_CHUNKS):
            here = slice(piece * CHUNK, (piece + 1) * CHUNK)
            if piece < REACH_CHUNKS - 1:
                keys_at = pl.ds(pl.multiple_of(key + piece * CHUNK, CHUNK), CHUNK)
                keys, values = kx_ref[keys_at, :], vx_ref[keys_at, :]
            else:
                keys, values = kf_ref[...], vf_ref[...]
            scores = rows_dot(keys, q_block)
            s_ref[here, :] = scores
            highest = jnp.maximum(highest, rows_max(scores))
            g_ref[here, :] = rows_dot(values, d_block)
        highest = jnp.max(highest, axis=0, keepdims=True) * LOG2_E
        total, grads = add_tiles(s_ref, g_ref, REACH_CHUNKS * CHUNK, highest, zeros, zeros)
        total = jnp.sum(total, axis=0, keepdims=True)
        place = query_lane + far_at
        scale = jnp.where((place >= left_from) & (place < right_to), 1.0 / total, 0.0)
        mean_grad = jnp.sum(grads, axis=0, keepdims=True) * scale
        for piece in range(CHUNK // TILE):
            at = slice(piece * TILE, (piece + 1) * TILE)
            near_at = pl.ds(pl.multiple_of(own_at - key + piece * TILE, TILE), TILE)
            probs = jnp.exp2(s_ref[near_at, :] * LOG2_E - highest) * scale
            p_ref[at, :] = probs.astype(BF16)
            d_ref[at, :] = (probs * (g_ref[near_at, :] - mean_grad)).astype(BF16)
        dk_ref[...] = jnp.dot(d_ref[0:CHUNK, :], q_block, preferred_element_type=F32)
        dv_ref[...] = jnp.dot(p_ref[0:CHUNK, :], d_block, preferred_element_type=F32)

    for step in range(MAIN - 1):
        slot = step + jnp.where(step >= 2 + half, 1, 0)
        begin = slot * CHUNK
        chunk_at = pl.ds(pl.multiple_of(begin, CHUNK), CHUNK)
        place = query_lane + begin
        valid = (place >= left_from) & (place < right_to)
        highest = sums_ref[slot, 0:1, :]
        scale = 1.0 / sums_ref[slot, 1:2, :]
        mean_grad = sums_ref[slot, 2:3, :] * scale
        for piece in range(CHUNK // TILE):
            at = slice(piece * TILE, (piece + 1) * TILE)
            probs = jnp.exp2(sn_ref[slot, at, :] * LOG2_E - highest) * scale
            d_scores = probs * (gn_ref[slot, at, :] - mean_grad)
            pn_ref[at, chunk_at] = jnp.where(valid, probs, 0.0).astype(BF16)
            dn_ref[at, chunk_at] = jnp.where(valid, d_scores, 0.0).astype(BF16)
    d_key = dk_ref[...] + jnp.dot(dn_ref[...], qx_ref[...], preferred_element_type=F32)
    d_value = dv_ref[...] + jnp.dot(pn_ref[...], dx_ref[...], preferred_element_type=F32)
    done_ref[:, 0:LANES] = own_out.astype(BF16)
    done_ref[:, LANES:] = jnp.where(low_lanes(), d_key, d_value).astype(BF16)
    share = 16
    for member in range(out_ref.shape[0]):
        block, core = member // 2, member % 2
        for part in range(out_ref.shape[1] // share):
            begin = (block * 8 + part * 2 + core) * share
            out_ref[member, part * share : (part + 1) * share, :] = done_ref[
                begin : begin + share, :
            ]


def attend_far(counts, far, near_parts):
    return pl.pallas_call(
        far_kernel,
        out_shape=jax.ShapeDtypeStruct((4, CHUNK // 4, 2 * LANES), BF16),
        in_specs=[SMEM] + [VMEM] * (1 + len(near_parts)),
        out_specs=VMEM,
        scratch_shapes=[pltpu.VMEM((CHUNK, LANES), BF16)] * 4
        + [pltpu.VMEM((LANES, CHUNK), BF16)]
        + [pltpu.VMEM((REACH_CHUNKS * CHUNK, CHUNK), F32)] * 2
        + [pltpu.VMEM(((MAIN + 1) * CHUNK, CHUNK), BF16)] * 2
        + [pltpu.VMEM((CHUNK, MAIN * CHUNK), BF16)] * 2
        + [pltpu.VMEM((MAIN + 1, 8, CHUNK), F32)]
        + [pltpu.VMEM((CHUNK, LANES), F32)] * 2
        + [pltpu.VMEM((CHUNK, 2 * LANES), BF16)],
        cost_estimate=pl.CostEstimate(
            flops=7000000000, bytes_accessed=1 << 20, transcendentals=1 << 20
        ),
        compiler_params=pltpu.CompilerParams(vmem_limit_bytes=VMEM_LIMIT),
    )(counts, far, *near_parts)


def project_kernel(parts_ref, gains_ref, raw_ref, weights_ref, weights_far_ref, out_ref):
    rows = parts_ref.shape[1]
    width = out_ref.shape[2] // 2
    share = out_ref.shape[1]
    core = lax.axis_index("core")
    low = low_lanes()

    def norm_grad(raw, gain, d_norm):
        raw = raw.astype(F32)
        inverse = head_scale(raw)
        scaled = d_norm * gain
        inner = head_sums(raw * scaled) * (1.0 / HEAD)
        return inverse * scaled - raw * (inverse * inverse * inverse * inner)

    def by_column(which, raw):
        head0 = parts_ref[which].astype(F32)
        head1 = parts_ref[2 + which].astype(F32)
        a0, a1 = head0[:, :LANES], head1[:, :LANES]
        b0, b1 = head0[:, LANES:], head1[:, LANES:]
        d_q = norm_grad(raw[0], gains_ref[0:1, :], jnp.where(low, a0, pltpu.roll(a1, HEAD, 1)))
        attn = jnp.where(low, pltpu.roll(a0, HEAD, 1), a1).astype(BF16)
        d_k = norm_grad(raw[1], gains_ref[1:2, :], jnp.where(low, b0, pltpu.roll(b1, HEAD, 1)))
        d_v = jnp.where(low, pltpu.roll(b0, HEAD, 1), b1)
        return attn, [values.astype(BF16) for values in (d_q, d_k, d_v)]

    raw_far = [
        weights_far_ref[4 * width + array * rows : 4 * width + (array + 1) * rows, :]
        for array in range(2)
    ]
    attn, grads = by_column(core, [raw_ref[0], raw_ref[1]])
    attn_far, grads_far = by_column(1 - core, raw_far)
    both = (weights_ref, weights_far_ref)
    mixed = jnp.dot(
        jnp.concatenate([attn, attn_far], axis=1),
        jnp.concatenate([w_out_of(ref, width) for ref in both], axis=0),
        preferred_element_type=F32,
    ).astype(BF16)
    weights = [ref[part * width : (part + 1) * width, :] for ref in both for part in range(3)]
    d_hidden = rows_dot(
        jnp.concatenate(grads + grads_far, axis=1), jnp.concatenate(weights, axis=1)
    ).astype(BF16)
    for place in range(out_ref.shape[0]):
        at = slice(place * share, (place + 1) * share)
        out_ref[place, :, :width] = mixed[at]
        out_ref[place, :, width:] = d_hidden[at]


def project(parts, gains, raw, weights, weights_far, x_count, width):
    return pl.pallas_call(
        project_kernel,
        out_shape=jax.ShapeDtypeStruct((x_count, parts.shape[1] // x_count, 2 * width), BF16),
        in_specs=[VMEM] * 5,
        out_specs=VMEM,
        compiler_params=pltpu.CompilerParams(vmem_limit_bytes=VMEM_LIMIT),
    )(parts, gains, raw, weights, weights_far)


def ready_kernel(
    counts_ref,
    tokens_ref,
    cotangent_ref,
    modulation_ref,
    rows_ref,
    factors_ref,
):
    rows = rows_ref.shape[1]
    first_row = (lax.axis_index("x") * 2 + lax.axis_index("core")) * rows
    first = block_index() * tokens_ref.shape[0] + first_row
    _, scale, gate = modulation_rows(counts_ref, modulation_ref, first, rows)
    at = pl.ds(pl.multiple_of(first_row, rows), rows)
    normed, inv_std = layer_norm(tokens_ref[at, :].astype(F32))
    rows_ref[0] = tokens_ref[at, :]
    rows_ref[1] = cotangent_ref[at, :]
    factors_ref[0] = gate
    factors_ref[1] = 1.0 + scale
    factors_ref[2] = normed
    factors_ref[3] = jnp.broadcast_to(inv_std, normed.shape)


def ready(counts, tokens, cotangent, modulation, share):
    width = tokens.shape[1]
    return pl.pallas_call(
        ready_kernel,
        out_shape=(
            jax.ShapeDtypeStruct((2, share, width), BF16),
            jax.ShapeDtypeStruct((4, share, width), F32),
        ),
        in_specs=[SMEM] + [VMEM] * 3,
        out_specs=(VMEM, VMEM),
        compiler_params=pltpu.CompilerParams(vmem_limit_bytes=VMEM_LIMIT),
    )(counts, tokens, cotangent, modulation)


def leave_kernel(rows_ref, factors_ref, shares_ref, layer_ref, grad_ref):
    width = layer_ref.shape[1]
    sums = shares_ref[0].astype(F32)
    for share in range(1, shares_ref.shape[0]):
        sums = sums + shares_ref[share].astype(F32)
    layer = rows_ref[0].astype(F32) + factors_ref[0] * sums[:, :width]
    layer_ref[...] = layer.astype(BF16)
    d_normed = sums[:, width:] * factors_ref[1]
    normed = factors_ref[2]
    input_grad = rows_ref[1].astype(F32) + factors_ref[3] * (
        d_normed
        - jnp.mean(d_normed, axis=-1, keepdims=True)
        - normed * jnp.mean(d_normed * normed, axis=-1, keepdims=True)
    )
    grad_ref[...] = input_grad.astype(BF16)


def leave(rows, factors, shares):
    out = jax.ShapeDtypeStruct(rows.shape[1:], BF16)
    return pl.pallas_call(
        leave_kernel,
        out_shape=(out, out),
        in_specs=[VMEM] * 3,
        out_specs=(VMEM, VMEM),
        compiler_params=pltpu.CompilerParams(vmem_limit_bytes=VMEM_LIMIT),
    )(rows, factors, shares)


def per_device(tokens, cotangent, w_qkv, w_out, qk_gain, modulation, image_counts):
    tok_rows, model_width = tokens.shape
    z_count = lax.axis_size("z")
    x_count = lax.axis_size("x")
    quad = 4
    pair_rows = 2 * tok_rows
    share = tok_rows // (2 * x_count)
    w_parts = w_qkv.transpose(1, 0, 2)
    mod_parts = modulation.transpose(1, 0, 2)
    gains = jnp.pad(jnp.concatenate([qk_gain, qk_gain], axis=1), ((0, 6), (0, 0)))

    heads, raw, raw_far = enter(
        image_counts, gains, tokens, cotangent, w_parts, w_out, mod_parts, quad
    )
    mine = lax.all_to_all(heads, ("yh", "yl"), 0, 0)
    mine = mine.reshape(quad * tok_rows, 2 * LANES)
    evens = range(0, z_count, 2)
    swaps = [(i, i + 1) for i in evens], [((i - 1) % z_count, i) for i in evens]
    first, second = (
        lax.ppermute(mine, "z", pairs + [(j, i) for i, j in pairs]) for pairs in swaps
    )
    halves = 4 * z_count
    far_half = jnp.where(
        lax.axis_index("yh") == lax.axis_index("core"), mine[pair_rows:], mine[:pair_rows]
    )

    def far_source(target):
        z, yh, core = target // 4, target // 2 % 2, target % 2
        return (z + (2 if yh else -2)) % z_count * 4 + (yh ^ core) * 2 + core

    far = lax.ppermute(
        far_half, ("z", "yh", "core"), [(far_source(i), i) for i in range(halves)]
    )
    _, tokens_late, cotangent_late, mod_late = lax.optimization_barrier(
        (mine, tokens, cotangent, mod_parts)
    )
    rows, factors = ready(image_counts, tokens_late, cotangent_late, mod_late, share)
    near_parts = attend_near(image_counts, first, mine, second)
    _, w_parts_late, w_out_late = lax.optimization_barrier((mine, w_parts, w_out))
    weights = pack(w_parts_late, w_out_late, raw_far)
    weights_far = lax.ppermute(weights, "core", [(0, 1), (1, 0)])
    parts = attend_far(image_counts, far, near_parts)
    parts = lax.all_to_all(parts, ("yl", "core"), 0, 0)
    partial = project(parts, gains, raw, weights, weights_far, x_count, model_width)
    shares = lax.all_to_all(partial, "x", 0, 0)
    return leave(rows, factors, shares)


def solution(mesh):
    split = jax.sharding.Mesh(mesh.devices.reshape(16, 2, 2, 4, 2), ("z", "yh", "yl", "x", "core"))
    dp, head = ("z", "yh", "yl"), ("x", "core")
    in_specs = (P(dp, None), P(dp, None), P(None, None, head), P(head, None), P(), P(), P())
    out_specs = (P(dp + head, None), P(dp + head, None))
    return jax.shard_map(
        per_device, mesh=split, in_specs=in_specs, out_specs=out_specs, check_vma=False
    )
```

```python
import math

import jax
import jax.numpy as jnp
from jax import lax
from jax.experimental import pallas as pl
from jax.experimental.pallas import tpu as pltpu
from jax.sharding import PartitionSpec as P

EPS = 1e-06
SAME_IMAGE = 512.0
LANES = 128
HEAD = 64
F32 = jnp.float32
BF16 = jnp.bfloat16
VMEM_LIMIT = 24 * 1024 * 1024
ENTER_LIMIT = 60 * 1024 * 1024
VMEM = pl.BlockSpec(memory_space=pltpu.VMEM)
SMEM = pl.BlockSpec(memory_space=pltpu.SMEM)


def rows_dot(a, b):
    return lax.dot_general(a, b, (((1,), (1,)), ((), ())), preferred_element_type=F32)


def block_index():
    return (lax.axis_index("z") * 2 + lax.axis_index("yh")) * 2 + lax.axis_index("yl")


def image_bounds(counts_ref, first_lane):
    lane = lax.broadcasted_iota(jnp.int32, (1, LANES), 1)
    starts = jnp.zeros((1, LANES), jnp.int32)
    ends = jnp.zeros((1, LANES), jnp.int32)
    total = jnp.int32(0)
    for image in range(counts_ref.shape[0]):
        here = lane == first_lane + image
        starts = jnp.where(here, total, starts)
        total = total + counts_ref[image]
        ends = jnp.where(here, total, ends)
    return starts, ends


def modulation_rows(counts_ref, modulation_ref, first, rows):
    starts, ends = image_bounds(counts_ref, 0)
    place = first + lax.broadcasted_iota(jnp.int32, (rows, LANES), 0)
    member = ((place >= starts) & (place < ends)).astype(F32).astype(BF16)
    member = member[:, : modulation_ref.shape[1]]
    return [
        jnp.dot(member, modulation_ref[part], preferred_element_type=F32) for part in range(3)
    ]


def layer_norm(values):
    average = jnp.mean(values, axis=-1, keepdims=True)
    centred = values - average
    inv_std = lax.rsqrt(jnp.mean(centred * centred, axis=-1, keepdims=True) + EPS)
    return centred * inv_std, inv_std


def w_out_of(weights_ref):
    tiles = weights_ref.shape[1] // LANES
    return jnp.concatenate(
        [weights_ref[3, tile * LANES : (tile + 1) * LANES, :] for tile in range(tiles)], axis=1
    )


def head_sums(values):
    lanes = (LANES, LANES)
    first = lax.broadcasted_iota(jnp.int32, lanes, 0) < HEAD
    second = lax.broadcasted_iota(jnp.int32, lanes, 1) < HEAD
    ones = (first == second).astype(F32).astype(BF16)
    large = values.astype(BF16)
    small = (values - large.astype(F32)).astype(BF16)
    large = jnp.dot(large, ones, preferred_element_type=F32)
    return large + jnp.dot(small, ones, preferred_element_type=F32)


def both_heads(gains_ref, which):
    gain = gains_ref[which : which + 1, :]
    return jnp.concatenate([gain, gain], axis=1)


def head_scale(raw):
    return lax.rsqrt(head_sums(raw * raw) * (1.0 / HEAD) + EPS)


def enter_kernel(
    counts_ref,
    gains_ref,
    tokens_ref,
    cotangent_ref,
    w_qkv_ref,
    w_out_ref,
    modulation_ref,
    out_ref,
    raw_ref,
    raw_far_ref,
    rows_ref,
):
    rows = tokens_ref.shape[0]
    first = block_index() * rows
    shift, scale, gate = modulation_rows(counts_ref, modulation_ref, first, rows)
    normed, _ = layer_norm(tokens_ref[...].astype(F32))
    hidden = (normed * (1.0 + scale) + shift).astype(BF16)
    weights = jnp.concatenate([w_qkv_ref[part] for part in range(3)], axis=1)
    qkv = jnp.dot(hidden, weights, preferred_element_type=F32)
    q, k, v = (qkv[:, part * LANES : (part + 1) * LANES] for part in range(3))
    d_mixed = (cotangent_ref[...].astype(F32) * gate).astype(BF16)
    d_attn = rows_dot(d_mixed, w_out_ref[...])
    rows_ref[0] = q.astype(BF16)
    rows_ref[1] = k.astype(BF16)
    q = rows_ref[0].astype(F32)
    k = rows_ref[1].astype(F32)
    q = q * head_scale(q) * (both_heads(gains_ref, 0) * (1.0 / math.sqrt(HEAD)))
    k = k * head_scale(k) * both_heads(gains_ref, 1)
    core = lax.axis_index("core")
    share = raw_ref.shape[1] // 4
    for ref, side in ((raw_ref, core), (raw_far_ref, 1 - core)):
        for part in range(4):
            begin = pl.multiple_of((2 * part + side) * share, share)
            for array in range(2):
                ref[array, part * share : (part + 1) * share, :] = rows_ref[
                    array, pl.ds(begin, share), :
                ]
    low = low_lanes()

    def beside(left, right):
        return jnp.where(low, left, right).astype(BF16)

    q_v = (beside(q, pltpu.roll(v, HEAD, 1)), beside(pltpu.roll(q, HEAD, 1), v))
    k_d = (beside(k, pltpu.roll(d_attn, HEAD, 1)), beside(pltpu.roll(k, HEAD, 1), d_attn))
    for place in range(out_ref.shape[0]):
        out_ref[place, :, 0:LANES] = q_v[place % 2]
        out_ref[place, :, LANES:] = k_d[place % 2]


def enter(counts, gains, tokens, cotangent, w_parts, w_out, modulation, quad):
    rows = tokens.shape[0]
    raw = jax.ShapeDtypeStruct((2, rows // 2, LANES), BF16)
    return pl.pallas_call(
        enter_kernel,
        out_shape=(jax.ShapeDtypeStruct((quad, rows, 2 * LANES), BF16), raw, raw),
        in_specs=[SMEM] + [VMEM] * 6,
        out_specs=(VMEM,) * 3,
        scratch_shapes=[pltpu.VMEM((2, rows, LANES), BF16)],
        compiler_params=pltpu.CompilerParams(vmem_limit_bytes=ENTER_LIMIT),
    )(counts, gains, tokens, cotangent, w_parts, w_out, modulation)


def pack_kernel(w_qkv_ref, w_out_ref, raw_ref, weights_ref, sems):
    width = w_out_ref.shape[1]
    rows = raw_ref.shape[1]
    pairs = []
    for part in range(3):
        pairs.append((w_qkv_ref.at[part], weights_ref.at[part * width : (part + 1) * width, :]))
    for tile in range(width // LANES):
        at = slice(tile * LANES, (tile + 1) * LANES)
        to = slice(3 * width + tile * LANES, 3 * width + (tile + 1) * LANES)
        pairs.append((w_out_ref.at[:, at], weights_ref.at[to, :]))
    for array in range(2):
        to = slice(4 * width + array * rows, 4 * width + (array + 1) * rows)
        pairs.append((raw_ref.at[array], weights_ref.at[to, :]))
    copies = [
        pltpu.make_async_copy(source, target, sems.at[place])
        for place, (source, target) in enumerate(pairs)
    ]
    for copy in copies:
        copy.start()
    for copy in copies:
        copy.wait()


def w_out_of(weights_ref):
    tiles = weights_ref.shape[1] // LANES
    return jnp.concatenate(
        [weights_ref[3, tile * LANES : (tile + 1) * LANES, :] for tile in range(tiles)], axis=1
    )


def head_sums(values):
    lanes = (LANES, LANES)
    first = lax.broadcasted_iota(jnp.int32, lanes, 0) < HEAD
    second = lax.broadcasted_iota(jnp.int32, lanes, 1) < HEAD
    ones = (first == second).astype(F32).astype(BF16)
    large = values.astype(BF16)
    small = (values - large.astype(F32)).astype(BF16)
    large = jnp.dot(large, ones, preferred_element_type=F32)
    return large + jnp.dot(small, ones, preferred_element_type=F32)


def both_heads(gains_ref, which):
    gain = gains_ref[which : which + 1, :]
    return jnp.concatenate([gain, gain], axis=1)


def head_scale(raw):
    return lax.rsqrt(head_sums(raw * raw) * (1.0 / HEAD) + EPS)


def enter_kernel(
    counts_ref,
    gains_ref,
    tokens_ref,
    cotangent_ref,
    w_qkv_ref,
    w_out_ref,
    modulation_ref,
    out_ref,
    raw_ref,
    raw_far_ref,
    rows_ref,
):
    rows = tokens_ref.shape[0]
    first = block_index() * rows
    shift, scale, gate = modulation_rows(counts_ref, modulation_ref, first, rows)
    normed, _ = layer_norm(tokens_ref[...].astype(F32))
    hidden = (normed * (1.0 + scale) + shift).astype(BF16)
    weights = jnp.concatenate([w_qkv_ref[part] for part in range(3)], axis=1)
    qkv = jnp.dot(hidden, weights, preferred_element_type=F32)
    q, k, v = (qkv[:, part * LANES : (part + 1) * LANES] for part in range(3))
    d_mixed = (cotangent_ref[...].astype(F32) * gate).astype(BF16)
    d_attn = rows_dot(d_mixed, w_out_ref[...])
    rows_ref[0] = q.astype(BF16)
    rows_ref[1] = k.astype(BF16)
    q = rows_ref[0].astype(F32)
    k = rows_ref[1].astype(F32)
    q = q * head_scale(q) * (both_heads(gains_ref, 0) * (1.0 / math.sqrt(HEAD)))
    k = k * head_scale(k) * both_heads(gains_ref, 1)
    core = lax.axis_index("core")
    share = raw_ref.shape[1] // 4
    for ref, side in ((raw_ref, core), (raw_far_ref, 1 - core)):
        for part in range(4):
            begin = pl.multiple_of((2 * part + side) * share, share)
            for array in range(2):
                ref[array, part * share : (part + 1) * share, :] = rows_ref[
                    array, pl.ds(begin, share), :
                ]
    low = low_lanes()

    def beside(left, right):
        return jnp.where(low, left, right).astype(BF16)

    q_v = (beside(q, pltpu.roll(v, HEAD, 1)), beside(pltpu.roll(q, HEAD, 1), v))
    k_d = (beside(k, pltpu.roll(d_attn, HEAD, 1)), beside(pltpu.roll(k, HEAD, 1), d_attn))
    for place in range(out_ref.shape[0]):
        out_ref[place, :, 0:LANES] = q_v[place % 2]
        out_ref[place, :, LANES:] = k_d[place % 2]


def enter(counts, gains, tokens, cotangent, w_parts, w_out, modulation, quad):
    rows = tokens.shape[0]
    raw = jax.ShapeDtypeStruct((2, rows // 2, LANES), BF16)
    return pl.pallas_call(
        enter_kernel,
        out_shape=(jax.ShapeDtypeStruct((quad, rows, 2 * LANES), BF16), raw, raw),
        in_specs=[SMEM] + [VMEM] * 6,
        out_specs=(VMEM,) * 3,
        scratch_shapes=[pltpu.VMEM((2, rows, LANES), BF16)],
        compiler_params=pltpu.CompilerParams(vmem_limit_bytes=ENTER_LIMIT),
    )(counts, gains, tokens, cotangent, w_parts, w_out, modulation)


def pack_kernel(w_qkv_ref, w_out_ref, raw_ref, weights_ref, sems):
    width = w_out_ref.shape[1]
    rows = raw_ref.shape[1]
    pairs = []
    for part in range(3):
        pairs.append((w_qkv_ref.at[part], weights_ref.at[part * width : (part + 1) * width, :]))
    for tile in range(width // LANES):
        at = slice(tile * LANES, (tile + 1) * LANES)
        to = slice(3 * width + tile * LANES, 3 * width + (tile + 1) * LANES)
        pairs.append((w_out_ref.at[:, at], weights_ref.at[to, :]))
    for array in range(2):
        to = slice(4 * width + array * rows, 4 * width + (array + 1) * rows)
        pairs.append((raw_ref.at[array], weights_ref.at[to, :]))
    copies = [
        pltpu.make_async_copy(source, target, sems.at[place])
        for place, (source, target) in enumerate(pairs)
    ]
    for copy in copies:
        copy.start()
    for copy in copies:
        copy.wait()


def pack(w_parts, w_out, raw):
    width = w_out.shape[1]
    whole = pl.BlockSpec(memory_space=pl.ANY)
    return pl.pallas_call(
        pack_kernel,
        out_shape=jax.ShapeDtypeStruct((4 * width + 2 * raw.shape[1], LANES), BF16),
        in_specs=[whole] * 3,
        out_specs=VMEM,
        scratch_shapes=[pltpu.SemaphoreType.DMA((5 + width // LANES,))],
        compiler_params=pltpu.CompilerParams(vmem_limit_bytes=8 * 1024 * 1024),
    )(w_parts, w_out, raw)


def w_out_of(weights_ref, width):
    return jnp.concatenate(
        [
            weights_ref[3 * width + tile * LANES : 3 * width + (tile + 1) * LANES, :]
            for tile in range(width // LANES)
        ],
        axis=1,
    )


LOG2_E = math.log2(math.e)
INV_ROOT = 1.0 / math.sqrt(HEAD)
CHUNK = 256
TILE = 64
MAIN = 6
REACH_CHUNKS = 4


def low_lanes():
    return lax.broadcasted_iota(jnp.int32, (1, LANES), 1) < HEAD


def place_block(source, place, starts, ends, stores):
    low = low_lanes()
    rows = source.shape[0]
    at = place + lax.broadcasted_iota(jnp.int32, (rows, LANES), 0)
    same = ((at >= starts) & (at < ends)).astype(F32)
    first = source[:, 0:LANES].astype(F32)
    second = source[:, LANES:].astype(F32)
    q_store, k_store, v_store, d_store, kv_store = stores
    q_store[...] = jnp.where(low, first, same * SAME_IMAGE).astype(BF16)
    k_store[...] = jnp.where(low, second, same).astype(BF16)
    v_store[...] = jnp.where(low, 0.0, first).astype(BF16)
    d_store[...] = source[:, LANES:]
    kv_store[...] = jnp.where(low, second, first).astype(BF16).T


def window_facts(counts_ref):
    half = lax.axis_index("yh")
    origin = (block_index() // 4 - 1) * 2 * CHUNK
    own_at = (2 + half) * CHUNK
    starts, ends = image_bounds(counts_ref, HEAD)
    left_from = jnp.int32(-CHUNK)
    right_to = jnp.int32((MAIN + 1) * CHUNK)
    total = -origin
    for image in range(counts_ref.shape[0]):
        left_from = jnp.where(total <= own_at, total, left_from)
        ended = total >= own_at + CHUNK
        total = total + counts_ref[image]
        right_to = jnp.where((total >= own_at + CHUNK) & jnp.logical_not(ended), total, right_to)
    return half, own_at, starts - origin, ends - origin, left_from, right_to


def by_eight(values):
    return values.reshape(values.shape[0] // 8, 8, values.shape[1])


def add_tiles(s_ref, g_ref, rows, highest, total, grads):
    for piece in range(rows // TILE):
        at = slice(piece * TILE, (piece + 1) * TILE)
        weights = jnp.exp2(s_ref[at, :] * LOG2_E - highest)
        total = total + jnp.sum(by_eight(weights), axis=0)
        grads = grads + jnp.sum(by_eight(weights * g_ref[at, :]), axis=0)
    return total, grads


def rows_max(values):
    return jnp.max(by_eight(values), axis=0)


def near_kernel(
    counts_ref,
    first_ref,
    quad_ref,
    second_ref,
    qx_ref,
    kx_ref,
    vx_ref,
    dx_ref,
    kv_ref,
    so_ref,
    go_ref,
    sn_ref,
    gn_ref,
    stats_ref,
    s_ref,
    g_ref,
):
    half, own_at, starts, ends, left_from, right_to = window_facts(counts_ref)
    block_rows = CHUNK // 2

    def place(source, begin):
        begin = pl.multiple_of(begin, block_rows)
        at = pl.ds(begin, block_rows)
        stores = [ref.at[at, :] for ref in (qx_ref, kx_ref, vx_ref, dx_ref)]
        place_block(source, begin, starts, ends, stores + [kv_ref.at[:, at]])

    to_first = jnp.where(lax.rem(lax.axis_index("z"), 2) == 0, 2 * CHUNK, -2 * CHUNK)
    for block in range(4):
        at = slice(block * block_rows, (block + 1) * block_rows)
        begin = 2 * CHUNK + block * block_rows
        place(quad_ref.at[at], begin)
        place(first_ref.at[at], begin + to_first)
        place(second_ref.at[at], begin - to_first)

    own_rows = pl.ds(pl.multiple_of(own_at, CHUNK), CHUNK)
    q_own = qx_ref[own_rows, :]
    d_own = dx_ref[own_rows, :]
    highest = jnp.full((8, CHUNK), -jnp.inf, F32)
    for piece in range(MAIN):
        at = slice(piece * CHUNK, (piece + 1) * CHUNK)
        scores = rows_dot(kx_ref[at, :], q_own)
        so_ref[at, :] = scores
        highest = jnp.maximum(highest, rows_max(scores))
        go_ref[at, :] = rows_dot(vx_ref[at, :], d_own)
    highest = jnp.max(highest, axis=0, keepdims=True) * LOG2_E
    total = jnp.zeros((8, CHUNK), F32)
    grads = jnp.zeros((8, CHUNK), F32)
    for piece in range(MAIN * CHUNK // TILE):
        at = slice(piece * TILE, (piece + 1) * TILE)
        weights = jnp.exp2(so_ref[at, :] * LOG2_E - highest)
        so_ref[at, :] = weights
        total = total + jnp.sum(by_eight(weights), axis=0)
        grads = grads + jnp.sum(by_eight(weights * go_ref[at, :]), axis=0)
    stats_ref[MAIN, 0:1, :] = highest
    stats_ref[MAIN, 1:2, :] = jnp.sum(total, axis=0, keepdims=True)
    stats_ref[MAIN, 2:3, :] = jnp.sum(grads, axis=0, keepdims=True)

    left_key = jnp.clip((left_from + CHUNK) // CHUNK - 1, 0, MAIN - REACH_CHUNKS)
    right_key = jnp.clip((right_to - 1) // CHUNK - (REACH_CHUNKS - 1), 0, MAIN - REACH_CHUNKS)

    def one_chunk(step, carry):
        slot = step + jnp.where(step >= 2 + half, 1, 0)
        begin = slot * CHUNK

        @pl.when((begin < right_to) & (begin + CHUNK > left_from))
        def _():
            at = pl.ds(pl.multiple_of(begin, CHUNK), CHUNK)
            key = jnp.where(begin < own_at, left_key, right_key) * CHUNK
            q_block = qx_ref[at, :]
            d_block = dx_ref[at, :]
            highest = jnp.full((8, CHUNK), -jnp.inf, F32)
            for piece in range(REACH_CHUNKS):
                keys_at = pl.ds(pl.multiple_of(key + piece * CHUNK, CHUNK), CHUNK)
                here = slice(piece * CHUNK, (piece + 1) * CHUNK)
                scores = rows_dot(kx_ref[keys_at, :], q_block)
                s_ref[here, :] = scores
                highest = jnp.maximum(highest, rows_max(scores))
                g_ref[here, :] = rows_dot(vx_ref[keys_at, :], d_block)
            highest = jnp.max(highest, axis=0, keepdims=True) * LOG2_E
            zeros = jnp.zeros((8, CHUNK), F32)
            total, grads = add_tiles(s_ref, g_ref, REACH_CHUNKS * CHUNK, highest, zeros, zeros)
            stats_ref[slot, 0:1, :] = highest
            stats_ref[slot, 1:2, :] = jnp.sum(total, axis=0, keepdims=True)
            stats_ref[slot, 2:3, :] = jnp.sum(grads, axis=0, keepdims=True)
            near_at = pl.ds(pl.multiple_of(own_at - key, CHUNK), CHUNK)
            sn_ref[slot, :, :] = s_ref[near_at, :]
            gn_ref[slot, :, :] = g_ref[near_at, :]

        return carry

    lax.fori_loop(0, MAIN - 1, one_chunk, 0)


def attend_near(counts, first, quad, second):
    rows = MAIN * CHUNK
    head_rows = jax.ShapeDtypeStruct((rows, LANES), BF16)
    scores = jax.ShapeDtypeStruct((rows, CHUNK), F32)
    tiles = jax.ShapeDtypeStruct((MAIN, CHUNK, CHUNK), F32)
    return pl.pallas_call(
        near_kernel,
        out_shape=(head_rows,) * 4
        + (jax.ShapeDtypeStruct((LANES, rows), BF16),)
        + (scores, scores, tiles, tiles, jax.ShapeDtypeStruct((MAIN + 1, 8, CHUNK), F32)),
        in_specs=[SMEM] + [VMEM] * 3,
        out_specs=(VMEM,) * 10,
        scratch_shapes=[pltpu.VMEM((REACH_CHUNKS * CHUNK, CHUNK), F32)] * 2,
        cost_estimate=pl.CostEstimate(
            flops=7000000000, bytes_accessed=1 << 20, transcendentals=1 << 20
        ),
        compiler_params=pltpu.CompilerParams(vmem_limit_bytes=VMEM_LIMIT),
    )(counts, first, quad, second)


def far_kernel(
    counts_ref,
    far_ref,
    qx_ref,
    kx_ref,
    vx_ref,
    dx_ref,
    kv_ref,
    so_ref,
    go_ref,
    sn_ref,
    gn_ref,
    stats_ref,
    out_ref,
    qf_ref,
    kf_ref,
    vf_ref,
    df_ref,
    kvf_ref,
    s_ref,
    g_ref,
    p_ref,
    d_ref,
    pn_ref,
    dn_ref,
    sums_ref,
    dk_ref,
    dv_ref,
    done_ref,
):
    half, own_at, starts, ends, left_from, right_to = window_facts(counts_ref)
    block_rows = CHUNK // 2
    rows = MAIN * CHUNK
    far_at = jnp.where(half == 0, -CHUNK, rows)
    for block in range(2):
        at = slice(block * block_rows, (block + 1) * block_rows)
        stores = [ref.at[at, :] for ref in (qf_ref, kf_ref, vf_ref, df_ref)]
        place_block(
            far_ref.at[at],
            far_at + block * block_rows,
            starts,
            ends,
            stores + [kvf_ref.at[:, at]],
        )

    own_rows = pl.ds(pl.multiple_of(own_at, CHUNK), CHUNK)
    q_own = qx_ref[own_rows, :]
    d_own = dx_ref[own_rows, :]
    scores = rows_dot(kf_ref[...], q_own)
    s_ref[0:CHUNK, :] = scores
    g_ref[0:CHUNK, :] = rows_dot(vf_ref[...], d_own)
    near_highest = stats_ref[MAIN, 0:1, :]
    highest = jnp.max(rows_max(scores), axis=0, keepdims=True) * LOG2_E
    highest = jnp.maximum(near_highest, highest)
    shrink = jnp.exp2(near_highest - highest)
    zeros = jnp.zeros((8, CHUNK), F32)
    total, grads = add_tiles(s_ref, g_ref, CHUNK, highest, zeros, zeros)
    total = jnp.sum(total, axis=0, keepdims=True) + stats_ref[MAIN, 1:2, :] * shrink
    grads = jnp.sum(grads, axis=0, keepdims=True) + stats_ref[MAIN, 2:3, :] * shrink
    scale = 1.0 / total
    mean_grad = grads * scale

    near_scale = shrink * scale
    for piece in range(rows // TILE):
        at = slice(piece * TILE, (piece + 1) * TILE)
        probs = so_ref[at, :] * near_scale
        p_ref[at, :] = probs.astype(BF16)
        d_ref[at, :] = (probs * (go_ref[at, :] - mean_grad)).astype(BF16)
    for piece in range(CHUNK // TILE):
        at = slice(piece * TILE, (piece + 1) * TILE)
        to = slice(rows + piece * TILE, rows + (piece + 1) * TILE)
        probs = jnp.exp2(s_ref[at, :] * LOG2_E - highest) * scale
        p_ref[to, :] = probs.astype(BF16)
        d_ref[to, :] = (probs * (g_ref[at, :] - mean_grad)).astype(BF16)
    pn_ref[:, own_rows] = p_ref[own_rows, :]
    dn_ref[:, own_rows] = d_ref[own_rows, :]

    def times_window(values_ref):
        main = jnp.dot(kv_ref[...], values_ref[0:rows, :], preferred_element_type=F32)
        return main + jnp.dot(
            kvf_ref[...], values_ref[rows : rows + CHUNK, :], preferred_element_type=F32
        )

    upper = lax.broadcasted_iota(jnp.int32, (LANES, CHUNK), 0) < HEAD
    own_out = jnp.where(upper, times_window(d_ref) * INV_ROOT, times_window(p_ref)).T

    query_lane = lax.broadcasted_iota(jnp.int32, (1, CHUNK), 1)
    reaches_far = jnp.where(half == 0, left_from < 0, right_to > rows)
    sums_ref[...] = stats_ref[...]
    dk_ref[...] = jnp.zeros_like(dk_ref)
    dv_ref[...] = jnp.zeros_like(dv_ref)

    @pl.when(reaches_far)
    def _():
        for step in range(2):
            slot = half * (MAIN - 2) + step
            begin = slot * CHUNK

            @pl.when((begin < right_to) & (begin + CHUNK > left_from))
            def _():
                at = pl.ds(pl.multiple_of(begin, CHUNK), CHUNK)
                scores = rows_dot(kf_ref[...], qx_ref[at, :])
                s_ref[0:CHUNK, :] = scores
                g_ref[0:CHUNK, :] = rows_dot(vf_ref[...], dx_ref[at, :])
                before = sums_ref[slot, 0:1, :]
                highest = jnp.max(rows_max(scores), axis=0, keepdims=True) * LOG2_E
                highest = jnp.maximum(before, highest)
                total, grads = add_tiles(s_ref, g_ref, CHUNK, highest, zeros, zeros)
                shrink = jnp.exp2(before - highest)
                total = jnp.sum(total, axis=0, keepdims=True)
                grads = jnp.sum(grads, axis=0, keepdims=True)
                sums_ref[slot, 0:1, :] = highest
                sums_ref[slot, 1:2, :] = sums_ref[slot, 1:2, :] * shrink + total
                sums_ref[slot, 2:3, :] = sums_ref[slot, 2:3, :] * shrink + grads

        q_block = qf_ref[...]
        d_block = df_ref[...]
        key = half * (MAIN // 2) * CHUNK
        highest = jnp.full((8, CHUNK), -jnp.inf, F32)
        for piece in range(REACH_CHUNKS):
            here = slice(piece * CHUNK, (piece + 1) * CHUNK)
            if piece < REACH_CHUNKS - 1:
                keys_at = pl.ds(pl.multiple_of(key + piece * CHUNK, CHUNK), CHUNK)
                keys, values = kx_ref[keys_at, :], vx_ref[keys_at, :]
            else:
                keys, values = kf_ref[...], vf_ref[...]
            scores = rows_dot(keys, q_block)
            s_ref[here, :] = scores
            highest = jnp.maximum(highest, rows_max(scores))
            g_ref[here, :] = rows_dot(values, d_block)
        highest = jnp.max(highest, axis=0, keepdims=True) * LOG2_E
        total, grads = add_tiles(s_ref, g_ref, REACH_CHUNKS * CHUNK, highest, zeros, zeros)
        total = jnp.sum(total, axis=0, keepdims=True)
        place = query_lane + far_at
        scale = jnp.where((place >= left_from) & (place < right_to), 1.0 / total, 0.0)
        mean_grad = jnp.sum(grads, axis=0, keepdims=True) * scale
        for piece in range(CHUNK // TILE):
            at = slice(piece * TILE, (piece + 1) * TILE)
            near_at = pl.ds(pl.multiple_of(own_at - key + piece * TILE, TILE), TILE)
            probs = jnp.exp2(s_ref[near_at, :] * LOG2_E - highest) * scale
            p_ref[at, :] = probs.astype(BF16)
            d_ref[at, :] = (probs * (g_ref[near_at, :] - mean_grad)).astype(BF16)
        dk_ref[...] = jnp.dot(d_ref[0:CHUNK, :], q_block, preferred_element_type=F32)
        dv_ref[...] = jnp.dot(p_ref[0:CHUNK, :], d_block, preferred_element_type=F32)

    for step in range(MAIN - 1):
        slot = step + jnp.where(step >= 2 + half, 1, 0)
        begin = slot * CHUNK
        chunk_at = pl.ds(pl.multiple_of(begin, CHUNK), CHUNK)
        place = query_lane + begin
        valid = (place >= left_from) & (place < right_to)
        highest = sums_ref[slot, 0:1, :]
        scale = 1.0 / sums_ref[slot, 1:2, :]
        mean_grad = sums_ref[slot, 2:3, :] * scale
        for piece in range(CHUNK // TILE):
            at = slice(piece * TILE, (piece + 1) * TILE)
            probs = jnp.exp2(sn_ref[slot, at, :] * LOG2_E - highest) * scale
            d_scores = probs * (gn_ref[slot, at, :] - mean_grad)
            pn_ref[at, chunk_at] = jnp.where(valid, probs, 0.0).astype(BF16)
            dn_ref[at, chunk_at] = jnp.where(valid, d_scores, 0.0).astype(BF16)
    d_key = dk_ref[...] + jnp.dot(dn_ref[...], qx_ref[...], preferred_element_type=F32)
    d_value = dv_ref[...] + jnp.dot(pn_ref[...], dx_ref[...], preferred_element_type=F32)
    done_ref[:, 0:LANES] = own_out.astype(BF16)
    done_ref[:, LANES:] = jnp.where(low_lanes(), d_key, d_value).astype(BF16)
    share = 16
    for member in range(out_ref.shape[0]):
        block, core = member // 2, member % 2
        for part in range(out_ref.shape[1] // share):
            begin = (block * 8 + part * 2 + core) * share
            out_ref[member, part * share : (part + 1) * share, :] = done_ref[
                begin : begin + share, :
            ]


def attend_far(counts, far, near_parts):
    return pl.pallas_call(
        far_kernel,
        out_shape=jax.ShapeDtypeStruct((4, CHUNK // 4, 2 * LANES), BF16),
        in_specs=[SMEM] + [VMEM] * (1 + len(near_parts)),
        out_specs=VMEM,
        scratch_shapes=[pltpu.VMEM((CHUNK, LANES), BF16)] * 4
        + [pltpu.VMEM((LANES, CHUNK), BF16)]
        + [pltpu.VMEM((REACH_CHUNKS * CHUNK, CHUNK), F32)] * 2
        + [pltpu.VMEM(((MAIN + 1) * CHUNK, CHUNK), BF16)] * 2
        + [pltpu.VMEM((CHUNK, MAIN * CHUNK), BF16)] * 2
        + [pltpu.VMEM((MAIN + 1, 8, CHUNK), F32)]
        + [pltpu.VMEM((CHUNK, LANES), F32)] * 2
        + [pltpu.VMEM((CHUNK, 2 * LANES), BF16)],
        cost_estimate=pl.CostEstimate(
            flops=7000000000, bytes_accessed=1 << 20, transcendentals=1 << 20
        ),
        compiler_params=pltpu.CompilerParams(vmem_limit_bytes=VMEM_LIMIT),
    )(counts, far, *near_parts)


def project_kernel(parts_ref, gains_ref, raw_ref, weights_ref, weights_far_ref, out_ref):
    rows = parts_ref.shape[1]
    width = out_ref.shape[2] // 2
    share = out_ref.shape[1]
    core = lax.axis_index("core")
    low = low_lanes()
    q_gain = both_heads(gains_ref, 0)
    k_gain = both_heads(gains_ref, 1)

    def norm_grad(raw, gain, d_norm):
        raw = raw.astype(F32)
        inverse = head_scale(raw)
        scaled = d_norm * gain
        inner = head_sums(raw * scaled) * (1.0 / HEAD)
        return inverse * scaled - raw * (inverse * inverse * inverse * inner)

    def by_column(which, raw):
        head0 = parts_ref[which].astype(F32)
        head1 = parts_ref[2 + which].astype(F32)
        a0, a1 = head0[:, :LANES], head1[:, :LANES]
        b0, b1 = head0[:, LANES:], head1[:, LANES:]
        d_q = norm_grad(raw[0], q_gain, jnp.where(low, a0, pltpu.roll(a1, HEAD, 1)))
        attn = jnp.where(low, pltpu.roll(a0, HEAD, 1), a1).astype(BF16)
        d_k = norm_grad(raw[1], k_gain, jnp.where(low, b0, pltpu.roll(b1, HEAD, 1)))
        d_v = jnp.where(low, pltpu.roll(b0, HEAD, 1), b1)
        return attn, [values.astype(BF16) for values in (d_q, d_k, d_v)]

    raw_far = [
        weights_far_ref[4 * width + array * rows : 4 * width + (array + 1) * rows, :]
        for array in range(2)
    ]
    attn, grads = by_column(core, [raw_ref[0], raw_ref[1]])
    attn_far, grads_far = by_column(1 - core, raw_far)
    both = (weights_ref, weights_far_ref)
    mixed = jnp.dot(
        jnp.concatenate([attn, attn_far], axis=1),
        jnp.concatenate([w_out_of(ref, width) for ref in both], axis=0),
        preferred_element_type=F32,
    ).astype(BF16)
    weights = [ref[part * width : (part + 1) * width, :] for ref in both for part in range(3)]
    d_hidden = rows_dot(
        jnp.concatenate(grads + grads_far, axis=1), jnp.concatenate(weights, axis=1)
    ).astype(BF16)
    for place in range(out_ref.shape[0]):
        at = slice(place * share, (place + 1) * share)
        out_ref[place, :, :width] = mixed[at]
        out_ref[place, :, width:] = d_hidden[at]


def project(parts, gains, raw, weights, weights_far, x_count, width):
    return pl.pallas_call(
        project_kernel,
        out_shape=jax.ShapeDtypeStruct((x_count, parts.shape[1] // x_count, 2 * width), BF16),
        in_specs=[VMEM] * 5,
        out_specs=VMEM,
        compiler_params=pltpu.CompilerParams(vmem_limit_bytes=VMEM_LIMIT),
    )(parts, gains, raw, weights, weights_far)


def ready_kernel(
    counts_ref,
    tokens_ref,
    cotangent_ref,
    modulation_ref,
    rows_ref,
    factors_ref,
):
    rows = rows_ref.shape[1]
    first_row = (lax.axis_index("x") * 2 + lax.axis_index("core")) * rows
    first = block_index() * tokens_ref.shape[0] + first_row
    _, scale, gate = modulation_rows(counts_ref, modulation_ref, first, rows)
    at = pl.ds(pl.multiple_of(first_row, rows), rows)
    normed, inv_std = layer_norm(tokens_ref[at, :].astype(F32))
    rows_ref[0] = tokens_ref[at, :]
    rows_ref[1] = cotangent_ref[at, :]
    factors_ref[0] = gate
    factors_ref[1] = 1.0 + scale
    factors_ref[2] = normed
    factors_ref[3] = jnp.broadcast_to(inv_std, normed.shape)


def ready(counts, tokens, cotangent, modulation, share):
    width = tokens.shape[1]
    return pl.pallas_call(
        ready_kernel,
        out_shape=(
            jax.ShapeDtypeStruct((2, share, width), BF16),
            jax.ShapeDtypeStruct((4, share, width), F32),
        ),
        in_specs=[SMEM] + [VMEM] * 3,
        out_specs=(VMEM, VMEM),
        compiler_params=pltpu.CompilerParams(vmem_limit_bytes=VMEM_LIMIT),
    )(counts, tokens, cotangent, modulation)


def leave_kernel(rows_ref, factors_ref, shares_ref, layer_ref, grad_ref):
    width = layer_ref.shape[1]
    sums = shares_ref[0].astype(F32)
    for share in range(1, shares_ref.shape[0]):
        sums = sums + shares_ref[share].astype(F32)
    layer = rows_ref[0].astype(F32) + factors_ref[0] * sums[:, :width]
    layer_ref[...] = layer.astype(BF16)
    d_normed = sums[:, width:] * factors_ref[1]
    normed = factors_ref[2]
    input_grad = rows_ref[1].astype(F32) + factors_ref[3] * (
        d_normed
        - jnp.mean(d_normed, axis=-1, keepdims=True)
        - normed * jnp.mean(d_normed * normed, axis=-1, keepdims=True)
    )
    grad_ref[...] = input_grad.astype(BF16)


def leave(rows, factors, shares):
    out = jax.ShapeDtypeStruct(rows.shape[1:], BF16)
    return pl.pallas_call(
        leave_kernel,
        out_shape=(out, out),
        in_specs=[VMEM] * 3,
        out_specs=(VMEM, VMEM),
        compiler_params=pltpu.CompilerParams(vmem_limit_bytes=VMEM_LIMIT),
    )(rows, factors, shares)


def per_device(tokens, cotangent, w_qkv, w_out, qk_gain, modulation, image_counts):
    tok_rows, model_width = tokens.shape
    z_count = lax.axis_size("z")
    x_count = lax.axis_size("x")
    quad = 4
    pair_rows = 2 * tok_rows
    share = tok_rows // (2 * x_count)
    w_parts = w_qkv.transpose(1, 0, 2)
    mod_parts = modulation.transpose(1, 0, 2)

    heads, raw, raw_far = enter(
        image_counts, qk_gain, tokens, cotangent, w_parts, w_out, mod_parts, quad
    )
    mine = lax.all_to_all(heads, ("yh", "yl"), 0, 0)
    mine = mine.reshape(quad * tok_rows, 2 * LANES)
    evens = range(0, z_count, 2)
    swaps = [(i, i + 1) for i in evens], [((i - 1) % z_count, i) for i in evens]
    first, second = (
        lax.ppermute(mine, "z", pairs + [(j, i) for i, j in pairs]) for pairs in swaps
    )
    halves = 4 * z_count
    far_half = jnp.where(
        lax.axis_index("yh") == lax.axis_index("core"), mine[pair_rows:], mine[:pair_rows]
    )

    def far_source(target):
        z, yh, core = target // 4, target // 2 % 2, target % 2
        return (z + (2 if yh else -2)) % z_count * 4 + (yh ^ core) * 2 + core

    far = lax.ppermute(
        far_half, ("z", "yh", "core"), [(far_source(i), i) for i in range(halves)]
    )
    _, tokens_late, cotangent_late, mod_late = lax.optimization_barrier(
        (mine, tokens, cotangent, mod_parts)
    )
    rows, factors = ready(image_counts, tokens_late, cotangent_late, mod_late, share)
    near_parts = attend_near(image_counts, first, mine, second)
    _, w_parts_late, w_out_late = lax.optimization_barrier((mine, w_parts, w_out))
    weights = pack(w_parts_late, w_out_late, raw_far)
    weights_far = lax.ppermute(weights, "core", [(0, 1), (1, 0)])
    parts = attend_far(image_counts, far, near_parts)
    parts = lax.all_to_all(parts, ("yl", "core"), 0, 0)
    partial = project(parts, qk_gain, raw, weights, weights_far, x_count, model_width)
    shares = lax.all_to_all(partial, "x", 0, 0)
    return leave(rows, factors, shares)


def solution(mesh):
    split = jax.sharding.Mesh(mesh.devices.reshape(16, 2, 2, 4, 2), ("z", "yh", "yl", "x", "core"))
    dp, head = ("z", "yh", "yl"), ("x", "core")
    in_specs = (P(dp, None), P(dp, None), P(None, None, head), P(head, None), P(), P(), P())
    out_specs = (P(dp + head, None), P(dp + head, None))
    return jax.shard_map(
        per_device, mesh=split, in_specs=in_specs, out_specs=out_specs, check_vma=False
    )
```

```python
import math

import jax
import jax.numpy as jnp
from jax import lax
from jax.experimental import pallas as pl
from jax.experimental.pallas import tpu as pltpu
from jax.sharding import PartitionSpec as P

EPS = 1e-06
SAME_IMAGE = 512.0
LANES = 128
HEAD = 64
F32 = jnp.float32
BF16 = jnp.bfloat16
VMEM_LIMIT = 24 * 1024 * 1024
ENTER_LIMIT = 60 * 1024 * 1024
VMEM = pl.BlockSpec(memory_space=pltpu.VMEM)
SMEM = pl.BlockSpec(memory_space=pltpu.SMEM)


def rows_dot(a, b):
    return lax.dot_general(a, b, (((1,), (1,)), ((), ())), preferred_element_type=F32)


def block_index():
    return (lax.axis_index("z") * 2 + lax.axis_index("yh")) * 2 + lax.axis_index("yl")


def image_bounds(counts_ref, first_lane):
    lane = lax.broadcasted_iota(jnp.int32, (1, LANES), 1)
    starts = jnp.zeros((1, LANES), jnp.int32)
    ends = jnp.zeros((1, LANES), jnp.int32)
    total = jnp.int32(0)
    for image in range(counts_ref.shape[0]):
        here = lane == first_lane + image
        starts = jnp.where(here, total, starts)
        total = total + counts_ref[image]
        ends = jnp.where(here, total, ends)
    return starts, ends


def modulation_rows(counts_ref, modulation_ref, first, rows):
    starts, ends = image_bounds(counts_ref, 0)
    place = first + lax.broadcasted_iota(jnp.int32, (rows, LANES), 0)
    member = ((place >= starts) & (place < ends)).astype(F32).astype(BF16)
    member = member[:, : modulation_ref.shape[1]]
    return [
        jnp.dot(member, modulation_ref[part], preferred_element_type=F32) for part in range(3)
    ]


def layer_norm(values):
    average = jnp.mean(values, axis=-1, keepdims=True)
    centred = values - average
    inv_std = lax.rsqrt(jnp.mean(centred * centred, axis=-1, keepdims=True) + EPS)
    return centred * inv_std, inv_std


def head_sums(values):
    lanes = (LANES, LANES)
    first = lax.broadcasted_iota(jnp.int32, lanes, 0) < HEAD
    second = lax.broadcasted_iota(jnp.int32, lanes, 1) < HEAD
    ones = (first == second).astype(F32).astype(BF16)
    large = values.astype(BF16)
    small = (values - large.astype(F32)).astype(BF16)
    large = jnp.dot(large, ones, preferred_element_type=F32)
    return large + jnp.dot(small, ones, preferred_element_type=F32)


def both_heads(gains_ref, which):
    gain = gains_ref[which : which + 1, :]
    return jnp.concatenate([gain, gain], axis=1)


def head_scale(raw):
    return lax.rsqrt(head_sums(raw * raw) * (1.0 / HEAD) + EPS)


def enter_kernel(
    counts_ref,
    gains_ref,
    tokens_ref,
    cotangent_ref,
    w_qkv_ref,
    w_out_ref,
    modulation_ref,
    out_ref,
    raw_ref,
    raw_far_ref,
    rows_ref,
):
    rows = tokens_ref.shape[0]
    first = block_index() * rows
    shift, scale, gate = modulation_rows(counts_ref, modulation_ref, first, rows)
    normed, _ = layer_norm(tokens_ref[...].astype(F32))
    hidden = (normed * (1.0 + scale) + shift).astype(BF16)
    weights = jnp.concatenate([w_qkv_ref[part] for part in range(3)], axis=1)
    qkv = jnp.dot(hidden, weights, preferred_element_type=F32)
    q, k, v = (qkv[:, part * LANES : (part + 1) * LANES] for part in range(3))
    d_mixed = (cotangent_ref[...].astype(F32) * gate).astype(BF16)
    d_attn = rows_dot(d_mixed, w_out_ref[...])
    rows_ref[0] = q.astype(BF16)
    rows_ref[1] = k.astype(BF16)
    q = rows_ref[0].astype(F32)
    k = rows_ref[1].astype(F32)
    q = q * head_scale(q) * (both_heads(gains_ref, 0) * (1.0 / math.sqrt(HEAD)))
    k = k * head_scale(k) * both_heads(gains_ref, 1)
    core = lax.axis_index("core")
    share = raw_ref.shape[1] // 4
    for ref, side in ((raw_ref, core), (raw_far_ref, 1 - core)):
        for part in range(4):
            begin = pl.multiple_of((2 * part + side) * share, share)
            for array in range(2):
                ref[array, part * share : (part + 1) * share, :] = rows_ref[
                    array, pl.ds(begin, share), :
                ]
    low = low_lanes()

    def beside(left, right):
        return jnp.where(low, left, right).astype(BF16)

    q_v = (beside(q, pltpu.roll(v, HEAD, 1)), beside(pltpu.roll(q, HEAD, 1), v))
    k_d = (beside(k, pltpu.roll(d_attn, HEAD, 1)), beside(pltpu.roll(k, HEAD, 1), d_attn))
    for place in range(out_ref.shape[0]):
        out_ref[place, :, 0:LANES] = q_v[place % 2]
        out_ref[place, :, LANES:] = k_d[place % 2]


def enter(counts, gains, tokens, cotangent, w_parts, w_out, modulation, quad):
    rows = tokens.shape[0]
    raw = jax.ShapeDtypeStruct((2, rows // 2, LANES), BF16)
    return pl.pallas_call(
        enter_kernel,
        out_shape=(jax.ShapeDtypeStruct((quad, rows, 2 * LANES), BF16), raw, raw),
        in_specs=[SMEM] + [VMEM] * 6,
        out_specs=(VMEM,) * 3,
        scratch_shapes=[pltpu.VMEM((2, rows, LANES), BF16)],
        compiler_params=pltpu.CompilerParams(vmem_limit_bytes=ENTER_LIMIT),
    )(counts, gains, tokens, cotangent, w_parts, w_out, modulation)


def pack_kernel(w_qkv_ref, w_out_ref, raw_ref, weights_ref, sems):
    width = w_out_ref.shape[1]
    rows = raw_ref.shape[1]
    pairs = []
    for part in range(3):
        pairs.append((w_qkv_ref.at[part], weights_ref.at[part * width : (part + 1) * width, :]))
    for tile in range(width // LANES):
        at = slice(tile * LANES, (tile + 1) * LANES)
        to = slice(3 * width + tile * LANES, 3 * width + (tile + 1) * LANES)
        pairs.append((w_out_ref.at[:, at], weights_ref.at[to, :]))
    for array in range(2):
        to = slice(4 * width + array * rows, 4 * width + (array + 1) * rows)
        pairs.append((raw_ref.at[array], weights_ref.at[to, :]))
    copies = [
        pltpu.make_async_copy(source, target, sems.at[place])
        for place, (source, target) in enumerate(pairs)
    ]
    for copy in copies:
        copy.start()
    for copy in copies:
        copy.wait()


def pack(w_parts, w_out, raw):
    width = w_out.shape[1]
    whole = pl.BlockSpec(memory_space=pl.ANY)
    return pl.pallas_call(
        pack_kernel,
        out_shape=jax.ShapeDtypeStruct((4 * width + 2 * raw.shape[1], LANES), BF16),
        in_specs=[whole] * 3,
        out_specs=whole,
        scratch_shapes=[pltpu.SemaphoreType.DMA((5 + width // LANES,))],
        compiler_params=pltpu.CompilerParams(vmem_limit_bytes=ENTER_LIMIT),
    )(w_parts, w_out, raw)


def w_out_of(weights_ref, width):
    return jnp.concatenate(
        [
            weights_ref[3 * width + tile * LANES : 3 * width + (tile + 1) * LANES, :]
            for tile in range(width // LANES)
        ],
        axis=1,
    )


LOG2_E = math.log2(math.e)
INV_ROOT = 1.0 / math.sqrt(HEAD)
CHUNK = 256
TILE = 64
MAIN = 6
REACH_CHUNKS = 4


def low_lanes():
    return lax.broadcasted_iota(jnp.int32, (1, LANES), 1) < HEAD


def place_block(source, place, starts, ends, stores):
    low = low_lanes()
    rows = source.shape[0]
    at = place + lax.broadcasted_iota(jnp.int32, (rows, LANES), 0)
    same = ((at >= starts) & (at < ends)).astype(F32)
    first = source[:, 0:LANES].astype(F32)
    second = source[:, LANES:].astype(F32)
    q_store, k_store, v_store, d_store, kv_store = stores
    q_store[...] = jnp.where(low, first, same * SAME_IMAGE).astype(BF16)
    k_store[...] = jnp.where(low, second, same).astype(BF16)
    v_store[...] = jnp.where(low, 0.0, first).astype(BF16)
    d_store[...] = source[:, LANES:]
    kv_store[...] = jnp.where(low, second, first).astype(BF16).T


def window_facts(counts_ref):
    half = lax.axis_index("yh")
    origin = (block_index() // 4 - 1) * 2 * CHUNK
    own_at = (2 + half) * CHUNK
    starts, ends = image_bounds(counts_ref, HEAD)
    left_from = jnp.int32(-CHUNK)
    right_to = jnp.int32((MAIN + 1) * CHUNK)
    total = -origin
    for image in range(counts_ref.shape[0]):
        left_from = jnp.where(total <= own_at, total, left_from)
        ended = total >= own_at + CHUNK
        total = total + counts_ref[image]
        right_to = jnp.where((total >= own_at + CHUNK) & jnp.logical_not(ended), total, right_to)
    return half, own_at, starts - origin, ends - origin, left_from, right_to


def by_eight(values):
    return values.reshape(values.shape[0] // 8, 8, values.shape[1])


def add_tiles(s_ref, g_ref, rows, highest, total, grads):
    for piece in range(rows // TILE):
        at = slice(piece * TILE, (piece + 1) * TILE)
        weights = jnp.exp2(s_ref[at, :] * LOG2_E - highest)
        total = total + jnp.sum(by_eight(weights), axis=0)
        grads = grads + jnp.sum(by_eight(weights * g_ref[at, :]), axis=0)
    return total, grads


def rows_max(values):
    return jnp.max(by_eight(values), axis=0)


def near_kernel(
    counts_ref,
    first_ref,
    quad_ref,
    second_ref,
    qx_ref,
    kx_ref,
    vx_ref,
    dx_ref,
    kv_ref,
    so_ref,
    go_ref,
    sn_ref,
    gn_ref,
    stats_ref,
    s_ref,
    g_ref,
):
    half, own_at, starts, ends, left_from, right_to = window_facts(counts_ref)
    block_rows = CHUNK // 2

    def place(source, begin):
        begin = pl.multiple_of(begin, block_rows)
        at = pl.ds(begin, block_rows)
        stores = [ref.at[at, :] for ref in (qx_ref, kx_ref, vx_ref, dx_ref)]
        place_block(source, begin, starts, ends, stores + [kv_ref.at[:, at]])

    to_first = jnp.where(lax.rem(lax.axis_index("z"), 2) == 0, 2 * CHUNK, -2 * CHUNK)
    for block in range(4):
        at = slice(block * block_rows, (block + 1) * block_rows)
        begin = 2 * CHUNK + block * block_rows
        place(quad_ref.at[at], begin)
        place(first_ref.at[at], begin + to_first)
        place(second_ref.at[at], begin - to_first)

    own_rows = pl.ds(pl.multiple_of(own_at, CHUNK), CHUNK)
    q_own = qx_ref[own_rows, :]
    d_own = dx_ref[own_rows, :]
    highest = jnp.full((8, CHUNK), -jnp.inf, F32)
    for piece in range(MAIN):
        at = slice(piece * CHUNK, (piece + 1) * CHUNK)
        scores = rows_dot(kx_ref[at, :], q_own)
        so_ref[at, :] = scores
        highest = jnp.maximum(highest, rows_max(scores))
        go_ref[at, :] = rows_dot(vx_ref[at, :], d_own)
    highest = jnp.max(highest, axis=0, keepdims=True) * LOG2_E
    total = jnp.zeros((8, CHUNK), F32)
    grads = jnp.zeros((8, CHUNK), F32)
    for piece in range(MAIN * CHUNK // TILE):
        at = slice(piece * TILE, (piece + 1) * TILE)
        weights = jnp.exp2(so_ref[at, :] * LOG2_E - highest)
        so_ref[at, :] = weights
        total = total + jnp.sum(by_eight(weights), axis=0)
        grads = grads + jnp.sum(by_eight(weights * go_ref[at, :]), axis=0)
    stats_ref[MAIN, 0:1, :] = highest
    stats_ref[MAIN, 1:2, :] = jnp.sum(total, axis=0, keepdims=True)
    stats_ref[MAIN, 2:3, :] = jnp.sum(grads, axis=0, keepdims=True)

    left_key = jnp.clip((left_from + CHUNK) // CHUNK - 1, 0, MAIN - REACH_CHUNKS)
    right_key = jnp.clip((right_to - 1) // CHUNK - (REACH_CHUNKS - 1), 0, MAIN - REACH_CHUNKS)

    def one_chunk(step, carry):
        slot = step + jnp.where(step >= 2 + half, 1, 0)
        begin = slot * CHUNK

        @pl.when((begin < right_to) & (begin + CHUNK > left_from))
        def _():
            at = pl.ds(pl.multiple_of(begin, CHUNK), CHUNK)
            key = jnp.where(begin < own_at, left_key, right_key) * CHUNK
            q_block = qx_ref[at, :]
            d_block = dx_ref[at, :]
            highest = jnp.full((8, CHUNK), -jnp.inf, F32)
            for piece in range(REACH_CHUNKS):
                keys_at = pl.ds(pl.multiple_of(key + piece * CHUNK, CHUNK), CHUNK)
                here = slice(piece * CHUNK, (piece + 1) * CHUNK)
                scores = rows_dot(kx_ref[keys_at, :], q_block)
                s_ref[here, :] = scores
                highest = jnp.maximum(highest, rows_max(scores))
                g_ref[here, :] = rows_dot(vx_ref[keys_at, :], d_block)
            highest = jnp.max(highest, axis=0, keepdims=True) * LOG2_E
            zeros = jnp.zeros((8, CHUNK), F32)
            total, grads = add_tiles(s_ref, g_ref, REACH_CHUNKS * CHUNK, highest, zeros, zeros)
            stats_ref[slot, 0:1, :] = highest
            stats_ref[slot, 1:2, :] = jnp.sum(total, axis=0, keepdims=True)
            stats_ref[slot, 2:3, :] = jnp.sum(grads, axis=0, keepdims=True)
            near_at = pl.ds(pl.multiple_of(own_at - key, CHUNK), CHUNK)
            sn_ref[slot, :, :] = s_ref[near_at, :]
            gn_ref[slot, :, :] = g_ref[near_at, :]

        return carry

    lax.fori_loop(0, MAIN - 1, one_chunk, 0)


def attend_near(counts, first, quad, second):
    rows = MAIN * CHUNK
    head_rows = jax.ShapeDtypeStruct((rows, LANES), BF16)
    scores = jax.ShapeDtypeStruct((rows, CHUNK), F32)
    tiles = jax.ShapeDtypeStruct((MAIN, CHUNK, CHUNK), F32)
    return pl.pallas_call(
        near_kernel,
        out_shape=(head_rows,) * 4
        + (jax.ShapeDtypeStruct((LANES, rows), BF16),)
        + (scores, scores, tiles, tiles, jax.ShapeDtypeStruct((MAIN + 1, 8, CHUNK), F32)),
        in_specs=[SMEM] + [VMEM] * 3,
        out_specs=(VMEM,) * 10,
        scratch_shapes=[pltpu.VMEM((REACH_CHUNKS * CHUNK, CHUNK), F32)] * 2,
        cost_estimate=pl.CostEstimate(
            flops=9000000000, bytes_accessed=1 << 20, transcendentals=1 << 20
        ),
        compiler_params=pltpu.CompilerParams(vmem_limit_bytes=VMEM_LIMIT),
    )(counts, first, quad, second)


def far_kernel(
    counts_ref,
    far_ref,
    qx_ref,
    kx_ref,
    vx_ref,
    dx_ref,
    kv_ref,
    so_ref,
    go_ref,
    sn_ref,
    gn_ref,
    stats_ref,
    out_ref,
    qf_ref,
    kf_ref,
    vf_ref,
    df_ref,
    kvf_ref,
    s_ref,
    g_ref,
    p_ref,
    d_ref,
    pn_ref,
    dn_ref,
    sums_ref,
    dk_ref,
    dv_ref,
    done_ref,
):
    half, own_at, starts, ends, left_from, right_to = window_facts(counts_ref)
    block_rows = CHUNK // 2
    rows = MAIN * CHUNK
    far_at = jnp.where(half == 0, -CHUNK, rows)
    for block in range(2):
        at = slice(block * block_rows, (block + 1) * block_rows)
        stores = [ref.at[at, :] for ref in (qf_ref, kf_ref, vf_ref, df_ref)]
        place_block(
            far_ref.at[at],
            far_at + block * block_rows,
            starts,
            ends,
            stores + [kvf_ref.at[:, at]],
        )

    own_rows = pl.ds(pl.multiple_of(own_at, CHUNK), CHUNK)
    q_own = qx_ref[own_rows, :]
    d_own = dx_ref[own_rows, :]
    scores = rows_dot(kf_ref[...], q_own)
    s_ref[0:CHUNK, :] = scores
    g_ref[0:CHUNK, :] = rows_dot(vf_ref[...], d_own)
    near_highest = stats_ref[MAIN, 0:1, :]
    highest = jnp.max(rows_max(scores), axis=0, keepdims=True) * LOG2_E
    highest = jnp.maximum(near_highest, highest)
    shrink = jnp.exp2(near_highest - highest)
    zeros = jnp.zeros((8, CHUNK), F32)
    total, grads = add_tiles(s_ref, g_ref, CHUNK, highest, zeros, zeros)
    total = jnp.sum(total, axis=0, keepdims=True) + stats_ref[MAIN, 1:2, :] * shrink
    grads = jnp.sum(grads, axis=0, keepdims=True) + stats_ref[MAIN, 2:3, :] * shrink
    scale = 1.0 / total
    mean_grad = grads * scale

    near_scale = shrink * scale
    for piece in range(rows // TILE):
        at = slice(piece * TILE, (piece + 1) * TILE)
        probs = so_ref[at, :] * near_scale
        p_ref[at, :] = probs.astype(BF16)
        d_ref[at, :] = (probs * (go_ref[at, :] - mean_grad)).astype(BF16)
    for piece in range(CHUNK // TILE):
        at = slice(piece * TILE, (piece + 1) * TILE)
        to = slice(rows + piece * TILE, rows + (piece + 1) * TILE)
        probs = jnp.exp2(s_ref[at, :] * LOG2_E - highest) * scale
        p_ref[to, :] = probs.astype(BF16)
        d_ref[to, :] = (probs * (g_ref[at, :] - mean_grad)).astype(BF16)
    pn_ref[:, own_rows] = p_ref[own_rows, :]
    dn_ref[:, own_rows] = d_ref[own_rows, :]

    def times_window(values_ref):
        main = jnp.dot(kv_ref[...], values_ref[0:rows, :], preferred_element_type=F32)
        return main + jnp.dot(
            kvf_ref[...], values_ref[rows : rows + CHUNK, :], preferred_element_type=F32
        )

    upper = lax.broadcasted_iota(jnp.int32, (LANES, CHUNK), 0) < HEAD
    own_out = jnp.where(upper, times_window(d_ref) * INV_ROOT, times_window(p_ref)).T

    query_lane = lax.broadcasted_iota(jnp.int32, (1, CHUNK), 1)
    reaches_far = jnp.where(half == 0, left_from < 0, right_to > rows)
    sums_ref[...] = stats_ref[...]
    dk_ref[...] = jnp.zeros_like(dk_ref)
    dv_ref[...] = jnp.zeros_like(dv_ref)

    @pl.when(reaches_far)
    def _():
        for step in range(2):
            slot = half * (MAIN - 2) + step
            begin = slot * CHUNK

            @pl.when((begin < right_to) & (begin + CHUNK > left_from))
            def _():
                at = pl.ds(pl.multiple_of(begin, CHUNK), CHUNK)
                scores = rows_dot(kf_ref[...], qx_ref[at, :])
                s_ref[0:CHUNK, :] = scores
                g_ref[0:CHUNK, :] = rows_dot(vf_ref[...], dx_ref[at, :])
                before = sums_ref[slot, 0:1, :]
                highest = jnp.max(rows_max(scores), axis=0, keepdims=True) * LOG2_E
                highest = jnp.maximum(before, highest)
                total, grads = add_tiles(s_ref, g_ref, CHUNK, highest, zeros, zeros)
                shrink = jnp.exp2(before - highest)
                total = jnp.sum(total, axis=0, keepdims=True)
                grads = jnp.sum(grads, axis=0, keepdims=True)
                sums_ref[slot, 0:1, :] = highest
                sums_ref[slot, 1:2, :] = sums_ref[slot, 1:2, :] * shrink + total
                sums_ref[slot, 2:3, :] = sums_ref[slot, 2:3, :] * shrink + grads

        q_block = qf_ref[...]
        d_block = df_ref[...]
        key = half * (MAIN // 2) * CHUNK
        highest = jnp.full((8, CHUNK), -jnp.inf, F32)
        for piece in range(REACH_CHUNKS):
            here = slice(piece * CHUNK, (piece + 1) * CHUNK)
            if piece < REACH_CHUNKS - 1:
                keys_at = pl.ds(pl.multiple_of(key + piece * CHUNK, CHUNK), CHUNK)
                keys, values = kx_ref[keys_at, :], vx_ref[keys_at, :]
            else:
                keys, values = kf_ref[...], vf_ref[...]
            scores = rows_dot(keys, q_block)
            s_ref[here, :] = scores
            highest = jnp.maximum(highest, rows_max(scores))
            g_ref[here, :] = rows_dot(values, d_block)
        highest = jnp.max(highest, axis=0, keepdims=True) * LOG2_E
        total, grads = add_tiles(s_ref, g_ref, REACH_CHUNKS * CHUNK, highest, zeros, zeros)
        total = jnp.sum(total, axis=0, keepdims=True)
        place = query_lane + far_at
        scale = jnp.where((place >= left_from) & (place < right_to), 1.0 / total, 0.0)
        mean_grad = jnp.sum(grads, axis=0, keepdims=True) * scale
        for piece in range(CHUNK // TILE):
            at = slice(piece * TILE, (piece + 1) * TILE)
            near_at = pl.ds(pl.multiple_of(own_at - key + piece * TILE, TILE), TILE)
            probs = jnp.exp2(s_ref[near_at, :] * LOG2_E - highest) * scale
            p_ref[at, :] = probs.astype(BF16)
            d_ref[at, :] = (probs * (g_ref[near_at, :] - mean_grad)).astype(BF16)
        dk_ref[...] = jnp.dot(d_ref[0:CHUNK, :], q_block, preferred_element_type=F32)
        dv_ref[...] = jnp.dot(p_ref[0:CHUNK, :], d_block, preferred_element_type=F32)

    for step in range(MAIN - 1):
        slot = step + jnp.where(step >= 2 + half, 1, 0)
        begin = slot * CHUNK
        chunk_at = pl.ds(pl.multiple_of(begin, CHUNK), CHUNK)
        place = query_lane + begin
        valid = (place >= left_from) & (place < right_to)
        highest = sums_ref[slot, 0:1, :]
        scale = 1.0 / sums_ref[slot, 1:2, :]
        mean_grad = sums_ref[slot, 2:3, :] * scale
        for piece in range(CHUNK // TILE):
            at = slice(piece * TILE, (piece + 1) * TILE)
            probs = jnp.exp2(sn_ref[slot, at, :] * LOG2_E - highest) * scale
            d_scores = probs * (gn_ref[slot, at, :] - mean_grad)
            pn_ref[at, chunk_at] = jnp.where(valid, probs, 0.0).astype(BF16)
            dn_ref[at, chunk_at] = jnp.where(valid, d_scores, 0.0).astype(BF16)
    d_key = dk_ref[...] + jnp.dot(dn_ref[...], qx_ref[...], preferred_element_type=F32)
    d_value = dv_ref[...] + jnp.dot(pn_ref[...], dx_ref[...], preferred_element_type=F32)
    done_ref[:, 0:LANES] = own_out.astype(BF16)
    done_ref[:, LANES:] = jnp.where(low_lanes(), d_key, d_value).astype(BF16)
    share = 16
    for member in range(out_ref.shape[0]):
        block, core = member // 2, member % 2
        for part in range(out_ref.shape[1] // share):
            begin = (block * 8 + part * 2 + core) * share
            out_ref[member, part * share : (part + 1) * share, :] = done_ref[
                begin : begin + share, :
            ]


def attend_far(counts, far, near_parts):
    return pl.pallas_call(
        far_kernel,
        out_shape=jax.ShapeDtypeStruct((4, CHUNK // 4, 2 * LANES), BF16),
        in_specs=[SMEM] + [VMEM] * (1 + len(near_parts)),
        out_specs=VMEM,
        scratch_shapes=[pltpu.VMEM((CHUNK, LANES), BF16)] * 4
        + [pltpu.VMEM((LANES, CHUNK), BF16)]
        + [pltpu.VMEM((REACH_CHUNKS * CHUNK, CHUNK), F32)] * 2
        + [pltpu.VMEM(((MAIN + 1) * CHUNK, CHUNK), BF16)] * 2
        + [pltpu.VMEM((CHUNK, MAIN * CHUNK), BF16)] * 2
        + [pltpu.VMEM((MAIN + 1, 8, CHUNK), F32)]
        + [pltpu.VMEM((CHUNK, LANES), F32)] * 2
        + [pltpu.VMEM((CHUNK, 2 * LANES), BF16)],
        cost_estimate=pl.CostEstimate(
            flops=9000000000, bytes_accessed=1 << 20, transcendentals=1 << 20
        ),
        compiler_params=pltpu.CompilerParams(vmem_limit_bytes=VMEM_LIMIT),
    )(counts, far, *near_parts)


def project_kernel(parts_ref, gains_ref, raw_ref, weights_ref, weights_far_ref, out_ref):
    rows = parts_ref.shape[1]
    width = out_ref.shape[2] // 2
    share = out_ref.shape[1]
    core = lax.axis_index("core")
    low = low_lanes()
    q_gain = both_heads(gains_ref, 0)
    k_gain = both_heads(gains_ref, 1)

    def norm_grad(raw, gain, d_norm):
        raw = raw.astype(F32)
        inverse = head_scale(raw)
        scaled = d_norm * gain
        inner = head_sums(raw * scaled) * (1.0 / HEAD)
        return inverse * scaled - raw * (inverse * inverse * inverse * inner)

    def by_column(which, raw):
        head0 = parts_ref[which].astype(F32)
        head1 = parts_ref[2 + which].astype(F32)
        a0, a1 = head0[:, :LANES], head1[:, :LANES]
        b0, b1 = head0[:, LANES:], head1[:, LANES:]
        d_q = norm_grad(raw[0], q_gain, jnp.where(low, a0, pltpu.roll(a1, HEAD, 1)))
        attn = jnp.where(low, pltpu.roll(a0, HEAD, 1), a1).astype(BF16)
        d_k = norm_grad(raw[1], k_gain, jnp.where(low, b0, pltpu.roll(b1, HEAD, 1)))
        d_v = jnp.where(low, pltpu.roll(b0, HEAD, 1), b1)
        return attn, [values.astype(BF16) for values in (d_q, d_k, d_v)]

    raw_far = [
        weights_far_ref[4 * width + array * rows : 4 * width + (array + 1) * rows, :]
        for array in range(2)
    ]
    attn, grads = by_column(core, [raw_ref[0], raw_ref[1]])
    attn_far, grads_far = by_column(1 - core, raw_far)
    both = (weights_ref, weights_far_ref)
    mixed = jnp.dot(
        jnp.concatenate([attn, attn_far], axis=1),
        jnp.concatenate([w_out_of(ref, width) for ref in both], axis=0),
        preferred_element_type=F32,
    ).astype(BF16)
    weights = [ref[part * width : (part + 1) * width, :] for ref in both for part in range(3)]
    d_hidden = rows_dot(
        jnp.concatenate(grads + grads_far, axis=1), jnp.concatenate(weights, axis=1)
    ).astype(BF16)
    for place in range(out_ref.shape[0]):
        at = slice(place * share, (place + 1) * share)
        out_ref[place, :, :width] = mixed[at]
        out_ref[place, :, width:] = d_hidden[at]


def project(parts, gains, raw, weights, weights_far, x_count, width):
    return pl.pallas_call(
        project_kernel,
        out_shape=jax.ShapeDtypeStruct((x_count, parts.shape[1] // x_count, 2 * width), BF16),
        in_specs=[VMEM] * 5,
        out_specs=VMEM,
        compiler_params=pltpu.CompilerParams(vmem_limit_bytes=VMEM_LIMIT),
    )(parts, gains, raw, weights, weights_far)


def ready_kernel(
    counts_ref,
    tokens_ref,
    cotangent_ref,
    modulation_ref,
    rows_ref,
    factors_ref,
):
    rows = rows_ref.shape[1]
    first_row = (lax.axis_index("x") * 2 + lax.axis_index("core")) * rows
    first = block_index() * tokens_ref.shape[0] + first_row
    _, scale, gate = modulation_rows(counts_ref, modulation_ref, first, rows)
    at = pl.ds(pl.multiple_of(first_row, rows), rows)
    normed, inv_std = layer_norm(tokens_ref[at, :].astype(F32))
    rows_ref[0] = tokens_ref[at, :]
    rows_ref[1] = cotangent_ref[at, :]
    factors_ref[0] = gate
    factors_ref[1] = 1.0 + scale
    factors_ref[2] = normed
    factors_ref[3] = jnp.broadcast_to(inv_std, normed.shape)


def ready(counts, tokens, cotangent, modulation, share):
    width = tokens.shape[1]
    return pl.pallas_call(
        ready_kernel,
        out_shape=(
            jax.ShapeDtypeStruct((2, share, width), BF16),
            jax.ShapeDtypeStruct((4, share, width), F32),
        ),
        in_specs=[SMEM] + [VMEM] * 3,
        out_specs=(VMEM, VMEM),
        compiler_params=pltpu.CompilerParams(vmem_limit_bytes=VMEM_LIMIT),
    )(counts, tokens, cotangent, modulation)


def leave_kernel(rows_ref, factors_ref, shares_ref, layer_ref, grad_ref):
    width = layer_ref.shape[1]
    sums = shares_ref[0].astype(F32)
    for share in range(1, shares_ref.shape[0]):
        sums = sums + shares_ref[share].astype(F32)
    layer = rows_ref[0].astype(F32) + factors_ref[0] * sums[:, :width]
    layer_ref[...] = layer.astype(BF16)
    d_normed = sums[:, width:] * factors_ref[1]
    normed = factors_ref[2]
    input_grad = rows_ref[1].astype(F32) + factors_ref[3] * (
        d_normed
        - jnp.mean(d_normed, axis=-1, keepdims=True)
        - normed * jnp.mean(d_normed * normed, axis=-1, keepdims=True)
    )
    grad_ref[...] = input_grad.astype(BF16)


def leave(rows, factors, shares):
    out = jax.ShapeDtypeStruct(rows.shape[1:], BF16)
    return pl.pallas_call(
        leave_kernel,
        out_shape=(out, out),
        in_specs=[VMEM] * 3,
        out_specs=(VMEM, VMEM),
        compiler_params=pltpu.CompilerParams(vmem_limit_bytes=VMEM_LIMIT),
    )(rows, factors, shares)


def per_device(tokens, cotangent, w_qkv, w_out, qk_gain, modulation, image_counts):
    tok_rows, model_width = tokens.shape
    z_count = lax.axis_size("z")
    x_count = lax.axis_size("x")
    quad = 4
    pair_rows = 2 * tok_rows
    share = tok_rows // (2 * x_count)
    w_parts = w_qkv.transpose(1, 0, 2)
    mod_parts = modulation.transpose(1, 0, 2)

    heads, raw, raw_far = enter(
        image_counts, qk_gain, tokens, cotangent, w_parts, w_out, mod_parts, quad
    )
    mine = lax.all_to_all(heads, ("yh", "yl"), 0, 0)
    mine = mine.reshape(quad * tok_rows, 2 * LANES)
    evens = range(0, z_count, 2)
    swaps = [(i, i + 1) for i in evens], [((i - 1) % z_count, i) for i in evens]
    first, second = (
        lax.ppermute(mine, "z", pairs + [(j, i) for i, j in pairs]) for pairs in swaps
    )
    halves = 4 * z_count
    far_half = jnp.where(
        lax.axis_index("yh") == lax.axis_index("core"), mine[pair_rows:], mine[:pair_rows]
    )

    def far_source(target):
        z, yh, core = target // 4, target // 2 % 2, target % 2
        return (z + (2 if yh else -2)) % z_count * 4 + (yh ^ core) * 2 + core

    far = lax.ppermute(
        far_half, ("z", "yh", "core"), [(far_source(i), i) for i in range(halves)]
    )
    _, tokens_late, cotangent_late, mod_late = lax.optimization_barrier(
        (mine, tokens, cotangent, mod_parts)
    )
    rows, factors = ready(image_counts, tokens_late, cotangent_late, mod_late, share)
    near_parts = attend_near(image_counts, first, mine, second)
    _, w_parts_late, w_out_late = lax.optimization_barrier((mine, w_parts, w_out))
    weights = pack(w_parts_late, w_out_late, raw_far)
    weights_far = lax.ppermute(weights, "core", [(0, 1), (1, 0)])
    parts = attend_far(image_counts, far, near_parts)
    parts = lax.all_to_all(parts, ("yl", "core"), 0, 0)
    partial = project(parts, qk_gain, raw, weights, weights_far, x_count, model_width)
    shares = lax.all_to_all(partial, "x", 0, 0)
    return leave(rows, factors, shares)


def solution(mesh):
    split = jax.sharding.Mesh(mesh.devices.reshape(16, 2, 2, 4, 2), ("z", "yh", "yl", "x", "core"))
    dp, head = ("z", "yh", "yl"), ("x", "core")
    in_specs = (P(dp, None), P(dp, None), P(None, None, head), P(head, None), P(), P(), P())
    out_specs = (P(dp + head, None), P(dp + head, None))
    return jax.shard_map(
        per_device, mesh=split, in_specs=in_specs, out_specs=out_specs, check_vma=False
    )
```

```python
import math

import jax
import jax.numpy as jnp
from jax import lax
from jax.experimental import pallas as pl
from jax.experimental.pallas import tpu as pltpu
from jax.sharding import PartitionSpec as P

EPS = 1e-06
SAME_IMAGE = 512.0
LANES = 128
HEAD = 64
F32 = jnp.float32
BF16 = jnp.bfloat16
VMEM_LIMIT = 24 * 1024 * 1024
ENTER_LIMIT = 60 * 1024 * 1024
VMEM = pl.BlockSpec(memory_space=pltpu.VMEM)
SMEM = pl.BlockSpec(memory_space=pltpu.SMEM)


def rows_dot(a, b):
    return lax.dot_general(a, b, (((1,), (1,)), ((), ())), preferred_element_type=F32)


def block_index():
    return (lax.axis_index("z") * 2 + lax.axis_index("yh")) * 2 + lax.axis_index("yl")


def image_bounds(counts_ref, first_lane):
    lane = lax.broadcasted_iota(jnp.int32, (1, LANES), 1)
    starts = jnp.zeros((1, LANES), jnp.int32)
    ends = jnp.zeros((1, LANES), jnp.int32)
    total = jnp.int32(0)
    for image in range(counts_ref.shape[0]):
        here = lane == first_lane + image
        starts = jnp.where(here, total, starts)
        total = total + counts_ref[image]
        ends = jnp.where(here, total, ends)
    return starts, ends


def modulation_rows(counts_ref, modulation_ref, first, rows):
    starts, ends = image_bounds(counts_ref, 0)
    place = first + lax.broadcasted_iota(jnp.int32, (rows, LANES), 0)
    member = ((place >= starts) & (place < ends)).astype(F32).astype(BF16)
    member = member[:, : modulation_ref.shape[1]]
    return [
        jnp.dot(member, modulation_ref[part], preferred_element_type=F32) for part in range(3)
    ]


def layer_norm(values):
    average = jnp.mean(values, axis=-1, keepdims=True)
    centred = values - average
    inv_std = lax.rsqrt(jnp.mean(centred * centred, axis=-1, keepdims=True) + EPS)
    return centred * inv_std, inv_std


def enter_kernel(
    counts_ref,
    tokens_hbm,
    cotangent_hbm,
    w_qkv_hbm,
    w_out_hbm,
    modulation_hbm,
    out_ref,
    tokens_ref,
    cotangent_ref,
    w_qkv_ref,
    w_out_ref,
    modulation_ref,
    sems,
):
    pairs = [
        (tokens_hbm, tokens_ref),
        (modulation_hbm, modulation_ref),
        (cotangent_hbm, cotangent_ref),
        (w_out_hbm, w_out_ref),
        (w_qkv_hbm, w_qkv_ref),
    ]
    copies = [
        pltpu.make_async_copy(source, target, sems.at[place])
        for place, (source, target) in enumerate(pairs)
    ]
    for copy in copies:
        copy.start()
    rows = tokens_ref.shape[0]
    first = block_index() * rows
    copies[0].wait()
    normed, _ = layer_norm(tokens_ref[...].astype(F32))
    copies[1].wait()
    shift, scale, gate = modulation_rows(counts_ref, modulation_ref, first, rows)
    hidden = (normed * (1.0 + scale) + shift).astype(BF16)
    copies[2].wait()
    d_mixed = (cotangent_ref[...].astype(F32) * gate).astype(BF16)
    copies[3].wait()
    d_attn = rows_dot(d_mixed, w_out_ref[...])
    copies[4].wait()
    weights = jnp.concatenate([w_qkv_ref[part] for part in range(3)], axis=1)
    qkv = jnp.dot(hidden, weights, preferred_element_type=F32)
    q, k, v = (qkv[:, part * LANES : (part + 1) * LANES] for part in range(3))
    low = lax.broadcasted_iota(jnp.int32, (rows, LANES), 1) < HEAD

    def beside(left, right):
        return jnp.where(low, left, right).astype(BF16)

    q_v = (beside(q, pltpu.roll(v, HEAD, 1)), beside(pltpu.roll(q, HEAD, 1), v))
    k_d = (beside(k, pltpu.roll(d_attn, HEAD, 1)), beside(pltpu.roll(k, HEAD, 1), d_attn))
    for place in range(out_ref.shape[0]):
        out_ref[place, :, 0:LANES] = q_v[place % 2]
        out_ref[place, :, LANES:] = k_d[place % 2]


def enter(counts, tokens, cotangent, w_parts, w_out, modulation, quad):
    whole = pl.BlockSpec(memory_space=pl.ANY)
    operands = (tokens, cotangent, w_parts, w_out, modulation)
    return pl.pallas_call(
        enter_kernel,
        out_shape=jax.ShapeDtypeStruct((quad, tokens.shape[0], 2 * LANES), BF16),
        in_specs=[SMEM] + [whole] * 5,
        out_specs=VMEM,
        scratch_shapes=[pltpu.VMEM(operand.shape, BF16) for operand in operands]
        + [pltpu.SemaphoreType.DMA((5,))],
        compiler_params=pltpu.CompilerParams(vmem_limit_bytes=ENTER_LIMIT),
    )(counts, *operands)


def pack_kernel(w_qkv_ref, w_out_ref, weights_ref, sems):
    pairs = [(w_qkv_ref, weights_ref.at[0:3])]
    for tile in range(weights_ref.shape[1] // LANES):
        at = slice(tile * LANES, (tile + 1) * LANES)
        pairs.append((w_out_ref.at[:, at], weights_ref.at[3, at, :]))
    copies = [
        pltpu.make_async_copy(source, target, sems.at[place])
        for place, (source, target) in enumerate(pairs)
    ]
    for copy in copies:
        copy.start()
    for copy in copies:
        copy.wait()


def pack(w_parts, w_out):
    width = w_out.shape[1]
    whole = pl.BlockSpec(memory_space=pl.ANY)
    return pl.pallas_call(
        pack_kernel,
        out_shape=jax.ShapeDtypeStruct((4, width, LANES), BF16),
        in_specs=[whole] * 2,
        out_specs=VMEM,
        scratch_shapes=[pltpu.SemaphoreType.DMA((1 + width // LANES,))],
        compiler_params=pltpu.CompilerParams(vmem_limit_bytes=8 * 1024 * 1024),
    )(w_parts, w_out)


def w_out_of(weights_ref):
    tiles = weights_ref.shape[1] // LANES
    return jnp.concatenate(
        [weights_ref[3, tile * LANES : (tile + 1) * LANES, :] for tile in range(tiles)], axis=1
    )


LOG2_E = math.log2(math.e)
INV_ROOT = 1.0 / math.sqrt(HEAD)
CHUNK = 256
TILE = 64
MAIN = 6
REACH_CHUNKS = 4


def low_lanes():
    return lax.broadcasted_iota(jnp.int32, (1, LANES), 1) < HEAD


def lower_mean(values):
    return jnp.sum(jnp.where(low_lanes(), values, 0.0), axis=-1, keepdims=True) * (1.0 / HEAD)


def lower_sums(values):
    ones = (lax.broadcasted_iota(jnp.int32, (LANES, LANES), 0) < HEAD).astype(F32).astype(BF16)
    squares = values * values
    large = squares.astype(BF16)
    small = (squares - large.astype(F32)).astype(BF16)
    large = jnp.dot(large, ones, preferred_element_type=F32)
    return large + jnp.dot(small, ones, preferred_element_type=F32)


def place_block(source, place, starts, ends, gains_ref, stores):
    low = low_lanes()
    rows = source.shape[0]
    at = place + lax.broadcasted_iota(jnp.int32, (rows, LANES), 0)
    same = ((at >= starts) & (at < ends)).astype(F32)
    first = source[:, 0:LANES].astype(F32)
    second = source[:, LANES:].astype(F32)

    def normed(raw, gain):
        return raw * lax.rsqrt(lower_sums(raw) * (1.0 / HEAD) + EPS) * gain

    keys = normed(second, gains_ref[1:2, :])
    queries = normed(first, gains_ref[0:1, :] * INV_ROOT)
    q_store, k_store, v_store, d_store, kv_store = stores
    q_store[...] = jnp.where(low, queries, same * SAME_IMAGE).astype(BF16)
    k_store[...] = jnp.where(low, keys, same).astype(BF16)
    v_store[...] = jnp.where(low, 0.0, first).astype(BF16)
    d_store[...] = source[:, LANES:]
    kv_store[...] = jnp.where(low, keys, first).astype(BF16).T


def window_facts(counts_ref):
    half = lax.axis_index("yh")
    origin = (block_index() // 4 - 1) * 2 * CHUNK
    own_at = (2 + half) * CHUNK
    starts, ends = image_bounds(counts_ref, HEAD)
    left_from = jnp.int32(-CHUNK)
    right_to = jnp.int32((MAIN + 1) * CHUNK)
    total = -origin
    for image in range(counts_ref.shape[0]):
        left_from = jnp.where(total <= own_at, total, left_from)
        ended = total >= own_at + CHUNK
        total = total + counts_ref[image]
        right_to = jnp.where((total >= own_at + CHUNK) & jnp.logical_not(ended), total, right_to)
    return half, own_at, starts - origin, ends - origin, left_from, right_to


def by_eight(values):
    return values.reshape(values.shape[0] // 8, 8, values.shape[1])


def add_tiles(s_ref, g_ref, rows, highest, total, grads):
    for piece in range(rows // TILE):
        at = slice(piece * TILE, (piece + 1) * TILE)
        weights = jnp.exp2(s_ref[at, :] * LOG2_E - highest)
        total = total + jnp.sum(by_eight(weights), axis=0)
        grads = grads + jnp.sum(by_eight(weights * g_ref[at, :]), axis=0)
    return total, grads


def rows_max(values):
    return jnp.max(by_eight(values), axis=0)


def near_kernel(
    counts_ref,
    gains_ref,
    first_ref,
    quad_ref,
    second_ref,
    qx_ref,
    kx_ref,
    vx_ref,
    dx_ref,
    kv_ref,
    so_ref,
    go_ref,
    sn_ref,
    gn_ref,
    stats_ref,
    s_ref,
    g_ref,
):
    half, own_at, starts, ends, left_from, right_to = window_facts(counts_ref)
    block_rows = CHUNK // 2

    def place(source, begin):
        begin = pl.multiple_of(begin, block_rows)
        at = pl.ds(begin, block_rows)
        stores = [ref.at[at, :] for ref in (qx_ref, kx_ref, vx_ref, dx_ref)]
        place_block(source, begin, starts, ends, gains_ref, stores + [kv_ref.at[:, at]])

    to_first = jnp.where(lax.rem(lax.axis_index("z"), 2) == 0, 2 * CHUNK, -2 * CHUNK)
    for block in range(4):
        at = slice(block * block_rows, (block + 1) * block_rows)
        begin = 2 * CHUNK + block * block_rows
        place(quad_ref.at[at], begin)
        place(first_ref.at[at], begin + to_first)
        place(second_ref.at[at], begin - to_first)

    own_rows = pl.ds(pl.multiple_of(own_at, CHUNK), CHUNK)
    q_own = qx_ref[own_rows, :]
    d_own = dx_ref[own_rows, :]
    highest = jnp.full((8, CHUNK), -jnp.inf, F32)
    for piece in range(MAIN):
        at = slice(piece * CHUNK, (piece + 1) * CHUNK)
        scores = rows_dot(kx_ref[at, :], q_own)
        so_ref[at, :] = scores
        highest = jnp.maximum(highest, rows_max(scores))
        go_ref[at, :] = rows_dot(vx_ref[at, :], d_own)
    highest = jnp.max(highest, axis=0, keepdims=True) * LOG2_E
    total = jnp.zeros((8, CHUNK), F32)
    grads = jnp.zeros((8, CHUNK), F32)
    for piece in range(MAIN * CHUNK // TILE):
        at = slice(piece * TILE, (piece + 1) * TILE)
        weights = jnp.exp2(so_ref[at, :] * LOG2_E - highest)
        so_ref[at, :] = weights
        total = total + jnp.sum(by_eight(weights), axis=0)
        grads = grads + jnp.sum(by_eight(weights * go_ref[at, :]), axis=0)
    stats_ref[MAIN, 0:1, :] = highest
    stats_ref[MAIN, 1:2, :] = jnp.sum(total, axis=0, keepdims=True)
    stats_ref[MAIN, 2:3, :] = jnp.sum(grads, axis=0, keepdims=True)

    left_key = jnp.clip((left_from + CHUNK) // CHUNK - 1, 0, MAIN - REACH_CHUNKS)
    right_key = jnp.clip((right_to - 1) // CHUNK - (REACH_CHUNKS - 1), 0, MAIN - REACH_CHUNKS)

    def one_chunk(step, carry):
        slot = step + jnp.where(step >= 2 + half, 1, 0)
        begin = slot * CHUNK

        @pl.when((begin < right_to) & (begin + CHUNK > left_from))
        def _():
            at = pl.ds(pl.multiple_of(begin, CHUNK), CHUNK)
            key = jnp.where(begin < own_at, left_key, right_key) * CHUNK
            q_block = qx_ref[at, :]
            d_block = dx_ref[at, :]
            highest = jnp.full((8, CHUNK), -jnp.inf, F32)
            for piece in range(REACH_CHUNKS):
                keys_at = pl.ds(pl.multiple_of(key + piece * CHUNK, CHUNK), CHUNK)
                here = slice(piece * CHUNK, (piece + 1) * CHUNK)
                scores = rows_dot(kx_ref[keys_at, :], q_block)
                s_ref[here, :] = scores
                highest = jnp.maximum(highest, rows_max(scores))
                g_ref[here, :] = rows_dot(vx_ref[keys_at, :], d_block)
            highest = jnp.max(highest, axis=0, keepdims=True) * LOG2_E
            zeros = jnp.zeros((8, CHUNK), F32)
            total, grads = add_tiles(s_ref, g_ref, REACH_CHUNKS * CHUNK, highest, zeros, zeros)
            stats_ref[slot, 0:1, :] = highest
            stats_ref[slot, 1:2, :] = jnp.sum(total, axis=0, keepdims=True)
            stats_ref[slot, 2:3, :] = jnp.sum(grads, axis=0, keepdims=True)
            near_at = pl.ds(pl.multiple_of(own_at - key, CHUNK), CHUNK)
            sn_ref[slot, :, :] = s_ref[near_at, :]
            gn_ref[slot, :, :] = g_ref[near_at, :]

        return carry

    lax.fori_loop(0, MAIN - 1, one_chunk, 0)


def attend_near(counts, gains, first, quad, second):
    rows = MAIN * CHUNK
    head_rows = jax.ShapeDtypeStruct((rows, LANES), BF16)
    scores = jax.ShapeDtypeStruct((rows, CHUNK), F32)
    tiles = jax.ShapeDtypeStruct((MAIN, CHUNK, CHUNK), F32)
    return pl.pallas_call(
        near_kernel,
        out_shape=(head_rows,) * 4
        + (jax.ShapeDtypeStruct((LANES, rows), BF16),)
        + (scores, scores, tiles, tiles, jax.ShapeDtypeStruct((MAIN + 1, 8, CHUNK), F32)),
        in_specs=[SMEM] + [VMEM] * 4,
        out_specs=(VMEM,) * 10,
        scratch_shapes=[pltpu.VMEM((REACH_CHUNKS * CHUNK, CHUNK), F32)] * 2,
        cost_estimate=pl.CostEstimate(
            flops=9000000000, bytes_accessed=1 << 20, transcendentals=1 << 20
        ),
        compiler_params=pltpu.CompilerParams(vmem_limit_bytes=VMEM_LIMIT),
    )(counts, gains, first, quad, second)


def far_kernel(
    counts_ref,
    gains_ref,
    far_ref,
    quad_ref,
    qx_ref,
    kx_ref,
    vx_ref,
    dx_ref,
    kv_ref,
    so_ref,
    go_ref,
    sn_ref,
    gn_ref,
    stats_ref,
    out_ref,
    qf_ref,
    kf_ref,
    vf_ref,
    df_ref,
    kvf_ref,
    s_ref,
    g_ref,
    p_ref,
    d_ref,
    sums_ref,
    dk_ref,
    dv_ref,
    done_ref,
):
    half, own_at, starts, ends, left_from, right_to = window_facts(counts_ref)
    block_rows = CHUNK // 2
    rows = MAIN * CHUNK
    far_at = jnp.where(half == 0, -CHUNK, rows)
    for block in range(2):
        at = slice(block * block_rows, (block + 1) * block_rows)
        stores = [ref.at[at, :] for ref in (qf_ref, kf_ref, vf_ref, df_ref)]
        place_block(
            far_ref.at[at],
            far_at + block * block_rows,
            starts,
            ends,
            gains_ref,
            stores + [kvf_ref.at[:, at]],
        )

    own_rows = pl.ds(pl.multiple_of(own_at, CHUNK), CHUNK)
    q_own = qx_ref[own_rows, :]
    d_own = dx_ref[own_rows, :]
    scores = rows_dot(kf_ref[...], q_own)
    s_ref[0:CHUNK, :] = scores
    g_ref[0:CHUNK, :] = rows_dot(vf_ref[...], d_own)
    near_highest = stats_ref[MAIN, 0:1, :]
    highest = jnp.max(rows_max(scores), axis=0, keepdims=True) * LOG2_E
    highest = jnp.maximum(near_highest, highest)
    shrink = jnp.exp2(near_highest - highest)
    zeros = jnp.zeros((8, CHUNK), F32)
    total, grads = add_tiles(s_ref, g_ref, CHUNK, highest, zeros, zeros)
    total = jnp.sum(total, axis=0, keepdims=True) + stats_ref[MAIN, 1:2, :] * shrink
    grads = jnp.sum(grads, axis=0, keepdims=True) + stats_ref[MAIN, 2:3, :] * shrink
    scale = 1.0 / total
    mean_grad = grads * scale

    def write_tile(scores, grads, highest, scale, mean_grad, to):
        probs = jnp.exp2(scores * LOG2_E - highest) * scale
        p_ref[to, :] = probs.astype(BF16)
        d_ref[to, :] = (probs * (grads - mean_grad)).astype(BF16)

    near_scale = shrink * scale
    for piece in range(rows // TILE):
        at = slice(piece * TILE, (piece + 1) * TILE)
        probs = so_ref[at, :] * near_scale
        p_ref[at, :] = probs.astype(BF16)
        d_ref[at, :] = (probs * (go_ref[at, :] - mean_grad)).astype(BF16)
    for piece in range(CHUNK // TILE):
        at = slice(piece * TILE, (piece + 1) * TILE)
        to = slice(rows + piece * TILE, rows + (piece + 1) * TILE)
        write_tile(s_ref[at, :], g_ref[at, :], highest, scale, mean_grad, to)
    dk_ref[...] = jnp.dot(d_ref[own_rows, :], q_own, preferred_element_type=F32)
    dv_ref[...] = jnp.dot(p_ref[own_rows, :], d_own, preferred_element_type=F32)

    def times_window(values_ref):
        main = jnp.dot(kv_ref[...], values_ref[0:rows, :], preferred_element_type=F32)
        return main + jnp.dot(
            kvf_ref[...], values_ref[rows : rows + CHUNK, :], preferred_element_type=F32
        )

    upper = lax.broadcasted_iota(jnp.int32, (LANES, CHUNK), 0) < HEAD
    own_out = jnp.where(upper, times_window(d_ref) * INV_ROOT, times_window(p_ref)).T

    query_lane = lax.broadcasted_iota(jnp.int32, (1, CHUNK), 1)
    reaches_far = jnp.where(half == 0, left_from < 0, right_to > rows)

    def add_gradients(tiles, begin, q_block, d_block, highest, total, grads):
        place = query_lane + begin
        scale = jnp.where((place >= left_from) & (place < right_to), 1.0 / total, 0.0)
        mean_grad = grads * scale
        for piece in range(CHUNK // TILE):
            scores, given = tiles(piece)
            at = slice(piece * TILE, (piece + 1) * TILE)
            write_tile(scores, given, highest, scale, mean_grad, at)
        dk_ref[...] += jnp.dot(d_ref[0:CHUNK, :], q_block, preferred_element_type=F32)
        dv_ref[...] += jnp.dot(p_ref[0:CHUNK, :], d_block, preferred_element_type=F32)

    def one_chunk(step, carry):
        slot = step + jnp.where(step >= 2 + half, 1, 0)
        begin = slot * CHUNK

        @pl.when((begin < right_to) & (begin + CHUNK > left_from))
        def _():
            at = pl.ds(pl.multiple_of(begin, CHUNK), CHUNK)
            q_block = qx_ref[at, :]
            d_block = dx_ref[at, :]
            sums_ref[...] = stats_ref[slot, :, :]
            same_side = (begin < own_at) == (half == 0)

            @pl.when(reaches_far & same_side)
            def _():
                scores = rows_dot(kf_ref[...], q_block)
                s_ref[0:CHUNK, :] = scores
                g_ref[0:CHUNK, :] = rows_dot(vf_ref[...], d_block)
                before = sums_ref[0:1, :]
                highest = jnp.max(rows_max(scores), axis=0, keepdims=True) * LOG2_E
                highest = jnp.maximum(before, highest)
                total, grads = add_tiles(s_ref, g_ref, CHUNK, highest, zeros, zeros)
                shrink = jnp.exp2(before - highest)
                sums_ref[0:1, :] = highest
                total = jnp.sum(total, axis=0, keepdims=True)
                grads = jnp.sum(grads, axis=0, keepdims=True)
                sums_ref[1:2, :] = sums_ref[1:2, :] * shrink + total
                sums_ref[2:3, :] = sums_ref[2:3, :] * shrink + grads

            def tiles(piece):
                at = slice(piece * TILE, (piece + 1) * TILE)
                return sn_ref[slot, at, :], gn_ref[slot, at, :]

            add_gradients(
                tiles, begin, q_block, d_block, sums_ref[0:1, :], sums_ref[1:2, :], sums_ref[2:3, :]
            )

        return carry

    lax.fori_loop(0, MAIN - 1, one_chunk, 0)

    @pl.when(reaches_far)
    def _():
        q_block = qf_ref[...]
        d_block = df_ref[...]
        key = half * (MAIN // 2) * CHUNK
        highest = jnp.full((8, CHUNK), -jnp.inf, F32)
        for piece in range(REACH_CHUNKS):
            here = slice(piece * CHUNK, (piece + 1) * CHUNK)
            if piece < REACH_CHUNKS - 1:
                keys_at = pl.ds(pl.multiple_of(key + piece * CHUNK, CHUNK), CHUNK)
                keys, values = kx_ref[keys_at, :], vx_ref[keys_at, :]
            else:
                keys, values = kf_ref[...], vf_ref[...]
            scores = rows_dot(keys, q_block)
            s_ref[here, :] = scores
            highest = jnp.maximum(highest, rows_max(scores))
            g_ref[here, :] = rows_dot(values, d_block)
        highest = jnp.max(highest, axis=0, keepdims=True) * LOG2_E
        total, grads = add_tiles(s_ref, g_ref, REACH_CHUNKS * CHUNK, highest, zeros, zeros)

        def tiles(piece):
            at = pl.ds(pl.multiple_of(own_at - key + piece * TILE, TILE), TILE)
            return s_ref[at, :], g_ref[at, :]

        add_gradients(
            tiles,
            far_at,
            q_block,
            d_block,
            highest,
            jnp.sum(total, axis=0, keepdims=True),
            jnp.sum(grads, axis=0, keepdims=True),
        )

    def norm_grad(raw, gain, d_norm):
        inverse = lax.rsqrt(lower_mean(raw * raw) + EPS)
        scaled = d_norm.astype(BF16).astype(F32) * gain
        inner = lower_mean(raw * scaled)
        return inverse * scaled - raw * (inverse * inverse * inverse * inner)

    low = low_lanes()
    own_in_quad = pl.ds(pl.multiple_of(half * CHUNK, CHUNK), CHUNK)
    raw_q = quad_ref[own_in_quad, 0:LANES].astype(F32)
    raw_k = quad_ref[own_in_quad, LANES:].astype(F32)
    d_q = norm_grad(raw_q, gains_ref[0:1, :], own_out)
    d_k = norm_grad(raw_k, gains_ref[1:2, :], dk_ref[...])
    done_ref[:, 0:LANES] = jnp.where(low, d_q, own_out).astype(BF16)
    done_ref[:, LANES:] = jnp.where(low, d_k, dv_ref[...]).astype(BF16)
    share = 16
    for member in range(out_ref.shape[0]):
        block, core = member // 2, member % 2
        for part in range(out_ref.shape[1] // share):
            begin = (block * 8 + part * 2 + core) * share
            out_ref[member, part * share : (part + 1) * share, :] = done_ref[
                begin : begin + share, :
            ]


def attend_far(counts, gains, far, quad, near_parts):
    return pl.pallas_call(
        far_kernel,
        out_shape=jax.ShapeDtypeStruct((4, CHUNK // 4, 2 * LANES), BF16),
        in_specs=[SMEM] + [VMEM] * (3 + len(near_parts)),
        out_specs=VMEM,
        scratch_shapes=[pltpu.VMEM((CHUNK, LANES), BF16)] * 4
        + [pltpu.VMEM((LANES, CHUNK), BF16)]
        + [pltpu.VMEM((REACH_CHUNKS * CHUNK, CHUNK), F32)] * 2
        + [pltpu.VMEM(((MAIN + 1) * CHUNK, CHUNK), BF16)] * 2
        + [pltpu.VMEM((8, CHUNK), F32)]
        + [pltpu.VMEM((CHUNK, LANES), F32)] * 2
        + [pltpu.VMEM((CHUNK, 2 * LANES), BF16)],
        cost_estimate=pl.CostEstimate(
            flops=9000000000, bytes_accessed=1 << 20, transcendentals=1 << 20
        ),
        compiler_params=pltpu.CompilerParams(vmem_limit_bytes=VMEM_LIMIT),
    )(counts, gains, far, quad, *near_parts)


def project_kernel(parts_ref, weights_ref, weights_far_ref, out_ref):
    rows = parts_ref.shape[1]
    width = weights_ref.shape[1]
    share = out_ref.shape[1]
    core = lax.axis_index("core")
    low = lax.broadcasted_iota(jnp.int32, (rows, LANES), 1) < HEAD

    def by_column(which):
        head0 = parts_ref[which].astype(F32)
        head1 = parts_ref[2 + which].astype(F32)
        a0, a1 = head0[:, :LANES], head1[:, :LANES]
        b0, b1 = head0[:, LANES:], head1[:, LANES:]
        d_q = jnp.where(low, a0, pltpu.roll(a1, HEAD, 1)).astype(BF16)
        attn = jnp.where(low, pltpu.roll(a0, HEAD, 1), a1).astype(BF16)
        d_k = jnp.where(low, b0, pltpu.roll(b1, HEAD, 1)).astype(BF16)
        d_v = jnp.where(low, pltpu.roll(b0, HEAD, 1), b1).astype(BF16)
        return attn, [d_q, d_k, d_v]

    attn, grads = by_column(core)
    attn_far, grads_far = by_column(1 - core)
    mixed = jnp.dot(
        jnp.concatenate([attn, attn_far], axis=1),
        jnp.concatenate([w_out_of(weights_ref), w_out_of(weights_far_ref)], axis=0),
        preferred_element_type=F32,
    ).astype(BF16)
    weights = [ref[part] for ref in (weights_ref, weights_far_ref) for part in range(3)]
    d_hidden = rows_dot(
        jnp.concatenate(grads + grads_far, axis=1), jnp.concatenate(weights, axis=1)
    ).astype(BF16)
    for place in range(out_ref.shape[0]):
        at = slice(place * share, (place + 1) * share)
        out_ref[place, :, :width] = mixed[at]
        out_ref[place, :, width:] = d_hidden[at]


def project(parts, weights, weights_far, x_count):
    return pl.pallas_call(
        project_kernel,
        out_shape=jax.ShapeDtypeStruct(
            (x_count, parts.shape[1] // x_count, 2 * weights.shape[1]), BF16
        ),
        in_specs=[VMEM] * 3,
        out_specs=VMEM,
        compiler_params=pltpu.CompilerParams(vmem_limit_bytes=VMEM_LIMIT),
    )(parts, weights, weights_far)


def ready_kernel(
    counts_ref,
    tokens_ref,
    cotangent_ref,
    modulation_ref,
    rows_ref,
    factors_ref,
):
    rows = rows_ref.shape[1]
    first_row = (lax.axis_index("x") * 2 + lax.axis_index("core")) * rows
    first = block_index() * tokens_ref.shape[0] + first_row
    _, scale, gate = modulation_rows(counts_ref, modulation_ref, first, rows)
    at = pl.ds(pl.multiple_of(first_row, rows), rows)
    normed, inv_std = layer_norm(tokens_ref[at, :].astype(F32))
    rows_ref[0] = tokens_ref[at, :]
    rows_ref[1] = cotangent_ref[at, :]
    factors_ref[0] = gate
    factors_ref[1] = 1.0 + scale
    factors_ref[2] = normed
    factors_ref[3] = jnp.broadcast_to(inv_std, normed.shape)


def ready(counts, tokens, cotangent, modulation, share):
    width = tokens.shape[1]
    return pl.pallas_call(
        ready_kernel,
        out_shape=(
            jax.ShapeDtypeStruct((2, share, width), BF16),
            jax.ShapeDtypeStruct((4, share, width), F32),
        ),
        in_specs=[SMEM] + [VMEM] * 3,
        out_specs=(VMEM, VMEM),
        compiler_params=pltpu.CompilerParams(vmem_limit_bytes=VMEM_LIMIT),
    )(counts, tokens, cotangent, modulation)


def leave_kernel(rows_ref, factors_ref, shares_ref, layer_ref, grad_ref):
    width = layer_ref.shape[1]
    sums = shares_ref[0].astype(F32)
    for share in range(1, shares_ref.shape[0]):
        sums = sums + shares_ref[share].astype(F32)
    layer = rows_ref[0].astype(F32) + factors_ref[0] * sums[:, :width]
    layer_ref[...] = layer.astype(BF16)
    d_normed = sums[:, width:] * factors_ref[1]
    normed = factors_ref[2]
    input_grad = rows_ref[1].astype(F32) + factors_ref[3] * (
        d_normed
        - jnp.mean(d_normed, axis=-1, keepdims=True)
        - normed * jnp.mean(d_normed * normed, axis=-1, keepdims=True)
    )
    grad_ref[...] = input_grad.astype(BF16)


def leave(rows, factors, shares):
    out = jax.ShapeDtypeStruct(rows.shape[1:], BF16)
    return pl.pallas_call(
        leave_kernel,
        out_shape=(out, out),
        in_specs=[VMEM] * 3,
        out_specs=(VMEM, VMEM),
        compiler_params=pltpu.CompilerParams(vmem_limit_bytes=VMEM_LIMIT),
    )(rows, factors, shares)


def per_device(tokens, cotangent, w_qkv, w_out, qk_gain, modulation, image_counts):
    tok_rows, model_width = tokens.shape
    z_count = lax.axis_size("z")
    x_count = lax.axis_size("x")
    quad = 4
    pair_rows = 2 * tok_rows
    share = tok_rows // (2 * x_count)
    w_parts = w_qkv.transpose(1, 0, 2)
    mod_parts = modulation.transpose(1, 0, 2)
    gains = jnp.pad(qk_gain, ((0, 6), (0, LANES - HEAD)))

    heads = enter(image_counts, tokens, cotangent, w_parts, w_out, mod_parts, quad)
    mine = lax.all_to_all(heads, ("yh", "yl"), 0, 0)
    mine = mine.reshape(quad * tok_rows, 2 * LANES)
    evens = range(0, z_count, 2)
    swaps = [(i, i + 1) for i in evens], [((i - 1) % z_count, i) for i in evens]
    first, second = (
        lax.ppermute(mine, "z", pairs + [(j, i) for i, j in pairs]) for pairs in swaps
    )
    halves = 4 * z_count
    far_half = jnp.where(
        lax.axis_index("yh") == lax.axis_index("core"), mine[pair_rows:], mine[:pair_rows]
    )

    def far_source(target):
        z, yh, core = target // 4, target // 2 % 2, target % 2
        return (z + (2 if yh else -2)) % z_count * 4 + (yh ^ core) * 2 + core

    far = lax.ppermute(
        far_half, ("z", "yh", "core"), [(far_source(i), i) for i in range(halves)]
    )
    _, tokens_late, cotangent_late, mod_late = lax.optimization_barrier(
        (mine, tokens, cotangent, mod_parts)
    )
    rows, factors = ready(image_counts, tokens_late, cotangent_late, mod_late, share)
    near_parts = attend_near(image_counts, gains, first, mine, second)
    _, w_parts_late, w_out_late = lax.optimization_barrier((mine, w_parts, w_out))
    weights = pack(w_parts_late, w_out_late)
    weights_far = lax.ppermute(weights, "core", [(0, 1), (1, 0)])
    parts = attend_far(image_counts, gains, far, mine, near_parts)
    parts = lax.all_to_all(parts, ("yl", "core"), 0, 0)
    partial = project(parts, weights, weights_far, x_count)
    shares = lax.all_to_all(partial, "x", 0, 0)
    return leave(rows, factors, shares)


def solution(mesh):
    split = jax.sharding.Mesh(mesh.devices.reshape(16, 2, 2, 4, 2), ("z", "yh", "yl", "x", "core"))
    dp, head = ("z", "yh", "yl"), ("x", "core")
    in_specs = (P(dp, None), P(dp, None), P(None, None, head), P(head, None), P(), P(), P())
    out_specs = (P(dp + head, None), P(dp + head, None))
    return jax.shard_map(
        per_device, mesh=split, in_specs=in_specs, out_specs=out_specs, check_vma=False
    )
```

```python
import math

import jax
import jax.numpy as jnp
from jax import lax
from jax.experimental import pallas as pl
from jax.experimental.pallas import tpu as pltpu
from jax.sharding import PartitionSpec as P

EPS = 1e-06
SAME_IMAGE = 512.0
LANES = 128
HEAD = 64
F32 = jnp.float32
BF16 = jnp.bfloat16
VMEM_LIMIT = 24 * 1024 * 1024
ENTER_LIMIT = 60 * 1024 * 1024
VMEM = pl.BlockSpec(memory_space=pltpu.VMEM)
SMEM = pl.BlockSpec(memory_space=pltpu.SMEM)


def rows_dot(a, b):
    return lax.dot_general(a, b, (((1,), (1,)), ((), ())), preferred_element_type=F32)


def block_index():
    return (lax.axis_index("z") * 2 + lax.axis_index("yh")) * 2 + lax.axis_index("yl")


def image_bounds(counts_ref, first_lane):
    lane = lax.broadcasted_iota(jnp.int32, (1, LANES), 1)
    starts = jnp.zeros((1, LANES), jnp.int32)
    ends = jnp.zeros((1, LANES), jnp.int32)
    total = jnp.int32(0)
    for image in range(counts_ref.shape[0]):
        here = lane == first_lane + image
        starts = jnp.where(here, total, starts)
        total = total + counts_ref[image]
        ends = jnp.where(here, total, ends)
    return starts, ends


def modulation_rows(counts_ref, modulation_ref, first, rows):
    starts, ends = image_bounds(counts_ref, 0)
    place = first + lax.broadcasted_iota(jnp.int32, (rows, LANES), 0)
    member = ((place >= starts) & (place < ends)).astype(F32).astype(BF16)
    member = member[:, : modulation_ref.shape[1]]
    return [
        jnp.dot(member, modulation_ref[part], preferred_element_type=F32) for part in range(3)
    ]


def layer_norm(values):
    average = jnp.mean(values, axis=-1, keepdims=True)
    centred = values - average
    inv_std = lax.rsqrt(jnp.mean(centred * centred, axis=-1, keepdims=True) + EPS)
    return centred * inv_std, inv_std


def enter_kernel(
    counts_ref, tokens_ref, cotangent_ref, w_qkv_ref, w_out_ref, modulation_ref, out_ref
):
    rows = tokens_ref.shape[0]
    first = block_index() * rows
    shift, scale, gate = modulation_rows(counts_ref, modulation_ref, first, rows)
    normed, _ = layer_norm(tokens_ref[...].astype(F32))
    hidden = (normed * (1.0 + scale) + shift).astype(BF16)
    weights = jnp.concatenate([w_qkv_ref[part] for part in range(3)], axis=1)
    qkv = jnp.dot(hidden, weights, preferred_element_type=F32)
    q, k, v = (qkv[:, part * LANES : (part + 1) * LANES] for part in range(3))
    d_mixed = (cotangent_ref[...].astype(F32) * gate).astype(BF16)
    d_attn = rows_dot(d_mixed, w_out_ref[...])
    low = lax.broadcasted_iota(jnp.int32, (rows, LANES), 1) < HEAD

    def beside(left, right):
        return jnp.where(low, left, right).astype(BF16)

    q_v = (beside(q, pltpu.roll(v, HEAD, 1)), beside(pltpu.roll(q, HEAD, 1), v))
    k_d = (beside(k, pltpu.roll(d_attn, HEAD, 1)), beside(pltpu.roll(k, HEAD, 1), d_attn))
    for place in range(out_ref.shape[0]):
        out_ref[place, :, 0:LANES] = q_v[place % 2]
        out_ref[place, :, LANES:] = k_d[place % 2]


def enter(counts, tokens, cotangent, w_parts, w_out, modulation, quad):
    return pl.pallas_call(
        enter_kernel,
        out_shape=jax.ShapeDtypeStruct((quad, tokens.shape[0], 2 * LANES), BF16),
        in_specs=[SMEM] + [VMEM] * 5,
        out_specs=VMEM,
        compiler_params=pltpu.CompilerParams(vmem_limit_bytes=ENTER_LIMIT),
    )(counts, tokens, cotangent, w_parts, w_out, modulation)


def pack_kernel(w_qkv_ref, w_out_ref, weights_ref, sems):
    pairs = [(w_qkv_ref, weights_ref.at[0:3])]
    for tile in range(weights_ref.shape[1] // LANES):
        at = slice(tile * LANES, (tile + 1) * LANES)
        pairs.append((w_out_ref.at[:, at], weights_ref.at[3, at, :]))
    copies = [
        pltpu.make_async_copy(source, target, sems.at[place])
        for place, (source, target) in enumerate(pairs)
    ]
    for copy in copies:
        copy.start()
    for copy in copies:
        copy.wait()


def pack(w_parts, w_out):
    width = w_out.shape[1]
    whole = pl.BlockSpec(memory_space=pl.ANY)
    return pl.pallas_call(
        pack_kernel,
        out_shape=jax.ShapeDtypeStruct((4, width, LANES), BF16),
        in_specs=[whole] * 2,
        out_specs=VMEM,
        scratch_shapes=[pltpu.SemaphoreType.DMA((1 + width // LANES,))],
        compiler_params=pltpu.CompilerParams(vmem_limit_bytes=8 * 1024 * 1024),
    )(w_parts, w_out)


def w_out_of(weights_ref):
    tiles = weights_ref.shape[1] // LANES
    return jnp.concatenate(
        [weights_ref[3, tile * LANES : (tile + 1) * LANES, :] for tile in range(tiles)], axis=1
    )


LOG2_E = math.log2(math.e)
INV_ROOT = 1.0 / math.sqrt(HEAD)
CHUNK = 256
TILE = 64
MAIN = 6
REACH_CHUNKS = 4


def low_lanes():
    return lax.broadcasted_iota(jnp.int32, (1, LANES), 1) < HEAD


def lower_mean(values):
    return jnp.sum(jnp.where(low_lanes(), values, 0.0), axis=-1, keepdims=True) * (1.0 / HEAD)


def lower_sums(values):
    ones = (lax.broadcasted_iota(jnp.int32, (LANES, LANES), 0) < HEAD).astype(F32).astype(BF16)
    squares = values * values
    large = squares.astype(BF16)
    small = (squares - large.astype(F32)).astype(BF16)
    large = jnp.dot(large, ones, preferred_element_type=F32)
    return large + jnp.dot(small, ones, preferred_element_type=F32)


def place_block(source, place, starts, ends, gains_ref, stores):
    low = low_lanes()
    rows = source.shape[0]
    at = place + lax.broadcasted_iota(jnp.int32, (rows, LANES), 0)
    same = ((at >= starts) & (at < ends)).astype(F32)
    first = source[:, 0:LANES].astype(F32)
    second = source[:, LANES:].astype(F32)

    def normed(raw, gain):
        return raw * lax.rsqrt(lower_sums(raw) * (1.0 / HEAD) + EPS) * gain

    keys = normed(second, gains_ref[1:2, :])
    queries = normed(first, gains_ref[0:1, :] * INV_ROOT)
    q_store, k_store, v_store, d_store, kv_store = stores
    q_store[...] = jnp.where(low, queries, same * SAME_IMAGE).astype(BF16)
    k_store[...] = jnp.where(low, keys, same).astype(BF16)
    v_store[...] = jnp.where(low, 0.0, first).astype(BF16)
    d_store[...] = source[:, LANES:]
    kv_store[...] = jnp.where(low, keys, first).astype(BF16).T


def window_facts(counts_ref):
    half = lax.axis_index("yh")
    origin = (block_index() // 4 - 1) * 2 * CHUNK
    own_at = (2 + half) * CHUNK
    starts, ends = image_bounds(counts_ref, HEAD)
    left_from = jnp.int32(-CHUNK)
    right_to = jnp.int32((MAIN + 1) * CHUNK)
    total = -origin
    for image in range(counts_ref.shape[0]):
        left_from = jnp.where(total <= own_at, total, left_from)
        ended = total >= own_at + CHUNK
        total = total + counts_ref[image]
        right_to = jnp.where((total >= own_at + CHUNK) & jnp.logical_not(ended), total, right_to)
    return half, own_at, starts - origin, ends - origin, left_from, right_to


def by_eight(values):
    return values.reshape(values.shape[0] // 8, 8, values.shape[1])


def add_tiles(s_ref, g_ref, rows, highest, total, grads):
    for piece in range(rows // TILE):
        at = slice(piece * TILE, (piece + 1) * TILE)
        weights = jnp.exp2(s_ref[at, :] * LOG2_E - highest)
        total = total + jnp.sum(by_eight(weights), axis=0)
        grads = grads + jnp.sum(by_eight(weights * g_ref[at, :]), axis=0)
    return total, grads


def rows_max(values):
    return jnp.max(by_eight(values), axis=0)


def near_kernel(
    counts_ref,
    gains_ref,
    first_ref,
    quad_ref,
    second_ref,
    qx_ref,
    kx_ref,
    vx_ref,
    dx_ref,
    kv_ref,
    so_ref,
    go_ref,
    sn_ref,
    gn_ref,
    stats_ref,
    s_ref,
    g_ref,
):
    half, own_at, starts, ends, left_from, right_to = window_facts(counts_ref)
    block_rows = CHUNK // 2

    def place(source, begin):
        begin = pl.multiple_of(begin, block_rows)
        at = pl.ds(begin, block_rows)
        stores = [ref.at[at, :] for ref in (qx_ref, kx_ref, vx_ref, dx_ref)]
        place_block(source, begin, starts, ends, gains_ref, stores + [kv_ref.at[:, at]])

    to_first = jnp.where(lax.rem(lax.axis_index("z"), 2) == 0, 2 * CHUNK, -2 * CHUNK)
    for block in range(4):
        at = slice(block * block_rows, (block + 1) * block_rows)
        begin = 2 * CHUNK + block * block_rows
        place(quad_ref.at[at], begin)
        place(first_ref.at[at], begin + to_first)
        place(second_ref.at[at], begin - to_first)

    own_rows = pl.ds(pl.multiple_of(own_at, CHUNK), CHUNK)
    q_own = qx_ref[own_rows, :]
    d_own = dx_ref[own_rows, :]
    highest = jnp.full((8, CHUNK), -jnp.inf, F32)
    for piece in range(MAIN):
        at = slice(piece * CHUNK, (piece + 1) * CHUNK)
        scores = rows_dot(kx_ref[at, :], q_own)
        so_ref[at, :] = scores
        highest = jnp.maximum(highest, rows_max(scores))
        go_ref[at, :] = rows_dot(vx_ref[at, :], d_own)
    highest = jnp.max(highest, axis=0, keepdims=True) * LOG2_E
    total = jnp.zeros((8, CHUNK), F32)
    grads = jnp.zeros((8, CHUNK), F32)
    for piece in range(MAIN * CHUNK // TILE):
        at = slice(piece * TILE, (piece + 1) * TILE)
        weights = jnp.exp2(so_ref[at, :] * LOG2_E - highest)
        so_ref[at, :] = weights
        total = total + jnp.sum(by_eight(weights), axis=0)
        grads = grads + jnp.sum(by_eight(weights * go_ref[at, :]), axis=0)
    stats_ref[MAIN, 0:1, :] = highest
    stats_ref[MAIN, 1:2, :] = jnp.sum(total, axis=0, keepdims=True)
    stats_ref[MAIN, 2:3, :] = jnp.sum(grads, axis=0, keepdims=True)

    left_key = jnp.clip((left_from + CHUNK) // CHUNK - 1, 0, MAIN - REACH_CHUNKS)
    right_key = jnp.clip((right_to - 1) // CHUNK - (REACH_CHUNKS - 1), 0, MAIN - REACH_CHUNKS)

    def one_chunk(step, carry):
        slot = step + jnp.where(step >= 2 + half, 1, 0)
        begin = slot * CHUNK

        @pl.when((begin < right_to) & (begin + CHUNK > left_from))
        def _():
            at = pl.ds(pl.multiple_of(begin, CHUNK), CHUNK)
            key = jnp.where(begin < own_at, left_key, right_key) * CHUNK
            q_block = qx_ref[at, :]
            d_block = dx_ref[at, :]
            highest = jnp.full((8, CHUNK), -jnp.inf, F32)
            for piece in range(REACH_CHUNKS):
                keys_at = pl.ds(pl.multiple_of(key + piece * CHUNK, CHUNK), CHUNK)
                here = slice(piece * CHUNK, (piece + 1) * CHUNK)
                scores = rows_dot(kx_ref[keys_at, :], q_block)
                s_ref[here, :] = scores
                highest = jnp.maximum(highest, rows_max(scores))
                g_ref[here, :] = rows_dot(vx_ref[keys_at, :], d_block)
            highest = jnp.max(highest, axis=0, keepdims=True) * LOG2_E
            zeros = jnp.zeros((8, CHUNK), F32)
            total, grads = add_tiles(s_ref, g_ref, REACH_CHUNKS * CHUNK, highest, zeros, zeros)
            stats_ref[slot, 0:1, :] = highest
            stats_ref[slot, 1:2, :] = jnp.sum(total, axis=0, keepdims=True)
            stats_ref[slot, 2:3, :] = jnp.sum(grads, axis=0, keepdims=True)
            near_at = pl.ds(pl.multiple_of(own_at - key, CHUNK), CHUNK)
            sn_ref[slot, :, :] = s_ref[near_at, :]
            gn_ref[slot, :, :] = g_ref[near_at, :]

        return carry

    lax.fori_loop(0, MAIN - 1, one_chunk, 0)


def attend_near(counts, gains, first, quad, second):
    rows = MAIN * CHUNK
    head_rows = jax.ShapeDtypeStruct((rows, LANES), BF16)
    scores = jax.ShapeDtypeStruct((rows, CHUNK), F32)
    tiles = jax.ShapeDtypeStruct((MAIN, CHUNK, CHUNK), F32)
    return pl.pallas_call(
        near_kernel,
        out_shape=(head_rows,) * 4
        + (jax.ShapeDtypeStruct((LANES, rows), BF16),)
        + (scores, scores, tiles, tiles, jax.ShapeDtypeStruct((MAIN + 1, 8, CHUNK), F32)),
        in_specs=[SMEM] + [VMEM] * 4,
        out_specs=(VMEM,) * 10,
        scratch_shapes=[pltpu.VMEM((REACH_CHUNKS * CHUNK, CHUNK), F32)] * 2,
        cost_estimate=pl.CostEstimate(
            flops=8000000000, bytes_accessed=1 << 20, transcendentals=1 << 20
        ),
        compiler_params=pltpu.CompilerParams(vmem_limit_bytes=VMEM_LIMIT),
    )(counts, gains, first, quad, second)


def far_kernel(
    counts_ref,
    gains_ref,
    far_ref,
    quad_ref,
    qx_ref,
    kx_ref,
    vx_ref,
    dx_ref,
    kv_ref,
    so_ref,
    go_ref,
    sn_ref,
    gn_ref,
    stats_ref,
    out_ref,
    qf_ref,
    kf_ref,
    vf_ref,
    df_ref,
    kvf_ref,
    s_ref,
    g_ref,
    p_ref,
    d_ref,
    sums_ref,
    dk_ref,
    dv_ref,
    done_ref,
):
    half, own_at, starts, ends, left_from, right_to = window_facts(counts_ref)
    block_rows = CHUNK // 2
    rows = MAIN * CHUNK
    far_at = jnp.where(half == 0, -CHUNK, rows)
    for block in range(2):
        at = slice(block * block_rows, (block + 1) * block_rows)
        stores = [ref.at[at, :] for ref in (qf_ref, kf_ref, vf_ref, df_ref)]
        place_block(
            far_ref.at[at],
            far_at + block * block_rows,
            starts,
            ends,
            gains_ref,
            stores + [kvf_ref.at[:, at]],
        )

    own_rows = pl.ds(pl.multiple_of(own_at, CHUNK), CHUNK)
    q_own = qx_ref[own_rows, :]
    d_own = dx_ref[own_rows, :]
    scores = rows_dot(kf_ref[...], q_own)
    s_ref[0:CHUNK, :] = scores
    g_ref[0:CHUNK, :] = rows_dot(vf_ref[...], d_own)
    near_highest = stats_ref[MAIN, 0:1, :]
    highest = jnp.max(rows_max(scores), axis=0, keepdims=True) * LOG2_E
    highest = jnp.maximum(near_highest, highest)
    shrink = jnp.exp2(near_highest - highest)
    zeros = jnp.zeros((8, CHUNK), F32)
    total, grads = add_tiles(s_ref, g_ref, CHUNK, highest, zeros, zeros)
    total = jnp.sum(total, axis=0, keepdims=True) + stats_ref[MAIN, 1:2, :] * shrink
    grads = jnp.sum(grads, axis=0, keepdims=True) + stats_ref[MAIN, 2:3, :] * shrink
    scale = 1.0 / total
    mean_grad = grads * scale

    def write_tile(scores, grads, highest, scale, mean_grad, to):
        probs = jnp.exp2(scores * LOG2_E - highest) * scale
        p_ref[to, :] = probs.astype(BF16)
        d_ref[to, :] = (probs * (grads - mean_grad)).astype(BF16)

    near_scale = shrink * scale
    for piece in range(rows // TILE):
        at = slice(piece * TILE, (piece + 1) * TILE)
        probs = so_ref[at, :] * near_scale
        p_ref[at, :] = probs.astype(BF16)
        d_ref[at, :] = (probs * (go_ref[at, :] - mean_grad)).astype(BF16)
    for piece in range(CHUNK // TILE):
        at = slice(piece * TILE, (piece + 1) * TILE)
        to = slice(rows + piece * TILE, rows + (piece + 1) * TILE)
        write_tile(s_ref[at, :], g_ref[at, :], highest, scale, mean_grad, to)
    dk_ref[...] = jnp.dot(d_ref[own_rows, :], q_own, preferred_element_type=F32)
    dv_ref[...] = jnp.dot(p_ref[own_rows, :], d_own, preferred_element_type=F32)

    def times_window(values_ref):
        main = jnp.dot(kv_ref[...], values_ref[0:rows, :], preferred_element_type=F32)
        return main + jnp.dot(
            kvf_ref[...], values_ref[rows : rows + CHUNK, :], preferred_element_type=F32
        )

    upper = lax.broadcasted_iota(jnp.int32, (LANES, CHUNK), 0) < HEAD
    own_out = jnp.where(upper, times_window(d_ref) * INV_ROOT, times_window(p_ref)).T

    query_lane = lax.broadcasted_iota(jnp.int32, (1, CHUNK), 1)
    reaches_far = jnp.where(half == 0, left_from < 0, right_to > rows)

    def add_gradients(tiles, begin, q_block, d_block, highest, total, grads):
        place = query_lane + begin
        scale = jnp.where((place >= left_from) & (place < right_to), 1.0 / total, 0.0)
        mean_grad = grads * scale
        for piece in range(CHUNK // TILE):
            scores, given = tiles(piece)
            at = slice(piece * TILE, (piece + 1) * TILE)
            write_tile(scores, given, highest, scale, mean_grad, at)
        dk_ref[...] += jnp.dot(d_ref[0:CHUNK, :], q_block, preferred_element_type=F32)
        dv_ref[...] += jnp.dot(p_ref[0:CHUNK, :], d_block, preferred_element_type=F32)

    def one_chunk(step, carry):
        slot = step + jnp.where(step >= 2 + half, 1, 0)
        begin = slot * CHUNK

        @pl.when((begin < right_to) & (begin + CHUNK > left_from))
        def _():
            at = pl.ds(pl.multiple_of(begin, CHUNK), CHUNK)
            q_block = qx_ref[at, :]
            d_block = dx_ref[at, :]
            sums_ref[...] = stats_ref[slot, :, :]
            same_side = (begin < own_at) == (half == 0)

            @pl.when(reaches_far & same_side)
            def _():
                scores = rows_dot(kf_ref[...], q_block)
                s_ref[0:CHUNK, :] = scores
                g_ref[0:CHUNK, :] = rows_dot(vf_ref[...], d_block)
                before = sums_ref[0:1, :]
                highest = jnp.max(rows_max(scores), axis=0, keepdims=True) * LOG2_E
                highest = jnp.maximum(before, highest)
                total, grads = add_tiles(s_ref, g_ref, CHUNK, highest, zeros, zeros)
                shrink = jnp.exp2(before - highest)
                sums_ref[0:1, :] = highest
                total = jnp.sum(total, axis=0, keepdims=True)
                grads = jnp.sum(grads, axis=0, keepdims=True)
                sums_ref[1:2, :] = sums_ref[1:2, :] * shrink + total
                sums_ref[2:3, :] = sums_ref[2:3, :] * shrink + grads

            def tiles(piece):
                at = slice(piece * TILE, (piece + 1) * TILE)
                return sn_ref[slot, at, :], gn_ref[slot, at, :]

            add_gradients(
                tiles, begin, q_block, d_block, sums_ref[0:1, :], sums_ref[1:2, :], sums_ref[2:3, :]
            )

        return carry

    lax.fori_loop(0, MAIN - 1, one_chunk, 0)

    @pl.when(reaches_far)
    def _():
        q_block = qf_ref[...]
        d_block = df_ref[...]
        key = half * (MAIN // 2) * CHUNK
        highest = jnp.full((8, CHUNK), -jnp.inf, F32)
        for piece in range(REACH_CHUNKS):
            here = slice(piece * CHUNK, (piece + 1) * CHUNK)
            if piece < REACH_CHUNKS - 1:
                keys_at = pl.ds(pl.multiple_of(key + piece * CHUNK, CHUNK), CHUNK)
                keys, values = kx_ref[keys_at, :], vx_ref[keys_at, :]
            else:
                keys, values = kf_ref[...], vf_ref[...]
            scores = rows_dot(keys, q_block)
            s_ref[here, :] = scores
            highest = jnp.maximum(highest, rows_max(scores))
            g_ref[here, :] = rows_dot(values, d_block)
        highest = jnp.max(highest, axis=0, keepdims=True) * LOG2_E
        total, grads = add_tiles(s_ref, g_ref, REACH_CHUNKS * CHUNK, highest, zeros, zeros)

        def tiles(piece):
            at = pl.ds(pl.multiple_of(own_at - key + piece * TILE, TILE), TILE)
            return s_ref[at, :], g_ref[at, :]

        add_gradients(
            tiles,
            far_at,
            q_block,
            d_block,
            highest,
            jnp.sum(total, axis=0, keepdims=True),
            jnp.sum(grads, axis=0, keepdims=True),
        )

    def norm_grad(raw, gain, d_norm):
        inverse = lax.rsqrt(lower_mean(raw * raw) + EPS)
        scaled = d_norm.astype(BF16).astype(F32) * gain
        inner = lower_mean(raw * scaled)
        return inverse * scaled - raw * (inverse * inverse * inverse * inner)

    low = low_lanes()
    own_in_quad = pl.ds(pl.multiple_of(half * CHUNK, CHUNK), CHUNK)
    raw_q = quad_ref[own_in_quad, 0:LANES].astype(F32)
    raw_k = quad_ref[own_in_quad, LANES:].astype(F32)
    d_q = norm_grad(raw_q, gains_ref[0:1, :], own_out)
    d_k = norm_grad(raw_k, gains_ref[1:2, :], dk_ref[...])
    done_ref[:, 0:LANES] = jnp.where(low, d_q, own_out).astype(BF16)
    done_ref[:, LANES:] = jnp.where(low, d_k, dv_ref[...]).astype(BF16)
    share = 16
    for member in range(out_ref.shape[0]):
        block, core = member // 2, member % 2
        for part in range(out_ref.shape[1] // share):
            begin = (block * 8 + part * 2 + core) * share
            out_ref[member, part * share : (part + 1) * share, :] = done_ref[
                begin : begin + share, :
            ]


def attend_far(counts, gains, far, quad, near_parts):
    return pl.pallas_call(
        far_kernel,
        out_shape=jax.ShapeDtypeStruct((4, CHUNK // 4, 2 * LANES), BF16),
        in_specs=[SMEM] + [VMEM] * (3 + len(near_parts)),
        out_specs=VMEM,
        scratch_shapes=[pltpu.VMEM((CHUNK, LANES), BF16)] * 4
        + [pltpu.VMEM((LANES, CHUNK), BF16)]
        + [pltpu.VMEM((REACH_CHUNKS * CHUNK, CHUNK), F32)] * 2
        + [pltpu.VMEM(((MAIN + 1) * CHUNK, CHUNK), BF16)] * 2
        + [pltpu.VMEM((8, CHUNK), F32)]
        + [pltpu.VMEM((CHUNK, LANES), F32)] * 2
        + [pltpu.VMEM((CHUNK, 2 * LANES), BF16)],
        cost_estimate=pl.CostEstimate(
            flops=8000000000, bytes_accessed=1 << 20, transcendentals=1 << 20
        ),
        compiler_params=pltpu.CompilerParams(vmem_limit_bytes=VMEM_LIMIT),
    )(counts, gains, far, quad, *near_parts)


def project_kernel(parts_ref, weights_ref, weights_far_ref, out_ref):
    rows = parts_ref.shape[1]
    width = weights_ref.shape[1]
    share = out_ref.shape[1]
    core = lax.axis_index("core")
    low = lax.broadcasted_iota(jnp.int32, (rows, LANES), 1) < HEAD

    def by_column(which):
        head0 = parts_ref[which].astype(F32)
        head1 = parts_ref[2 + which].astype(F32)
        a0, a1 = head0[:, :LANES], head1[:, :LANES]
        b0, b1 = head0[:, LANES:], head1[:, LANES:]
        d_q = jnp.where(low, a0, pltpu.roll(a1, HEAD, 1)).astype(BF16)
        attn = jnp.where(low, pltpu.roll(a0, HEAD, 1), a1).astype(BF16)
        d_k = jnp.where(low, b0, pltpu.roll(b1, HEAD, 1)).astype(BF16)
        d_v = jnp.where(low, pltpu.roll(b0, HEAD, 1), b1).astype(BF16)
        return attn, [d_q, d_k, d_v]

    attn, grads = by_column(core)
    attn_far, grads_far = by_column(1 - core)
    mixed = jnp.dot(
        jnp.concatenate([attn, attn_far], axis=1),
        jnp.concatenate([w_out_of(weights_ref), w_out_of(weights_far_ref)], axis=0),
        preferred_element_type=F32,
    ).astype(BF16)
    weights = [ref[part] for ref in (weights_ref, weights_far_ref) for part in range(3)]
    d_hidden = rows_dot(
        jnp.concatenate(grads + grads_far, axis=1), jnp.concatenate(weights, axis=1)
    ).astype(BF16)
    for place in range(out_ref.shape[0]):
        at = slice(place * share, (place + 1) * share)
        out_ref[place, :, :width] = mixed[at]
        out_ref[place, :, width:] = d_hidden[at]


def project(parts, weights, weights_far, x_count):
    return pl.pallas_call(
        project_kernel,
        out_shape=jax.ShapeDtypeStruct(
            (x_count, parts.shape[1] // x_count, 2 * weights.shape[1]), BF16
        ),
        in_specs=[VMEM] * 3,
        out_specs=VMEM,
        compiler_params=pltpu.CompilerParams(vmem_limit_bytes=VMEM_LIMIT),
    )(parts, weights, weights_far)


def ready_kernel(
    counts_ref,
    tokens_ref,
    cotangent_ref,
    modulation_ref,
    rows_ref,
    factors_ref,
):
    rows = rows_ref.shape[1]
    first_row = (lax.axis_index("x") * 2 + lax.axis_index("core")) * rows
    first = block_index() * tokens_ref.shape[0] + first_row
    _, scale, gate = modulation_rows(counts_ref, modulation_ref, first, rows)
    at = pl.ds(pl.multiple_of(first_row, rows), rows)
    normed, inv_std = layer_norm(tokens_ref[at, :].astype(F32))
    rows_ref[0] = tokens_ref[at, :]
    rows_ref[1] = cotangent_ref[at, :]
    factors_ref[0] = gate
    factors_ref[1] = 1.0 + scale
    factors_ref[2] = normed
    factors_ref[3] = jnp.broadcast_to(inv_std, normed.shape)


def ready(counts, tokens, cotangent, modulation, share):
    width = tokens.shape[1]
    return pl.pallas_call(
        ready_kernel,
        out_shape=(
            jax.ShapeDtypeStruct((2, share, width), BF16),
            jax.ShapeDtypeStruct((4, share, width), F32),
        ),
        in_specs=[SMEM] + [VMEM] * 3,
        out_specs=(VMEM, VMEM),
        compiler_params=pltpu.CompilerParams(vmem_limit_bytes=VMEM_LIMIT),
    )(counts, tokens, cotangent, modulation)


def leave_kernel(rows_ref, factors_ref, shares_ref, layer_ref, grad_ref):
    width = layer_ref.shape[1]
    sums = shares_ref[0].astype(F32)
    for share in range(1, shares_ref.shape[0]):
        sums = sums + shares_ref[share].astype(F32)
    layer = rows_ref[0].astype(F32) + factors_ref[0] * sums[:, :width]
    layer_ref[...] = layer.astype(BF16)
    d_normed = sums[:, width:] * factors_ref[1]
    normed = factors_ref[2]
    input_grad = rows_ref[1].astype(F32) + factors_ref[3] * (
        d_normed
        - jnp.mean(d_normed, axis=-1, keepdims=True)
        - normed * jnp.mean(d_normed * normed, axis=-1, keepdims=True)
    )
    grad_ref[...] = input_grad.astype(BF16)


def leave(rows, factors, shares):
    out = jax.ShapeDtypeStruct(rows.shape[1:], BF16)
    return pl.pallas_call(
        leave_kernel,
        out_shape=(out, out),
        in_specs=[VMEM] * 3,
        out_specs=(VMEM, VMEM),
        compiler_params=pltpu.CompilerParams(vmem_limit_bytes=VMEM_LIMIT),
    )(rows, factors, shares)


def per_device(tokens, cotangent, w_qkv, w_out, qk_gain, modulation, image_counts):
    tok_rows, model_width = tokens.shape
    z_count = lax.axis_size("z")
    x_count = lax.axis_size("x")
    quad = 4
    pair_rows = 2 * tok_rows
    share = tok_rows // (2 * x_count)
    w_parts = w_qkv.transpose(1, 0, 2)
    mod_parts = modulation.transpose(1, 0, 2)
    gains = jnp.pad(qk_gain, ((0, 6), (0, LANES - HEAD)))

    heads = enter(image_counts, tokens, cotangent, w_parts, w_out, mod_parts, quad)
    mine = lax.all_to_all(heads, ("yh", "yl"), 0, 0)
    mine = mine.reshape(quad * tok_rows, 2 * LANES)
    evens = range(0, z_count, 2)
    swaps = [(i, i + 1) for i in evens], [((i - 1) % z_count, i) for i in evens]
    first, second = (
        lax.ppermute(mine, "z", pairs + [(j, i) for i, j in pairs]) for pairs in swaps
    )
    halves = 2 * z_count
    lower = lax.axis_index("yh") == 0
    from_second = (lax.rem(lax.axis_index("z"), 2) == 0) == lower
    far_half = jnp.where(
        lower,
        jnp.where(from_second, second[pair_rows:], first[pair_rows:]),
        jnp.where(from_second, second[:pair_rows], first[:pair_rows]),
    )
    far = lax.ppermute(
        far_half,
        ("z", "yh"),
        [(i, (i + (2 if i % 2 == 0 else -2)) % halves) for i in range(halves)],
    )
    _, tokens_late, cotangent_late, mod_late = lax.optimization_barrier(
        (mine, tokens, cotangent, mod_parts)
    )
    rows, factors = ready(image_counts, tokens_late, cotangent_late, mod_late, share)
    near_parts = attend_near(image_counts, gains, first, mine, second)
    _, w_parts_late, w_out_late = lax.optimization_barrier((mine, w_parts, w_out))
    weights = pack(w_parts_late, w_out_late)
    weights_far = lax.ppermute(weights, "core", [(0, 1), (1, 0)])
    parts = attend_far(image_counts, gains, far, mine, near_parts)
    parts = lax.all_to_all(parts, ("yl", "core"), 0, 0)
    partial = project(parts, weights, weights_far, x_count)
    shares = lax.all_to_all(partial, "x", 0, 0)
    return leave(rows, factors, shares)


def solution(mesh):
    split = jax.sharding.Mesh(mesh.devices.reshape(16, 2, 2, 4, 2), ("z", "yh", "yl", "x", "core"))
    dp, head = ("z", "yh", "yl"), ("x", "core")
    in_specs = (P(dp, None), P(dp, None), P(None, None, head), P(head, None), P(), P(), P())
    out_specs = (P(dp + head, None), P(dp + head, None))
    return jax.shard_map(
        per_device, mesh=split, in_specs=in_specs, out_specs=out_specs, check_vma=False
    )
```

```python
import math

import jax
import jax.numpy as jnp
from jax import lax
from jax.experimental import pallas as pl
from jax.experimental.pallas import tpu as pltpu
from jax.sharding import PartitionSpec as P

EPS = 1e-06
SAME_IMAGE = 512.0
LANES = 128
HEAD = 64
F32 = jnp.float32
BF16 = jnp.bfloat16
VMEM_LIMIT = 24 * 1024 * 1024
ENTER_LIMIT = 60 * 1024 * 1024
VMEM = pl.BlockSpec(memory_space=pltpu.VMEM)
SMEM = pl.BlockSpec(memory_space=pltpu.SMEM)


def rows_dot(a, b):
    return lax.dot_general(a, b, (((1,), (1,)), ((), ())), preferred_element_type=F32)


def block_index():
    return (lax.axis_index("z") * 2 + lax.axis_index("yh")) * 2 + lax.axis_index("yl")


def image_bounds(counts_ref, first_lane):
    lane = lax.broadcasted_iota(jnp.int32, (1, LANES), 1)
    starts = jnp.zeros((1, LANES), jnp.int32)
    ends = jnp.zeros((1, LANES), jnp.int32)
    total = jnp.int32(0)
    for image in range(counts_ref.shape[0]):
        here = lane == first_lane + image
        starts = jnp.where(here, total, starts)
        total = total + counts_ref[image]
        ends = jnp.where(here, total, ends)
    return starts, ends


def modulation_rows(counts_ref, modulation_ref, first, rows):
    starts, ends = image_bounds(counts_ref, 0)
    place = first + lax.broadcasted_iota(jnp.int32, (rows, LANES), 0)
    member = ((place >= starts) & (place < ends)).astype(F32).astype(BF16)
    member = member[:, : modulation_ref.shape[1]]
    return [
        jnp.dot(member, modulation_ref[part], preferred_element_type=F32) for part in range(3)
    ]


def layer_norm(values):
    average = jnp.mean(values, axis=-1, keepdims=True)
    centred = values - average
    inv_std = lax.rsqrt(jnp.mean(centred * centred, axis=-1, keepdims=True) + EPS)
    return centred * inv_std, inv_std


def enter_kernel(
    counts_ref, tokens_ref, cotangent_ref, w_qkv_ref, w_out_ref, modulation_ref, out_ref
):
    rows = tokens_ref.shape[0]
    first = block_index() * rows
    shift, scale, gate = modulation_rows(counts_ref, modulation_ref, first, rows)
    normed, _ = layer_norm(tokens_ref[...].astype(F32))
    hidden = (normed * (1.0 + scale) + shift).astype(BF16)
    weights = jnp.concatenate([w_qkv_ref[part] for part in range(3)], axis=1)
    qkv = jnp.dot(hidden, weights, preferred_element_type=F32)
    q, k, v = (qkv[:, part * LANES : (part + 1) * LANES] for part in range(3))
    d_mixed = (cotangent_ref[...].astype(F32) * gate).astype(BF16)
    d_attn = rows_dot(d_mixed, w_out_ref[...])
    low = lax.broadcasted_iota(jnp.int32, (rows, LANES), 1) < HEAD

    def beside(left, right):
        return jnp.where(low, left, right).astype(BF16)

    q_v = (beside(q, pltpu.roll(v, HEAD, 1)), beside(pltpu.roll(q, HEAD, 1), v))
    k_d = (beside(k, pltpu.roll(d_attn, HEAD, 1)), beside(pltpu.roll(k, HEAD, 1), d_attn))
    for place in range(out_ref.shape[0]):
        out_ref[place, :, 0:LANES] = q_v[place % 2]
        out_ref[place, :, LANES:] = k_d[place % 2]


def enter(counts, tokens, cotangent, w_parts, w_out, modulation, quad):
    return pl.pallas_call(
        enter_kernel,
        out_shape=jax.ShapeDtypeStruct((quad, tokens.shape[0], 2 * LANES), BF16),
        in_specs=[SMEM] + [VMEM] * 5,
        out_specs=VMEM,
        compiler_params=pltpu.CompilerParams(vmem_limit_bytes=ENTER_LIMIT),
    )(counts, tokens, cotangent, w_parts, w_out, modulation)


def pack_kernel(w_qkv_ref, w_out_ref, weights_ref, sems):
    pairs = [(w_qkv_ref, weights_ref.at[0:3])]
    for tile in range(weights_ref.shape[1] // LANES):
        at = slice(tile * LANES, (tile + 1) * LANES)
        pairs.append((w_out_ref.at[:, at], weights_ref.at[3, at, :]))
    copies = [
        pltpu.make_async_copy(source, target, sems.at[place])
        for place, (source, target) in enumerate(pairs)
    ]
    for copy in copies:
        copy.start()
    for copy in copies:
        copy.wait()


def pack(w_parts, w_out):
    width = w_out.shape[1]
    whole = pl.BlockSpec(memory_space=pl.ANY)
    return pl.pallas_call(
        pack_kernel,
        out_shape=jax.ShapeDtypeStruct((4, width, LANES), BF16),
        in_specs=[whole] * 2,
        out_specs=VMEM,
        scratch_shapes=[pltpu.SemaphoreType.DMA((1 + width // LANES,))],
        compiler_params=pltpu.CompilerParams(vmem_limit_bytes=8 * 1024 * 1024),
    )(w_parts, w_out)


def w_out_of(weights_ref):
    tiles = weights_ref.shape[1] // LANES
    return jnp.concatenate(
        [weights_ref[3, tile * LANES : (tile + 1) * LANES, :] for tile in range(tiles)], axis=1
    )


LOG2_E = math.log2(math.e)
INV_ROOT = 1.0 / math.sqrt(HEAD)
CHUNK = 256
TILE = 64
MAIN = 6
REACH_CHUNKS = 4


def low_lanes():
    return lax.broadcasted_iota(jnp.int32, (1, LANES), 1) < HEAD


def lower_mean(values):
    return jnp.sum(jnp.where(low_lanes(), values, 0.0), axis=-1, keepdims=True) * (1.0 / HEAD)


def lower_sums(values):
    ones = (lax.broadcasted_iota(jnp.int32, (LANES, LANES), 0) < HEAD).astype(F32).astype(BF16)
    squares = values * values
    large = squares.astype(BF16)
    small = (squares - large.astype(F32)).astype(BF16)
    large = jnp.dot(large, ones, preferred_element_type=F32)
    return large + jnp.dot(small, ones, preferred_element_type=F32)


def place_block(source, place, starts, ends, gains_ref, stores):
    low = low_lanes()
    rows = source.shape[0]
    at = place + lax.broadcasted_iota(jnp.int32, (rows, LANES), 0)
    same = ((at >= starts) & (at < ends)).astype(F32)
    first = source[:, 0:LANES].astype(F32)
    second = source[:, LANES:].astype(F32)

    def normed(raw, gain):
        return raw * lax.rsqrt(lower_sums(raw) * (1.0 / HEAD) + EPS) * gain

    keys = normed(second, gains_ref[1:2, :])
    queries = normed(first, gains_ref[0:1, :] * INV_ROOT)
    q_store, k_store, v_store, d_store, kv_store = stores
    q_store[...] = jnp.where(low, queries, same * SAME_IMAGE).astype(BF16)
    k_store[...] = jnp.where(low, keys, same).astype(BF16)
    v_store[...] = jnp.where(low, 0.0, first).astype(BF16)
    d_store[...] = source[:, LANES:]
    kv_store[...] = jnp.where(low, keys, first).astype(BF16).T


def window_facts(counts_ref):
    half = lax.axis_index("yh")
    origin = (block_index() // 4 - 1) * 2 * CHUNK
    own_at = (2 + half) * CHUNK
    starts, ends = image_bounds(counts_ref, HEAD)
    left_from = jnp.int32(-CHUNK)
    right_to = jnp.int32((MAIN + 1) * CHUNK)
    total = -origin
    for image in range(counts_ref.shape[0]):
        left_from = jnp.where(total <= own_at, total, left_from)
        ended = total >= own_at + CHUNK
        total = total + counts_ref[image]
        right_to = jnp.where((total >= own_at + CHUNK) & jnp.logical_not(ended), total, right_to)
    return half, own_at, starts - origin, ends - origin, left_from, right_to


def by_eight(values):
    return values.reshape(values.shape[0] // 8, 8, values.shape[1])


def add_tiles(s_ref, g_ref, rows, highest, total, grads):
    for piece in range(rows // TILE):
        at = slice(piece * TILE, (piece + 1) * TILE)
        weights = jnp.exp2(s_ref[at, :] * LOG2_E - highest)
        total = total + jnp.sum(by_eight(weights), axis=0)
        grads = grads + jnp.sum(by_eight(weights * g_ref[at, :]), axis=0)
    return total, grads


def rows_max(values):
    return jnp.max(by_eight(values), axis=0)


def near_kernel(
    counts_ref,
    gains_ref,
    first_ref,
    quad_ref,
    second_ref,
    qx_ref,
    kx_ref,
    vx_ref,
    dx_ref,
    kv_ref,
    so_ref,
    go_ref,
    sn_ref,
    gn_ref,
    stats_ref,
    s_ref,
    g_ref,
):
    half, own_at, starts, ends, left_from, right_to = window_facts(counts_ref)
    block_rows = CHUNK // 2

    def place(source, begin):
        begin = pl.multiple_of(begin, block_rows)
        at = pl.ds(begin, block_rows)
        stores = [ref.at[at, :] for ref in (qx_ref, kx_ref, vx_ref, dx_ref)]
        place_block(source, begin, starts, ends, gains_ref, stores + [kv_ref.at[:, at]])

    to_first = jnp.where(lax.rem(lax.axis_index("z"), 2) == 0, 2 * CHUNK, -2 * CHUNK)
    for block in range(4):
        at = slice(block * block_rows, (block + 1) * block_rows)
        begin = 2 * CHUNK + block * block_rows
        place(quad_ref.at[at], begin)
        place(first_ref.at[at], begin + to_first)
        place(second_ref.at[at], begin - to_first)

    own_rows = pl.ds(pl.multiple_of(own_at, CHUNK), CHUNK)
    q_own = qx_ref[own_rows, :]
    d_own = dx_ref[own_rows, :]
    highest = jnp.full((8, CHUNK), -jnp.inf, F32)
    for piece in range(MAIN):
        at = slice(piece * CHUNK, (piece + 1) * CHUNK)
        scores = rows_dot(kx_ref[at, :], q_own)
        so_ref[at, :] = scores
        highest = jnp.maximum(highest, rows_max(scores))
        go_ref[at, :] = rows_dot(vx_ref[at, :], d_own)
    highest = jnp.max(highest, axis=0, keepdims=True) * LOG2_E
    total = jnp.zeros((8, CHUNK), F32)
    grads = jnp.zeros((8, CHUNK), F32)
    for piece in range(MAIN * CHUNK // TILE):
        at = slice(piece * TILE, (piece + 1) * TILE)
        weights = jnp.exp2(so_ref[at, :] * LOG2_E - highest)
        so_ref[at, :] = weights
        total = total + jnp.sum(by_eight(weights), axis=0)
        grads = grads + jnp.sum(by_eight(weights * go_ref[at, :]), axis=0)
    stats_ref[MAIN, 0:1, :] = highest
    stats_ref[MAIN, 1:2, :] = jnp.sum(total, axis=0, keepdims=True)
    stats_ref[MAIN, 2:3, :] = jnp.sum(grads, axis=0, keepdims=True)

    left_key = jnp.clip((left_from + CHUNK) // CHUNK - 1, 0, MAIN - REACH_CHUNKS)
    right_key = jnp.clip((right_to - 1) // CHUNK - (REACH_CHUNKS - 1), 0, MAIN - REACH_CHUNKS)

    def one_chunk(step, carry):
        slot = step + jnp.where(step >= 2 + half, 1, 0)
        begin = slot * CHUNK

        @pl.when((begin < right_to) & (begin + CHUNK > left_from))
        def _():
            at = pl.ds(pl.multiple_of(begin, CHUNK), CHUNK)
            key = jnp.where(begin < own_at, left_key, right_key) * CHUNK
            q_block = qx_ref[at, :]
            d_block = dx_ref[at, :]
            keys_at = pl.ds(pl.multiple_of(key, CHUNK), REACH_CHUNKS * CHUNK)
            s_ref[...] = rows_dot(kx_ref[keys_at, :], q_block)
            g_ref[...] = rows_dot(vx_ref[keys_at, :], d_block)
            highest = jnp.full((8, CHUNK), -jnp.inf, F32)
            for piece in range(REACH_CHUNKS * CHUNK // TILE):
                here = slice(piece * TILE, (piece + 1) * TILE)
                highest = jnp.maximum(highest, rows_max(s_ref[here, :]))
            highest = jnp.max(highest, axis=0, keepdims=True) * LOG2_E
            zeros = jnp.zeros((8, CHUNK), F32)
            total, grads = add_tiles(s_ref, g_ref, REACH_CHUNKS * CHUNK, highest, zeros, zeros)
            stats_ref[slot, 0:1, :] = highest
            stats_ref[slot, 1:2, :] = jnp.sum(total, axis=0, keepdims=True)
            stats_ref[slot, 2:3, :] = jnp.sum(grads, axis=0, keepdims=True)
            near_at = pl.ds(pl.multiple_of(own_at - key, CHUNK), CHUNK)
            sn_ref[slot, :, :] = s_ref[near_at, :]
            gn_ref[slot, :, :] = g_ref[near_at, :]

        return carry

    lax.fori_loop(0, MAIN - 1, one_chunk, 0)


def attend_near(counts, gains, first, quad, second):
    rows = MAIN * CHUNK
    head_rows = jax.ShapeDtypeStruct((rows, LANES), BF16)
    scores = jax.ShapeDtypeStruct((rows, CHUNK), F32)
    tiles = jax.ShapeDtypeStruct((MAIN, CHUNK, CHUNK), F32)
    return pl.pallas_call(
        near_kernel,
        out_shape=(head_rows,) * 4
        + (jax.ShapeDtypeStruct((LANES, rows), BF16),)
        + (scores, scores, tiles, tiles, jax.ShapeDtypeStruct((MAIN + 1, 8, CHUNK), F32)),
        in_specs=[SMEM] + [VMEM] * 4,
        out_specs=(VMEM,) * 10,
        scratch_shapes=[pltpu.VMEM((REACH_CHUNKS * CHUNK, CHUNK), F32)] * 2,
        cost_estimate=pl.CostEstimate(
            flops=7000000000, bytes_accessed=1 << 20, transcendentals=1 << 20
        ),
        compiler_params=pltpu.CompilerParams(vmem_limit_bytes=VMEM_LIMIT),
    )(counts, gains, first, quad, second)


def far_kernel(
    counts_ref,
    gains_ref,
    far_ref,
    quad_ref,
    qx_ref,
    kx_ref,
    vx_ref,
    dx_ref,
    kv_ref,
    so_ref,
    go_ref,
    sn_ref,
    gn_ref,
    stats_ref,
    out_ref,
    qf_ref,
    kf_ref,
    vf_ref,
    df_ref,
    kvf_ref,
    s_ref,
    g_ref,
    p_ref,
    d_ref,
    sums_ref,
    dk_ref,
    dv_ref,
    done_ref,
):
    half, own_at, starts, ends, left_from, right_to = window_facts(counts_ref)
    block_rows = CHUNK // 2
    rows = MAIN * CHUNK
    far_at = jnp.where(half == 0, -CHUNK, rows)
    for block in range(2):
        at = slice(block * block_rows, (block + 1) * block_rows)
        stores = [ref.at[at, :] for ref in (qf_ref, kf_ref, vf_ref, df_ref)]
        place_block(
            far_ref.at[at],
            far_at + block * block_rows,
            starts,
            ends,
            gains_ref,
            stores + [kvf_ref.at[:, at]],
        )

    own_rows = pl.ds(pl.multiple_of(own_at, CHUNK), CHUNK)
    q_own = qx_ref[own_rows, :]
    d_own = dx_ref[own_rows, :]
    scores = rows_dot(kf_ref[...], q_own)
    s_ref[0:CHUNK, :] = scores
    g_ref[0:CHUNK, :] = rows_dot(vf_ref[...], d_own)
    near_highest = stats_ref[MAIN, 0:1, :]
    highest = jnp.max(rows_max(scores), axis=0, keepdims=True) * LOG2_E
    highest = jnp.maximum(near_highest, highest)
    shrink = jnp.exp2(near_highest - highest)
    zeros = jnp.zeros((8, CHUNK), F32)
    total, grads = add_tiles(s_ref, g_ref, CHUNK, highest, zeros, zeros)
    total = jnp.sum(total, axis=0, keepdims=True) + stats_ref[MAIN, 1:2, :] * shrink
    grads = jnp.sum(grads, axis=0, keepdims=True) + stats_ref[MAIN, 2:3, :] * shrink
    scale = 1.0 / total
    mean_grad = grads * scale

    def write_tile(scores, grads, highest, scale, mean_grad, to):
        probs = jnp.exp2(scores * LOG2_E - highest) * scale
        p_ref[to, :] = probs.astype(BF16)
        d_ref[to, :] = (probs * (grads - mean_grad)).astype(BF16)

    near_scale = shrink * scale
    for piece in range(rows // TILE):
        at = slice(piece * TILE, (piece + 1) * TILE)
        probs = so_ref[at, :] * near_scale
        p_ref[at, :] = probs.astype(BF16)
        d_ref[at, :] = (probs * (go_ref[at, :] - mean_grad)).astype(BF16)
    for piece in range(CHUNK // TILE):
        at = slice(piece * TILE, (piece + 1) * TILE)
        to = slice(rows + piece * TILE, rows + (piece + 1) * TILE)
        write_tile(s_ref[at, :], g_ref[at, :], highest, scale, mean_grad, to)
    dk_ref[...] = jnp.dot(d_ref[own_rows, :], q_own, preferred_element_type=F32)
    dv_ref[...] = jnp.dot(p_ref[own_rows, :], d_own, preferred_element_type=F32)

    def times_window(values_ref):
        main = jnp.dot(kv_ref[...], values_ref[0:rows, :], preferred_element_type=F32)
        return main + jnp.dot(
            kvf_ref[...], values_ref[rows : rows + CHUNK, :], preferred_element_type=F32
        )

    upper = lax.broadcasted_iota(jnp.int32, (LANES, CHUNK), 0) < HEAD
    own_out = jnp.where(upper, times_window(d_ref) * INV_ROOT, times_window(p_ref)).T

    query_lane = lax.broadcasted_iota(jnp.int32, (1, CHUNK), 1)
    reaches_far = jnp.where(half == 0, left_from < 0, right_to > rows)

    def add_gradients(tiles, begin, q_block, d_block, highest, total, grads):
        place = query_lane + begin
        scale = jnp.where((place >= left_from) & (place < right_to), 1.0 / total, 0.0)
        mean_grad = grads * scale
        for piece in range(CHUNK // TILE):
            scores, given = tiles(piece)
            at = slice(piece * TILE, (piece + 1) * TILE)
            write_tile(scores, given, highest, scale, mean_grad, at)
        dk_ref[...] += jnp.dot(d_ref[0:CHUNK, :], q_block, preferred_element_type=F32)
        dv_ref[...] += jnp.dot(p_ref[0:CHUNK, :], d_block, preferred_element_type=F32)

    def one_chunk(step, carry):
        slot = step + jnp.where(step >= 2 + half, 1, 0)
        begin = slot * CHUNK

        @pl.when((begin < right_to) & (begin + CHUNK > left_from))
        def _():
            at = pl.ds(pl.multiple_of(begin, CHUNK), CHUNK)
            q_block = qx_ref[at, :]
            d_block = dx_ref[at, :]
            sums_ref[...] = stats_ref[slot, :, :]
            same_side = (begin < own_at) == (half == 0)

            @pl.when(reaches_far & same_side)
            def _():
                scores = rows_dot(kf_ref[...], q_block)
                s_ref[0:CHUNK, :] = scores
                g_ref[0:CHUNK, :] = rows_dot(vf_ref[...], d_block)
                before = sums_ref[0:1, :]
                highest = jnp.max(rows_max(scores), axis=0, keepdims=True) * LOG2_E
                highest = jnp.maximum(before, highest)
                total, grads = add_tiles(s_ref, g_ref, CHUNK, highest, zeros, zeros)
                shrink = jnp.exp2(before - highest)
                sums_ref[0:1, :] = highest
                total = jnp.sum(total, axis=0, keepdims=True)
                grads = jnp.sum(grads, axis=0, keepdims=True)
                sums_ref[1:2, :] = sums_ref[1:2, :] * shrink + total
                sums_ref[2:3, :] = sums_ref[2:3, :] * shrink + grads

            def tiles(piece):
                at = slice(piece * TILE, (piece + 1) * TILE)
                return sn_ref[slot, at, :], gn_ref[slot, at, :]

            add_gradients(
                tiles, begin, q_block, d_block, sums_ref[0:1, :], sums_ref[1:2, :], sums_ref[2:3, :]
            )

        return carry

    lax.fori_loop(0, MAIN - 1, one_chunk, 0)

    @pl.when(reaches_far)
    def _():
        q_block = qf_ref[...]
        d_block = df_ref[...]
        key = half * (MAIN // 2) * CHUNK
        highest = jnp.full((8, CHUNK), -jnp.inf, F32)
        for piece in range(REACH_CHUNKS):
            here = slice(piece * CHUNK, (piece + 1) * CHUNK)
            if piece < REACH_CHUNKS - 1:
                keys_at = pl.ds(pl.multiple_of(key + piece * CHUNK, CHUNK), CHUNK)
                keys, values = kx_ref[keys_at, :], vx_ref[keys_at, :]
            else:
                keys, values = kf_ref[...], vf_ref[...]
            scores = rows_dot(keys, q_block)
            s_ref[here, :] = scores
            highest = jnp.maximum(highest, rows_max(scores))
            g_ref[here, :] = rows_dot(values, d_block)
        highest = jnp.max(highest, axis=0, keepdims=True) * LOG2_E
        total, grads = add_tiles(s_ref, g_ref, REACH_CHUNKS * CHUNK, highest, zeros, zeros)

        def tiles(piece):
            at = pl.ds(pl.multiple_of(own_at - key + piece * TILE, TILE), TILE)
            return s_ref[at, :], g_ref[at, :]

        add_gradients(
            tiles,
            far_at,
            q_block,
            d_block,
            highest,
            jnp.sum(total, axis=0, keepdims=True),
            jnp.sum(grads, axis=0, keepdims=True),
        )

    def norm_grad(raw, gain, d_norm):
        inverse = lax.rsqrt(lower_mean(raw * raw) + EPS)
        scaled = d_norm.astype(BF16).astype(F32) * gain
        inner = lower_mean(raw * scaled)
        return inverse * scaled - raw * (inverse * inverse * inverse * inner)

    low = low_lanes()
    own_in_quad = pl.ds(pl.multiple_of(half * CHUNK, CHUNK), CHUNK)
    raw_q = quad_ref[own_in_quad, 0:LANES].astype(F32)
    raw_k = quad_ref[own_in_quad, LANES:].astype(F32)
    d_q = norm_grad(raw_q, gains_ref[0:1, :], own_out)
    d_k = norm_grad(raw_k, gains_ref[1:2, :], dk_ref[...])
    done_ref[:, 0:LANES] = jnp.where(low, d_q, own_out).astype(BF16)
    done_ref[:, LANES:] = jnp.where(low, d_k, dv_ref[...]).astype(BF16)
    share = 16
    for member in range(out_ref.shape[0]):
        block, core = member // 2, member % 2
        for part in range(out_ref.shape[1] // share):
            begin = (block * 8 + part * 2 + core) * share
            out_ref[member, part * share : (part + 1) * share, :] = done_ref[
                begin : begin + share, :
            ]


def attend_far(counts, gains, far, quad, near_parts):
    return pl.pallas_call(
        far_kernel,
        out_shape=jax.ShapeDtypeStruct((4, CHUNK // 4, 2 * LANES), BF16),
        in_specs=[SMEM] + [VMEM] * (3 + len(near_parts)),
        out_specs=VMEM,
        scratch_shapes=[pltpu.VMEM((CHUNK, LANES), BF16)] * 4
        + [pltpu.VMEM((LANES, CHUNK), BF16)]
        + [pltpu.VMEM((REACH_CHUNKS * CHUNK, CHUNK), F32)] * 2
        + [pltpu.VMEM(((MAIN + 1) * CHUNK, CHUNK), BF16)] * 2
        + [pltpu.VMEM((8, CHUNK), F32)]
        + [pltpu.VMEM((CHUNK, LANES), F32)] * 2
        + [pltpu.VMEM((CHUNK, 2 * LANES), BF16)],
        cost_estimate=pl.CostEstimate(
            flops=7000000000, bytes_accessed=1 << 20, transcendentals=1 << 20
        ),
        compiler_params=pltpu.CompilerParams(vmem_limit_bytes=VMEM_LIMIT),
    )(counts, gains, far, quad, *near_parts)


def project_kernel(parts_ref, weights_ref, weights_far_ref, out_ref):
    rows = parts_ref.shape[1]
    width = weights_ref.shape[1]
    share = out_ref.shape[1]
    core = lax.axis_index("core")
    low = lax.broadcasted_iota(jnp.int32, (rows, LANES), 1) < HEAD

    def by_column(which):
        head0 = parts_ref[which].astype(F32)
        head1 = parts_ref[2 + which].astype(F32)
        a0, a1 = head0[:, :LANES], head1[:, :LANES]
        b0, b1 = head0[:, LANES:], head1[:, LANES:]
        d_q = jnp.where(low, a0, pltpu.roll(a1, HEAD, 1)).astype(BF16)
        attn = jnp.where(low, pltpu.roll(a0, HEAD, 1), a1).astype(BF16)
        d_k = jnp.where(low, b0, pltpu.roll(b1, HEAD, 1)).astype(BF16)
        d_v = jnp.where(low, pltpu.roll(b0, HEAD, 1), b1).astype(BF16)
        return attn, [d_q, d_k, d_v]

    attn, grads = by_column(core)
    attn_far, grads_far = by_column(1 - core)
    mixed = jnp.dot(
        jnp.concatenate([attn, attn_far], axis=1),
        jnp.concatenate([w_out_of(weights_ref), w_out_of(weights_far_ref)], axis=0),
        preferred_element_type=F32,
    ).astype(BF16)
    weights = [ref[part] for ref in (weights_ref, weights_far_ref) for part in range(3)]
    d_hidden = rows_dot(
        jnp.concatenate(grads + grads_far, axis=1), jnp.concatenate(weights, axis=1)
    ).astype(BF16)
    for place in range(out_ref.shape[0]):
        at = slice(place * share, (place + 1) * share)
        out_ref[place, :, :width] = mixed[at]
        out_ref[place, :, width:] = d_hidden[at]


def project(parts, weights, weights_far, x_count):
    return pl.pallas_call(
        project_kernel,
        out_shape=jax.ShapeDtypeStruct(
            (x_count, parts.shape[1] // x_count, 2 * weights.shape[1]), BF16
        ),
        in_specs=[VMEM] * 3,
        out_specs=VMEM,
        compiler_params=pltpu.CompilerParams(vmem_limit_bytes=VMEM_LIMIT),
    )(parts, weights, weights_far)


def ready_kernel(
    counts_ref,
    tokens_ref,
    cotangent_ref,
    modulation_ref,
    rows_ref,
    factors_ref,
):
    rows = rows_ref.shape[1]
    first_row = (lax.axis_index("x") * 2 + lax.axis_index("core")) * rows
    first = block_index() * tokens_ref.shape[0] + first_row
    _, scale, gate = modulation_rows(counts_ref, modulation_ref, first, rows)
    at = pl.ds(pl.multiple_of(first_row, rows), rows)
    normed, inv_std = layer_norm(tokens_ref[at, :].astype(F32))
    rows_ref[0] = tokens_ref[at, :]
    rows_ref[1] = cotangent_ref[at, :]
    factors_ref[0] = gate
    factors_ref[1] = 1.0 + scale
    factors_ref[2] = normed
    factors_ref[3] = jnp.broadcast_to(inv_std, normed.shape)


def ready(counts, tokens, cotangent, modulation, share):
    width = tokens.shape[1]
    return pl.pallas_call(
        ready_kernel,
        out_shape=(
            jax.ShapeDtypeStruct((2, share, width), BF16),
            jax.ShapeDtypeStruct((4, share, width), F32),
        ),
        in_specs=[SMEM] + [VMEM] * 3,
        out_specs=(VMEM, VMEM),
        compiler_params=pltpu.CompilerParams(vmem_limit_bytes=VMEM_LIMIT),
    )(counts, tokens, cotangent, modulation)


def leave_kernel(rows_ref, factors_ref, shares_ref, layer_ref, grad_ref):
    width = layer_ref.shape[1]
    sums = shares_ref[0].astype(F32)
    for share in range(1, shares_ref.shape[0]):
        sums = sums + shares_ref[share].astype(F32)
    layer = rows_ref[0].astype(F32) + factors_ref[0] * sums[:, :width]
    layer_ref[...] = layer.astype(BF16)
    d_normed = sums[:, width:] * factors_ref[1]
    normed = factors_ref[2]
    input_grad = rows_ref[1].astype(F32) + factors_ref[3] * (
        d_normed
        - jnp.mean(d_normed, axis=-1, keepdims=True)
        - normed * jnp.mean(d_normed * normed, axis=-1, keepdims=True)
    )
    grad_ref[...] = input_grad.astype(BF16)


def leave(rows, factors, shares):
    out = jax.ShapeDtypeStruct(rows.shape[1:], BF16)
    return pl.pallas_call(
        leave_kernel,
        out_shape=(out, out),
        in_specs=[VMEM] * 3,
        out_specs=(VMEM, VMEM),
        compiler_params=pltpu.CompilerParams(vmem_limit_bytes=VMEM_LIMIT),
    )(rows, factors, shares)


def per_device(tokens, cotangent, w_qkv, w_out, qk_gain, modulation, image_counts):
    tok_rows, model_width = tokens.shape
    z_count = lax.axis_size("z")
    x_count = lax.axis_size("x")
    quad = 4
    pair_rows = 2 * tok_rows
    share = tok_rows // (2 * x_count)
    w_parts = w_qkv.transpose(1, 0, 2)
    mod_parts = modulation.transpose(1, 0, 2)
    gains = jnp.pad(qk_gain, ((0, 6), (0, LANES - HEAD)))

    heads = enter(image_counts, tokens, cotangent, w_parts, w_out, mod_parts, quad)
    mine = lax.all_to_all(heads, ("yh", "yl"), 0, 0)
    mine = mine.reshape(quad * tok_rows, 2 * LANES)
    evens = range(0, z_count, 2)
    swaps = [(i, i + 1) for i in evens], [((i - 1) % z_count, i) for i in evens]
    first, second = (
        lax.ppermute(mine, "z", pairs + [(j, i) for i, j in pairs]) for pairs in swaps
    )
    halves = 4 * z_count
    far_half = jnp.where(
        lax.axis_index("yh") == lax.axis_index("core"), mine[pair_rows:], mine[:pair_rows]
    )

    def far_source(target):
        z, yh, core = target // 4, target // 2 % 2, target % 2
        return (z + (2 if yh else -2)) % z_count * 4 + (yh ^ core) * 2 + core

    far = lax.ppermute(
        far_half, ("z", "yh", "core"), [(far_source(i), i) for i in range(halves)]
    )
    _, tokens_late, cotangent_late, mod_late = lax.optimization_barrier(
        (mine, tokens, cotangent, mod_parts)
    )
    rows, factors = ready(image_counts, tokens_late, cotangent_late, mod_late, share)
    first, rows, factors = lax.optimization_barrier((first, rows, factors))
    near_parts = attend_near(image_counts, gains, first, mine, second)
    _, w_parts_late, w_out_late = lax.optimization_barrier((mine, w_parts, w_out))
    weights = pack(w_parts_late, w_out_late)
    weights_far = lax.ppermute(weights, "core", [(0, 1), (1, 0)])
    parts = attend_far(image_counts, gains, far, mine, near_parts)
    parts = lax.all_to_all(parts, ("yl", "core"), 0, 0)
    partial = project(parts, weights, weights_far, x_count)
    shares = lax.all_to_all(partial, "x", 0, 0)
    return leave(rows, factors, shares)


def solution(mesh):
    split = jax.sharding.Mesh(mesh.devices.reshape(16, 2, 2, 4, 2), ("z", "yh", "yl", "x", "core"))
    dp, head = ("z", "yh", "yl"), ("x", "core")
    in_specs = (P(dp, None), P(dp, None), P(None, None, head), P(head, None), P(), P(), P())
    out_specs = (P(dp + head, None), P(dp + head, None))
    return jax.shard_map(
        per_device, mesh=split, in_specs=in_specs, out_specs=out_specs, check_vma=False
    )
```

```python
import math

import jax
import jax.numpy as jnp
from jax import lax
from jax.experimental import pallas as pl
from jax.experimental.pallas import tpu as pltpu
from jax.sharding import PartitionSpec as P

EPS = 1e-06
SAME_IMAGE = 512.0
LANES = 128
HEAD = 64
F32 = jnp.float32
BF16 = jnp.bfloat16
VMEM_LIMIT = 24 * 1024 * 1024
ENTER_LIMIT = 60 * 1024 * 1024
VMEM = pl.BlockSpec(memory_space=pltpu.VMEM)
SMEM = pl.BlockSpec(memory_space=pltpu.SMEM)


def rows_dot(a, b):
    return lax.dot_general(a, b, (((1,), (1,)), ((), ())), preferred_element_type=F32)


def block_index():
    return (lax.axis_index("z") * 2 + lax.axis_index("yh")) * 2 + lax.axis_index("yl")


def image_bounds(counts_ref, first_lane):
    lane = lax.broadcasted_iota(jnp.int32, (1, LANES), 1)
    starts = jnp.zeros((1, LANES), jnp.int32)
    ends = jnp.zeros((1, LANES), jnp.int32)
    total = jnp.int32(0)
    for image in range(counts_ref.shape[0]):
        here = lane == first_lane + image
        starts = jnp.where(here, total, starts)
        total = total + counts_ref[image]
        ends = jnp.where(here, total, ends)
    return starts, ends


def modulation_rows(counts_ref, modulation_ref, first, rows):
    starts, ends = image_bounds(counts_ref, 0)
    place = first + lax.broadcasted_iota(jnp.int32, (rows, LANES), 0)
    member = ((place >= starts) & (place < ends)).astype(F32).astype(BF16)
    member = member[:, : modulation_ref.shape[1]]
    return [
        jnp.dot(member, modulation_ref[part], preferred_element_type=F32) for part in range(3)
    ]


def layer_norm(values):
    average = jnp.mean(values, axis=-1, keepdims=True)
    centred = values - average
    inv_std = lax.rsqrt(jnp.mean(centred * centred, axis=-1, keepdims=True) + EPS)
    return centred * inv_std, inv_std


def enter_kernel(
    counts_ref, tokens_ref, cotangent_ref, w_qkv_ref, w_out_ref, modulation_ref, out_ref
):
    rows = tokens_ref.shape[0]
    first = block_index() * rows
    shift, scale, gate = modulation_rows(counts_ref, modulation_ref, first, rows)
    normed, _ = layer_norm(tokens_ref[...].astype(F32))
    hidden = (normed * (1.0 + scale) + shift).astype(BF16)
    weights = jnp.concatenate([w_qkv_ref[part] for part in range(3)], axis=1)
    qkv = jnp.dot(hidden, weights, preferred_element_type=F32)
    q, k, v = (qkv[:, part * LANES : (part + 1) * LANES] for part in range(3))
    d_mixed = (cotangent_ref[...].astype(F32) * gate).astype(BF16)
    d_attn = rows_dot(d_mixed, w_out_ref[...])
    low = lax.broadcasted_iota(jnp.int32, (rows, LANES), 1) < HEAD

    def beside(left, right):
        return jnp.where(low, left, right).astype(BF16)

    q_v = (beside(q, pltpu.roll(v, HEAD, 1)), beside(pltpu.roll(q, HEAD, 1), v))
    k_d = (beside(k, pltpu.roll(d_attn, HEAD, 1)), beside(pltpu.roll(k, HEAD, 1), d_attn))
    for place in range(out_ref.shape[0]):
        out_ref[place, :, 0:LANES] = q_v[place % 2]
        out_ref[place, :, LANES:] = k_d[place % 2]


def enter(counts, tokens, cotangent, w_parts, w_out, modulation, quad):
    return pl.pallas_call(
        enter_kernel,
        out_shape=jax.ShapeDtypeStruct((quad, tokens.shape[0], 2 * LANES), BF16),
        in_specs=[SMEM] + [VMEM] * 5,
        out_specs=VMEM,
        compiler_params=pltpu.CompilerParams(vmem_limit_bytes=ENTER_LIMIT),
    )(counts, tokens, cotangent, w_parts, w_out, modulation)


def pack_kernel(w_qkv_ref, w_out_ref, weights_ref, sems):
    pairs = [(w_qkv_ref, weights_ref.at[0:3])]
    for tile in range(weights_ref.shape[1] // LANES):
        at = slice(tile * LANES, (tile + 1) * LANES)
        pairs.append((w_out_ref.at[:, at], weights_ref.at[3, at, :]))
    copies = [
        pltpu.make_async_copy(source, target, sems.at[place])
        for place, (source, target) in enumerate(pairs)
    ]
    for copy in copies:
        copy.start()
    for copy in copies:
        copy.wait()


def pack(w_parts, w_out):
    width = w_out.shape[1]
    whole = pl.BlockSpec(memory_space=pl.ANY)
    return pl.pallas_call(
        pack_kernel,
        out_shape=jax.ShapeDtypeStruct((4, width, LANES), BF16),
        in_specs=[whole] * 2,
        out_specs=VMEM,
        scratch_shapes=[pltpu.SemaphoreType.DMA((1 + width // LANES,))],
        compiler_params=pltpu.CompilerParams(vmem_limit_bytes=8 * 1024 * 1024),
    )(w_parts, w_out)


def w_out_of(weights_ref):
    tiles = weights_ref.shape[1] // LANES
    return jnp.concatenate(
        [weights_ref[3, tile * LANES : (tile + 1) * LANES, :] for tile in range(tiles)], axis=1
    )


LOG2_E = math.log2(math.e)
INV_ROOT = 1.0 / math.sqrt(HEAD)
CHUNK = 256
TILE = 64
MAIN = 6
REACH_CHUNKS = 4


def low_lanes():
    return lax.broadcasted_iota(jnp.int32, (1, LANES), 1) < HEAD


def lower_mean(values):
    return jnp.sum(jnp.where(low_lanes(), values, 0.0), axis=-1, keepdims=True) * (1.0 / HEAD)


def lower_sums(values):
    ones = (lax.broadcasted_iota(jnp.int32, (LANES, LANES), 0) < HEAD).astype(F32).astype(BF16)
    squares = values * values
    large = squares.astype(BF16)
    small = (squares - large.astype(F32)).astype(BF16)
    large = jnp.dot(large, ones, preferred_element_type=F32)
    return large + jnp.dot(small, ones, preferred_element_type=F32)


def place_block(source, place, starts, ends, gains_ref, stores):
    low = low_lanes()
    rows = source.shape[0]
    at = place + lax.broadcasted_iota(jnp.int32, (rows, LANES), 0)
    same = ((at >= starts) & (at < ends)).astype(F32)
    first = source[:, 0:LANES].astype(F32)
    second = source[:, LANES:].astype(F32)

    def normed(raw, gain):
        return raw * lax.rsqrt(lower_sums(raw) * (1.0 / HEAD) + EPS) * gain

    keys = normed(second, gains_ref[1:2, :])
    queries = normed(first, gains_ref[0:1, :] * INV_ROOT)
    q_store, k_store, v_store, d_store, kv_store = stores
    q_store[...] = jnp.where(low, queries, same * SAME_IMAGE).astype(BF16)
    k_store[...] = jnp.where(low, keys, same).astype(BF16)
    v_store[...] = jnp.where(low, 0.0, first).astype(BF16)
    d_store[...] = source[:, LANES:]
    kv_store[...] = jnp.where(low, keys, first).astype(BF16).T


def window_facts(counts_ref):
    half = lax.axis_index("yh")
    origin = (block_index() // 4 - 1) * 2 * CHUNK
    own_at = (2 + half) * CHUNK
    starts, ends = image_bounds(counts_ref, HEAD)
    left_from = jnp.int32(-CHUNK)
    right_to = jnp.int32((MAIN + 1) * CHUNK)
    total = -origin
    for image in range(counts_ref.shape[0]):
        left_from = jnp.where(total <= own_at, total, left_from)
        ended = total >= own_at + CHUNK
        total = total + counts_ref[image]
        right_to = jnp.where((total >= own_at + CHUNK) & jnp.logical_not(ended), total, right_to)
    return half, own_at, starts - origin, ends - origin, left_from, right_to


def by_eight(values):
    return values.reshape(values.shape[0] // 8, 8, values.shape[1])


def add_tiles(s_ref, g_ref, rows, highest, total, grads):
    for piece in range(rows // TILE):
        at = slice(piece * TILE, (piece + 1) * TILE)
        weights = jnp.exp2(s_ref[at, :] * LOG2_E - highest)
        total = total + jnp.sum(by_eight(weights), axis=0)
        grads = grads + jnp.sum(by_eight(weights * g_ref[at, :]), axis=0)
    return total, grads


def rows_max(values):
    return jnp.max(by_eight(values), axis=0)


def running_sums(k_ref, v_ref, key, chunks, q_block, d_block, s_ref, g_ref):
    highest = jnp.full((8, CHUNK), -jnp.inf, F32)
    total = jnp.zeros((8, CHUNK), F32)
    grads = jnp.zeros((8, CHUNK), F32)
    for piece in range(chunks):
        keys_at = pl.ds(pl.multiple_of(key + piece * CHUNK, CHUNK), CHUNK)
        here = slice(piece * CHUNK, (piece + 1) * CHUNK)
        scores = rows_dot(k_ref[keys_at, :], q_block)
        s_ref[here, :] = scores
        g_ref[here, :] = rows_dot(v_ref[keys_at, :], d_block)
        higher = jnp.maximum(highest, rows_max(scores) * LOG2_E)
        shrink = jnp.exp2(highest - higher)
        total = total * shrink
        grads = grads * shrink
        highest = higher
        for tile in range(CHUNK // TILE):
            at = slice(piece * CHUNK + tile * TILE, piece * CHUNK + (tile + 1) * TILE)
            weights = jnp.exp2(by_eight(s_ref[at, :]) * LOG2_E - highest[None])
            total = total + jnp.sum(weights, axis=0)
            grads = grads + jnp.sum(weights * by_eight(g_ref[at, :]), axis=0)
    top = jnp.max(highest, axis=0, keepdims=True)
    shrink = jnp.exp2(highest - top)
    total = jnp.sum(total * shrink, axis=0, keepdims=True)
    return top, total, jnp.sum(grads * shrink, axis=0, keepdims=True)


def near_kernel(
    counts_ref,
    gains_ref,
    first_ref,
    quad_ref,
    second_ref,
    qx_ref,
    kx_ref,
    vx_ref,
    dx_ref,
    kv_ref,
    so_ref,
    go_ref,
    sn_ref,
    gn_ref,
    stats_ref,
    s_ref,
    g_ref,
):
    half, own_at, starts, ends, left_from, right_to = window_facts(counts_ref)
    block_rows = CHUNK // 2

    def place(source, begin):
        begin = pl.multiple_of(begin, block_rows)
        at = pl.ds(begin, block_rows)
        stores = [ref.at[at, :] for ref in (qx_ref, kx_ref, vx_ref, dx_ref)]
        place_block(source, begin, starts, ends, gains_ref, stores + [kv_ref.at[:, at]])

    to_first = jnp.where(lax.rem(lax.axis_index("z"), 2) == 0, 2 * CHUNK, -2 * CHUNK)
    for block in range(4):
        at = slice(block * block_rows, (block + 1) * block_rows)
        begin = 2 * CHUNK + block * block_rows
        place(quad_ref.at[at], begin)
        place(first_ref.at[at], begin + to_first)
        place(second_ref.at[at], begin - to_first)

    own_rows = pl.ds(pl.multiple_of(own_at, CHUNK), CHUNK)
    q_own = qx_ref[own_rows, :]
    d_own = dx_ref[own_rows, :]
    highest = jnp.full((8, CHUNK), -jnp.inf, F32)
    for piece in range(MAIN):
        at = slice(piece * CHUNK, (piece + 1) * CHUNK)
        scores = rows_dot(kx_ref[at, :], q_own)
        so_ref[at, :] = scores
        highest = jnp.maximum(highest, rows_max(scores))
        go_ref[at, :] = rows_dot(vx_ref[at, :], d_own)
    highest = jnp.max(highest, axis=0, keepdims=True) * LOG2_E
    total = jnp.zeros((8, CHUNK), F32)
    grads = jnp.zeros((8, CHUNK), F32)
    for piece in range(MAIN * CHUNK // TILE):
        at = slice(piece * TILE, (piece + 1) * TILE)
        weights = jnp.exp2(so_ref[at, :] * LOG2_E - highest)
        so_ref[at, :] = weights
        total = total + jnp.sum(by_eight(weights), axis=0)
        grads = grads + jnp.sum(by_eight(weights * go_ref[at, :]), axis=0)
    stats_ref[MAIN, 0:1, :] = highest
    stats_ref[MAIN, 1:2, :] = jnp.sum(total, axis=0, keepdims=True)
    stats_ref[MAIN, 2:3, :] = jnp.sum(grads, axis=0, keepdims=True)

    left_key = jnp.clip((left_from + CHUNK) // CHUNK - 1, 0, MAIN - REACH_CHUNKS)
    right_key = jnp.clip((right_to - 1) // CHUNK - (REACH_CHUNKS - 1), 0, MAIN - REACH_CHUNKS)

    def one_chunk(step, carry):
        slot = step + jnp.where(step >= 2 + half, 1, 0)
        begin = slot * CHUNK

        @pl.when((begin < right_to) & (begin + CHUNK > left_from))
        def _():
            at = pl.ds(pl.multiple_of(begin, CHUNK), CHUNK)
            key = jnp.where(begin < own_at, left_key, right_key) * CHUNK
            q_block = qx_ref[at, :]
            d_block = dx_ref[at, :]
            highest, total, grads = running_sums(
                kx_ref, vx_ref, key, REACH_CHUNKS, q_block, d_block, s_ref, g_ref
            )
            stats_ref[slot, 0:1, :] = highest
            stats_ref[slot, 1:2, :] = total
            stats_ref[slot, 2:3, :] = grads
            near_at = pl.ds(pl.multiple_of(own_at - key, CHUNK), CHUNK)
            sn_ref[slot, :, :] = s_ref[near_at, :]
            gn_ref[slot, :, :] = g_ref[near_at, :]

        return carry

    lax.fori_loop(0, MAIN - 1, one_chunk, 0)


def attend_near(counts, gains, first, quad, second):
    rows = MAIN * CHUNK
    head_rows = jax.ShapeDtypeStruct((rows, LANES), BF16)
    scores = jax.ShapeDtypeStruct((rows, CHUNK), F32)
    tiles = jax.ShapeDtypeStruct((MAIN, CHUNK, CHUNK), F32)
    return pl.pallas_call(
        near_kernel,
        out_shape=(head_rows,) * 4
        + (jax.ShapeDtypeStruct((LANES, rows), BF16),)
        + (scores, scores, tiles, tiles, jax.ShapeDtypeStruct((MAIN + 1, 8, CHUNK), F32)),
        in_specs=[SMEM] + [VMEM] * 4,
        out_specs=(VMEM,) * 10,
        scratch_shapes=[pltpu.VMEM((REACH_CHUNKS * CHUNK, CHUNK), F32)] * 2,
        cost_estimate=pl.CostEstimate(
            flops=9000000000, bytes_accessed=1 << 20, transcendentals=1 << 20
        ),
        compiler_params=pltpu.CompilerParams(vmem_limit_bytes=VMEM_LIMIT),
    )(counts, gains, first, quad, second)


def far_kernel(
    counts_ref,
    gains_ref,
    far_ref,
    quad_ref,
    qx_ref,
    kx_ref,
    vx_ref,
    dx_ref,
    kv_ref,
    so_ref,
    go_ref,
    sn_ref,
    gn_ref,
    stats_ref,
    out_ref,
    qf_ref,
    kf_ref,
    vf_ref,
    df_ref,
    kvf_ref,
    s_ref,
    g_ref,
    p_ref,
    d_ref,
    sums_ref,
    dk_ref,
    dv_ref,
    done_ref,
):
    half, own_at, starts, ends, left_from, right_to = window_facts(counts_ref)
    block_rows = CHUNK // 2
    rows = MAIN * CHUNK
    far_at = jnp.where(half == 0, -CHUNK, rows)
    for block in range(2):
        at = slice(block * block_rows, (block + 1) * block_rows)
        stores = [ref.at[at, :] for ref in (qf_ref, kf_ref, vf_ref, df_ref)]
        place_block(
            far_ref.at[at],
            far_at + block * block_rows,
            starts,
            ends,
            gains_ref,
            stores + [kvf_ref.at[:, at]],
        )

    own_rows = pl.ds(pl.multiple_of(own_at, CHUNK), CHUNK)
    q_own = qx_ref[own_rows, :]
    d_own = dx_ref[own_rows, :]
    scores = rows_dot(kf_ref[...], q_own)
    s_ref[0:CHUNK, :] = scores
    g_ref[0:CHUNK, :] = rows_dot(vf_ref[...], d_own)
    near_highest = stats_ref[MAIN, 0:1, :]
    highest = jnp.max(rows_max(scores), axis=0, keepdims=True) * LOG2_E
    highest = jnp.maximum(near_highest, highest)
    shrink = jnp.exp2(near_highest - highest)
    zeros = jnp.zeros((8, CHUNK), F32)
    total, grads = add_tiles(s_ref, g_ref, CHUNK, highest, zeros, zeros)
    total = jnp.sum(total, axis=0, keepdims=True) + stats_ref[MAIN, 1:2, :] * shrink
    grads = jnp.sum(grads, axis=0, keepdims=True) + stats_ref[MAIN, 2:3, :] * shrink
    scale = 1.0 / total
    mean_grad = grads * scale

    def write_tile(scores, grads, highest, scale, mean_grad, to):
        probs = jnp.exp2(scores * LOG2_E - highest) * scale
        p_ref[to, :] = probs.astype(BF16)
        d_ref[to, :] = (probs * (grads - mean_grad)).astype(BF16)

    near_scale = shrink * scale
    for piece in range(rows // TILE):
        at = slice(piece * TILE, (piece + 1) * TILE)
        probs = so_ref[at, :] * near_scale
        p_ref[at, :] = probs.astype(BF16)
        d_ref[at, :] = (probs * (go_ref[at, :] - mean_grad)).astype(BF16)
    for piece in range(CHUNK // TILE):
        at = slice(piece * TILE, (piece + 1) * TILE)
        to = slice(rows + piece * TILE, rows + (piece + 1) * TILE)
        write_tile(s_ref[at, :], g_ref[at, :], highest, scale, mean_grad, to)
    dk_ref[...] = jnp.dot(d_ref[own_rows, :], q_own, preferred_element_type=F32)
    dv_ref[...] = jnp.dot(p_ref[own_rows, :], d_own, preferred_element_type=F32)

    def times_window(values_ref):
        main = jnp.dot(kv_ref[...], values_ref[0:rows, :], preferred_element_type=F32)
        return main + jnp.dot(
            kvf_ref[...], values_ref[rows : rows + CHUNK, :], preferred_element_type=F32
        )

    upper = lax.broadcasted_iota(jnp.int32, (LANES, CHUNK), 0) < HEAD
    own_out = jnp.where(upper, times_window(d_ref) * INV_ROOT, times_window(p_ref)).T

    query_lane = lax.broadcasted_iota(jnp.int32, (1, CHUNK), 1)
    reaches_far = jnp.where(half == 0, left_from < 0, right_to > rows)

    def add_gradients(tiles, begin, q_block, d_block, highest, total, grads):
        place = query_lane + begin
        scale = jnp.where((place >= left_from) & (place < right_to), 1.0 / total, 0.0)
        mean_grad = grads * scale
        for piece in range(CHUNK // TILE):
            scores, given = tiles(piece)
            at = slice(piece * TILE, (piece + 1) * TILE)
            write_tile(scores, given, highest, scale, mean_grad, at)
        dk_ref[...] += jnp.dot(d_ref[0:CHUNK, :], q_block, preferred_element_type=F32)
        dv_ref[...] += jnp.dot(p_ref[0:CHUNK, :], d_block, preferred_element_type=F32)

    def one_chunk(step, carry):
        slot = step + jnp.where(step >= 2 + half, 1, 0)
        begin = slot * CHUNK

        @pl.when((begin < right_to) & (begin + CHUNK > left_from))
        def _():
            at = pl.ds(pl.multiple_of(begin, CHUNK), CHUNK)
            q_block = qx_ref[at, :]
            d_block = dx_ref[at, :]
            sums_ref[...] = stats_ref[slot, :, :]
            same_side = (begin < own_at) == (half == 0)

            @pl.when(reaches_far & same_side)
            def _():
                scores = rows_dot(kf_ref[...], q_block)
                s_ref[0:CHUNK, :] = scores
                g_ref[0:CHUNK, :] = rows_dot(vf_ref[...], d_block)
                before = sums_ref[0:1, :]
                highest = jnp.max(rows_max(scores), axis=0, keepdims=True) * LOG2_E
                highest = jnp.maximum(before, highest)
                total, grads = add_tiles(s_ref, g_ref, CHUNK, highest, zeros, zeros)
                shrink = jnp.exp2(before - highest)
                sums_ref[0:1, :] = highest
                total = jnp.sum(total, axis=0, keepdims=True)
                grads = jnp.sum(grads, axis=0, keepdims=True)
                sums_ref[1:2, :] = sums_ref[1:2, :] * shrink + total
                sums_ref[2:3, :] = sums_ref[2:3, :] * shrink + grads

            def tiles(piece):
                at = slice(piece * TILE, (piece + 1) * TILE)
                return sn_ref[slot, at, :], gn_ref[slot, at, :]

            add_gradients(
                tiles, begin, q_block, d_block, sums_ref[0:1, :], sums_ref[1:2, :], sums_ref[2:3, :]
            )

        return carry

    lax.fori_loop(0, MAIN - 1, one_chunk, 0)

    @pl.when(reaches_far)
    def _():
        q_block = qf_ref[...]
        d_block = df_ref[...]
        key = half * (MAIN // 2) * CHUNK
        highest = jnp.full((8, CHUNK), -jnp.inf, F32)
        for piece in range(REACH_CHUNKS):
            here = slice(piece * CHUNK, (piece + 1) * CHUNK)
            if piece < REACH_CHUNKS - 1:
                keys_at = pl.ds(pl.multiple_of(key + piece * CHUNK, CHUNK), CHUNK)
                keys, values = kx_ref[keys_at, :], vx_ref[keys_at, :]
            else:
                keys, values = kf_ref[...], vf_ref[...]
            scores = rows_dot(keys, q_block)
            s_ref[here, :] = scores
            highest = jnp.maximum(highest, rows_max(scores))
            g_ref[here, :] = rows_dot(values, d_block)
        highest = jnp.max(highest, axis=0, keepdims=True) * LOG2_E
        total, grads = add_tiles(s_ref, g_ref, REACH_CHUNKS * CHUNK, highest, zeros, zeros)

        def tiles(piece):
            at = pl.ds(pl.multiple_of(own_at - key + piece * TILE, TILE), TILE)
            return s_ref[at, :], g_ref[at, :]

        add_gradients(
            tiles,
            far_at,
            q_block,
            d_block,
            highest,
            jnp.sum(total, axis=0, keepdims=True),
            jnp.sum(grads, axis=0, keepdims=True),
        )

    def norm_grad(raw, gain, d_norm):
        inverse = lax.rsqrt(lower_mean(raw * raw) + EPS)
        scaled = d_norm.astype(BF16).astype(F32) * gain
        inner = lower_mean(raw * scaled)
        return inverse * scaled - raw * (inverse * inverse * inverse * inner)

    low = low_lanes()
    own_in_quad = pl.ds(pl.multiple_of(half * CHUNK, CHUNK), CHUNK)
    raw_q = quad_ref[own_in_quad, 0:LANES].astype(F32)
    raw_k = quad_ref[own_in_quad, LANES:].astype(F32)
    d_q = norm_grad(raw_q, gains_ref[0:1, :], own_out)
    d_k = norm_grad(raw_k, gains_ref[1:2, :], dk_ref[...])
    done_ref[:, 0:LANES] = jnp.where(low, d_q, own_out).astype(BF16)
    done_ref[:, LANES:] = jnp.where(low, d_k, dv_ref[...]).astype(BF16)
    share = 16
    for member in range(out_ref.shape[0]):
        block, core = member // 2, member % 2
        for part in range(out_ref.shape[1] // share):
            begin = (block * 8 + part * 2 + core) * share
            out_ref[member, part * share : (part + 1) * share, :] = done_ref[
                begin : begin + share, :
            ]


def attend_far(counts, gains, far, quad, near_parts):
    return pl.pallas_call(
        far_kernel,
        out_shape=jax.ShapeDtypeStruct((4, CHUNK // 4, 2 * LANES), BF16),
        in_specs=[SMEM] + [VMEM] * (3 + len(near_parts)),
        out_specs=VMEM,
        scratch_shapes=[pltpu.VMEM((CHUNK, LANES), BF16)] * 4
        + [pltpu.VMEM((LANES, CHUNK), BF16)]
        + [pltpu.VMEM((REACH_CHUNKS * CHUNK, CHUNK), F32)] * 2
        + [pltpu.VMEM(((MAIN + 1) * CHUNK, CHUNK), BF16)] * 2
        + [pltpu.VMEM((8, CHUNK), F32)]
        + [pltpu.VMEM((CHUNK, LANES), F32)] * 2
        + [pltpu.VMEM((CHUNK, 2 * LANES), BF16)],
        cost_estimate=pl.CostEstimate(
            flops=9000000000, bytes_accessed=1 << 20, transcendentals=1 << 20
        ),
        compiler_params=pltpu.CompilerParams(vmem_limit_bytes=VMEM_LIMIT),
    )(counts, gains, far, quad, *near_parts)


def project_kernel(parts_ref, weights_ref, weights_far_ref, out_ref):
    rows = parts_ref.shape[1]
    width = weights_ref.shape[1]
    share = out_ref.shape[1]
    core = lax.axis_index("core")
    low = lax.broadcasted_iota(jnp.int32, (rows, LANES), 1) < HEAD

    def by_column(which):
        head0 = parts_ref[which].astype(F32)
        head1 = parts_ref[2 + which].astype(F32)
        a0, a1 = head0[:, :LANES], head1[:, :LANES]
        b0, b1 = head0[:, LANES:], head1[:, LANES:]
        d_q = jnp.where(low, a0, pltpu.roll(a1, HEAD, 1)).astype(BF16)
        attn = jnp.where(low, pltpu.roll(a0, HEAD, 1), a1).astype(BF16)
        d_k = jnp.where(low, b0, pltpu.roll(b1, HEAD, 1)).astype(BF16)
        d_v = jnp.where(low, pltpu.roll(b0, HEAD, 1), b1).astype(BF16)
        return attn, [d_q, d_k, d_v]

    attn, grads = by_column(core)
    attn_far, grads_far = by_column(1 - core)
    mixed = jnp.dot(
        jnp.concatenate([attn, attn_far], axis=1),
        jnp.concatenate([w_out_of(weights_ref), w_out_of(weights_far_ref)], axis=0),
        preferred_element_type=F32,
    ).astype(BF16)
    weights = [ref[part] for ref in (weights_ref, weights_far_ref) for part in range(3)]
    d_hidden = rows_dot(
        jnp.concatenate(grads + grads_far, axis=1), jnp.concatenate(weights, axis=1)
    ).astype(BF16)
    for place in range(out_ref.shape[0]):
        at = slice(place * share, (place + 1) * share)
        out_ref[place, :, :width] = mixed[at]
        out_ref[place, :, width:] = d_hidden[at]


def project(parts, weights, weights_far, x_count):
    return pl.pallas_call(
        project_kernel,
        out_shape=jax.ShapeDtypeStruct(
            (x_count, parts.shape[1] // x_count, 2 * weights.shape[1]), BF16
        ),
        in_specs=[VMEM] * 3,
        out_specs=VMEM,
        compiler_params=pltpu.CompilerParams(vmem_limit_bytes=VMEM_LIMIT),
    )(parts, weights, weights_far)


def ready_kernel(
    counts_ref,
    tokens_ref,
    cotangent_ref,
    modulation_ref,
    rows_ref,
    factors_ref,
):
    rows = rows_ref.shape[1]
    first_row = (lax.axis_index("x") * 2 + lax.axis_index("core")) * rows
    first = block_index() * tokens_ref.shape[0] + first_row
    _, scale, gate = modulation_rows(counts_ref, modulation_ref, first, rows)
    at = pl.ds(pl.multiple_of(first_row, rows), rows)
    normed, inv_std = layer_norm(tokens_ref[at, :].astype(F32))
    rows_ref[0] = tokens_ref[at, :]
    rows_ref[1] = cotangent_ref[at, :]
    factors_ref[0] = gate
    factors_ref[1] = 1.0 + scale
    factors_ref[2] = normed
    factors_ref[3] = jnp.broadcast_to(inv_std, normed.shape)


def ready(counts, tokens, cotangent, modulation, share):
    width = tokens.shape[1]
    return pl.pallas_call(
        ready_kernel,
        out_shape=(
            jax.ShapeDtypeStruct((2, share, width), BF16),
            jax.ShapeDtypeStruct((4, share, width), F32),
        ),
        in_specs=[SMEM] + [VMEM] * 3,
        out_specs=(VMEM, VMEM),
        compiler_params=pltpu.CompilerParams(vmem_limit_bytes=VMEM_LIMIT),
    )(counts, tokens, cotangent, modulation)


def leave_kernel(rows_ref, factors_ref, shares_ref, layer_ref, grad_ref):
    width = layer_ref.shape[1]
    sums = shares_ref[0].astype(F32)
    for share in range(1, shares_ref.shape[0]):
        sums = sums + shares_ref[share].astype(F32)
    layer = rows_ref[0].astype(F32) + factors_ref[0] * sums[:, :width]
    layer_ref[...] = layer.astype(BF16)
    d_normed = sums[:, width:] * factors_ref[1]
    normed = factors_ref[2]
    input_grad = rows_ref[1].astype(F32) + factors_ref[3] * (
        d_normed
        - jnp.mean(d_normed, axis=-1, keepdims=True)
        - normed * jnp.mean(d_normed * normed, axis=-1, keepdims=True)
    )
    grad_ref[...] = input_grad.astype(BF16)


def leave(rows, factors, shares):
    out = jax.ShapeDtypeStruct(rows.shape[1:], BF16)
    return pl.pallas_call(
        leave_kernel,
        out_shape=(out, out),
        in_specs=[VMEM] * 3,
        out_specs=(VMEM, VMEM),
        compiler_params=pltpu.CompilerParams(vmem_limit_bytes=VMEM_LIMIT),
    )(rows, factors, shares)


def per_device(tokens, cotangent, w_qkv, w_out, qk_gain, modulation, image_counts):
    tok_rows, model_width = tokens.shape
    z_count = lax.axis_size("z")
    x_count = lax.axis_size("x")
    quad = 4
    pair_rows = 2 * tok_rows
    share = tok_rows // (2 * x_count)
    w_parts = w_qkv.transpose(1, 0, 2)
    mod_parts = modulation.transpose(1, 0, 2)
    gains = jnp.pad(qk_gain, ((0, 6), (0, LANES - HEAD)))

    heads = enter(image_counts, tokens, cotangent, w_parts, w_out, mod_parts, quad)
    mine = lax.all_to_all(heads, ("yh", "yl"), 0, 0)
    mine = mine.reshape(quad * tok_rows, 2 * LANES)
    evens = range(0, z_count, 2)
    swaps = [(i, i + 1) for i in evens], [((i - 1) % z_count, i) for i in evens]
    first, second = (
        lax.ppermute(mine, "z", pairs + [(j, i) for i, j in pairs]) for pairs in swaps
    )
    halves = 4 * z_count
    far_half = jnp.where(
        lax.axis_index("yh") == lax.axis_index("core"), mine[pair_rows:], mine[:pair_rows]
    )

    def far_source(target):
        z, yh, core = target // 4, target // 2 % 2, target % 2
        return (z + (2 if yh else -2)) % z_count * 4 + (yh ^ core) * 2 + core

    far = lax.ppermute(
        far_half, ("z", "yh", "core"), [(far_source(i), i) for i in range(halves)]
    )
    _, tokens_late, cotangent_late, mod_late = lax.optimization_barrier(
        (mine, tokens, cotangent, mod_parts)
    )
    rows, factors = ready(image_counts, tokens_late, cotangent_late, mod_late, share)
    first, rows, factors = lax.optimization_barrier((first, rows, factors))
    near_parts = attend_near(image_counts, gains, first, mine, second)
    _, w_parts_late, w_out_late = lax.optimization_barrier((mine, w_parts, w_out))
    weights = pack(w_parts_late, w_out_late)
    weights_far = lax.ppermute(weights, "core", [(0, 1), (1, 0)])
    parts = attend_far(image_counts, gains, far, mine, near_parts)
    parts = lax.all_to_all(parts, ("yl", "core"), 0, 0)
    partial = project(parts, weights, weights_far, x_count)
    shares = lax.all_to_all(partial, "x", 0, 0)
    return leave(rows, factors, shares)


def solution(mesh):
    split = jax.sharding.Mesh(mesh.devices.reshape(16, 2, 2, 4, 2), ("z", "yh", "yl", "x", "core"))
    dp, head = ("z", "yh", "yl"), ("x", "core")
    in_specs = (P(dp, None), P(dp, None), P(None, None, head), P(head, None), P(), P(), P())
    out_specs = (P(dp + head, None), P(dp + head, None))
    return jax.shard_map(
        per_device, mesh=split, in_specs=in_specs, out_specs=out_specs, check_vma=False
    )
```

```python
import math

import jax
import jax.numpy as jnp
from jax import lax
from jax.experimental import pallas as pl
from jax.experimental.pallas import tpu as pltpu
from jax.sharding import PartitionSpec as P

EPS = 1e-06
SAME_IMAGE = 512.0
LANES = 128
HEAD = 64
F32 = jnp.float32
BF16 = jnp.bfloat16
VMEM_LIMIT = 24 * 1024 * 1024
ENTER_LIMIT = 60 * 1024 * 1024
VMEM = pl.BlockSpec(memory_space=pltpu.VMEM)
SMEM = pl.BlockSpec(memory_space=pltpu.SMEM)


def rows_dot(a, b):
    return lax.dot_general(a, b, (((1,), (1,)), ((), ())), preferred_element_type=F32)


def block_index():
    return (lax.axis_index("z") * 2 + lax.axis_index("yh")) * 2 + lax.axis_index("yl")


def image_bounds(counts_ref, first_lane):
    lane = lax.broadcasted_iota(jnp.int32, (1, LANES), 1)
    starts = jnp.zeros((1, LANES), jnp.int32)
    ends = jnp.zeros((1, LANES), jnp.int32)
    total = jnp.int32(0)
    for image in range(counts_ref.shape[0]):
        here = lane == first_lane + image
        starts = jnp.where(here, total, starts)
        total = total + counts_ref[image]
        ends = jnp.where(here, total, ends)
    return starts, ends


def modulation_rows(counts_ref, modulation_ref, first, rows):
    starts, ends = image_bounds(counts_ref, 0)
    place = first + lax.broadcasted_iota(jnp.int32, (rows, LANES), 0)
    member = ((place >= starts) & (place < ends)).astype(F32).astype(BF16)
    member = member[:, : modulation_ref.shape[1]]
    return [
        jnp.dot(member, modulation_ref[part], preferred_element_type=F32) for part in range(3)
    ]


def layer_norm(values):
    average = jnp.mean(values, axis=-1, keepdims=True)
    centred = values - average
    inv_std = lax.rsqrt(jnp.mean(centred * centred, axis=-1, keepdims=True) + EPS)
    return centred * inv_std, inv_std


def enter_kernel(
    counts_ref, tokens_ref, cotangent_ref, w_qkv_ref, w_out_ref, modulation_ref, out_ref
):
    rows = tokens_ref.shape[0]
    first = block_index() * rows
    shift, scale, gate = modulation_rows(counts_ref, modulation_ref, first, rows)
    normed, _ = layer_norm(tokens_ref[...].astype(F32))
    hidden = (normed * (1.0 + scale) + shift).astype(BF16)
    weights = jnp.concatenate([w_qkv_ref[part] for part in range(3)], axis=1)
    qkv = jnp.dot(hidden, weights, preferred_element_type=F32)
    q, k, v = (qkv[:, part * LANES : (part + 1) * LANES] for part in range(3))
    d_mixed = (cotangent_ref[...].astype(F32) * gate).astype(BF16)
    d_attn = rows_dot(d_mixed, w_out_ref[...])
    low = lax.broadcasted_iota(jnp.int32, (rows, LANES), 1) < HEAD

    def beside(left, right):
        return jnp.where(low, left, right).astype(BF16)

    q_v = (beside(q, pltpu.roll(v, HEAD, 1)), beside(pltpu.roll(q, HEAD, 1), v))
    k_d = (beside(k, pltpu.roll(d_attn, HEAD, 1)), beside(pltpu.roll(k, HEAD, 1), d_attn))
    for place in range(out_ref.shape[0]):
        out_ref[place, :, 0:LANES] = q_v[place % 2]
        out_ref[place, :, LANES:] = k_d[place % 2]


def enter(counts, tokens, cotangent, w_parts, w_out, modulation, quad):
    return pl.pallas_call(
        enter_kernel,
        out_shape=jax.ShapeDtypeStruct((quad, tokens.shape[0], 2 * LANES), BF16),
        in_specs=[SMEM] + [VMEM] * 5,
        out_specs=VMEM,
        compiler_params=pltpu.CompilerParams(vmem_limit_bytes=ENTER_LIMIT),
    )(counts, tokens, cotangent, w_parts, w_out, modulation)


def pack_kernel(w_qkv_ref, w_out_ref, weights_ref, sems):
    pairs = [(w_qkv_ref, weights_ref.at[0:3])]
    for tile in range(weights_ref.shape[1] // LANES):
        at = slice(tile * LANES, (tile + 1) * LANES)
        pairs.append((w_out_ref.at[:, at], weights_ref.at[3, at, :]))
    copies = [
        pltpu.make_async_copy(source, target, sems.at[place])
        for place, (source, target) in enumerate(pairs)
    ]
    for copy in copies:
        copy.start()
    for copy in copies:
        copy.wait()


def pack(w_parts, w_out):
    width = w_out.shape[1]
    whole = pl.BlockSpec(memory_space=pl.ANY)
    return pl.pallas_call(
        pack_kernel,
        out_shape=jax.ShapeDtypeStruct((4, width, LANES), BF16),
        in_specs=[whole] * 2,
        out_specs=VMEM,
        scratch_shapes=[pltpu.SemaphoreType.DMA((1 + width // LANES,))],
        compiler_params=pltpu.CompilerParams(vmem_limit_bytes=8 * 1024 * 1024),
    )(w_parts, w_out)


def w_out_of(weights_ref):
    tiles = weights_ref.shape[1] // LANES
    return jnp.concatenate(
        [weights_ref[3, tile * LANES : (tile + 1) * LANES, :] for tile in range(tiles)], axis=1
    )


LOG2_E = math.log2(math.e)
INV_ROOT = 1.0 / math.sqrt(HEAD)
CHUNK = 256
TILE = 64
MAIN = 6
REACH_CHUNKS = 4


def low_lanes():
    return lax.broadcasted_iota(jnp.int32, (1, LANES), 1) < HEAD


def lower_mean(values):
    return jnp.sum(jnp.where(low_lanes(), values, 0.0), axis=-1, keepdims=True) * (1.0 / HEAD)


def lower_sums(values):
    ones = (lax.broadcasted_iota(jnp.int32, (LANES, LANES), 0) < HEAD).astype(F32).astype(BF16)
    squares = values * values
    large = squares.astype(BF16)
    small = (squares - large.astype(F32)).astype(BF16)
    large = jnp.dot(large, ones, preferred_element_type=F32)
    return large + jnp.dot(small, ones, preferred_element_type=F32)


def place_block(source, place, starts, ends, gains_ref, stores):
    low = low_lanes()
    rows = source.shape[0]
    at = place + lax.broadcasted_iota(jnp.int32, (rows, LANES), 0)
    same = ((at >= starts) & (at < ends)).astype(F32)
    first = source[:, 0:LANES].astype(F32)
    second = source[:, LANES:].astype(F32)

    def normed(raw, gain):
        return raw * lax.rsqrt(lower_sums(raw) * (1.0 / HEAD) + EPS) * gain

    keys = normed(second, gains_ref[1:2, :])
    queries = normed(first, gains_ref[0:1, :] * INV_ROOT)
    q_store, k_store, v_store, d_store, kv_store = stores
    q_store[...] = jnp.where(low, queries, same * SAME_IMAGE).astype(BF16)
    k_store[...] = jnp.where(low, keys, same).astype(BF16)
    v_store[...] = jnp.where(low, 0.0, first).astype(BF16)
    d_store[...] = source[:, LANES:]
    kv_store[...] = jnp.where(low, keys, first).astype(BF16).T


def window_facts(counts_ref):
    half = lax.axis_index("yh")
    origin = (block_index() // 4 - 1) * 2 * CHUNK
    own_at = (2 + half) * CHUNK
    starts, ends = image_bounds(counts_ref, HEAD)
    left_from = jnp.int32(-CHUNK)
    right_to = jnp.int32((MAIN + 1) * CHUNK)
    total = -origin
    for image in range(counts_ref.shape[0]):
        left_from = jnp.where(total <= own_at, total, left_from)
        ended = total >= own_at + CHUNK
        total = total + counts_ref[image]
        right_to = jnp.where((total >= own_at + CHUNK) & jnp.logical_not(ended), total, right_to)
    return half, own_at, starts - origin, ends - origin, left_from, right_to


def by_eight(values):
    return values.reshape(values.shape[0] // 8, 8, values.shape[1])


def add_tiles(s_ref, g_ref, rows, highest, total, grads):
    for piece in range(rows // TILE):
        at = slice(piece * TILE, (piece + 1) * TILE)
        weights = jnp.exp2(s_ref[at, :] * LOG2_E - highest)
        total = total + jnp.sum(by_eight(weights), axis=0)
        grads = grads + jnp.sum(by_eight(weights * g_ref[at, :]), axis=0)
    return total, grads


def rows_max(values):
    return jnp.max(by_eight(values), axis=0)


def chunks_from(key, count, *refs):
    rows = [pl.ds(pl.multiple_of(key + i * CHUNK, CHUNK), CHUNK) for i in range(count)]
    return [tuple(ref.at[at, :] for ref in refs) for at in rows]


def running_sums(pieces, q_block, d_block, s_ref, g_ref):
    highest = jnp.full((8, CHUNK), -jnp.inf, F32)
    total = jnp.zeros((8, CHUNK), F32)
    grads = jnp.zeros((8, CHUNK), F32)
    for piece, (keys_ref, values_ref) in enumerate(pieces):
        here = slice(piece * CHUNK, (piece + 1) * CHUNK)
        scores = rows_dot(keys_ref[...], q_block)
        s_ref[here, :] = scores
        g_ref[here, :] = rows_dot(values_ref[...], d_block)
        higher = jnp.maximum(highest, rows_max(scores) * LOG2_E)
        shrink = jnp.exp2(highest - higher)
        total = total * shrink
        grads = grads * shrink
        highest = higher
        for tile in range(CHUNK // TILE):
            at = slice(piece * CHUNK + tile * TILE, piece * CHUNK + (tile + 1) * TILE)
            weights = jnp.exp2(by_eight(s_ref[at, :]) * LOG2_E - highest[None])
            total = total + jnp.sum(weights, axis=0)
            grads = grads + jnp.sum(weights * by_eight(g_ref[at, :]), axis=0)
    top = jnp.max(highest, axis=0, keepdims=True)
    shrink = jnp.exp2(highest - top)
    total = jnp.sum(total * shrink, axis=0, keepdims=True)
    return top, total, jnp.sum(grads * shrink, axis=0, keepdims=True)


def near_kernel(
    counts_ref,
    gains_ref,
    first_ref,
    quad_ref,
    second_ref,
    qx_ref,
    kx_ref,
    vx_ref,
    dx_ref,
    kv_ref,
    so_ref,
    go_ref,
    sn_ref,
    gn_ref,
    stats_ref,
    s_ref,
    g_ref,
):
    half, own_at, starts, ends, left_from, right_to = window_facts(counts_ref)
    block_rows = CHUNK // 2

    def place(source, begin):
        begin = pl.multiple_of(begin, block_rows)
        at = pl.ds(begin, block_rows)
        stores = [ref.at[at, :] for ref in (qx_ref, kx_ref, vx_ref, dx_ref)]
        place_block(source, begin, starts, ends, gains_ref, stores + [kv_ref.at[:, at]])

    to_first = jnp.where(lax.rem(lax.axis_index("z"), 2) == 0, 2 * CHUNK, -2 * CHUNK)
    for block in range(4):
        at = slice(block * block_rows, (block + 1) * block_rows)
        begin = 2 * CHUNK + block * block_rows
        place(quad_ref.at[at], begin)
        place(first_ref.at[at], begin + to_first)
        place(second_ref.at[at], begin - to_first)

    own_rows = pl.ds(pl.multiple_of(own_at, CHUNK), CHUNK)
    q_own = qx_ref[own_rows, :]
    d_own = dx_ref[own_rows, :]
    highest = jnp.full((8, CHUNK), -jnp.inf, F32)
    for piece in range(MAIN):
        at = slice(piece * CHUNK, (piece + 1) * CHUNK)
        scores = rows_dot(kx_ref[at, :], q_own)
        so_ref[at, :] = scores
        highest = jnp.maximum(highest, rows_max(scores))
        go_ref[at, :] = rows_dot(vx_ref[at, :], d_own)
    highest = jnp.max(highest, axis=0, keepdims=True) * LOG2_E
    total = jnp.zeros((8, CHUNK), F32)
    grads = jnp.zeros((8, CHUNK), F32)
    for piece in range(MAIN * CHUNK // TILE):
        at = slice(piece * TILE, (piece + 1) * TILE)
        weights = jnp.exp2(so_ref[at, :] * LOG2_E - highest)
        so_ref[at, :] = weights
        total = total + jnp.sum(by_eight(weights), axis=0)
        grads = grads + jnp.sum(by_eight(weights * go_ref[at, :]), axis=0)
    stats_ref[MAIN, 0:1, :] = highest
    stats_ref[MAIN, 1:2, :] = jnp.sum(total, axis=0, keepdims=True)
    stats_ref[MAIN, 2:3, :] = jnp.sum(grads, axis=0, keepdims=True)

    left_key = jnp.clip((left_from + CHUNK) // CHUNK - 1, 0, MAIN - REACH_CHUNKS)
    right_key = jnp.clip((right_to - 1) // CHUNK - (REACH_CHUNKS - 1), 0, MAIN - REACH_CHUNKS)

    def one_chunk(step, carry):
        slot = step + jnp.where(step >= 2 + half, 1, 0)
        begin = slot * CHUNK

        @pl.when((begin < right_to) & (begin + CHUNK > left_from))
        def _():
            at = pl.ds(pl.multiple_of(begin, CHUNK), CHUNK)
            key = jnp.where(begin < own_at, left_key, right_key) * CHUNK
            q_block = qx_ref[at, :]
            d_block = dx_ref[at, :]
            pieces = chunks_from(key, REACH_CHUNKS, kx_ref, vx_ref)
            highest, total, grads = running_sums(pieces, q_block, d_block, s_ref, g_ref)
            stats_ref[slot, 0:1, :] = highest
            stats_ref[slot, 1:2, :] = total
            stats_ref[slot, 2:3, :] = grads
            near_at = pl.ds(pl.multiple_of(own_at - key, CHUNK), CHUNK)
            sn_ref[slot, :, :] = s_ref[near_at, :]
            gn_ref[slot, :, :] = g_ref[near_at, :]

        return carry

    lax.fori_loop(0, MAIN - 1, one_chunk, 0)


def attend_near(counts, gains, first, quad, second):
    rows = MAIN * CHUNK
    head_rows = jax.ShapeDtypeStruct((rows, LANES), BF16)
    scores = jax.ShapeDtypeStruct((rows, CHUNK), F32)
    tiles = jax.ShapeDtypeStruct((MAIN, CHUNK, CHUNK), F32)
    return pl.pallas_call(
        near_kernel,
        out_shape=(head_rows,) * 4
        + (jax.ShapeDtypeStruct((LANES, rows), BF16),)
        + (scores, scores, tiles, tiles, jax.ShapeDtypeStruct((MAIN + 1, 8, CHUNK), F32)),
        in_specs=[SMEM] + [VMEM] * 4,
        out_specs=(VMEM,) * 10,
        scratch_shapes=[pltpu.VMEM((REACH_CHUNKS * CHUNK, CHUNK), F32)] * 2,
        cost_estimate=pl.CostEstimate(
            flops=9000000000, bytes_accessed=1 << 20, transcendentals=1 << 20
        ),
        compiler_params=pltpu.CompilerParams(vmem_limit_bytes=VMEM_LIMIT),
    )(counts, gains, first, quad, second)


def far_kernel(
    counts_ref,
    gains_ref,
    far_ref,
    quad_ref,
    qx_ref,
    kx_ref,
    vx_ref,
    dx_ref,
    kv_ref,
    so_ref,
    go_ref,
    sn_ref,
    gn_ref,
    stats_ref,
    out_ref,
    qf_ref,
    kf_ref,
    vf_ref,
    df_ref,
    kvf_ref,
    s_ref,
    g_ref,
    p_ref,
    d_ref,
    pn_ref,
    dn_ref,
    sums_ref,
    dk_ref,
    dv_ref,
    own_out_ref,
    done_ref,
):
    half, own_at, starts, ends, left_from, right_to = window_facts(counts_ref)
    block_rows = CHUNK // 2
    rows = MAIN * CHUNK
    far_at = jnp.where(half == 0, -CHUNK, rows)
    for block in range(2):
        at = slice(block * block_rows, (block + 1) * block_rows)
        stores = [ref.at[at, :] for ref in (qf_ref, kf_ref, vf_ref, df_ref)]
        place_block(
            far_ref.at[at],
            far_at + block * block_rows,
            starts,
            ends,
            gains_ref,
            stores + [kvf_ref.at[:, at]],
        )

    own_rows = pl.ds(pl.multiple_of(own_at, CHUNK), CHUNK)
    q_own = qx_ref[own_rows, :]
    d_own = dx_ref[own_rows, :]
    scores = rows_dot(kf_ref[...], q_own)
    s_ref[0:CHUNK, :] = scores
    g_ref[0:CHUNK, :] = rows_dot(vf_ref[...], d_own)
    near_highest = stats_ref[MAIN, 0:1, :]
    highest = jnp.max(rows_max(scores), axis=0, keepdims=True) * LOG2_E
    highest = jnp.maximum(near_highest, highest)
    shrink = jnp.exp2(near_highest - highest)
    zeros = jnp.zeros((8, CHUNK), F32)
    total, grads = add_tiles(s_ref, g_ref, CHUNK, highest, zeros, zeros)
    total = jnp.sum(total, axis=0, keepdims=True) + stats_ref[MAIN, 1:2, :] * shrink
    grads = jnp.sum(grads, axis=0, keepdims=True) + stats_ref[MAIN, 2:3, :] * shrink
    scale = 1.0 / total
    mean_grad = grads * scale

    near_scale = shrink * scale
    for piece in range(rows // TILE):
        at = slice(piece * TILE, (piece + 1) * TILE)
        probs = so_ref[at, :] * near_scale
        p_ref[at, :] = probs.astype(BF16)
        d_ref[at, :] = (probs * (go_ref[at, :] - mean_grad)).astype(BF16)
    for piece in range(CHUNK // TILE):
        at = slice(piece * TILE, (piece + 1) * TILE)
        to = slice(rows + piece * TILE, rows + (piece + 1) * TILE)
        probs = jnp.exp2(s_ref[at, :] * LOG2_E - highest) * scale
        p_ref[to, :] = probs.astype(BF16)
        d_ref[to, :] = (probs * (g_ref[at, :] - mean_grad)).astype(BF16)
    pn_ref[:, own_rows] = p_ref[own_rows, :]
    dn_ref[:, own_rows] = d_ref[own_rows, :]

    def times_window(values_ref):
        main = jnp.dot(kv_ref[...], values_ref[0:rows, :], preferred_element_type=F32)
        return main + jnp.dot(
            kvf_ref[...], values_ref[rows : rows + CHUNK, :], preferred_element_type=F32
        )

    upper = lax.broadcasted_iota(jnp.int32, (LANES, CHUNK), 0) < HEAD
    own_out_ref[...] = jnp.where(
        upper, times_window(d_ref) * INV_ROOT, times_window(p_ref)
    ).T

    query_lane = lax.broadcasted_iota(jnp.int32, (1, CHUNK), 1)
    reaches_far = jnp.where(half == 0, left_from < 0, right_to > rows)
    sums_ref[...] = stats_ref[...]
    dk_ref[...] = jnp.zeros_like(dk_ref)
    dv_ref[...] = jnp.zeros_like(dv_ref)

    @pl.when(reaches_far)
    def _():
        for step in range(2):
            slot = half * (MAIN - 2) + step
            at = pl.ds(pl.multiple_of(slot * CHUNK, CHUNK), CHUNK)
            space = pl.ds((REACH_CHUNKS + step) * CHUNK, CHUNK)
            highest, total, grads = running_sums(
                [(kf_ref, vf_ref)], qx_ref[at, :], dx_ref[at, :], s_ref.at[space], g_ref.at[space]
            )
            before = sums_ref[slot, 0:1, :]
            higher = jnp.maximum(before, highest)
            old = jnp.exp2(before - higher)
            new = jnp.exp2(highest - higher)
            sums_ref[slot, 0:1, :] = higher
            sums_ref[slot, 1:2, :] = sums_ref[slot, 1:2, :] * old + total * new
            sums_ref[slot, 2:3, :] = sums_ref[slot, 2:3, :] * old + grads * new

        q_block = qf_ref[...]
        d_block = df_ref[...]
        key = half * (MAIN // 2) * CHUNK
        pieces = chunks_from(key, REACH_CHUNKS - 1, kx_ref, vx_ref) + [(kf_ref, vf_ref)]
        highest, total, grads = running_sums(pieces, q_block, d_block, s_ref, g_ref)
        place = query_lane + far_at
        scale = jnp.where((place >= left_from) & (place < right_to), 1.0 / total, 0.0)
        mean_grad = grads * scale
        for piece in range(CHUNK // TILE):
            at = slice(piece * TILE, (piece + 1) * TILE)
            near_at = pl.ds(pl.multiple_of(own_at - key + piece * TILE, TILE), TILE)
            probs = jnp.exp2(s_ref[near_at, :] * LOG2_E - highest) * scale
            p_ref[at, :] = probs.astype(BF16)
            d_ref[at, :] = (probs * (g_ref[near_at, :] - mean_grad)).astype(BF16)
        dk_ref[...] = jnp.dot(d_ref[0:CHUNK, :], q_block, preferred_element_type=F32)
        dv_ref[...] = jnp.dot(p_ref[0:CHUNK, :], d_block, preferred_element_type=F32)

    for step in range(MAIN - 1):
        slot = step + jnp.where(step >= 2 + half, 1, 0)
        begin = slot * CHUNK
        chunk_at = pl.ds(pl.multiple_of(begin, CHUNK), CHUNK)
        place = query_lane + begin
        valid = (place >= left_from) & (place < right_to)
        highest = sums_ref[slot, 0:1, :]
        scale = 1.0 / sums_ref[slot, 1:2, :]
        mean_grad = sums_ref[slot, 2:3, :] * scale
        for piece in range(CHUNK // TILE):
            at = slice(piece * TILE, (piece + 1) * TILE)
            probs = jnp.exp2(sn_ref[slot, at, :] * LOG2_E - highest) * scale
            d_scores = probs * (gn_ref[slot, at, :] - mean_grad)
            pn_ref[at, chunk_at] = jnp.where(valid, probs, 0.0).astype(BF16)
            dn_ref[at, chunk_at] = jnp.where(valid, d_scores, 0.0).astype(BF16)
    d_key = dk_ref[...] + jnp.dot(dn_ref[...], qx_ref[...], preferred_element_type=F32)
    d_value = dv_ref[...] + jnp.dot(pn_ref[...], dx_ref[...], preferred_element_type=F32)
    own_out = own_out_ref[...]

    def norm_grad(raw, gain, d_norm):
        inverse = lax.rsqrt(lower_mean(raw * raw) + EPS)
        scaled = d_norm.astype(BF16).astype(F32) * gain
        inner = lower_mean(raw * scaled)
        return inverse * scaled - raw * (inverse * inverse * inverse * inner)

    low = low_lanes()
    own_in_quad = pl.ds(pl.multiple_of(half * CHUNK, CHUNK), CHUNK)
    raw_q = quad_ref[own_in_quad, 0:LANES].astype(F32)
    raw_k = quad_ref[own_in_quad, LANES:].astype(F32)
    d_q = norm_grad(raw_q, gains_ref[0:1, :], own_out)
    d_k = norm_grad(raw_k, gains_ref[1:2, :], d_key)
    done_ref[:, 0:LANES] = jnp.where(low, d_q, own_out).astype(BF16)
    done_ref[:, LANES:] = jnp.where(low, d_k, d_value).astype(BF16)
    share = 16
    for member in range(out_ref.shape[0]):
        block, core = member // 2, member % 2
        for part in range(out_ref.shape[1] // share):
            begin = (block * 8 + part * 2 + core) * share
            out_ref[member, part * share : (part + 1) * share, :] = done_ref[
                begin : begin + share, :
            ]


def attend_far(counts, gains, far, quad, near_parts):
    return pl.pallas_call(
        far_kernel,
        out_shape=jax.ShapeDtypeStruct((4, CHUNK // 4, 2 * LANES), BF16),
        in_specs=[SMEM] + [VMEM] * (3 + len(near_parts)),
        out_specs=VMEM,
        scratch_shapes=[pltpu.VMEM((CHUNK, LANES), BF16)] * 4
        + [pltpu.VMEM((LANES, CHUNK), BF16)]
        + [pltpu.VMEM(((REACH_CHUNKS + 2) * CHUNK, CHUNK), F32)] * 2
        + [pltpu.VMEM(((MAIN + 1) * CHUNK, CHUNK), BF16)] * 2
        + [pltpu.VMEM((CHUNK, MAIN * CHUNK), BF16)] * 2
        + [pltpu.VMEM((MAIN + 1, 8, CHUNK), F32)]
        + [pltpu.VMEM((CHUNK, LANES), F32)] * 3
        + [pltpu.VMEM((CHUNK, 2 * LANES), BF16)],
        cost_estimate=pl.CostEstimate(
            flops=9000000000, bytes_accessed=1 << 20, transcendentals=1 << 20
        ),
        compiler_params=pltpu.CompilerParams(vmem_limit_bytes=VMEM_LIMIT),
    )(counts, gains, far, quad, *near_parts)


def project_kernel(parts_ref, weights_ref, weights_far_ref, out_ref):
    rows = parts_ref.shape[1]
    width = weights_ref.shape[1]
    share = out_ref.shape[1]
    core = lax.axis_index("core")
    low = lax.broadcasted_iota(jnp.int32, (rows, LANES), 1) < HEAD

    def by_column(which):
        head0 = parts_ref[which].astype(F32)
        head1 = parts_ref[2 + which].astype(F32)
        a0, a1 = head0[:, :LANES], head1[:, :LANES]
        b0, b1 = head0[:, LANES:], head1[:, LANES:]
        d_q = jnp.where(low, a0, pltpu.roll(a1, HEAD, 1)).astype(BF16)
        attn = jnp.where(low, pltpu.roll(a0, HEAD, 1), a1).astype(BF16)
        d_k = jnp.where(low, b0, pltpu.roll(b1, HEAD, 1)).astype(BF16)
        d_v = jnp.where(low, pltpu.roll(b0, HEAD, 1), b1).astype(BF16)
        return attn, [d_q, d_k, d_v]

    attn, grads = by_column(core)
    attn_far, grads_far = by_column(1 - core)
    mixed = jnp.dot(
        jnp.concatenate([attn, attn_far], axis=1),
        jnp.concatenate([w_out_of(weights_ref), w_out_of(weights_far_ref)], axis=0),
        preferred_element_type=F32,
    ).astype(BF16)
    weights = [ref[part] for ref in (weights_ref, weights_far_ref) for part in range(3)]
    d_hidden = rows_dot(
        jnp.concatenate(grads + grads_far, axis=1), jnp.concatenate(weights, axis=1)
    ).astype(BF16)
    for place in range(out_ref.shape[0]):
        at = slice(place * share, (place + 1) * share)
        out_ref[place, :, :width] = mixed[at]
        out_ref[place, :, width:] = d_hidden[at]


def project(parts, weights, weights_far, x_count):
    return pl.pallas_call(
        project_kernel,
        out_shape=jax.ShapeDtypeStruct(
            (x_count, parts.shape[1] // x_count, 2 * weights.shape[1]), BF16
        ),
        in_specs=[VMEM] * 3,
        out_specs=VMEM,
        compiler_params=pltpu.CompilerParams(vmem_limit_bytes=VMEM_LIMIT),
    )(parts, weights, weights_far)


def ready_kernel(
    counts_ref,
    tokens_ref,
    cotangent_ref,
    modulation_ref,
    rows_ref,
    factors_ref,
):
    rows = rows_ref.shape[1]
    first_row = (lax.axis_index("x") * 2 + lax.axis_index("core")) * rows
    first = block_index() * tokens_ref.shape[0] + first_row
    _, scale, gate = modulation_rows(counts_ref, modulation_ref, first, rows)
    at = pl.ds(pl.multiple_of(first_row, rows), rows)
    normed, inv_std = layer_norm(tokens_ref[at, :].astype(F32))
    rows_ref[0] = tokens_ref[at, :]
    rows_ref[1] = cotangent_ref[at, :]
    factors_ref[0] = gate
    factors_ref[1] = 1.0 + scale
    factors_ref[2] = normed
    factors_ref[3] = jnp.broadcast_to(inv_std, normed.shape)


def ready(counts, tokens, cotangent, modulation, share):
    width = tokens.shape[1]
    return pl.pallas_call(
        ready_kernel,
        out_shape=(
            jax.ShapeDtypeStruct((2, share, width), BF16),
            jax.ShapeDtypeStruct((4, share, width), F32),
        ),
        in_specs=[SMEM] + [VMEM] * 3,
        out_specs=(VMEM, VMEM),
        compiler_params=pltpu.CompilerParams(vmem_limit_bytes=VMEM_LIMIT),
    )(counts, tokens, cotangent, modulation)


def leave_kernel(rows_ref, factors_ref, shares_ref, layer_ref, grad_ref):
    width = layer_ref.shape[1]
    sums = shares_ref[0].astype(F32)
    for share in range(1, shares_ref.shape[0]):
        sums = sums + shares_ref[share].astype(F32)
    layer = rows_ref[0].astype(F32) + factors_ref[0] * sums[:, :width]
    layer_ref[...] = layer.astype(BF16)
    d_normed = sums[:, width:] * factors_ref[1]
    normed = factors_ref[2]
    input_grad = rows_ref[1].astype(F32) + factors_ref[3] * (
        d_normed
        - jnp.mean(d_normed, axis=-1, keepdims=True)
        - normed * jnp.mean(d_normed * normed, axis=-1, keepdims=True)
    )
    grad_ref[...] = input_grad.astype(BF16)


def leave(rows, factors, shares):
    out = jax.ShapeDtypeStruct(rows.shape[1:], BF16)
    return pl.pallas_call(
        leave_kernel,
        out_shape=(out, out),
        in_specs=[VMEM] * 3,
        out_specs=(VMEM, VMEM),
        compiler_params=pltpu.CompilerParams(vmem_limit_bytes=VMEM_LIMIT),
    )(rows, factors, shares)


def per_device(tokens, cotangent, w_qkv, w_out, qk_gain, modulation, image_counts):
    tok_rows, model_width = tokens.shape
    z_count = lax.axis_size("z")
    x_count = lax.axis_size("x")
    quad = 4
    pair_rows = 2 * tok_rows
    share = tok_rows // (2 * x_count)
    w_parts = w_qkv.transpose(1, 0, 2)
    mod_parts = modulation.transpose(1, 0, 2)
    gains = jnp.pad(qk_gain, ((0, 6), (0, LANES - HEAD)))

    heads = enter(image_counts, tokens, cotangent, w_parts, w_out, mod_parts, quad)
    mine = lax.all_to_all(heads, ("yh", "yl"), 0, 0)
    mine = mine.reshape(quad * tok_rows, 2 * LANES)
    evens = range(0, z_count, 2)
    swaps = [(i, i + 1) for i in evens], [((i - 1) % z_count, i) for i in evens]
    first, second = (
        lax.ppermute(mine, "z", pairs + [(j, i) for i, j in pairs]) for pairs in swaps
    )
    halves = 4 * z_count
    far_half = jnp.where(
        lax.axis_index("yh") == lax.axis_index("core"), mine[pair_rows:], mine[:pair_rows]
    )

    def far_source(target):
        z, yh, core = target // 4, target // 2 % 2, target % 2
        return (z + (2 if yh else -2)) % z_count * 4 + (yh ^ core) * 2 + core

    far = lax.ppermute(
        far_half, ("z", "yh", "core"), [(far_source(i), i) for i in range(halves)]
    )
    _, tokens_late, cotangent_late, mod_late = lax.optimization_barrier(
        (mine, tokens, cotangent, mod_parts)
    )
    rows, factors = ready(image_counts, tokens_late, cotangent_late, mod_late, share)
    first, rows, factors = lax.optimization_barrier((first, rows, factors))
    near_parts = attend_near(image_counts, gains, first, mine, second)
    _, w_parts_late, w_out_late = lax.optimization_barrier((mine, w_parts, w_out))
    weights = pack(w_parts_late, w_out_late)
    weights_far = lax.ppermute(weights, "core", [(0, 1), (1, 0)])
    parts = attend_far(image_counts, gains, far, mine, near_parts)
    parts = lax.all_to_all(parts, ("yl", "core"), 0, 0)
    partial = project(parts, weights, weights_far, x_count)
    shares = lax.all_to_all(partial, "x", 0, 0)
    return leave(rows, factors, shares)


def solution(mesh):
    split = jax.sharding.Mesh(mesh.devices.reshape(16, 2, 2, 4, 2), ("z", "yh", "yl", "x", "core"))
    dp, head = ("z", "yh", "yl"), ("x", "core")
    in_specs = (P(dp, None), P(dp, None), P(None, None, head), P(head, None), P(), P(), P())
    out_specs = (P(dp + head, None), P(dp + head, None))
    return jax.shard_map(
        per_device, mesh=split, in_specs=in_specs, out_specs=out_specs, check_vma=False
    )
```

```python
import math

import jax
import jax.numpy as jnp
from jax import lax
from jax.experimental import pallas as pl
from jax.experimental.pallas import tpu as pltpu
from jax.sharding import PartitionSpec as P

EPS = 1e-06
SAME_IMAGE = 512.0
LANES = 128
HEAD = 64
F32 = jnp.float32
BF16 = jnp.bfloat16
VMEM_LIMIT = 24 * 1024 * 1024
ENTER_LIMIT = 60 * 1024 * 1024
VMEM = pl.BlockSpec(memory_space=pltpu.VMEM)
SMEM = pl.BlockSpec(memory_space=pltpu.SMEM)


def rows_dot(a, b):
    return lax.dot_general(a, b, (((1,), (1,)), ((), ())), preferred_element_type=F32)


def block_index():
    return (lax.axis_index("z") * 2 + lax.axis_index("yh")) * 2 + lax.axis_index("yl")


def image_bounds(counts_ref, first_lane):
    lane = lax.broadcasted_iota(jnp.int32, (1, LANES), 1)
    starts = jnp.zeros((1, LANES), jnp.int32)
    ends = jnp.zeros((1, LANES), jnp.int32)
    total = jnp.int32(0)
    for image in range(counts_ref.shape[0]):
        here = lane == first_lane + image
        starts = jnp.where(here, total, starts)
        total = total + counts_ref[image]
        ends = jnp.where(here, total, ends)
    return starts, ends


def modulation_rows(counts_ref, modulation_ref, first, rows):
    starts, ends = image_bounds(counts_ref, 0)
    place = first + lax.broadcasted_iota(jnp.int32, (rows, LANES), 0)
    member = ((place >= starts) & (place < ends)).astype(F32).astype(BF16)
    member = member[:, : modulation_ref.shape[1]]
    return [
        jnp.dot(member, modulation_ref[part], preferred_element_type=F32) for part in range(3)
    ]


def layer_norm(values):
    average = jnp.mean(values, axis=-1, keepdims=True)
    centred = values - average
    inv_std = lax.rsqrt(jnp.mean(centred * centred, axis=-1, keepdims=True) + EPS)
    return centred * inv_std, inv_std


def enter_kernel(
    counts_ref, tokens_ref, cotangent_ref, w_qkv_ref, w_out_ref, modulation_ref, out_ref
):
    rows = tokens_ref.shape[0]
    first = block_index() * rows
    shift, scale, gate = modulation_rows(counts_ref, modulation_ref, first, rows)
    normed, _ = layer_norm(tokens_ref[...].astype(F32))
    hidden = (normed * (1.0 + scale) + shift).astype(BF16)
    weights = jnp.concatenate([w_qkv_ref[part] for part in range(3)], axis=1)
    qkv = jnp.dot(hidden, weights, preferred_element_type=F32)
    q, k, v = (qkv[:, part * LANES : (part + 1) * LANES] for part in range(3))
    d_mixed = (cotangent_ref[...].astype(F32) * gate).astype(BF16)
    d_attn = rows_dot(d_mixed, w_out_ref[...])
    low = lax.broadcasted_iota(jnp.int32, (rows, LANES), 1) < HEAD

    def beside(left, right):
        return jnp.where(low, left, right).astype(BF16)

    q_v = (beside(q, pltpu.roll(v, HEAD, 1)), beside(pltpu.roll(q, HEAD, 1), v))
    k_d = (beside(k, pltpu.roll(d_attn, HEAD, 1)), beside(pltpu.roll(k, HEAD, 1), d_attn))
    for place in range(out_ref.shape[0]):
        out_ref[place, :, 0:LANES] = q_v[place % 2]
        out_ref[place, :, LANES:] = k_d[place % 2]


def enter(counts, tokens, cotangent, w_parts, w_out, modulation, quad):
    return pl.pallas_call(
        enter_kernel,
        out_shape=jax.ShapeDtypeStruct((quad, tokens.shape[0], 2 * LANES), BF16),
        in_specs=[SMEM] + [VMEM] * 5,
        out_specs=VMEM,
        compiler_params=pltpu.CompilerParams(vmem_limit_bytes=ENTER_LIMIT),
    )(counts, tokens, cotangent, w_parts, w_out, modulation)


def pack_kernel(w_qkv_ref, w_out_ref, weights_ref, sems):
    pairs = [(w_qkv_ref, weights_ref.at[0:3])]
    for tile in range(weights_ref.shape[1] // LANES):
        at = slice(tile * LANES, (tile + 1) * LANES)
        pairs.append((w_out_ref.at[:, at], weights_ref.at[3, at, :]))
    copies = [
        pltpu.make_async_copy(source, target, sems.at[place])
        for place, (source, target) in enumerate(pairs)
    ]
    for copy in copies:
        copy.start()
    for copy in copies:
        copy.wait()


def pack(w_parts, w_out):
    width = w_out.shape[1]
    whole = pl.BlockSpec(memory_space=pl.ANY)
    return pl.pallas_call(
        pack_kernel,
        out_shape=jax.ShapeDtypeStruct((4, width, LANES), BF16),
        in_specs=[whole] * 2,
        out_specs=VMEM,
        scratch_shapes=[pltpu.SemaphoreType.DMA((1 + width // LANES,))],
        compiler_params=pltpu.CompilerParams(vmem_limit_bytes=8 * 1024 * 1024),
    )(w_parts, w_out)


def w_out_of(weights_ref):
    tiles = weights_ref.shape[1] // LANES
    return jnp.concatenate(
        [weights_ref[3, tile * LANES : (tile + 1) * LANES, :] for tile in range(tiles)], axis=1
    )


LOG2_E = math.log2(math.e)
INV_ROOT = 1.0 / math.sqrt(HEAD)
CHUNK = 256
TILE = 64
MAIN = 6
REACH_CHUNKS = 4


def low_lanes():
    return lax.broadcasted_iota(jnp.int32, (1, LANES), 1) < HEAD


def lower_mean(values):
    return jnp.sum(jnp.where(low_lanes(), values, 0.0), axis=-1, keepdims=True) * (1.0 / HEAD)


def lower_sums(values):
    ones = (lax.broadcasted_iota(jnp.int32, (LANES, LANES), 0) < HEAD).astype(F32).astype(BF16)
    squares = values * values
    large = squares.astype(BF16)
    small = (squares - large.astype(F32)).astype(BF16)
    large = jnp.dot(large, ones, preferred_element_type=F32)
    return large + jnp.dot(small, ones, preferred_element_type=F32)


def place_block(source, place, starts, ends, gains_ref, stores):
    low = low_lanes()
    rows = source.shape[0]
    at = place + lax.broadcasted_iota(jnp.int32, (rows, LANES), 0)
    same = ((at >= starts) & (at < ends)).astype(F32)
    first = source[:, 0:LANES].astype(F32)
    second = source[:, LANES:].astype(F32)

    def normed(raw, gain):
        return raw * lax.rsqrt(lower_sums(raw) * (1.0 / HEAD) + EPS) * gain

    keys = normed(second, gains_ref[1:2, :])
    queries = normed(first, gains_ref[0:1, :] * INV_ROOT)
    q_store, k_store, v_store, d_store, kv_store = stores
    q_store[...] = jnp.where(low, queries, same * SAME_IMAGE).astype(BF16)
    k_store[...] = jnp.where(low, keys, same).astype(BF16)
    v_store[...] = jnp.where(low, 0.0, first).astype(BF16)
    d_store[...] = source[:, LANES:]
    kv_store[...] = jnp.where(low, keys, first).astype(BF16).T


def window_facts(counts_ref):
    half = lax.axis_index("yh")
    origin = (block_index() // 4 - 1) * 2 * CHUNK
    own_at = (2 + half) * CHUNK
    starts, ends = image_bounds(counts_ref, HEAD)
    left_from = jnp.int32(-CHUNK)
    right_to = jnp.int32((MAIN + 1) * CHUNK)
    total = -origin
    for image in range(counts_ref.shape[0]):
        left_from = jnp.where(total <= own_at, total, left_from)
        ended = total >= own_at + CHUNK
        total = total + counts_ref[image]
        right_to = jnp.where((total >= own_at + CHUNK) & jnp.logical_not(ended), total, right_to)
    return half, own_at, starts - origin, ends - origin, left_from, right_to


def by_eight(values):
    return values.reshape(values.shape[0] // 8, 8, values.shape[1])


def add_tiles(s_ref, g_ref, rows, highest, total, grads):
    for piece in range(rows // TILE):
        at = slice(piece * TILE, (piece + 1) * TILE)
        weights = jnp.exp2(s_ref[at, :] * LOG2_E - highest)
        total = total + jnp.sum(by_eight(weights), axis=0)
        grads = grads + jnp.sum(by_eight(weights * g_ref[at, :]), axis=0)
    return total, grads


def rows_max(values):
    return jnp.max(by_eight(values), axis=0)


def chunks_from(key, count, *refs):
    rows = [pl.ds(pl.multiple_of(key + i * CHUNK, CHUNK), CHUNK) for i in range(count)]
    return [tuple(ref.at[at, :] for ref in refs) for at in rows]


def running_sums(pieces, q_block, d_block, s_ref, g_ref):
    highest = jnp.full((8, CHUNK), -jnp.inf, F32)
    total = jnp.zeros((8, CHUNK), F32)
    grads = jnp.zeros((8, CHUNK), F32)
    for piece, (keys_ref, values_ref) in enumerate(pieces):
        here = slice(piece * CHUNK, (piece + 1) * CHUNK)
        scores = rows_dot(keys_ref[...], q_block)
        s_ref[here, :] = scores
        g_ref[here, :] = rows_dot(values_ref[...], d_block)
        higher = jnp.maximum(highest, rows_max(scores) * LOG2_E)
        shrink = jnp.exp2(highest - higher)
        total = total * shrink
        grads = grads * shrink
        highest = higher
        for tile in range(CHUNK // TILE):
            at = slice(piece * CHUNK + tile * TILE, piece * CHUNK + (tile + 1) * TILE)
            weights = jnp.exp2(by_eight(s_ref[at, :]) * LOG2_E - highest[None])
            total = total + jnp.sum(weights, axis=0)
            grads = grads + jnp.sum(weights * by_eight(g_ref[at, :]), axis=0)
    top = jnp.max(highest, axis=0, keepdims=True)
    shrink = jnp.exp2(highest - top)
    total = jnp.sum(total * shrink, axis=0, keepdims=True)
    return top, total, jnp.sum(grads * shrink, axis=0, keepdims=True)


def near_kernel(
    counts_ref,
    gains_ref,
    first_ref,
    quad_ref,
    second_ref,
    qx_ref,
    kx_ref,
    vx_ref,
    dx_ref,
    kv_ref,
    so_ref,
    go_ref,
    sn_ref,
    gn_ref,
    stats_ref,
    s_ref,
    g_ref,
):
    half, own_at, starts, ends, left_from, right_to = window_facts(counts_ref)
    block_rows = CHUNK // 2

    def place(source, begin):
        begin = pl.multiple_of(begin, block_rows)
        at = pl.ds(begin, block_rows)
        stores = [ref.at[at, :] for ref in (qx_ref, kx_ref, vx_ref, dx_ref)]
        place_block(source, begin, starts, ends, gains_ref, stores + [kv_ref.at[:, at]])

    to_first = jnp.where(lax.rem(lax.axis_index("z"), 2) == 0, 2 * CHUNK, -2 * CHUNK)
    for block in range(4):
        at = slice(block * block_rows, (block + 1) * block_rows)
        begin = 2 * CHUNK + block * block_rows
        place(quad_ref.at[at], begin)
        place(first_ref.at[at], begin + to_first)
        place(second_ref.at[at], begin - to_first)

    own_rows = pl.ds(pl.multiple_of(own_at, CHUNK), CHUNK)
    q_own = qx_ref[own_rows, :]
    d_own = dx_ref[own_rows, :]
    highest = jnp.full((8, CHUNK), -jnp.inf, F32)
    for piece in range(MAIN):
        at = slice(piece * CHUNK, (piece + 1) * CHUNK)
        scores = rows_dot(kx_ref[at, :], q_own)
        so_ref[at, :] = scores
        highest = jnp.maximum(highest, rows_max(scores))
        go_ref[at, :] = rows_dot(vx_ref[at, :], d_own)
    highest = jnp.max(highest, axis=0, keepdims=True) * LOG2_E
    total = jnp.zeros((8, CHUNK), F32)
    grads = jnp.zeros((8, CHUNK), F32)
    for piece in range(MAIN * CHUNK // TILE):
        at = slice(piece * TILE, (piece + 1) * TILE)
        weights = jnp.exp2(so_ref[at, :] * LOG2_E - highest)
        so_ref[at, :] = weights
        total = total + jnp.sum(by_eight(weights), axis=0)
        grads = grads + jnp.sum(by_eight(weights * go_ref[at, :]), axis=0)
    stats_ref[MAIN, 0:1, :] = highest
    stats_ref[MAIN, 1:2, :] = jnp.sum(total, axis=0, keepdims=True)
    stats_ref[MAIN, 2:3, :] = jnp.sum(grads, axis=0, keepdims=True)

    left_key = jnp.clip((left_from + CHUNK) // CHUNK - 1, 0, MAIN - REACH_CHUNKS)
    right_key = jnp.clip((right_to - 1) // CHUNK - (REACH_CHUNKS - 1), 0, MAIN - REACH_CHUNKS)

    def one_chunk(step, carry):
        slot = step + jnp.where(step >= 2 + half, 1, 0)
        begin = slot * CHUNK

        @pl.when((begin < right_to) & (begin + CHUNK > left_from))
        def _():
            at = pl.ds(pl.multiple_of(begin, CHUNK), CHUNK)
            key = jnp.where(begin < own_at, left_key, right_key) * CHUNK
            q_block = qx_ref[at, :]
            d_block = dx_ref[at, :]
            pieces = chunks_from(key, REACH_CHUNKS, kx_ref, vx_ref)
            highest, total, grads = running_sums(pieces, q_block, d_block, s_ref, g_ref)
            stats_ref[slot, 0:1, :] = highest
            stats_ref[slot, 1:2, :] = total
            stats_ref[slot, 2:3, :] = grads
            near_at = pl.ds(pl.multiple_of(own_at - key, CHUNK), CHUNK)
            sn_ref[slot, :, :] = s_ref[near_at, :]
            gn_ref[slot, :, :] = g_ref[near_at, :]

        return carry

    lax.fori_loop(0, MAIN - 1, one_chunk, 0)


def attend_near(counts, gains, first, quad, second):
    rows = MAIN * CHUNK
    head_rows = jax.ShapeDtypeStruct((rows, LANES), BF16)
    scores = jax.ShapeDtypeStruct((rows, CHUNK), F32)
    tiles = jax.ShapeDtypeStruct((MAIN, CHUNK, CHUNK), F32)
    return pl.pallas_call(
        near_kernel,
        out_shape=(head_rows,) * 4
        + (jax.ShapeDtypeStruct((LANES, rows), BF16),)
        + (scores, scores, tiles, tiles, jax.ShapeDtypeStruct((MAIN + 1, 8, CHUNK), F32)),
        in_specs=[SMEM] + [VMEM] * 4,
        out_specs=(VMEM,) * 10,
        scratch_shapes=[pltpu.VMEM((REACH_CHUNKS * CHUNK, CHUNK), F32)] * 2,
        cost_estimate=pl.CostEstimate(
            flops=9000000000, bytes_accessed=1 << 20, transcendentals=1 << 20
        ),
        compiler_params=pltpu.CompilerParams(vmem_limit_bytes=VMEM_LIMIT),
    )(counts, gains, first, quad, second)


def far_kernel(
    counts_ref,
    gains_ref,
    far_ref,
    quad_ref,
    qx_ref,
    kx_ref,
    vx_ref,
    dx_ref,
    kv_ref,
    so_ref,
    go_ref,
    sn_ref,
    gn_ref,
    stats_ref,
    out_ref,
    qf_ref,
    kf_ref,
    vf_ref,
    df_ref,
    kvf_ref,
    s_ref,
    g_ref,
    p_ref,
    d_ref,
    pn_ref,
    dn_ref,
    sums_ref,
    dk_ref,
    dv_ref,
    own_out_ref,
    done_ref,
):
    half, own_at, starts, ends, left_from, right_to = window_facts(counts_ref)
    block_rows = CHUNK // 2
    rows = MAIN * CHUNK
    far_at = jnp.where(half == 0, -CHUNK, rows)
    for block in range(2):
        at = slice(block * block_rows, (block + 1) * block_rows)
        stores = [ref.at[at, :] for ref in (qf_ref, kf_ref, vf_ref, df_ref)]
        place_block(
            far_ref.at[at],
            far_at + block * block_rows,
            starts,
            ends,
            gains_ref,
            stores + [kvf_ref.at[:, at]],
        )

    own_rows = pl.ds(pl.multiple_of(own_at, CHUNK), CHUNK)
    q_own = qx_ref[own_rows, :]
    d_own = dx_ref[own_rows, :]
    scores = rows_dot(kf_ref[...], q_own)
    s_ref[0:CHUNK, :] = scores
    g_ref[0:CHUNK, :] = rows_dot(vf_ref[...], d_own)
    near_highest = stats_ref[MAIN, 0:1, :]
    highest = jnp.max(rows_max(scores), axis=0, keepdims=True) * LOG2_E
    highest = jnp.maximum(near_highest, highest)
    shrink = jnp.exp2(near_highest - highest)
    zeros = jnp.zeros((8, CHUNK), F32)
    total, grads = add_tiles(s_ref, g_ref, CHUNK, highest, zeros, zeros)
    total = jnp.sum(total, axis=0, keepdims=True) + stats_ref[MAIN, 1:2, :] * shrink
    grads = jnp.sum(grads, axis=0, keepdims=True) + stats_ref[MAIN, 2:3, :] * shrink
    scale = 1.0 / total
    mean_grad = grads * scale

    near_scale = shrink * scale
    for piece in range(rows // TILE):
        at = slice(piece * TILE, (piece + 1) * TILE)
        probs = so_ref[at, :] * near_scale
        p_ref[at, :] = probs.astype(BF16)
        d_ref[at, :] = (probs * (go_ref[at, :] - mean_grad)).astype(BF16)
    for piece in range(CHUNK // TILE):
        at = slice(piece * TILE, (piece + 1) * TILE)
        to = slice(rows + piece * TILE, rows + (piece + 1) * TILE)
        probs = jnp.exp2(s_ref[at, :] * LOG2_E - highest) * scale
        p_ref[to, :] = probs.astype(BF16)
        d_ref[to, :] = (probs * (g_ref[at, :] - mean_grad)).astype(BF16)
    pn_ref[:, own_rows] = p_ref[own_rows, :]
    dn_ref[:, own_rows] = d_ref[own_rows, :]

    def times_window(values_ref):
        main = jnp.dot(kv_ref[...], values_ref[0:rows, :], preferred_element_type=F32)
        return main + jnp.dot(
            kvf_ref[...], values_ref[rows : rows + CHUNK, :], preferred_element_type=F32
        )

    upper = lax.broadcasted_iota(jnp.int32, (LANES, CHUNK), 0) < HEAD
    own_out_ref[...] = jnp.where(
        upper, times_window(d_ref) * INV_ROOT, times_window(p_ref)
    ).T

    query_lane = lax.broadcasted_iota(jnp.int32, (1, CHUNK), 1)
    reaches_far = jnp.where(half == 0, left_from < 0, right_to > rows)
    sums_ref[...] = stats_ref[...]
    dk_ref[...] = jnp.zeros_like(dk_ref)
    dv_ref[...] = jnp.zeros_like(dv_ref)

    @pl.when(reaches_far)
    def _():
        for step in range(2):
            slot = half * (MAIN - 2) + step
            at = pl.ds(pl.multiple_of(slot * CHUNK, CHUNK), CHUNK)
            space = pl.ds((REACH_CHUNKS + step) * CHUNK, CHUNK)
            highest, total, grads = running_sums(
                [(kf_ref, vf_ref)], qx_ref[at, :], dx_ref[at, :], s_ref.at[space], g_ref.at[space]
            )
            before = sums_ref[slot, 0:1, :]
            higher = jnp.maximum(before, highest)
            old = jnp.exp2(before - higher)
            new = jnp.exp2(highest - higher)
            sums_ref[slot, 0:1, :] = higher
            sums_ref[slot, 1:2, :] = sums_ref[slot, 1:2, :] * old + total * new
            sums_ref[slot, 2:3, :] = sums_ref[slot, 2:3, :] * old + grads * new

        q_block = qf_ref[...]
        d_block = df_ref[...]
        key = half * (MAIN // 2) * CHUNK
        pieces = chunks_from(key, REACH_CHUNKS - 1, kx_ref, vx_ref) + [(kf_ref, vf_ref)]
        highest, total, grads = running_sums(pieces, q_block, d_block, s_ref, g_ref)
        place = query_lane + far_at
        scale = jnp.where((place >= left_from) & (place < right_to), 1.0 / total, 0.0)
        mean_grad = grads * scale
        for piece in range(CHUNK // TILE):
            at = slice(piece * TILE, (piece + 1) * TILE)
            near_at = pl.ds(pl.multiple_of(own_at - key + piece * TILE, TILE), TILE)
            probs = jnp.exp2(s_ref[near_at, :] * LOG2_E - highest) * scale
            p_ref[at, :] = probs.astype(BF16)
            d_ref[at, :] = (probs * (g_ref[near_at, :] - mean_grad)).astype(BF16)
        dk_ref[...] = jnp.dot(d_ref[0:CHUNK, :], q_block, preferred_element_type=F32)
        dv_ref[...] = jnp.dot(p_ref[0:CHUNK, :], d_block, preferred_element_type=F32)

    for step in range(MAIN - 1):
        slot = step + jnp.where(step >= 2 + half, 1, 0)
        begin = slot * CHUNK
        chunk_at = pl.ds(pl.multiple_of(begin, CHUNK), CHUNK)
        place = query_lane + begin
        valid = (place >= left_from) & (place < right_to)
        highest = sums_ref[slot, 0:1, :]
        scale = 1.0 / sums_ref[slot, 1:2, :]
        mean_grad = sums_ref[slot, 2:3, :] * scale
        for piece in range(CHUNK // TILE):
            at = slice(piece * TILE, (piece + 1) * TILE)
            probs = jnp.exp2(sn_ref[slot, at, :] * LOG2_E - highest) * scale
            d_scores = probs * (gn_ref[slot, at, :] - mean_grad)
            pn_ref[at, chunk_at] = jnp.where(valid, probs, 0.0).astype(BF16)
            dn_ref[at, chunk_at] = jnp.where(valid, d_scores, 0.0).astype(BF16)
    d_key = dk_ref[...] + jnp.dot(dn_ref[...], qx_ref[...], preferred_element_type=F32)
    d_value = dv_ref[...] + jnp.dot(pn_ref[...], dx_ref[...], preferred_element_type=F32)
    own_out = own_out_ref[...]

    def norm_grad(raw, gain, d_norm):
        inverse = lax.rsqrt(lower_mean(raw * raw) + EPS)
        scaled = d_norm.astype(BF16).astype(F32) * gain
        inner = lower_mean(raw * scaled)
        return inverse * scaled - raw * (inverse * inverse * inverse * inner)

    low = low_lanes()
    own_in_quad = pl.ds(pl.multiple_of(half * CHUNK, CHUNK), CHUNK)
    raw_q = quad_ref[own_in_quad, 0:LANES].astype(F32)
    raw_k = quad_ref[own_in_quad, LANES:].astype(F32)
    d_q = norm_grad(raw_q, gains_ref[0:1, :], own_out)
    d_k = norm_grad(raw_k, gains_ref[1:2, :], d_key)
    done_ref[:, 0:LANES] = jnp.where(low, d_q, own_out).astype(BF16)
    done_ref[:, LANES:] = jnp.where(low, d_k, d_value).astype(BF16)
    share = 16
    for member in range(out_ref.shape[0]):
        block, core = member // 2, member % 2
        for part in range(out_ref.shape[1] // share):
            begin = (block * 8 + part * 2 + core) * share
            out_ref[member, part * share : (part + 1) * share, :] = done_ref[
                begin : begin + share, :
            ]


def attend_far(counts, gains, far, quad, near_parts):
    return pl.pallas_call(
        far_kernel,
        out_shape=jax.ShapeDtypeStruct((4, CHUNK // 4, 2 * LANES), BF16),
        in_specs=[SMEM] + [VMEM] * (3 + len(near_parts)),
        out_specs=VMEM,
        scratch_shapes=[pltpu.VMEM((CHUNK, LANES), BF16)] * 4
        + [pltpu.VMEM((LANES, CHUNK), BF16)]
        + [pltpu.VMEM(((REACH_CHUNKS + 2) * CHUNK, CHUNK), F32)] * 2
        + [pltpu.VMEM(((MAIN + 1) * CHUNK, CHUNK), BF16)] * 2
        + [pltpu.VMEM((CHUNK, MAIN * CHUNK), BF16)] * 2
        + [pltpu.VMEM((MAIN + 1, 8, CHUNK), F32)]
        + [pltpu.VMEM((CHUNK, LANES), F32)] * 3
        + [pltpu.VMEM((CHUNK, 2 * LANES), BF16)],
        cost_estimate=pl.CostEstimate(
            flops=9000000000, bytes_accessed=1 << 20, transcendentals=1 << 20
        ),
        compiler_params=pltpu.CompilerParams(vmem_limit_bytes=VMEM_LIMIT),
    )(counts, gains, far, quad, *near_parts)


def project_kernel(parts_ref, weights_ref, weights_far_ref, out_ref):
    rows = parts_ref.shape[1]
    width = weights_ref.shape[1]
    share = out_ref.shape[1]
    core = lax.axis_index("core")
    low = lax.broadcasted_iota(jnp.int32, (rows, LANES), 1) < HEAD

    def by_column(which):
        head0 = parts_ref[which].astype(F32)
        head1 = parts_ref[2 + which].astype(F32)
        a0, a1 = head0[:, :LANES], head1[:, :LANES]
        b0, b1 = head0[:, LANES:], head1[:, LANES:]
        d_q = jnp.where(low, a0, pltpu.roll(a1, HEAD, 1)).astype(BF16)
        attn = jnp.where(low, pltpu.roll(a0, HEAD, 1), a1).astype(BF16)
        d_k = jnp.where(low, b0, pltpu.roll(b1, HEAD, 1)).astype(BF16)
        d_v = jnp.where(low, pltpu.roll(b0, HEAD, 1), b1).astype(BF16)
        return attn, [d_q, d_k, d_v]

    attn, grads = by_column(core)
    attn_far, grads_far = by_column(1 - core)
    mixed = jnp.dot(
        jnp.concatenate([attn, attn_far], axis=1),
        jnp.concatenate([w_out_of(weights_ref), w_out_of(weights_far_ref)], axis=0),
        preferred_element_type=F32,
    ).astype(BF16)
    weights = [ref[part] for ref in (weights_ref, weights_far_ref) for part in range(3)]
    d_hidden = rows_dot(
        jnp.concatenate(grads + grads_far, axis=1), jnp.concatenate(weights, axis=1)
    ).astype(BF16)
    for place in range(out_ref.shape[0]):
        at = slice(place * share, (place + 1) * share)
        out_ref[place, :, :width] = mixed[at]
        out_ref[place, :, width:] = d_hidden[at]


def project(parts, weights, weights_far, x_count):
    return pl.pallas_call(
        project_kernel,
        out_shape=jax.ShapeDtypeStruct(
            (x_count, parts.shape[1] // x_count, 2 * weights.shape[1]), BF16
        ),
        in_specs=[VMEM] * 3,
        out_specs=VMEM,
        compiler_params=pltpu.CompilerParams(vmem_limit_bytes=VMEM_LIMIT),
    )(parts, weights, weights_far)


def ready_kernel(
    counts_ref,
    tokens_ref,
    cotangent_ref,
    modulation_ref,
    rows_ref,
    factors_ref,
):
    rows = rows_ref.shape[1]
    first_row = (lax.axis_index("x") * 2 + lax.axis_index("core")) * rows
    first = block_index() * tokens_ref.shape[0] + first_row
    _, scale, gate = modulation_rows(counts_ref, modulation_ref, first, rows)
    at = pl.ds(pl.multiple_of(first_row, rows), rows)
    normed, inv_std = layer_norm(tokens_ref[at, :].astype(F32))
    rows_ref[0] = tokens_ref[at, :]
    rows_ref[1] = cotangent_ref[at, :]
    factors_ref[0] = gate
    factors_ref[1] = 1.0 + scale
    factors_ref[2] = normed
    factors_ref[3] = jnp.broadcast_to(inv_std, normed.shape)


def ready(counts, tokens, cotangent, modulation, share):
    width = tokens.shape[1]
    return pl.pallas_call(
        ready_kernel,
        out_shape=(
            jax.ShapeDtypeStruct((2, share, width), BF16),
            jax.ShapeDtypeStruct((4, share, width), F32),
        ),
        in_specs=[SMEM] + [VMEM] * 3,
        out_specs=(VMEM, VMEM),
        compiler_params=pltpu.CompilerParams(vmem_limit_bytes=VMEM_LIMIT),
    )(counts, tokens, cotangent, modulation)


def leave_kernel(rows_ref, factors_ref, shares_ref, layer_ref, grad_ref):
    width = layer_ref.shape[1]
    sums = shares_ref[0].astype(F32)
    for share in range(1, shares_ref.shape[0]):
        sums = sums + shares_ref[share].astype(F32)
    layer = rows_ref[0].astype(F32) + factors_ref[0] * sums[:, :width]
    layer_ref[...] = layer.astype(BF16)
    d_normed = sums[:, width:] * factors_ref[1]
    normed = factors_ref[2]
    input_grad = rows_ref[1].astype(F32) + factors_ref[3] * (
        d_normed
        - jnp.mean(d_normed, axis=-1, keepdims=True)
        - normed * jnp.mean(d_normed * normed, axis=-1, keepdims=True)
    )
    grad_ref[...] = input_grad.astype(BF16)


def leave(rows, factors, shares):
    out = jax.ShapeDtypeStruct(rows.shape[1:], BF16)
    return pl.pallas_call(
        leave_kernel,
        out_shape=(out, out),
        in_specs=[VMEM] * 3,
        out_specs=(VMEM, VMEM),
        compiler_params=pltpu.CompilerParams(vmem_limit_bytes=VMEM_LIMIT),
    )(rows, factors, shares)


def per_device(tokens, cotangent, w_qkv, w_out, qk_gain, modulation, image_counts):
    tok_rows, model_width = tokens.shape
    z_count = lax.axis_size("z")
    x_count = lax.axis_size("x")
    quad = 4
    pair_rows = 2 * tok_rows
    share = tok_rows // (2 * x_count)
    w_parts = w_qkv.transpose(1, 0, 2)
    mod_parts = modulation.transpose(1, 0, 2)
    gains = jnp.pad(qk_gain, ((0, 6), (0, LANES - HEAD)))

    heads = enter(image_counts, tokens, cotangent, w_parts, w_out, mod_parts, quad)
    _, tokens_late, cotangent_late, mod_late, w_parts_late, w_out_late = (
        lax.optimization_barrier((heads, tokens, cotangent, mod_parts, w_parts, w_out))
    )
    rows, factors = ready(image_counts, tokens_late, cotangent_late, mod_late, share)
    weights = pack(w_parts_late, w_out_late)
    mine = lax.all_to_all(heads, ("yh", "yl"), 0, 0)
    mine, rows, factors, weights = lax.optimization_barrier((mine, rows, factors, weights))
    mine = mine.reshape(quad * tok_rows, 2 * LANES)
    evens = range(0, z_count, 2)
    swaps = [(i, i + 1) for i in evens], [((i - 1) % z_count, i) for i in evens]
    first, second = (
        lax.ppermute(mine, "z", pairs + [(j, i) for i, j in pairs]) for pairs in swaps
    )
    halves = 4 * z_count
    far_half = jnp.where(
        lax.axis_index("yh") == lax.axis_index("core"), mine[pair_rows:], mine[:pair_rows]
    )

    def far_source(target):
        z, yh, core = target // 4, target // 2 % 2, target % 2
        return (z + (2 if yh else -2)) % z_count * 4 + (yh ^ core) * 2 + core

    far = lax.ppermute(
        far_half, ("z", "yh", "core"), [(far_source(i), i) for i in range(halves)]
    )
    near_parts = attend_near(image_counts, gains, first, mine, second)
    weights_far = lax.ppermute(weights, "core", [(0, 1), (1, 0)])
    parts = attend_far(image_counts, gains, far, mine, near_parts)
    parts = lax.all_to_all(parts, ("yl", "core"), 0, 0)
    partial = project(parts, weights, weights_far, x_count)
    shares = lax.all_to_all(partial, "x", 0, 0)
    return leave(rows, factors, shares)


def solution(mesh):
    split = jax.sharding.Mesh(mesh.devices.reshape(16, 2, 2, 4, 2), ("z", "yh", "yl", "x", "core"))
    dp, head = ("z", "yh", "yl"), ("x", "core")
    in_specs = (P(dp, None), P(dp, None), P(None, None, head), P(head, None), P(), P(), P())
    out_specs = (P(dp + head, None), P(dp + head, None))
    return jax.shard_map(
        per_device, mesh=split, in_specs=in_specs, out_specs=out_specs, check_vma=False
    )
```

```python
import math

import jax
import jax.numpy as jnp
from jax import lax
from jax.experimental import pallas as pl
from jax.experimental.pallas import tpu as pltpu
from jax.sharding import PartitionSpec as P

EPS = 1e-06
SAME_IMAGE = 512.0
LANES = 128
HEAD = 64
F32 = jnp.float32
BF16 = jnp.bfloat16
VMEM_LIMIT = 24 * 1024 * 1024
ENTER_LIMIT = 60 * 1024 * 1024
VMEM = pl.BlockSpec(memory_space=pltpu.VMEM)
SMEM = pl.BlockSpec(memory_space=pltpu.SMEM)


def rows_dot(a, b):
    return lax.dot_general(a, b, (((1,), (1,)), ((), ())), preferred_element_type=F32)


def block_index():
    return (lax.axis_index("z") * 2 + lax.axis_index("yh")) * 2 + lax.axis_index("yl")


def image_bounds(counts_ref, first_lane):
    lane = lax.broadcasted_iota(jnp.int32, (1, LANES), 1)
    starts = jnp.zeros((1, LANES), jnp.int32)
    ends = jnp.zeros((1, LANES), jnp.int32)
    total = jnp.int32(0)
    for image in range(counts_ref.shape[0]):
        here = lane == first_lane + image
        starts = jnp.where(here, total, starts)
        total = total + counts_ref[image]
        ends = jnp.where(here, total, ends)
    return starts, ends


def modulation_rows(counts_ref, modulation_ref, first, rows):
    starts, ends = image_bounds(counts_ref, 0)
    place = first + lax.broadcasted_iota(jnp.int32, (rows, LANES), 0)
    member = ((place >= starts) & (place < ends)).astype(F32).astype(BF16)
    member = member[:, : modulation_ref.shape[1]]
    return [
        jnp.dot(member, modulation_ref[part], preferred_element_type=F32) for part in range(3)
    ]


def layer_norm(values):
    average = jnp.mean(values, axis=-1, keepdims=True)
    centred = values - average
    inv_std = lax.rsqrt(jnp.mean(centred * centred, axis=-1, keepdims=True) + EPS)
    return centred * inv_std, inv_std


def head_sums(values):
    lanes = (LANES, LANES)
    first = lax.broadcasted_iota(jnp.int32, lanes, 0) < HEAD
    second = lax.broadcasted_iota(jnp.int32, lanes, 1) < HEAD
    ones = (first == second).astype(F32).astype(BF16)
    large = values.astype(BF16)
    small = (values - large.astype(F32)).astype(BF16)
    large = jnp.dot(large, ones, preferred_element_type=F32)
    return large + jnp.dot(small, ones, preferred_element_type=F32)


def both_heads(gains_ref, which):
    gain = gains_ref[which : which + 1, :]
    return jnp.concatenate([gain, gain], axis=1)


def head_scale(raw):
    return lax.rsqrt(head_sums(raw * raw) * (1.0 / HEAD) + EPS)


def enter_kernel(
    counts_ref,
    gains_ref,
    tokens_ref,
    cotangent_ref,
    w_qkv_ref,
    w_out_ref,
    modulation_ref,
    out_ref,
    raw_ref,
    raw_far_ref,
    rows_ref,
):
    rows = tokens_ref.shape[0]
    first = block_index() * rows
    shift, scale, gate = modulation_rows(counts_ref, modulation_ref, first, rows)
    normed, _ = layer_norm(tokens_ref[...].astype(F32))
    hidden = (normed * (1.0 + scale) + shift).astype(BF16)
    weights = jnp.concatenate([w_qkv_ref[part] for part in range(3)], axis=1)
    qkv = jnp.dot(hidden, weights, preferred_element_type=F32)
    q, k, v = (qkv[:, part * LANES : (part + 1) * LANES] for part in range(3))
    d_mixed = (cotangent_ref[...].astype(F32) * gate).astype(BF16)
    d_attn = rows_dot(d_mixed, w_out_ref[...])
    rows_ref[0] = q.astype(BF16)
    rows_ref[1] = k.astype(BF16)
    q = rows_ref[0].astype(F32)
    k = rows_ref[1].astype(F32)
    q = q * head_scale(q) * (both_heads(gains_ref, 0) * (1.0 / math.sqrt(HEAD)))
    k = k * head_scale(k) * both_heads(gains_ref, 1)
    core = lax.axis_index("core")
    share = raw_ref.shape[1] // 4
    for ref, side in ((raw_ref, core), (raw_far_ref, 1 - core)):
        for part in range(4):
            begin = pl.multiple_of((2 * part + side) * share, share)
            for array in range(2):
                ref[array, part * share : (part + 1) * share, :] = rows_ref[
                    array, pl.ds(begin, share), :
                ]
    low = low_lanes()

    def beside(left, right):
        return jnp.where(low, left, right).astype(BF16)

    q_v = (beside(q, pltpu.roll(v, HEAD, 1)), beside(pltpu.roll(q, HEAD, 1), v))
    k_d = (beside(k, pltpu.roll(d_attn, HEAD, 1)), beside(pltpu.roll(k, HEAD, 1), d_attn))
    for place in range(out_ref.shape[0]):
        out_ref[place, :, 0:LANES] = q_v[place % 2]
        out_ref[place, :, LANES:] = k_d[place % 2]


def enter(counts, gains, tokens, cotangent, w_parts, w_out, modulation, quad):
    rows = tokens.shape[0]
    raw = jax.ShapeDtypeStruct((2, rows // 2, LANES), BF16)
    return pl.pallas_call(
        enter_kernel,
        out_shape=(jax.ShapeDtypeStruct((quad, rows, 2 * LANES), BF16), raw, raw),
        in_specs=[SMEM] + [VMEM] * 6,
        out_specs=(VMEM,) * 3,
        scratch_shapes=[pltpu.VMEM((2, rows, LANES), BF16)],
        compiler_params=pltpu.CompilerParams(vmem_limit_bytes=ENTER_LIMIT),
    )(counts, gains, tokens, cotangent, w_parts, w_out, modulation)


def pack_kernel(w_qkv_ref, w_out_ref, raw_ref, weights_ref, sems):
    width = w_out_ref.shape[1]
    rows = raw_ref.shape[1]
    pairs = []
    for part in range(3):
        pairs.append((w_qkv_ref.at[part], weights_ref.at[part * width : (part + 1) * width, :]))
    for tile in range(width // LANES):
        at = slice(tile * LANES, (tile + 1) * LANES)
        to = slice(3 * width + tile * LANES, 3 * width + (tile + 1) * LANES)
        pairs.append((w_out_ref.at[:, at], weights_ref.at[to, :]))
    for array in range(2):
        to = slice(4 * width + array * rows, 4 * width + (array + 1) * rows)
        pairs.append((raw_ref.at[array], weights_ref.at[to, :]))
    copies = [
        pltpu.make_async_copy(source, target, sems.at[place])
        for place, (source, target) in enumerate(pairs)
    ]
    for copy in copies:
        copy.start()
    for copy in copies:
        copy.wait()


def pack(w_parts, w_out, raw):
    width = w_out.shape[1]
    whole = pl.BlockSpec(memory_space=pl.ANY)
    return pl.pallas_call(
        pack_kernel,
        out_shape=jax.ShapeDtypeStruct((4 * width + 2 * raw.shape[1], LANES), BF16),
        in_specs=[whole] * 3,
        out_specs=VMEM,
        scratch_shapes=[pltpu.SemaphoreType.DMA((5 + width // LANES,))],
        compiler_params=pltpu.CompilerParams(vmem_limit_bytes=8 * 1024 * 1024),
    )(w_parts, w_out, raw)


def w_out_of(weights_ref, width):
    return jnp.concatenate(
        [
            weights_ref[3 * width + tile * LANES : 3 * width + (tile + 1) * LANES, :]
            for tile in range(width // LANES)
        ],
        axis=1,
    )


LOG2_E = math.log2(math.e)
INV_ROOT = 1.0 / math.sqrt(HEAD)
CHUNK = 256
TILE = 64
MAIN = 6
REACH_CHUNKS = 4


def low_lanes():
    return lax.broadcasted_iota(jnp.int32, (1, LANES), 1) < HEAD


def place_block(source, place, starts, ends, stores):
    low = low_lanes()
    rows = source.shape[0]
    at = place + lax.broadcasted_iota(jnp.int32, (rows, LANES), 0)
    same = ((at >= starts) & (at < ends)).astype(F32)
    first = source[:, 0:LANES].astype(F32)
    second = source[:, LANES:].astype(F32)
    q_store, k_store, v_store, d_store, kv_store = stores
    q_store[...] = jnp.where(low, first, same * SAME_IMAGE).astype(BF16)
    k_store[...] = jnp.where(low, second, same).astype(BF16)
    v_store[...] = jnp.where(low, 0.0, first).astype(BF16)
    d_store[...] = source[:, LANES:]
    kv_store[...] = jnp.where(low, second, first).astype(BF16).T


def window_facts(counts_ref):
    half = lax.axis_index("yh")
    origin = (block_index() // 4 - 1) * 2 * CHUNK
    own_at = (2 + half) * CHUNK
    starts, ends = image_bounds(counts_ref, HEAD)
    left_from = jnp.int32(-CHUNK)
    right_to = jnp.int32((MAIN + 1) * CHUNK)
    total = -origin
    for image in range(counts_ref.shape[0]):
        left_from = jnp.where(total <= own_at, total, left_from)
        ended = total >= own_at + CHUNK
        total = total + counts_ref[image]
        right_to = jnp.where((total >= own_at + CHUNK) & jnp.logical_not(ended), total, right_to)
    return half, own_at, starts - origin, ends - origin, left_from, right_to


def by_eight(values):
    return values.reshape(values.shape[0] // 8, 8, values.shape[1])


def add_tiles(s_ref, g_ref, rows, highest, total, grads):
    for piece in range(rows // TILE):
        at = slice(piece * TILE, (piece + 1) * TILE)
        weights = jnp.exp2(s_ref[at, :] * LOG2_E - highest)
        total = total + jnp.sum(by_eight(weights), axis=0)
        grads = grads + jnp.sum(by_eight(weights * g_ref[at, :]), axis=0)
    return total, grads


def rows_max(values):
    return jnp.max(by_eight(values), axis=0)


def chunks_from(key, count, *refs):
    rows = [pl.ds(pl.multiple_of(key + i * CHUNK, CHUNK), CHUNK) for i in range(count)]
    return [tuple(ref.at[at, :] for ref in refs) for at in rows]


def running_sums(pieces, q_block, d_block, s_ref, g_ref):
    highest = jnp.full((8, CHUNK), -jnp.inf, F32)
    total = jnp.zeros((8, CHUNK), F32)
    grads = jnp.zeros((8, CHUNK), F32)
    for piece, (keys_ref, values_ref) in enumerate(pieces):
        here = slice(piece * CHUNK, (piece + 1) * CHUNK)
        scores = rows_dot(keys_ref[...], q_block)
        s_ref[here, :] = scores
        g_ref[here, :] = rows_dot(values_ref[...], d_block)
        higher = jnp.maximum(highest, rows_max(scores) * LOG2_E)
        shrink = jnp.exp2(highest - higher)
        total = total * shrink
        grads = grads * shrink
        highest = higher
        for tile in range(CHUNK // TILE):
            at = slice(piece * CHUNK + tile * TILE, piece * CHUNK + (tile + 1) * TILE)
            weights = jnp.exp2(by_eight(s_ref[at, :]) * LOG2_E - highest[None])
            total = total + jnp.sum(weights, axis=0)
            grads = grads + jnp.sum(weights * by_eight(g_ref[at, :]), axis=0)
    top = jnp.max(highest, axis=0, keepdims=True)
    shrink = jnp.exp2(highest - top)
    total = jnp.sum(total * shrink, axis=0, keepdims=True)
    return top, total, jnp.sum(grads * shrink, axis=0, keepdims=True)


def near_kernel(
    counts_ref,
    first_ref,
    quad_ref,
    second_ref,
    qx_ref,
    kx_ref,
    vx_ref,
    dx_ref,
    kv_ref,
    so_ref,
    go_ref,
    sn_ref,
    gn_ref,
    stats_ref,
    s_ref,
    g_ref,
):
    half, own_at, starts, ends, left_from, right_to = window_facts(counts_ref)
    block_rows = CHUNK // 2

    def place(source, begin):
        begin = pl.multiple_of(begin, block_rows)
        at = pl.ds(begin, block_rows)
        stores = [ref.at[at, :] for ref in (qx_ref, kx_ref, vx_ref, dx_ref)]
        place_block(source, begin, starts, ends, stores + [kv_ref.at[:, at]])

    to_first = jnp.where(lax.rem(lax.axis_index("z"), 2) == 0, 2 * CHUNK, -2 * CHUNK)
    for block in range(4):
        at = slice(block * block_rows, (block + 1) * block_rows)
        begin = 2 * CHUNK + block * block_rows
        place(quad_ref.at[at], begin)
        place(first_ref.at[at], begin + to_first)
        place(second_ref.at[at], begin - to_first)

    own_rows = pl.ds(pl.multiple_of(own_at, CHUNK), CHUNK)
    q_own = qx_ref[own_rows, :]
    d_own = dx_ref[own_rows, :]
    highest = jnp.full((8, CHUNK), -jnp.inf, F32)
    for piece in range(MAIN):
        at = slice(piece * CHUNK, (piece + 1) * CHUNK)
        scores = rows_dot(kx_ref[at, :], q_own)
        so_ref[at, :] = scores
        highest = jnp.maximum(highest, rows_max(scores))
        go_ref[at, :] = rows_dot(vx_ref[at, :], d_own)
    highest = jnp.max(highest, axis=0, keepdims=True) * LOG2_E
    total = jnp.zeros((8, CHUNK), F32)
    grads = jnp.zeros((8, CHUNK), F32)
    for piece in range(MAIN * CHUNK // TILE):
        at = slice(piece * TILE, (piece + 1) * TILE)
        weights = jnp.exp2(so_ref[at, :] * LOG2_E - highest)
        so_ref[at, :] = weights
        total = total + jnp.sum(by_eight(weights), axis=0)
        grads = grads + jnp.sum(by_eight(weights * go_ref[at, :]), axis=0)
    stats_ref[MAIN, 0:1, :] = highest
    stats_ref[MAIN, 1:2, :] = jnp.sum(total, axis=0, keepdims=True)
    stats_ref[MAIN, 2:3, :] = jnp.sum(grads, axis=0, keepdims=True)

    left_key = jnp.clip((left_from + CHUNK) // CHUNK - 1, 0, MAIN - REACH_CHUNKS)
    right_key = jnp.clip((right_to - 1) // CHUNK - (REACH_CHUNKS - 1), 0, MAIN - REACH_CHUNKS)

    def one_chunk(step, carry):
        slot = step + jnp.where(step >= 2 + half, 1, 0)
        begin = slot * CHUNK

        @pl.when((begin < right_to) & (begin + CHUNK > left_from))
        def _():
            at = pl.ds(pl.multiple_of(begin, CHUNK), CHUNK)
            key = jnp.where(begin < own_at, left_key, right_key) * CHUNK
            q_block = qx_ref[at, :]
            d_block = dx_ref[at, :]
            pieces = chunks_from(key, REACH_CHUNKS, kx_ref, vx_ref)
            highest, total, grads = running_sums(pieces, q_block, d_block, s_ref, g_ref)
            stats_ref[slot, 0:1, :] = highest
            stats_ref[slot, 1:2, :] = total
            stats_ref[slot, 2:3, :] = grads
            near_at = pl.ds(pl.multiple_of(own_at - key, CHUNK), CHUNK)
            sn_ref[slot, :, :] = s_ref[near_at, :]
            gn_ref[slot, :, :] = g_ref[near_at, :]

        return carry

    lax.fori_loop(0, MAIN - 1, one_chunk, 0)


def attend_near(counts, first, quad, second):
    rows = MAIN * CHUNK
    head_rows = jax.ShapeDtypeStruct((rows, LANES), BF16)
    scores = jax.ShapeDtypeStruct((rows, CHUNK), F32)
    tiles = jax.ShapeDtypeStruct((MAIN, CHUNK, CHUNK), F32)
    return pl.pallas_call(
        near_kernel,
        out_shape=(head_rows,) * 4
        + (jax.ShapeDtypeStruct((LANES, rows), BF16),)
        + (scores, scores, tiles, tiles, jax.ShapeDtypeStruct((MAIN + 1, 8, CHUNK), F32)),
        in_specs=[SMEM] + [VMEM] * 3,
        out_specs=(VMEM,) * 10,
        scratch_shapes=[pltpu.VMEM((REACH_CHUNKS * CHUNK, CHUNK), F32)] * 2,
        cost_estimate=pl.CostEstimate(
            flops=9000000000, bytes_accessed=1 << 20, transcendentals=1 << 20
        ),
        compiler_params=pltpu.CompilerParams(vmem_limit_bytes=VMEM_LIMIT),
    )(counts, first, quad, second)


def far_kernel(
    counts_ref,
    far_ref,
    qx_ref,
    kx_ref,
    vx_ref,
    dx_ref,
    kv_ref,
    so_ref,
    go_ref,
    sn_ref,
    gn_ref,
    stats_ref,
    out_ref,
    qf_ref,
    kf_ref,
    vf_ref,
    df_ref,
    kvf_ref,
    s_ref,
    g_ref,
    p_ref,
    d_ref,
    pn_ref,
    dn_ref,
    sums_ref,
    dk_ref,
    dv_ref,
    own_out_ref,
    done_ref,
):
    half, own_at, starts, ends, left_from, right_to = window_facts(counts_ref)
    block_rows = CHUNK // 2
    rows = MAIN * CHUNK
    far_at = jnp.where(half == 0, -CHUNK, rows)
    for block in range(2):
        at = slice(block * block_rows, (block + 1) * block_rows)
        stores = [ref.at[at, :] for ref in (qf_ref, kf_ref, vf_ref, df_ref)]
        place_block(
            far_ref.at[at],
            far_at + block * block_rows,
            starts,
            ends,
            stores + [kvf_ref.at[:, at]],
        )

    own_rows = pl.ds(pl.multiple_of(own_at, CHUNK), CHUNK)
    q_own = qx_ref[own_rows, :]
    d_own = dx_ref[own_rows, :]
    scores = rows_dot(kf_ref[...], q_own)
    s_ref[0:CHUNK, :] = scores
    g_ref[0:CHUNK, :] = rows_dot(vf_ref[...], d_own)
    near_highest = stats_ref[MAIN, 0:1, :]
    highest = jnp.max(rows_max(scores), axis=0, keepdims=True) * LOG2_E
    highest = jnp.maximum(near_highest, highest)
    shrink = jnp.exp2(near_highest - highest)
    zeros = jnp.zeros((8, CHUNK), F32)
    total, grads = add_tiles(s_ref, g_ref, CHUNK, highest, zeros, zeros)
    total = jnp.sum(total, axis=0, keepdims=True) + stats_ref[MAIN, 1:2, :] * shrink
    grads = jnp.sum(grads, axis=0, keepdims=True) + stats_ref[MAIN, 2:3, :] * shrink
    scale = 1.0 / total
    mean_grad = grads * scale

    near_scale = shrink * scale
    for piece in range(rows // TILE):
        at = slice(piece * TILE, (piece + 1) * TILE)
        probs = so_ref[at, :] * near_scale
        p_ref[at, :] = probs.astype(BF16)
        d_ref[at, :] = (probs * (go_ref[at, :] - mean_grad)).astype(BF16)
    for piece in range(CHUNK // TILE):
        at = slice(piece * TILE, (piece + 1) * TILE)
        to = slice(rows + piece * TILE, rows + (piece + 1) * TILE)
        probs = jnp.exp2(s_ref[at, :] * LOG2_E - highest) * scale
        p_ref[to, :] = probs.astype(BF16)
        d_ref[to, :] = (probs * (g_ref[at, :] - mean_grad)).astype(BF16)
    pn_ref[:, own_rows] = p_ref[own_rows, :]
    dn_ref[:, own_rows] = d_ref[own_rows, :]

    def times_window(values_ref):
        main = jnp.dot(kv_ref[...], values_ref[0:rows, :], preferred_element_type=F32)
        return main + jnp.dot(
            kvf_ref[...], values_ref[rows : rows + CHUNK, :], preferred_element_type=F32
        )

    upper = lax.broadcasted_iota(jnp.int32, (LANES, CHUNK), 0) < HEAD
    own_out_ref[...] = jnp.where(
        upper, times_window(d_ref) * INV_ROOT, times_window(p_ref)
    ).T

    query_lane = lax.broadcasted_iota(jnp.int32, (1, CHUNK), 1)
    reaches_far = jnp.where(half == 0, left_from < 0, right_to > rows)
    sums_ref[...] = stats_ref[...]
    dk_ref[...] = jnp.zeros_like(dk_ref)
    dv_ref[...] = jnp.zeros_like(dv_ref)

    @pl.when(reaches_far)
    def _():
        for step in range(2):
            slot = half * (MAIN - 2) + step
            at = pl.ds(pl.multiple_of(slot * CHUNK, CHUNK), CHUNK)
            space = pl.ds((REACH_CHUNKS + step) * CHUNK, CHUNK)
            highest, total, grads = running_sums(
                [(kf_ref, vf_ref)], qx_ref[at, :], dx_ref[at, :], s_ref.at[space], g_ref.at[space]
            )
            before = sums_ref[slot, 0:1, :]
            higher = jnp.maximum(before, highest)
            old = jnp.exp2(before - higher)
            new = jnp.exp2(highest - higher)
            sums_ref[slot, 0:1, :] = higher
            sums_ref[slot, 1:2, :] = sums_ref[slot, 1:2, :] * old + total * new
            sums_ref[slot, 2:3, :] = sums_ref[slot, 2:3, :] * old + grads * new

        q_block = qf_ref[...]
        d_block = df_ref[...]
        key = half * (MAIN // 2) * CHUNK
        pieces = chunks_from(key, REACH_CHUNKS - 1, kx_ref, vx_ref) + [(kf_ref, vf_ref)]
        highest, total, grads = running_sums(pieces, q_block, d_block, s_ref, g_ref)
        place = query_lane + far_at
        scale = jnp.where((place >= left_from) & (place < right_to), 1.0 / total, 0.0)
        mean_grad = grads * scale
        for piece in range(CHUNK // TILE):
            at = slice(piece * TILE, (piece + 1) * TILE)
            near_at = pl.ds(pl.multiple_of(own_at - key + piece * TILE, TILE), TILE)
            probs = jnp.exp2(s_ref[near_at, :] * LOG2_E - highest) * scale
            p_ref[at, :] = probs.astype(BF16)
            d_ref[at, :] = (probs * (g_ref[near_at, :] - mean_grad)).astype(BF16)
        dk_ref[...] = jnp.dot(d_ref[0:CHUNK, :], q_block, preferred_element_type=F32)
        dv_ref[...] = jnp.dot(p_ref[0:CHUNK, :], d_block, preferred_element_type=F32)

    for step in range(MAIN - 1):
        slot = step + jnp.where(step >= 2 + half, 1, 0)
        begin = slot * CHUNK
        chunk_at = pl.ds(pl.multiple_of(begin, CHUNK), CHUNK)
        place = query_lane + begin
        valid = (place >= left_from) & (place < right_to)
        highest = sums_ref[slot, 0:1, :]
        scale = 1.0 / sums_ref[slot, 1:2, :]
        mean_grad = sums_ref[slot, 2:3, :] * scale
        for piece in range(CHUNK // TILE):
            at = slice(piece * TILE, (piece + 1) * TILE)
            probs = jnp.exp2(sn_ref[slot, at, :] * LOG2_E - highest) * scale
            d_scores = probs * (gn_ref[slot, at, :] - mean_grad)
            pn_ref[at, chunk_at] = jnp.where(valid, probs, 0.0).astype(BF16)
            dn_ref[at, chunk_at] = jnp.where(valid, d_scores, 0.0).astype(BF16)
    d_key = dk_ref[...] + jnp.dot(dn_ref[...], qx_ref[...], preferred_element_type=F32)
    d_value = dv_ref[...] + jnp.dot(pn_ref[...], dx_ref[...], preferred_element_type=F32)
    done_ref[:, 0:LANES] = own_out_ref[...].astype(BF16)
    done_ref[:, LANES:] = jnp.where(low_lanes(), d_key, d_value).astype(BF16)
    share = 16
    for member in range(out_ref.shape[0]):
        block, core = member // 2, member % 2
        for part in range(out_ref.shape[1] // share):
            begin = (block * 8 + part * 2 + core) * share
            out_ref[member, part * share : (part + 1) * share, :] = done_ref[
                begin : begin + share, :
            ]


def attend_far(counts, far, near_parts):
    return pl.pallas_call(
        far_kernel,
        out_shape=jax.ShapeDtypeStruct((4, CHUNK // 4, 2 * LANES), BF16),
        in_specs=[SMEM] + [VMEM] * (1 + len(near_parts)),
        out_specs=VMEM,
        scratch_shapes=[pltpu.VMEM((CHUNK, LANES), BF16)] * 4
        + [pltpu.VMEM((LANES, CHUNK), BF16)]
        + [pltpu.VMEM(((REACH_CHUNKS + 2) * CHUNK, CHUNK), F32)] * 2
        + [pltpu.VMEM(((MAIN + 1) * CHUNK, CHUNK), BF16)] * 2
        + [pltpu.VMEM((CHUNK, MAIN * CHUNK), BF16)] * 2
        + [pltpu.VMEM((MAIN + 1, 8, CHUNK), F32)]
        + [pltpu.VMEM((CHUNK, LANES), F32)] * 3
        + [pltpu.VMEM((CHUNK, 2 * LANES), BF16)],
        cost_estimate=pl.CostEstimate(
            flops=9000000000, bytes_accessed=1 << 20, transcendentals=1 << 20
        ),
        compiler_params=pltpu.CompilerParams(vmem_limit_bytes=VMEM_LIMIT),
    )(counts, far, *near_parts)


def project_kernel(parts_ref, gains_ref, raw_ref, weights_ref, weights_far_ref, out_ref):
    rows = parts_ref.shape[1]
    width = out_ref.shape[2] // 2
    share = out_ref.shape[1]
    core = lax.axis_index("core")
    low = low_lanes()
    q_gain = both_heads(gains_ref, 0)
    k_gain = both_heads(gains_ref, 1)

    def norm_grad(raw, gain, d_norm):
        raw = raw.astype(F32)
        inverse = head_scale(raw)
        scaled = d_norm * gain
        inner = head_sums(raw * scaled) * (1.0 / HEAD)
        return inverse * scaled - raw * (inverse * inverse * inverse * inner)

    def by_column(which, raw):
        head0 = parts_ref[which].astype(F32)
        head1 = parts_ref[2 + which].astype(F32)
        a0, a1 = head0[:, :LANES], head1[:, :LANES]
        b0, b1 = head0[:, LANES:], head1[:, LANES:]
        d_q = norm_grad(raw[0], q_gain, jnp.where(low, a0, pltpu.roll(a1, HEAD, 1)))
        attn = jnp.where(low, pltpu.roll(a0, HEAD, 1), a1).astype(BF16)
        d_k = norm_grad(raw[1], k_gain, jnp.where(low, b0, pltpu.roll(b1, HEAD, 1)))
        d_v = jnp.where(low, pltpu.roll(b0, HEAD, 1), b1)
        return attn, [values.astype(BF16) for values in (d_q, d_k, d_v)]

    raw_far = [
        weights_far_ref[4 * width + array * rows : 4 * width + (array + 1) * rows, :]
        for array in range(2)
    ]
    attn, grads = by_column(core, [raw_ref[0], raw_ref[1]])
    attn_far, grads_far = by_column(1 - core, raw_far)
    both = (weights_ref, weights_far_ref)
    mixed = jnp.dot(
        jnp.concatenate([attn, attn_far], axis=1),
        jnp.concatenate([w_out_of(ref, width) for ref in both], axis=0),
        preferred_element_type=F32,
    ).astype(BF16)
    weights = [ref[part * width : (part + 1) * width, :] for ref in both for part in range(3)]
    d_hidden = rows_dot(
        jnp.concatenate(grads + grads_far, axis=1), jnp.concatenate(weights, axis=1)
    ).astype(BF16)
    for place in range(out_ref.shape[0]):
        at = slice(place * share, (place + 1) * share)
        out_ref[place, :, :width] = mixed[at]
        out_ref[place, :, width:] = d_hidden[at]


def project(parts, gains, raw, weights, weights_far, x_count, width):
    return pl.pallas_call(
        project_kernel,
        out_shape=jax.ShapeDtypeStruct((x_count, parts.shape[1] // x_count, 2 * width), BF16),
        in_specs=[VMEM] * 5,
        out_specs=VMEM,
        compiler_params=pltpu.CompilerParams(vmem_limit_bytes=VMEM_LIMIT),
    )(parts, gains, raw, weights, weights_far)


def ready_kernel(
    counts_ref,
    tokens_ref,
    cotangent_ref,
    modulation_ref,
    rows_ref,
    factors_ref,
):
    rows = rows_ref.shape[1]
    first_row = (lax.axis_index("x") * 2 + lax.axis_index("core")) * rows
    first = block_index() * tokens_ref.shape[0] + first_row
    _, scale, gate = modulation_rows(counts_ref, modulation_ref, first, rows)
    at = pl.ds(pl.multiple_of(first_row, rows), rows)
    normed, inv_std = layer_norm(tokens_ref[at, :].astype(F32))
    rows_ref[0] = tokens_ref[at, :]
    rows_ref[1] = cotangent_ref[at, :]
    factors_ref[0] = gate
    factors_ref[1] = 1.0 + scale
    factors_ref[2] = normed
    factors_ref[3] = jnp.broadcast_to(inv_std, normed.shape)


def ready(counts, tokens, cotangent, modulation, share):
    width = tokens.shape[1]
    return pl.pallas_call(
        ready_kernel,
        out_shape=(
            jax.ShapeDtypeStruct((2, share, width), BF16),
            jax.ShapeDtypeStruct((4, share, width), F32),
        ),
        in_specs=[SMEM] + [VMEM] * 3,
        out_specs=(VMEM, VMEM),
        compiler_params=pltpu.CompilerParams(vmem_limit_bytes=VMEM_LIMIT),
    )(counts, tokens, cotangent, modulation)


def leave_kernel(rows_ref, factors_ref, shares_ref, layer_ref, grad_ref):
    width = layer_ref.shape[1]
    sums = shares_ref[0].astype(F32)
    for share in range(1, shares_ref.shape[0]):
        sums = sums + shares_ref[share].astype(F32)
    layer = rows_ref[0].astype(F32) + factors_ref[0] * sums[:, :width]
    layer_ref[...] = layer.astype(BF16)
    d_normed = sums[:, width:] * factors_ref[1]
    normed = factors_ref[2]
    input_grad = rows_ref[1].astype(F32) + factors_ref[3] * (
        d_normed
        - jnp.mean(d_normed, axis=-1, keepdims=True)
        - normed * jnp.mean(d_normed * normed, axis=-1, keepdims=True)
    )
    grad_ref[...] = input_grad.astype(BF16)


def leave(rows, factors, shares):
    out = jax.ShapeDtypeStruct(rows.shape[1:], BF16)
    return pl.pallas_call(
        leave_kernel,
        out_shape=(out, out),
        in_specs=[VMEM] * 3,
        out_specs=(VMEM, VMEM),
        compiler_params=pltpu.CompilerParams(vmem_limit_bytes=VMEM_LIMIT),
    )(rows, factors, shares)


def per_device(tokens, cotangent, w_qkv, w_out, qk_gain, modulation, image_counts):
    tok_rows, model_width = tokens.shape
    z_count = lax.axis_size("z")
    x_count = lax.axis_size("x")
    quad = 4
    pair_rows = 2 * tok_rows
    share = tok_rows // (2 * x_count)
    w_parts = w_qkv.transpose(1, 0, 2)
    mod_parts = modulation.transpose(1, 0, 2)

    heads, raw, raw_far = enter(
        image_counts, qk_gain, tokens, cotangent, w_parts, w_out, mod_parts, quad
    )
    _, tokens_late, cotangent_late, mod_late, w_parts_late, w_out_late = (
        lax.optimization_barrier((heads, tokens, cotangent, mod_parts, w_parts, w_out))
    )
    rows, factors = ready(image_counts, tokens_late, cotangent_late, mod_late, share)
    weights = pack(w_parts_late, w_out_late, raw_far)
    mine = lax.all_to_all(heads, ("yh", "yl"), 0, 0)
    mine, rows, factors, weights = lax.optimization_barrier((mine, rows, factors, weights))
    mine = mine.reshape(quad * tok_rows, 2 * LANES)
    evens = range(0, z_count, 2)
    swaps = [(i, i + 1) for i in evens], [((i - 1) % z_count, i) for i in evens]
    first, second = (
        lax.ppermute(mine, "z", pairs + [(j, i) for i, j in pairs]) for pairs in swaps
    )
    halves = 4 * z_count
    far_half = jnp.where(
        lax.axis_index("yh") == lax.axis_index("core"), mine[pair_rows:], mine[:pair_rows]
    )

    def far_source(target):
        z, yh, core = target // 4, target // 2 % 2, target % 2
        return (z + (2 if yh else -2)) % z_count * 4 + (yh ^ core) * 2 + core

    far = lax.ppermute(
        far_half, ("z", "yh", "core"), [(far_source(i), i) for i in range(halves)]
    )
    near_parts = attend_near(image_counts, first, mine, second)
    weights_far = lax.ppermute(weights, "core", [(0, 1), (1, 0)])
    parts = attend_far(image_counts, far, near_parts)
    parts = lax.all_to_all(parts, ("yl", "core"), 0, 0)
    partial = project(parts, qk_gain, raw, weights, weights_far, x_count, model_width)
    shares = lax.all_to_all(partial, "x", 0, 0)
    return leave(rows, factors, shares)


def solution(mesh):
    split = jax.sharding.Mesh(mesh.devices.reshape(16, 2, 2, 4, 2), ("z", "yh", "yl", "x", "core"))
    dp, head = ("z", "yh", "yl"), ("x", "core")
    in_specs = (P(dp, None), P(dp, None), P(None, None, head), P(head, None), P(), P(), P())
    out_specs = (P(dp + head, None), P(dp + head, None))
    return jax.shard_map(
        per_device, mesh=split, in_specs=in_specs, out_specs=out_specs, check_vma=False
    )
```

```python
import math

import jax
import jax.numpy as jnp
from jax import lax
from jax.experimental import pallas as pl
from jax.experimental.pallas import tpu as pltpu
from jax.sharding import PartitionSpec as P

EPS = 1e-06
SAME_IMAGE = 512.0
LANES = 128
HEAD = 64
F32 = jnp.float32
BF16 = jnp.bfloat16
VMEM_LIMIT = 24 * 1024 * 1024
ENTER_LIMIT = 60 * 1024 * 1024
VMEM = pl.BlockSpec(memory_space=pltpu.VMEM)
SMEM = pl.BlockSpec(memory_space=pltpu.SMEM)


def rows_dot(a, b):
    return lax.dot_general(a, b, (((1,), (1,)), ((), ())), preferred_element_type=F32)


def block_index():
    return (lax.axis_index("z") * 2 + lax.axis_index("yh")) * 2 + lax.axis_index("yl")


def image_bounds(counts_ref, first_lane):
    lane = lax.broadcasted_iota(jnp.int32, (1, LANES), 1)
    starts = jnp.zeros((1, LANES), jnp.int32)
    ends = jnp.zeros((1, LANES), jnp.int32)
    total = jnp.int32(0)
    for image in range(counts_ref.shape[0]):
        here = lane == first_lane + image
        starts = jnp.where(here, total, starts)
        total = total + counts_ref[image]
        ends = jnp.where(here, total, ends)
    return starts, ends


def modulation_rows(counts_ref, modulation_ref, first, rows):
    starts, ends = image_bounds(counts_ref, 0)
    place = first + lax.broadcasted_iota(jnp.int32, (rows, LANES), 0)
    member = ((place >= starts) & (place < ends)).astype(F32).astype(BF16)
    member = member[:, : modulation_ref.shape[1]]
    return [
        jnp.dot(member, modulation_ref[part], preferred_element_type=F32) for part in range(3)
    ]


def layer_norm(values):
    average = jnp.mean(values, axis=-1, keepdims=True)
    centred = values - average
    inv_std = lax.rsqrt(jnp.mean(centred * centred, axis=-1, keepdims=True) + EPS)
    return centred * inv_std, inv_std


def head_sums(values):
    lanes = (LANES, LANES)
    first = lax.broadcasted_iota(jnp.int32, lanes, 0) < HEAD
    second = lax.broadcasted_iota(jnp.int32, lanes, 1) < HEAD
    ones = (first == second).astype(F32).astype(BF16)
    large = values.astype(BF16)
    small = (values - large.astype(F32)).astype(BF16)
    large = jnp.dot(large, ones, preferred_element_type=F32)
    return large + jnp.dot(small, ones, preferred_element_type=F32)


def both_heads(gains_ref, which):
    gain = gains_ref[which : which + 1, :]
    return jnp.concatenate([gain, gain], axis=1)


def head_scale(raw):
    return lax.rsqrt(head_sums(raw * raw) * (1.0 / HEAD) + EPS)


def enter_kernel(
    counts_ref,
    gains_ref,
    tokens_ref,
    cotangent_ref,
    w_qkv_ref,
    w_out_ref,
    modulation_ref,
    out_ref,
    raw_ref,
    raw_far_ref,
    rows_ref,
):
    rows = tokens_ref.shape[0]
    first = block_index() * rows
    shift, scale, gate = modulation_rows(counts_ref, modulation_ref, first, rows)
    normed, _ = layer_norm(tokens_ref[...].astype(F32))
    hidden = (normed * (1.0 + scale) + shift).astype(BF16)
    weights = jnp.concatenate([w_qkv_ref[part] for part in range(3)], axis=1)
    qkv = jnp.dot(hidden, weights, preferred_element_type=F32)
    q, k, v = (qkv[:, part * LANES : (part + 1) * LANES] for part in range(3))
    d_mixed = (cotangent_ref[...].astype(F32) * gate).astype(BF16)
    d_attn = rows_dot(d_mixed, w_out_ref[...])
    rows_ref[0] = q.astype(BF16)
    rows_ref[1] = k.astype(BF16)
    q = rows_ref[0].astype(F32)
    k = rows_ref[1].astype(F32)
    q = q * head_scale(q) * (both_heads(gains_ref, 0) * (1.0 / math.sqrt(HEAD)))
    k = k * head_scale(k) * both_heads(gains_ref, 1)
    core = lax.axis_index("core")
    share = raw_ref.shape[1] // 4
    for ref, side in ((raw_ref, core), (raw_far_ref, 1 - core)):
        for part in range(4):
            begin = pl.multiple_of((2 * part + side) * share, share)
            for array in range(2):
                ref[array, part * share : (part + 1) * share, :] = rows_ref[
                    array, pl.ds(begin, share), :
                ]
    low = low_lanes()

    def beside(left, right):
        return jnp.where(low, left, right).astype(BF16)

    q_v = (beside(q, pltpu.roll(v, HEAD, 1)), beside(pltpu.roll(q, HEAD, 1), v))
    k_d = (beside(k, pltpu.roll(d_attn, HEAD, 1)), beside(pltpu.roll(k, HEAD, 1), d_attn))
    for place in range(out_ref.shape[0]):
        out_ref[place, :, 0:LANES] = q_v[place % 2]
        out_ref[place, :, LANES:] = k_d[place % 2]


def enter(counts, gains, tokens, cotangent, w_parts, w_out, modulation, quad):
    rows = tokens.shape[0]
    raw = jax.ShapeDtypeStruct((2, rows // 2, LANES), BF16)
    return pl.pallas_call(
        enter_kernel,
        out_shape=(jax.ShapeDtypeStruct((quad, rows, 2 * LANES), BF16), raw, raw),
        in_specs=[SMEM] + [VMEM] * 6,
        out_specs=(VMEM,) * 3,
        scratch_shapes=[pltpu.VMEM((2, rows, LANES), BF16)],
        compiler_params=pltpu.CompilerParams(vmem_limit_bytes=ENTER_LIMIT),
    )(counts, gains, tokens, cotangent, w_parts, w_out, modulation)


def pack_kernel(w_qkv_ref, w_out_ref, raw_ref, weights_ref, sems):
    width = w_out_ref.shape[1]
    rows = raw_ref.shape[1]
    pairs = []
    for part in range(3):
        pairs.append((w_qkv_ref.at[part], weights_ref.at[part * width : (part + 1) * width, :]))
    for tile in range(width // LANES):
        at = slice(tile * LANES, (tile + 1) * LANES)
        to = slice(3 * width + tile * LANES, 3 * width + (tile + 1) * LANES)
        pairs.append((w_out_ref.at[:, at], weights_ref.at[to, :]))
    for array in range(2):
        to = slice(4 * width + array * rows, 4 * width + (array + 1) * rows)
        pairs.append((raw_ref.at[array], weights_ref.at[to, :]))
    copies = [
        pltpu.make_async_copy(source, target, sems.at[place])
        for place, (source, target) in enumerate(pairs)
    ]
    for copy in copies:
        copy.start()
    for copy in copies:
        copy.wait()


def pack(w_parts, w_out, raw):
    width = w_out.shape[1]
    whole = pl.BlockSpec(memory_space=pl.ANY)
    return pl.pallas_call(
        pack_kernel,
        out_shape=jax.ShapeDtypeStruct((4 * width + 2 * raw.shape[1], LANES), BF16),
        in_specs=[whole] * 3,
        out_specs=VMEM,
        scratch_shapes=[pltpu.SemaphoreType.DMA((5 + width // LANES,))],
        compiler_params=pltpu.CompilerParams(vmem_limit_bytes=8 * 1024 * 1024),
    )(w_parts, w_out, raw)


def w_out_of(weights_ref, width):
    return jnp.concatenate(
        [
            weights_ref[3 * width + tile * LANES : 3 * width + (tile + 1) * LANES, :]
            for tile in range(width // LANES)
        ],
        axis=1,
    )


LOG2_E = math.log2(math.e)
INV_ROOT = 1.0 / math.sqrt(HEAD)
CHUNK = 256
TILE = 64
MAIN = 6
REACH_CHUNKS = 4


def low_lanes():
    return lax.broadcasted_iota(jnp.int32, (1, LANES), 1) < HEAD


def place_block(source, place, starts, ends, stores):
    low = low_lanes()
    rows = source.shape[0]
    at = place + lax.broadcasted_iota(jnp.int32, (rows, LANES), 0)
    same = ((at >= starts) & (at < ends)).astype(F32)
    first = source[:, 0:LANES].astype(F32)
    second = source[:, LANES:].astype(F32)
    q_store, k_store, v_store, d_store, kv_store = stores
    q_store[...] = jnp.where(low, first, same * SAME_IMAGE).astype(BF16)
    k_store[...] = jnp.where(low, second, same).astype(BF16)
    v_store[...] = jnp.where(low, 0.0, first).astype(BF16)
    d_store[...] = source[:, LANES:]
    kv_store[...] = jnp.where(low, second, first).astype(BF16).T


def window_facts(counts_ref):
    half = lax.axis_index("yh")
    origin = (block_index() // 4 - 1) * 2 * CHUNK
    own_at = (2 + half) * CHUNK
    starts, ends = image_bounds(counts_ref, HEAD)
    left_from = jnp.int32(-CHUNK)
    right_to = jnp.int32((MAIN + 1) * CHUNK)
    total = -origin
    for image in range(counts_ref.shape[0]):
        left_from = jnp.where(total <= own_at, total, left_from)
        ended = total >= own_at + CHUNK
        total = total + counts_ref[image]
        right_to = jnp.where((total >= own_at + CHUNK) & jnp.logical_not(ended), total, right_to)
    return half, own_at, starts - origin, ends - origin, left_from, right_to


def by_eight(values):
    return values.reshape(values.shape[0] // 8, 8, values.shape[1])


def add_tiles(s_ref, g_ref, rows, highest, total, grads):
    for piece in range(rows // TILE):
        at = slice(piece * TILE, (piece + 1) * TILE)
        weights = jnp.exp2(s_ref[at, :] * LOG2_E - highest)
        total = total + jnp.sum(by_eight(weights), axis=0)
        grads = grads + jnp.sum(by_eight(weights * g_ref[at, :]), axis=0)
    return total, grads


def rows_max(values):
    return jnp.max(by_eight(values), axis=0)


def chunks_from(key, count, *refs):
    rows = [pl.ds(pl.multiple_of(key + i * CHUNK, CHUNK), CHUNK) for i in range(count)]
    return [tuple(ref.at[at, :] for ref in refs) for at in rows]


def running_sums(pieces, q_block, d_block, s_ref, g_ref):
    highest = jnp.full((8, CHUNK), -jnp.inf, F32)
    total = jnp.zeros((8, CHUNK), F32)
    grads = jnp.zeros((8, CHUNK), F32)
    for piece, (keys_ref, values_ref) in enumerate(pieces):
        here = slice(piece * CHUNK, (piece + 1) * CHUNK)
        scores = rows_dot(keys_ref[...], q_block)
        s_ref[here, :] = scores
        g_ref[here, :] = rows_dot(values_ref[...], d_block)
        higher = jnp.maximum(highest, rows_max(scores) * LOG2_E)
        shrink = jnp.exp2(highest - higher)
        total = total * shrink
        grads = grads * shrink
        highest = higher
        for tile in range(CHUNK // TILE):
            at = slice(piece * CHUNK + tile * TILE, piece * CHUNK + (tile + 1) * TILE)
            weights = jnp.exp2(by_eight(s_ref[at, :]) * LOG2_E - highest[None])
            total = total + jnp.sum(weights, axis=0)
            grads = grads + jnp.sum(weights * by_eight(g_ref[at, :]), axis=0)
    top = jnp.max(highest, axis=0, keepdims=True)
    shrink = jnp.exp2(highest - top)
    total = jnp.sum(total * shrink, axis=0, keepdims=True)
    return top, total, jnp.sum(grads * shrink, axis=0, keepdims=True)


def early_kernel(
    counts_ref,
    first_ref,
    quad_ref,
    qa_ref,
    ka_ref,
    va_ref,
    da_ref,
    kva_ref,
    sa_ref,
    ga_ref,
    top_ref,
):
    half, _, starts, ends, _, _ = window_facts(counts_ref)
    block_rows = CHUNK // 2
    to_first = jnp.where(lax.rem(lax.axis_index("z"), 2) == 0, 2 * CHUNK, -2 * CHUNK)
    for block in range(8):
        at = slice(block * block_rows, (block + 1) * block_rows)
        inner = slice(block % 4 * block_rows, (block % 4 + 1) * block_rows)
        place = 2 * CHUNK + block % 4 * block_rows
        stores = [ref.at[at, :] for ref in (qa_ref, ka_ref, va_ref, da_ref)]
        stores.append(kva_ref.at[:, at])
        if block < 4:
            place_block(quad_ref.at[inner], place, starts, ends, stores)
        else:
            place_block(first_ref.at[inner], place + to_first, starts, ends, stores)

    own_rows = pl.ds(pl.multiple_of(half * CHUNK, CHUNK), CHUNK)
    q_own = qa_ref[own_rows, :]
    d_own = da_ref[own_rows, :]
    highest = jnp.full((8, CHUNK), -jnp.inf, F32)
    for piece in range(4):
        at = slice(piece * CHUNK, (piece + 1) * CHUNK)
        scores = rows_dot(ka_ref[at, :], q_own)
        sa_ref[at, :] = scores
        highest = jnp.maximum(highest, rows_max(scores))
        ga_ref[at, :] = rows_dot(va_ref[at, :], d_own)
    top_ref[...] = highest


def attend_early(counts, first, quad):
    rows = 4 * CHUNK
    head_rows = jax.ShapeDtypeStruct((rows, LANES), BF16)
    scores = jax.ShapeDtypeStruct((rows, CHUNK), F32)
    return pl.pallas_call(
        early_kernel,
        out_shape=(head_rows,) * 4
        + (jax.ShapeDtypeStruct((LANES, rows), BF16), scores, scores)
        + (jax.ShapeDtypeStruct((8, CHUNK), F32),),
        in_specs=[SMEM] + [VMEM] * 2,
        out_specs=(VMEM,) * 8,
        compiler_params=pltpu.CompilerParams(vmem_limit_bytes=VMEM_LIMIT),
    )(counts, first, quad)


def near_kernel(
    counts_ref,
    second_ref,
    qa_ref,
    ka_ref,
    va_ref,
    da_ref,
    kva_ref,
    sa_ref,
    ga_ref,
    top_ref,
    qx_ref,
    kx_ref,
    vx_ref,
    dx_ref,
    kv_ref,
    so_ref,
    go_ref,
    sn_ref,
    gn_ref,
    stats_ref,
    s_ref,
    g_ref,
):
    half, own_at, starts, ends, left_from, right_to = window_facts(counts_ref)
    block_rows = CHUNK // 2
    even = lax.rem(lax.axis_index("z"), 2) == 0
    first_at = pl.multiple_of(jnp.where(even, 4 * CHUNK, 0), 2 * CHUNK)
    second_at = pl.multiple_of(jnp.where(even, 0, 4 * CHUNK), 2 * CHUNK)
    early = ((qa_ref, qx_ref), (ka_ref, kx_ref), (va_ref, vx_ref), (da_ref, dx_ref))
    for source, target in early:
        target[2 * CHUNK : 4 * CHUNK, :] = source[0 : 2 * CHUNK, :]
        target[pl.ds(first_at, 2 * CHUNK), :] = source[2 * CHUNK : 4 * CHUNK, :]
    kv_ref[:, 2 * CHUNK : 4 * CHUNK] = kva_ref[:, 0 : 2 * CHUNK]
    kv_ref[:, pl.ds(first_at, 2 * CHUNK)] = kva_ref[:, 2 * CHUNK : 4 * CHUNK]
    for block in range(4):
        inner = slice(block * block_rows, (block + 1) * block_rows)
        begin = pl.multiple_of(second_at + block * block_rows, block_rows)
        at = pl.ds(begin, block_rows)
        stores = [ref.at[at, :] for ref in (qx_ref, kx_ref, vx_ref, dx_ref)]
        place_block(second_ref.at[inner], begin, starts, ends, stores + [kv_ref.at[:, at]])

    own_rows = pl.ds(pl.multiple_of(half * CHUNK, CHUNK), CHUNK)
    q_own = qa_ref[own_rows, :]
    d_own = da_ref[own_rows, :]
    highest = top_ref[...]
    for piece in range(2):
        at = pl.ds(pl.multiple_of(second_at + piece * CHUNK, CHUNK), CHUNK)
        scores = rows_dot(kx_ref[at, :], q_own)
        so_ref[at, :] = scores
        highest = jnp.maximum(highest, rows_max(scores))
        go_ref[at, :] = rows_dot(vx_ref[at, :], d_own)
    highest = jnp.max(highest, axis=0, keepdims=True) * LOG2_E
    total = jnp.zeros((8, CHUNK), F32)
    grads = jnp.zeros((8, CHUNK), F32)
    for piece in range(MAIN * CHUNK // TILE):
        inner = piece * TILE
        if inner < 2 * CHUNK:
            to = pl.ds(2 * CHUNK + inner, TILE)
        elif inner < 4 * CHUNK:
            to = pl.ds(pl.multiple_of(first_at + inner - 2 * CHUNK, TILE), TILE)
        else:
            to = pl.ds(pl.multiple_of(second_at + inner - 4 * CHUNK, TILE), TILE)
        if inner < 4 * CHUNK:
            scores = sa_ref[inner : inner + TILE, :]
            given = ga_ref[inner : inner + TILE, :]
            go_ref[to, :] = given
        else:
            scores = so_ref[to, :]
            given = go_ref[to, :]
        weights = jnp.exp2(scores * LOG2_E - highest)
        so_ref[to, :] = weights
        total = total + jnp.sum(by_eight(weights), axis=0)
        grads = grads + jnp.sum(by_eight(weights * given), axis=0)
    stats_ref[MAIN, 0:1, :] = highest
    stats_ref[MAIN, 1:2, :] = jnp.sum(total, axis=0, keepdims=True)
    stats_ref[MAIN, 2:3, :] = jnp.sum(grads, axis=0, keepdims=True)

    left_key = jnp.clip((left_from + CHUNK) // CHUNK - 1, 0, MAIN - REACH_CHUNKS)
    right_key = jnp.clip((right_to - 1) // CHUNK - (REACH_CHUNKS - 1), 0, MAIN - REACH_CHUNKS)

    def one_chunk(step, carry):
        slot = step + jnp.where(step >= 2 + half, 1, 0)
        begin = slot * CHUNK

        @pl.when((begin < right_to) & (begin + CHUNK > left_from))
        def _():
            at = pl.ds(pl.multiple_of(begin, CHUNK), CHUNK)
            key = jnp.where(begin < own_at, left_key, right_key) * CHUNK
            q_block = qx_ref[at, :]
            d_block = dx_ref[at, :]
            pieces = chunks_from(key, REACH_CHUNKS, kx_ref, vx_ref)
            highest, total, grads = running_sums(pieces, q_block, d_block, s_ref, g_ref)
            stats_ref[slot, 0:1, :] = highest
            stats_ref[slot, 1:2, :] = total
            stats_ref[slot, 2:3, :] = grads
            near_at = pl.ds(pl.multiple_of(own_at - key, CHUNK), CHUNK)
            sn_ref[slot, :, :] = s_ref[near_at, :]
            gn_ref[slot, :, :] = g_ref[near_at, :]

        return carry

    lax.fori_loop(0, MAIN - 1, one_chunk, 0)


def attend_near(counts, second, early):
    rows = MAIN * CHUNK
    head_rows = jax.ShapeDtypeStruct((rows, LANES), BF16)
    scores = jax.ShapeDtypeStruct((rows, CHUNK), F32)
    tiles = jax.ShapeDtypeStruct((MAIN, CHUNK, CHUNK), F32)
    return pl.pallas_call(
        near_kernel,
        out_shape=(head_rows,) * 4
        + (jax.ShapeDtypeStruct((LANES, rows), BF16),)
        + (scores, scores, tiles, tiles, jax.ShapeDtypeStruct((MAIN + 1, 8, CHUNK), F32)),
        in_specs=[SMEM] + [VMEM] * (1 + len(early)),
        out_specs=(VMEM,) * 10,
        scratch_shapes=[pltpu.VMEM((REACH_CHUNKS * CHUNK, CHUNK), F32)] * 2,
        cost_estimate=pl.CostEstimate(
            flops=9000000000, bytes_accessed=1 << 20, transcendentals=1 << 20
        ),
        compiler_params=pltpu.CompilerParams(vmem_limit_bytes=VMEM_LIMIT),
    )(counts, second, *early)


def far_kernel(
    counts_ref,
    far_ref,
    qx_ref,
    kx_ref,
    vx_ref,
    dx_ref,
    kv_ref,
    so_ref,
    go_ref,
    sn_ref,
    gn_ref,
    stats_ref,
    out_ref,
    qf_ref,
    kf_ref,
    vf_ref,
    df_ref,
    kvf_ref,
    s_ref,
    g_ref,
    p_ref,
    d_ref,
    pn_ref,
    dn_ref,
    sums_ref,
    dk_ref,
    dv_ref,
    own_out_ref,
    done_ref,
):
    half, own_at, starts, ends, left_from, right_to = window_facts(counts_ref)
    block_rows = CHUNK // 2
    rows = MAIN * CHUNK
    far_at = jnp.where(half == 0, -CHUNK, rows)
    for block in range(2):
        at = slice(block * block_rows, (block + 1) * block_rows)
        stores = [ref.at[at, :] for ref in (qf_ref, kf_ref, vf_ref, df_ref)]
        place_block(
            far_ref.at[at],
            far_at + block * block_rows,
            starts,
            ends,
            stores + [kvf_ref.at[:, at]],
        )

    own_rows = pl.ds(pl.multiple_of(own_at, CHUNK), CHUNK)
    q_own = qx_ref[own_rows, :]
    d_own = dx_ref[own_rows, :]
    scores = rows_dot(kf_ref[...], q_own)
    s_ref[0:CHUNK, :] = scores
    g_ref[0:CHUNK, :] = rows_dot(vf_ref[...], d_own)
    near_highest = stats_ref[MAIN, 0:1, :]
    highest = jnp.max(rows_max(scores), axis=0, keepdims=True) * LOG2_E
    highest = jnp.maximum(near_highest, highest)
    shrink = jnp.exp2(near_highest - highest)
    zeros = jnp.zeros((8, CHUNK), F32)
    total, grads = add_tiles(s_ref, g_ref, CHUNK, highest, zeros, zeros)
    total = jnp.sum(total, axis=0, keepdims=True) + stats_ref[MAIN, 1:2, :] * shrink
    grads = jnp.sum(grads, axis=0, keepdims=True) + stats_ref[MAIN, 2:3, :] * shrink
    scale = 1.0 / total
    mean_grad = grads * scale

    near_scale = shrink * scale
    for piece in range(rows // TILE):
        at = slice(piece * TILE, (piece + 1) * TILE)
        probs = so_ref[at, :] * near_scale
        p_ref[at, :] = probs.astype(BF16)
        d_ref[at, :] = (probs * (go_ref[at, :] - mean_grad)).astype(BF16)
    for piece in range(CHUNK // TILE):
        at = slice(piece * TILE, (piece + 1) * TILE)
        to = slice(rows + piece * TILE, rows + (piece + 1) * TILE)
        probs = jnp.exp2(s_ref[at, :] * LOG2_E - highest) * scale
        p_ref[to, :] = probs.astype(BF16)
        d_ref[to, :] = (probs * (g_ref[at, :] - mean_grad)).astype(BF16)
    pn_ref[:, own_rows] = p_ref[own_rows, :]
    dn_ref[:, own_rows] = d_ref[own_rows, :]

    def times_window(values_ref):
        main = jnp.dot(kv_ref[...], values_ref[0:rows, :], preferred_element_type=F32)
        return main + jnp.dot(
            kvf_ref[...], values_ref[rows : rows + CHUNK, :], preferred_element_type=F32
        )

    upper = lax.broadcasted_iota(jnp.int32, (LANES, CHUNK), 0) < HEAD
    own_out_ref[...] = jnp.where(
        upper, times_window(d_ref) * INV_ROOT, times_window(p_ref)
    ).T

    query_lane = lax.broadcasted_iota(jnp.int32, (1, CHUNK), 1)
    reaches_far = jnp.where(half == 0, left_from < 0, right_to > rows)
    sums_ref[...] = stats_ref[...]
    dk_ref[...] = jnp.zeros_like(dk_ref)
    dv_ref[...] = jnp.zeros_like(dv_ref)

    @pl.when(reaches_far)
    def _():
        for step in range(2):
            slot = half * (MAIN - 2) + step
            at = pl.ds(pl.multiple_of(slot * CHUNK, CHUNK), CHUNK)
            space = pl.ds((REACH_CHUNKS + step) * CHUNK, CHUNK)
            highest, total, grads = running_sums(
                [(kf_ref, vf_ref)], qx_ref[at, :], dx_ref[at, :], s_ref.at[space], g_ref.at[space]
            )
            before = sums_ref[slot, 0:1, :]
            higher = jnp.maximum(before, highest)
            old = jnp.exp2(before - higher)
            new = jnp.exp2(highest - higher)
            sums_ref[slot, 0:1, :] = higher
            sums_ref[slot, 1:2, :] = sums_ref[slot, 1:2, :] * old + total * new
            sums_ref[slot, 2:3, :] = sums_ref[slot, 2:3, :] * old + grads * new

        q_block = qf_ref[...]
        d_block = df_ref[...]
        key = half * (MAIN // 2) * CHUNK
        pieces = chunks_from(key, REACH_CHUNKS - 1, kx_ref, vx_ref) + [(kf_ref, vf_ref)]
        highest, total, grads = running_sums(pieces, q_block, d_block, s_ref, g_ref)
        place = query_lane + far_at
        scale = jnp.where((place >= left_from) & (place < right_to), 1.0 / total, 0.0)
        mean_grad = grads * scale
        for piece in range(CHUNK // TILE):
            at = slice(piece * TILE, (piece + 1) * TILE)
            near_at = pl.ds(pl.multiple_of(own_at - key + piece * TILE, TILE), TILE)
            probs = jnp.exp2(s_ref[near_at, :] * LOG2_E - highest) * scale
            p_ref[at, :] = probs.astype(BF16)
            d_ref[at, :] = (probs * (g_ref[near_at, :] - mean_grad)).astype(BF16)
        dk_ref[...] = jnp.dot(d_ref[0:CHUNK, :], q_block, preferred_element_type=F32)
        dv_ref[...] = jnp.dot(p_ref[0:CHUNK, :], d_block, preferred_element_type=F32)

    for step in range(MAIN - 1):
        slot = step + jnp.where(step >= 2 + half, 1, 0)
        begin = slot * CHUNK
        chunk_at = pl.ds(pl.multiple_of(begin, CHUNK), CHUNK)
        place = query_lane + begin
        valid = (place >= left_from) & (place < right_to)
        highest = sums_ref[slot, 0:1, :]
        scale = 1.0 / sums_ref[slot, 1:2, :]
        mean_grad = sums_ref[slot, 2:3, :] * scale
        for piece in range(CHUNK // TILE):
            at = slice(piece * TILE, (piece + 1) * TILE)
            probs = jnp.exp2(sn_ref[slot, at, :] * LOG2_E - highest) * scale
            d_scores = probs * (gn_ref[slot, at, :] - mean_grad)
            pn_ref[at, chunk_at] = jnp.where(valid, probs, 0.0).astype(BF16)
            dn_ref[at, chunk_at] = jnp.where(valid, d_scores, 0.0).astype(BF16)
    d_key = dk_ref[...] + jnp.dot(dn_ref[...], qx_ref[...], preferred_element_type=F32)
    d_value = dv_ref[...] + jnp.dot(pn_ref[...], dx_ref[...], preferred_element_type=F32)
    done_ref[:, 0:LANES] = own_out_ref[...].astype(BF16)
    done_ref[:, LANES:] = jnp.where(low_lanes(), d_key, d_value).astype(BF16)
    share = 16
    for member in range(out_ref.shape[0]):
        block, core = member // 2, member % 2
        for part in range(out_ref.shape[1] // share):
            begin = (block * 8 + part * 2 + core) * share
            out_ref[member, part * share : (part + 1) * share, :] = done_ref[
                begin : begin + share, :
            ]


def attend_far(counts, far, near_parts):
    return pl.pallas_call(
        far_kernel,
        out_shape=jax.ShapeDtypeStruct((4, CHUNK // 4, 2 * LANES), BF16),
        in_specs=[SMEM] + [VMEM] * (1 + len(near_parts)),
        out_specs=VMEM,
        scratch_shapes=[pltpu.VMEM((CHUNK, LANES), BF16)] * 4
        + [pltpu.VMEM((LANES, CHUNK), BF16)]
        + [pltpu.VMEM(((REACH_CHUNKS + 2) * CHUNK, CHUNK), F32)] * 2
        + [pltpu.VMEM(((MAIN + 1) * CHUNK, CHUNK), BF16)] * 2
        + [pltpu.VMEM((CHUNK, MAIN * CHUNK), BF16)] * 2
        + [pltpu.VMEM((MAIN + 1, 8, CHUNK), F32)]
        + [pltpu.VMEM((CHUNK, LANES), F32)] * 3
        + [pltpu.VMEM((CHUNK, 2 * LANES), BF16)],
        cost_estimate=pl.CostEstimate(
            flops=9000000000, bytes_accessed=1 << 20, transcendentals=1 << 20
        ),
        compiler_params=pltpu.CompilerParams(vmem_limit_bytes=VMEM_LIMIT),
    )(counts, far, *near_parts)


def project_kernel(parts_ref, gains_ref, raw_ref, weights_ref, weights_far_ref, out_ref):
    rows = parts_ref.shape[1]
    width = out_ref.shape[2] // 2
    share = out_ref.shape[1]
    core = lax.axis_index("core")
    low = low_lanes()
    q_gain = both_heads(gains_ref, 0)
    k_gain = both_heads(gains_ref, 1)

    def norm_grad(raw, gain, d_norm):
        raw = raw.astype(F32)
        inverse = head_scale(raw)
        scaled = d_norm * gain
        inner = head_sums(raw * scaled) * (1.0 / HEAD)
        return inverse * scaled - raw * (inverse * inverse * inverse * inner)

    def by_column(which, raw):
        head0 = parts_ref[which].astype(F32)
        head1 = parts_ref[2 + which].astype(F32)
        a0, a1 = head0[:, :LANES], head1[:, :LANES]
        b0, b1 = head0[:, LANES:], head1[:, LANES:]
        d_q = norm_grad(raw[0], q_gain, jnp.where(low, a0, pltpu.roll(a1, HEAD, 1)))
        attn = jnp.where(low, pltpu.roll(a0, HEAD, 1), a1).astype(BF16)
        d_k = norm_grad(raw[1], k_gain, jnp.where(low, b0, pltpu.roll(b1, HEAD, 1)))
        d_v = jnp.where(low, pltpu.roll(b0, HEAD, 1), b1)
        return attn, [values.astype(BF16) for values in (d_q, d_k, d_v)]

    raw_far = [
        weights_far_ref[4 * width + array * rows : 4 * width + (array + 1) * rows, :]
        for array in range(2)
    ]
    attn, grads = by_column(core, [raw_ref[0], raw_ref[1]])
    attn_far, grads_far = by_column(1 - core, raw_far)
    both = (weights_ref, weights_far_ref)
    mixed = jnp.dot(
        jnp.concatenate([attn, attn_far], axis=1),
        jnp.concatenate([w_out_of(ref, width) for ref in both], axis=0),
        preferred_element_type=F32,
    ).astype(BF16)
    weights = [ref[part * width : (part + 1) * width, :] for ref in both for part in range(3)]
    d_hidden = rows_dot(
        jnp.concatenate(grads + grads_far, axis=1), jnp.concatenate(weights, axis=1)
    ).astype(BF16)
    for place in range(out_ref.shape[0]):
        at = slice(place * share, (place + 1) * share)
        out_ref[place, :, :width] = mixed[at]
        out_ref[place, :, width:] = d_hidden[at]


def project(parts, gains, raw, weights, weights_far, x_count, width):
    return pl.pallas_call(
        project_kernel,
        out_shape=jax.ShapeDtypeStruct((x_count, parts.shape[1] // x_count, 2 * width), BF16),
        in_specs=[VMEM] * 5,
        out_specs=VMEM,
        compiler_params=pltpu.CompilerParams(vmem_limit_bytes=VMEM_LIMIT),
    )(parts, gains, raw, weights, weights_far)


def ready_kernel(
    counts_ref,
    tokens_ref,
    cotangent_ref,
    modulation_ref,
    rows_ref,
    factors_ref,
):
    rows = rows_ref.shape[1]
    first_row = (lax.axis_index("x") * 2 + lax.axis_index("core")) * rows
    first = block_index() * tokens_ref.shape[0] + first_row
    _, scale, gate = modulation_rows(counts_ref, modulation_ref, first, rows)
    at = pl.ds(pl.multiple_of(first_row, rows), rows)
    normed, inv_std = layer_norm(tokens_ref[at, :].astype(F32))
    rows_ref[0] = tokens_ref[at, :]
    rows_ref[1] = cotangent_ref[at, :]
    factors_ref[0] = gate
    factors_ref[1] = 1.0 + scale
    factors_ref[2] = normed
    factors_ref[3] = jnp.broadcast_to(inv_std, normed.shape)


def ready(counts, tokens, cotangent, modulation, share):
    width = tokens.shape[1]
    return pl.pallas_call(
        ready_kernel,
        out_shape=(
            jax.ShapeDtypeStruct((2, share, width), BF16),
            jax.ShapeDtypeStruct((4, share, width), F32),
        ),
        in_specs=[SMEM] + [VMEM] * 3,
        out_specs=(VMEM, VMEM),
        compiler_params=pltpu.CompilerParams(vmem_limit_bytes=VMEM_LIMIT),
    )(counts, tokens, cotangent, modulation)


def leave_kernel(rows_ref, factors_ref, shares_ref, layer_ref, grad_ref):
    width = layer_ref.shape[1]
    sums = shares_ref[0].astype(F32)
    for share in range(1, shares_ref.shape[0]):
        sums = sums + shares_ref[share].astype(F32)
    layer = rows_ref[0].astype(F32) + factors_ref[0] * sums[:, :width]
    layer_ref[...] = layer.astype(BF16)
    d_normed = sums[:, width:] * factors_ref[1]
    normed = factors_ref[2]
    input_grad = rows_ref[1].astype(F32) + factors_ref[3] * (
        d_normed
        - jnp.mean(d_normed, axis=-1, keepdims=True)
        - normed * jnp.mean(d_normed * normed, axis=-1, keepdims=True)
    )
    grad_ref[...] = input_grad.astype(BF16)


def leave(rows, factors, shares):
    out = jax.ShapeDtypeStruct(rows.shape[1:], BF16)
    return pl.pallas_call(
        leave_kernel,
        out_shape=(out, out),
        in_specs=[VMEM] * 3,
        out_specs=(VMEM, VMEM),
        compiler_params=pltpu.CompilerParams(vmem_limit_bytes=VMEM_LIMIT),
    )(rows, factors, shares)


def per_device(tokens, cotangent, w_qkv, w_out, qk_gain, modulation, image_counts):
    tok_rows, model_width = tokens.shape
    z_count = lax.axis_size("z")
    x_count = lax.axis_size("x")
    quad = 4
    pair_rows = 2 * tok_rows
    share = tok_rows // (2 * x_count)
    w_parts = w_qkv.transpose(1, 0, 2)
    mod_parts = modulation.transpose(1, 0, 2)

    heads, raw, raw_far = enter(
        image_counts, qk_gain, tokens, cotangent, w_parts, w_out, mod_parts, quad
    )
    _, tokens_late, cotangent_late, mod_late, w_parts_late, w_out_late = (
        lax.optimization_barrier((heads, tokens, cotangent, mod_parts, w_parts, w_out))
    )
    rows, factors = ready(image_counts, tokens_late, cotangent_late, mod_late, share)
    weights = pack(w_parts_late, w_out_late, raw_far)
    mine = lax.all_to_all(heads, ("yh", "yl"), 0, 0)
    mine, rows, factors, weights = lax.optimization_barrier((mine, rows, factors, weights))
    mine = mine.reshape(quad * tok_rows, 2 * LANES)
    evens = range(0, z_count, 2)
    swaps = [(i, i + 1) for i in evens], [((i - 1) % z_count, i) for i in evens]
    first, second = (
        lax.ppermute(mine, "z", pairs + [(j, i) for i, j in pairs]) for pairs in swaps
    )
    halves = 4 * z_count
    far_half = jnp.where(
        lax.axis_index("yh") == lax.axis_index("core"), mine[pair_rows:], mine[:pair_rows]
    )

    def far_source(target):
        z, yh, core = target // 4, target // 2 % 2, target % 2
        return (z + (2 if yh else -2)) % z_count * 4 + (yh ^ core) * 2 + core

    far = lax.ppermute(
        far_half, ("z", "yh", "core"), [(far_source(i), i) for i in range(halves)]
    )
    early = attend_early(image_counts, first, mine)
    near_parts = attend_near(image_counts, second, early)
    weights_far = lax.ppermute(weights, "core", [(0, 1), (1, 0)])
    parts = attend_far(image_counts, far, near_parts)
    parts = lax.all_to_all(parts, ("yl", "core"), 0, 0)
    partial = project(parts, qk_gain, raw, weights, weights_far, x_count, model_width)
    shares = lax.all_to_all(partial, "x", 0, 0)
    return leave(rows, factors, shares)


def solution(mesh):
    split = jax.sharding.Mesh(mesh.devices.reshape(16, 2, 2, 4, 2), ("z", "yh", "yl", "x", "core"))
    dp, head = ("z", "yh", "yl"), ("x", "core")
    in_specs = (P(dp, None), P(dp, None), P(None, None, head), P(head, None), P(), P(), P())
    out_specs = (P(dp + head, None), P(dp + head, None))
    return jax.shard_map(
        per_device, mesh=split, in_specs=in_specs, out_specs=out_specs, check_vma=False
    )
```

```python
import math

import jax
import jax.numpy as jnp
from jax import lax
from jax.experimental import pallas as pl
from jax.experimental.pallas import tpu as pltpu
from jax.sharding import PartitionSpec as P

EPS = 1e-06
SAME_IMAGE = 512.0
LANES = 128
HEAD = 64
F32 = jnp.float32
BF16 = jnp.bfloat16
VMEM_LIMIT = 24 * 1024 * 1024
ENTER_LIMIT = 60 * 1024 * 1024
VMEM = pl.BlockSpec(memory_space=pltpu.VMEM)
SMEM = pl.BlockSpec(memory_space=pltpu.SMEM)


def rows_dot(a, b):
    return lax.dot_general(a, b, (((1,), (1,)), ((), ())), preferred_element_type=F32)


def block_index():
    return (lax.axis_index("z") * 2 + lax.axis_index("yh")) * 2 + lax.axis_index("yl")


def image_bounds(counts_ref, first_lane):
    lane = lax.broadcasted_iota(jnp.int32, (1, LANES), 1)
    starts = jnp.zeros((1, LANES), jnp.int32)
    ends = jnp.zeros((1, LANES), jnp.int32)
    total = jnp.int32(0)
    for image in range(counts_ref.shape[0]):
        here = lane == first_lane + image
        starts = jnp.where(here, total, starts)
        total = total + counts_ref[image]
        ends = jnp.where(here, total, ends)
    return starts, ends


def modulation_rows(counts_ref, modulation_ref, first, rows):
    starts, ends = image_bounds(counts_ref, 0)
    place = first + lax.broadcasted_iota(jnp.int32, (rows, LANES), 0)
    member = ((place >= starts) & (place < ends)).astype(F32).astype(BF16)
    member = member[:, : modulation_ref.shape[1]]
    return [
        jnp.dot(member, modulation_ref[part], preferred_element_type=F32) for part in range(3)
    ]


def layer_norm(values):
    average = jnp.mean(values, axis=-1, keepdims=True)
    centred = values - average
    inv_std = lax.rsqrt(jnp.mean(centred * centred, axis=-1, keepdims=True) + EPS)
    return centred * inv_std, inv_std


def head_sums(values):
    lanes = (LANES, LANES)
    first = lax.broadcasted_iota(jnp.int32, lanes, 0) < HEAD
    second = lax.broadcasted_iota(jnp.int32, lanes, 1) < HEAD
    ones = (first == second).astype(F32).astype(BF16)
    large = values.astype(BF16)
    small = (values - large.astype(F32)).astype(BF16)
    large = jnp.dot(large, ones, preferred_element_type=F32)
    return large + jnp.dot(small, ones, preferred_element_type=F32)


def both_heads(gains_ref, which):
    gain = gains_ref[which : which + 1, :]
    return jnp.concatenate([gain, gain], axis=1)


def head_scale(raw):
    return lax.rsqrt(head_sums(raw * raw) * (1.0 / HEAD) + EPS)


def enter_kernel(
    counts_ref,
    gains_ref,
    tokens_ref,
    cotangent_ref,
    w_qkv_ref,
    w_out_ref,
    modulation_ref,
    out_ref,
    raw_ref,
    raw_far_ref,
    rows_ref,
    factors_ref,
    hidden_ref,
    d_mixed_ref,
):
    rows = tokens_ref.shape[0]
    starts, ends = image_bounds(counts_ref, 0)
    place = block_index() * rows + lax.broadcasted_iota(jnp.int32, (rows, LANES), 0)
    member = ((place >= starts) & (place < ends)).astype(F32).astype(BF16)
    member = member[:, : modulation_ref.shape[1]]
    for part in range(3):
        factors_ref[part] = jnp.dot(member, modulation_ref[part], preferred_element_type=F32)
    for begin in range(0, rows, 16):
        at = slice(begin, begin + 16)
        normed, _ = layer_norm(tokens_ref[at, :].astype(F32))
        hidden = normed * (1.0 + factors_ref[1, at, :]) + factors_ref[0, at, :]
        hidden_ref[at, :] = hidden.astype(BF16)
        d_mixed = cotangent_ref[at, :].astype(F32) * factors_ref[2, at, :]
        d_mixed_ref[at, :] = d_mixed.astype(BF16)
    weights = jnp.concatenate([w_qkv_ref[part] for part in range(3)], axis=1)
    qkv = jnp.dot(hidden_ref[...], weights, preferred_element_type=F32)
    q, k, v = (qkv[:, part * LANES : (part + 1) * LANES] for part in range(3))
    d_attn = rows_dot(d_mixed_ref[...], w_out_ref[...])
    rows_ref[0] = q.astype(BF16)
    rows_ref[1] = k.astype(BF16)
    q = rows_ref[0].astype(F32)
    k = rows_ref[1].astype(F32)
    q = q * head_scale(q) * (both_heads(gains_ref, 0) * (1.0 / math.sqrt(HEAD)))
    k = k * head_scale(k) * both_heads(gains_ref, 1)
    core = lax.axis_index("core")
    share = raw_ref.shape[1] // 4
    for ref, side in ((raw_ref, core), (raw_far_ref, 1 - core)):
        for part in range(4):
            begin = pl.multiple_of((2 * part + side) * share, share)
            for array in range(2):
                ref[array, part * share : (part + 1) * share, :] = rows_ref[
                    array, pl.ds(begin, share), :
                ]
    low = low_lanes()

    def beside(left, right):
        return jnp.where(low, left, right).astype(BF16)

    q_v = (beside(q, pltpu.roll(v, HEAD, 1)), beside(pltpu.roll(q, HEAD, 1), v))
    k_d = (beside(k, pltpu.roll(d_attn, HEAD, 1)), beside(pltpu.roll(k, HEAD, 1), d_attn))
    for place in range(out_ref.shape[0]):
        out_ref[place, :, 0:LANES] = q_v[place % 2]
        out_ref[place, :, LANES:] = k_d[place % 2]


def enter(counts, gains, tokens, cotangent, w_parts, w_out, modulation, quad):
    rows = tokens.shape[0]
    raw = jax.ShapeDtypeStruct((2, rows // 2, LANES), BF16)
    return pl.pallas_call(
        enter_kernel,
        out_shape=(jax.ShapeDtypeStruct((quad, rows, 2 * LANES), BF16), raw, raw),
        in_specs=[SMEM] + [VMEM] * 6,
        out_specs=(VMEM,) * 3,
        scratch_shapes=[
            pltpu.VMEM((2, rows, LANES), BF16),
            pltpu.VMEM((3,) + tokens.shape, F32),
            pltpu.VMEM(tokens.shape, BF16),
            pltpu.VMEM(tokens.shape, BF16),
        ],
        compiler_params=pltpu.CompilerParams(vmem_limit_bytes=ENTER_LIMIT),
    )(counts, gains, tokens, cotangent, w_parts, w_out, modulation)


def pack_kernel(w_qkv_ref, w_out_ref, raw_ref, weights_ref, sems):
    width = w_out_ref.shape[1]
    rows = raw_ref.shape[1]
    pairs = []
    for part in range(3):
        pairs.append((w_qkv_ref.at[part], weights_ref.at[part * width : (part + 1) * width, :]))
    for tile in range(width // LANES):
        at = slice(tile * LANES, (tile + 1) * LANES)
        to = slice(3 * width + tile * LANES, 3 * width + (tile + 1) * LANES)
        pairs.append((w_out_ref.at[:, at], weights_ref.at[to, :]))
    for array in range(2):
        to = slice(4 * width + array * rows, 4 * width + (array + 1) * rows)
        pairs.append((raw_ref.at[array], weights_ref.at[to, :]))
    copies = [
        pltpu.make_async_copy(source, target, sems.at[place])
        for place, (source, target) in enumerate(pairs)
    ]
    for copy in copies:
        copy.start()
    for copy in copies:
        copy.wait()


def pack(w_parts, w_out, raw):
    width = w_out.shape[1]
    whole = pl.BlockSpec(memory_space=pl.ANY)
    return pl.pallas_call(
        pack_kernel,
        out_shape=jax.ShapeDtypeStruct((4 * width + 2 * raw.shape[1], LANES), BF16),
        in_specs=[whole] * 3,
        out_specs=VMEM,
        scratch_shapes=[pltpu.SemaphoreType.DMA((5 + width // LANES,))],
        compiler_params=pltpu.CompilerParams(vmem_limit_bytes=8 * 1024 * 1024),
    )(w_parts, w_out, raw)


def w_out_of(weights_ref, width):
    return jnp.concatenate(
        [
            weights_ref[3 * width + tile * LANES : 3 * width + (tile + 1) * LANES, :]
            for tile in range(width // LANES)
        ],
        axis=1,
    )


LOG2_E = math.log2(math.e)
INV_ROOT = 1.0 / math.sqrt(HEAD)
CHUNK = 256
TILE = 64
MAIN = 6
REACH_CHUNKS = 4


def low_lanes():
    return lax.broadcasted_iota(jnp.int32, (1, LANES), 1) < HEAD


def place_block(source, place, starts, ends, stores):
    low = low_lanes()
    rows = source.shape[0]
    at = place + lax.broadcasted_iota(jnp.int32, (rows, LANES), 0)
    same = ((at >= starts) & (at < ends)).astype(F32)
    first = source[:, 0:LANES].astype(F32)
    second = source[:, LANES:].astype(F32)
    q_store, k_store, v_store, d_store, kv_store = stores
    q_store[...] = jnp.where(low, first, same * SAME_IMAGE).astype(BF16)
    k_store[...] = jnp.where(low, second, same).astype(BF16)
    v_store[...] = jnp.where(low, 0.0, first).astype(BF16)
    d_store[...] = source[:, LANES:]
    kv_store[...] = jnp.where(low, second, first).astype(BF16).T


def window_facts(counts_ref):
    half = lax.axis_index("yh")
    origin = (block_index() // 4 - 1) * 2 * CHUNK
    own_at = (2 + half) * CHUNK
    starts, ends = image_bounds(counts_ref, HEAD)
    left_from = jnp.int32(-CHUNK)
    right_to = jnp.int32((MAIN + 1) * CHUNK)
    total = -origin
    for image in range(counts_ref.shape[0]):
        left_from = jnp.where(total <= own_at, total, left_from)
        ended = total >= own_at + CHUNK
        total = total + counts_ref[image]
        right_to = jnp.where((total >= own_at + CHUNK) & jnp.logical_not(ended), total, right_to)
    return half, own_at, starts - origin, ends - origin, left_from, right_to


def by_eight(values):
    return values.reshape(values.shape[0] // 8, 8, values.shape[1])


def add_tiles(s_ref, g_ref, rows, highest, total, grads):
    for piece in range(rows // TILE):
        at = slice(piece * TILE, (piece + 1) * TILE)
        weights = jnp.exp2(s_ref[at, :] * LOG2_E - highest)
        total = total + jnp.sum(by_eight(weights), axis=0)
        grads = grads + jnp.sum(by_eight(weights * g_ref[at, :]), axis=0)
    return total, grads


def rows_max(values):
    return jnp.max(by_eight(values), axis=0)


def chunks_from(key, count, *refs):
    rows = [pl.ds(pl.multiple_of(key + i * CHUNK, CHUNK), CHUNK) for i in range(count)]
    return [tuple(ref.at[at, :] for ref in refs) for at in rows]


def running_sums(pieces, q_block, d_block, s_ref, g_ref):
    highest = jnp.full((8, CHUNK), -jnp.inf, F32)
    total = jnp.zeros((8, CHUNK), F32)
    grads = jnp.zeros((8, CHUNK), F32)
    for piece, (keys_ref, values_ref) in enumerate(pieces):
        here = slice(piece * CHUNK, (piece + 1) * CHUNK)
        scores = rows_dot(keys_ref[...], q_block)
        s_ref[here, :] = scores
        g_ref[here, :] = rows_dot(values_ref[...], d_block)
        higher = jnp.maximum(highest, rows_max(scores) * LOG2_E)
        shrink = jnp.exp2(highest - higher)
        total = total * shrink
        grads = grads * shrink
        highest = higher
        for tile in range(CHUNK // TILE):
            at = slice(piece * CHUNK + tile * TILE, piece * CHUNK + (tile + 1) * TILE)
            weights = jnp.exp2(by_eight(s_ref[at, :]) * LOG2_E - highest[None])
            total = total + jnp.sum(weights, axis=0)
            grads = grads + jnp.sum(weights * by_eight(g_ref[at, :]), axis=0)
    top = jnp.max(highest, axis=0, keepdims=True)
    shrink = jnp.exp2(highest - top)
    total = jnp.sum(total * shrink, axis=0, keepdims=True)
    return top, total, jnp.sum(grads * shrink, axis=0, keepdims=True)


def early_kernel(
    counts_ref,
    first_ref,
    quad_ref,
    qa_ref,
    ka_ref,
    va_ref,
    da_ref,
    kva_ref,
    sa_ref,
    ga_ref,
    top_ref,
):
    half, _, starts, ends, _, _ = window_facts(counts_ref)
    block_rows = CHUNK // 2
    to_first = jnp.where(lax.rem(lax.axis_index("z"), 2) == 0, 2 * CHUNK, -2 * CHUNK)
    for block in range(8):
        at = slice(block * block_rows, (block + 1) * block_rows)
        inner = slice(block % 4 * block_rows, (block % 4 + 1) * block_rows)
        place = 2 * CHUNK + block % 4 * block_rows
        stores = [ref.at[at, :] for ref in (qa_ref, ka_ref, va_ref, da_ref)]
        stores.append(kva_ref.at[:, at])
        if block < 4:
            place_block(quad_ref.at[inner], place, starts, ends, stores)
        else:
            place_block(first_ref.at[inner], place + to_first, starts, ends, stores)

    own_rows = pl.ds(pl.multiple_of(half * CHUNK, CHUNK), CHUNK)
    q_own = qa_ref[own_rows, :]
    d_own = da_ref[own_rows, :]
    highest = jnp.full((8, CHUNK), -jnp.inf, F32)
    for piece in range(4):
        at = slice(piece * CHUNK, (piece + 1) * CHUNK)
        scores = rows_dot(ka_ref[at, :], q_own)
        sa_ref[at, :] = scores
        highest = jnp.maximum(highest, rows_max(scores))
        ga_ref[at, :] = rows_dot(va_ref[at, :], d_own)
    top_ref[...] = highest


def attend_early(counts, first, quad):
    rows = 4 * CHUNK
    head_rows = jax.ShapeDtypeStruct((rows, LANES), BF16)
    scores = jax.ShapeDtypeStruct((rows, CHUNK), F32)
    return pl.pallas_call(
        early_kernel,
        out_shape=(head_rows,) * 4
        + (jax.ShapeDtypeStruct((LANES, rows), BF16), scores, scores)
        + (jax.ShapeDtypeStruct((8, CHUNK), F32),),
        in_specs=[SMEM] + [VMEM] * 2,
        out_specs=(VMEM,) * 8,
        compiler_params=pltpu.CompilerParams(vmem_limit_bytes=VMEM_LIMIT),
    )(counts, first, quad)


def near_kernel(
    counts_ref,
    second_ref,
    qa_ref,
    ka_ref,
    va_ref,
    da_ref,
    kva_ref,
    sa_ref,
    ga_ref,
    top_ref,
    qx_ref,
    kx_ref,
    vx_ref,
    dx_ref,
    kv_ref,
    so_ref,
    go_ref,
    sn_ref,
    gn_ref,
    stats_ref,
    s_ref,
    g_ref,
):
    half, own_at, starts, ends, left_from, right_to = window_facts(counts_ref)
    block_rows = CHUNK // 2
    even = lax.rem(lax.axis_index("z"), 2) == 0
    first_at = pl.multiple_of(jnp.where(even, 4 * CHUNK, 0), 2 * CHUNK)
    second_at = pl.multiple_of(jnp.where(even, 0, 4 * CHUNK), 2 * CHUNK)
    early = ((qa_ref, qx_ref), (ka_ref, kx_ref), (va_ref, vx_ref), (da_ref, dx_ref))
    for source, target in early:
        target[2 * CHUNK : 4 * CHUNK, :] = source[0 : 2 * CHUNK, :]
        target[pl.ds(first_at, 2 * CHUNK), :] = source[2 * CHUNK : 4 * CHUNK, :]
    kv_ref[:, 2 * CHUNK : 4 * CHUNK] = kva_ref[:, 0 : 2 * CHUNK]
    kv_ref[:, pl.ds(first_at, 2 * CHUNK)] = kva_ref[:, 2 * CHUNK : 4 * CHUNK]
    for block in range(4):
        inner = slice(block * block_rows, (block + 1) * block_rows)
        begin = pl.multiple_of(second_at + block * block_rows, block_rows)
        at = pl.ds(begin, block_rows)
        stores = [ref.at[at, :] for ref in (qx_ref, kx_ref, vx_ref, dx_ref)]
        place_block(second_ref.at[inner], begin, starts, ends, stores + [kv_ref.at[:, at]])

    own_rows = pl.ds(pl.multiple_of(half * CHUNK, CHUNK), CHUNK)
    q_own = qa_ref[own_rows, :]
    d_own = da_ref[own_rows, :]
    highest = top_ref[...]
    for piece in range(2):
        at = pl.ds(pl.multiple_of(second_at + piece * CHUNK, CHUNK), CHUNK)
        scores = rows_dot(kx_ref[at, :], q_own)
        so_ref[at, :] = scores
        highest = jnp.maximum(highest, rows_max(scores))
        go_ref[at, :] = rows_dot(vx_ref[at, :], d_own)
    highest = jnp.max(highest, axis=0, keepdims=True) * LOG2_E
    total = jnp.zeros((8, CHUNK), F32)
    grads = jnp.zeros((8, CHUNK), F32)
    for piece in range(MAIN * CHUNK // TILE):
        inner = piece * TILE
        if inner < 2 * CHUNK:
            to = pl.ds(2 * CHUNK + inner, TILE)
        elif inner < 4 * CHUNK:
            to = pl.ds(pl.multiple_of(first_at + inner - 2 * CHUNK, TILE), TILE)
        else:
            to = pl.ds(pl.multiple_of(second_at + inner - 4 * CHUNK, TILE), TILE)
        if inner < 4 * CHUNK:
            scores = sa_ref[inner : inner + TILE, :]
            given = ga_ref[inner : inner + TILE, :]
            go_ref[to, :] = given
        else:
            scores = so_ref[to, :]
            given = go_ref[to, :]
        weights = jnp.exp2(scores * LOG2_E - highest)
        so_ref[to, :] = weights
        total = total + jnp.sum(by_eight(weights), axis=0)
        grads = grads + jnp.sum(by_eight(weights * given), axis=0)
    stats_ref[MAIN, 0:1, :] = highest
    stats_ref[MAIN, 1:2, :] = jnp.sum(total, axis=0, keepdims=True)
    stats_ref[MAIN, 2:3, :] = jnp.sum(grads, axis=0, keepdims=True)

    left_key = jnp.clip((left_from + CHUNK) // CHUNK - 1, 0, MAIN - REACH_CHUNKS)
    right_key = jnp.clip((right_to - 1) // CHUNK - (REACH_CHUNKS - 1), 0, MAIN - REACH_CHUNKS)

    def one_chunk(step, carry):
        slot = step + jnp.where(step >= 2 + half, 1, 0)
        begin = slot * CHUNK

        @pl.when((begin < right_to) & (begin + CHUNK > left_from))
        def _():
            at = pl.ds(pl.multiple_of(begin, CHUNK), CHUNK)
            key = jnp.where(begin < own_at, left_key, right_key) * CHUNK
            q_block = qx_ref[at, :]
            d_block = dx_ref[at, :]
            pieces = chunks_from(key, REACH_CHUNKS, kx_ref, vx_ref)
            highest, total, grads = running_sums(pieces, q_block, d_block, s_ref, g_ref)
            stats_ref[slot, 0:1, :] = highest
            stats_ref[slot, 1:2, :] = total
            stats_ref[slot, 2:3, :] = grads
            near_at = pl.ds(pl.multiple_of(own_at - key, CHUNK), CHUNK)
            sn_ref[slot, :, :] = s_ref[near_at, :]
            gn_ref[slot, :, :] = g_ref[near_at, :]

        return carry

    lax.fori_loop(0, MAIN - 1, one_chunk, 0)


def attend_near(counts, second, early):
    rows = MAIN * CHUNK
    head_rows = jax.ShapeDtypeStruct((rows, LANES), BF16)
    scores = jax.ShapeDtypeStruct((rows, CHUNK), F32)
    tiles = jax.ShapeDtypeStruct((MAIN, CHUNK, CHUNK), F32)
    return pl.pallas_call(
        near_kernel,
        out_shape=(head_rows,) * 4
        + (jax.ShapeDtypeStruct((LANES, rows), BF16),)
        + (scores, scores, tiles, tiles, jax.ShapeDtypeStruct((MAIN + 1, 8, CHUNK), F32)),
        in_specs=[SMEM] + [VMEM] * (1 + len(early)),
        out_specs=(VMEM,) * 10,
        scratch_shapes=[pltpu.VMEM((REACH_CHUNKS * CHUNK, CHUNK), F32)] * 2,
        cost_estimate=pl.CostEstimate(
            flops=9000000000, bytes_accessed=1 << 20, transcendentals=1 << 20
        ),
        compiler_params=pltpu.CompilerParams(vmem_limit_bytes=VMEM_LIMIT),
    )(counts, second, *early)


def far_kernel(
    counts_ref,
    far_ref,
    qx_ref,
    kx_ref,
    vx_ref,
    dx_ref,
    kv_ref,
    so_ref,
    go_ref,
    sn_ref,
    gn_ref,
    stats_ref,
    out_ref,
    qf_ref,
    kf_ref,
    vf_ref,
    df_ref,
    kvf_ref,
    s_ref,
    g_ref,
    p_ref,
    d_ref,
    pn_ref,
    dn_ref,
    sums_ref,
    dk_ref,
    dv_ref,
    own_out_ref,
    done_ref,
):
    half, own_at, starts, ends, left_from, right_to = window_facts(counts_ref)
    block_rows = CHUNK // 2
    rows = MAIN * CHUNK
    far_at = jnp.where(half == 0, -CHUNK, rows)
    for block in range(2):
        at = slice(block * block_rows, (block + 1) * block_rows)
        stores = [ref.at[at, :] for ref in (qf_ref, kf_ref, vf_ref, df_ref)]
        place_block(
            far_ref.at[at],
            far_at + block * block_rows,
            starts,
            ends,
            stores + [kvf_ref.at[:, at]],
        )

    own_rows = pl.ds(pl.multiple_of(own_at, CHUNK), CHUNK)
    q_own = qx_ref[own_rows, :]
    d_own = dx_ref[own_rows, :]
    scores = rows_dot(kf_ref[...], q_own)
    s_ref[0:CHUNK, :] = scores
    g_ref[0:CHUNK, :] = rows_dot(vf_ref[...], d_own)
    near_highest = stats_ref[MAIN, 0:1, :]
    highest = jnp.max(rows_max(scores), axis=0, keepdims=True) * LOG2_E
    highest = jnp.maximum(near_highest, highest)
    shrink = jnp.exp2(near_highest - highest)
    zeros = jnp.zeros((8, CHUNK), F32)
    total, grads = add_tiles(s_ref, g_ref, CHUNK, highest, zeros, zeros)
    total = jnp.sum(total, axis=0, keepdims=True) + stats_ref[MAIN, 1:2, :] * shrink
    grads = jnp.sum(grads, axis=0, keepdims=True) + stats_ref[MAIN, 2:3, :] * shrink
    scale = 1.0 / total
    mean_grad = grads * scale

    near_scale = shrink * scale
    for piece in range(rows // TILE):
        at = slice(piece * TILE, (piece + 1) * TILE)
        probs = so_ref[at, :] * near_scale
        p_ref[at, :] = probs.astype(BF16)
        d_ref[at, :] = (probs * (go_ref[at, :] - mean_grad)).astype(BF16)
    for piece in range(CHUNK // TILE):
        at = slice(piece * TILE, (piece + 1) * TILE)
        to = slice(rows + piece * TILE, rows + (piece + 1) * TILE)
        probs = jnp.exp2(s_ref[at, :] * LOG2_E - highest) * scale
        p_ref[to, :] = probs.astype(BF16)
        d_ref[to, :] = (probs * (g_ref[at, :] - mean_grad)).astype(BF16)
    pn_ref[:, own_rows] = p_ref[own_rows, :]
    dn_ref[:, own_rows] = d_ref[own_rows, :]

    def times_window(values_ref):
        main = jnp.dot(kv_ref[...], values_ref[0:rows, :], preferred_element_type=F32)
        return main + jnp.dot(
            kvf_ref[...], values_ref[rows : rows + CHUNK, :], preferred_element_type=F32
        )

    upper = lax.broadcasted_iota(jnp.int32, (LANES, CHUNK), 0) < HEAD
    own_out_ref[...] = jnp.where(
        upper, times_window(d_ref) * INV_ROOT, times_window(p_ref)
    ).T

    query_lane = lax.broadcasted_iota(jnp.int32, (1, CHUNK), 1)
    reaches_far = jnp.where(half == 0, left_from < 0, right_to > rows)
    sums_ref[...] = stats_ref[...]
    dk_ref[...] = jnp.zeros_like(dk_ref)
    dv_ref[...] = jnp.zeros_like(dv_ref)

    @pl.when(reaches_far)
    def _():
        for step in range(2):
            slot = half * (MAIN - 2) + step
            at = pl.ds(pl.multiple_of(slot * CHUNK, CHUNK), CHUNK)
            space = pl.ds((REACH_CHUNKS + step) * CHUNK, CHUNK)
            highest, total, grads = running_sums(
                [(kf_ref, vf_ref)], qx_ref[at, :], dx_ref[at, :], s_ref.at[space], g_ref.at[space]
            )
            before = sums_ref[slot, 0:1, :]
            higher = jnp.maximum(before, highest)
            old = jnp.exp2(before - higher)
            new = jnp.exp2(highest - higher)
            sums_ref[slot, 0:1, :] = higher
            sums_ref[slot, 1:2, :] = sums_ref[slot, 1:2, :] * old + total * new
            sums_ref[slot, 2:3, :] = sums_ref[slot, 2:3, :] * old + grads * new

        q_block = qf_ref[...]
        d_block = df_ref[...]
        key = half * (MAIN // 2) * CHUNK
        pieces = chunks_from(key, REACH_CHUNKS - 1, kx_ref, vx_ref) + [(kf_ref, vf_ref)]
        highest, total, grads = running_sums(pieces, q_block, d_block, s_ref, g_ref)
        place = query_lane + far_at
        scale = jnp.where((place >= left_from) & (place < right_to), 1.0 / total, 0.0)
        mean_grad = grads * scale
        for piece in range(CHUNK // TILE):
            at = slice(piece * TILE, (piece + 1) * TILE)
            near_at = pl.ds(pl.multiple_of(own_at - key + piece * TILE, TILE), TILE)
            probs = jnp.exp2(s_ref[near_at, :] * LOG2_E - highest) * scale
            p_ref[at, :] = probs.astype(BF16)
            d_ref[at, :] = (probs * (g_ref[near_at, :] - mean_grad)).astype(BF16)
        dk_ref[...] = jnp.dot(d_ref[0:CHUNK, :], q_block, preferred_element_type=F32)
        dv_ref[...] = jnp.dot(p_ref[0:CHUNK, :], d_block, preferred_element_type=F32)

    for step in range(MAIN - 1):
        slot = step + jnp.where(step >= 2 + half, 1, 0)
        begin = slot * CHUNK
        chunk_at = pl.ds(pl.multiple_of(begin, CHUNK), CHUNK)
        place = query_lane + begin
        valid = (place >= left_from) & (place < right_to)
        highest = sums_ref[slot, 0:1, :]
        scale = 1.0 / sums_ref[slot, 1:2, :]
        mean_grad = sums_ref[slot, 2:3, :] * scale
        for piece in range(CHUNK // TILE):
            at = slice(piece * TILE, (piece + 1) * TILE)
            probs = jnp.exp2(sn_ref[slot, at, :] * LOG2_E - highest) * scale
            d_scores = probs * (gn_ref[slot, at, :] - mean_grad)
            pn_ref[at, chunk_at] = jnp.where(valid, probs, 0.0).astype(BF16)
            dn_ref[at, chunk_at] = jnp.where(valid, d_scores, 0.0).astype(BF16)
    d_key = dk_ref[...] + jnp.dot(dn_ref[...], qx_ref[...], preferred_element_type=F32)
    d_value = dv_ref[...] + jnp.dot(pn_ref[...], dx_ref[...], preferred_element_type=F32)
    done_ref[:, 0:LANES] = own_out_ref[...].astype(BF16)
    done_ref[:, LANES:] = jnp.where(low_lanes(), d_key, d_value).astype(BF16)
    share = 16
    for member in range(out_ref.shape[0]):
        block, core = member // 2, member % 2
        for part in range(out_ref.shape[1] // share):
            begin = (block * 8 + part * 2 + core) * share
            out_ref[member, part * share : (part + 1) * share, :] = done_ref[
                begin : begin + share, :
            ]


def attend_far(counts, far, near_parts):
    return pl.pallas_call(
        far_kernel,
        out_shape=jax.ShapeDtypeStruct((4, CHUNK // 4, 2 * LANES), BF16),
        in_specs=[SMEM] + [VMEM] * (1 + len(near_parts)),
        out_specs=VMEM,
        scratch_shapes=[pltpu.VMEM((CHUNK, LANES), BF16)] * 4
        + [pltpu.VMEM((LANES, CHUNK), BF16)]
        + [pltpu.VMEM(((REACH_CHUNKS + 2) * CHUNK, CHUNK), F32)] * 2
        + [pltpu.VMEM(((MAIN + 1) * CHUNK, CHUNK), BF16)] * 2
        + [pltpu.VMEM((CHUNK, MAIN * CHUNK), BF16)] * 2
        + [pltpu.VMEM((MAIN + 1, 8, CHUNK), F32)]
        + [pltpu.VMEM((CHUNK, LANES), F32)] * 3
        + [pltpu.VMEM((CHUNK, 2 * LANES), BF16)],
        cost_estimate=pl.CostEstimate(
            flops=9000000000, bytes_accessed=1 << 20, transcendentals=1 << 20
        ),
        compiler_params=pltpu.CompilerParams(vmem_limit_bytes=VMEM_LIMIT),
    )(counts, far, *near_parts)


def project_kernel(parts_ref, gains_ref, raw_ref, weights_ref, weights_far_ref, out_ref):
    rows = parts_ref.shape[1]
    width = out_ref.shape[2] // 2
    share = out_ref.shape[1]
    core = lax.axis_index("core")
    low = low_lanes()
    q_gain = both_heads(gains_ref, 0)
    k_gain = both_heads(gains_ref, 1)

    def norm_grad(raw, gain, d_norm):
        raw = raw.astype(F32)
        inverse = head_scale(raw)
        scaled = d_norm * gain
        inner = head_sums(raw * scaled) * (1.0 / HEAD)
        return inverse * scaled - raw * (inverse * inverse * inverse * inner)

    def by_column(which, raw):
        head0 = parts_ref[which].astype(F32)
        head1 = parts_ref[2 + which].astype(F32)
        a0, a1 = head0[:, :LANES], head1[:, :LANES]
        b0, b1 = head0[:, LANES:], head1[:, LANES:]
        d_q = norm_grad(raw[0], q_gain, jnp.where(low, a0, pltpu.roll(a1, HEAD, 1)))
        attn = jnp.where(low, pltpu.roll(a0, HEAD, 1), a1).astype(BF16)
        d_k = norm_grad(raw[1], k_gain, jnp.where(low, b0, pltpu.roll(b1, HEAD, 1)))
        d_v = jnp.where(low, pltpu.roll(b0, HEAD, 1), b1)
        return attn, [values.astype(BF16) for values in (d_q, d_k, d_v)]

    raw_far = [
        weights_far_ref[4 * width + array * rows : 4 * width + (array + 1) * rows, :]
        for array in range(2)
    ]
    attn, grads = by_column(core, [raw_ref[0], raw_ref[1]])
    attn_far, grads_far = by_column(1 - core, raw_far)
    both = (weights_ref, weights_far_ref)
    mixed = jnp.dot(
        jnp.concatenate([attn, attn_far], axis=1),
        jnp.concatenate([w_out_of(ref, width) for ref in both], axis=0),
        preferred_element_type=F32,
    ).astype(BF16)
    weights = [ref[part * width : (part + 1) * width, :] for ref in both for part in range(3)]
    d_hidden = rows_dot(
        jnp.concatenate(grads + grads_far, axis=1), jnp.concatenate(weights, axis=1)
    ).astype(BF16)
    for place in range(out_ref.shape[0]):
        at = slice(place * share, (place + 1) * share)
        out_ref[place, :, :width] = mixed[at]
        out_ref[place, :, width:] = d_hidden[at]


def project(parts, gains, raw, weights, weights_far, x_count, width):
    return pl.pallas_call(
        project_kernel,
        out_shape=jax.ShapeDtypeStruct((x_count, parts.shape[1] // x_count, 2 * width), BF16),
        in_specs=[VMEM] * 5,
        out_specs=VMEM,
        compiler_params=pltpu.CompilerParams(vmem_limit_bytes=VMEM_LIMIT),
    )(parts, gains, raw, weights, weights_far)


def ready_kernel(
    counts_ref,
    tokens_ref,
    cotangent_ref,
    modulation_ref,
    rows_ref,
    factors_ref,
):
    rows = rows_ref.shape[1]
    first_row = (lax.axis_index("x") * 2 + lax.axis_index("core")) * rows
    first = block_index() * tokens_ref.shape[0] + first_row
    _, scale, gate = modulation_rows(counts_ref, modulation_ref, first, rows)
    at = pl.ds(pl.multiple_of(first_row, rows), rows)
    normed, inv_std = layer_norm(tokens_ref[at, :].astype(F32))
    rows_ref[0] = tokens_ref[at, :]
    rows_ref[1] = cotangent_ref[at, :]
    factors_ref[0] = gate
    factors_ref[1] = 1.0 + scale
    factors_ref[2] = normed
    factors_ref[3] = jnp.broadcast_to(inv_std, normed.shape)


def ready(counts, tokens, cotangent, modulation, share):
    width = tokens.shape[1]
    return pl.pallas_call(
        ready_kernel,
        out_shape=(
            jax.ShapeDtypeStruct((2, share, width), BF16),
            jax.ShapeDtypeStruct((4, share, width), F32),
        ),
        in_specs=[SMEM] + [VMEM] * 3,
        out_specs=(VMEM, VMEM),
        compiler_params=pltpu.CompilerParams(vmem_limit_bytes=VMEM_LIMIT),
    )(counts, tokens, cotangent, modulation)


def leave_kernel(rows_ref, factors_ref, shares_ref, layer_ref, grad_ref):
    width = layer_ref.shape[1]
    sums = shares_ref[0].astype(F32)
    for share in range(1, shares_ref.shape[0]):
        sums = sums + shares_ref[share].astype(F32)
    layer = rows_ref[0].astype(F32) + factors_ref[0] * sums[:, :width]
    layer_ref[...] = layer.astype(BF16)
    d_normed = sums[:, width:] * factors_ref[1]
    normed = factors_ref[2]
    input_grad = rows_ref[1].astype(F32) + factors_ref[3] * (
        d_normed
        - jnp.mean(d_normed, axis=-1, keepdims=True)
        - normed * jnp.mean(d_normed * normed, axis=-1, keepdims=True)
    )
    grad_ref[...] = input_grad.astype(BF16)


def leave(rows, factors, shares):
    out = jax.ShapeDtypeStruct(rows.shape[1:], BF16)
    return pl.pallas_call(
        leave_kernel,
        out_shape=(out, out),
        in_specs=[VMEM] * 3,
        out_specs=(VMEM, VMEM),
        compiler_params=pltpu.CompilerParams(vmem_limit_bytes=VMEM_LIMIT),
    )(rows, factors, shares)


def per_device(tokens, cotangent, w_qkv, w_out, qk_gain, modulation, image_counts):
    tok_rows, model_width = tokens.shape
    z_count = lax.axis_size("z")
    x_count = lax.axis_size("x")
    quad = 4
    pair_rows = 2 * tok_rows
    share = tok_rows // (2 * x_count)
    w_parts = w_qkv.transpose(1, 0, 2)
    mod_parts = modulation.transpose(1, 0, 2)

    heads, raw, raw_far = enter(
        image_counts, qk_gain, tokens, cotangent, w_parts, w_out, mod_parts, quad
    )
    _, tokens_late, cotangent_late, mod_late, w_parts_late, w_out_late = (
        lax.optimization_barrier((heads, tokens, cotangent, mod_parts, w_parts, w_out))
    )
    rows, factors = ready(image_counts, tokens_late, cotangent_late, mod_late, share)
    weights = pack(w_parts_late, w_out_late, raw_far)
    mine = lax.all_to_all(heads, ("yh", "yl"), 0, 0)
    mine, rows, factors, weights = lax.optimization_barrier((mine, rows, factors, weights))
    mine = mine.reshape(quad * tok_rows, 2 * LANES)
    evens = range(0, z_count, 2)
    swaps = [(i, i + 1) for i in evens], [((i - 1) % z_count, i) for i in evens]
    first, second = (
        lax.ppermute(mine, "z", pairs + [(j, i) for i, j in pairs]) for pairs in swaps
    )
    halves = 4 * z_count
    far_half = jnp.where(
        lax.axis_index("yh") == lax.axis_index("core"), mine[pair_rows:], mine[:pair_rows]
    )

    def far_source(target):
        z, yh, core = target // 4, target // 2 % 2, target % 2
        return (z + (2 if yh else -2)) % z_count * 4 + (yh ^ core) * 2 + core

    far = lax.ppermute(
        far_half, ("z", "yh", "core"), [(far_source(i), i) for i in range(halves)]
    )
    early = attend_early(image_counts, first, mine)
    near_parts = attend_near(image_counts, second, early)
    weights_far = lax.ppermute(weights, "core", [(0, 1), (1, 0)])
    parts = attend_far(image_counts, far, near_parts)
    parts = lax.all_to_all(parts, ("yl", "core"), 0, 0)
    partial = project(parts, qk_gain, raw, weights, weights_far, x_count, model_width)
    shares = lax.all_to_all(partial, "x", 0, 0)
    return leave(rows, factors, shares)


def solution(mesh):
    split = jax.sharding.Mesh(mesh.devices.reshape(16, 2, 2, 4, 2), ("z", "yh", "yl", "x", "core"))
    dp, head = ("z", "yh", "yl"), ("x", "core")
    in_specs = (P(dp, None), P(dp, None), P(None, None, head), P(head, None), P(), P(), P())
    out_specs = (P(dp + head, None), P(dp + head, None))
    return jax.shard_map(
        per_device, mesh=split, in_specs=in_specs, out_specs=out_specs, check_vma=False
    )
```

```python
import math

import jax
import jax.numpy as jnp
from jax import lax
from jax.experimental import pallas as pl
from jax.experimental.pallas import tpu as pltpu
from jax.sharding import PartitionSpec as P

EPS = 1e-06
SAME_IMAGE = 512.0
LANES = 128
HEAD = 64
F32 = jnp.float32
BF16 = jnp.bfloat16
VMEM_LIMIT = 24 * 1024 * 1024
ENTER_LIMIT = 60 * 1024 * 1024
VMEM = pl.BlockSpec(memory_space=pltpu.VMEM)
SMEM = pl.BlockSpec(memory_space=pltpu.SMEM)


def rows_dot(a, b):
    return lax.dot_general(a, b, (((1,), (1,)), ((), ())), preferred_element_type=F32)


def block_index():
    return (lax.axis_index("z") * 2 + lax.axis_index("yh")) * 2 + lax.axis_index("yl")


def image_bounds(counts_ref, first_lane):
    lane = lax.broadcasted_iota(jnp.int32, (1, LANES), 1)
    starts = jnp.zeros((1, LANES), jnp.int32)
    ends = jnp.zeros((1, LANES), jnp.int32)
    total = jnp.int32(0)
    for image in range(counts_ref.shape[0]):
        here = lane == first_lane + image
        starts = jnp.where(here, total, starts)
        total = total + counts_ref[image]
        ends = jnp.where(here, total, ends)
    return starts, ends


def modulation_rows(counts_ref, modulation_ref, first, rows):
    starts, ends = image_bounds(counts_ref, 0)
    place = first + lax.broadcasted_iota(jnp.int32, (rows, LANES), 0)
    member = ((place >= starts) & (place < ends)).astype(F32).astype(BF16)
    member = member[:, : modulation_ref.shape[1]]
    return [
        jnp.dot(member, modulation_ref[part], preferred_element_type=F32) for part in range(3)
    ]


def layer_norm(values):
    average = jnp.mean(values, axis=-1, keepdims=True)
    centred = values - average
    inv_std = lax.rsqrt(jnp.mean(centred * centred, axis=-1, keepdims=True) + EPS)
    return centred * inv_std, inv_std


def head_sums(values):
    lanes = (LANES, LANES)
    first = lax.broadcasted_iota(jnp.int32, lanes, 0) < HEAD
    second = lax.broadcasted_iota(jnp.int32, lanes, 1) < HEAD
    ones = (first == second).astype(F32).astype(BF16)
    large = values.astype(BF16)
    small = (values - large.astype(F32)).astype(BF16)
    large = jnp.dot(large, ones, preferred_element_type=F32)
    return large + jnp.dot(small, ones, preferred_element_type=F32)


def both_heads(gains_ref, which):
    gain = gains_ref[which : which + 1, :]
    return jnp.concatenate([gain, gain], axis=1)


def head_scale(raw):
    return lax.rsqrt(head_sums(raw * raw) * (1.0 / HEAD) + EPS)


def enter_kernel(
    counts_ref,
    gains_ref,
    tokens_ref,
    cotangent_ref,
    w_qkv_ref,
    w_out_ref,
    modulation_ref,
    out_ref,
    raw_ref,
    raw_far_ref,
    rows_ref,
    factors_ref,
    hidden_ref,
    d_mixed_ref,
):
    rows = tokens_ref.shape[0]
    starts, ends = image_bounds(counts_ref, 0)
    place = block_index() * rows + lax.broadcasted_iota(jnp.int32, (rows, LANES), 0)
    member = ((place >= starts) & (place < ends)).astype(F32).astype(BF16)
    member = member[:, : modulation_ref.shape[1]]
    for part in range(3):
        factors_ref[part] = jnp.dot(member, modulation_ref[part], preferred_element_type=F32)
    for begin in range(0, rows, 16):
        at = slice(begin, begin + 16)
        normed, _ = layer_norm(tokens_ref[at, :].astype(F32))
        hidden = normed * (1.0 + factors_ref[1, at, :]) + factors_ref[0, at, :]
        hidden_ref[at, :] = hidden.astype(BF16)
        d_mixed = cotangent_ref[at, :].astype(F32) * factors_ref[2, at, :]
        d_mixed_ref[at, :] = d_mixed.astype(BF16)
    weights = jnp.concatenate([w_qkv_ref[part] for part in range(3)], axis=1)
    qkv = jnp.dot(hidden_ref[...], weights, preferred_element_type=F32)
    q, k, v = (qkv[:, part * LANES : (part + 1) * LANES] for part in range(3))
    d_attn = rows_dot(d_mixed_ref[...], w_out_ref[...])
    rows_ref[0] = q.astype(BF16)
    rows_ref[1] = k.astype(BF16)
    q = rows_ref[0].astype(F32)
    k = rows_ref[1].astype(F32)
    q = q * head_scale(q) * (both_heads(gains_ref, 0) * (1.0 / math.sqrt(HEAD)))
    k = k * head_scale(k) * both_heads(gains_ref, 1)
    core = lax.axis_index("core")
    share = raw_ref.shape[1] // 4
    for ref, side in ((raw_ref, core), (raw_far_ref, 1 - core)):
        for part in range(4):
            begin = pl.multiple_of((2 * part + side) * share, share)
            for array in range(2):
                ref[array, part * share : (part + 1) * share, :] = rows_ref[
                    array, pl.ds(begin, share), :
                ]
    low = low_lanes()

    def beside(left, right):
        return jnp.where(low, left, right).astype(BF16)

    q_v = (beside(q, pltpu.roll(v, HEAD, 1)), beside(pltpu.roll(q, HEAD, 1), v))
    k_d = (beside(k, pltpu.roll(d_attn, HEAD, 1)), beside(pltpu.roll(k, HEAD, 1), d_attn))
    for place in range(out_ref.shape[0]):
        out_ref[place, :, 0:LANES] = q_v[place % 2]
        out_ref[place, :, LANES:] = k_d[place % 2]


def enter(counts, gains, tokens, cotangent, w_parts, w_out, modulation, quad):
    rows = tokens.shape[0]
    raw = jax.ShapeDtypeStruct((2, rows // 2, LANES), BF16)
    return pl.pallas_call(
        enter_kernel,
        out_shape=(jax.ShapeDtypeStruct((quad, rows, 2 * LANES), BF16), raw, raw),
        in_specs=[SMEM] + [VMEM] * 6,
        out_specs=(VMEM,) * 3,
        scratch_shapes=[
            pltpu.VMEM((2, rows, LANES), BF16),
            pltpu.VMEM((3,) + tokens.shape, F32),
            pltpu.VMEM(tokens.shape, BF16),
            pltpu.VMEM(tokens.shape, BF16),
        ],
        compiler_params=pltpu.CompilerParams(vmem_limit_bytes=ENTER_LIMIT),
    )(counts, gains, tokens, cotangent, w_parts, w_out, modulation)


def pack_kernel(w_qkv_ref, w_out_ref, raw_ref, weights_ref, sems):
    width = w_out_ref.shape[1]
    rows = raw_ref.shape[1]
    pairs = []
    for part in range(3):
        pairs.append((w_qkv_ref.at[part], weights_ref.at[part * width : (part + 1) * width, :]))
    for tile in range(width // LANES):
        at = slice(tile * LANES, (tile + 1) * LANES)
        to = slice(3 * width + tile * LANES, 3 * width + (tile + 1) * LANES)
        pairs.append((w_out_ref.at[:, at], weights_ref.at[to, :]))
    for array in range(2):
        to = slice(4 * width + array * rows, 4 * width + (array + 1) * rows)
        pairs.append((raw_ref.at[array], weights_ref.at[to, :]))
    copies = [
        pltpu.make_async_copy(source, target, sems.at[place])
        for place, (source, target) in enumerate(pairs)
    ]
    for copy in copies:
        copy.start()
    for copy in copies:
        copy.wait()


def pack(w_parts, w_out, raw):
    width = w_out.shape[1]
    whole = pl.BlockSpec(memory_space=pl.ANY)
    return pl.pallas_call(
        pack_kernel,
        out_shape=jax.ShapeDtypeStruct((4 * width + 2 * raw.shape[1], LANES), BF16),
        in_specs=[whole] * 3,
        out_specs=VMEM,
        scratch_shapes=[pltpu.SemaphoreType.DMA((5 + width // LANES,))],
        compiler_params=pltpu.CompilerParams(vmem_limit_bytes=8 * 1024 * 1024),
    )(w_parts, w_out, raw)


def w_out_of(weights_ref, width):
    return jnp.concatenate(
        [
            weights_ref[3 * width + tile * LANES : 3 * width + (tile + 1) * LANES, :]
            for tile in range(width // LANES)
        ],
        axis=1,
    )


LOG2_E = math.log2(math.e)
INV_ROOT = 1.0 / math.sqrt(HEAD)
CHUNK = 256
TILE = 64
MAIN = 6
REACH_CHUNKS = 4


def low_lanes():
    return lax.broadcasted_iota(jnp.int32, (1, LANES), 1) < HEAD


def place_block(source, place, starts, ends, stores):
    low = low_lanes()
    rows = source.shape[0]
    at = place + lax.broadcasted_iota(jnp.int32, (rows, LANES), 0)
    same = ((at >= starts) & (at < ends)).astype(F32)
    first = source[:, 0:LANES].astype(F32)
    second = source[:, LANES:].astype(F32)
    q_store, k_store, v_store, d_store, kv_store = stores
    q_store[...] = jnp.where(low, first, same * SAME_IMAGE).astype(BF16)
    k_store[...] = jnp.where(low, second, same).astype(BF16)
    v_store[...] = jnp.where(low, 0.0, first).astype(BF16)
    d_store[...] = source[:, LANES:]
    kv_store[...] = jnp.where(low, second, first).astype(BF16).T


def window_facts(counts_ref):
    half = lax.axis_index("yh")
    origin = (block_index() // 4 - 1) * 2 * CHUNK
    own_at = (2 + half) * CHUNK
    starts, ends = image_bounds(counts_ref, HEAD)
    left_from = jnp.int32(-CHUNK)
    right_to = jnp.int32((MAIN + 1) * CHUNK)
    total = -origin
    for image in range(counts_ref.shape[0]):
        left_from = jnp.where(total <= own_at, total, left_from)
        ended = total >= own_at + CHUNK
        total = total + counts_ref[image]
        right_to = jnp.where((total >= own_at + CHUNK) & jnp.logical_not(ended), total, right_to)
    return half, own_at, starts - origin, ends - origin, left_from, right_to


def by_eight(values):
    return values.reshape(values.shape[0] // 8, 8, values.shape[1])


def add_tiles(s_ref, g_ref, rows, highest, total, grads):
    for piece in range(rows // TILE):
        at = slice(piece * TILE, (piece + 1) * TILE)
        weights = jnp.exp2(s_ref[at, :] * LOG2_E - highest)
        total = total + jnp.sum(by_eight(weights), axis=0)
        grads = grads + jnp.sum(by_eight(weights * g_ref[at, :]), axis=0)
    return total, grads


def rows_max(values):
    return jnp.max(by_eight(values), axis=0)


def chunks_from(key, count, *refs):
    rows = [pl.ds(pl.multiple_of(key + i * CHUNK, CHUNK), CHUNK) for i in range(count)]
    return [tuple(ref.at[at, :] for ref in refs) for at in rows]


def running_sums(pieces, q_block, d_block, s_ref, g_ref):
    highest = jnp.full((8, CHUNK), -jnp.inf, F32)
    total = jnp.zeros((8, CHUNK), F32)
    grads = jnp.zeros((8, CHUNK), F32)
    for piece, (keys_ref, values_ref) in enumerate(pieces):
        here = slice(piece * CHUNK, (piece + 1) * CHUNK)
        scores = rows_dot(keys_ref[...], q_block)
        s_ref[here, :] = scores
        g_ref[here, :] = rows_dot(values_ref[...], d_block)
        higher = jnp.maximum(highest, rows_max(scores) * LOG2_E)
        shrink = jnp.exp2(highest - higher)
        total = total * shrink
        grads = grads * shrink
        highest = higher
        for tile in range(CHUNK // TILE):
            at = slice(piece * CHUNK + tile * TILE, piece * CHUNK + (tile + 1) * TILE)
            weights = jnp.exp2(by_eight(s_ref[at, :]) * LOG2_E - highest[None])
            total = total + jnp.sum(weights, axis=0)
            grads = grads + jnp.sum(weights * by_eight(g_ref[at, :]), axis=0)
    top = jnp.max(highest, axis=0, keepdims=True)
    shrink = jnp.exp2(highest - top)
    total = jnp.sum(total * shrink, axis=0, keepdims=True)
    return top, total, jnp.sum(grads * shrink, axis=0, keepdims=True)


def early_kernel(
    counts_ref,
    first_ref,
    quad_ref,
    qa_ref,
    ka_ref,
    va_ref,
    da_ref,
    kva_ref,
    sa_ref,
    ga_ref,
    top_ref,
):
    half, _, starts, ends, _, _ = window_facts(counts_ref)
    block_rows = CHUNK // 2
    to_first = jnp.where(lax.rem(lax.axis_index("z"), 2) == 0, 2 * CHUNK, -2 * CHUNK)
    for block in range(8):
        at = slice(block * block_rows, (block + 1) * block_rows)
        inner = slice(block % 4 * block_rows, (block % 4 + 1) * block_rows)
        place = 2 * CHUNK + block % 4 * block_rows
        stores = [ref.at[at, :] for ref in (qa_ref, ka_ref, va_ref, da_ref)]
        stores.append(kva_ref.at[:, at])
        if block < 4:
            place_block(quad_ref.at[inner], place, starts, ends, stores)
        else:
            place_block(first_ref.at[inner], place + to_first, starts, ends, stores)

    own_rows = pl.ds(pl.multiple_of(half * CHUNK, CHUNK), CHUNK)
    q_own = qa_ref[own_rows, :]
    d_own = da_ref[own_rows, :]
    highest = jnp.full((8, CHUNK), -jnp.inf, F32)
    for piece in range(4):
        at = slice(piece * CHUNK, (piece + 1) * CHUNK)
        scores = rows_dot(ka_ref[at, :], q_own)
        sa_ref[at, :] = scores
        highest = jnp.maximum(highest, rows_max(scores))
        ga_ref[at, :] = rows_dot(va_ref[at, :], d_own)
    top_ref[...] = highest


def attend_early(counts, first, quad):
    rows = 4 * CHUNK
    head_rows = jax.ShapeDtypeStruct((rows, LANES), BF16)
    scores = jax.ShapeDtypeStruct((rows, CHUNK), F32)
    return pl.pallas_call(
        early_kernel,
        out_shape=(head_rows,) * 4
        + (jax.ShapeDtypeStruct((LANES, rows), BF16), scores, scores)
        + (jax.ShapeDtypeStruct((8, CHUNK), F32),),
        in_specs=[SMEM] + [VMEM] * 2,
        out_specs=(VMEM,) * 8,
        compiler_params=pltpu.CompilerParams(vmem_limit_bytes=VMEM_LIMIT),
    )(counts, first, quad)


def near_kernel(
    counts_ref,
    second_ref,
    qa_ref,
    ka_ref,
    va_ref,
    da_ref,
    kva_ref,
    sa_ref,
    ga_ref,
    top_ref,
    qx_ref,
    kx_ref,
    vx_ref,
    dx_ref,
    kv_ref,
    so_ref,
    go_ref,
    sn_ref,
    gn_ref,
    stats_ref,
    s_ref,
    g_ref,
):
    half, own_at, starts, ends, left_from, right_to = window_facts(counts_ref)
    block_rows = CHUNK // 2
    even = lax.rem(lax.axis_index("z"), 2) == 0
    first_at = pl.multiple_of(jnp.where(even, 4 * CHUNK, 0), 2 * CHUNK)
    second_at = pl.multiple_of(jnp.where(even, 0, 4 * CHUNK), 2 * CHUNK)
    early = ((qa_ref, qx_ref), (ka_ref, kx_ref), (va_ref, vx_ref), (da_ref, dx_ref))
    for source, target in early:
        target[2 * CHUNK : 4 * CHUNK, :] = source[0 : 2 * CHUNK, :]
        target[pl.ds(first_at, 2 * CHUNK), :] = source[2 * CHUNK : 4 * CHUNK, :]
    kv_ref[:, 2 * CHUNK : 4 * CHUNK] = kva_ref[:, 0 : 2 * CHUNK]
    kv_ref[:, pl.ds(first_at, 2 * CHUNK)] = kva_ref[:, 2 * CHUNK : 4 * CHUNK]
    for block in range(4):
        inner = slice(block * block_rows, (block + 1) * block_rows)
        begin = pl.multiple_of(second_at + block * block_rows, block_rows)
        at = pl.ds(begin, block_rows)
        stores = [ref.at[at, :] for ref in (qx_ref, kx_ref, vx_ref, dx_ref)]
        place_block(second_ref.at[inner], begin, starts, ends, stores + [kv_ref.at[:, at]])

    own_rows = pl.ds(pl.multiple_of(half * CHUNK, CHUNK), CHUNK)
    q_own = qa_ref[own_rows, :]
    d_own = da_ref[own_rows, :]
    highest = top_ref[...]
    for piece in range(2):
        at = pl.ds(pl.multiple_of(second_at + piece * CHUNK, CHUNK), CHUNK)
        scores = rows_dot(kx_ref[at, :], q_own)
        so_ref[at, :] = scores
        highest = jnp.maximum(highest, rows_max(scores))
        go_ref[at, :] = rows_dot(vx_ref[at, :], d_own)
    highest = jnp.max(highest, axis=0, keepdims=True) * LOG2_E
    total = jnp.zeros((8, CHUNK), F32)
    grads = jnp.zeros((8, CHUNK), F32)
    for piece in range(MAIN * CHUNK // TILE):
        inner = piece * TILE
        if inner < 2 * CHUNK:
            to = pl.ds(2 * CHUNK + inner, TILE)
        elif inner < 4 * CHUNK:
            to = pl.ds(pl.multiple_of(first_at + inner - 2 * CHUNK, TILE), TILE)
        else:
            to = pl.ds(pl.multiple_of(second_at + inner - 4 * CHUNK, TILE), TILE)
        if inner < 4 * CHUNK:
            scores = sa_ref[inner : inner + TILE, :]
            given = ga_ref[inner : inner + TILE, :]
            go_ref[to, :] = given
        else:
            scores = so_ref[to, :]
            given = go_ref[to, :]
        weights = jnp.exp2(scores * LOG2_E - highest)
        so_ref[to, :] = weights
        total = total + jnp.sum(by_eight(weights), axis=0)
        grads = grads + jnp.sum(by_eight(weights * given), axis=0)
    stats_ref[MAIN, 0:1, :] = highest
    stats_ref[MAIN, 1:2, :] = jnp.sum(total, axis=0, keepdims=True)
    stats_ref[MAIN, 2:3, :] = jnp.sum(grads, axis=0, keepdims=True)

    left_key = jnp.clip((left_from + CHUNK) // CHUNK - 1, 0, MAIN - REACH_CHUNKS)
    right_key = jnp.clip((right_to - 1) // CHUNK - (REACH_CHUNKS - 1), 0, MAIN - REACH_CHUNKS)

    def one_chunk(step, carry):
        slot = step + jnp.where(step >= 2 + half, 1, 0)
        begin = slot * CHUNK

        @pl.when((begin < right_to) & (begin + CHUNK > left_from))
        def _():
            at = pl.ds(pl.multiple_of(begin, CHUNK), CHUNK)
            key = jnp.where(begin < own_at, left_key, right_key) * CHUNK
            q_block = qx_ref[at, :]
            d_block = dx_ref[at, :]
            pieces = chunks_from(key, REACH_CHUNKS, kx_ref, vx_ref)
            highest, total, grads = running_sums(pieces, q_block, d_block, s_ref, g_ref)
            stats_ref[slot, 0:1, :] = highest
            stats_ref[slot, 1:2, :] = total
            stats_ref[slot, 2:3, :] = grads
            near_at = pl.ds(pl.multiple_of(own_at - key, CHUNK), CHUNK)
            sn_ref[slot, :, :] = s_ref[near_at, :]
            gn_ref[slot, :, :] = g_ref[near_at, :]

        return carry

    lax.fori_loop(0, MAIN - 1, one_chunk, 0)


def attend_near(counts, second, early):
    rows = MAIN * CHUNK
    head_rows = jax.ShapeDtypeStruct((rows, LANES), BF16)
    scores = jax.ShapeDtypeStruct((rows, CHUNK), F32)
    tiles = jax.ShapeDtypeStruct((MAIN, CHUNK, CHUNK), F32)
    return pl.pallas_call(
        near_kernel,
        out_shape=(head_rows,) * 4
        + (jax.ShapeDtypeStruct((LANES, rows), BF16),)
        + (scores, scores, tiles, tiles, jax.ShapeDtypeStruct((MAIN + 1, 8, CHUNK), F32)),
        in_specs=[SMEM] + [VMEM] * (1 + len(early)),
        out_specs=(VMEM,) * 10,
        scratch_shapes=[pltpu.VMEM((REACH_CHUNKS * CHUNK, CHUNK), F32)] * 2,
        cost_estimate=pl.CostEstimate(
            flops=5000000000, bytes_accessed=1 << 20, transcendentals=1 << 20
        ),
        compiler_params=pltpu.CompilerParams(vmem_limit_bytes=VMEM_LIMIT),
    )(counts, second, *early)


def far_kernel(
    counts_ref,
    far_ref,
    qx_ref,
    kx_ref,
    vx_ref,
    dx_ref,
    kv_ref,
    so_ref,
    go_ref,
    sn_ref,
    gn_ref,
    stats_ref,
    out_ref,
    qf_ref,
    kf_ref,
    vf_ref,
    df_ref,
    kvf_ref,
    s_ref,
    g_ref,
    p_ref,
    d_ref,
    pn_ref,
    dn_ref,
    sums_ref,
    dk_ref,
    dv_ref,
    own_out_ref,
    done_ref,
):
    half, own_at, starts, ends, left_from, right_to = window_facts(counts_ref)
    block_rows = CHUNK // 2
    rows = MAIN * CHUNK
    far_at = jnp.where(half == 0, -CHUNK, rows)
    for block in range(2):
        at = slice(block * block_rows, (block + 1) * block_rows)
        stores = [ref.at[at, :] for ref in (qf_ref, kf_ref, vf_ref, df_ref)]
        place_block(
            far_ref.at[at],
            far_at + block * block_rows,
            starts,
            ends,
            stores + [kvf_ref.at[:, at]],
        )

    own_rows = pl.ds(pl.multiple_of(own_at, CHUNK), CHUNK)
    q_own = qx_ref[own_rows, :]
    d_own = dx_ref[own_rows, :]
    scores = rows_dot(kf_ref[...], q_own)
    s_ref[0:CHUNK, :] = scores
    g_ref[0:CHUNK, :] = rows_dot(vf_ref[...], d_own)
    near_highest = stats_ref[MAIN, 0:1, :]
    highest = jnp.max(rows_max(scores), axis=0, keepdims=True) * LOG2_E
    highest = jnp.maximum(near_highest, highest)
    shrink = jnp.exp2(near_highest - highest)
    zeros = jnp.zeros((8, CHUNK), F32)
    total, grads = add_tiles(s_ref, g_ref, CHUNK, highest, zeros, zeros)
    total = jnp.sum(total, axis=0, keepdims=True) + stats_ref[MAIN, 1:2, :] * shrink
    grads = jnp.sum(grads, axis=0, keepdims=True) + stats_ref[MAIN, 2:3, :] * shrink
    scale = 1.0 / total
    mean_grad = grads * scale

    near_scale = shrink * scale
    for piece in range(rows // TILE):
        at = slice(piece * TILE, (piece + 1) * TILE)
        probs = so_ref[at, :] * near_scale
        p_ref[at, :] = probs.astype(BF16)
        d_ref[at, :] = (probs * (go_ref[at, :] - mean_grad)).astype(BF16)
    for piece in range(CHUNK // TILE):
        at = slice(piece * TILE, (piece + 1) * TILE)
        to = slice(rows + piece * TILE, rows + (piece + 1) * TILE)
        probs = jnp.exp2(s_ref[at, :] * LOG2_E - highest) * scale
        p_ref[to, :] = probs.astype(BF16)
        d_ref[to, :] = (probs * (g_ref[at, :] - mean_grad)).astype(BF16)
    pn_ref[:, own_rows] = p_ref[own_rows, :]
    dn_ref[:, own_rows] = d_ref[own_rows, :]

    def times_window(values_ref):
        main = jnp.dot(kv_ref[...], values_ref[0:rows, :], preferred_element_type=F32)
        return main + jnp.dot(
            kvf_ref[...], values_ref[rows : rows + CHUNK, :], preferred_element_type=F32
        )

    upper = lax.broadcasted_iota(jnp.int32, (LANES, CHUNK), 0) < HEAD
    own_out_ref[...] = jnp.where(
        upper, times_window(d_ref) * INV_ROOT, times_window(p_ref)
    ).T

    query_lane = lax.broadcasted_iota(jnp.int32, (1, CHUNK), 1)
    reaches_far = jnp.where(half == 0, left_from < 0, right_to > rows)
    sums_ref[...] = stats_ref[...]
    dk_ref[...] = jnp.zeros_like(dk_ref)
    dv_ref[...] = jnp.zeros_like(dv_ref)

    @pl.when(reaches_far)
    def _():
        for step in range(2):
            slot = half * (MAIN - 2) + step
            at = pl.ds(pl.multiple_of(slot * CHUNK, CHUNK), CHUNK)
            space = pl.ds((REACH_CHUNKS + step) * CHUNK, CHUNK)
            highest, total, grads = running_sums(
                [(kf_ref, vf_ref)], qx_ref[at, :], dx_ref[at, :], s_ref.at[space], g_ref.at[space]
            )
            before = sums_ref[slot, 0:1, :]
            higher = jnp.maximum(before, highest)
            old = jnp.exp2(before - higher)
            new = jnp.exp2(highest - higher)
            sums_ref[slot, 0:1, :] = higher
            sums_ref[slot, 1:2, :] = sums_ref[slot, 1:2, :] * old + total * new
            sums_ref[slot, 2:3, :] = sums_ref[slot, 2:3, :] * old + grads * new

        q_block = qf_ref[...]
        d_block = df_ref[...]
        key = half * (MAIN // 2) * CHUNK
        pieces = chunks_from(key, REACH_CHUNKS - 1, kx_ref, vx_ref) + [(kf_ref, vf_ref)]
        highest, total, grads = running_sums(pieces, q_block, d_block, s_ref, g_ref)
        place = query_lane + far_at
        scale = jnp.where((place >= left_from) & (place < right_to), 1.0 / total, 0.0)
        mean_grad = grads * scale
        for piece in range(CHUNK // TILE):
            at = slice(piece * TILE, (piece + 1) * TILE)
            near_at = pl.ds(pl.multiple_of(own_at - key + piece * TILE, TILE), TILE)
            probs = jnp.exp2(s_ref[near_at, :] * LOG2_E - highest) * scale
            p_ref[at, :] = probs.astype(BF16)
            d_ref[at, :] = (probs * (g_ref[near_at, :] - mean_grad)).astype(BF16)
        dk_ref[...] = jnp.dot(d_ref[0:CHUNK, :], q_block, preferred_element_type=F32)
        dv_ref[...] = jnp.dot(p_ref[0:CHUNK, :], d_block, preferred_element_type=F32)

    for step in range(MAIN - 1):
        slot = step + jnp.where(step >= 2 + half, 1, 0)
        begin = slot * CHUNK
        chunk_at = pl.ds(pl.multiple_of(begin, CHUNK), CHUNK)
        place = query_lane + begin
        valid = (place >= left_from) & (place < right_to)
        highest = sums_ref[slot, 0:1, :]
        scale = 1.0 / sums_ref[slot, 1:2, :]
        mean_grad = sums_ref[slot, 2:3, :] * scale
        for piece in range(CHUNK // TILE):
            at = slice(piece * TILE, (piece + 1) * TILE)
            probs = jnp.exp2(sn_ref[slot, at, :] * LOG2_E - highest) * scale
            d_scores = probs * (gn_ref[slot, at, :] - mean_grad)
            pn_ref[at, chunk_at] = jnp.where(valid, probs, 0.0).astype(BF16)
            dn_ref[at, chunk_at] = jnp.where(valid, d_scores, 0.0).astype(BF16)
    d_key = dk_ref[...] + jnp.dot(dn_ref[...], qx_ref[...], preferred_element_type=F32)
    d_value = dv_ref[...] + jnp.dot(pn_ref[...], dx_ref[...], preferred_element_type=F32)
    done_ref[:, 0:LANES] = own_out_ref[...].astype(BF16)
    done_ref[:, LANES:] = jnp.where(low_lanes(), d_key, d_value).astype(BF16)
    share = 16
    for member in range(out_ref.shape[0]):
        block, core = member // 2, member % 2
        for part in range(out_ref.shape[1] // share):
            begin = (block * 8 + part * 2 + core) * share
            out_ref[member, part * share : (part + 1) * share, :] = done_ref[
                begin : begin + share, :
            ]


def attend_far(counts, far, near_parts):
    return pl.pallas_call(
        far_kernel,
        out_shape=jax.ShapeDtypeStruct((4, CHUNK // 4, 2 * LANES), BF16),
        in_specs=[SMEM] + [VMEM] * (1 + len(near_parts)),
        out_specs=VMEM,
        scratch_shapes=[pltpu.VMEM((CHUNK, LANES), BF16)] * 4
        + [pltpu.VMEM((LANES, CHUNK), BF16)]
        + [pltpu.VMEM(((REACH_CHUNKS + 2) * CHUNK, CHUNK), F32)] * 2
        + [pltpu.VMEM(((MAIN + 1) * CHUNK, CHUNK), BF16)] * 2
        + [pltpu.VMEM((CHUNK, MAIN * CHUNK), BF16)] * 2
        + [pltpu.VMEM((MAIN + 1, 8, CHUNK), F32)]
        + [pltpu.VMEM((CHUNK, LANES), F32)] * 3
        + [pltpu.VMEM((CHUNK, 2 * LANES), BF16)],
        cost_estimate=pl.CostEstimate(
            flops=5000000000, bytes_accessed=1 << 20, transcendentals=1 << 20
        ),
        compiler_params=pltpu.CompilerParams(vmem_limit_bytes=VMEM_LIMIT),
    )(counts, far, *near_parts)


def project_kernel(parts_ref, gains_ref, raw_ref, weights_ref, weights_far_ref, out_ref):
    rows = parts_ref.shape[1]
    width = out_ref.shape[2] // 2
    share = out_ref.shape[1]
    core = lax.axis_index("core")
    low = low_lanes()
    q_gain = both_heads(gains_ref, 0)
    k_gain = both_heads(gains_ref, 1)

    def norm_grad(raw, gain, d_norm):
        raw = raw.astype(F32)
        inverse = head_scale(raw)
        scaled = d_norm * gain
        inner = head_sums(raw * scaled) * (1.0 / HEAD)
        return inverse * scaled - raw * (inverse * inverse * inverse * inner)

    def by_column(which, raw):
        head0 = parts_ref[which].astype(F32)
        head1 = parts_ref[2 + which].astype(F32)
        a0, a1 = head0[:, :LANES], head1[:, :LANES]
        b0, b1 = head0[:, LANES:], head1[:, LANES:]
        d_q = norm_grad(raw[0], q_gain, jnp.where(low, a0, pltpu.roll(a1, HEAD, 1)))
        attn = jnp.where(low, pltpu.roll(a0, HEAD, 1), a1).astype(BF16)
        d_k = norm_grad(raw[1], k_gain, jnp.where(low, b0, pltpu.roll(b1, HEAD, 1)))
        d_v = jnp.where(low, pltpu.roll(b0, HEAD, 1), b1)
        return attn, [values.astype(BF16) for values in (d_q, d_k, d_v)]

    raw_far = [
        weights_far_ref[4 * width + array * rows : 4 * width + (array + 1) * rows, :]
        for array in range(2)
    ]
    attn, grads = by_column(core, [raw_ref[0], raw_ref[1]])
    attn_far, grads_far = by_column(1 - core, raw_far)
    both = (weights_ref, weights_far_ref)
    mixed = jnp.dot(
        jnp.concatenate([attn, attn_far], axis=1),
        jnp.concatenate([w_out_of(ref, width) for ref in both], axis=0),
        preferred_element_type=F32,
    ).astype(BF16)
    weights = [ref[part * width : (part + 1) * width, :] for ref in both for part in range(3)]
    d_hidden = rows_dot(
        jnp.concatenate(grads + grads_far, axis=1), jnp.concatenate(weights, axis=1)
    ).astype(BF16)
    for place in range(out_ref.shape[0]):
        at = slice(place * share, (place + 1) * share)
        out_ref[place, :, :width] = mixed[at]
        out_ref[place, :, width:] = d_hidden[at]


def project(parts, gains, raw, weights, weights_far, x_count, width):
    return pl.pallas_call(
        project_kernel,
        out_shape=jax.ShapeDtypeStruct((x_count, parts.shape[1] // x_count, 2 * width), BF16),
        in_specs=[VMEM] * 5,
        out_specs=VMEM,
        compiler_params=pltpu.CompilerParams(vmem_limit_bytes=VMEM_LIMIT),
    )(parts, gains, raw, weights, weights_far)


def ready_kernel(
    counts_ref,
    tokens_ref,
    cotangent_ref,
    modulation_ref,
    rows_ref,
    factors_ref,
):
    rows = rows_ref.shape[1]
    first_row = (lax.axis_index("x") * 2 + lax.axis_index("core")) * rows
    first = block_index() * tokens_ref.shape[0] + first_row
    _, scale, gate = modulation_rows(counts_ref, modulation_ref, first, rows)
    at = pl.ds(pl.multiple_of(first_row, rows), rows)
    normed, inv_std = layer_norm(tokens_ref[at, :].astype(F32))
    rows_ref[0] = tokens_ref[at, :]
    rows_ref[1] = cotangent_ref[at, :]
    factors_ref[0] = gate
    factors_ref[1] = 1.0 + scale
    factors_ref[2] = normed
    factors_ref[3] = jnp.broadcast_to(inv_std, normed.shape)


def ready(counts, tokens, cotangent, modulation, share):
    width = tokens.shape[1]
    return pl.pallas_call(
        ready_kernel,
        out_shape=(
            jax.ShapeDtypeStruct((2, share, width), BF16),
            jax.ShapeDtypeStruct((4, share, width), F32),
        ),
        in_specs=[SMEM] + [VMEM] * 3,
        out_specs=(VMEM, VMEM),
        compiler_params=pltpu.CompilerParams(vmem_limit_bytes=VMEM_LIMIT),
    )(counts, tokens, cotangent, modulation)


def leave_kernel(rows_ref, factors_ref, shares_ref, layer_ref, grad_ref):
    width = layer_ref.shape[1]
    sums = shares_ref[0].astype(F32)
    for share in range(1, shares_ref.shape[0]):
        sums = sums + shares_ref[share].astype(F32)
    layer = rows_ref[0].astype(F32) + factors_ref[0] * sums[:, :width]
    layer_ref[...] = layer.astype(BF16)
    d_normed = sums[:, width:] * factors_ref[1]
    normed = factors_ref[2]
    input_grad = rows_ref[1].astype(F32) + factors_ref[3] * (
        d_normed
        - jnp.mean(d_normed, axis=-1, keepdims=True)
        - normed * jnp.mean(d_normed * normed, axis=-1, keepdims=True)
    )
    grad_ref[...] = input_grad.astype(BF16)


def leave(rows, factors, shares):
    out = jax.ShapeDtypeStruct(rows.shape[1:], BF16)
    return pl.pallas_call(
        leave_kernel,
        out_shape=(out, out),
        in_specs=[VMEM] * 3,
        out_specs=(VMEM, VMEM),
        compiler_params=pltpu.CompilerParams(vmem_limit_bytes=VMEM_LIMIT),
    )(rows, factors, shares)


def per_device(tokens, cotangent, w_qkv, w_out, qk_gain, modulation, image_counts):
    tok_rows, model_width = tokens.shape
    z_count = lax.axis_size("z")
    x_count = lax.axis_size("x")
    quad = 4
    pair_rows = 2 * tok_rows
    share = tok_rows // (2 * x_count)
    w_parts = w_qkv.transpose(1, 0, 2)
    mod_parts = modulation.transpose(1, 0, 2)

    heads, raw, raw_far = enter(
        image_counts, qk_gain, tokens, cotangent, w_parts, w_out, mod_parts, quad
    )
    _, tokens_late, cotangent_late, mod_late, w_parts_late, w_out_late = (
        lax.optimization_barrier((heads, tokens, cotangent, mod_parts, w_parts, w_out))
    )
    rows, factors = ready(image_counts, tokens_late, cotangent_late, mod_late, share)
    weights = pack(w_parts_late, w_out_late, raw_far)
    mine = lax.all_to_all(heads, ("yh", "yl"), 0, 0)
    mine, rows, factors, weights = lax.optimization_barrier((mine, rows, factors, weights))
    mine = mine.reshape(quad * tok_rows, 2 * LANES)
    evens = range(0, z_count, 2)
    swaps = [(i, i + 1) for i in evens], [((i - 1) % z_count, i) for i in evens]
    first, second = (
        lax.ppermute(mine, "z", pairs + [(j, i) for i, j in pairs]) for pairs in swaps
    )
    halves = 4 * z_count
    far_half = jnp.where(
        lax.axis_index("yh") == lax.axis_index("core"), mine[pair_rows:], mine[:pair_rows]
    )

    def far_source(target):
        z, yh, core = target // 4, target // 2 % 2, target % 2
        return (z + (2 if yh else -2)) % z_count * 4 + (yh ^ core) * 2 + core

    far = lax.ppermute(
        far_half, ("z", "yh", "core"), [(far_source(i), i) for i in range(halves)]
    )
    early = attend_early(image_counts, first, mine)
    near_parts = attend_near(image_counts, second, early)
    weights_far = lax.ppermute(weights, "core", [(0, 1), (1, 0)])
    parts = attend_far(image_counts, far, near_parts)
    parts = lax.all_to_all(parts, ("yl", "core"), 0, 0)
    partial = project(parts, qk_gain, raw, weights, weights_far, x_count, model_width)
    shares = lax.all_to_all(partial, "x", 0, 0)
    return leave(rows, factors, shares)


def solution(mesh):
    split = jax.sharding.Mesh(mesh.devices.reshape(16, 2, 2, 4, 2), ("z", "yh", "yl", "x", "core"))
    dp, head = ("z", "yh", "yl"), ("x", "core")
    in_specs = (P(dp, None), P(dp, None), P(None, None, head), P(head, None), P(), P(), P())
    out_specs = (P(dp + head, None), P(dp + head, None))
    return jax.shard_map(
        per_device, mesh=split, in_specs=in_specs, out_specs=out_specs, check_vma=False
    )
```

```python
import math

import jax
import jax.numpy as jnp
from jax import lax
from jax.experimental import pallas as pl
from jax.experimental.pallas import tpu as pltpu
from jax.sharding import PartitionSpec as P

EPS = 1e-06
SAME_IMAGE = 512.0
LANES = 128
HEAD = 64
F32 = jnp.float32
BF16 = jnp.bfloat16
VMEM_LIMIT = 24 * 1024 * 1024
ENTER_LIMIT = 60 * 1024 * 1024
VMEM = pl.BlockSpec(memory_space=pltpu.VMEM)
SMEM = pl.BlockSpec(memory_space=pltpu.SMEM)


def rows_dot(a, b):
    return lax.dot_general(a, b, (((1,), (1,)), ((), ())), preferred_element_type=F32)


def block_index():
    return (lax.axis_index("z") * 2 + lax.axis_index("yh")) * 2 + lax.axis_index("yl")


def image_bounds(counts_ref, first_lane):
    lane = lax.broadcasted_iota(jnp.int32, (1, LANES), 1)
    starts = jnp.zeros((1, LANES), jnp.int32)
    ends = jnp.zeros((1, LANES), jnp.int32)
    total = jnp.int32(0)
    for image in range(counts_ref.shape[0]):
        here = lane == first_lane + image
        starts = jnp.where(here, total, starts)
        total = total + counts_ref[image]
        ends = jnp.where(here, total, ends)
    return starts, ends


def modulation_rows(counts_ref, modulation_ref, first, rows):
    starts, ends = image_bounds(counts_ref, 0)
    place = first + lax.broadcasted_iota(jnp.int32, (rows, LANES), 0)
    member = ((place >= starts) & (place < ends)).astype(F32).astype(BF16)
    member = member[:, : modulation_ref.shape[1]]
    return [
        jnp.dot(member, modulation_ref[part], preferred_element_type=F32) for part in range(3)
    ]


def layer_norm(values):
    average = jnp.mean(values, axis=-1, keepdims=True)
    centred = values - average
    inv_std = lax.rsqrt(jnp.mean(centred * centred, axis=-1, keepdims=True) + EPS)
    return centred * inv_std, inv_std


def head_sums(values):
    lanes = (LANES, LANES)
    first = lax.broadcasted_iota(jnp.int32, lanes, 0) < HEAD
    second = lax.broadcasted_iota(jnp.int32, lanes, 1) < HEAD
    ones = (first == second).astype(F32).astype(BF16)
    large = values.astype(BF16)
    small = (values - large.astype(F32)).astype(BF16)
    large = jnp.dot(large, ones, preferred_element_type=F32)
    return large + jnp.dot(small, ones, preferred_element_type=F32)


def both_heads(gains_ref, which):
    gain = gains_ref[which : which + 1, :]
    return jnp.concatenate([gain, gain], axis=1)


def head_scale(raw):
    return lax.rsqrt(head_sums(raw * raw) * (1.0 / HEAD) + EPS)


def enter_kernel(
    counts_ref,
    gains_ref,
    tokens_ref,
    cotangent_ref,
    w_qkv_ref,
    w_out_ref,
    modulation_ref,
    out_ref,
    raw_ref,
    raw_far_ref,
    rows_ref,
    factors_ref,
    hidden_ref,
    d_mixed_ref,
):
    rows = tokens_ref.shape[0]
    starts, ends = image_bounds(counts_ref, 0)
    place = block_index() * rows + lax.broadcasted_iota(jnp.int32, (rows, LANES), 0)
    member = ((place >= starts) & (place < ends)).astype(F32).astype(BF16)
    member = member[:, : modulation_ref.shape[1]]
    for part in range(3):
        factors_ref[part] = jnp.dot(member, modulation_ref[part], preferred_element_type=F32)
    for begin in range(0, rows, 16):
        at = slice(begin, begin + 16)
        normed, _ = layer_norm(tokens_ref[at, :].astype(F32))
        hidden = normed * (1.0 + factors_ref[1, at, :]) + factors_ref[0, at, :]
        hidden_ref[at, :] = hidden.astype(BF16)
        d_mixed = cotangent_ref[at, :].astype(F32) * factors_ref[2, at, :]
        d_mixed_ref[at, :] = d_mixed.astype(BF16)
    weights = jnp.concatenate([w_qkv_ref[part] for part in range(3)], axis=1)
    qkv = jnp.dot(hidden_ref[...], weights, preferred_element_type=F32)
    q, k, v = (qkv[:, part * LANES : (part + 1) * LANES] for part in range(3))
    d_attn = rows_dot(d_mixed_ref[...], w_out_ref[...])
    rows_ref[0] = q.astype(BF16)
    rows_ref[1] = k.astype(BF16)
    q = rows_ref[0].astype(F32)
    k = rows_ref[1].astype(F32)
    q = q * head_scale(q) * (both_heads(gains_ref, 0) * (1.0 / math.sqrt(HEAD)))
    k = k * head_scale(k) * both_heads(gains_ref, 1)
    core = lax.axis_index("core")
    share = raw_ref.shape[1] // 4
    for ref, side in ((raw_ref, core), (raw_far_ref, 1 - core)):
        for part in range(4):
            begin = pl.multiple_of((2 * part + side) * share, share)
            for array in range(2):
                ref[array, part * share : (part + 1) * share, :] = rows_ref[
                    array, pl.ds(begin, share), :
                ]
    low = low_lanes()

    def beside(left, right):
        return jnp.where(low, left, right).astype(BF16)

    q_v = (beside(q, pltpu.roll(v, HEAD, 1)), beside(pltpu.roll(q, HEAD, 1), v))
    k_d = (beside(k, pltpu.roll(d_attn, HEAD, 1)), beside(pltpu.roll(k, HEAD, 1), d_attn))
    for place in range(out_ref.shape[0]):
        out_ref[place, :, 0:LANES] = q_v[place % 2]
        out_ref[place, :, LANES:] = k_d[place % 2]


def enter(counts, gains, tokens, cotangent, w_parts, w_out, modulation, quad):
    rows = tokens.shape[0]
    raw = jax.ShapeDtypeStruct((2, rows // 2, LANES), BF16)
    return pl.pallas_call(
        enter_kernel,
        out_shape=(jax.ShapeDtypeStruct((quad, rows, 2 * LANES), BF16), raw, raw),
        in_specs=[SMEM] + [VMEM] * 6,
        out_specs=(VMEM,) * 3,
        scratch_shapes=[
            pltpu.VMEM((2, rows, LANES), BF16),
            pltpu.VMEM((3,) + tokens.shape, F32),
            pltpu.VMEM(tokens.shape, BF16),
            pltpu.VMEM(tokens.shape, BF16),
        ],
        compiler_params=pltpu.CompilerParams(vmem_limit_bytes=ENTER_LIMIT),
    )(counts, gains, tokens, cotangent, w_parts, w_out, modulation)


def pack_kernel(w_qkv_ref, w_out_ref, raw_ref, weights_ref, sems):
    width = w_out_ref.shape[1]
    rows = raw_ref.shape[1]
    pairs = []
    for part in range(3):
        pairs.append((w_qkv_ref.at[part], weights_ref.at[part * width : (part + 1) * width, :]))
    for tile in range(width // LANES):
        at = slice(tile * LANES, (tile + 1) * LANES)
        to = slice(3 * width + tile * LANES, 3 * width + (tile + 1) * LANES)
        pairs.append((w_out_ref.at[:, at], weights_ref.at[to, :]))
    for array in range(2):
        to = slice(4 * width + array * rows, 4 * width + (array + 1) * rows)
        pairs.append((raw_ref.at[array], weights_ref.at[to, :]))
    copies = [
        pltpu.make_async_copy(source, target, sems.at[place])
        for place, (source, target) in enumerate(pairs)
    ]
    for copy in copies:
        copy.start()
    for copy in copies:
        copy.wait()


def pack(w_parts, w_out, raw):
    width = w_out.shape[1]
    whole = pl.BlockSpec(memory_space=pl.ANY)
    return pl.pallas_call(
        pack_kernel,
        out_shape=jax.ShapeDtypeStruct((4 * width + 2 * raw.shape[1], LANES), BF16),
        in_specs=[whole] * 3,
        out_specs=VMEM,
        scratch_shapes=[pltpu.SemaphoreType.DMA((5 + width // LANES,))],
        compiler_params=pltpu.CompilerParams(vmem_limit_bytes=8 * 1024 * 1024),
    )(w_parts, w_out, raw)


def w_out_of(weights_ref, width):
    return jnp.concatenate(
        [
            weights_ref[3 * width + tile * LANES : 3 * width + (tile + 1) * LANES, :]
            for tile in range(width // LANES)
        ],
        axis=1,
    )


LOG2_E = math.log2(math.e)
INV_ROOT = 1.0 / math.sqrt(HEAD)
CHUNK = 256
TILE = 64
MAIN = 6
REACH_CHUNKS = 4


def low_lanes():
    return lax.broadcasted_iota(jnp.int32, (1, LANES), 1) < HEAD


def place_block(source, place, starts, ends, stores):
    low = low_lanes()
    rows = source.shape[0]
    at = place + lax.broadcasted_iota(jnp.int32, (rows, LANES), 0)
    same = ((at >= starts) & (at < ends)).astype(F32)
    first = source[:, 0:LANES].astype(F32)
    second = source[:, LANES:].astype(F32)
    q_store, k_store, v_store, d_store, kv_store = stores
    q_store[...] = jnp.where(low, first, same * SAME_IMAGE).astype(BF16)
    k_store[...] = jnp.where(low, second, same).astype(BF16)
    v_store[...] = jnp.where(low, 0.0, first).astype(BF16)
    d_store[...] = source[:, LANES:]
    kv_store[...] = jnp.where(low, second, first).astype(BF16).T


def window_facts(counts_ref):
    half = lax.axis_index("yh")
    origin = (block_index() // 4 - 1) * 2 * CHUNK
    own_at = (2 + half) * CHUNK
    starts, ends = image_bounds(counts_ref, HEAD)
    left_from = jnp.int32(-CHUNK)
    right_to = jnp.int32((MAIN + 1) * CHUNK)
    total = -origin
    for image in range(counts_ref.shape[0]):
        left_from = jnp.where(total <= own_at, total, left_from)
        ended = total >= own_at + CHUNK
        total = total + counts_ref[image]
        right_to = jnp.where((total >= own_at + CHUNK) & jnp.logical_not(ended), total, right_to)
    return half, own_at, starts - origin, ends - origin, left_from, right_to


def by_eight(values):
    return values.reshape(values.shape[0] // 8, 8, values.shape[1])


def add_tiles(s_ref, g_ref, rows, highest, total, grads):
    for piece in range(rows // TILE):
        at = slice(piece * TILE, (piece + 1) * TILE)
        weights = jnp.exp2(s_ref[at, :] * LOG2_E - highest)
        total = total + jnp.sum(by_eight(weights), axis=0)
        grads = grads + jnp.sum(by_eight(weights * g_ref[at, :]), axis=0)
    return total, grads


def rows_max(values):
    return jnp.max(by_eight(values), axis=0)


def chunks_from(key, count, *refs):
    rows = [pl.ds(pl.multiple_of(key + i * CHUNK, CHUNK), CHUNK) for i in range(count)]
    return [tuple(ref.at[at, :] for ref in refs) for at in rows]


def running_sums(pieces, q_block, d_block, s_ref, g_ref):
    highest = jnp.full((8, CHUNK), -jnp.inf, F32)
    total = jnp.zeros((8, CHUNK), F32)
    grads = jnp.zeros((8, CHUNK), F32)
    for piece, (keys_ref, values_ref) in enumerate(pieces):
        here = slice(piece * CHUNK, (piece + 1) * CHUNK)
        scores = rows_dot(keys_ref[...], q_block)
        s_ref[here, :] = scores
        g_ref[here, :] = rows_dot(values_ref[...], d_block)
        higher = jnp.maximum(highest, rows_max(scores) * LOG2_E)
        shrink = jnp.exp2(highest - higher)
        total = total * shrink
        grads = grads * shrink
        highest = higher
        for tile in range(CHUNK // TILE):
            at = slice(piece * CHUNK + tile * TILE, piece * CHUNK + (tile + 1) * TILE)
            weights = jnp.exp2(by_eight(s_ref[at, :]) * LOG2_E - highest[None])
            total = total + jnp.sum(weights, axis=0)
            grads = grads + jnp.sum(weights * by_eight(g_ref[at, :]), axis=0)
    top = jnp.max(highest, axis=0, keepdims=True)
    shrink = jnp.exp2(highest - top)
    total = jnp.sum(total * shrink, axis=0, keepdims=True)
    return top, total, jnp.sum(grads * shrink, axis=0, keepdims=True)


def early_kernel(
    counts_ref,
    first_ref,
    quad_ref,
    qa_ref,
    ka_ref,
    va_ref,
    da_ref,
    kva_ref,
    sa_ref,
    ga_ref,
    top_ref,
):
    half, _, starts, ends, _, _ = window_facts(counts_ref)
    block_rows = CHUNK // 2
    to_first = jnp.where(lax.rem(lax.axis_index("z"), 2) == 0, 2 * CHUNK, -2 * CHUNK)
    for block in range(8):
        at = slice(block * block_rows, (block + 1) * block_rows)
        inner = slice(block % 4 * block_rows, (block % 4 + 1) * block_rows)
        place = 2 * CHUNK + block % 4 * block_rows
        stores = [ref.at[at, :] for ref in (qa_ref, ka_ref, va_ref, da_ref)]
        stores.append(kva_ref.at[:, at])
        if block < 4:
            place_block(quad_ref.at[inner], place, starts, ends, stores)
        else:
            place_block(first_ref.at[inner], place + to_first, starts, ends, stores)

    own_rows = pl.ds(pl.multiple_of(half * CHUNK, CHUNK), CHUNK)
    q_own = qa_ref[own_rows, :]
    d_own = da_ref[own_rows, :]
    highest = jnp.full((8, CHUNK), -jnp.inf, F32)
    for piece in range(4):
        at = slice(piece * CHUNK, (piece + 1) * CHUNK)
        scores = rows_dot(ka_ref[at, :], q_own)
        sa_ref[at, :] = scores
        highest = jnp.maximum(highest, rows_max(scores))
        ga_ref[at, :] = rows_dot(va_ref[at, :], d_own)
    top_ref[...] = highest


def attend_early(counts, first, quad):
    rows = 4 * CHUNK
    head_rows = jax.ShapeDtypeStruct((rows, LANES), BF16)
    scores = jax.ShapeDtypeStruct((rows, CHUNK), F32)
    return pl.pallas_call(
        early_kernel,
        out_shape=(head_rows,) * 4
        + (jax.ShapeDtypeStruct((LANES, rows), BF16), scores, scores)
        + (jax.ShapeDtypeStruct((8, CHUNK), F32),),
        in_specs=[SMEM] + [VMEM] * 2,
        out_specs=(VMEM,) * 8,
        compiler_params=pltpu.CompilerParams(vmem_limit_bytes=VMEM_LIMIT),
    )(counts, first, quad)


def near_kernel(
    counts_ref,
    second_ref,
    qa_ref,
    ka_ref,
    va_ref,
    da_ref,
    kva_ref,
    sa_ref,
    ga_ref,
    top_ref,
    qx_ref,
    kx_ref,
    vx_ref,
    dx_ref,
    kv_ref,
    so_ref,
    go_ref,
    sn_ref,
    gn_ref,
    stats_ref,
    s_ref,
    g_ref,
):
    half, own_at, starts, ends, left_from, right_to = window_facts(counts_ref)
    block_rows = CHUNK // 2
    even = lax.rem(lax.axis_index("z"), 2) == 0
    first_at = pl.multiple_of(jnp.where(even, 4 * CHUNK, 0), 2 * CHUNK)
    second_at = pl.multiple_of(jnp.where(even, 0, 4 * CHUNK), 2 * CHUNK)
    early = ((qa_ref, qx_ref), (ka_ref, kx_ref), (va_ref, vx_ref), (da_ref, dx_ref))
    for source, target in early:
        target[2 * CHUNK : 4 * CHUNK, :] = source[0 : 2 * CHUNK, :]
        target[pl.ds(first_at, 2 * CHUNK), :] = source[2 * CHUNK : 4 * CHUNK, :]
    kv_ref[:, 2 * CHUNK : 4 * CHUNK] = kva_ref[:, 0 : 2 * CHUNK]
    kv_ref[:, pl.ds(first_at, 2 * CHUNK)] = kva_ref[:, 2 * CHUNK : 4 * CHUNK]
    for block in range(4):
        inner = slice(block * block_rows, (block + 1) * block_rows)
        begin = pl.multiple_of(second_at + block * block_rows, block_rows)
        at = pl.ds(begin, block_rows)
        stores = [ref.at[at, :] for ref in (qx_ref, kx_ref, vx_ref, dx_ref)]
        place_block(second_ref.at[inner], begin, starts, ends, stores + [kv_ref.at[:, at]])

    own_rows = pl.ds(pl.multiple_of(half * CHUNK, CHUNK), CHUNK)
    q_own = qa_ref[own_rows, :]
    d_own = da_ref[own_rows, :]
    highest = top_ref[...]
    for piece in range(2):
        at = pl.ds(pl.multiple_of(second_at + piece * CHUNK, CHUNK), CHUNK)
        scores = rows_dot(kx_ref[at, :], q_own)
        so_ref[at, :] = scores
        highest = jnp.maximum(highest, rows_max(scores))
        go_ref[at, :] = rows_dot(vx_ref[at, :], d_own)
    highest = jnp.max(highest, axis=0, keepdims=True) * LOG2_E
    total = jnp.zeros((8, CHUNK), F32)
    grads = jnp.zeros((8, CHUNK), F32)
    for piece in range(MAIN * CHUNK // TILE):
        inner = piece * TILE
        if inner < 2 * CHUNK:
            to = pl.ds(2 * CHUNK + inner, TILE)
        elif inner < 4 * CHUNK:
            to = pl.ds(pl.multiple_of(first_at + inner - 2 * CHUNK, TILE), TILE)
        else:
            to = pl.ds(pl.multiple_of(second_at + inner - 4 * CHUNK, TILE), TILE)
        if inner < 4 * CHUNK:
            scores = sa_ref[inner : inner + TILE, :]
            given = ga_ref[inner : inner + TILE, :]
            go_ref[to, :] = given
        else:
            scores = so_ref[to, :]
            given = go_ref[to, :]
        weights = jnp.exp2(scores * LOG2_E - highest)
        so_ref[to, :] = weights
        total = total + jnp.sum(by_eight(weights), axis=0)
        grads = grads + jnp.sum(by_eight(weights * given), axis=0)
    stats_ref[MAIN, 0:1, :] = highest
    stats_ref[MAIN, 1:2, :] = jnp.sum(total, axis=0, keepdims=True)
    stats_ref[MAIN, 2:3, :] = jnp.sum(grads, axis=0, keepdims=True)

    left_key = jnp.clip((left_from + CHUNK) // CHUNK - 1, 0, MAIN - REACH_CHUNKS)
    right_key = jnp.clip((right_to - 1) // CHUNK - (REACH_CHUNKS - 1), 0, MAIN - REACH_CHUNKS)

    def one_chunk(step, carry):
        slot = step + jnp.where(step >= 2 + half, 1, 0)
        begin = slot * CHUNK

        @pl.when((begin < right_to) & (begin + CHUNK > left_from))
        def _():
            at = pl.ds(pl.multiple_of(begin, CHUNK), CHUNK)
            key = jnp.where(begin < own_at, left_key, right_key) * CHUNK
            q_block = qx_ref[at, :]
            d_block = dx_ref[at, :]
            pieces = chunks_from(key, REACH_CHUNKS, kx_ref, vx_ref)
            highest, total, grads = running_sums(pieces, q_block, d_block, s_ref, g_ref)
            stats_ref[slot, 0:1, :] = highest
            stats_ref[slot, 1:2, :] = total
            stats_ref[slot, 2:3, :] = grads
            near_at = pl.ds(pl.multiple_of(own_at - key, CHUNK), CHUNK)
            sn_ref[slot, :, :] = s_ref[near_at, :]
            gn_ref[slot, :, :] = g_ref[near_at, :]

        return carry

    lax.fori_loop(0, MAIN - 1, one_chunk, 0)


def attend_near(counts, second, early):
    rows = MAIN * CHUNK
    head_rows = jax.ShapeDtypeStruct((rows, LANES), BF16)
    scores = jax.ShapeDtypeStruct((rows, CHUNK), F32)
    tiles = jax.ShapeDtypeStruct((MAIN, CHUNK, CHUNK), F32)
    return pl.pallas_call(
        near_kernel,
        out_shape=(head_rows,) * 4
        + (jax.ShapeDtypeStruct((LANES, rows), BF16),)
        + (scores, scores, tiles, tiles, jax.ShapeDtypeStruct((MAIN + 1, 8, CHUNK), F32)),
        in_specs=[SMEM] + [VMEM] * (1 + len(early)),
        out_specs=(VMEM,) * 10,
        scratch_shapes=[pltpu.VMEM((REACH_CHUNKS * CHUNK, CHUNK), F32)] * 2,
        cost_estimate=pl.CostEstimate(
            flops=9000000000, bytes_accessed=1 << 20, transcendentals=1 << 20
        ),
        compiler_params=pltpu.CompilerParams(vmem_limit_bytes=VMEM_LIMIT),
    )(counts, second, *early)


def far_kernel(
    counts_ref,
    far_ref,
    qx_ref,
    kx_ref,
    vx_ref,
    dx_ref,
    kv_ref,
    so_ref,
    go_ref,
    sn_ref,
    gn_ref,
    stats_ref,
    out_ref,
    qf_ref,
    kf_ref,
    vf_ref,
    df_ref,
    kvf_ref,
    s_ref,
    g_ref,
    p_ref,
    d_ref,
    pn_ref,
    dn_ref,
    sums_ref,
    dk_ref,
    dv_ref,
    own_out_ref,
    done_ref,
):
    half, own_at, starts, ends, left_from, right_to = window_facts(counts_ref)
    block_rows = CHUNK // 2
    rows = MAIN * CHUNK
    far_at = jnp.where(half == 0, -CHUNK, rows)
    for block in range(2):
        at = slice(block * block_rows, (block + 1) * block_rows)
        stores = [ref.at[at, :] for ref in (qf_ref, kf_ref, vf_ref, df_ref)]
        place_block(
            far_ref.at[at],
            far_at + block * block_rows,
            starts,
            ends,
            stores + [kvf_ref.at[:, at]],
        )

    own_rows = pl.ds(pl.multiple_of(own_at, CHUNK), CHUNK)
    q_own = qx_ref[own_rows, :]
    d_own = dx_ref[own_rows, :]
    scores = rows_dot(kf_ref[...], q_own)
    s_ref[0:CHUNK, :] = scores
    g_ref[0:CHUNK, :] = rows_dot(vf_ref[...], d_own)
    near_highest = stats_ref[MAIN, 0:1, :]
    highest = jnp.max(rows_max(scores), axis=0, keepdims=True) * LOG2_E
    highest = jnp.maximum(near_highest, highest)
    shrink = jnp.exp2(near_highest - highest)
    zeros = jnp.zeros((8, CHUNK), F32)
    total, grads = add_tiles(s_ref, g_ref, CHUNK, highest, zeros, zeros)
    total = jnp.sum(total, axis=0, keepdims=True) + stats_ref[MAIN, 1:2, :] * shrink
    grads = jnp.sum(grads, axis=0, keepdims=True) + stats_ref[MAIN, 2:3, :] * shrink
    scale = 1.0 / total
    mean_grad = grads * scale

    near_scale = shrink * scale
    for piece in range(rows // TILE):
        at = slice(piece * TILE, (piece + 1) * TILE)
        probs = so_ref[at, :] * near_scale
        p_ref[at, :] = probs.astype(BF16)
        d_ref[at, :] = (probs * (go_ref[at, :] - mean_grad)).astype(BF16)
    for piece in range(CHUNK // TILE):
        at = slice(piece * TILE, (piece + 1) * TILE)
        to = slice(rows + piece * TILE, rows + (piece + 1) * TILE)
        probs = jnp.exp2(s_ref[at, :] * LOG2_E - highest) * scale
        p_ref[to, :] = probs.astype(BF16)
        d_ref[to, :] = (probs * (g_ref[at, :] - mean_grad)).astype(BF16)
    pn_ref[:, own_rows] = p_ref[own_rows, :]
    dn_ref[:, own_rows] = d_ref[own_rows, :]

    def times_window(values_ref):
        main = jnp.dot(kv_ref[...], values_ref[0:rows, :], preferred_element_type=F32)
        return main + jnp.dot(
            kvf_ref[...], values_ref[rows : rows + CHUNK, :], preferred_element_type=F32
        )

    upper = lax.broadcasted_iota(jnp.int32, (LANES, CHUNK), 0) < HEAD
    own_out_ref[...] = jnp.where(
        upper, times_window(d_ref) * INV_ROOT, times_window(p_ref)
    ).T

    query_lane = lax.broadcasted_iota(jnp.int32, (1, CHUNK), 1)
    reaches_far = jnp.where(half == 0, left_from < 0, right_to > rows)
    sums_ref[...] = stats_ref[...]
    dk_ref[...] = jnp.zeros_like(dk_ref)
    dv_ref[...] = jnp.zeros_like(dv_ref)

    @pl.when(reaches_far)
    def _():
        for step in range(2):
            slot = half * (MAIN - 2) + step
            at = pl.ds(pl.multiple_of(slot * CHUNK, CHUNK), CHUNK)
            space = pl.ds((REACH_CHUNKS + step) * CHUNK, CHUNK)
            highest, total, grads = running_sums(
                [(kf_ref, vf_ref)], qx_ref[at, :], dx_ref[at, :], s_ref.at[space], g_ref.at[space]
            )
            before = sums_ref[slot, 0:1, :]
            higher = jnp.maximum(before, highest)
            old = jnp.exp2(before - higher)
            new = jnp.exp2(highest - higher)
            sums_ref[slot, 0:1, :] = higher
            sums_ref[slot, 1:2, :] = sums_ref[slot, 1:2, :] * old + total * new
            sums_ref[slot, 2:3, :] = sums_ref[slot, 2:3, :] * old + grads * new

        q_block = qf_ref[...]
        d_block = df_ref[...]
        key = half * (MAIN // 2) * CHUNK
        pieces = chunks_from(key, REACH_CHUNKS - 1, kx_ref, vx_ref) + [(kf_ref, vf_ref)]
        highest, total, grads = running_sums(pieces, q_block, d_block, s_ref, g_ref)
        place = query_lane + far_at
        scale = jnp.where((place >= left_from) & (place < right_to), 1.0 / total, 0.0)
        mean_grad = grads * scale
        for piece in range(CHUNK // TILE):
            at = slice(piece * TILE, (piece + 1) * TILE)
            near_at = pl.ds(pl.multiple_of(own_at - key + piece * TILE, TILE), TILE)
            probs = jnp.exp2(s_ref[near_at, :] * LOG2_E - highest) * scale
            p_ref[at, :] = probs.astype(BF16)
            d_ref[at, :] = (probs * (g_ref[near_at, :] - mean_grad)).astype(BF16)
        dk_ref[...] = jnp.dot(d_ref[0:CHUNK, :], q_block, preferred_element_type=F32)
        dv_ref[...] = jnp.dot(p_ref[0:CHUNK, :], d_block, preferred_element_type=F32)

    for step in range(MAIN - 1):
        slot = step + jnp.where(step >= 2 + half, 1, 0)
        begin = slot * CHUNK
        chunk_at = pl.ds(pl.multiple_of(begin, CHUNK), CHUNK)
        place = query_lane + begin
        valid = (place >= left_from) & (place < right_to)
        highest = sums_ref[slot, 0:1, :]
        scale = 1.0 / sums_ref[slot, 1:2, :]
        mean_grad = sums_ref[slot, 2:3, :] * scale
        for piece in range(CHUNK // TILE):
            at = slice(piece * TILE, (piece + 1) * TILE)
            probs = jnp.exp2(sn_ref[slot, at, :] * LOG2_E - highest) * scale
            d_scores = probs * (gn_ref[slot, at, :] - mean_grad)
            pn_ref[at, chunk_at] = jnp.where(valid, probs, 0.0).astype(BF16)
            dn_ref[at, chunk_at] = jnp.where(valid, d_scores, 0.0).astype(BF16)
    d_key = dk_ref[...] + jnp.dot(dn_ref[...], qx_ref[...], preferred_element_type=F32)
    d_value = dv_ref[...] + jnp.dot(pn_ref[...], dx_ref[...], preferred_element_type=F32)
    done_ref[:, 0:LANES] = own_out_ref[...].astype(BF16)
    done_ref[:, LANES:] = jnp.where(low_lanes(), d_key, d_value).astype(BF16)
    share = 16
    for member in range(out_ref.shape[0]):
        block, core = member // 2, member % 2
        for part in range(out_ref.shape[1] // share):
            begin = (block * 8 + part * 2 + core) * share
            out_ref[member, part * share : (part + 1) * share, :] = done_ref[
                begin : begin + share, :
            ]


def attend_far(counts, far, near_parts):
    return pl.pallas_call(
        far_kernel,
        out_shape=jax.ShapeDtypeStruct((4, CHUNK // 4, 2 * LANES), BF16),
        in_specs=[SMEM] + [VMEM] * (1 + len(near_parts)),
        out_specs=VMEM,
        scratch_shapes=[pltpu.VMEM((CHUNK, LANES), BF16)] * 4
        + [pltpu.VMEM((LANES, CHUNK), BF16)]
        + [pltpu.VMEM(((REACH_CHUNKS + 2) * CHUNK, CHUNK), F32)] * 2
        + [pltpu.VMEM(((MAIN + 1) * CHUNK, CHUNK), BF16)] * 2
        + [pltpu.VMEM((CHUNK, MAIN * CHUNK), BF16)] * 2
        + [pltpu.VMEM((MAIN + 1, 8, CHUNK), F32)]
        + [pltpu.VMEM((CHUNK, LANES), F32)] * 3
        + [pltpu.VMEM((CHUNK, 2 * LANES), BF16)],
        cost_estimate=pl.CostEstimate(
            flops=9000000000, bytes_accessed=1 << 20, transcendentals=1 << 20
        ),
        compiler_params=pltpu.CompilerParams(vmem_limit_bytes=VMEM_LIMIT),
    )(counts, far, *near_parts)


def project_kernel(parts_ref, gains_ref, raw_ref, weights_ref, weights_far_ref, out_ref):
    rows = parts_ref.shape[1]
    width = out_ref.shape[2] // 2
    share = out_ref.shape[1]
    core = lax.axis_index("core")
    low = low_lanes()
    q_gain = both_heads(gains_ref, 0)
    k_gain = both_heads(gains_ref, 1)

    def norm_grad(raw, gain, d_norm):
        raw = raw.astype(F32)
        inverse = head_scale(raw)
        scaled = d_norm * gain
        inner = head_sums(raw * scaled) * (1.0 / HEAD)
        return inverse * scaled - raw * (inverse * inverse * inverse * inner)

    def by_column(which, raw):
        head0 = parts_ref[which].astype(F32)
        head1 = parts_ref[2 + which].astype(F32)
        a0, a1 = head0[:, :LANES], head1[:, :LANES]
        b0, b1 = head0[:, LANES:], head1[:, LANES:]
        d_q = norm_grad(raw[0], q_gain, jnp.where(low, a0, pltpu.roll(a1, HEAD, 1)))
        attn = jnp.where(low, pltpu.roll(a0, HEAD, 1), a1).astype(BF16)
        d_k = norm_grad(raw[1], k_gain, jnp.where(low, b0, pltpu.roll(b1, HEAD, 1)))
        d_v = jnp.where(low, pltpu.roll(b0, HEAD, 1), b1)
        return attn, [values.astype(BF16) for values in (d_q, d_k, d_v)]

    raw_far = [
        weights_far_ref[4 * width + array * rows : 4 * width + (array + 1) * rows, :]
        for array in range(2)
    ]
    attn, grads = by_column(core, [raw_ref[0], raw_ref[1]])
    attn_far, grads_far = by_column(1 - core, raw_far)
    both = (weights_ref, weights_far_ref)
    mixed = jnp.dot(
        jnp.concatenate([attn, attn_far], axis=1),
        jnp.concatenate([w_out_of(ref, width) for ref in both], axis=0),
        preferred_element_type=F32,
    ).astype(BF16)
    weights = [ref[part * width : (part + 1) * width, :] for ref in both for part in range(3)]
    d_hidden = rows_dot(
        jnp.concatenate(grads + grads_far, axis=1), jnp.concatenate(weights, axis=1)
    ).astype(BF16)
    for place in range(out_ref.shape[0]):
        at = slice(place * share, (place + 1) * share)
        out_ref[place, :, :width] = mixed[at]
        out_ref[place, :, width:] = d_hidden[at]


def project(parts, gains, raw, weights, weights_far, x_count, width):
    return pl.pallas_call(
        project_kernel,
        out_shape=jax.ShapeDtypeStruct((x_count, parts.shape[1] // x_count, 2 * width), BF16),
        in_specs=[VMEM] * 5,
        out_specs=VMEM,
        compiler_params=pltpu.CompilerParams(vmem_limit_bytes=VMEM_LIMIT),
    )(parts, gains, raw, weights, weights_far)


def ready_kernel(
    counts_ref,
    tokens_ref,
    cotangent_ref,
    modulation_ref,
    rows_ref,
    factors_ref,
):
    rows = rows_ref.shape[1]
    first_row = (lax.axis_index("x") * 2 + lax.axis_index("core")) * rows
    first = block_index() * tokens_ref.shape[0] + first_row
    _, scale, gate = modulation_rows(counts_ref, modulation_ref, first, rows)
    at = pl.ds(pl.multiple_of(first_row, rows), rows)
    normed, inv_std = layer_norm(tokens_ref[at, :].astype(F32))
    rows_ref[0] = tokens_ref[at, :]
    rows_ref[1] = cotangent_ref[at, :]
    factors_ref[0] = gate
    factors_ref[1] = 1.0 + scale
    factors_ref[2] = normed
    factors_ref[3] = jnp.broadcast_to(inv_std, normed.shape)


def ready(counts, tokens, cotangent, modulation, share):
    width = tokens.shape[1]
    return pl.pallas_call(
        ready_kernel,
        out_shape=(
            jax.ShapeDtypeStruct((2, share, width), BF16),
            jax.ShapeDtypeStruct((4, share, width), F32),
        ),
        in_specs=[SMEM] + [VMEM] * 3,
        out_specs=(VMEM, VMEM),
        compiler_params=pltpu.CompilerParams(vmem_limit_bytes=VMEM_LIMIT),
    )(counts, tokens, cotangent, modulation)


def leave_kernel(rows_ref, factors_ref, shares_ref, layer_ref, grad_ref):
    width = layer_ref.shape[1]
    sums = shares_ref[0].astype(F32)
    for share in range(1, shares_ref.shape[0]):
        sums = sums + shares_ref[share].astype(F32)
    layer = rows_ref[0].astype(F32) + factors_ref[0] * sums[:, :width]
    layer_ref[...] = layer.astype(BF16)
    d_normed = sums[:, width:] * factors_ref[1]
    normed = factors_ref[2]
    input_grad = rows_ref[1].astype(F32) + factors_ref[3] * (
        d_normed
        - jnp.mean(d_normed, axis=-1, keepdims=True)
        - normed * jnp.mean(d_normed * normed, axis=-1, keepdims=True)
    )
    grad_ref[...] = input_grad.astype(BF16)


def leave(rows, factors, shares):
    out = jax.ShapeDtypeStruct(rows.shape[1:], BF16)
    return pl.pallas_call(
        leave_kernel,
        out_shape=(out, out),
        in_specs=[VMEM] * 3,
        out_specs=(VMEM, VMEM),
        compiler_params=pltpu.CompilerParams(vmem_limit_bytes=VMEM_LIMIT),
    )(rows, factors, shares)


def per_device(tokens, cotangent, w_qkv, w_out, qk_gain, modulation, image_counts):
    tok_rows, model_width = tokens.shape
    z_count = lax.axis_size("z")
    x_count = lax.axis_size("x")
    quad = 4
    pair_rows = 2 * tok_rows
    share = tok_rows // (2 * x_count)
    w_parts = w_qkv.transpose(1, 0, 2)
    mod_parts = modulation.transpose(1, 0, 2)

    heads, raw, raw_far = enter(
        image_counts, qk_gain, tokens, cotangent, w_parts, w_out, mod_parts, quad
    )
    _, tokens_late, cotangent_late, mod_late, w_parts_late, w_out_late = (
        lax.optimization_barrier((heads, tokens, cotangent, mod_parts, w_parts, w_out))
    )
    rows, factors = ready(image_counts, tokens_late, cotangent_late, mod_late, share)
    weights = pack(w_parts_late, w_out_late, raw_far)
    mine = lax.all_to_all(heads, ("yh", "yl"), 0, 0)
    mine, rows, factors, weights = lax.optimization_barrier((mine, rows, factors, weights))
    mine = mine.reshape(quad * tok_rows, 2 * LANES)
    evens = range(0, z_count, 2)
    swaps = [(i, i + 1) for i in evens], [((i - 1) % z_count, i) for i in evens]
    first, second = (
        lax.ppermute(mine, "z", pairs + [(j, i) for i, j in pairs]) for pairs in swaps
    )
    halves = 4 * z_count
    crosses = (lax.rem(lax.axis_index("z"), 2) == lax.axis_index("core")).astype(jnp.int32)
    far_half = jnp.where(
        lax.axis_index("yh") == crosses, mine[pair_rows:], mine[:pair_rows]
    )

    def far_source(target):
        z, yh, core = target // 4, target // 2 % 2, target % 2
        other = yh ^ int(z % 2 == core)
        return (z + (2 if yh else -2)) % z_count * 4 + other * 2 + core

    far = lax.ppermute(
        far_half, ("z", "yh", "core"), [(far_source(i), i) for i in range(halves)]
    )
    early = attend_early(image_counts, first, mine)
    near_parts = attend_near(image_counts, second, early)
    weights_far = lax.ppermute(weights, "core", [(0, 1), (1, 0)])
    parts = attend_far(image_counts, far, near_parts)
    parts = lax.all_to_all(parts, ("yl", "core"), 0, 0)
    partial = project(parts, qk_gain, raw, weights, weights_far, x_count, model_width)
    shares = lax.all_to_all(partial, "x", 0, 0)
    return leave(rows, factors, shares)


def solution(mesh):
    split = jax.sharding.Mesh(mesh.devices.reshape(16, 2, 2, 4, 2), ("z", "yh", "yl", "x", "core"))
    dp, head = ("z", "yh", "yl"), ("x", "core")
    in_specs = (P(dp, None), P(dp, None), P(None, None, head), P(head, None), P(), P(), P())
    out_specs = (P(dp + head, None), P(dp + head, None))
    return jax.shard_map(
        per_device, mesh=split, in_specs=in_specs, out_specs=out_specs, check_vma=False
    )
```

```python
import math

import jax
import jax.numpy as jnp
from jax import lax
from jax.experimental import pallas as pl
from jax.experimental.pallas import tpu as pltpu
from jax.sharding import PartitionSpec as P

EPS = 1e-06
SAME_IMAGE = 512.0
LANES = 128
HEAD = 64
F32 = jnp.float32
BF16 = jnp.bfloat16
VMEM_LIMIT = 24 * 1024 * 1024
ENTER_LIMIT = 60 * 1024 * 1024
VMEM = pl.BlockSpec(memory_space=pltpu.VMEM)
SMEM = pl.BlockSpec(memory_space=pltpu.SMEM)


def rows_dot(a, b):
    return lax.dot_general(a, b, (((1,), (1,)), ((), ())), preferred_element_type=F32)


def block_index():
    return (lax.axis_index("z") * 2 + lax.axis_index("yh")) * 2 + lax.axis_index("yl")


def image_bounds(counts_ref, first_lane):
    lane = lax.broadcasted_iota(jnp.int32, (1, LANES), 1)
    starts = jnp.zeros((1, LANES), jnp.int32)
    ends = jnp.zeros((1, LANES), jnp.int32)
    total = jnp.int32(0)
    for image in range(counts_ref.shape[0]):
        here = lane == first_lane + image
        starts = jnp.where(here, total, starts)
        total = total + counts_ref[image]
        ends = jnp.where(here, total, ends)
    return starts, ends


def modulation_rows(counts_ref, modulation_ref, first, rows):
    starts, ends = image_bounds(counts_ref, 0)
    place = first + lax.broadcasted_iota(jnp.int32, (rows, LANES), 0)
    member = ((place >= starts) & (place < ends)).astype(F32).astype(BF16)
    member = member[:, : modulation_ref.shape[1]]
    return [
        jnp.dot(member, modulation_ref[part], preferred_element_type=F32) for part in range(3)
    ]


def layer_norm(values):
    average = jnp.mean(values, axis=-1, keepdims=True)
    centred = values - average
    inv_std = lax.rsqrt(jnp.mean(centred * centred, axis=-1, keepdims=True) + EPS)
    return centred * inv_std, inv_std


def head_sums(values):
    lanes = (LANES, LANES)
    first = lax.broadcasted_iota(jnp.int32, lanes, 0) < HEAD
    second = lax.broadcasted_iota(jnp.int32, lanes, 1) < HEAD
    ones = (first == second).astype(F32).astype(BF16)
    large = values.astype(BF16)
    small = (values - large.astype(F32)).astype(BF16)
    large = jnp.dot(large, ones, preferred_element_type=F32)
    return large + jnp.dot(small, ones, preferred_element_type=F32)


def both_heads(gains_ref, which):
    gain = gains_ref[which : which + 1, :]
    return jnp.concatenate([gain, gain], axis=1)


def head_scale(raw):
    return lax.rsqrt(head_sums(raw * raw) * (1.0 / HEAD) + EPS)


def enter_kernel(
    counts_ref,
    gains_ref,
    tokens_ref,
    cotangent_ref,
    w_qkv_ref,
    w_out_ref,
    modulation_ref,
    out_ref,
    raw_ref,
    raw_far_ref,
    rows_ref,
    factors_ref,
    hidden_ref,
    d_mixed_ref,
):
    rows = tokens_ref.shape[0]
    starts, ends = image_bounds(counts_ref, 0)
    place = block_index() * rows + lax.broadcasted_iota(jnp.int32, (rows, LANES), 0)
    member = ((place >= starts) & (place < ends)).astype(F32).astype(BF16)
    member = member[:, : modulation_ref.shape[1]]
    for part in range(3):
        factors_ref[part] = jnp.dot(member, modulation_ref[part], preferred_element_type=F32)
    for begin in range(0, rows, 16):
        at = slice(begin, begin + 16)
        normed, _ = layer_norm(tokens_ref[at, :].astype(F32))
        hidden = normed * (1.0 + factors_ref[1, at, :]) + factors_ref[0, at, :]
        hidden_ref[at, :] = hidden.astype(BF16)
        d_mixed = cotangent_ref[at, :].astype(F32) * factors_ref[2, at, :]
        d_mixed_ref[at, :] = d_mixed.astype(BF16)
    weights = jnp.concatenate([w_qkv_ref[part] for part in range(3)], axis=1)
    qkv = jnp.dot(hidden_ref[...], weights, preferred_element_type=F32)
    q, k, v = (qkv[:, part * LANES : (part + 1) * LANES] for part in range(3))
    d_attn = rows_dot(d_mixed_ref[...], w_out_ref[...])
    rows_ref[0] = q.astype(BF16)
    rows_ref[1] = k.astype(BF16)
    q = rows_ref[0].astype(F32)
    k = rows_ref[1].astype(F32)
    q = q * head_scale(q) * (both_heads(gains_ref, 0) * (1.0 / math.sqrt(HEAD)))
    k = k * head_scale(k) * both_heads(gains_ref, 1)
    core = lax.axis_index("core")
    share = raw_ref.shape[1] // 4
    for ref, side in ((raw_ref, core), (raw_far_ref, 1 - core)):
        for part in range(4):
            begin = pl.multiple_of((2 * part + side) * share, share)
            for array in range(2):
                ref[array, part * share : (part + 1) * share, :] = rows_ref[
                    array, pl.ds(begin, share), :
                ]
    low = low_lanes()

    def beside(left, right):
        return jnp.where(low, left, right).astype(BF16)

    q_v = (beside(q, pltpu.roll(v, HEAD, 1)), beside(pltpu.roll(q, HEAD, 1), v))
    k_d = (beside(k, pltpu.roll(d_attn, HEAD, 1)), beside(pltpu.roll(k, HEAD, 1), d_attn))
    for place in range(out_ref.shape[0]):
        out_ref[place, :, 0:LANES] = q_v[place % 2]
        out_ref[place, :, LANES:] = k_d[place % 2]


def enter(counts, gains, tokens, cotangent, w_parts, w_out, modulation, quad):
    rows = tokens.shape[0]
    raw = jax.ShapeDtypeStruct((2, rows // 2, LANES), BF16)
    return pl.pallas_call(
        enter_kernel,
        out_shape=(jax.ShapeDtypeStruct((quad, rows, 2 * LANES), BF16), raw, raw),
        in_specs=[SMEM] + [VMEM] * 6,
        out_specs=(VMEM,) * 3,
        scratch_shapes=[
            pltpu.VMEM((2, rows, LANES), BF16),
            pltpu.VMEM((3,) + tokens.shape, F32),
            pltpu.VMEM(tokens.shape, BF16),
            pltpu.VMEM(tokens.shape, BF16),
        ],
        compiler_params=pltpu.CompilerParams(vmem_limit_bytes=ENTER_LIMIT),
    )(counts, gains, tokens, cotangent, w_parts, w_out, modulation)


def pack_kernel(w_qkv_ref, w_out_ref, raw_ref, weights_ref, sems):
    width = w_out_ref.shape[1]
    rows = raw_ref.shape[1]
    pairs = []
    for part in range(3):
        pairs.append((w_qkv_ref.at[part], weights_ref.at[part * width : (part + 1) * width, :]))
    for tile in range(width // LANES):
        at = slice(tile * LANES, (tile + 1) * LANES)
        to = slice(3 * width + tile * LANES, 3 * width + (tile + 1) * LANES)
        pairs.append((w_out_ref.at[:, at], weights_ref.at[to, :]))
    for array in range(2):
        to = slice(4 * width + array * rows, 4 * width + (array + 1) * rows)
        pairs.append((raw_ref.at[array], weights_ref.at[to, :]))
    copies = [
        pltpu.make_async_copy(source, target, sems.at[place])
        for place, (source, target) in enumerate(pairs)
    ]
    for copy in copies:
        copy.start()
    for copy in copies:
        copy.wait()


def pack(w_parts, w_out, raw):
    width = w_out.shape[1]
    whole = pl.BlockSpec(memory_space=pl.ANY)
    return pl.pallas_call(
        pack_kernel,
        out_shape=jax.ShapeDtypeStruct((4 * width + 2 * raw.shape[1], LANES), BF16),
        in_specs=[whole] * 3,
        out_specs=VMEM,
        scratch_shapes=[pltpu.SemaphoreType.DMA((5 + width // LANES,))],
        compiler_params=pltpu.CompilerParams(vmem_limit_bytes=8 * 1024 * 1024),
    )(w_parts, w_out, raw)


def w_out_of(weights_ref, width):
    return jnp.concatenate(
        [
            weights_ref[3 * width + tile * LANES : 3 * width + (tile + 1) * LANES, :]
            for tile in range(width // LANES)
        ],
        axis=1,
    )


LOG2_E = math.log2(math.e)
INV_ROOT = 1.0 / math.sqrt(HEAD)
CHUNK = 256
TILE = 64
MAIN = 6
REACH_CHUNKS = 4


def low_lanes():
    return lax.broadcasted_iota(jnp.int32, (1, LANES), 1) < HEAD


def place_block(source, place, starts, ends, stores):
    low = low_lanes()
    rows = source.shape[0]
    at = place + lax.broadcasted_iota(jnp.int32, (rows, LANES), 0)
    same = ((at >= starts) & (at < ends)).astype(F32)
    first = source[:, 0:LANES].astype(F32)
    second = source[:, LANES:].astype(F32)
    q_store, k_store, v_store, d_store, kv_store = stores
    q_store[...] = jnp.where(low, first, same * SAME_IMAGE).astype(BF16)
    k_store[...] = jnp.where(low, second, same).astype(BF16)
    v_store[...] = jnp.where(low, 0.0, first).astype(BF16)
    d_store[...] = source[:, LANES:]
    kv_store[...] = jnp.where(low, second, first).astype(BF16).T


def window_facts(counts_ref):
    half = lax.axis_index("yh")
    origin = (block_index() // 4 - 1) * 2 * CHUNK
    own_at = (2 + half) * CHUNK
    starts, ends = image_bounds(counts_ref, HEAD)
    left_from = jnp.int32(-CHUNK)
    right_to = jnp.int32((MAIN + 1) * CHUNK)
    total = -origin
    for image in range(counts_ref.shape[0]):
        left_from = jnp.where(total <= own_at, total, left_from)
        ended = total >= own_at + CHUNK
        total = total + counts_ref[image]
        right_to = jnp.where((total >= own_at + CHUNK) & jnp.logical_not(ended), total, right_to)
    return half, own_at, starts - origin, ends - origin, left_from, right_to


def by_eight(values):
    return values.reshape(values.shape[0] // 8, 8, values.shape[1])


def add_tiles(s_ref, g_ref, rows, highest, total, grads):
    for piece in range(rows // TILE):
        at = slice(piece * TILE, (piece + 1) * TILE)
        weights = jnp.exp2(s_ref[at, :] * LOG2_E - highest)
        total = total + jnp.sum(by_eight(weights), axis=0)
        grads = grads + jnp.sum(by_eight(weights * g_ref[at, :]), axis=0)
    return total, grads


def rows_max(values):
    return jnp.max(by_eight(values), axis=0)


def chunks_from(key, count, *refs):
    rows = [pl.ds(pl.multiple_of(key + i * CHUNK, CHUNK), CHUNK) for i in range(count)]
    return [tuple(ref.at[at, :] for ref in refs) for at in rows]


def running_sums(pieces, q_block, d_block, s_ref, g_ref):
    highest = jnp.full((8, CHUNK), -jnp.inf, F32)
    total = jnp.zeros((8, CHUNK), F32)
    grads = jnp.zeros((8, CHUNK), F32)
    for piece, (keys_ref, values_ref) in enumerate(pieces):
        here = slice(piece * CHUNK, (piece + 1) * CHUNK)
        scores = rows_dot(keys_ref[...], q_block)
        s_ref[here, :] = scores
        g_ref[here, :] = rows_dot(values_ref[...], d_block)
        higher = jnp.maximum(highest, rows_max(scores) * LOG2_E)
        shrink = jnp.exp2(highest - higher)
        total = total * shrink
        grads = grads * shrink
        highest = higher
        for tile in range(CHUNK // TILE):
            at = slice(piece * CHUNK + tile * TILE, piece * CHUNK + (tile + 1) * TILE)
            weights = jnp.exp2(by_eight(s_ref[at, :]) * LOG2_E - highest[None])
            total = total + jnp.sum(weights, axis=0)
            grads = grads + jnp.sum(weights * by_eight(g_ref[at, :]), axis=0)
    top = jnp.max(highest, axis=0, keepdims=True)
    shrink = jnp.exp2(highest - top)
    total = jnp.sum(total * shrink, axis=0, keepdims=True)
    return top, total, jnp.sum(grads * shrink, axis=0, keepdims=True)


def early_kernel(
    counts_ref,
    first_ref,
    quad_ref,
    qa_ref,
    ka_ref,
    va_ref,
    da_ref,
    kva_ref,
    sa_ref,
    ga_ref,
    top_ref,
):
    half, _, starts, ends, _, _ = window_facts(counts_ref)
    block_rows = CHUNK // 2
    to_first = jnp.where(lax.rem(lax.axis_index("z"), 2) == 1, 2 * CHUNK, -2 * CHUNK)
    for block in range(8):
        at = slice(block * block_rows, (block + 1) * block_rows)
        inner = slice(block % 4 * block_rows, (block % 4 + 1) * block_rows)
        place = 2 * CHUNK + block % 4 * block_rows
        stores = [ref.at[at, :] for ref in (qa_ref, ka_ref, va_ref, da_ref)]
        stores.append(kva_ref.at[:, at])
        if block < 4:
            place_block(quad_ref.at[inner], place, starts, ends, stores)
        else:
            place_block(first_ref.at[inner], place + to_first, starts, ends, stores)

    own_rows = pl.ds(pl.multiple_of(half * CHUNK, CHUNK), CHUNK)
    q_own = qa_ref[own_rows, :]
    d_own = da_ref[own_rows, :]
    highest = jnp.full((8, CHUNK), -jnp.inf, F32)
    for piece in range(4):
        at = slice(piece * CHUNK, (piece + 1) * CHUNK)
        scores = rows_dot(ka_ref[at, :], q_own)
        sa_ref[at, :] = scores
        highest = jnp.maximum(highest, rows_max(scores))
        ga_ref[at, :] = rows_dot(va_ref[at, :], d_own)
    top_ref[...] = highest


def attend_early(counts, first, quad):
    rows = 4 * CHUNK
    head_rows = jax.ShapeDtypeStruct((rows, LANES), BF16)
    scores = jax.ShapeDtypeStruct((rows, CHUNK), F32)
    return pl.pallas_call(
        early_kernel,
        out_shape=(head_rows,) * 4
        + (jax.ShapeDtypeStruct((LANES, rows), BF16), scores, scores)
        + (jax.ShapeDtypeStruct((8, CHUNK), F32),),
        in_specs=[SMEM] + [VMEM] * 2,
        out_specs=(VMEM,) * 8,
        compiler_params=pltpu.CompilerParams(vmem_limit_bytes=VMEM_LIMIT),
    )(counts, first, quad)


def near_kernel(
    counts_ref,
    second_ref,
    qa_ref,
    ka_ref,
    va_ref,
    da_ref,
    kva_ref,
    sa_ref,
    ga_ref,
    top_ref,
    qx_ref,
    kx_ref,
    vx_ref,
    dx_ref,
    kv_ref,
    so_ref,
    go_ref,
    sn_ref,
    gn_ref,
    stats_ref,
    s_ref,
    g_ref,
):
    half, own_at, starts, ends, left_from, right_to = window_facts(counts_ref)
    block_rows = CHUNK // 2
    odd = lax.rem(lax.axis_index("z"), 2) == 1
    first_at = pl.multiple_of(jnp.where(odd, 4 * CHUNK, 0), 2 * CHUNK)
    second_at = pl.multiple_of(jnp.where(odd, 0, 4 * CHUNK), 2 * CHUNK)
    early = ((qa_ref, qx_ref), (ka_ref, kx_ref), (va_ref, vx_ref), (da_ref, dx_ref))
    for source, target in early:
        target[2 * CHUNK : 4 * CHUNK, :] = source[0 : 2 * CHUNK, :]
        target[pl.ds(first_at, 2 * CHUNK), :] = source[2 * CHUNK : 4 * CHUNK, :]
    kv_ref[:, 2 * CHUNK : 4 * CHUNK] = kva_ref[:, 0 : 2 * CHUNK]
    kv_ref[:, pl.ds(first_at, 2 * CHUNK)] = kva_ref[:, 2 * CHUNK : 4 * CHUNK]
    for block in range(4):
        inner = slice(block * block_rows, (block + 1) * block_rows)
        begin = pl.multiple_of(second_at + block * block_rows, block_rows)
        at = pl.ds(begin, block_rows)
        stores = [ref.at[at, :] for ref in (qx_ref, kx_ref, vx_ref, dx_ref)]
        place_block(second_ref.at[inner], begin, starts, ends, stores + [kv_ref.at[:, at]])

    own_rows = pl.ds(pl.multiple_of(half * CHUNK, CHUNK), CHUNK)
    q_own = qa_ref[own_rows, :]
    d_own = da_ref[own_rows, :]
    highest = top_ref[...]
    for piece in range(2):
        at = pl.ds(pl.multiple_of(second_at + piece * CHUNK, CHUNK), CHUNK)
        scores = rows_dot(kx_ref[at, :], q_own)
        so_ref[at, :] = scores
        highest = jnp.maximum(highest, rows_max(scores))
        go_ref[at, :] = rows_dot(vx_ref[at, :], d_own)
    highest = jnp.max(highest, axis=0, keepdims=True) * LOG2_E
    total = jnp.zeros((8, CHUNK), F32)
    grads = jnp.zeros((8, CHUNK), F32)
    for piece in range(MAIN * CHUNK // TILE):
        inner = piece * TILE
        if inner < 2 * CHUNK:
            to = pl.ds(2 * CHUNK + inner, TILE)
        elif inner < 4 * CHUNK:
            to = pl.ds(pl.multiple_of(first_at + inner - 2 * CHUNK, TILE), TILE)
        else:
            to = pl.ds(pl.multiple_of(second_at + inner - 4 * CHUNK, TILE), TILE)
        if inner < 4 * CHUNK:
            scores = sa_ref[inner : inner + TILE, :]
            given = ga_ref[inner : inner + TILE, :]
            go_ref[to, :] = given
        else:
            scores = so_ref[to, :]
            given = go_ref[to, :]
        weights = jnp.exp2(scores * LOG2_E - highest)
        so_ref[to, :] = weights
        total = total + jnp.sum(by_eight(weights), axis=0)
        grads = grads + jnp.sum(by_eight(weights * given), axis=0)
    stats_ref[MAIN, 0:1, :] = highest
    stats_ref[MAIN, 1:2, :] = jnp.sum(total, axis=0, keepdims=True)
    stats_ref[MAIN, 2:3, :] = jnp.sum(grads, axis=0, keepdims=True)

    left_key = jnp.clip((left_from + CHUNK) // CHUNK - 1, 0, MAIN - REACH_CHUNKS)
    right_key = jnp.clip((right_to - 1) // CHUNK - (REACH_CHUNKS - 1), 0, MAIN - REACH_CHUNKS)

    def one_chunk(step, carry):
        slot = step + jnp.where(step >= 2 + half, 1, 0)
        begin = slot * CHUNK

        @pl.when((begin < right_to) & (begin + CHUNK > left_from))
        def _():
            at = pl.ds(pl.multiple_of(begin, CHUNK), CHUNK)
            key = jnp.where(begin < own_at, left_key, right_key) * CHUNK
            q_block = qx_ref[at, :]
            d_block = dx_ref[at, :]
            pieces = chunks_from(key, REACH_CHUNKS, kx_ref, vx_ref)
            highest, total, grads = running_sums(pieces, q_block, d_block, s_ref, g_ref)
            stats_ref[slot, 0:1, :] = highest
            stats_ref[slot, 1:2, :] = total
            stats_ref[slot, 2:3, :] = grads
            near_at = pl.ds(pl.multiple_of(own_at - key, CHUNK), CHUNK)
            sn_ref[slot, :, :] = s_ref[near_at, :]
            gn_ref[slot, :, :] = g_ref[near_at, :]

        return carry

    lax.fori_loop(0, MAIN - 1, one_chunk, 0)


def attend_near(counts, second, early):
    rows = MAIN * CHUNK
    head_rows = jax.ShapeDtypeStruct((rows, LANES), BF16)
    scores = jax.ShapeDtypeStruct((rows, CHUNK), F32)
    tiles = jax.ShapeDtypeStruct((MAIN, CHUNK, CHUNK), F32)
    return pl.pallas_call(
        near_kernel,
        out_shape=(head_rows,) * 4
        + (jax.ShapeDtypeStruct((LANES, rows), BF16),)
        + (scores, scores, tiles, tiles, jax.ShapeDtypeStruct((MAIN + 1, 8, CHUNK), F32)),
        in_specs=[SMEM] + [VMEM] * (1 + len(early)),
        out_specs=(VMEM,) * 10,
        scratch_shapes=[pltpu.VMEM((REACH_CHUNKS * CHUNK, CHUNK), F32)] * 2,
        cost_estimate=pl.CostEstimate(
            flops=9000000000, bytes_accessed=1 << 20, transcendentals=1 << 20
        ),
        compiler_params=pltpu.CompilerParams(vmem_limit_bytes=VMEM_LIMIT),
    )(counts, second, *early)


def far_kernel(
    counts_ref,
    far_ref,
    qx_ref,
    kx_ref,
    vx_ref,
    dx_ref,
    kv_ref,
    so_ref,
    go_ref,
    sn_ref,
    gn_ref,
    stats_ref,
    out_ref,
    qf_ref,
    kf_ref,
    vf_ref,
    df_ref,
    kvf_ref,
    s_ref,
    g_ref,
    p_ref,
    d_ref,
    pn_ref,
    dn_ref,
    sums_ref,
    dk_ref,
    dv_ref,
    own_out_ref,
    done_ref,
):
    half, own_at, starts, ends, left_from, right_to = window_facts(counts_ref)
    block_rows = CHUNK // 2
    rows = MAIN * CHUNK
    far_at = jnp.where(half == 0, -CHUNK, rows)
    for block in range(2):
        at = slice(block * block_rows, (block + 1) * block_rows)
        stores = [ref.at[at, :] for ref in (qf_ref, kf_ref, vf_ref, df_ref)]
        place_block(
            far_ref.at[at],
            far_at + block * block_rows,
            starts,
            ends,
            stores + [kvf_ref.at[:, at]],
        )

    own_rows = pl.ds(pl.multiple_of(own_at, CHUNK), CHUNK)
    q_own = qx_ref[own_rows, :]
    d_own = dx_ref[own_rows, :]
    scores = rows_dot(kf_ref[...], q_own)
    s_ref[0:CHUNK, :] = scores
    g_ref[0:CHUNK, :] = rows_dot(vf_ref[...], d_own)
    near_highest = stats_ref[MAIN, 0:1, :]
    highest = jnp.max(rows_max(scores), axis=0, keepdims=True) * LOG2_E
    highest = jnp.maximum(near_highest, highest)
    shrink = jnp.exp2(near_highest - highest)
    zeros = jnp.zeros((8, CHUNK), F32)
    total, grads = add_tiles(s_ref, g_ref, CHUNK, highest, zeros, zeros)
    total = jnp.sum(total, axis=0, keepdims=True) + stats_ref[MAIN, 1:2, :] * shrink
    grads = jnp.sum(grads, axis=0, keepdims=True) + stats_ref[MAIN, 2:3, :] * shrink
    scale = 1.0 / total
    mean_grad = grads * scale

    near_scale = shrink * scale
    for piece in range(rows // TILE):
        at = slice(piece * TILE, (piece + 1) * TILE)
        probs = so_ref[at, :] * near_scale
        p_ref[at, :] = probs.astype(BF16)
        d_ref[at, :] = (probs * (go_ref[at, :] - mean_grad)).astype(BF16)
    for piece in range(CHUNK // TILE):
        at = slice(piece * TILE, (piece + 1) * TILE)
        to = slice(rows + piece * TILE, rows + (piece + 1) * TILE)
        probs = jnp.exp2(s_ref[at, :] * LOG2_E - highest) * scale
        p_ref[to, :] = probs.astype(BF16)
        d_ref[to, :] = (probs * (g_ref[at, :] - mean_grad)).astype(BF16)
    pn_ref[:, own_rows] = p_ref[own_rows, :]
    dn_ref[:, own_rows] = d_ref[own_rows, :]

    def times_window(values_ref):
        main = jnp.dot(kv_ref[...], values_ref[0:rows, :], preferred_element_type=F32)
        return main + jnp.dot(
            kvf_ref[...], values_ref[rows : rows + CHUNK, :], preferred_element_type=F32
        )

    upper = lax.broadcasted_iota(jnp.int32, (LANES, CHUNK), 0) < HEAD
    own_out_ref[...] = jnp.where(
        upper, times_window(d_ref) * INV_ROOT, times_window(p_ref)
    ).T

    query_lane = lax.broadcasted_iota(jnp.int32, (1, CHUNK), 1)
    reaches_far = jnp.where(half == 0, left_from < 0, right_to > rows)
    sums_ref[...] = stats_ref[...]
    dk_ref[...] = jnp.zeros_like(dk_ref)
    dv_ref[...] = jnp.zeros_like(dv_ref)

    @pl.when(reaches_far)
    def _():
        for step in range(2):
            slot = half * (MAIN - 2) + step
            at = pl.ds(pl.multiple_of(slot * CHUNK, CHUNK), CHUNK)
            space = pl.ds((REACH_CHUNKS + step) * CHUNK, CHUNK)
            highest, total, grads = running_sums(
                [(kf_ref, vf_ref)], qx_ref[at, :], dx_ref[at, :], s_ref.at[space], g_ref.at[space]
            )
            before = sums_ref[slot, 0:1, :]
            higher = jnp.maximum(before, highest)
            old = jnp.exp2(before - higher)
            new = jnp.exp2(highest - higher)
            sums_ref[slot, 0:1, :] = higher
            sums_ref[slot, 1:2, :] = sums_ref[slot, 1:2, :] * old + total * new
            sums_ref[slot, 2:3, :] = sums_ref[slot, 2:3, :] * old + grads * new

        q_block = qf_ref[...]
        d_block = df_ref[...]
        key = half * (MAIN // 2) * CHUNK
        pieces = chunks_from(key, REACH_CHUNKS - 1, kx_ref, vx_ref) + [(kf_ref, vf_ref)]
        highest, total, grads = running_sums(pieces, q_block, d_block, s_ref, g_ref)
        place = query_lane + far_at
        scale = jnp.where((place >= left_from) & (place < right_to), 1.0 / total, 0.0)
        mean_grad = grads * scale
        for piece in range(CHUNK // TILE):
            at = slice(piece * TILE, (piece + 1) * TILE)
            near_at = pl.ds(pl.multiple_of(own_at - key + piece * TILE, TILE), TILE)
            probs = jnp.exp2(s_ref[near_at, :] * LOG2_E - highest) * scale
            p_ref[at, :] = probs.astype(BF16)
            d_ref[at, :] = (probs * (g_ref[near_at, :] - mean_grad)).astype(BF16)
        dk_ref[...] = jnp.dot(d_ref[0:CHUNK, :], q_block, preferred_element_type=F32)
        dv_ref[...] = jnp.dot(p_ref[0:CHUNK, :], d_block, preferred_element_type=F32)

    for step in range(MAIN - 1):
        slot = step + jnp.where(step >= 2 + half, 1, 0)
        begin = slot * CHUNK
        chunk_at = pl.ds(pl.multiple_of(begin, CHUNK), CHUNK)
        place = query_lane + begin
        valid = (place >= left_from) & (place < right_to)
        highest = sums_ref[slot, 0:1, :]
        scale = 1.0 / sums_ref[slot, 1:2, :]
        mean_grad = sums_ref[slot, 2:3, :] * scale
        for piece in range(CHUNK // TILE):
            at = slice(piece * TILE, (piece + 1) * TILE)
            probs = jnp.exp2(sn_ref[slot, at, :] * LOG2_E - highest) * scale
            d_scores = probs * (gn_ref[slot, at, :] - mean_grad)
            pn_ref[at, chunk_at] = jnp.where(valid, probs, 0.0).astype(BF16)
            dn_ref[at, chunk_at] = jnp.where(valid, d_scores, 0.0).astype(BF16)
    d_key = dk_ref[...] + jnp.dot(dn_ref[...], qx_ref[...], preferred_element_type=F32)
    d_value = dv_ref[...] + jnp.dot(pn_ref[...], dx_ref[...], preferred_element_type=F32)
    done_ref[:, 0:LANES] = own_out_ref[...].astype(BF16)
    done_ref[:, LANES:] = jnp.where(low_lanes(), d_key, d_value).astype(BF16)
    share = 16
    for member in range(out_ref.shape[0]):
        block, core = member // 2, member % 2
        for part in range(out_ref.shape[1] // share):
            begin = (block * 8 + part * 2 + core) * share
            out_ref[member, part * share : (part + 1) * share, :] = done_ref[
                begin : begin + share, :
            ]


def attend_far(counts, far, near_parts):
    return pl.pallas_call(
        far_kernel,
        out_shape=jax.ShapeDtypeStruct((4, CHUNK // 4, 2 * LANES), BF16),
        in_specs=[SMEM] + [VMEM] * (1 + len(near_parts)),
        out_specs=VMEM,
        scratch_shapes=[pltpu.VMEM((CHUNK, LANES), BF16)] * 4
        + [pltpu.VMEM((LANES, CHUNK), BF16)]
        + [pltpu.VMEM(((REACH_CHUNKS + 2) * CHUNK, CHUNK), F32)] * 2
        + [pltpu.VMEM(((MAIN + 1) * CHUNK, CHUNK), BF16)] * 2
        + [pltpu.VMEM((CHUNK, MAIN * CHUNK), BF16)] * 2
        + [pltpu.VMEM((MAIN + 1, 8, CHUNK), F32)]
        + [pltpu.VMEM((CHUNK, LANES), F32)] * 3
        + [pltpu.VMEM((CHUNK, 2 * LANES), BF16)],
        cost_estimate=pl.CostEstimate(
            flops=9000000000, bytes_accessed=1 << 20, transcendentals=1 << 20
        ),
        compiler_params=pltpu.CompilerParams(vmem_limit_bytes=VMEM_LIMIT),
    )(counts, far, *near_parts)


def project_kernel(parts_ref, gains_ref, raw_ref, weights_ref, weights_far_ref, out_ref):
    rows = parts_ref.shape[1]
    width = out_ref.shape[2] // 2
    share = out_ref.shape[1]
    core = lax.axis_index("core")
    low = low_lanes()
    q_gain = both_heads(gains_ref, 0)
    k_gain = both_heads(gains_ref, 1)

    def norm_grad(raw, gain, d_norm):
        raw = raw.astype(F32)
        inverse = head_scale(raw)
        scaled = d_norm * gain
        inner = head_sums(raw * scaled) * (1.0 / HEAD)
        return inverse * scaled - raw * (inverse * inverse * inverse * inner)

    def by_column(which, raw):
        head0 = parts_ref[which].astype(F32)
        head1 = parts_ref[2 + which].astype(F32)
        a0, a1 = head0[:, :LANES], head1[:, :LANES]
        b0, b1 = head0[:, LANES:], head1[:, LANES:]
        d_q = norm_grad(raw[0], q_gain, jnp.where(low, a0, pltpu.roll(a1, HEAD, 1)))
        attn = jnp.where(low, pltpu.roll(a0, HEAD, 1), a1).astype(BF16)
        d_k = norm_grad(raw[1], k_gain, jnp.where(low, b0, pltpu.roll(b1, HEAD, 1)))
        d_v = jnp.where(low, pltpu.roll(b0, HEAD, 1), b1)
        return attn, [values.astype(BF16) for values in (d_q, d_k, d_v)]

    raw_far = [
        weights_far_ref[4 * width + array * rows : 4 * width + (array + 1) * rows, :]
        for array in range(2)
    ]
    attn, grads = by_column(core, [raw_ref[0], raw_ref[1]])
    attn_far, grads_far = by_column(1 - core, raw_far)
    both = (weights_ref, weights_far_ref)
    mixed = jnp.dot(
        jnp.concatenate([attn, attn_far], axis=1),
        jnp.concatenate([w_out_of(ref, width) for ref in both], axis=0),
        preferred_element_type=F32,
    ).astype(BF16)
    weights = [ref[part * width : (part + 1) * width, :] for ref in both for part in range(3)]
    d_hidden = rows_dot(
        jnp.concatenate(grads + grads_far, axis=1), jnp.concatenate(weights, axis=1)
    ).astype(BF16)
    for place in range(out_ref.shape[0]):
        at = slice(place * share, (place + 1) * share)
        out_ref[place, :, :width] = mixed[at]
        out_ref[place, :, width:] = d_hidden[at]


def project(parts, gains, raw, weights, weights_far, x_count, width):
    return pl.pallas_call(
        project_kernel,
        out_shape=jax.ShapeDtypeStruct((x_count, parts.shape[1] // x_count, 2 * width), BF16),
        in_specs=[VMEM] * 5,
        out_specs=VMEM,
        compiler_params=pltpu.CompilerParams(vmem_limit_bytes=VMEM_LIMIT),
    )(parts, gains, raw, weights, weights_far)


def ready_kernel(
    counts_ref,
    tokens_ref,
    cotangent_ref,
    modulation_ref,
    rows_ref,
    factors_ref,
):
    rows = rows_ref.shape[1]
    first_row = (lax.axis_index("x") * 2 + lax.axis_index("core")) * rows
    first = block_index() * tokens_ref.shape[0] + first_row
    _, scale, gate = modulation_rows(counts_ref, modulation_ref, first, rows)
    at = pl.ds(pl.multiple_of(first_row, rows), rows)
    normed, inv_std = layer_norm(tokens_ref[at, :].astype(F32))
    rows_ref[0] = tokens_ref[at, :]
    rows_ref[1] = cotangent_ref[at, :]
    factors_ref[0] = gate
    factors_ref[1] = 1.0 + scale
    factors_ref[2] = normed
    factors_ref[3] = jnp.broadcast_to(inv_std, normed.shape)


def ready(counts, tokens, cotangent, modulation, share):
    width = tokens.shape[1]
    return pl.pallas_call(
        ready_kernel,
        out_shape=(
            jax.ShapeDtypeStruct((2, share, width), BF16),
            jax.ShapeDtypeStruct((4, share, width), F32),
        ),
        in_specs=[SMEM] + [VMEM] * 3,
        out_specs=(VMEM, VMEM),
        compiler_params=pltpu.CompilerParams(vmem_limit_bytes=VMEM_LIMIT),
    )(counts, tokens, cotangent, modulation)


def leave_kernel(rows_ref, factors_ref, shares_ref, layer_ref, grad_ref):
    width = layer_ref.shape[1]
    sums = shares_ref[0].astype(F32)
    for share in range(1, shares_ref.shape[0]):
        sums = sums + shares_ref[share].astype(F32)
    layer = rows_ref[0].astype(F32) + factors_ref[0] * sums[:, :width]
    layer_ref[...] = layer.astype(BF16)
    d_normed = sums[:, width:] * factors_ref[1]
    normed = factors_ref[2]
    input_grad = rows_ref[1].astype(F32) + factors_ref[3] * (
        d_normed
        - jnp.mean(d_normed, axis=-1, keepdims=True)
        - normed * jnp.mean(d_normed * normed, axis=-1, keepdims=True)
    )
    grad_ref[...] = input_grad.astype(BF16)


def leave(rows, factors, shares):
    out = jax.ShapeDtypeStruct(rows.shape[1:], BF16)
    return pl.pallas_call(
        leave_kernel,
        out_shape=(out, out),
        in_specs=[VMEM] * 3,
        out_specs=(VMEM, VMEM),
        compiler_params=pltpu.CompilerParams(vmem_limit_bytes=VMEM_LIMIT),
    )(rows, factors, shares)


def per_device(tokens, cotangent, w_qkv, w_out, qk_gain, modulation, image_counts):
    tok_rows, model_width = tokens.shape
    z_count = lax.axis_size("z")
    x_count = lax.axis_size("x")
    quad = 4
    pair_rows = 2 * tok_rows
    share = tok_rows // (2 * x_count)
    w_parts = w_qkv.transpose(1, 0, 2)
    mod_parts = modulation.transpose(1, 0, 2)

    heads, raw, raw_far = enter(
        image_counts, qk_gain, tokens, cotangent, w_parts, w_out, mod_parts, quad
    )
    _, tokens_late, cotangent_late, mod_late, w_parts_late, w_out_late = (
        lax.optimization_barrier((heads, tokens, cotangent, mod_parts, w_parts, w_out))
    )
    rows, factors = ready(image_counts, tokens_late, cotangent_late, mod_late, share)
    weights = pack(w_parts_late, w_out_late, raw_far)
    mine = lax.all_to_all(heads, ("yh", "yl"), 0, 0)
    mine, rows, factors, weights = lax.optimization_barrier((mine, rows, factors, weights))
    mine = mine.reshape(quad * tok_rows, 2 * LANES)
    evens = range(0, z_count, 2)
    swaps = [((i - 1) % z_count, i) for i in evens], [(i, i + 1) for i in evens]
    first, second = (
        lax.ppermute(mine, "z", pairs + [(j, i) for i, j in pairs]) for pairs in swaps
    )
    halves = 4 * z_count
    far_half = jnp.where(
        lax.axis_index("yh") == lax.axis_index("core"), mine[pair_rows:], mine[:pair_rows]
    )

    def far_source(target):
        z, yh, core = target // 4, target // 2 % 2, target % 2
        return (z + (2 if yh else -2)) % z_count * 4 + (yh ^ core) * 2 + core

    far = lax.ppermute(
        far_half, ("z", "yh", "core"), [(far_source(i), i) for i in range(halves)]
    )
    early = attend_early(image_counts, first, mine)
    near_parts = attend_near(image_counts, second, early)
    weights_far = lax.ppermute(weights, "core", [(0, 1), (1, 0)])
    parts = attend_far(image_counts, far, near_parts)
    parts = lax.all_to_all(parts, ("yl", "core"), 0, 0)
    partial = project(parts, qk_gain, raw, weights, weights_far, x_count, model_width)
    shares = lax.all_to_all(partial, "x", 0, 0)
    return leave(rows, factors, shares)


def solution(mesh):
    split = jax.sharding.Mesh(mesh.devices.reshape(16, 2, 2, 4, 2), ("z", "yh", "yl", "x", "core"))
    dp, head = ("z", "yh", "yl"), ("x", "core")
    in_specs = (P(dp, None), P(dp, None), P(None, None, head), P(head, None), P(), P(), P())
    out_specs = (P(dp + head, None), P(dp + head, None))
    return jax.shard_map(
        per_device, mesh=split, in_specs=in_specs, out_specs=out_specs, check_vma=False
    )
```

```python
import math

import jax
import jax.numpy as jnp
from jax import lax
from jax.experimental import pallas as pl
from jax.experimental.pallas import tpu as pltpu
from jax.sharding import PartitionSpec as P

EPS = 1e-06
SAME_IMAGE = 512.0
LANES = 128
HEAD = 64
F32 = jnp.float32
BF16 = jnp.bfloat16
VMEM_LIMIT = 24 * 1024 * 1024
ENTER_LIMIT = 60 * 1024 * 1024
VMEM = pl.BlockSpec(memory_space=pltpu.VMEM)
SMEM = pl.BlockSpec(memory_space=pltpu.SMEM)


def rows_dot(a, b):
    return lax.dot_general(a, b, (((1,), (1,)), ((), ())), preferred_element_type=F32)


def block_index():
    return (lax.axis_index("z") * 2 + lax.axis_index("yh")) * 2 + lax.axis_index("yl")


def image_bounds(counts_ref, first_lane):
    lane = lax.broadcasted_iota(jnp.int32, (1, LANES), 1)
    starts = jnp.zeros((1, LANES), jnp.int32)
    ends = jnp.zeros((1, LANES), jnp.int32)
    total = jnp.int32(0)
    for image in range(counts_ref.shape[0]):
        here = lane == first_lane + image
        starts = jnp.where(here, total, starts)
        total = total + counts_ref[image]
        ends = jnp.where(here, total, ends)
    return starts, ends


def modulation_rows(counts_ref, modulation_ref, first, rows):
    starts, ends = image_bounds(counts_ref, 0)
    place = first + lax.broadcasted_iota(jnp.int32, (rows, LANES), 0)
    member = ((place >= starts) & (place < ends)).astype(F32).astype(BF16)
    member = member[:, : modulation_ref.shape[1]]
    return [
        jnp.dot(member, modulation_ref[part], preferred_element_type=F32) for part in range(3)
    ]


def layer_norm(values):
    average = jnp.mean(values, axis=-1, keepdims=True)
    centred = values - average
    inv_std = lax.rsqrt(jnp.mean(centred * centred, axis=-1, keepdims=True) + EPS)
    return centred * inv_std, inv_std


def head_sums(values):
    lanes = (LANES, LANES)
    first = lax.broadcasted_iota(jnp.int32, lanes, 0) < HEAD
    second = lax.broadcasted_iota(jnp.int32, lanes, 1) < HEAD
    ones = (first == second).astype(F32).astype(BF16)
    large = values.astype(BF16)
    small = (values - large.astype(F32)).astype(BF16)
    large = jnp.dot(large, ones, preferred_element_type=F32)
    return large + jnp.dot(small, ones, preferred_element_type=F32)


def both_heads(gains_ref, which):
    gain = gains_ref[which : which + 1, :]
    return jnp.concatenate([gain, gain], axis=1)


def head_scale(raw):
    return lax.rsqrt(head_sums(raw * raw) * (1.0 / HEAD) + EPS)


def enter_kernel(
    counts_ref,
    gains_ref,
    tokens_ref,
    cotangent_ref,
    w_qkv_ref,
    w_out_ref,
    modulation_ref,
    out_ref,
    raw_ref,
    raw_far_ref,
    rows_ref,
    factors_ref,
    hidden_ref,
    d_mixed_ref,
):
    rows = tokens_ref.shape[0]
    starts, ends = image_bounds(counts_ref, 0)
    place = block_index() * rows + lax.broadcasted_iota(jnp.int32, (rows, LANES), 0)
    member = ((place >= starts) & (place < ends)).astype(F32).astype(BF16)
    member = member[:, : modulation_ref.shape[1]]
    for part in range(3):
        factors_ref[part] = jnp.dot(member, modulation_ref[part], preferred_element_type=F32)
    for begin in range(0, rows, 16):
        at = slice(begin, begin + 16)
        normed, _ = layer_norm(tokens_ref[at, :].astype(F32))
        hidden = normed * (1.0 + factors_ref[1, at, :]) + factors_ref[0, at, :]
        hidden_ref[at, :] = hidden.astype(BF16)
        d_mixed = cotangent_ref[at, :].astype(F32) * factors_ref[2, at, :]
        d_mixed_ref[at, :] = d_mixed.astype(BF16)
    weights = jnp.concatenate([w_qkv_ref[part] for part in range(3)], axis=1)
    qkv = jnp.dot(hidden_ref[...], weights, preferred_element_type=F32)
    q, k, v = (qkv[:, part * LANES : (part + 1) * LANES] for part in range(3))
    d_attn = rows_dot(d_mixed_ref[...], w_out_ref[...])
    rows_ref[0] = q.astype(BF16)
    rows_ref[1] = k.astype(BF16)
    q = rows_ref[0].astype(F32)
    k = rows_ref[1].astype(F32)
    q = q * head_scale(q) * (both_heads(gains_ref, 0) * (1.0 / math.sqrt(HEAD)))
    k = k * head_scale(k) * both_heads(gains_ref, 1)
    core = lax.axis_index("core")
    share = raw_ref.shape[1] // 4
    for ref, side in ((raw_ref, core), (raw_far_ref, 1 - core)):
        for part in range(4):
            begin = pl.multiple_of((2 * part + side) * share, share)
            for array in range(2):
                ref[array, part * share : (part + 1) * share, :] = rows_ref[
                    array, pl.ds(begin, share), :
                ]
    low = low_lanes()

    def beside(left, right):
        return jnp.where(low, left, right).astype(BF16)

    q_v = (beside(q, pltpu.roll(v, HEAD, 1)), beside(pltpu.roll(q, HEAD, 1), v))
    k_d = (beside(k, pltpu.roll(d_attn, HEAD, 1)), beside(pltpu.roll(k, HEAD, 1), d_attn))
    for place in range(out_ref.shape[0]):
        out_ref[place, :, 0:LANES] = q_v[place % 2]
        out_ref[place, :, LANES:] = k_d[place % 2]


def enter(counts, gains, tokens, cotangent, w_parts, w_out, modulation, quad):
    rows = tokens.shape[0]
    raw = jax.ShapeDtypeStruct((2, rows // 2, LANES), BF16)
    return pl.pallas_call(
        enter_kernel,
        out_shape=(jax.ShapeDtypeStruct((quad, rows, 2 * LANES), BF16), raw, raw),
        in_specs=[SMEM] + [VMEM] * 6,
        out_specs=(VMEM,) * 3,
        scratch_shapes=[
            pltpu.VMEM((2, rows, LANES), BF16),
            pltpu.VMEM((3,) + tokens.shape, F32),
            pltpu.VMEM(tokens.shape, BF16),
            pltpu.VMEM(tokens.shape, BF16),
        ],
        compiler_params=pltpu.CompilerParams(vmem_limit_bytes=ENTER_LIMIT),
    )(counts, gains, tokens, cotangent, w_parts, w_out, modulation)


def pack_kernel(w_qkv_ref, w_out_ref, raw_ref, weights_ref, sems):
    width = w_out_ref.shape[1]
    rows = raw_ref.shape[1]
    pairs = []
    for part in range(3):
        pairs.append((w_qkv_ref.at[part], weights_ref.at[part * width : (part + 1) * width, :]))
    for tile in range(width // LANES):
        at = slice(tile * LANES, (tile + 1) * LANES)
        to = slice(3 * width + tile * LANES, 3 * width + (tile + 1) * LANES)
        pairs.append((w_out_ref.at[:, at], weights_ref.at[to, :]))
    for array in range(2):
        to = slice(4 * width + array * rows, 4 * width + (array + 1) * rows)
        pairs.append((raw_ref.at[array], weights_ref.at[to, :]))
    copies = [
        pltpu.make_async_copy(source, target, sems.at[place])
        for place, (source, target) in enumerate(pairs)
    ]
    for copy in copies:
        copy.start()
    for copy in copies:
        copy.wait()


def pack(w_parts, w_out, raw):
    width = w_out.shape[1]
    whole = pl.BlockSpec(memory_space=pl.ANY)
    return pl.pallas_call(
        pack_kernel,
        out_shape=jax.ShapeDtypeStruct((4 * width + 2 * raw.shape[1], LANES), BF16),
        in_specs=[whole] * 3,
        out_specs=VMEM,
        scratch_shapes=[pltpu.SemaphoreType.DMA((5 + width // LANES,))],
        compiler_params=pltpu.CompilerParams(vmem_limit_bytes=8 * 1024 * 1024),
    )(w_parts, w_out, raw)


def w_out_of(weights_ref, width):
    return jnp.concatenate(
        [
            weights_ref[3 * width + tile * LANES : 3 * width + (tile + 1) * LANES, :]
            for tile in range(width // LANES)
        ],
        axis=1,
    )


LOG2_E = math.log2(math.e)
INV_ROOT = 1.0 / math.sqrt(HEAD)
CHUNK = 256
TILE = 64
MAIN = 6
REACH_CHUNKS = 4


def low_lanes():
    return lax.broadcasted_iota(jnp.int32, (1, LANES), 1) < HEAD


def place_block(source, place, starts, ends, stores):
    low = low_lanes()
    rows = source.shape[0]
    at = place + lax.broadcasted_iota(jnp.int32, (rows, LANES), 0)
    same = ((at >= starts) & (at < ends)).astype(F32)
    first = source[:, 0:LANES].astype(F32)
    second = source[:, LANES:].astype(F32)
    q_store, k_store, v_store, d_store, kv_store = stores
    q_store[...] = jnp.where(low, first, same * SAME_IMAGE).astype(BF16)
    k_store[...] = jnp.where(low, second, same).astype(BF16)
    v_store[...] = jnp.where(low, 0.0, first).astype(BF16)
    d_store[...] = source[:, LANES:]
    kv_store[...] = jnp.where(low, second, first).astype(BF16).T


def window_facts(counts_ref):
    half = lax.axis_index("yh")
    origin = (block_index() // 4 - 1) * 2 * CHUNK
    own_at = (2 + half) * CHUNK
    starts, ends = image_bounds(counts_ref, HEAD)
    left_from = jnp.int32(-CHUNK)
    right_to = jnp.int32((MAIN + 1) * CHUNK)
    total = -origin
    for image in range(counts_ref.shape[0]):
        left_from = jnp.where(total <= own_at, total, left_from)
        ended = total >= own_at + CHUNK
        total = total + counts_ref[image]
        right_to = jnp.where((total >= own_at + CHUNK) & jnp.logical_not(ended), total, right_to)
    return half, own_at, starts - origin, ends - origin, left_from, right_to


def by_eight(values):
    return values.reshape(values.shape[0] // 8, 8, values.shape[1])


def add_tiles(s_ref, g_ref, rows, highest, total, grads):
    for piece in range(rows // TILE):
        at = slice(piece * TILE, (piece + 1) * TILE)
        weights = jnp.exp2(s_ref[at, :] * LOG2_E - highest)
        total = total + jnp.sum(by_eight(weights), axis=0)
        grads = grads + jnp.sum(by_eight(weights * g_ref[at, :]), axis=0)
    return total, grads


def rows_max(values):
    return jnp.max(by_eight(values), axis=0)


def chunks_from(key, count, *refs):
    rows = [pl.ds(pl.multiple_of(key + i * CHUNK, CHUNK), CHUNK) for i in range(count)]
    return [tuple(ref.at[at, :] for ref in refs) for at in rows]


def running_sums(pieces, q_block, d_block, s_ref, g_ref):
    highest = jnp.full((8, CHUNK), -jnp.inf, F32)
    total = jnp.zeros((8, CHUNK), F32)
    grads = jnp.zeros((8, CHUNK), F32)
    for piece, (keys_ref, values_ref) in enumerate(pieces):
        here = slice(piece * CHUNK, (piece + 1) * CHUNK)
        scores = rows_dot(keys_ref[...], q_block)
        s_ref[here, :] = scores
        g_ref[here, :] = rows_dot(values_ref[...], d_block)
        higher = jnp.maximum(highest, rows_max(scores) * LOG2_E)
        shrink = jnp.exp2(highest - higher)
        total = total * shrink
        grads = grads * shrink
        highest = higher
        for tile in range(CHUNK // TILE):
            at = slice(piece * CHUNK + tile * TILE, piece * CHUNK + (tile + 1) * TILE)
            weights = jnp.exp2(by_eight(s_ref[at, :]) * LOG2_E - highest[None])
            total = total + jnp.sum(weights, axis=0)
            grads = grads + jnp.sum(weights * by_eight(g_ref[at, :]), axis=0)
    top = jnp.max(highest, axis=0, keepdims=True)
    shrink = jnp.exp2(highest - top)
    total = jnp.sum(total * shrink, axis=0, keepdims=True)
    return top, total, jnp.sum(grads * shrink, axis=0, keepdims=True)


def early_kernel(
    counts_ref,
    first_ref,
    quad_ref,
    qa_ref,
    ka_ref,
    va_ref,
    da_ref,
    kva_ref,
    sa_ref,
    ga_ref,
    top_ref,
):
    half, _, starts, ends, _, _ = window_facts(counts_ref)
    block_rows = CHUNK // 2
    to_first = jnp.where(lax.rem(lax.axis_index("z"), 2) == 0, 2 * CHUNK, -2 * CHUNK)
    for block in range(8):
        at = slice(block * block_rows, (block + 1) * block_rows)
        inner = slice(block % 4 * block_rows, (block % 4 + 1) * block_rows)
        place = 2 * CHUNK + block % 4 * block_rows
        stores = [ref.at[at, :] for ref in (qa_ref, ka_ref, va_ref, da_ref)]
        stores.append(kva_ref.at[:, at])
        if block < 4:
            place_block(quad_ref.at[inner], place, starts, ends, stores)
        else:
            place_block(first_ref.at[inner], place + to_first, starts, ends, stores)

    own_rows = pl.ds(pl.multiple_of(half * CHUNK, CHUNK), CHUNK)
    q_own = qa_ref[own_rows, :]
    d_own = da_ref[own_rows, :]
    highest = jnp.full((8, CHUNK), -jnp.inf, F32)
    for piece in range(4):
        at = slice(piece * CHUNK, (piece + 1) * CHUNK)
        scores = rows_dot(ka_ref[at, :], q_own)
        sa_ref[at, :] = scores
        highest = jnp.maximum(highest, rows_max(scores))
        ga_ref[at, :] = rows_dot(va_ref[at, :], d_own)
    top_ref[...] = highest


def attend_early(counts, first, quad):
    rows = 4 * CHUNK
    head_rows = jax.ShapeDtypeStruct((rows, LANES), BF16)
    scores = jax.ShapeDtypeStruct((rows, CHUNK), F32)
    return pl.pallas_call(
        early_kernel,
        out_shape=(head_rows,) * 4
        + (jax.ShapeDtypeStruct((LANES, rows), BF16), scores, scores)
        + (jax.ShapeDtypeStruct((8, CHUNK), F32),),
        in_specs=[SMEM] + [VMEM] * 2,
        out_specs=(VMEM,) * 8,
        compiler_params=pltpu.CompilerParams(vmem_limit_bytes=VMEM_LIMIT),
    )(counts, first, quad)


def near_kernel(
    counts_ref,
    second_ref,
    qa_ref,
    ka_ref,
    va_ref,
    da_ref,
    kva_ref,
    sa_ref,
    ga_ref,
    top_ref,
    qx_ref,
    kx_ref,
    vx_ref,
    dx_ref,
    kv_ref,
    so_ref,
    go_ref,
    sn_ref,
    gn_ref,
    stats_ref,
    s_ref,
    g_ref,
):
    half, own_at, starts, ends, left_from, right_to = window_facts(counts_ref)
    block_rows = CHUNK // 2
    even = lax.rem(lax.axis_index("z"), 2) == 0
    first_at = pl.multiple_of(jnp.where(even, 4 * CHUNK, 0), 2 * CHUNK)
    second_at = pl.multiple_of(jnp.where(even, 0, 4 * CHUNK), 2 * CHUNK)
    early = ((qa_ref, qx_ref), (ka_ref, kx_ref), (va_ref, vx_ref), (da_ref, dx_ref))
    for source, target in early:
        target[2 * CHUNK : 4 * CHUNK, :] = source[0 : 2 * CHUNK, :]
        target[pl.ds(first_at, 2 * CHUNK), :] = source[2 * CHUNK : 4 * CHUNK, :]
    kv_ref[:, 2 * CHUNK : 4 * CHUNK] = kva_ref[:, 0 : 2 * CHUNK]
    kv_ref[:, pl.ds(first_at, 2 * CHUNK)] = kva_ref[:, 2 * CHUNK : 4 * CHUNK]
    for block in range(4):
        inner = slice(block * block_rows, (block + 1) * block_rows)
        begin = pl.multiple_of(second_at + block * block_rows, block_rows)
        at = pl.ds(begin, block_rows)
        stores = [ref.at[at, :] for ref in (qx_ref, kx_ref, vx_ref, dx_ref)]
        place_block(second_ref.at[inner], begin, starts, ends, stores + [kv_ref.at[:, at]])

    own_rows = pl.ds(pl.multiple_of(half * CHUNK, CHUNK), CHUNK)
    q_own = qa_ref[own_rows, :]
    d_own = da_ref[own_rows, :]
    highest = top_ref[...]
    for piece in range(2):
        at = pl.ds(pl.multiple_of(second_at + piece * CHUNK, CHUNK), CHUNK)
        scores = rows_dot(kx_ref[at, :], q_own)
        so_ref[at, :] = scores
        highest = jnp.maximum(highest, rows_max(scores))
        go_ref[at, :] = rows_dot(vx_ref[at, :], d_own)
    highest = jnp.max(highest, axis=0, keepdims=True) * LOG2_E
    total = jnp.zeros((8, CHUNK), F32)
    grads = jnp.zeros((8, CHUNK), F32)
    for piece in range(MAIN * CHUNK // TILE):
        inner = piece * TILE
        if inner < 2 * CHUNK:
            to = pl.ds(2 * CHUNK + inner, TILE)
        elif inner < 4 * CHUNK:
            to = pl.ds(pl.multiple_of(first_at + inner - 2 * CHUNK, TILE), TILE)
        else:
            to = pl.ds(pl.multiple_of(second_at + inner - 4 * CHUNK, TILE), TILE)
        if inner < 4 * CHUNK:
            scores = sa_ref[inner : inner + TILE, :]
            given = ga_ref[inner : inner + TILE, :]
            go_ref[to, :] = given
        else:
            scores = so_ref[to, :]
            given = go_ref[to, :]
        weights = jnp.exp2(scores * LOG2_E - highest)
        so_ref[to, :] = weights
        total = total + jnp.sum(by_eight(weights), axis=0)
        grads = grads + jnp.sum(by_eight(weights * given), axis=0)
    stats_ref[MAIN, 0:1, :] = highest
    stats_ref[MAIN, 1:2, :] = jnp.sum(total, axis=0, keepdims=True)
    stats_ref[MAIN, 2:3, :] = jnp.sum(grads, axis=0, keepdims=True)

    left_key = jnp.clip((left_from + CHUNK) // CHUNK - 1, 0, MAIN - REACH_CHUNKS)
    right_key = jnp.clip((right_to - 1) // CHUNK - (REACH_CHUNKS - 1), 0, MAIN - REACH_CHUNKS)

    def one_chunk(step, carry):
        slot = step + jnp.where(step >= 2 + half, 1, 0)
        begin = slot * CHUNK

        @pl.when((begin < right_to) & (begin + CHUNK > left_from))
        def _():
            at = pl.ds(pl.multiple_of(begin, CHUNK), CHUNK)
            key = jnp.where(begin < own_at, left_key, right_key) * CHUNK
            q_block = qx_ref[at, :]
            d_block = dx_ref[at, :]
            pieces = chunks_from(key, REACH_CHUNKS, kx_ref, vx_ref)
            highest, total, grads = running_sums(pieces, q_block, d_block, s_ref, g_ref)
            stats_ref[slot, 0:1, :] = highest
            stats_ref[slot, 1:2, :] = total
            stats_ref[slot, 2:3, :] = grads
            near_at = pl.ds(pl.multiple_of(own_at - key, CHUNK), CHUNK)
            sn_ref[slot, :, :] = s_ref[near_at, :]
            gn_ref[slot, :, :] = g_ref[near_at, :]

        return carry

    lax.fori_loop(0, MAIN - 1, one_chunk, 0)


def attend_near(counts, second, early):
    rows = MAIN * CHUNK
    head_rows = jax.ShapeDtypeStruct((rows, LANES), BF16)
    scores = jax.ShapeDtypeStruct((rows, CHUNK), F32)
    tiles = jax.ShapeDtypeStruct((MAIN, CHUNK, CHUNK), F32)
    return pl.pallas_call(
        near_kernel,
        out_shape=(head_rows,) * 4
        + (jax.ShapeDtypeStruct((LANES, rows), BF16),)
        + (scores, scores, tiles, tiles, jax.ShapeDtypeStruct((MAIN + 1, 8, CHUNK), F32)),
        in_specs=[SMEM] + [VMEM] * (1 + len(early)),
        out_specs=(VMEM,) * 10,
        scratch_shapes=[pltpu.VMEM((REACH_CHUNKS * CHUNK, CHUNK), F32)] * 2,
        cost_estimate=pl.CostEstimate(
            flops=9000000000, bytes_accessed=1 << 20, transcendentals=1 << 20
        ),
        compiler_params=pltpu.CompilerParams(vmem_limit_bytes=VMEM_LIMIT),
    )(counts, second, *early)


def far_kernel(
    counts_ref,
    far_ref,
    qx_ref,
    kx_ref,
    vx_ref,
    dx_ref,
    kv_ref,
    so_ref,
    go_ref,
    sn_ref,
    gn_ref,
    stats_ref,
    out_ref,
    qf_ref,
    kf_ref,
    vf_ref,
    df_ref,
    kvf_ref,
    s_ref,
    g_ref,
    p_ref,
    d_ref,
    pn_ref,
    dn_ref,
    sums_ref,
    dk_ref,
    dv_ref,
    own_out_ref,
    done_ref,
):
    half, own_at, starts, ends, left_from, right_to = window_facts(counts_ref)
    block_rows = CHUNK // 2
    rows = MAIN * CHUNK
    far_at = jnp.where(half == 0, -CHUNK, rows)
    for block in range(2):
        at = slice(block * block_rows, (block + 1) * block_rows)
        stores = [ref.at[at, :] for ref in (qf_ref, kf_ref, vf_ref, df_ref)]
        place_block(
            far_ref.at[at],
            far_at + block * block_rows,
            starts,
            ends,
            stores + [kvf_ref.at[:, at]],
        )

    own_rows = pl.ds(pl.multiple_of(own_at, CHUNK), CHUNK)
    q_own = qx_ref[own_rows, :]
    d_own = dx_ref[own_rows, :]
    scores = rows_dot(kf_ref[...], q_own)
    s_ref[0:CHUNK, :] = scores
    g_ref[0:CHUNK, :] = rows_dot(vf_ref[...], d_own)
    near_highest = stats_ref[MAIN, 0:1, :]
    highest = jnp.max(rows_max(scores), axis=0, keepdims=True) * LOG2_E
    highest = jnp.maximum(near_highest, highest)
    shrink = jnp.exp2(near_highest - highest)
    zeros = jnp.zeros((8, CHUNK), F32)
    total, grads = add_tiles(s_ref, g_ref, CHUNK, highest, zeros, zeros)
    total = jnp.sum(total, axis=0, keepdims=True) + stats_ref[MAIN, 1:2, :] * shrink
    grads = jnp.sum(grads, axis=0, keepdims=True) + stats_ref[MAIN, 2:3, :] * shrink
    scale = 1.0 / total
    mean_grad = grads * scale

    near_scale = shrink * scale
    for piece in range(rows // TILE):
        at = slice(piece * TILE, (piece + 1) * TILE)
        probs = so_ref[at, :] * near_scale
        p_ref[at, :] = probs.astype(BF16)
        d_ref[at, :] = (probs * (go_ref[at, :] - mean_grad)).astype(BF16)
    for piece in range(CHUNK // TILE):
        at = slice(piece * TILE, (piece + 1) * TILE)
        to = slice(rows + piece * TILE, rows + (piece + 1) * TILE)
        probs = jnp.exp2(s_ref[at, :] * LOG2_E - highest) * scale
        p_ref[to, :] = probs.astype(BF16)
        d_ref[to, :] = (probs * (g_ref[at, :] - mean_grad)).astype(BF16)
    pn_ref[:, own_rows] = p_ref[own_rows, :]
    dn_ref[:, own_rows] = d_ref[own_rows, :]

    def times_window(values_ref):
        main = jnp.dot(kv_ref[...], values_ref[0:rows, :], preferred_element_type=F32)
        return main + jnp.dot(
            kvf_ref[...], values_ref[rows : rows + CHUNK, :], preferred_element_type=F32
        )

    upper = lax.broadcasted_iota(jnp.int32, (LANES, CHUNK), 0) < HEAD
    own_out_ref[...] = jnp.where(
        upper, times_window(d_ref) * INV_ROOT, times_window(p_ref)
    ).T

    query_lane = lax.broadcasted_iota(jnp.int32, (1, CHUNK), 1)
    reaches_far = jnp.where(half == 0, left_from < 0, right_to > rows)
    sums_ref[...] = stats_ref[...]
    dk_ref[...] = jnp.zeros_like(dk_ref)
    dv_ref[...] = jnp.zeros_like(dv_ref)

    @pl.when(reaches_far)
    def _():
        for step in range(2):
            slot = half * (MAIN - 2) + step
            at = pl.ds(pl.multiple_of(slot * CHUNK, CHUNK), CHUNK)
            space = pl.ds((REACH_CHUNKS + step) * CHUNK, CHUNK)
            highest, total, grads = running_sums(
                [(kf_ref, vf_ref)], qx_ref[at, :], dx_ref[at, :], s_ref.at[space], g_ref.at[space]
            )
            before = sums_ref[slot, 0:1, :]
            higher = jnp.maximum(before, highest)
            old = jnp.exp2(before - higher)
            new = jnp.exp2(highest - higher)
            sums_ref[slot, 0:1, :] = higher
            sums_ref[slot, 1:2, :] = sums_ref[slot, 1:2, :] * old + total * new
            sums_ref[slot, 2:3, :] = sums_ref[slot, 2:3, :] * old + grads * new

        q_block = qf_ref[...]
        d_block = df_ref[...]
        key = half * (MAIN // 2) * CHUNK
        pieces = chunks_from(key, REACH_CHUNKS - 1, kx_ref, vx_ref) + [(kf_ref, vf_ref)]
        highest, total, grads = running_sums(pieces, q_block, d_block, s_ref, g_ref)
        place = query_lane + far_at
        scale = jnp.where((place >= left_from) & (place < right_to), 1.0 / total, 0.0)
        mean_grad = grads * scale
        for piece in range(CHUNK // TILE):
            at = slice(piece * TILE, (piece + 1) * TILE)
            near_at = pl.ds(pl.multiple_of(own_at - key + piece * TILE, TILE), TILE)
            probs = jnp.exp2(s_ref[near_at, :] * LOG2_E - highest) * scale
            p_ref[at, :] = probs.astype(BF16)
            d_ref[at, :] = (probs * (g_ref[near_at, :] - mean_grad)).astype(BF16)
        dk_ref[...] = jnp.dot(d_ref[0:CHUNK, :], q_block, preferred_element_type=F32)
        dv_ref[...] = jnp.dot(p_ref[0:CHUNK, :], d_block, preferred_element_type=F32)

    for step in range(MAIN - 1):
        slot = step + jnp.where(step >= 2 + half, 1, 0)
        begin = slot * CHUNK
        chunk_at = pl.ds(pl.multiple_of(begin, CHUNK), CHUNK)
        place = query_lane + begin
        valid = (place >= left_from) & (place < right_to)
        highest = sums_ref[slot, 0:1, :]
        scale = 1.0 / sums_ref[slot, 1:2, :]
        mean_grad = sums_ref[slot, 2:3, :] * scale
        for piece in range(CHUNK // TILE):
            at = slice(piece * TILE, (piece + 1) * TILE)
            probs = jnp.exp2(sn_ref[slot, at, :] * LOG2_E - highest) * scale
            d_scores = probs * (gn_ref[slot, at, :] - mean_grad)
            pn_ref[at, chunk_at] = jnp.where(valid, probs, 0.0).astype(BF16)
            dn_ref[at, chunk_at] = jnp.where(valid, d_scores, 0.0).astype(BF16)
    d_key = dk_ref[...] + jnp.dot(dn_ref[...], qx_ref[...], preferred_element_type=F32)
    d_value = dv_ref[...] + jnp.dot(pn_ref[...], dx_ref[...], preferred_element_type=F32)
    done_ref[:, 0:LANES] = own_out_ref[...].astype(BF16)
    done_ref[:, LANES:] = jnp.where(low_lanes(), d_key, d_value).astype(BF16)
    share = 16
    for member in range(out_ref.shape[0]):
        block, core = member // 2, member % 2
        for part in range(out_ref.shape[1] // share):
            begin = (block * 8 + part * 2 + core) * share
            out_ref[member, part * share : (part + 1) * share, :] = done_ref[
                begin : begin + share, :
            ]


def attend_far(counts, far, near_parts):
    return pl.pallas_call(
        far_kernel,
        out_shape=jax.ShapeDtypeStruct((4, CHUNK // 4, 2 * LANES), BF16),
        in_specs=[SMEM] + [VMEM] * (1 + len(near_parts)),
        out_specs=VMEM,
        scratch_shapes=[pltpu.VMEM((CHUNK, LANES), BF16)] * 4
        + [pltpu.VMEM((LANES, CHUNK), BF16)]
        + [pltpu.VMEM(((REACH_CHUNKS + 2) * CHUNK, CHUNK), F32)] * 2
        + [pltpu.VMEM(((MAIN + 1) * CHUNK, CHUNK), BF16)] * 2
        + [pltpu.VMEM((CHUNK, MAIN * CHUNK), BF16)] * 2
        + [pltpu.VMEM((MAIN + 1, 8, CHUNK), F32)]
        + [pltpu.VMEM((CHUNK, LANES), F32)] * 3
        + [pltpu.VMEM((CHUNK, 2 * LANES), BF16)],
        cost_estimate=pl.CostEstimate(
            flops=9000000000, bytes_accessed=1 << 20, transcendentals=1 << 20
        ),
        compiler_params=pltpu.CompilerParams(vmem_limit_bytes=VMEM_LIMIT),
    )(counts, far, *near_parts)


def project_kernel(parts_ref, gains_ref, raw_ref, weights_ref, weights_far_ref, out_ref):
    rows = parts_ref.shape[1]
    width = out_ref.shape[2] // 2
    share = out_ref.shape[1]
    core = lax.axis_index("core")
    low = low_lanes()
    q_gain = both_heads(gains_ref, 0)
    k_gain = both_heads(gains_ref, 1)

    def norm_grad(raw, gain, d_norm):
        raw = raw.astype(F32)
        inverse = head_scale(raw)
        scaled = d_norm * gain
        inner = head_sums(raw * scaled) * (1.0 / HEAD)
        return inverse * scaled - raw * (inverse * inverse * inverse * inner)

    def by_column(which, raw):
        head0 = parts_ref[which].astype(F32)
        head1 = parts_ref[2 + which].astype(F32)
        a0, a1 = head0[:, :LANES], head1[:, :LANES]
        b0, b1 = head0[:, LANES:], head1[:, LANES:]
        d_q = norm_grad(raw[0], q_gain, jnp.where(low, a0, pltpu.roll(a1, HEAD, 1)))
        attn = jnp.where(low, pltpu.roll(a0, HEAD, 1), a1).astype(BF16)
        d_k = norm_grad(raw[1], k_gain, jnp.where(low, b0, pltpu.roll(b1, HEAD, 1)))
        d_v = jnp.where(low, pltpu.roll(b0, HEAD, 1), b1)
        return attn, [values.astype(BF16) for values in (d_q, d_k, d_v)]

    raw_far = [
        weights_far_ref[4 * width + array * rows : 4 * width + (array + 1) * rows, :]
        for array in range(2)
    ]
    attn, grads = by_column(core, [raw_ref[0], raw_ref[1]])
    attn_far, grads_far = by_column(1 - core, raw_far)
    both = (weights_ref, weights_far_ref)
    mixed = jnp.dot(
        jnp.concatenate([attn, attn_far], axis=1),
        jnp.concatenate([w_out_of(ref, width) for ref in both], axis=0),
        preferred_element_type=F32,
    ).astype(BF16)
    weights = [ref[part * width : (part + 1) * width, :] for ref in both for part in range(3)]
    d_hidden = rows_dot(
        jnp.concatenate(grads + grads_far, axis=1), jnp.concatenate(weights, axis=1)
    ).astype(BF16)
    for place in range(out_ref.shape[0]):
        at = slice(place * share, (place + 1) * share)
        out_ref[place, :, :width] = mixed[at]
        out_ref[place, :, width:] = d_hidden[at]


def project(parts, gains, raw, weights, weights_far, x_count, width):
    return pl.pallas_call(
        project_kernel,
        out_shape=jax.ShapeDtypeStruct((x_count, parts.shape[1] // x_count, 2 * width), BF16),
        in_specs=[VMEM] * 5,
        out_specs=VMEM,
        compiler_params=pltpu.CompilerParams(vmem_limit_bytes=VMEM_LIMIT),
    )(parts, gains, raw, weights, weights_far)


def ready_kernel(
    counts_ref,
    tokens_ref,
    cotangent_ref,
    modulation_ref,
    rows_ref,
    factors_ref,
):
    rows = rows_ref.shape[1]
    first_row = (lax.axis_index("x") * 2 + lax.axis_index("core")) * rows
    first = block_index() * tokens_ref.shape[0] + first_row
    _, scale, gate = modulation_rows(counts_ref, modulation_ref, first, rows)
    at = pl.ds(pl.multiple_of(first_row, rows), rows)
    normed, inv_std = layer_norm(tokens_ref[at, :].astype(F32))
    rows_ref[0] = tokens_ref[at, :]
    rows_ref[1] = cotangent_ref[at, :]
    factors_ref[0] = gate
    factors_ref[1] = 1.0 + scale
    factors_ref[2] = normed
    factors_ref[3] = jnp.broadcast_to(inv_std, normed.shape)


def ready(counts, tokens, cotangent, modulation, share):
    width = tokens.shape[1]
    return pl.pallas_call(
        ready_kernel,
        out_shape=(
            jax.ShapeDtypeStruct((2, share, width), BF16),
            jax.ShapeDtypeStruct((4, share, width), F32),
        ),
        in_specs=[SMEM] + [VMEM] * 3,
        out_specs=(VMEM, VMEM),
        compiler_params=pltpu.CompilerParams(vmem_limit_bytes=VMEM_LIMIT),
    )(counts, tokens, cotangent, modulation)


def leave_kernel(rows_ref, factors_ref, shares_ref, layer_ref, grad_ref):
    width = layer_ref.shape[1]
    sums = shares_ref[0].astype(F32)
    for share in range(1, shares_ref.shape[0]):
        sums = sums + shares_ref[share].astype(F32)
    layer = rows_ref[0].astype(F32) + factors_ref[0] * sums[:, :width]
    layer_ref[...] = layer.astype(BF16)
    d_normed = sums[:, width:] * factors_ref[1]
    normed = factors_ref[2]
    input_grad = rows_ref[1].astype(F32) + factors_ref[3] * (
        d_normed
        - jnp.mean(d_normed, axis=-1, keepdims=True)
        - normed * jnp.mean(d_normed * normed, axis=-1, keepdims=True)
    )
    grad_ref[...] = input_grad.astype(BF16)


def leave(rows, factors, shares):
    out = jax.ShapeDtypeStruct(rows.shape[1:], BF16)
    return pl.pallas_call(
        leave_kernel,
        out_shape=(out, out),
        in_specs=[VMEM] * 3,
        out_specs=(VMEM, VMEM),
        compiler_params=pltpu.CompilerParams(vmem_limit_bytes=VMEM_LIMIT),
    )(rows, factors, shares)


def per_device(tokens, cotangent, w_qkv, w_out, qk_gain, modulation, image_counts):
    tok_rows, model_width = tokens.shape
    z_count = lax.axis_size("z")
    x_count = lax.axis_size("x")
    quad = 4
    pair_rows = 2 * tok_rows
    share = tok_rows // (2 * x_count)
    w_parts = w_qkv.transpose(1, 0, 2)
    mod_parts = modulation.transpose(1, 0, 2)

    heads, raw, raw_far = enter(
        image_counts, qk_gain, tokens, cotangent, w_parts, w_out, mod_parts, quad
    )
    _, tokens_late, cotangent_late, mod_late, w_parts_late, w_out_late = (
        lax.optimization_barrier((heads, tokens, cotangent, mod_parts, w_parts, w_out))
    )
    rows, factors = ready(image_counts, tokens_late, cotangent_late, mod_late, share)
    weights = pack(w_parts_late, w_out_late, raw_far)
    mine = lax.all_to_all(heads, ("yh", "yl"), 0, 0)
    mine, rows, factors, weights = lax.optimization_barrier((mine, rows, factors, weights))
    mine = mine.reshape(quad * tok_rows, 2 * LANES)
    evens = range(0, z_count, 2)
    swaps = [(i, i + 1) for i in evens], [((i - 1) % z_count, i) for i in evens]
    first, second = (
        lax.ppermute(mine, "z", pairs + [(j, i) for i, j in pairs]) for pairs in swaps
    )
    halves = 4 * z_count
    far_half = jnp.where(
        lax.axis_index("yh") == lax.axis_index("core"), mine[pair_rows:], mine[:pair_rows]
    )

    def far_source(target):
        z, yh, core = target // 4, target // 2 % 2, target % 2
        return (z + (2 if yh else -2)) % z_count * 4 + (yh ^ core) * 2 + core

    far = lax.ppermute(
        far_half, ("z", "yh", "core"), [(far_source(i), i) for i in range(halves)]
    )
    early = attend_early(image_counts, first, mine)
    weights_late, early_first = lax.optimization_barrier((weights, early[0]))
    early = (early_first,) + tuple(early[1:])
    near_parts = attend_near(image_counts, second, early)
    weights_far = lax.ppermute(weights_late, "core", [(0, 1), (1, 0)])
    parts = attend_far(image_counts, far, near_parts)
    parts = lax.all_to_all(parts, ("yl", "core"), 0, 0)
    partial = project(parts, qk_gain, raw, weights, weights_far, x_count, model_width)
    shares = lax.all_to_all(partial, "x", 0, 0)
    return leave(rows, factors, shares)


def solution(mesh):
    split = jax.sharding.Mesh(mesh.devices.reshape(16, 2, 2, 4, 2), ("z", "yh", "yl", "x", "core"))
    dp, head = ("z", "yh", "yl"), ("x", "core")
    in_specs = (P(dp, None), P(dp, None), P(None, None, head), P(head, None), P(), P(), P())
    out_specs = (P(dp + head, None), P(dp + head, None))
    return jax.shard_map(
        per_device, mesh=split, in_specs=in_specs, out_specs=out_specs, check_vma=False
    )
```
